32 devices in a mesh: dp: 8 (over z, x), tensor: 4 (over y, core).
Axes of the slice: x: 2, y: 2, z: 4, core: 2. Of those that a mesh axis runs over, the one named last changes fastest.
Arguments:
- layer_input: bfloat16 [16384, 1536], P(('dp', 'tensor')), may hold values from -6 to 6
- out_grad: bfloat16 [16384, 1536], P(('dp', 'tensor')), may hold values from -6 to 6
- small_params: float32 [21392], replicated, may hold values from -7 to 3, as said below
- small_first: float32 [21392], replicated, as said below
- small_second: float32 [21392], replicated, may hold values from 862 to 3449
- w_zx: float32 [1536, 2, 3072], P('dp', None, 'tensor'), may hold values from -1 to 1, as said below
- zx_first: float32 [1536, 2, 3072], P('dp', None, 'tensor'), as said below
- zx_second: float32 [1536, 2, 3072], P('dp', None, 'tensor'), may hold values from 215 to 862
- w_bc: float32 [1536, 256], P('dp'), may hold values from -0.15625 to 0.15625
- bc_first: float32 [1536, 256], P('dp'), as said below
- bc_second: float32 [1536, 256], P('dp'), may hold values from 862 to 3449
- w_dt: float32 [1536, 48], P('dp', 'tensor'), may hold values from -0.15625 to 0.15625
- dt_first: float32 [1536, 48], P('dp', 'tensor'), as said below
- dt_second: float32 [1536, 48], P('dp', 'tensor'), may hold values from 862 to 3449
- w_out: float32 [1536, 3072], P('dp', 'tensor'), may hold values from -0.109375 to 0.109375
- out_first: float32 [1536, 3072], P('dp', 'tensor'), as said below
- out_second: float32 [1536, 3072], P('dp', 'tensor'), may hold values from 862 to 3449
Outputs:
- layer_output: bfloat16 [16384, 1536], P(('dp', 'tensor'))
- input_grad: float32 [16384, 1536], P(('dp', 'tensor'))
- small_new: float32 [21392], replicated
- small_first_new: float32 [21392], replicated
- small_second_new: float32 [21392], replicated
- zx_new: float32 [1536, 2, 3072], P('dp', None, 'tensor')
- zx_first_new: float32 [1536, 2, 3072], P('dp', None, 'tensor')
- zx_second_new: float32 [1536, 2, 3072], P('dp', None, 'tensor')
- bc_new: float32 [1536, 256], P('dp')
- bc_first_new: float32 [1536, 256], P('dp')
- bc_second_new: float32 [1536, 256], P('dp')
- dt_new: float32 [1536, 48], P('dp', 'tensor')
- dt_first_new: float32 [1536, 48], P('dp', 'tensor')
- dt_second_new: float32 [1536, 48], P('dp', 'tensor')
- out_new: float32 [1536, 3072], P('dp', 'tensor')
- out_first_new: float32 [1536, 3072], P('dp', 'tensor')
- out_second_new: float32 [1536, 3072], P('dp', 'tensor')
The draws below stay inside these ranges and needn't reach their ends.
Inputs may be any that keep to these rules, and one draw needn't show every extreme that they name: `small_params`: gains near 1, convolution entries and biases within -0.5 to 0.5, softplus(dt_bias) within 0.001 to 0.1, exp(a_log) within 1 to 16, d_skip within 0.5 to 1.5. `small_first`: entries of both signs. `w_zx`: entries of order 1536 ** -0.5. `zx_first`: entries of both signs. `bc_first`: entries of both signs. `dt_first`: entries of both signs. `out_first`: entries of both signs.
All inputs are finite; a program needn't handle non-finite values.
Results may differ from the reference program's by a relative error of at most 0.0087.
The reference program's roundings to bfloat16 on the way count: a program that leaves them out, or rounds other values in their place, can miss the bound.
Values may be sent and summed in bfloat16 or wider, within the bound.
A program may use at most 256 MiB of HBM per device.

```python
import math
import jax
import jax.numpy as jnp
from jax import lax

D = 1536
DI = 3072
H = 48
NS = 128
P_SIZE = 64
CONV = 4
SPAN = 256
LEN = 2048
STEP = 10
TOKENS = 16384
NSMALL = 21392


def draw_small_params(key, part):
    key = jax.random.fold_in(key, 5)
    gain_in = 1.0 + 0.15 * jax.random.uniform(jax.random.fold_in(key, 1), (D,), jnp.float32, -1.0, 1.0)
    gate_gain = 1.0 + 0.15 * jax.random.uniform(jax.random.fold_in(key, 2), (DI,), jnp.float32, -1.0, 1.0)
    conv_x = jax.random.uniform(jax.random.fold_in(key, 3), (CONV * DI,), jnp.float32, -0.5, 0.5)
    bias_x = jax.random.uniform(jax.random.fold_in(key, 4), (DI,), jnp.float32, -0.5, 0.5)
    conv_bc = jax.random.uniform(jax.random.fold_in(key, 5), (CONV * 2 * NS,), jnp.float32, -0.5, 0.5)
    bias_bc = jax.random.uniform(jax.random.fold_in(key, 6), (2 * NS,), jnp.float32, -0.5, 0.5)
    step_size = jnp.exp(jax.random.uniform(jax.random.fold_in(key, 7), (H,), jnp.float32, math.log(0.001), math.log(0.1)))
    dt_bias = jnp.log(jnp.expm1(step_size))
    a_log = jnp.log(jax.random.uniform(jax.random.fold_in(key, 8), (H,), jnp.float32, 1.0, 16.0))
    d_skip = jax.random.uniform(jax.random.fold_in(key, 9), (H,), jnp.float32, 0.5, 1.5)
    return jnp.concatenate([gain_in, gate_gain, conv_x, bias_x, conv_bc, bias_bc, dt_bias, a_log, d_skip])


def draw_w_zx(key, part):
    key = jax.random.fold_in(key, 3)
    column = jnp.arange(DI, dtype=jnp.float32) / DI
    base = jnp.clip(jax.random.normal(key, (D, 2, DI), jnp.float32), -3.0, 3.0)
    rising = 0.6 + 1.2 * column
    return base * rising[None, None, :] / math.sqrt(D)


def draw_small_first(key, part):
    key = jax.random.fold_in(key, 11)
    base = jnp.clip(jax.random.normal(key, (D + (CONV + 2) * DI + (CONV + 1) * 2 * NS + 3 * H,), jnp.float32), -3.0, 3.0)
    return base * (math.sqrt(TOKENS) / 9.0)


def draw_zx_first(key, part):
    key = jax.random.fold_in(key, 13)
    base = jnp.clip(jax.random.normal(key, (D, 2, DI), jnp.float32), -3.0, 3.0)
    return base * (0.5 * math.sqrt(TOKENS) / 9.0)


def draw_bc_first(key, part):
    key = jax.random.fold_in(key, 17)
    base = jnp.clip(jax.random.normal(key, (D, 2 * NS), jnp.float32), -3.0, 3.0)
    return base * (math.sqrt(TOKENS) / 9.0)


def draw_dt_first(key, part):
    key = jax.random.fold_in(key, 19)
    base = jnp.clip(jax.random.normal(key, (D, H), jnp.float32), -3.0, 3.0)
    return base * (math.sqrt(TOKENS) / 9.0)


def draw_out_first(key, part):
    key = jax.random.fold_in(key, 23)
    base = jnp.clip(jax.random.normal(key, (D, DI), jnp.float32), -3.0, 3.0)
    return base * (math.sqrt(TOKENS) / 9.0)


def shard_levels(key, dims, shards, smallest, high):
    def one(position, blocks):
        heights = jax.random.uniform(jax.random.fold_in(jax.random.fold_in(key, 6), position), (blocks,), jnp.float32, smallest / len(shards), high / len(shards))
        return jnp.repeat(jnp.exp(heights), dims[position] // blocks).reshape((-1,) + (1,) * (len(dims) - position - 1))

    gain = one(*shards[0])
    for cut in shards[1:]:
        gain = gain * one(*cut)
    return gain


def gaussian(key, shape, scale, bound, cuts=(), held_as=jnp.bfloat16):
    level = shard_levels(key, shape, cuts, -0.22, 0.18) if cuts else 1.0
    values = jax.random.normal(key, shape, jnp.float32) * scale * level
    return jnp.minimum(jnp.maximum(values, -bound), bound).astype(held_as)


def setup_inputs(seed: int = 0) -> dict:
    streams_of = jax.random.split(jax.random.key(seed), 18)
    return {
        "layer_input": gaussian(streams_of[0], (TOKENS, D), 1.0, 6.0, ((0, 32),)),
        "out_grad": gaussian(streams_of[1], (TOKENS, D), 1.0, 6.0, ((0, 32),)),
        "small_params": draw_small_params(jax.random.fold_in(streams_of[17], 71), 0),
        "small_first": draw_small_first(jax.random.fold_in(streams_of[17], 71), 0),
        "small_second": jnp.clip(jnp.exp(jax.random.uniform(streams_of[4], (NSMALL,), jnp.float32, math.log(862.0), math.log(3449.0))), 862.0, 3449.0),
        "w_zx": draw_w_zx(jax.random.fold_in(streams_of[17], 71), 0),
        "zx_first": draw_zx_first(jax.random.fold_in(streams_of[17], 71), 0),
        "zx_second": jnp.clip(jnp.exp(math.log(862.0) - 1.38861724 * jax.random.uniform(streams_of[7], (D, 2, DI), jnp.float32) ** shard_levels(streams_of[7], (D, 2, DI), ((0, 8), (2, 4)), -0.2, 0.2)), 215.0, 862.0),
        "w_bc": gaussian(streams_of[8], (D, 2 * NS), D ** -0.5, 0.15625, ((0, 8),), jnp.float32),
        "bc_first": draw_bc_first(jax.random.fold_in(streams_of[17], 71), 0),
        "bc_second": jnp.clip(jnp.exp(math.log(3449.0) - 1.3865843422731479 * jax.random.uniform(streams_of[10], (D, 2 * NS), jnp.float32) ** shard_levels(streams_of[10], (D, 2 * NS), ((0, 8),), -0.2, 0.2)), 862.0, 3449.0),
        "w_dt": gaussian(streams_of[11], (D, H), D ** -0.5, 0.15625, ((0, 8), (1, 4)), jnp.float32),
        "dt_first": draw_dt_first(jax.random.fold_in(streams_of[17], 71), 0),
        "dt_second": jnp.clip(jnp.exp(math.log(3449.0) - 1.3865843422731479 * jax.random.uniform(streams_of[13], (D, H), jnp.float32) ** shard_levels(streams_of[13], (D, H), ((0, 8), (1, 4)), -0.2, 0.2)), 862.0, 3449.0),
        "w_out": gaussian(streams_of[14], (D, DI), DI ** -0.5, 0.109375, ((0, 8), (1, 4)), jnp.float32),
        "out_first": draw_out_first(jax.random.fold_in(streams_of[17], 71), 0),
        "out_second": jnp.clip(jnp.exp(math.log(3449.0) - 1.3865843422731479 * jax.random.uniform(streams_of[16], (D, DI), jnp.float32) ** shard_levels(streams_of[16], (D, DI), ((0, 8), (1, 4)), -0.2, 0.2)), 862.0, 3449.0),
    }


@jax.custom_vjp
def low(v):
    return lax.optimization_barrier(v.astype(jnp.bfloat16)).astype(jnp.float32)

@jax.custom_vjp
def low_back(v):
    return v

def low_keep(v):
    return (low(v), None)

def low_pass(kept, grad):
    return (grad,)

def back_keep(v):
    return (v, None)

def back_low(kept, grad):
    return (low(grad),)
low.defvjp(low_keep, low_pass)
low_back.defvjp(back_keep, back_low)
HIGHEST = lax.Precision.HIGHEST
norm_eps = 1e-05
adam_eps = 1e-08
beta_first = 0.9
beta_second = 0.95
matrix_rate = 0.01
small_rate = 0.1
matrix_decay = 0.1

def unpack(flat):
    gain_in = flat[:D]
    cursor = D
    gate_gain = flat[cursor:cursor + DI]
    cursor = cursor + DI
    conv_x = flat[cursor:cursor + CONV * DI].reshape(CONV, DI)
    cursor = cursor + CONV * DI
    bias_x = flat[cursor:cursor + DI]
    cursor = cursor + DI
    conv_bc = flat[cursor:cursor + CONV * 2 * NS].reshape(CONV, 2 * NS)
    cursor = cursor + CONV * 2 * NS
    bias_bc = flat[cursor:cursor + 2 * NS]
    cursor = cursor + 2 * NS
    dt_bias = flat[cursor:cursor + H]
    a_log = flat[cursor + H:cursor + 2 * H]
    d_skip = flat[cursor + 2 * H:cursor + 3 * H]
    return (gain_in, gate_gain, conv_x, bias_x, conv_bc, bias_bc, dt_bias, a_log, d_skip)

def causal_conv(values, conv_taps, conv_bias):
    length = values.shape[0]
    padded = jnp.pad(values, ((CONV - 1, 0), (0, 0)))
    result = conv_bias[None, :] + conv_taps[0][None, :] * padded[0:length]
    for tap_index in range(1, CONV):
        result = result + conv_taps[tap_index][None, :] * padded[tap_index:tap_index + length]
    return result

def ssd(inputs, steps_dt, decay_rates, b_rows, c_rows, d_skip):
    length, head_count = steps_dt.shape
    blocks = length // SPAN
    x_blocks = inputs.reshape(blocks, SPAN, head_count, P_SIZE)
    dt_blocks = steps_dt.reshape(blocks, SPAN, head_count)
    b_blocks = b_rows.reshape(blocks, SPAN, NS)
    c_blocks = c_rows.reshape(blocks, SPAN, NS)
    below_diag = jnp.arange(SPAN)[:, None] >= jnp.arange(SPAN)[None, :]

    def within(block):
        x_part, dt_part, b_part, c_part = block
        log_decay = jnp.cumsum(dt_part * decay_rates[None, :], axis=0)
        log_gaps = log_decay[:, None, :] - log_decay[None, :, :]
        causal_mask = below_diag[:, :, None]
        decays = jnp.where(causal_mask, jnp.exp(jnp.where(causal_mask, log_gaps, 0.0)), 0.0)
        scores = jnp.dot(c_part, b_part.T, precision=HIGHEST)
        mixing = scores[:, :, None] * decays * dt_part[None, :, :]
        y_part = jnp.einsum('ijh,jhp->ihp', mixing, x_part, precision=HIGHEST)
        tail_decay = jnp.exp(log_decay[-1][None, :] - log_decay) * dt_part
        block_state = jnp.einsum('jh,jhp,jn->hpn', tail_decay, x_part, b_part, precision=HIGHEST)
        return (y_part, block_state, log_decay)
    y_within, states, log_decay = lax.map(jax.checkpoint(within), (x_blocks, dt_blocks, b_blocks, c_blocks))

    def carry_step(running, block):
        block_state, block_total = block
        return (jnp.exp(block_total)[:, None, None] * running + block_state, running)
    start_state = jnp.zeros((head_count, P_SIZE, NS), jnp.float32)
    last_state, entering = lax.scan(carry_step, start_state, (states, log_decay[:, -1, :]))
    y_across = jnp.einsum('cih,cin,chpn->cihp', jnp.exp(log_decay), c_blocks, entering, precision=HIGHEST)
    y_all = (y_within + y_across).reshape(length, head_count, P_SIZE)
    return y_all + d_skip[None, :, None] * inputs

def mixer(z_part, x_part, bc_part, dt_raw, conv_x, bias_x, conv_bc, bias_bc, dt_bias, a_log, d_skip):
    x_act = jax.nn.silu(causal_conv(x_part, conv_x, bias_x))
    bc_act = jax.nn.silu(causal_conv(bc_part, conv_bc, bias_bc))
    steps_dt = jax.nn.softplus(dt_raw + dt_bias[None, :])
    head_count = dt_raw.shape[1]
    y_heads = ssd(x_act.reshape(-1, head_count, P_SIZE), steps_dt, -jnp.exp(a_log), bc_act[:, :NS], bc_act[:, NS:], d_skip)
    return y_heads.reshape(-1, head_count * P_SIZE) * jax.nn.silu(z_part)

def layer(sequence, small, w_zx, w_bc, w_dt, w_out):
    gain_in, gate_gain, conv_x, bias_x, conv_bc, bias_bc, dt_bias, a_log, d_skip = unpack(small)
    normed_in = sequence * lax.rsqrt(lax.optimization_barrier(jnp.mean(sequence * sequence, axis=-1, keepdims=True)) + norm_eps) * gain_in[None, :]
    rounded = low(normed_in)
    zx_proj = low_back(jnp.einsum('ld,dkc->lkc', rounded, low(w_zx), precision=HIGHEST))
    bc_proj = low_back(jnp.dot(rounded, low(w_bc), precision=HIGHEST))
    dt_raw = low_back(jnp.dot(rounded, low(w_dt), precision=HIGHEST))
    gated = mixer(zx_proj[:, 0], zx_proj[:, 1], bc_proj, dt_raw, conv_x, bias_x, conv_bc, bias_bc, dt_bias, a_log, d_skip)
    normed = gated * lax.rsqrt(lax.optimization_barrier(jnp.mean(gated * gated, axis=-1, keepdims=True)) + norm_eps) * gate_gain[None, :]
    branch = jnp.einsum('lc,dc->ld', low(normed), low(w_out), precision=HIGHEST)
    return sequence + branch

def adamw_step(weight, first, second, grad, rate, decay):
    first_new = beta_first * first + (1.0 - beta_first) * grad
    second_new = beta_second * second + (1.0 - beta_second) * grad * grad
    hat_first = first_new / (1.0 - beta_first ** STEP)
    hat_second = second_new / (1.0 - beta_second ** STEP)
    weight_new = weight - rate * (hat_first / (jnp.sqrt(hat_second) + adam_eps) + decay * weight)
    return (weight_new, first_new, second_new)

def reference(layer_input, out_grad, small_params, small_first, small_second, w_zx, zx_first, zx_second, w_bc, bc_first, bc_second, w_dt, dt_first, dt_second, w_out, out_first, out_second):
    seq_count = TOKENS // LEN
    sequences = layer_input.astype(jnp.float32).reshape(seq_count, LEN, D)
    cotangents = out_grad.astype(jnp.float32).reshape(seq_count, LEN, D)
    params = (small_params, w_zx, w_bc, w_dt, w_out)

    def one_sequence(totals, pair):
        output, pull = jax.vjp(layer, pair[0], *params)
        grads = pull(pair[1])
        summed = tuple((before + fresh for before, fresh in zip(totals, grads[1:])))
        return (summed, (output.astype(jnp.bfloat16), grads[0]))
    zero_grads = tuple((jnp.zeros_like(item) for item in params))
    totals, (outputs, input_grads) = lax.scan(one_sequence, zero_grads, (sequences, cotangents))
    small_new, small_first_new, small_second_new = adamw_step(small_params, small_first, small_second, totals[0], small_rate, 0.0)
    zx_new, zx_first_new, zx_second_new = adamw_step(w_zx, zx_first, zx_second, totals[1], matrix_rate, matrix_decay)
    bc_new, bc_first_new, bc_second_new = adamw_step(w_bc, bc_first, bc_second, totals[2], matrix_rate, matrix_decay)
    dt_new, dt_first_new, dt_second_new = adamw_step(w_dt, dt_first, dt_second, totals[3], matrix_rate, matrix_decay)
    out_new, out_first_new, out_second_new = adamw_step(w_out, out_first, out_second, totals[4], matrix_rate, matrix_decay)
    return (outputs.reshape(TOKENS, D), input_grads.reshape(TOKENS, D), small_new, small_first_new, small_second_new, zx_new, zx_first_new, zx_second_new, bc_new, bc_first_new, bc_second_new, dt_new, dt_first_new, dt_second_new, out_new, out_first_new, out_second_new)
```

```python
import functools

import jax
import jax.numpy as jnp
from jax import lax
from jax.experimental import pallas as pl
from jax.experimental.pallas import tpu as pltpu
from jax.sharding import PartitionSpec as P

D = 1536
DI = 3072
H = 48
NS = 128
P_SIZE = 64
CONV = 4
LEN = 2048
STEP = 10

T = 128
ROWS = 256
LANES = 128

norm_eps = 1e-05
adam_eps = 1e-08
beta_first = 0.9
beta_second = 0.95
matrix_rate = 0.01
small_rate = 0.1
matrix_decay = 0.1

f32 = jnp.float32
bf16 = jnp.bfloat16
NN = (((1,), (0,)), ((), ()))
NT = (((1,), (1,)), ((), ()))
TN = (((0,), (0,)), ((), ()))
HIGHEST = lax.Precision.HIGHEST


def unpack(flat):
    gain_in = flat[:D]
    cursor = D
    gate_gain = flat[cursor : cursor + DI]
    cursor = cursor + DI
    conv_x = flat[cursor : cursor + CONV * DI].reshape(CONV, DI)
    cursor = cursor + CONV * DI
    bias_x = flat[cursor : cursor + DI]
    cursor = cursor + DI
    conv_bc = flat[cursor : cursor + CONV * 2 * NS].reshape(CONV, 2 * NS)
    cursor = cursor + CONV * 2 * NS
    bias_bc = flat[cursor : cursor + 2 * NS]
    cursor = cursor + 2 * NS
    dt_bias = flat[cursor : cursor + H]
    a_log = flat[cursor + H : cursor + 2 * H]
    d_skip = flat[cursor + 2 * H : cursor + 3 * H]
    return (gain_in, gate_gain, conv_x, bias_x, conv_bc, bias_bc, dt_bias, a_log, d_skip)


def mm(a, b, dims=NN):
    return lax.dot_general(a, b, dims, preferred_element_type=f32)


def mm_exact(a, b, dims=NN):
    return lax.dot_general(a, b, dims, preferred_element_type=f32, precision=HIGHEST)


def sigmoid(v):
    return 0.5 * jnp.tanh(0.5 * v) + 0.5


def softplus(v):
    return jnp.maximum(v, 0.0) + jnp.log1p(jnp.exp(-jnp.abs(v)))


def spread(col):
    return jnp.broadcast_to(col, (T, LANES))


def block_iota(axis):
    return lax.broadcasted_iota(jnp.int32, (T, LANES), axis)


def head_rows(dr_ref, head_ref, rows):
    raw = dr_ref[rows, :] + head_ref[0:1, :]
    dt = softplus(raw)
    low_tri = jnp.where(block_iota(0) >= block_iota(1), 1.0, 0.0).astype(f32)
    decay = mm_exact(low_tri, dt * head_ref[1:2, :])
    return raw, dt, decay


def forward_body(
    width,
    xg_ref, w_ref, cot_ref, wo_ref, taps_ref, head_ref, chan_ref,
    z_ref, v_ref, xc_ref, dr_ref, y_ref, dn_ref, st_ref, red_ref,
    halo, state,
):
    pairs = width // LANES
    step = pl.program_id(0)

    @pl.when(step == 0)
    def _():
        halo[0:8, :] = jnp.zeros((8, halo.shape[1]), f32)
        state[...] = jnp.zeros_like(state)

    wide = width + 2 * NS
    dr_ref[...] = mm(xg_ref[...], w_ref[:, width + wide :])
    halo[8 : 8 + ROWS, :] = mm(xg_ref[...], w_ref[:, width : width + wide])
    z_ref[...] = mm(xg_ref[...], w_ref[:, :width])
    dn_ref[...] = mm(cot_ref[...], wo_ref[...])
    low_half = block_iota(1) < P_SIZE
    causal = block_iota(0) >= block_iota(1)

    def convolved(sub, block):
        cols = slice(block * LANES, (block + 1) * LANES)
        total = taps_ref[CONV : CONV + 1, cols]
        for k in range(CONV):
            first = 8 - (CONV - 1) + k + sub * T
            total = total + taps_ref[k : k + 1, cols] * halo[first : first + T, cols]
        rows = slice(sub * T, (sub + 1) * T)
        xc_ref[rows, cols] = total
        v_ref[rows, cols] = halo[8 + sub * T : 8 + (sub + 1) * T, cols].astype(bf16)
        return total * sigmoid(total)

    for sub in range(ROWS // T):
        rows = slice(sub * T, (sub + 1) * T)
        raw, dt, decay = head_rows(dr_ref, head_ref, rows)
        decay_t = decay.T
        b_low = convolved(sub, pairs).astype(bf16)
        c_low = convolved(sub, pairs + 1).astype(bf16)
        b_t = b_low.T
        scores = jnp.where(causal, mm(c_low, b_low, NT), 0.0)
        squares = jnp.zeros((T, LANES), f32)
        inner = jnp.zeros((T, LANES), f32)
        st_ref[sub] = state[...].astype(bf16)
        for p in range(pairs):
            cols = slice(p * LANES, (p + 1) * LANES)
            x = convolved(sub, p)
            l1, l2 = spread(decay[:, 2 * p : 2 * p + 1]), spread(decay[:, 2 * p + 1 : 2 * p + 2])
            both = jnp.where(low_half, l1, l2)
            dtb = jnp.where(
                low_half, spread(dt[:, 2 * p : 2 * p + 1]), spread(dt[:, 2 * p + 1 : 2 * p + 2])
            )
            u = x * dtb
            m1 = scores * jnp.exp(jnp.minimum(l1 - decay_t[2 * p : 2 * p + 1, :], 0.0))
            m2 = scores * jnp.exp(jnp.minimum(l2 - decay_t[2 * p + 1 : 2 * p + 2, :], 0.0))
            mixing = jnp.concatenate([m1.astype(bf16), m2.astype(bf16)], axis=1)
            parts = jnp.concatenate(
                [jnp.where(low_half, u, 0.0).astype(bf16), jnp.where(low_half, 0.0, u).astype(bf16)],
                axis=0,
            )
            last = both[T - 1 : T, :]
            entering = st_ref[sub, :, cols]
            y = mm(mixing, parts) + jnp.exp(both) * mm(c_low, entering) + chan_ref[1:2, cols] * x
            tail = (u * jnp.exp(last - both)).astype(bf16)
            state[:, cols] = jnp.exp(last) * state[:, cols] + mm(b_t, tail)
            y_ref[rows, cols] = y
            z = z_ref[rows, cols]
            gated = y * (z * sigmoid(z))
            squares = squares + gated * gated
            inner = inner + gated * chan_ref[0:1, cols] * dn_ref[rows, cols]
        ones = jnp.ones((8, LANES), f32)
        red_ref[0:8, rows] = mm_exact(ones, squares, NT)
        red_ref[8:16, rows] = mm_exact(ones, inner, NT)
    halo[0:8, :] = halo[ROWS : ROWS + 8, :]


def ssd_forward(xg, w_cat, cot, w_out, taps, head, chan):
    tokens = xg.shape[0]
    width = w_out.shape[1]
    wide = width + 2 * NS
    steps = tokens // ROWS
    subs = ROWS // T
    per_seq = LEN // ROWS
    assert per_seq == steps
    row = lambda n: pl.BlockSpec((ROWS, n), lambda i: (i, 0))
    whole = lambda a: pl.BlockSpec(a.shape, lambda i: (0,) * a.ndim, pipeline_mode=pl.Buffered(1))
    return pl.pallas_call(
        functools.partial(forward_body, width),
        grid=(steps,),
        in_specs=[row(D), whole(w_cat), row(D), whole(w_out), whole(taps), whole(head), whole(chan)],
        out_specs=[
            row(width), row(wide), row(wide), row(LANES), row(width), row(width),
            pl.BlockSpec((subs, NS, width), lambda i: (i, 0, 0)),
            pl.BlockSpec((16, ROWS), lambda i: (0, i)),
        ],
        out_shape=[
            jax.ShapeDtypeStruct((tokens, width), f32),
            jax.ShapeDtypeStruct((tokens, wide), bf16),
            jax.ShapeDtypeStruct((tokens, wide), f32),
            jax.ShapeDtypeStruct((tokens, LANES), f32),
            jax.ShapeDtypeStruct((tokens, width), f32),
            jax.ShapeDtypeStruct((tokens, width), f32),
            jax.ShapeDtypeStruct((tokens // T, NS, width), bf16),
            jax.ShapeDtypeStruct((16, tokens), f32),
        ],
        scratch_shapes=[pltpu.VMEM((ROWS + 8, wide), f32), pltpu.VMEM((NS, width), f32)],
        compiler_params=pltpu.CompilerParams(vmem_limit_bytes=56 * 2**20),
        name="layer_forward",
    )(xg, w_cat, cot, w_out, taps, head, chan)


def backward_body(
    width,
    z_ref, v_ref, xc_ref, dr_ref, y_ref, dn_ref, st_ref, red_ref, taps_ref, head_ref, chan_ref, pick_ref,
    nl_ref, d_ref, acc_ref, hacc_ref,
    dxh, dstate, yst, bds, dyeb, utb, gin, gout, xdu, turn,
):
    pairs = width // LANES
    wide = width + 2 * NS
    step = pl.program_id(0)

    @pl.when(step == 0)
    def _():
        dxh[T : T + 8, :] = jnp.zeros((8, wide), f32)
        dstate[...] = jnp.zeros_like(dstate)
        acc_ref[...] = jnp.zeros_like(acc_ref)
        hacc_ref[...] = jnp.zeros_like(hacc_ref)
        turn[...] = jnp.zeros_like(turn)

    low_half = block_iota(1) < P_SIZE
    row_at, col_at = block_iota(0), block_iota(1)
    until = row_at <= col_at
    before = row_at < col_at
    upper = jnp.where(until, 1.0, 0.0).astype(f32)
    strict = jnp.where(before, 1.0, 0.0).astype(f32)
    low_tri = jnp.where(row_at >= col_at, 1.0, 0.0).astype(bf16)

    def add(index, cols, value):
        acc_ref[index, :, cols] += jnp.sum(value.reshape(T // 8, 8, LANES), axis=0)

    def conv_back(rows, block, d_act, xc, s, act):
        cols = slice(block * LANES, (block + 1) * LANES)
        dxh[0:T, cols] = d_act * (s + act * (1.0 - s))
        v = v_ref[rows, cols].astype(f32)
        total = None
        for m in range(CONV):
            moved = dxh[m : m + T, cols]
            if m == 0:
                add(CONV, cols, moved)
            add(CONV - 1 - m, cols, v * moved)
            term = taps_ref[CONV - 1 - m : CONV - m, cols] * moved
            total = term if total is None else total + term
        d_ref[rows, width + block * LANES : width + (block + 1) * LANES] = total.astype(bf16)

    for sub in reversed(range(ROWS // T)):
        rows = slice(sub * T, (sub + 1) * T)
        raw, dt, decay = head_rows(dr_ref, head_ref, rows)
        decay_t = decay.T
        sums = red_ref[:, rows]
        q_row = lax.rsqrt(sums[0:8] / DI + norm_eps)
        k_row = q_row * q_row * q_row * sums[8:16] / DI
        q = spread(q_row.T[:, 0:1])
        kk = spread(k_row.T[:, 0:1])
        b_cols = slice(width, width + NS)
        c_cols = slice(width + NS, width + 2 * NS)
        b_xc, c_xc = xc_ref[rows, b_cols], xc_ref[rows, c_cols]
        b_s, c_s = sigmoid(b_xc), sigmoid(c_xc)
        b_act, c_act = b_xc * b_s, c_xc * c_s
        b_low, c_low = b_act.astype(bf16), c_act.astype(bf16)
        c_t = c_low.T
        scores_t = jnp.where(until, mm(b_low, c_low, NT), 0.0)
        ds_low = dstate[...].astype(bf16)
        yst[...] = mm(c_low, st_ref[sub])
        bds[...] = mm(b_low, ds_low)
        d_scores = jnp.zeros((T, LANES), f32)
        for p in range(pairs):
            cols = slice(p * LANES, (p + 1) * LANES)
            z, y, dn = z_ref[rows, cols], y_ref[rows, cols], dn_ref[rows, cols]
            gain = chan_ref[0:1, cols]
            s = sigmoid(z)
            sz = z * s
            gated = y * sz
            gq = gated * q
            dg = q * gain * dn - gated * kk
            add(CONV + 1, cols, gq * dn)
            nl_ref[rows, cols] = (gq * gain).astype(bf16)
            d_ref[rows, cols] = (dg * y * (s + sz * (1.0 - s))).astype(bf16)
            dy = dg * sz
            xc = xc_ref[rows, cols]
            xs = sigmoid(xc)
            x = xc * xs
            l1, l2 = spread(decay[:, 2 * p : 2 * p + 1]), spread(decay[:, 2 * p + 1 : 2 * p + 2])
            both = jnp.where(low_half, l1, l2)
            dtb = jnp.where(
                low_half, spread(dt[:, 2 * p : 2 * p + 1]), spread(dt[:, 2 * p + 1 : 2 * p + 2])
            )
            u = x * dtb
            last = both[T - 1 : T, :]
            e1 = jnp.exp(jnp.minimum(decay_t[2 * p : 2 * p + 1, :] - l1, 0.0))
            e2 = jnp.exp(jnp.minimum(decay_t[2 * p + 1 : 2 * p + 2, :] - l2, 0.0))
            dy_low = dy.astype(bf16)
            zero = jnp.zeros_like(dy_low)
            u_low = u.astype(bf16)
            du_in = mm(
                jnp.concatenate([(scores_t * e1).astype(bf16), (scores_t * e2).astype(bf16)], axis=1),
                jnp.concatenate(
                    [jnp.where(low_half, dy_low, zero), jnp.where(low_half, zero, dy_low)], axis=0
                ),
            )
            d_mix = mm(
                jnp.concatenate(
                    [jnp.where(low_half, u_low, zero), jnp.where(low_half, zero, u_low)], axis=0
                ),
                dy_low,
                NT,
            )
            d1, d2 = d_mix[:T] * e1, d_mix[T:] * e2
            d_scores = d_scores + d1 + d2
            reach = mm(
                jnp.concatenate([(d1 * scores_t).astype(bf16), (d2 * scores_t).astype(bf16)], axis=0),
                low_tri,
            )
            turn[2 * p : 2 * p + 1, :] = jnp.sum(jnp.where(before, reach[:T], 0.0), axis=0, keepdims=True)
            turn[2 * p + 1 : 2 * p + 2, :] = jnp.sum(
                jnp.where(before, reach[T:], 0.0), axis=0, keepdims=True
            )
            tail = jnp.exp(last - both)
            dye = dy * jnp.exp(both)
            du_out = tail * bds[:, cols]
            du = du_in + du_out
            gin[:, cols] = (dye * yst[:, cols]).astype(bf16)
            gout[:, cols] = (u * du_out).astype(bf16)
            xdu[:, cols] = (x * du).astype(bf16)
            dyeb[:, cols] = dye.astype(bf16)
            utb[:, cols] = (u * tail).astype(bf16)
            add(CONV + 2, cols, dy * x)
            conv_back(rows, p, dtb * du + chan_ref[1:2, cols] * dy, xc, xs, x)
        d_scores = jnp.where(until, d_scores, 0.0).astype(bf16)
        d_b = mm(d_scores, c_low) + mm(utb[...], ds_low, NT)
        d_c = mm(d_scores, b_low, TN) + mm(dyeb[...], st_ref[sub], NT)
        conv_back(rows, pairs, d_b, b_xc, b_s, b_act)
        conv_back(rows, pairs + 1, d_c, c_xc, c_s, c_act)
        ended = jnp.zeros((1, LANES), f32)
        for p in range(pairs):
            cols = slice(p * LANES, (p + 1) * LANES)
            last = jnp.where(
                low_half[0:1], decay[T - 1 : T, 2 * p : 2 * p + 1], decay[T - 1 : T, 2 * p + 1 : 2 * p + 2]
            )
            fade = jnp.exp(last)
            before_ds = dstate[:, cols]
            through = jnp.sum(before_ds * st_ref[sub, :, cols].astype(f32), axis=0, keepdims=True) * fade
            ended = ended + mm_exact(through, pick_ref[cols, :].astype(f32))
            dstate[:, cols] = fade * before_ds + mm(c_t, dyeb[:, cols])
        gin_heads = mm(gin[...], pick_ref[...])
        gout_heads = mm(gout[...], pick_ref[...])
        reached = (
            turn[...].T
            + mm_exact(upper, gin_heads)
            + mm_exact(strict, gout_heads, TN)
            + ended
        )
        d_raw = (head_ref[1:2, :] * reached + mm(xdu[...], pick_ref[...])) * sigmoid(raw)
        d_ref[rows, width + wide :] = d_raw.astype(bf16)
        hacc_ref[0] += jnp.sum(d_raw.reshape(T // 8, 8, LANES), axis=0)
        hacc_ref[1] += jnp.sum((dt * reached).reshape(T // 8, 8, LANES), axis=0)
        dxh[T : T + 8, :] = dxh[0:8, :]


def ssd_backward(z, v, xc, dr, y, dn, st, red, taps, head, chan, pick):
    tokens, width = z.shape
    wide = width + 2 * NS
    steps = tokens // ROWS
    subs = ROWS // T
    row = lambda n: pl.BlockSpec((ROWS, n), lambda i: (steps - 1 - i, 0))
    whole = lambda a: pl.BlockSpec(a.shape, lambda i: (0,) * a.ndim, pipeline_mode=pl.Buffered(1))
    total = width + wide + LANES
    vm = pltpu.VMEM
    return pl.pallas_call(
        functools.partial(backward_body, width),
        grid=(steps,),
        in_specs=[
            row(width), row(wide), row(wide), row(LANES), row(width), row(width),
            pl.BlockSpec((subs, NS, width), lambda i: (steps - 1 - i, 0, 0)),
            pl.BlockSpec((16, ROWS), lambda i: (0, steps - 1 - i)),
            whole(taps), whole(head), whole(chan), whole(pick),
        ],
        out_specs=[
            row(width), row(total),
            pl.BlockSpec((CONV + 3, 8, wide), lambda i: (0, 0, 0)),
            pl.BlockSpec((2, 8, LANES), lambda i: (0, 0, 0)),
        ],
        out_shape=[
            jax.ShapeDtypeStruct((tokens, width), bf16),
            jax.ShapeDtypeStruct((tokens, total), bf16),
            jax.ShapeDtypeStruct((CONV + 3, 8, wide), f32),
            jax.ShapeDtypeStruct((2, 8, LANES), f32),
        ],
        scratch_shapes=[
            vm((T + 8, wide), f32), vm((NS, width), f32), vm((T, width), f32), vm((T, width), f32),
            vm((T, width), bf16), vm((T, width), bf16), vm((T, width), bf16), vm((T, width), bf16),
            vm((T, width), bf16), vm((T, LANES), f32),
        ],
        compiler_params=pltpu.CompilerParams(vmem_limit_bytes=56 * 2**20),
        name="layer_backward",
    )(z, v, xc, dr, y, dn, st, red, taps, head, chan, pick)


def adamw_step(weight, first, second, grad, rate, decay):
    first_new = beta_first * first + (1.0 - beta_first) * grad
    second_new = beta_second * second + (1.0 - beta_second) * grad * grad
    hat_first = first_new / (1.0 - beta_first**STEP)
    hat_second = second_new / (1.0 - beta_second**STEP)
    weight_new = weight - rate * (hat_first / (jnp.sqrt(hat_second) + adam_eps) + decay * weight)
    return (weight_new, first_new, second_new)


def local(
    layer_input,
    out_grad,
    small_params,
    small_first,
    small_second,
    w_zx,
    zx_first,
    zx_second,
    w_bc,
    bc_first,
    bc_second,
    w_dt,
    dt_first,
    dt_second,
    w_out,
    out_first,
    out_second,
):
    tensor_index = lax.axis_index("tensor")
    local_in = layer_input.astype(f32)
    gain_in, gate_gain, conv_x, bias_x, conv_bc, bias_bc, dt_bias, a_log, d_skip = unpack(
        small_params
    )
    rows_own = w_zx.shape[0]
    width = w_zx.shape[2]
    heads = w_dt.shape[1]
    chan_start = tensor_index * width
    head_start = tensor_index * heads
    gate_local = lax.dynamic_slice_in_dim(gate_gain, chan_start, width, 0)
    conv_local = lax.dynamic_slice_in_dim(conv_x, chan_start, width, 1)
    bias_local = lax.dynamic_slice_in_dim(bias_x, chan_start, width, 0)
    dtb_local = lax.dynamic_slice_in_dim(dt_bias, head_start, heads, 0)
    a_local = -jnp.exp(lax.dynamic_slice_in_dim(a_log, head_start, heads, 0))
    dskip_local = lax.dynamic_slice_in_dim(d_skip, head_start, heads, 0)
    taps = jnp.concatenate(
        [
            jnp.concatenate([conv_local, conv_bc], axis=1),
            jnp.concatenate([bias_local, bias_bc])[None, :],
            jnp.zeros((8 - CONV - 1, width + 2 * NS), f32),
        ],
        axis=0,
    )
    lanes = lambda v: jnp.pad(v, (0, LANES - heads))
    head = jnp.pad(jnp.stack([lanes(dtb_local), lanes(a_local)]), ((0, 6), (0, 0)))
    chan = jnp.pad(jnp.stack([gate_local, jnp.repeat(dskip_local, P_SIZE)]), ((0, 6), (0, 0)))
    pick = jnp.asarray(
        (jnp.arange(width)[:, None] // P_SIZE == jnp.arange(LANES)[None, :]), bf16
    )

    inv_in = lax.rsqrt(jnp.mean(local_in * local_in, axis=-1, keepdims=True) + norm_eps)
    normed_in = local_in * inv_in * gain_in[None, :]
    w_cat = jnp.concatenate(
        [
            w_zx.reshape(rows_own, 2 * width).astype(bf16),
            w_bc.astype(bf16),
            jnp.pad(w_dt, ((0, 0), (0, LANES - heads))).astype(bf16),
        ],
        axis=1,
    )
    xg = lax.all_gather(normed_in.astype(bf16), "tensor", axis=0, tiled=True)
    w_all = lax.all_gather(w_cat, "dp", axis=0, tiled=True)
    wo_all = lax.all_gather(w_out.astype(bf16), "dp", axis=0, tiled=True)
    cot_all = lax.all_gather(out_grad, "tensor", axis=0, tiled=True)

    z, v, xc, dr, y, dn, st, red = ssd_forward(xg, w_all, cot_all, wo_all, taps, head, chan)
    sums = lax.psum(red[::8], "tensor")
    red = jnp.repeat(sums, 8, axis=0)
    normed_low, d_cat, acc, hacc = ssd_backward(z, v, xc, dr, y, dn, st, red, taps, head, chan, pick)

    branch = mm(normed_low, wo_all, NT).astype(bf16)
    own_branch = lax.psum_scatter(branch, "tensor", scatter_dimension=0, tiled=True)
    layer_output = (local_in + own_branch.astype(f32)).astype(bf16)
    grad_out = mm(cot_all, normed_low, TN).astype(bf16)
    owner_out = lax.psum_scatter(grad_out, "dp", scatter_dimension=0, tiled=True).astype(f32)

    back = mm(d_cat, w_all, NT).astype(bf16)
    d_normed_in = lax.psum_scatter(back, "tensor", scatter_dimension=0, tiled=True).astype(f32)
    grad_cat = mm(xg, d_cat, TN).astype(bf16)
    owner_cat = lax.psum_scatter(grad_cat, "dp", scatter_dimension=0, tiled=True).astype(f32)
    owner_zx = owner_cat[:, : 2 * width].reshape(rows_own, 2, width)
    owner_bc = lax.psum(owner_cat[:, 2 * width : 2 * width + 2 * NS], "tensor")
    owner_dt = owner_cat[:, 2 * width + 2 * NS : 2 * width + 2 * NS + heads]

    inner_in = jnp.sum(local_in * gain_in[None, :] * d_normed_in, axis=-1, keepdims=True)
    input_grad = (
        out_grad.astype(f32)
        + inv_in * gain_in[None, :] * d_normed_in
        - local_in * (inv_in * inv_in * inv_in * inner_in / D)
    )
    grad_gain_in = jnp.sum(local_in * inv_in * d_normed_in, axis=0)

    acc = jnp.sum(acc, axis=1)
    hacc = jnp.sum(hacc, axis=1)[:, :heads]
    grad_skip = jnp.sum(acc[CONV + 2, :width].reshape(heads, P_SIZE), axis=1)
    place = lambda whole, part, start, axis: lax.dynamic_update_slice_in_dim(
        jnp.zeros_like(whole), part, start, axis
    )
    flat_grad = jnp.concatenate(
        [
            grad_gain_in,
            place(gate_gain, acc[CONV + 1, :width], chan_start, 0),
            place(conv_x, acc[:CONV, :width], chan_start, 1).reshape(-1),
            place(bias_x, acc[CONV, :width], chan_start, 0),
            acc[:CONV, width:].reshape(-1),
            acc[CONV, width:],
            place(dt_bias, hacc[0], head_start, 0),
            place(a_log, hacc[1] * a_local, head_start, 0),
            place(d_skip, grad_skip, head_start, 0),
        ]
    )
    small_grad = lax.psum(flat_grad, ("dp", "tensor"))
    small_new, small_first_new, small_second_new = adamw_step(
        small_params, small_first, small_second, small_grad, small_rate, 0.0
    )
    zx_new, zx_first_new, zx_second_new = adamw_step(
        w_zx, zx_first, zx_second, owner_zx, matrix_rate, matrix_decay
    )
    bc_new, bc_first_new, bc_second_new = adamw_step(
        w_bc, bc_first, bc_second, owner_bc, matrix_rate, matrix_decay
    )
    dt_new, dt_first_new, dt_second_new = adamw_step(
        w_dt, dt_first, dt_second, owner_dt, matrix_rate, matrix_decay
    )
    out_new, out_first_new, out_second_new = adamw_step(
        w_out, out_first, out_second, owner_out, matrix_rate, matrix_decay
    )
    return (
        layer_output,
        input_grad,
        small_new,
        small_first_new,
        small_second_new,
        zx_new,
        zx_first_new,
        zx_second_new,
        bc_new,
        bc_first_new,
        bc_second_new,
        dt_new,
        dt_first_new,
        dt_second_new,
        out_new,
        out_first_new,
        out_second_new,
    )


def solution(mesh):
    return jax.shard_map(
        local,
        mesh=mesh,
        in_specs=(
            P(("dp", "tensor"), None),
            P(("dp", "tensor"), None),
            P(),
            P(),
            P(),
            P("dp", None, "tensor"),
            P("dp", None, "tensor"),
            P("dp", None, "tensor"),
            P("dp", None),
            P("dp", None),
            P("dp", None),
            P("dp", "tensor"),
            P("dp", "tensor"),
            P("dp", "tensor"),
            P("dp", "tensor"),
            P("dp", "tensor"),
            P("dp", "tensor"),
        ),
        out_specs=(
            P(("dp", "tensor"), None),
            P(("dp", "tensor"), None),
            P(),
            P(),
            P(),
            P("dp", None, "tensor"),
            P("dp", None, "tensor"),
            P("dp", None, "tensor"),
            P("dp", None),
            P("dp", None),
            P("dp", None),
            P("dp", "tensor"),
            P("dp", "tensor"),
            P("dp", "tensor"),
            P("dp", "tensor"),
            P("dp", "tensor"),
            P("dp", "tensor"),
        ),
        check_vma=False,
    )
```

```python
import functools

import jax
import jax.numpy as jnp
from jax import lax
from jax.experimental import pallas as pl
from jax.experimental.pallas import tpu as pltpu
from jax.sharding import PartitionSpec as P

D = 1536
DI = 3072
H = 48
NS = 128
P_SIZE = 64
CONV = 4
LEN = 2048
STEP = 10

T = 128
ROWS = 256
LANES = 128

norm_eps = 1e-05
adam_eps = 1e-08
beta_first = 0.9
beta_second = 0.95
matrix_rate = 0.01
small_rate = 0.1
matrix_decay = 0.1

f32 = jnp.float32
bf16 = jnp.bfloat16
NN = (((1,), (0,)), ((), ()))
NT = (((1,), (1,)), ((), ()))
TN = (((0,), (0,)), ((), ()))
HIGHEST = lax.Precision.HIGHEST


def unpack(flat):
    gain_in = flat[:D]
    cursor = D
    gate_gain = flat[cursor : cursor + DI]
    cursor = cursor + DI
    conv_x = flat[cursor : cursor + CONV * DI].reshape(CONV, DI)
    cursor = cursor + CONV * DI
    bias_x = flat[cursor : cursor + DI]
    cursor = cursor + DI
    conv_bc = flat[cursor : cursor + CONV * 2 * NS].reshape(CONV, 2 * NS)
    cursor = cursor + CONV * 2 * NS
    bias_bc = flat[cursor : cursor + 2 * NS]
    cursor = cursor + 2 * NS
    dt_bias = flat[cursor : cursor + H]
    a_log = flat[cursor + H : cursor + 2 * H]
    d_skip = flat[cursor + 2 * H : cursor + 3 * H]
    return (gain_in, gate_gain, conv_x, bias_x, conv_bc, bias_bc, dt_bias, a_log, d_skip)


def mm(a, b, dims=NN):
    return lax.dot_general(a, b, dims, preferred_element_type=f32)


def mm_exact(a, b, dims=NN):
    return lax.dot_general(a, b, dims, preferred_element_type=f32, precision=HIGHEST)


def sigmoid(v):
    return 0.5 * jnp.tanh(0.5 * v) + 0.5


def softplus(v):
    return jnp.maximum(v, 0.0) + jnp.log1p(jnp.exp(-jnp.abs(v)))


def spread(col):
    return jnp.broadcast_to(col, (T, LANES))


def block_iota(axis):
    return lax.broadcasted_iota(jnp.int32, (T, LANES), axis)


def head_rows(dr_ref, head_ref, rows):
    raw = dr_ref[rows, :] + head_ref[0:1, :]
    dt = softplus(raw)
    low_tri = jnp.where(block_iota(0) >= block_iota(1), 1.0, 0.0).astype(f32)
    decay = mm_exact(low_tri, dt * head_ref[1:2, :])
    return raw, dt, decay


def forward_body(
    width,
    xg_ref, w_ref, cot_ref, wo_ref, taps_ref, head_ref, chan_ref,
    z_ref, v_ref, xc_ref, dr_ref, y_ref, dn_ref, st_ref, red_ref,
    halo, state,
):
    pairs = width // LANES
    step = pl.program_id(0)

    @pl.when(step == 0)
    def _():
        halo[0:8, :] = jnp.zeros((8, halo.shape[1]), f32)
        state[...] = jnp.zeros_like(state)

    wide = width + 2 * NS
    dr_ref[...] = mm(xg_ref[...], w_ref[:, width + wide :])
    halo[8 : 8 + ROWS, :] = mm(xg_ref[...], w_ref[:, width : width + wide])
    z_ref[...] = mm(xg_ref[...], w_ref[:, :width])
    dn_ref[...] = mm(cot_ref[...], wo_ref[...])
    low_half = block_iota(1) < P_SIZE
    causal = block_iota(0) >= block_iota(1)

    def convolved(sub, block):
        cols = slice(block * LANES, (block + 1) * LANES)
        total = taps_ref[CONV : CONV + 1, cols]
        for k in range(CONV):
            first = 8 - (CONV - 1) + k + sub * T
            total = total + taps_ref[k : k + 1, cols] * halo[first : first + T, cols]
        rows = slice(sub * T, (sub + 1) * T)
        xc_ref[rows, cols] = total
        v_ref[rows, cols] = halo[8 + sub * T : 8 + (sub + 1) * T, cols].astype(bf16)
        return total * sigmoid(total)

    for sub in range(ROWS // T):
        rows = slice(sub * T, (sub + 1) * T)
        raw, dt, decay = head_rows(dr_ref, head_ref, rows)
        decay_t = decay.T
        b_low = convolved(sub, pairs).astype(bf16)
        c_low = convolved(sub, pairs + 1).astype(bf16)
        b_t = b_low.T
        scores = jnp.where(causal, mm(c_low, b_low, NT), 0.0)
        squares = jnp.zeros((T, LANES), f32)
        inner = jnp.zeros((T, LANES), f32)
        st_ref[sub] = state[...].astype(bf16)
        for p in range(pairs):
            cols = slice(p * LANES, (p + 1) * LANES)
            x = convolved(sub, p)
            l1, l2 = spread(decay[:, 2 * p : 2 * p + 1]), spread(decay[:, 2 * p + 1 : 2 * p + 2])
            both = jnp.where(low_half, l1, l2)
            dtb = jnp.where(
                low_half, spread(dt[:, 2 * p : 2 * p + 1]), spread(dt[:, 2 * p + 1 : 2 * p + 2])
            )
            u = x * dtb
            m1 = scores * jnp.exp(jnp.minimum(l1 - decay_t[2 * p : 2 * p + 1, :], 0.0))
            m2 = scores * jnp.exp(jnp.minimum(l2 - decay_t[2 * p + 1 : 2 * p + 2, :], 0.0))
            mixing = jnp.concatenate([m1.astype(bf16), m2.astype(bf16)], axis=1)
            parts = jnp.concatenate(
                [jnp.where(low_half, u, 0.0).astype(bf16), jnp.where(low_half, 0.0, u).astype(bf16)],
                axis=0,
            )
            last = both[T - 1 : T, :]
            entering = st_ref[sub, :, cols]
            y = mm(mixing, parts) + jnp.exp(both) * mm(c_low, entering) + chan_ref[1:2, cols] * x
            tail = (u * jnp.exp(last - both)).astype(bf16)
            state[:, cols] = jnp.exp(last) * state[:, cols] + mm(b_t, tail)
            y_ref[rows, cols] = y
            z = z_ref[rows, cols]
            gated = y * (z * sigmoid(z))
            squares = squares + gated * gated
            inner = inner + gated * chan_ref[0:1, cols] * dn_ref[rows, cols]
        ones = jnp.ones((8, LANES), f32)
        red_ref[0:8, rows] = mm_exact(ones, squares, NT)
        red_ref[8:16, rows] = mm_exact(ones, inner, NT)
    halo[0:8, :] = halo[ROWS : ROWS + 8, :]


def ssd_forward(xg, w_cat, cot, w_out, taps, head, chan):
    tokens = xg.shape[0]
    width = w_out.shape[1]
    wide = width + 2 * NS
    steps = tokens // ROWS
    subs = ROWS // T
    per_seq = LEN // ROWS
    assert per_seq == steps
    row = lambda n: pl.BlockSpec((ROWS, n), lambda i: (i, 0))
    whole = lambda a: pl.BlockSpec(a.shape, lambda i: (0,) * a.ndim, pipeline_mode=pl.Buffered(1))
    return pl.pallas_call(
        functools.partial(forward_body, width),
        grid=(steps,),
        in_specs=[row(D), whole(w_cat), row(D), whole(w_out), whole(taps), whole(head), whole(chan)],
        out_specs=[
            row(width), row(wide), row(wide), row(LANES), row(width), row(width),
            pl.BlockSpec((subs, NS, width), lambda i: (i, 0, 0)),
            pl.BlockSpec((16, ROWS), lambda i: (0, i)),
        ],
        out_shape=[
            jax.ShapeDtypeStruct((tokens, width), f32),
            jax.ShapeDtypeStruct((tokens, wide), bf16),
            jax.ShapeDtypeStruct((tokens, wide), f32),
            jax.ShapeDtypeStruct((tokens, LANES), f32),
            jax.ShapeDtypeStruct((tokens, width), f32),
            jax.ShapeDtypeStruct((tokens, width), f32),
            jax.ShapeDtypeStruct((tokens // T, NS, width), bf16),
            jax.ShapeDtypeStruct((16, tokens), f32),
        ],
        scratch_shapes=[pltpu.VMEM((ROWS + 8, wide), f32), pltpu.VMEM((NS, width), f32)],
        compiler_params=pltpu.CompilerParams(vmem_limit_bytes=56 * 2**20),
        name="layer_forward",
    )(xg, w_cat, cot, w_out, taps, head, chan)


def backward_body(
    width,
    z_ref, v_ref, xc_ref, dr_ref, y_ref, dn_ref, st_ref, red_ref, taps_ref, head_ref, chan_ref, pick_ref,
    nl_ref, d_ref, acc_ref, hacc_ref,
    dxh, dstate, yst, bds, dyeb, utb, gin, gout, xdu, turn,
):
    pairs = width // LANES
    wide = width + 2 * NS
    step = pl.program_id(0)

    @pl.when(step == 0)
    def _():
        dxh[T : T + 8, :] = jnp.zeros((8, wide), f32)
        dstate[...] = jnp.zeros_like(dstate)
        acc_ref[...] = jnp.zeros_like(acc_ref)
        hacc_ref[...] = jnp.zeros_like(hacc_ref)
        turn[...] = jnp.zeros_like(turn)

    low_half = block_iota(1) < P_SIZE
    row_at, col_at = block_iota(0), block_iota(1)
    until = row_at <= col_at
    before = row_at < col_at
    upper = jnp.where(until, 1.0, 0.0).astype(f32)
    strict = jnp.where(before, 1.0, 0.0).astype(f32)
    low_tri = jnp.where(row_at >= col_at, 1.0, 0.0).astype(bf16)

    def add(index, cols, value):
        acc_ref[index, :, cols] += jnp.sum(value.reshape(T // 8, 8, LANES), axis=0)

    def conv_back(rows, block, d_act, xc, s, act):
        cols = slice(block * LANES, (block + 1) * LANES)
        dxh[0:T, cols] = d_act * (s + act * (1.0 - s))
        v = v_ref[rows, cols].astype(f32)
        total = None
        for m in range(CONV):
            moved = dxh[m : m + T, cols]
            if m == 0:
                add(CONV, cols, moved)
            add(CONV - 1 - m, cols, v * moved)
            term = taps_ref[CONV - 1 - m : CONV - m, cols] * moved
            total = term if total is None else total + term
        d_ref[rows, width + block * LANES : width + (block + 1) * LANES] = total.astype(bf16)

    for sub in reversed(range(ROWS // T)):
        rows = slice(sub * T, (sub + 1) * T)
        raw, dt, decay = head_rows(dr_ref, head_ref, rows)
        decay_t = decay.T
        sums = red_ref[:, rows]
        q_row = lax.rsqrt(sums[0:8] / DI + norm_eps)
        k_row = q_row * q_row * q_row * sums[8:16] / DI
        q = spread(q_row.T[:, 0:1])
        kk = spread(k_row.T[:, 0:1])
        b_cols = slice(width, width + NS)
        c_cols = slice(width + NS, width + 2 * NS)
        b_xc, c_xc = xc_ref[rows, b_cols], xc_ref[rows, c_cols]
        b_s, c_s = sigmoid(b_xc), sigmoid(c_xc)
        b_act, c_act = b_xc * b_s, c_xc * c_s
        b_low, c_low = b_act.astype(bf16), c_act.astype(bf16)
        c_t = c_low.T
        scores_t = jnp.where(until, mm(b_low, c_low, NT), 0.0)
        ds_low = dstate[...].astype(bf16)
        yst[...] = mm(c_low, st_ref[sub])
        bds[...] = mm(b_low, ds_low)
        d_scores = jnp.zeros((T, LANES), f32)
        for p in range(pairs):
            cols = slice(p * LANES, (p + 1) * LANES)
            z, y, dn = z_ref[rows, cols], y_ref[rows, cols], dn_ref[rows, cols]
            gain = chan_ref[0:1, cols]
            s = sigmoid(z)
            sz = z * s
            gated = y * sz
            gq = gated * q
            dg = q * gain * dn - gated * kk
            add(CONV + 1, cols, gq * dn)
            nl_ref[rows, cols] = (gq * gain).astype(bf16)
            d_ref[rows, cols] = (dg * y * (s + sz * (1.0 - s))).astype(bf16)
            dy = dg * sz
            xc = xc_ref[rows, cols]
            xs = sigmoid(xc)
            x = xc * xs
            l1, l2 = spread(decay[:, 2 * p : 2 * p + 1]), spread(decay[:, 2 * p + 1 : 2 * p + 2])
            both = jnp.where(low_half, l1, l2)
            dtb = jnp.where(
                low_half, spread(dt[:, 2 * p : 2 * p + 1]), spread(dt[:, 2 * p + 1 : 2 * p + 2])
            )
            u = x * dtb
            last = both[T - 1 : T, :]
            e1 = jnp.exp(jnp.minimum(decay_t[2 * p : 2 * p + 1, :] - l1, 0.0))
            e2 = jnp.exp(jnp.minimum(decay_t[2 * p + 1 : 2 * p + 2, :] - l2, 0.0))
            dy_low = dy.astype(bf16)
            zero = jnp.zeros_like(dy_low)
            u_low = u.astype(bf16)
            du_in = mm(
                jnp.concatenate([(scores_t * e1).astype(bf16), (scores_t * e2).astype(bf16)], axis=1),
                jnp.concatenate(
                    [jnp.where(low_half, dy_low, zero), jnp.where(low_half, zero, dy_low)], axis=0
                ),
            )
            d_mix = mm(
                jnp.concatenate(
                    [jnp.where(low_half, u_low, zero), jnp.where(low_half, zero, u_low)], axis=0
                ),
                dy_low,
                NT,
            )
            d1, d2 = d_mix[:T] * e1, d_mix[T:] * e2
            d_scores = d_scores + d1 + d2
            reach = mm(
                jnp.concatenate([(d1 * scores_t).astype(bf16), (d2 * scores_t).astype(bf16)], axis=0),
                low_tri,
            )
            turn[2 * p : 2 * p + 1, :] = jnp.sum(jnp.where(before, reach[:T], 0.0), axis=0, keepdims=True)
            turn[2 * p + 1 : 2 * p + 2, :] = jnp.sum(
                jnp.where(before, reach[T:], 0.0), axis=0, keepdims=True
            )
            tail = jnp.exp(last - both)
            dye = dy * jnp.exp(both)
            du_out = tail * bds[:, cols]
            du = du_in + du_out
            gin[:, cols] = (dye * yst[:, cols]).astype(bf16)
            gout[:, cols] = (u * du_out).astype(bf16)
            xdu[:, cols] = (x * du).astype(bf16)
            dyeb[:, cols] = dye.astype(bf16)
            utb[:, cols] = (u * tail).astype(bf16)
            add(CONV + 2, cols, dy * x)
            conv_back(rows, p, dtb * du + chan_ref[1:2, cols] * dy, xc, xs, x)
        d_scores = jnp.where(until, d_scores, 0.0).astype(bf16)
        d_b = mm(d_scores, c_low) + mm(utb[...], ds_low, NT)
        d_c = mm(d_scores, b_low, TN) + mm(dyeb[...], st_ref[sub], NT)
        conv_back(rows, pairs, d_b, b_xc, b_s, b_act)
        conv_back(rows, pairs + 1, d_c, c_xc, c_s, c_act)
        ended = jnp.zeros((1, LANES), f32)
        for p in range(pairs):
            cols = slice(p * LANES, (p + 1) * LANES)
            last = jnp.where(
                low_half[0:1], decay[T - 1 : T, 2 * p : 2 * p + 1], decay[T - 1 : T, 2 * p + 1 : 2 * p + 2]
            )
            fade = jnp.exp(last)
            before_ds = dstate[:, cols]
            through = jnp.sum(before_ds * st_ref[sub, :, cols].astype(f32), axis=0, keepdims=True) * fade
            ended = ended + mm_exact(through, pick_ref[cols, :].astype(f32))
            dstate[:, cols] = fade * before_ds + mm(c_t, dyeb[:, cols])
        gin_heads = mm(gin[...], pick_ref[...])
        gout_heads = mm(gout[...], pick_ref[...])
        reached = (
            turn[...].T
            + mm_exact(upper, gin_heads)
            + mm_exact(strict, gout_heads, TN)
            + ended
        )
        d_raw = (head_ref[1:2, :] * reached + mm(xdu[...], pick_ref[...])) * sigmoid(raw)
        d_ref[rows, width + wide :] = d_raw.astype(bf16)
        hacc_ref[0] += jnp.sum(d_raw.reshape(T // 8, 8, LANES), axis=0)
        hacc_ref[1] += jnp.sum((dt * reached).reshape(T // 8, 8, LANES), axis=0)
        dxh[T : T + 8, :] = dxh[0:8, :]


def ssd_backward(z, v, xc, dr, y, dn, st, red, taps, head, chan, pick):
    tokens, width = z.shape
    wide = width + 2 * NS
    steps = tokens // ROWS
    subs = ROWS // T
    row = lambda n: pl.BlockSpec((ROWS, n), lambda i: (steps - 1 - i, 0))
    whole = lambda a: pl.BlockSpec(a.shape, lambda i: (0,) * a.ndim, pipeline_mode=pl.Buffered(1))
    total = width + wide + LANES
    vm = pltpu.VMEM
    return pl.pallas_call(
        functools.partial(backward_body, width),
        grid=(steps,),
        in_specs=[
            row(width), row(wide), row(wide), row(LANES), row(width), row(width),
            pl.BlockSpec((subs, NS, width), lambda i: (steps - 1 - i, 0, 0)),
            pl.BlockSpec((16, ROWS), lambda i: (0, steps - 1 - i)),
            whole(taps), whole(head), whole(chan), whole(pick),
        ],
        out_specs=[
            row(width), row(total),
            pl.BlockSpec((CONV + 3, 8, wide), lambda i: (0, 0, 0)),
            pl.BlockSpec((2, 8, LANES), lambda i: (0, 0, 0)),
        ],
        out_shape=[
            jax.ShapeDtypeStruct((tokens, width), bf16),
            jax.ShapeDtypeStruct((tokens, total), bf16),
            jax.ShapeDtypeStruct((CONV + 3, 8, wide), f32),
            jax.ShapeDtypeStruct((2, 8, LANES), f32),
        ],
        scratch_shapes=[
            vm((T + 8, wide), f32), vm((NS, width), f32), vm((T, width), f32), vm((T, width), f32),
            vm((T, width), bf16), vm((T, width), bf16), vm((T, width), bf16), vm((T, width), bf16),
            vm((T, width), bf16), vm((T, LANES), f32),
        ],
        compiler_params=pltpu.CompilerParams(vmem_limit_bytes=56 * 2**20),
        name="layer_backward",
    )(z, v, xc, dr, y, dn, st, red, taps, head, chan, pick)


def ring_place(n):
    me = lax.axis_index("dp")
    z, x = lax.div(me, 2), lax.rem(me, 2)
    return z + x * (n - 1 - 2 * z)


def ring_index(pos, n):
    back = lax.div(pos, n // 2)
    return 2 * pos + back * (2 * n - 1 - 4 * pos)


def neighbours(n):
    pos = ring_place(n)
    right = ring_index(lax.rem(pos + 1, n), n)
    left = ring_index(lax.rem(pos + n - 1, n), n)
    me = lax.axis_index("tensor")
    y, core = lax.div(me, 2), lax.rem(me, 2)
    across = 2 * (1 - y) + core
    beside = 2 * y + 1 - core
    return pos, ({"dp": right}, {"dp": left}), me, {"tensor": across}, {"tensor": beside}


def enter(peers):
    barrier = pltpu.get_barrier_semaphore()
    for peer in peers:
        pl.semaphore_signal(barrier, inc=1, device_id=peer, device_id_type=pl.DeviceIdType.MESH)
    pl.semaphore_wait(barrier, len(peers))


def remote(src, dst, send_sem, recv_sem, peer):
    return pltpu.make_async_remote_copy(
        src_ref=src, dst_ref=dst, send_sem=send_sem, recv_sem=recv_sem,
        device_id=peer, device_id_type=pl.DeviceIdType.MESH,
    )


def span(start, size):
    return pl.ds(pl.multiple_of(start, 16), size)


def cut_rows(rows):
    top = rows // 32 * 16
    return ((0, top), (top, rows - top))


def gather_body(
    n, rows, tokens,
    x_ref, cot_ref, w_ref, wo_ref, xg_ref, cots_ref, ws_ref, wos_ref,
    own_sem, ring_send, ring_recv, over_send, over_recv, side_send, side_recv, pass_send, pass_recv,
):
    pos, ring, me, across, beside = neighbours(n)
    enter((*ring, across, beside))
    half = tokens // 2
    started = []

    def go(*args):
        copy = remote(*args)
        copy.start()
        started.append(copy)

    sides = [(x_ref, xg_ref, 0), (x_ref, xg_ref, 1), (cot_ref, cots_ref, 0), (cot_ref, cots_ref, 1)]
    opposite = lax.rem(me + 2, 4)
    pieces = [(src, dst, part) for part in (0, 1) for src, dst in ((w_ref, ws_ref), (wo_ref, wos_ref))]
    cuts = cut_rows(rows)

    def ring_step(step):
        last = step == n // 2 - 1
        for k, (own, full, part) in enumerate(pieces):
            first, size = cuts[part]
            for way in (0, 1):
                block = ring_index(lax.rem(pos + (step if way else n - step), n), n)
                here = full.at[span(block * rows + first, size)]
                if step > 0:
                    remote(
                        here, here, ring_send.at[way, k, step - 1], ring_recv.at[way, k, step - 1], ring[way]
                    ).wait_recv()
                if last and part != way:
                    continue
                src = own.at[pl.ds(first, size)] if step == 0 else here
                go(src, here, ring_send.at[way, k, step], ring_recv.at[way, k, step], ring[way])

    def pass_on(k):
        _, full, part = sides[k]
        here = full.at[span(opposite * tokens + part * half, half)]
        remote(here, here, over_send.at[k], over_recv.at[k], across).wait_recv()
        go(here, here, pass_send.at[k], pass_recv.at[k], beside)

    for k, (own, full, part) in enumerate(sides):
        go(
            own.at[pl.ds(part * half, half)], full.at[span(me * tokens + part * half, half)],
            over_send.at[k], over_recv.at[k], across,
        )
    ring_step(0)
    for k, (own, full) in enumerate(((x_ref, xg_ref), (cot_ref, cots_ref))):
        go(own, full.at[span(me * tokens, tokens)], side_send.at[k], side_recv.at[k], beside)
    mine = ring_index(pos, n)
    locals_ = []
    for k, (own, dst) in enumerate(
        (
            (x_ref, xg_ref.at[span(me * tokens, tokens)]),
            (cot_ref, cots_ref.at[span(me * tokens, tokens)]),
            (w_ref, ws_ref.at[span(mine * rows, rows)]),
            (wo_ref, wos_ref.at[span(mine * rows, rows)]),
        )
    ):
        copy = pltpu.make_async_copy(own, dst, own_sem.at[k])
        copy.start()
        locals_.append(copy)
    passed = 0
    for step in range(1, n // 2):
        ring_step(step)
        if passed < len(sides) - 1:
            pass_on(passed)
            passed += 1
    while passed < len(sides):
        pass_on(passed)
        passed += 1
    step = n // 2
    for k, (own, full, part) in enumerate(pieces):
        first, size = cuts[part]
        block = ring_index(lax.rem(pos + n // 2, n), n)
        here = full.at[span(block * rows + first, size)]
        remote(
            here, here, ring_send.at[part, k, step - 1], ring_recv.at[part, k, step - 1], ring[part]
        ).wait_recv()
    other = lax.rem(me, 2)
    next_door = me + 1 - 2 * other
    far = lax.rem(next_door + 2, 4)
    for k, (own, full) in enumerate(((x_ref, xg_ref), (cot_ref, cots_ref))):
        here = full.at[span(next_door * tokens, tokens)]
        remote(here, here, side_send.at[k], side_recv.at[k], beside).wait_recv()
    for k, (own, full, part) in enumerate(sides):
        here = full.at[span(far * tokens + part * half, half)]
        remote(here, here, pass_send.at[k], pass_recv.at[k], beside).wait_recv()
    for copy in locals_:
        copy.wait()
    for copy in started:
        copy.wait_send()


def gather_all(n, x, cot, w, wo):
    tokens, rows = x.shape[0], w.shape[0]
    dma = pltpu.SemaphoreType.DMA
    anywhere = pl.BlockSpec(memory_space=pl.ANY)
    whole = lambda a, k: jax.ShapeDtypeStruct((a.shape[0] * k, a.shape[1]), a.dtype)
    return pl.pallas_call(
        functools.partial(gather_body, n, rows, tokens),
        in_specs=[anywhere] * 4,
        out_specs=[anywhere] * 4,
        out_shape=[whole(x, 4), whole(cot, 4), whole(w, n), whole(wo, n)],
        scratch_shapes=[
            dma((4,)), dma((2, 4, n // 2)), dma((2, 4, n // 2)), dma((4,)), dma((4,)),
            dma((2,)), dma((2,)), dma((4,)), dma((4,)),
        ],
        compiler_params=pltpu.CompilerParams(collective_id=0, has_side_effects=True),
        name="gather_all",
    )(x, cot, w, wo)


def reduce_body(
    n, rows, tokens, starts,
    gc_ref, go_ref, branch_ref, back_ref, small_ref,
    oc_ref, oo_ref, obranch_ref, oback_ref, bc_ref, osmall_ref,
    gc, go_, slots, held, near, over, smalls, tens, bc_slot,
    load_sem, ring_send, ring_recv, near_send, near_recv, over_send, over_recv,
    small_send, small_recv, ten_send, ten_recv, bc_send, bc_recv,
):
    pos, ring, me, across, beside = neighbours(n)
    enter((*ring, across, beside))
    cuts = cut_rows(rows)
    started = []

    def go(*args):
        copy = remote(*args)
        copy.start()
        started.append(copy)
        return copy

    core = lax.rem(me, 2)
    opposite = lax.rem(me + 2, 4)
    next_door = me + 1 - 2 * core
    far = lax.rem(next_door + 2, 4)
    half = tokens // 2
    items = [(gc_ref, gc, oc_ref, lo, hi) for lo, hi in starts] + [(go_ref, go_, oo_ref, 0, go_.shape[1])]

    def block_at(way, steps):
        return ring_index(lax.rem(pos + (steps if way else n - steps), n), n)

    for k, (src, _, _, lo, hi) in enumerate(items):
        for way in (0, 1):
            first, size = cuts[way]
            go(
                src.at[span(block_at(way, 1) * rows + first, size), pl.ds(lo, hi - lo)],
                slots[way][k].at[0],
                ring_send.at[way, k, 0], ring_recv.at[way, k, 0], ring[way],
            )
    sides = [(branch_ref, 0), (back_ref, 1)]
    for turn, target in ((0, far), (1, next_door)):
        for src, k in sides:
            for part in (0, 1):
                go(
                    src.at[span(target * tokens + part * half, half)],
                    near.at[k, turn, part],
                    near_send.at[k, turn, part], near_recv.at[k, turn, part], beside,
                )
    loads = {}
    for turn, target in ((0, opposite), (1, me)):
        for src, k in sides:
            for part in (0, 1):
                copy = pltpu.make_async_copy(
                    src.at[span(target * tokens + part * half, half)],
                    held.at[k, turn, part], load_sem.at[4 * turn + 2 * k + part],
                )
                copy.start()
                loads[k, turn, part] = copy
    for k, (src, dst) in enumerate(((gc_ref, gc), (go_ref, go_))):
        copy = pltpu.make_async_copy(src, dst, load_sem.at[8 + k])
        copy.start()
        loads["ring", k] = copy
    small_load = pltpu.make_async_copy(small_ref, smalls.at[pos], load_sem.at[10])
    small_load.start()

    def add_side(k, turn, part, dst):
        def some(i, _):
            at = span(i * 16, 16)
            total = held[k, turn, part, at, :].astype(f32) + near[k, turn, part, at, :].astype(f32)
            if dst is None:
                held[k, turn, part, at, :] = total.astype(bf16)
            else:
                dst[span(part * half + i * 16, 16), :] = total
            return 0

        lax.fori_loop(0, half // 16, some, 0)

    def near_ready(k, turn, part):
        loads[k, turn, part].wait()
        remote(
            near.at[k, turn, part], near.at[k, turn, part],
            near_send.at[k, turn, part], near_recv.at[k, turn, part], beside,
        ).wait_recv()

    for k in (0, 1):
        for part in (0, 1):
            near_ready(k, 0, part)
            add_side(k, 0, part, None)
            go(held.at[k, 0, part], over.at[k, part], over_send.at[k, part], over_recv.at[k, part], across)

    small_load.wait()
    loads["ring", 0].wait()
    loads["ring", 1].wait()
    outs = (obranch_ref, oback_ref)
    todo = [(k, part) for k in (0, 1) for part in (0, 1)]

    for step in range(n - 1):
        here = smalls.at[lax.rem(pos + n - step, n)]
        go(here, here, small_send.at[step], small_recv.at[step], ring[0])
        for k, (_, own, out, lo, hi) in enumerate(items):
            for way in (0, 1):
                first, size = cuts[way]
                slot = slots[way][k].at[step]
                remote(
                    slot, slot, ring_send.at[way, k, step], ring_recv.at[way, k, step], ring[way]
                ).wait_recv()
                block = block_at(way, 2 + step) if step < n - 2 else block_at(way, 0)

                def some(i, _, way=way, k=k, step=step, own=own, out=out, lo=lo, hi=hi, first=first, block=block):
                    total = slots[way][k][step, span(i * 16, 16), :].astype(f32)
                    total = total + own[span(block * rows + first + i * 16, 16), lo:hi].astype(f32)
                    if step < n - 2:
                        slots[way][k][step, span(i * 16, 16), :] = total.astype(bf16)
                    else:
                        out[span(first + i * 16, 16), lo:hi] = total
                    return 0

                lax.fori_loop(0, size // 16, some, 0)
                if step < n - 2:
                    go(
                        slot, slots[way][k].at[step + 1],
                        ring_send.at[way, k, step + 1], ring_recv.at[way, k, step + 1], ring[way],
                    )
            if step == n - 2 and k == 0:
                bc_slot[0] = oc_ref[:, starts[0][0] : starts[0][0] + 2 * NS]
                go(bc_slot.at[0], bc_slot.at[1], bc_send.at[0], bc_recv.at[0], beside)
        here = smalls.at[lax.rem(pos + 2 * n - step - 1, n)]
        remote(here, here, small_send.at[step], small_recv.at[step], ring[0]).wait_recv()
        if todo and step >= 1:
            k, part = todo.pop(0)
            near_ready(k, 1, part)
            add_side(k, 1, part, outs[k])
    for k, part in todo:
        near_ready(k, 1, part)
        add_side(k, 1, part, outs[k])

    total = smalls[0]
    for i in range(1, n):
        total = total + smalls[i]
    tens[me] = total
    go(tens.at[me], tens.at[me], ten_send.at[0], ten_recv.at[0], beside)
    remote(bc_slot.at[1], bc_slot.at[1], bc_send.at[0], bc_recv.at[0], beside).wait_recv()
    bc_slot[2] = bc_slot[0] + bc_slot[1]
    go(bc_slot.at[2], bc_slot.at[3], bc_send.at[1], bc_recv.at[1], across)
    here = tens.at[next_door]
    remote(here, here, ten_send.at[0], ten_recv.at[0], beside).wait_recv()
    for k, target in ((0, me), (1, next_door)):
        here = tens.at[target]
        go(here, here, ten_send.at[1 + k], ten_recv.at[1 + k], across)
    for k in (0, 1):
        for part in (0, 1):
            slot = over.at[k, part]
            remote(slot, slot, over_send.at[k, part], over_recv.at[k, part], across).wait_recv()

            def some(i, _, k=k, part=part):
                at = span(part * half + i * 16, 16)
                outs[k][at, :] = outs[k][at, :] + over[k, part, span(i * 16, 16), :].astype(f32)
                return 0

            lax.fori_loop(0, half // 16, some, 0)
    for k, target in ((0, opposite), (1, far)):
        here = tens.at[target]
        remote(here, here, ten_send.at[1 + k], ten_recv.at[1 + k], across).wait_recv()
    osmall_ref[...] = tens[...]
    remote(bc_slot.at[3], bc_slot.at[3], bc_send.at[1], bc_recv.at[1], across).wait_recv()
    bc_ref[...] = bc_slot[2] + bc_slot[3]
    for copy in started:
        copy.wait_send()


def reduce_all(n, grad_cat, grad_out, branch, back, small):
    rows, tokens = grad_cat.shape[0] // n, branch.shape[0] // 4
    wide, width = grad_cat.shape[1], grad_out.shape[1]
    starts = ((2 * width, wide), (0, 2 * width))
    widths = [hi - lo for lo, hi in starts] + [width]
    sizes = [size for _, size in cut_rows(rows)]
    half = tokens // 2
    dma, vm = pltpu.SemaphoreType.DMA, pltpu.VMEM
    anywhere = pl.BlockSpec(memory_space=pl.ANY)
    inside = pl.BlockSpec(memory_space=pltpu.VMEM)
    return pl.pallas_call(
        functools.partial(reduce_body, n, rows, tokens, starts),
        in_specs=[anywhere] * 5,
        out_specs=[inside] * 6,
        out_shape=[
            jax.ShapeDtypeStruct((rows, wide), f32),
            jax.ShapeDtypeStruct((rows, width), f32),
            jax.ShapeDtypeStruct((tokens, D), f32),
            jax.ShapeDtypeStruct((tokens, D), f32),
            jax.ShapeDtypeStruct((rows, 2 * NS), f32),
            jax.ShapeDtypeStruct((4, *small.shape), f32),
        ],
        scratch_shapes=[
            vm(grad_cat.shape, bf16), vm(grad_out.shape, bf16),
            [[vm((n - 1, size, w), bf16) for w in widths] for size in sizes],
            vm((2, 2, 2, half, D), bf16), vm((2, 2, 2, half, D), bf16), vm((2, 2, half, D), bf16),
            vm((n, *small.shape), f32), vm((4, *small.shape), f32), vm((4, rows, 2 * NS), f32),
            dma((11,)), dma((2, 3, n - 1)), dma((2, 3, n - 1)), dma((2, 2, 2)), dma((2, 2, 2)),
            dma((2, 2)), dma((2, 2)), dma((n - 1,)), dma((n - 1,)), dma((3,)), dma((3,)), dma((2,)), dma((2,)),
        ],
        compiler_params=pltpu.CompilerParams(
            collective_id=1, has_side_effects=True, vmem_limit_bytes=60 * 2**20
        ),
        name="reduce_all",
    )(grad_cat, grad_out, branch, back, small)


def adamw_step(weight, first, second, grad, rate, decay):
    first_new = beta_first * first + (1.0 - beta_first) * grad
    second_new = beta_second * second + (1.0 - beta_second) * grad * grad
    hat_first = first_new / (1.0 - beta_first**STEP)
    hat_second = second_new / (1.0 - beta_second**STEP)
    weight_new = weight - rate * (hat_first / (jnp.sqrt(hat_second) + adam_eps) + decay * weight)
    return (weight_new, first_new, second_new)


def local(
    layer_input,
    out_grad,
    small_params,
    small_first,
    small_second,
    w_zx,
    zx_first,
    zx_second,
    w_bc,
    bc_first,
    bc_second,
    w_dt,
    dt_first,
    dt_second,
    w_out,
    out_first,
    out_second,
):
    tensor_index = lax.axis_index("tensor")
    local_in = layer_input.astype(f32)
    gain_in, gate_gain, conv_x, bias_x, conv_bc, bias_bc, dt_bias, a_log, d_skip = unpack(
        small_params
    )
    rows_own = w_zx.shape[0]
    width = w_zx.shape[2]
    heads = w_dt.shape[1]
    chan_start = tensor_index * width
    head_start = tensor_index * heads
    gate_local = lax.dynamic_slice_in_dim(gate_gain, chan_start, width, 0)
    conv_local = lax.dynamic_slice_in_dim(conv_x, chan_start, width, 1)
    bias_local = lax.dynamic_slice_in_dim(bias_x, chan_start, width, 0)
    dtb_local = lax.dynamic_slice_in_dim(dt_bias, head_start, heads, 0)
    a_local = -jnp.exp(lax.dynamic_slice_in_dim(a_log, head_start, heads, 0))
    dskip_local = lax.dynamic_slice_in_dim(d_skip, head_start, heads, 0)
    taps = jnp.concatenate(
        [
            jnp.concatenate([conv_local, conv_bc], axis=1),
            jnp.concatenate([bias_local, bias_bc])[None, :],
            jnp.zeros((8 - CONV - 1, width + 2 * NS), f32),
        ],
        axis=0,
    )
    lanes = lambda v: jnp.pad(v, (0, LANES - heads))
    head = jnp.pad(jnp.stack([lanes(dtb_local), lanes(a_local)]), ((0, 6), (0, 0)))
    chan = jnp.pad(jnp.stack([gate_local, jnp.repeat(dskip_local, P_SIZE)]), ((0, 6), (0, 0)))
    pick = jnp.asarray(
        (jnp.arange(width)[:, None] // P_SIZE == jnp.arange(LANES)[None, :]), bf16
    )

    inv_in = lax.rsqrt(jnp.mean(local_in * local_in, axis=-1, keepdims=True) + norm_eps)
    normed_in = local_in * inv_in * gain_in[None, :]
    w_cat = jnp.concatenate(
        [
            w_zx.reshape(rows_own, 2 * width).astype(bf16),
            w_bc.astype(bf16),
            jnp.pad(w_dt, ((0, 0), (0, LANES - heads))).astype(bf16),
        ],
        axis=1,
    )
    n = lax.axis_size("dp")
    xg, cot_all, w_all, wo_all = gather_all(
        n, normed_in.astype(bf16), out_grad, w_cat, w_out.astype(bf16)
    )

    z, v, xc, dr, y, dn, st, red = ssd_forward(xg, w_all, cot_all, wo_all, taps, head, chan)
    sums = lax.psum(red[::8], "tensor")
    red = jnp.repeat(sums, 8, axis=0)
    normed_low, d_cat, acc, hacc = ssd_backward(z, v, xc, dr, y, dn, st, red, taps, head, chan, pick)

    branch = mm(normed_low, wo_all, NT).astype(bf16)
    grad_out = mm(cot_all, normed_low, TN).astype(bf16)
    back = mm(d_cat, w_all, NT)
    gain_part = jnp.sum(xg.astype(f32) * back, axis=0) / gain_in
    grad_cat = mm(xg, d_cat, TN).astype(bf16)
    acc = jnp.sum(acc, axis=1)
    hacc = jnp.sum(hacc, axis=1)
    skip_part = jnp.sum(acc[CONV + 2, :width].reshape(heads, P_SIZE), axis=1)
    small = jnp.concatenate(
        [
            acc[: CONV + 1].reshape(-1), acc[CONV + 1, :width], hacc[0], hacc[1],
            gain_part, jnp.pad(skip_part, (0, 4 * LANES - heads)),
        ]
    ).reshape(8, width + 2 * NS)
    owner_cat, owner_out, own_branch, d_normed_in, owner_bc, tens = reduce_all(
        n, grad_cat, grad_out, branch, back.astype(bf16), small
    )
    layer_output = (local_in + own_branch).astype(bf16)
    owner_zx = owner_cat[:, : 2 * width].reshape(rows_own, 2, width)
    owner_dt = owner_cat[:, 2 * width + 2 * NS : 2 * width + 2 * NS + heads]

    inner_in = jnp.sum(local_in * gain_in[None, :] * d_normed_in, axis=-1, keepdims=True)
    input_grad = (
        out_grad.astype(f32)
        + inv_in * gain_in[None, :] * d_normed_in
        - local_in * (inv_in * inv_in * inv_in * inner_in / D)
    )
    gain_sum = jnp.sum(tens[:, 6:8], axis=0).reshape(-1)[:D]
    bc_sum = jnp.sum(tens[:, : CONV + 1, width:], axis=0)
    small_grad = jnp.concatenate(
        [
            gain_sum,
            tens[:, CONV + 1, :width].reshape(-1),
            jnp.moveaxis(tens[:, :CONV, :width], 0, 1).reshape(-1),
            tens[:, CONV, :width].reshape(-1),
            bc_sum.reshape(-1),
            tens[:, CONV + 1, width : width + heads].reshape(-1),
            tens[:, CONV + 1, width + LANES : width + LANES + heads].reshape(-1) * -jnp.exp(a_log),
            tens[:, 7, 512 : 512 + heads].reshape(-1),
        ]
    )
    small_new, small_first_new, small_second_new = adamw_step(
        small_params, small_first, small_second, small_grad, small_rate, 0.0
    )
    zx_new, zx_first_new, zx_second_new = adamw_step(
        w_zx, zx_first, zx_second, owner_zx, matrix_rate, matrix_decay
    )
    bc_new, bc_first_new, bc_second_new = adamw_step(
        w_bc, bc_first, bc_second, owner_bc, matrix_rate, matrix_decay
    )
    dt_new, dt_first_new, dt_second_new = adamw_step(
        w_dt, dt_first, dt_second, owner_dt, matrix_rate, matrix_decay
    )
    out_new, out_first_new, out_second_new = adamw_step(
        w_out, out_first, out_second, owner_out, matrix_rate, matrix_decay
    )
    return (
        layer_output,
        input_grad,
        small_new,
        small_first_new,
        small_second_new,
        zx_new,
        zx_first_new,
        zx_second_new,
        bc_new,
        bc_first_new,
        bc_second_new,
        dt_new,
        dt_first_new,
        dt_second_new,
        out_new,
        out_first_new,
        out_second_new,
    )


def solution(mesh):
    return jax.shard_map(
        local,
        mesh=mesh,
        in_specs=(
            P(("dp", "tensor"), None),
            P(("dp", "tensor"), None),
            P(),
            P(),
            P(),
            P("dp", None, "tensor"),
            P("dp", None, "tensor"),
            P("dp", None, "tensor"),
            P("dp", None),
            P("dp", None),
            P("dp", None),
            P("dp", "tensor"),
            P("dp", "tensor"),
            P("dp", "tensor"),
            P("dp", "tensor"),
            P("dp", "tensor"),
            P("dp", "tensor"),
        ),
        out_specs=(
            P(("dp", "tensor"), None),
            P(("dp", "tensor"), None),
            P(),
            P(),
            P(),
            P("dp", None, "tensor"),
            P("dp", None, "tensor"),
            P("dp", None, "tensor"),
            P("dp", None),
            P("dp", None),
            P("dp", None),
            P("dp", "tensor"),
            P("dp", "tensor"),
            P("dp", "tensor"),
            P("dp", "tensor"),
            P("dp", "tensor"),
            P("dp", "tensor"),
        ),
        check_vma=False,
    )
```

```python
import functools

import jax
import jax.numpy as jnp
from jax import lax
from jax.experimental import pallas as pl
from jax.experimental.pallas import tpu as pltpu
from jax.sharding import PartitionSpec as P

D = 1536
DI = 3072
H = 48
NS = 128
P_SIZE = 64
CONV = 4
LEN = 2048
STEP = 10

T = 128
ROWS = 256
LANES = 128

norm_eps = 1e-05
adam_eps = 1e-08
beta_first = 0.9
beta_second = 0.95
matrix_rate = 0.01
small_rate = 0.1
matrix_decay = 0.1

f32 = jnp.float32
bf16 = jnp.bfloat16
NN = (((1,), (0,)), ((), ()))
NT = (((1,), (1,)), ((), ()))
TN = (((0,), (0,)), ((), ()))
HIGHEST = lax.Precision.HIGHEST


def unpack(flat):
    gain_in = flat[:D]
    cursor = D
    gate_gain = flat[cursor : cursor + DI]
    cursor = cursor + DI
    conv_x = flat[cursor : cursor + CONV * DI].reshape(CONV, DI)
    cursor = cursor + CONV * DI
    bias_x = flat[cursor : cursor + DI]
    cursor = cursor + DI
    conv_bc = flat[cursor : cursor + CONV * 2 * NS].reshape(CONV, 2 * NS)
    cursor = cursor + CONV * 2 * NS
    bias_bc = flat[cursor : cursor + 2 * NS]
    cursor = cursor + 2 * NS
    dt_bias = flat[cursor : cursor + H]
    a_log = flat[cursor + H : cursor + 2 * H]
    d_skip = flat[cursor + 2 * H : cursor + 3 * H]
    return (gain_in, gate_gain, conv_x, bias_x, conv_bc, bias_bc, dt_bias, a_log, d_skip)


def mm(a, b, dims=NN):
    return lax.dot_general(a, b, dims, preferred_element_type=f32)


def mm_exact(a, b, dims=NN):
    return lax.dot_general(a, b, dims, preferred_element_type=f32, precision=HIGHEST)


def sigmoid(v):
    return 0.5 * jnp.tanh(0.5 * v) + 0.5


def softplus(v):
    return jnp.maximum(v, 0.0) + jnp.log1p(jnp.exp(-jnp.abs(v)))


def spread(col):
    return jnp.broadcast_to(col, (T, LANES))


def block_iota(axis):
    return lax.broadcasted_iota(jnp.int32, (T, LANES), axis)


def head_rows(dr_ref, head_ref, rows):
    raw = dr_ref[rows, :] + head_ref[0:1, :]
    dt = softplus(raw)
    low_tri = jnp.where(block_iota(0) >= block_iota(1), 1.0, 0.0).astype(f32)
    decay = mm_exact(low_tri, dt * head_ref[1:2, :])
    return raw, dt, decay


def forward_body(
    width,
    xg_ref, w_ref, cot_ref, wo_ref, taps_ref, head_ref, chan_ref,
    z_ref, v_ref, xc_ref, dr_ref, y_ref, dn_ref, st_ref, red_ref,
    halo, state,
):
    pairs = width // LANES
    step = pl.program_id(0)

    @pl.when(step == 0)
    def _():
        halo[0:8, :] = jnp.zeros((8, halo.shape[1]), f32)
        state[...] = jnp.zeros_like(state)

    wide = width + 2 * NS
    dr_ref[...] = mm(xg_ref[...], w_ref[:, width + wide :])
    halo[8 : 8 + ROWS, :] = mm(xg_ref[...], w_ref[:, width : width + wide])
    z_ref[...] = mm(xg_ref[...], w_ref[:, :width])
    dn_ref[...] = mm(cot_ref[...], wo_ref[...])
    low_half = block_iota(1) < P_SIZE
    causal = block_iota(0) >= block_iota(1)

    def convolved(sub, block):
        cols = slice(block * LANES, (block + 1) * LANES)
        total = taps_ref[CONV : CONV + 1, cols]
        for k in range(CONV):
            first = 8 - (CONV - 1) + k + sub * T
            total = total + taps_ref[k : k + 1, cols] * halo[first : first + T, cols]
        rows = slice(sub * T, (sub + 1) * T)
        xc_ref[rows, cols] = total
        v_ref[rows, cols] = halo[8 + sub * T : 8 + (sub + 1) * T, cols].astype(bf16)
        return total * sigmoid(total)

    for sub in range(ROWS // T):
        rows = slice(sub * T, (sub + 1) * T)
        raw, dt, decay = head_rows(dr_ref, head_ref, rows)
        decay_t = decay.T
        b_low = convolved(sub, pairs).astype(bf16)
        c_low = convolved(sub, pairs + 1).astype(bf16)
        b_t = b_low.T
        scores = jnp.where(causal, mm(c_low, b_low, NT), 0.0)
        squares = jnp.zeros((T, LANES), f32)
        inner = jnp.zeros((T, LANES), f32)
        st_ref[sub] = state[...].astype(bf16)
        for p in range(pairs):
            cols = slice(p * LANES, (p + 1) * LANES)
            x = convolved(sub, p)
            l1, l2 = spread(decay[:, 2 * p : 2 * p + 1]), spread(decay[:, 2 * p + 1 : 2 * p + 2])
            both = jnp.where(low_half, l1, l2)
            dtb = jnp.where(
                low_half, spread(dt[:, 2 * p : 2 * p + 1]), spread(dt[:, 2 * p + 1 : 2 * p + 2])
            )
            u = x * dtb
            m1 = scores * jnp.exp(jnp.minimum(l1 - decay_t[2 * p : 2 * p + 1, :], 0.0))
            m2 = scores * jnp.exp(jnp.minimum(l2 - decay_t[2 * p + 1 : 2 * p + 2, :], 0.0))
            mixing = jnp.concatenate([m1.astype(bf16), m2.astype(bf16)], axis=1)
            parts = jnp.concatenate(
                [jnp.where(low_half, u, 0.0).astype(bf16), jnp.where(low_half, 0.0, u).astype(bf16)],
                axis=0,
            )
            last = both[T - 1 : T, :]
            entering = st_ref[sub, :, cols]
            y = mm(mixing, parts) + jnp.exp(both) * mm(c_low, entering) + chan_ref[1:2, cols] * x
            tail = (u * jnp.exp(last - both)).astype(bf16)
            state[:, cols] = jnp.exp(last) * state[:, cols] + mm(b_t, tail)
            y_ref[rows, cols] = y
            z = z_ref[rows, cols]
            gated = y * (z * sigmoid(z))
            squares = squares + gated * gated
            inner = inner + gated * chan_ref[0:1, cols] * dn_ref[rows, cols]
        ones = jnp.ones((8, LANES), f32)
        red_ref[0:8, rows] = mm_exact(ones, squares, NT)
        red_ref[8:16, rows] = mm_exact(ones, inner, NT)
    halo[0:8, :] = halo[ROWS : ROWS + 8, :]


def ssd_forward(xg, w_cat, cot, w_out, taps, head, chan):
    tokens = xg.shape[0]
    width = w_out.shape[1]
    wide = width + 2 * NS
    steps = tokens // ROWS
    subs = ROWS // T
    per_seq = LEN // ROWS
    assert per_seq == steps
    row = lambda n: pl.BlockSpec((ROWS, n), lambda i: (i, 0))
    whole = lambda a: pl.BlockSpec(a.shape, lambda i: (0,) * a.ndim, pipeline_mode=pl.Buffered(1))
    return pl.pallas_call(
        functools.partial(forward_body, width),
        grid=(steps,),
        in_specs=[row(D), whole(w_cat), row(D), whole(w_out), whole(taps), whole(head), whole(chan)],
        out_specs=[
            row(width), row(wide), row(wide), row(LANES), row(width), row(width),
            pl.BlockSpec((subs, NS, width), lambda i: (i, 0, 0)),
            pl.BlockSpec((16, ROWS), lambda i: (0, i)),
        ],
        out_shape=[
            jax.ShapeDtypeStruct((tokens, width), f32),
            jax.ShapeDtypeStruct((tokens, wide), bf16),
            jax.ShapeDtypeStruct((tokens, wide), f32),
            jax.ShapeDtypeStruct((tokens, LANES), f32),
            jax.ShapeDtypeStruct((tokens, width), f32),
            jax.ShapeDtypeStruct((tokens, width), f32),
            jax.ShapeDtypeStruct((tokens // T, NS, width), bf16),
            jax.ShapeDtypeStruct((16, tokens), f32),
        ],
        scratch_shapes=[pltpu.VMEM((ROWS + 8, wide), f32), pltpu.VMEM((NS, width), f32)],
        compiler_params=pltpu.CompilerParams(vmem_limit_bytes=56 * 2**20),
        name="layer_forward",
    )(xg, w_cat, cot, w_out, taps, head, chan)


def backward_body(
    width,
    z_ref, v_ref, xc_ref, dr_ref, y_ref, dn_ref, st_ref, red_ref, taps_ref, head_ref, chan_ref, pick_ref,
    nl_ref, d_ref, acc_ref, hacc_ref,
    dxh, dstate, yst, bds, dyeb, utb, gin, gout, xdu, turn,
):
    pairs = width // LANES
    wide = width + 2 * NS
    step = pl.program_id(0)

    @pl.when(step == 0)
    def _():
        dxh[T : T + 8, :] = jnp.zeros((8, wide), f32)
        dstate[...] = jnp.zeros_like(dstate)
        acc_ref[...] = jnp.zeros_like(acc_ref)
        hacc_ref[...] = jnp.zeros_like(hacc_ref)
        turn[...] = jnp.zeros_like(turn)

    low_half = block_iota(1) < P_SIZE
    row_at, col_at = block_iota(0), block_iota(1)
    until = row_at <= col_at
    before = row_at < col_at
    upper = jnp.where(until, 1.0, 0.0).astype(f32)
    strict = jnp.where(before, 1.0, 0.0).astype(f32)
    low_tri = jnp.where(row_at >= col_at, 1.0, 0.0).astype(bf16)

    def add(index, cols, value):
        acc_ref[index, :, cols] += jnp.sum(value.reshape(T // 8, 8, LANES), axis=0)

    def conv_back(rows, block, d_act, xc, s, act):
        cols = slice(block * LANES, (block + 1) * LANES)
        dxh[0:T, cols] = d_act * (s + act * (1.0 - s))
        v = v_ref[rows, cols].astype(f32)
        total = None
        for m in range(CONV):
            moved = dxh[m : m + T, cols]
            if m == 0:
                add(CONV, cols, moved)
            add(CONV - 1 - m, cols, v * moved)
            term = taps_ref[CONV - 1 - m : CONV - m, cols] * moved
            total = term if total is None else total + term
        d_ref[rows, width + block * LANES : width + (block + 1) * LANES] = total.astype(bf16)

    for sub in reversed(range(ROWS // T)):
        rows = slice(sub * T, (sub + 1) * T)
        raw, dt, decay = head_rows(dr_ref, head_ref, rows)
        decay_t = decay.T
        sums = red_ref[:, rows]
        q_row = lax.rsqrt(sums[0:8] / DI + norm_eps)
        k_row = q_row * q_row * q_row * sums[8:16] / DI
        q = spread(q_row.T[:, 0:1])
        kk = spread(k_row.T[:, 0:1])
        b_cols = slice(width, width + NS)
        c_cols = slice(width + NS, width + 2 * NS)
        b_xc, c_xc = xc_ref[rows, b_cols], xc_ref[rows, c_cols]
        b_s, c_s = sigmoid(b_xc), sigmoid(c_xc)
        b_act, c_act = b_xc * b_s, c_xc * c_s
        b_low, c_low = b_act.astype(bf16), c_act.astype(bf16)
        c_t = c_low.T
        scores_t = jnp.where(until, mm(b_low, c_low, NT), 0.0)
        ds_low = dstate[...].astype(bf16)
        yst[...] = mm(c_low, st_ref[sub])
        bds[...] = mm(b_low, ds_low)
        d_scores = jnp.zeros((T, LANES), f32)
        for p in range(pairs):
            cols = slice(p * LANES, (p + 1) * LANES)
            z, y, dn = z_ref[rows, cols], y_ref[rows, cols], dn_ref[rows, cols]
            gain = chan_ref[0:1, cols]
            s = sigmoid(z)
            sz = z * s
            gated = y * sz
            gq = gated * q
            dg = q * gain * dn - gated * kk
            add(CONV + 1, cols, gq * dn)
            nl_ref[rows, cols] = (gq * gain).astype(bf16)
            d_ref[rows, cols] = (dg * y * (s + sz * (1.0 - s))).astype(bf16)
            dy = dg * sz
            xc = xc_ref[rows, cols]
            xs = sigmoid(xc)
            x = xc * xs
            l1, l2 = spread(decay[:, 2 * p : 2 * p + 1]), spread(decay[:, 2 * p + 1 : 2 * p + 2])
            both = jnp.where(low_half, l1, l2)
            dtb = jnp.where(
                low_half, spread(dt[:, 2 * p : 2 * p + 1]), spread(dt[:, 2 * p + 1 : 2 * p + 2])
            )
            u = x * dtb
            last = both[T - 1 : T, :]
            e1 = jnp.exp(jnp.minimum(decay_t[2 * p : 2 * p + 1, :] - l1, 0.0))
            e2 = jnp.exp(jnp.minimum(decay_t[2 * p + 1 : 2 * p + 2, :] - l2, 0.0))
            dy_low = dy.astype(bf16)
            zero = jnp.zeros_like(dy_low)
            u_low = u.astype(bf16)
            du_in = mm(
                jnp.concatenate([(scores_t * e1).astype(bf16), (scores_t * e2).astype(bf16)], axis=1),
                jnp.concatenate(
                    [jnp.where(low_half, dy_low, zero), jnp.where(low_half, zero, dy_low)], axis=0
                ),
            )
            d_mix = mm(
                jnp.concatenate(
                    [jnp.where(low_half, u_low, zero), jnp.where(low_half, zero, u_low)], axis=0
                ),
                dy_low,
                NT,
            )
            d1, d2 = d_mix[:T] * e1, d_mix[T:] * e2
            d_scores = d_scores + d1 + d2
            reach = mm(
                jnp.concatenate([(d1 * scores_t).astype(bf16), (d2 * scores_t).astype(bf16)], axis=0),
                low_tri,
            )
            turn[2 * p : 2 * p + 1, :] = jnp.sum(jnp.where(before, reach[:T], 0.0), axis=0, keepdims=True)
            turn[2 * p + 1 : 2 * p + 2, :] = jnp.sum(
                jnp.where(before, reach[T:], 0.0), axis=0, keepdims=True
            )
            tail = jnp.exp(last - both)
            dye = dy * jnp.exp(both)
            du_out = tail * bds[:, cols]
            du = du_in + du_out
            gin[:, cols] = (dye * yst[:, cols]).astype(bf16)
            gout[:, cols] = (u * du_out).astype(bf16)
            xdu[:, cols] = (x * du).astype(bf16)
            dyeb[:, cols] = dye.astype(bf16)
            utb[:, cols] = (u * tail).astype(bf16)
            add(CONV + 2, cols, dy * x)
            conv_back(rows, p, dtb * du + chan_ref[1:2, cols] * dy, xc, xs, x)
        d_scores = jnp.where(until, d_scores, 0.0).astype(bf16)
        d_b = mm(d_scores, c_low) + mm(utb[...], ds_low, NT)
        d_c = mm(d_scores, b_low, TN) + mm(dyeb[...], st_ref[sub], NT)
        conv_back(rows, pairs, d_b, b_xc, b_s, b_act)
        conv_back(rows, pairs + 1, d_c, c_xc, c_s, c_act)
        ended = jnp.zeros((1, LANES), f32)
        for p in range(pairs):
            cols = slice(p * LANES, (p + 1) * LANES)
            last = jnp.where(
                low_half[0:1], decay[T - 1 : T, 2 * p : 2 * p + 1], decay[T - 1 : T, 2 * p + 1 : 2 * p + 2]
            )
            fade = jnp.exp(last)
            before_ds = dstate[:, cols]
            through = jnp.sum(before_ds * st_ref[sub, :, cols].astype(f32), axis=0, keepdims=True) * fade
            ended = ended + mm_exact(through, pick_ref[cols, :].astype(f32))
            dstate[:, cols] = fade * before_ds + mm(c_t, dyeb[:, cols])
        gin_heads = mm(gin[...], pick_ref[...])
        gout_heads = mm(gout[...], pick_ref[...])
        reached = (
            turn[...].T
            + mm_exact(upper, gin_heads)
            + mm_exact(strict, gout_heads, TN)
            + ended
        )
        d_raw = (head_ref[1:2, :] * reached + mm(xdu[...], pick_ref[...])) * sigmoid(raw)
        d_ref[rows, width + wide :] = d_raw.astype(bf16)
        hacc_ref[0] += jnp.sum(d_raw.reshape(T // 8, 8, LANES), axis=0)
        hacc_ref[1] += jnp.sum((dt * reached).reshape(T // 8, 8, LANES), axis=0)
        dxh[T : T + 8, :] = dxh[0:8, :]


def ssd_backward(z, v, xc, dr, y, dn, st, red, taps, head, chan, pick):
    tokens, width = z.shape
    wide = width + 2 * NS
    steps = tokens // ROWS
    subs = ROWS // T
    row = lambda n: pl.BlockSpec((ROWS, n), lambda i: (steps - 1 - i, 0))
    whole = lambda a: pl.BlockSpec(a.shape, lambda i: (0,) * a.ndim, pipeline_mode=pl.Buffered(1))
    total = width + wide + LANES
    vm = pltpu.VMEM
    return pl.pallas_call(
        functools.partial(backward_body, width),
        grid=(steps,),
        in_specs=[
            row(width), row(wide), row(wide), row(LANES), row(width), row(width),
            pl.BlockSpec((subs, NS, width), lambda i: (steps - 1 - i, 0, 0)),
            pl.BlockSpec((16, ROWS), lambda i: (0, steps - 1 - i)),
            whole(taps), whole(head), whole(chan), whole(pick),
        ],
        out_specs=[
            row(width), row(total),
            pl.BlockSpec((CONV + 3, 8, wide), lambda i: (0, 0, 0)),
            pl.BlockSpec((2, 8, LANES), lambda i: (0, 0, 0)),
        ],
        out_shape=[
            jax.ShapeDtypeStruct((tokens, width), bf16),
            jax.ShapeDtypeStruct((tokens, total), bf16),
            jax.ShapeDtypeStruct((CONV + 3, 8, wide), f32),
            jax.ShapeDtypeStruct((2, 8, LANES), f32),
        ],
        scratch_shapes=[
            vm((T + 8, wide), f32), vm((NS, width), f32), vm((T, width), f32), vm((T, width), f32),
            vm((T, width), bf16), vm((T, width), bf16), vm((T, width), bf16), vm((T, width), bf16),
            vm((T, width), bf16), vm((T, LANES), f32),
        ],
        compiler_params=pltpu.CompilerParams(vmem_limit_bytes=56 * 2**20),
        name="layer_backward",
    )(z, v, xc, dr, y, dn, st, red, taps, head, chan, pick)


def ring_place(n):
    me = lax.axis_index("dp")
    z, x = lax.div(me, 2), lax.rem(me, 2)
    return z + x * (n - 1 - 2 * z)


def ring_index(pos, n):
    back = lax.div(pos, n // 2)
    return 2 * pos + back * (2 * n - 1 - 4 * pos)


def neighbours(n):
    pos = ring_place(n)
    right = ring_index(lax.rem(pos + 1, n), n)
    left = ring_index(lax.rem(pos + n - 1, n), n)
    me = lax.axis_index("tensor")
    y, core = lax.div(me, 2), lax.rem(me, 2)
    across = 2 * (1 - y) + core
    beside = 2 * y + 1 - core
    return pos, ({"dp": right}, {"dp": left}), me, {"tensor": across}, {"tensor": beside}


def enter(peers):
    barrier = pltpu.get_barrier_semaphore()
    for peer in peers:
        pl.semaphore_signal(barrier, inc=1, device_id=peer, device_id_type=pl.DeviceIdType.MESH)
    pl.semaphore_wait(barrier, len(peers))


def remote(src, dst, send_sem, recv_sem, peer):
    return pltpu.make_async_remote_copy(
        src_ref=src, dst_ref=dst, send_sem=send_sem, recv_sem=recv_sem,
        device_id=peer, device_id_type=pl.DeviceIdType.MESH,
    )


def span(start, size):
    return pl.ds(pl.multiple_of(start, 16), size)


def cut_rows(rows):
    top = rows // 32 * 16
    return ((0, top), (top, rows - top))


def gather_body(
    n, rows, tokens,
    x_ref, cot_ref, w_ref, wo_ref, xg_ref, cots_ref, ws_ref, wos_ref,
    own_sem, ring_send, ring_recv, over_send, over_recv, side_send, side_recv, pass_send, pass_recv,
):
    pos, ring, me, across, beside = neighbours(n)
    enter((*ring, across, beside))
    half = tokens // 2
    started = []

    def go(*args):
        copy = remote(*args)
        copy.start()
        started.append(copy)

    sides = [(x_ref, xg_ref, 0), (x_ref, xg_ref, 1), (cot_ref, cots_ref, 0), (cot_ref, cots_ref, 1)]
    opposite = lax.rem(me + 2, 4)
    pieces = [(src, dst, part) for part in (0, 1) for src, dst in ((w_ref, ws_ref), (wo_ref, wos_ref))]
    cuts = cut_rows(rows)

    def ring_step(step):
        last = step == n // 2 - 1
        for k, (own, full, part) in enumerate(pieces):
            first, size = cuts[part]
            for way in (0, 1):
                block = ring_index(lax.rem(pos + (step if way else n - step), n), n)
                here = full.at[span(block * rows + first, size)]
                if step > 0:
                    remote(
                        here, here, ring_send.at[way, k, step - 1], ring_recv.at[way, k, step - 1], ring[way]
                    ).wait_recv()
                if last and part != way:
                    continue
                src = own.at[pl.ds(first, size)] if step == 0 else here
                go(src, here, ring_send.at[way, k, step], ring_recv.at[way, k, step], ring[way])

    def pass_on(k):
        _, full, part = sides[k]
        here = full.at[span(opposite * tokens + part * half, half)]
        remote(here, here, over_send.at[k], over_recv.at[k], across).wait_recv()
        go(here, here, pass_send.at[k], pass_recv.at[k], beside)

    def send_over(k):
        own, full, part = sides[k]
        go(
            own.at[pl.ds(part * half, half)], full.at[span(me * tokens + part * half, half)],
            over_send.at[k], over_recv.at[k], across,
        )

    send_over(0)
    send_over(1)
    ring_step(0)
    for k, (own, full) in enumerate(((x_ref, xg_ref), (cot_ref, cots_ref))):
        go(own, full.at[span(me * tokens, tokens)], side_send.at[k], side_recv.at[k], beside)
    mine = ring_index(pos, n)
    locals_ = []
    for k, (own, dst) in enumerate(
        (
            (x_ref, xg_ref.at[span(me * tokens, tokens)]),
            (cot_ref, cots_ref.at[span(me * tokens, tokens)]),
            (w_ref, ws_ref.at[span(mine * rows, rows)]),
            (wo_ref, wos_ref.at[span(mine * rows, rows)]),
        )
    ):
        copy = pltpu.make_async_copy(own, dst, own_sem.at[k])
        copy.start()
        locals_.append(copy)
    for step in range(1, n // 2):
        ring_step(step)
        if step == 1:
            pass_on(0)
            pass_on(1)
            send_over(2)
            send_over(3)
    pass_on(2)
    pass_on(3)
    step = n // 2
    for k, (own, full, part) in enumerate(pieces):
        first, size = cuts[part]
        block = ring_index(lax.rem(pos + n // 2, n), n)
        here = full.at[span(block * rows + first, size)]
        remote(
            here, here, ring_send.at[part, k, step - 1], ring_recv.at[part, k, step - 1], ring[part]
        ).wait_recv()
    other = lax.rem(me, 2)
    next_door = me + 1 - 2 * other
    far = lax.rem(next_door + 2, 4)
    for k, (own, full) in enumerate(((x_ref, xg_ref), (cot_ref, cots_ref))):
        here = full.at[span(next_door * tokens, tokens)]
        remote(here, here, side_send.at[k], side_recv.at[k], beside).wait_recv()
    for k, (own, full, part) in enumerate(sides):
        here = full.at[span(far * tokens + part * half, half)]
        remote(here, here, pass_send.at[k], pass_recv.at[k], beside).wait_recv()
    for copy in locals_:
        copy.wait()
    for copy in started:
        copy.wait_send()


def gather_all(n, x, cot, w, wo):
    tokens, rows = x.shape[0], w.shape[0]
    dma = pltpu.SemaphoreType.DMA
    anywhere = pl.BlockSpec(memory_space=pl.ANY)
    whole = lambda a, k: jax.ShapeDtypeStruct((a.shape[0] * k, a.shape[1]), a.dtype)
    return pl.pallas_call(
        functools.partial(gather_body, n, rows, tokens),
        in_specs=[anywhere] * 4,
        out_specs=[anywhere] * 4,
        out_shape=[whole(x, 4), whole(cot, 4), whole(w, n), whole(wo, n)],
        scratch_shapes=[
            dma((4,)), dma((2, 4, n // 2)), dma((2, 4, n // 2)), dma((4,)), dma((4,)),
            dma((2,)), dma((2,)), dma((4,)), dma((4,)),
        ],
        compiler_params=pltpu.CompilerParams(collective_id=0, has_side_effects=True),
        name="gather_all",
    )(x, cot, w, wo)


def reduce_body(
    n, rows, tokens, starts,
    gc_ref, go_ref, branch_ref, back_ref, small_ref,
    oc_ref, oo_ref, obranch_ref, oback_ref, bc_ref, osmall_ref,
    gc, go_, slots, held, near, over, smalls, tens, bc_slot,
    load_sem, ring_send, ring_recv, near_send, near_recv, over_send, over_recv,
    small_send, small_recv, ten_send, ten_recv, bc_send, bc_recv,
):
    pos, ring, me, across, beside = neighbours(n)
    enter((*ring, across, beside))
    cuts = cut_rows(rows)
    started = []

    def go(*args):
        copy = remote(*args)
        copy.start()
        started.append(copy)
        return copy

    core = lax.rem(me, 2)
    opposite = lax.rem(me + 2, 4)
    next_door = me + 1 - 2 * core
    far = lax.rem(next_door + 2, 4)
    half = tokens // 2
    items = [(gc_ref, gc, oc_ref, lo, hi) for lo, hi in starts] + [(go_ref, go_, oo_ref, 0, go_.shape[1])]

    def block_at(way, steps):
        return ring_index(lax.rem(pos + (steps if way else n - steps), n), n)

    for k, (src, _, _, lo, hi) in enumerate(items):
        for way in (0, 1):
            first, size = cuts[way]
            go(
                src.at[span(block_at(way, 1) * rows + first, size), pl.ds(lo, hi - lo)],
                slots[way][k].at[0],
                ring_send.at[way, k, 0], ring_recv.at[way, k, 0], ring[way],
            )
    sides = [(branch_ref, 0), (back_ref, 1)]
    for turn, target in ((0, far), (1, next_door)):
        for src, k in sides:
            for part in (0, 1):
                go(
                    src.at[span(target * tokens + part * half, half)],
                    near.at[k, turn, part],
                    near_send.at[k, turn, part], near_recv.at[k, turn, part], beside,
                )
    loads = {}
    for turn, target in ((0, opposite), (1, me)):
        for src, k in sides:
            for part in (0, 1):
                copy = pltpu.make_async_copy(
                    src.at[span(target * tokens + part * half, half)],
                    held.at[k, turn, part], load_sem.at[4 * turn + 2 * k + part],
                )
                copy.start()
                loads[k, turn, part] = copy
    for k, (src, dst) in enumerate(((gc_ref, gc), (go_ref, go_))):
        copy = pltpu.make_async_copy(src, dst, load_sem.at[8 + k])
        copy.start()
        loads["ring", k] = copy
    small_load = pltpu.make_async_copy(small_ref, smalls.at[pos], load_sem.at[10])
    small_load.start()

    def add_side(k, turn, part, dst):
        def some(i, _):
            at = span(i * 16, 16)
            total = held[k, turn, part, at, :].astype(f32) + near[k, turn, part, at, :].astype(f32)
            if dst is None:
                held[k, turn, part, at, :] = total.astype(bf16)
            else:
                dst[span(part * half + i * 16, 16), :] = total
            return 0

        lax.fori_loop(0, half // 16, some, 0)

    def near_ready(k, turn, part):
        loads[k, turn, part].wait()
        remote(
            near.at[k, turn, part], near.at[k, turn, part],
            near_send.at[k, turn, part], near_recv.at[k, turn, part], beside,
        ).wait_recv()

    for k in (0, 1):
        for part in (0, 1):
            near_ready(k, 0, part)
            add_side(k, 0, part, None)
            go(held.at[k, 0, part], over.at[k, part], over_send.at[k, part], over_recv.at[k, part], across)

    small_load.wait()
    loads["ring", 0].wait()
    loads["ring", 1].wait()
    outs = (obranch_ref, oback_ref)
    todo = [(k, part) for k in (0, 1) for part in (0, 1)]

    for step in range(n - 1):
        here = smalls.at[lax.rem(pos + n - step, n)]
        go(here, here, small_send.at[step], small_recv.at[step], ring[0])
        for k, (_, own, out, lo, hi) in enumerate(items):
            for way in (0, 1):
                first, size = cuts[way]
                slot = slots[way][k].at[step]
                remote(
                    slot, slot, ring_send.at[way, k, step], ring_recv.at[way, k, step], ring[way]
                ).wait_recv()
                block = block_at(way, 2 + step) if step < n - 2 else block_at(way, 0)

                def some(i, _, way=way, k=k, step=step, own=own, out=out, lo=lo, hi=hi, first=first, block=block):
                    total = slots[way][k][step, span(i * 16, 16), :].astype(f32)
                    total = total + own[span(block * rows + first + i * 16, 16), lo:hi].astype(f32)
                    if step < n - 2:
                        slots[way][k][step, span(i * 16, 16), :] = total.astype(bf16)
                    else:
                        out[span(first + i * 16, 16), lo:hi] = total
                    return 0

                lax.fori_loop(0, size // 16, some, 0)
                if step < n - 2:
                    go(
                        slot, slots[way][k].at[step + 1],
                        ring_send.at[way, k, step + 1], ring_recv.at[way, k, step + 1], ring[way],
                    )
            if step == n - 2 and k == 0:
                bc_slot[0] = oc_ref[:, starts[0][0] : starts[0][0] + 2 * NS]
                go(bc_slot.at[0], bc_slot.at[1], bc_send.at[0], bc_recv.at[0], beside)
        here = smalls.at[lax.rem(pos + 2 * n - step - 1, n)]
        remote(here, here, small_send.at[step], small_recv.at[step], ring[0]).wait_recv()
        if todo and step >= 1:
            k, part = todo.pop(0)
            near_ready(k, 1, part)
            add_side(k, 1, part, outs[k])
    for k, part in todo:
        near_ready(k, 1, part)
        add_side(k, 1, part, outs[k])

    total = smalls[0]
    for i in range(1, n):
        total = total + smalls[i]
    tens[me] = total
    go(tens.at[me], tens.at[me], ten_send.at[0], ten_recv.at[0], beside)
    remote(bc_slot.at[1], bc_slot.at[1], bc_send.at[0], bc_recv.at[0], beside).wait_recv()
    bc_slot[2] = bc_slot[0] + bc_slot[1]
    go(bc_slot.at[2], bc_slot.at[3], bc_send.at[1], bc_recv.at[1], across)
    here = tens.at[next_door]
    remote(here, here, ten_send.at[0], ten_recv.at[0], beside).wait_recv()
    for k, target in ((0, me), (1, next_door)):
        here = tens.at[target]
        go(here, here, ten_send.at[1 + k], ten_recv.at[1 + k], across)
    for k in (0, 1):
        for part in (0, 1):
            slot = over.at[k, part]
            remote(slot, slot, over_send.at[k, part], over_recv.at[k, part], across).wait_recv()

            def some(i, _, k=k, part=part):
                at = span(part * half + i * 16, 16)
                outs[k][at, :] = outs[k][at, :] + over[k, part, span(i * 16, 16), :].astype(f32)
                return 0

            lax.fori_loop(0, half // 16, some, 0)
    for k, target in ((0, opposite), (1, far)):
        here = tens.at[target]
        remote(here, here, ten_send.at[1 + k], ten_recv.at[1 + k], across).wait_recv()
    osmall_ref[...] = tens[...]
    remote(bc_slot.at[3], bc_slot.at[3], bc_send.at[1], bc_recv.at[1], across).wait_recv()
    bc_ref[...] = bc_slot[2] + bc_slot[3]
    for copy in started:
        copy.wait_send()


def reduce_all(n, grad_cat, grad_out, branch, back, small):
    rows, tokens = grad_cat.shape[0] // n, branch.shape[0] // 4
    wide, width = grad_cat.shape[1], grad_out.shape[1]
    starts = ((2 * width, wide), (0, 2 * width))
    widths = [hi - lo for lo, hi in starts] + [width]
    sizes = [size for _, size in cut_rows(rows)]
    half = tokens // 2
    dma, vm = pltpu.SemaphoreType.DMA, pltpu.VMEM
    anywhere = pl.BlockSpec(memory_space=pl.ANY)
    inside = pl.BlockSpec(memory_space=pltpu.VMEM)
    return pl.pallas_call(
        functools.partial(reduce_body, n, rows, tokens, starts),
        in_specs=[anywhere] * 5,
        out_specs=[inside] * 6,
        out_shape=[
            jax.ShapeDtypeStruct((rows, wide), f32),
            jax.ShapeDtypeStruct((rows, width), f32),
            jax.ShapeDtypeStruct((tokens, D), f32),
            jax.ShapeDtypeStruct((tokens, D), f32),
            jax.ShapeDtypeStruct((rows, 2 * NS), f32),
            jax.ShapeDtypeStruct((4, *small.shape), f32),
        ],
        scratch_shapes=[
            vm(grad_cat.shape, bf16), vm(grad_out.shape, bf16),
            [[vm((n - 1, size, w), bf16) for w in widths] for size in sizes],
            vm((2, 2, 2, half, D), bf16), vm((2, 2, 2, half, D), bf16), vm((2, 2, half, D), bf16),
            vm((n, *small.shape), f32), vm((4, *small.shape), f32), vm((4, rows, 2 * NS), f32),
            dma((11,)), dma((2, 3, n - 1)), dma((2, 3, n - 1)), dma((2, 2, 2)), dma((2, 2, 2)),
            dma((2, 2)), dma((2, 2)), dma((n - 1,)), dma((n - 1,)), dma((3,)), dma((3,)), dma((2,)), dma((2,)),
        ],
        compiler_params=pltpu.CompilerParams(
            collective_id=1, has_side_effects=True, vmem_limit_bytes=60 * 2**20
        ),
        name="reduce_all",
    )(grad_cat, grad_out, branch, back, small)


def adamw_step(weight, first, second, grad, rate, decay):
    first_new = beta_first * first + (1.0 - beta_first) * grad
    second_new = beta_second * second + (1.0 - beta_second) * grad * grad
    hat_first = first_new / (1.0 - beta_first**STEP)
    hat_second = second_new / (1.0 - beta_second**STEP)
    weight_new = weight - rate * (hat_first / (jnp.sqrt(hat_second) + adam_eps) + decay * weight)
    return (weight_new, first_new, second_new)


def local(
    layer_input,
    out_grad,
    small_params,
    small_first,
    small_second,
    w_zx,
    zx_first,
    zx_second,
    w_bc,
    bc_first,
    bc_second,
    w_dt,
    dt_first,
    dt_second,
    w_out,
    out_first,
    out_second,
):
    tensor_index = lax.axis_index("tensor")
    local_in = layer_input.astype(f32)
    gain_in, gate_gain, conv_x, bias_x, conv_bc, bias_bc, dt_bias, a_log, d_skip = unpack(
        small_params
    )
    rows_own = w_zx.shape[0]
    width = w_zx.shape[2]
    heads = w_dt.shape[1]
    chan_start = tensor_index * width
    head_start = tensor_index * heads
    gate_local = lax.dynamic_slice_in_dim(gate_gain, chan_start, width, 0)
    conv_local = lax.dynamic_slice_in_dim(conv_x, chan_start, width, 1)
    bias_local = lax.dynamic_slice_in_dim(bias_x, chan_start, width, 0)
    dtb_local = lax.dynamic_slice_in_dim(dt_bias, head_start, heads, 0)
    a_local = -jnp.exp(lax.dynamic_slice_in_dim(a_log, head_start, heads, 0))
    dskip_local = lax.dynamic_slice_in_dim(d_skip, head_start, heads, 0)
    taps = jnp.concatenate(
        [
            jnp.concatenate([conv_local, conv_bc], axis=1),
            jnp.concatenate([bias_local, bias_bc])[None, :],
            jnp.zeros((8 - CONV - 1, width + 2 * NS), f32),
        ],
        axis=0,
    )
    lanes = lambda v: jnp.pad(v, (0, LANES - heads))
    head = jnp.pad(jnp.stack([lanes(dtb_local), lanes(a_local)]), ((0, 6), (0, 0)))
    chan = jnp.pad(jnp.stack([gate_local, jnp.repeat(dskip_local, P_SIZE)]), ((0, 6), (0, 0)))
    pick = jnp.asarray(
        (jnp.arange(width)[:, None] // P_SIZE == jnp.arange(LANES)[None, :]), bf16
    )

    inv_in = lax.rsqrt(jnp.mean(local_in * local_in, axis=-1, keepdims=True) + norm_eps)
    normed_in = local_in * inv_in * gain_in[None, :]
    w_cat = jnp.concatenate(
        [
            w_zx.reshape(rows_own, 2 * width).astype(bf16),
            w_bc.astype(bf16),
            jnp.pad(w_dt, ((0, 0), (0, LANES - heads))).astype(bf16),
        ],
        axis=1,
    )
    n = lax.axis_size("dp")
    xg, cot_all, w_all, wo_all = gather_all(
        n, normed_in.astype(bf16), out_grad, w_cat, w_out.astype(bf16)
    )

    z, v, xc, dr, y, dn, st, red = ssd_forward(xg, w_all, cot_all, wo_all, taps, head, chan)
    sums = lax.psum(red[::8], "tensor")
    red = jnp.repeat(sums, 8, axis=0)
    normed_low, d_cat, acc, hacc = ssd_backward(z, v, xc, dr, y, dn, st, red, taps, head, chan, pick)

    branch = mm(normed_low, wo_all, NT).astype(bf16)
    grad_out = mm(cot_all, normed_low, TN).astype(bf16)
    back = mm(d_cat, w_all, NT)
    gain_part = jnp.sum(xg.astype(f32) * back, axis=0) / gain_in
    grad_cat = mm(xg, d_cat, TN).astype(bf16)
    acc = jnp.sum(acc, axis=1)
    hacc = jnp.sum(hacc, axis=1)
    skip_part = jnp.sum(acc[CONV + 2, :width].reshape(heads, P_SIZE), axis=1)
    small = jnp.concatenate(
        [
            acc[: CONV + 1].reshape(-1), acc[CONV + 1, :width], hacc[0], hacc[1],
            gain_part, jnp.pad(skip_part, (0, 4 * LANES - heads)),
        ]
    ).reshape(8, width + 2 * NS)
    owner_cat, owner_out, own_branch, d_normed_in, owner_bc, tens = reduce_all(
        n, grad_cat, grad_out, branch, back.astype(bf16), small
    )
    layer_output = (local_in + own_branch).astype(bf16)
    owner_zx = owner_cat[:, : 2 * width].reshape(rows_own, 2, width)
    owner_dt = owner_cat[:, 2 * width + 2 * NS : 2 * width + 2 * NS + heads]

    inner_in = jnp.sum(local_in * gain_in[None, :] * d_normed_in, axis=-1, keepdims=True)
    input_grad = (
        out_grad.astype(f32)
        + inv_in * gain_in[None, :] * d_normed_in
        - local_in * (inv_in * inv_in * inv_in * inner_in / D)
    )
    gain_sum = jnp.sum(tens[:, 6:8], axis=0).reshape(-1)[:D]
    bc_sum = jnp.sum(tens[:, : CONV + 1, width:], axis=0)
    small_grad = jnp.concatenate(
        [
            gain_sum,
            tens[:, CONV + 1, :width].reshape(-1),
            jnp.moveaxis(tens[:, :CONV, :width], 0, 1).reshape(-1),
            tens[:, CONV, :width].reshape(-1),
            bc_sum.reshape(-1),
            tens[:, CONV + 1, width : width + heads].reshape(-1),
            tens[:, CONV + 1, width + LANES : width + LANES + heads].reshape(-1) * -jnp.exp(a_log),
            tens[:, 7, 512 : 512 + heads].reshape(-1),
        ]
    )
    small_new, small_first_new, small_second_new = adamw_step(
        small_params, small_first, small_second, small_grad, small_rate, 0.0
    )
    zx_new, zx_first_new, zx_second_new = adamw_step(
        w_zx, zx_first, zx_second, owner_zx, matrix_rate, matrix_decay
    )
    bc_new, bc_first_new, bc_second_new = adamw_step(
        w_bc, bc_first, bc_second, owner_bc, matrix_rate, matrix_decay
    )
    dt_new, dt_first_new, dt_second_new = adamw_step(
        w_dt, dt_first, dt_second, owner_dt, matrix_rate, matrix_decay
    )
    out_new, out_first_new, out_second_new = adamw_step(
        w_out, out_first, out_second, owner_out, matrix_rate, matrix_decay
    )
    return (
        layer_output,
        input_grad,
        small_new,
        small_first_new,
        small_second_new,
        zx_new,
        zx_first_new,
        zx_second_new,
        bc_new,
        bc_first_new,
        bc_second_new,
        dt_new,
        dt_first_new,
        dt_second_new,
        out_new,
        out_first_new,
        out_second_new,
    )


def solution(mesh):
    return jax.shard_map(
        local,
        mesh=mesh,
        in_specs=(
            P(("dp", "tensor"), None),
            P(("dp", "tensor"), None),
            P(),
            P(),
            P(),
            P("dp", None, "tensor"),
            P("dp", None, "tensor"),
            P("dp", None, "tensor"),
            P("dp", None),
            P("dp", None),
            P("dp", None),
            P("dp", "tensor"),
            P("dp", "tensor"),
            P("dp", "tensor"),
            P("dp", "tensor"),
            P("dp", "tensor"),
            P("dp", "tensor"),
        ),
        out_specs=(
            P(("dp", "tensor"), None),
            P(("dp", "tensor"), None),
            P(),
            P(),
            P(),
            P("dp", None, "tensor"),
            P("dp", None, "tensor"),
            P("dp", None, "tensor"),
            P("dp", None),
            P("dp", None),
            P("dp", None),
            P("dp", "tensor"),
            P("dp", "tensor"),
            P("dp", "tensor"),
            P("dp", "tensor"),
            P("dp", "tensor"),
            P("dp", "tensor"),
        ),
        check_vma=False,
    )
```

```python
import functools

import jax
import jax.numpy as jnp
from jax import lax
from jax.experimental import pallas as pl
from jax.experimental.pallas import tpu as pltpu
from jax.sharding import PartitionSpec as P

D = 1536
DI = 3072
H = 48
NS = 128
P_SIZE = 64
CONV = 4
LEN = 2048
STEP = 10

T = 128
ROWS = 256
LANES = 128

norm_eps = 1e-05
adam_eps = 1e-08
beta_first = 0.9
beta_second = 0.95
matrix_rate = 0.01
small_rate = 0.1
matrix_decay = 0.1

f32 = jnp.float32
bf16 = jnp.bfloat16
NN = (((1,), (0,)), ((), ()))
NT = (((1,), (1,)), ((), ()))
TN = (((0,), (0,)), ((), ()))
HIGHEST = lax.Precision.HIGHEST


def unpack(flat):
    gain_in = flat[:D]
    cursor = D
    gate_gain = flat[cursor : cursor + DI]
    cursor = cursor + DI
    conv_x = flat[cursor : cursor + CONV * DI].reshape(CONV, DI)
    cursor = cursor + CONV * DI
    bias_x = flat[cursor : cursor + DI]
    cursor = cursor + DI
    conv_bc = flat[cursor : cursor + CONV * 2 * NS].reshape(CONV, 2 * NS)
    cursor = cursor + CONV * 2 * NS
    bias_bc = flat[cursor : cursor + 2 * NS]
    cursor = cursor + 2 * NS
    dt_bias = flat[cursor : cursor + H]
    a_log = flat[cursor + H : cursor + 2 * H]
    d_skip = flat[cursor + 2 * H : cursor + 3 * H]
    return (gain_in, gate_gain, conv_x, bias_x, conv_bc, bias_bc, dt_bias, a_log, d_skip)


def mm(a, b, dims=NN):
    return lax.dot_general(a, b, dims, preferred_element_type=f32)


def mm_exact(a, b, dims=NN):
    return lax.dot_general(a, b, dims, preferred_element_type=f32, precision=HIGHEST)


def sigmoid(v):
    return 0.5 * jnp.tanh(0.5 * v) + 0.5


def softplus(v):
    return jnp.maximum(v, 0.0) + jnp.log1p(jnp.exp(-jnp.abs(v)))


def spread(col):
    return jnp.broadcast_to(col, (T, LANES))


def block_iota(axis):
    return lax.broadcasted_iota(jnp.int32, (T, LANES), axis)


def head_rows(dr_ref, head_ref, rows):
    raw = dr_ref[rows, :] + head_ref[0:1, :]
    dt = softplus(raw)
    low_tri = jnp.where(block_iota(0) >= block_iota(1), 1.0, 0.0).astype(f32)
    decay = mm_exact(low_tri, dt * head_ref[1:2, :])
    return raw, dt, decay


def forward_body(
    width,
    xg_ref, w_ref, cot_ref, wo_ref, taps_ref, head_ref, chan_ref,
    z_ref, v_ref, xc_ref, dr_ref, y_ref, dn_ref, st_ref, red_ref,
    halo, state,
):
    pairs = width // LANES
    step = pl.program_id(0)

    @pl.when(step == 0)
    def _():
        halo[0:8, :] = jnp.zeros((8, halo.shape[1]), f32)
        state[...] = jnp.zeros_like(state)

    wide = width + 2 * NS
    dr_ref[...] = mm(xg_ref[...], w_ref[:, width + wide :])
    halo[8 : 8 + ROWS, :] = mm(xg_ref[...], w_ref[:, width : width + wide])
    z_ref[...] = mm(xg_ref[...], w_ref[:, :width])
    dn_ref[...] = mm(cot_ref[...], wo_ref[...])
    low_half = block_iota(1) < P_SIZE
    causal = block_iota(0) >= block_iota(1)

    def convolved(sub, block):
        cols = slice(block * LANES, (block + 1) * LANES)
        total = taps_ref[CONV : CONV + 1, cols]
        for k in range(CONV):
            first = 8 - (CONV - 1) + k + sub * T
            total = total + taps_ref[k : k + 1, cols] * halo[first : first + T, cols]
        rows = slice(sub * T, (sub + 1) * T)
        xc_ref[rows, cols] = total
        v_ref[rows, cols] = halo[8 + sub * T : 8 + (sub + 1) * T, cols].astype(bf16)
        return total * sigmoid(total)

    for sub in range(ROWS // T):
        rows = slice(sub * T, (sub + 1) * T)
        raw, dt, decay = head_rows(dr_ref, head_ref, rows)
        decay_t = decay.T
        b_low = convolved(sub, pairs).astype(bf16)
        c_low = convolved(sub, pairs + 1).astype(bf16)
        b_t = b_low.T
        scores = jnp.where(causal, mm(c_low, b_low, NT), 0.0)
        squares = jnp.zeros((T, LANES), f32)
        inner = jnp.zeros((T, LANES), f32)
        st_ref[sub] = state[...].astype(bf16)
        for p in range(pairs):
            cols = slice(p * LANES, (p + 1) * LANES)
            x = convolved(sub, p)
            l1, l2 = spread(decay[:, 2 * p : 2 * p + 1]), spread(decay[:, 2 * p + 1 : 2 * p + 2])
            both = jnp.where(low_half, l1, l2)
            dtb = jnp.where(
                low_half, spread(dt[:, 2 * p : 2 * p + 1]), spread(dt[:, 2 * p + 1 : 2 * p + 2])
            )
            u = x * dtb
            m1 = scores * jnp.exp(jnp.minimum(l1 - decay_t[2 * p : 2 * p + 1, :], 0.0))
            m2 = scores * jnp.exp(jnp.minimum(l2 - decay_t[2 * p + 1 : 2 * p + 2, :], 0.0))
            mixing = jnp.concatenate([m1.astype(bf16), m2.astype(bf16)], axis=1)
            parts = jnp.concatenate(
                [jnp.where(low_half, u, 0.0).astype(bf16), jnp.where(low_half, 0.0, u).astype(bf16)],
                axis=0,
            )
            last = both[T - 1 : T, :]
            entering = st_ref[sub, :, cols]
            y = mm(mixing, parts) + jnp.exp(both) * mm(c_low, entering) + chan_ref[1:2, cols] * x
            tail = (u * jnp.exp(last - both)).astype(bf16)
            state[:, cols] = jnp.exp(last) * state[:, cols] + mm(b_t, tail)
            y_ref[rows, cols] = y
            z = z_ref[rows, cols]
            gated = y * (z * sigmoid(z))
            squares = squares + gated * gated
            inner = inner + gated * chan_ref[0:1, cols] * dn_ref[rows, cols]
        ones = jnp.ones((8, LANES), f32)
        red_ref[0:8, rows] = mm_exact(ones, squares, NT)
        red_ref[8:16, rows] = mm_exact(ones, inner, NT)
    halo[0:8, :] = halo[ROWS : ROWS + 8, :]


def ssd_forward(xg, w_cat, cot, w_out, taps, head, chan):
    tokens = xg.shape[0]
    width = w_out.shape[1]
    wide = width + 2 * NS
    steps = tokens // ROWS
    subs = ROWS // T
    per_seq = LEN // ROWS
    assert per_seq == steps
    row = lambda n: pl.BlockSpec((ROWS, n), lambda i: (i, 0))
    whole = lambda a: pl.BlockSpec(a.shape, lambda i: (0,) * a.ndim, pipeline_mode=pl.Buffered(1))
    return pl.pallas_call(
        functools.partial(forward_body, width),
        grid=(steps,),
        in_specs=[row(D), whole(w_cat), row(D), whole(w_out), whole(taps), whole(head), whole(chan)],
        out_specs=[
            row(width), row(wide), row(wide), row(LANES), row(width), row(width),
            pl.BlockSpec((subs, NS, width), lambda i: (i, 0, 0)),
            pl.BlockSpec((16, ROWS), lambda i: (0, i)),
        ],
        out_shape=[
            jax.ShapeDtypeStruct((tokens, width), f32),
            jax.ShapeDtypeStruct((tokens, wide), bf16),
            jax.ShapeDtypeStruct((tokens, wide), f32),
            jax.ShapeDtypeStruct((tokens, LANES), f32),
            jax.ShapeDtypeStruct((tokens, width), f32),
            jax.ShapeDtypeStruct((tokens, width), f32),
            jax.ShapeDtypeStruct((tokens // T, NS, width), bf16),
            jax.ShapeDtypeStruct((16, tokens), f32),
        ],
        scratch_shapes=[pltpu.VMEM((ROWS + 8, wide), f32), pltpu.VMEM((NS, width), f32)],
        compiler_params=pltpu.CompilerParams(vmem_limit_bytes=56 * 2**20),
        name="layer_forward",
    )(xg, w_cat, cot, w_out, taps, head, chan)


def backward_body(
    width,
    z_ref, v_ref, xc_ref, dr_ref, y_ref, dn_ref, st_ref, red_ref, taps_ref, head_ref, chan_ref, pick_ref,
    nl_ref, d_ref, acc_ref, hacc_ref,
    dxh, dstate, yst, bds, dyeb, utb, gin, gout, xdu, turn,
):
    pairs = width // LANES
    wide = width + 2 * NS
    step = pl.program_id(0)

    @pl.when(step == 0)
    def _():
        dxh[T : T + 8, :] = jnp.zeros((8, wide), f32)
        dstate[...] = jnp.zeros_like(dstate)
        acc_ref[...] = jnp.zeros_like(acc_ref)
        hacc_ref[...] = jnp.zeros_like(hacc_ref)
        turn[...] = jnp.zeros_like(turn)

    low_half = block_iota(1) < P_SIZE
    row_at, col_at = block_iota(0), block_iota(1)
    until = row_at <= col_at
    before = row_at < col_at
    upper = jnp.where(until, 1.0, 0.0).astype(f32)
    strict = jnp.where(before, 1.0, 0.0).astype(f32)
    low_tri = jnp.where(row_at >= col_at, 1.0, 0.0).astype(bf16)

    def add(index, cols, value):
        acc_ref[index, :, cols] += jnp.sum(value.reshape(T // 8, 8, LANES), axis=0)

    def conv_back(rows, block, d_act, xc, s, act):
        cols = slice(block * LANES, (block + 1) * LANES)
        dxh[0:T, cols] = d_act * (s + act * (1.0 - s))
        v = v_ref[rows, cols].astype(f32)
        total = None
        for m in range(CONV):
            moved = dxh[m : m + T, cols]
            if m == 0:
                add(CONV, cols, moved)
            add(CONV - 1 - m, cols, v * moved)
            term = taps_ref[CONV - 1 - m : CONV - m, cols] * moved
            total = term if total is None else total + term
        d_ref[rows, width + block * LANES : width + (block + 1) * LANES] = total.astype(bf16)

    for sub in reversed(range(ROWS // T)):
        rows = slice(sub * T, (sub + 1) * T)
        raw, dt, decay = head_rows(dr_ref, head_ref, rows)
        decay_t = decay.T
        sums = red_ref[:, rows]
        q_row = lax.rsqrt(sums[0:8] / DI + norm_eps)
        k_row = q_row * q_row * q_row * sums[8:16] / DI
        q = spread(q_row.T[:, 0:1])
        kk = spread(k_row.T[:, 0:1])
        b_cols = slice(width, width + NS)
        c_cols = slice(width + NS, width + 2 * NS)
        b_xc, c_xc = xc_ref[rows, b_cols], xc_ref[rows, c_cols]
        b_s, c_s = sigmoid(b_xc), sigmoid(c_xc)
        b_act, c_act = b_xc * b_s, c_xc * c_s
        b_low, c_low = b_act.astype(bf16), c_act.astype(bf16)
        c_t = c_low.T
        scores_t = jnp.where(until, mm(b_low, c_low, NT), 0.0)
        ds_low = dstate[...].astype(bf16)
        yst[...] = mm(c_low, st_ref[sub])
        bds[...] = mm(b_low, ds_low)
        d_scores = jnp.zeros((T, LANES), f32)
        for p in range(pairs):
            cols = slice(p * LANES, (p + 1) * LANES)
            z, y, dn = z_ref[rows, cols], y_ref[rows, cols], dn_ref[rows, cols]
            gain = chan_ref[0:1, cols]
            s = sigmoid(z)
            sz = z * s
            gated = y * sz
            gq = gated * q
            dg = q * gain * dn - gated * kk
            add(CONV + 1, cols, gq * dn)
            nl_ref[rows, cols] = (gq * gain).astype(bf16)
            d_ref[rows, cols] = (dg * y * (s + sz * (1.0 - s))).astype(bf16)
            dy = dg * sz
            xc = xc_ref[rows, cols]
            xs = sigmoid(xc)
            x = xc * xs
            l1, l2 = spread(decay[:, 2 * p : 2 * p + 1]), spread(decay[:, 2 * p + 1 : 2 * p + 2])
            both = jnp.where(low_half, l1, l2)
            dtb = jnp.where(
                low_half, spread(dt[:, 2 * p : 2 * p + 1]), spread(dt[:, 2 * p + 1 : 2 * p + 2])
            )
            u = x * dtb
            last = both[T - 1 : T, :]
            e1 = jnp.exp(jnp.minimum(decay_t[2 * p : 2 * p + 1, :] - l1, 0.0))
            e2 = jnp.exp(jnp.minimum(decay_t[2 * p + 1 : 2 * p + 2, :] - l2, 0.0))
            dy_low = dy.astype(bf16)
            zero = jnp.zeros_like(dy_low)
            u_low = u.astype(bf16)
            du_in = mm(
                jnp.concatenate([(scores_t * e1).astype(bf16), (scores_t * e2).astype(bf16)], axis=1),
                jnp.concatenate(
                    [jnp.where(low_half, dy_low, zero), jnp.where(low_half, zero, dy_low)], axis=0
                ),
            )
            d_mix = mm(
                jnp.concatenate(
                    [jnp.where(low_half, u_low, zero), jnp.where(low_half, zero, u_low)], axis=0
                ),
                dy_low,
                NT,
            )
            d1, d2 = d_mix[:T] * e1, d_mix[T:] * e2
            d_scores = d_scores + d1 + d2
            reach = mm(
                jnp.concatenate([(d1 * scores_t).astype(bf16), (d2 * scores_t).astype(bf16)], axis=0),
                low_tri,
            )
            turn[2 * p : 2 * p + 1, :] = jnp.sum(jnp.where(before, reach[:T], 0.0), axis=0, keepdims=True)
            turn[2 * p + 1 : 2 * p + 2, :] = jnp.sum(
                jnp.where(before, reach[T:], 0.0), axis=0, keepdims=True
            )
            tail = jnp.exp(last - both)
            dye = dy * jnp.exp(both)
            du_out = tail * bds[:, cols]
            du = du_in + du_out
            gin[:, cols] = (dye * yst[:, cols]).astype(bf16)
            gout[:, cols] = (u * du_out).astype(bf16)
            xdu[:, cols] = (x * du).astype(bf16)
            dyeb[:, cols] = dye.astype(bf16)
            utb[:, cols] = (u * tail).astype(bf16)
            add(CONV + 2, cols, dy * x)
            conv_back(rows, p, dtb * du + chan_ref[1:2, cols] * dy, xc, xs, x)
        d_scores = jnp.where(until, d_scores, 0.0).astype(bf16)
        d_b = mm(d_scores, c_low) + mm(utb[...], ds_low, NT)
        d_c = mm(d_scores, b_low, TN) + mm(dyeb[...], st_ref[sub], NT)
        conv_back(rows, pairs, d_b, b_xc, b_s, b_act)
        conv_back(rows, pairs + 1, d_c, c_xc, c_s, c_act)
        ended = jnp.zeros((1, LANES), f32)
        for p in range(pairs):
            cols = slice(p * LANES, (p + 1) * LANES)
            last = jnp.where(
                low_half[0:1], decay[T - 1 : T, 2 * p : 2 * p + 1], decay[T - 1 : T, 2 * p + 1 : 2 * p + 2]
            )
            fade = jnp.exp(last)
            before_ds = dstate[:, cols]
            through = jnp.sum(before_ds * st_ref[sub, :, cols].astype(f32), axis=0, keepdims=True) * fade
            ended = ended + mm_exact(through, pick_ref[cols, :].astype(f32))
            dstate[:, cols] = fade * before_ds + mm(c_t, dyeb[:, cols])
        gin_heads = mm(gin[...], pick_ref[...])
        gout_heads = mm(gout[...], pick_ref[...])
        reached = (
            turn[...].T
            + mm_exact(upper, gin_heads)
            + mm_exact(strict, gout_heads, TN)
            + ended
        )
        d_raw = (head_ref[1:2, :] * reached + mm(xdu[...], pick_ref[...])) * sigmoid(raw)
        d_ref[rows, width + wide :] = d_raw.astype(bf16)
        hacc_ref[0] += jnp.sum(d_raw.reshape(T // 8, 8, LANES), axis=0)
        hacc_ref[1] += jnp.sum((dt * reached).reshape(T // 8, 8, LANES), axis=0)
        dxh[T : T + 8, :] = dxh[0:8, :]


def ssd_backward(z, v, xc, dr, y, dn, st, red, taps, head, chan, pick):
    tokens, width = z.shape
    wide = width + 2 * NS
    steps = tokens // ROWS
    subs = ROWS // T
    row = lambda n: pl.BlockSpec((ROWS, n), lambda i: (steps - 1 - i, 0))
    whole = lambda a: pl.BlockSpec(a.shape, lambda i: (0,) * a.ndim, pipeline_mode=pl.Buffered(1))
    total = width + wide + LANES
    vm = pltpu.VMEM
    return pl.pallas_call(
        functools.partial(backward_body, width),
        grid=(steps,),
        in_specs=[
            row(width), row(wide), row(wide), row(LANES), row(width), row(width),
            pl.BlockSpec((subs, NS, width), lambda i: (steps - 1 - i, 0, 0)),
            pl.BlockSpec((16, ROWS), lambda i: (0, steps - 1 - i)),
            whole(taps), whole(head), whole(chan), whole(pick),
        ],
        out_specs=[
            row(width), row(total),
            pl.BlockSpec((CONV + 3, 8, wide), lambda i: (0, 0, 0)),
            pl.BlockSpec((2, 8, LANES), lambda i: (0, 0, 0)),
        ],
        out_shape=[
            jax.ShapeDtypeStruct((tokens, width), bf16),
            jax.ShapeDtypeStruct((tokens, total), bf16),
            jax.ShapeDtypeStruct((CONV + 3, 8, wide), f32),
            jax.ShapeDtypeStruct((2, 8, LANES), f32),
        ],
        scratch_shapes=[
            vm((T + 8, wide), f32), vm((NS, width), f32), vm((T, width), f32), vm((T, width), f32),
            vm((T, width), bf16), vm((T, width), bf16), vm((T, width), bf16), vm((T, width), bf16),
            vm((T, width), bf16), vm((T, LANES), f32),
        ],
        compiler_params=pltpu.CompilerParams(vmem_limit_bytes=56 * 2**20),
        name="layer_backward",
    )(z, v, xc, dr, y, dn, st, red, taps, head, chan, pick)


def ring_place(n):
    me = lax.axis_index("dp")
    z, x = lax.div(me, 2), lax.rem(me, 2)
    return z + x * (n - 1 - 2 * z)


def ring_index(pos, n):
    back = lax.div(pos, n // 2)
    return 2 * pos + back * (2 * n - 1 - 4 * pos)


def neighbours(n):
    pos = ring_place(n)
    right = ring_index(lax.rem(pos + 1, n), n)
    left = ring_index(lax.rem(pos + n - 1, n), n)
    me = lax.axis_index("tensor")
    y, core = lax.div(me, 2), lax.rem(me, 2)
    across = 2 * (1 - y) + core
    beside = 2 * y + 1 - core
    return pos, ({"dp": right}, {"dp": left}), me, {"tensor": across}, {"tensor": beside}


def enter(peers):
    barrier = pltpu.get_barrier_semaphore()
    for peer in peers:
        pl.semaphore_signal(barrier, inc=1, device_id=peer, device_id_type=pl.DeviceIdType.MESH)
    pl.semaphore_wait(barrier, len(peers))


def remote(src, dst, send_sem, recv_sem, peer):
    return pltpu.make_async_remote_copy(
        src_ref=src, dst_ref=dst, send_sem=send_sem, recv_sem=recv_sem,
        device_id=peer, device_id_type=pl.DeviceIdType.MESH,
    )


def span(start, size):
    return pl.ds(pl.multiple_of(start, 16), size)


def cut_rows(rows):
    top = rows // 32 * 16
    return ((0, top), (top, rows - top))


def gather_body(
    n, rows, tokens,
    x_ref, cot_ref, w_ref, wo_ref, xg_ref, cots_ref, ws_ref, wos_ref,
    xg, cots, ws, wos,
    own_sem, ring_keep, pass_keep, side_keep, ring_send, ring_recv, over_send, over_recv,
    side_send, side_recv, pass_send, pass_recv, over_keep,
):
    pos, ring, me, across, beside = neighbours(n)
    enter((*ring, across, beside))
    half = tokens // 2
    started, kept = [], []

    def go(*args):
        copy = remote(*args)
        copy.start()
        started.append(copy)

    def keep(src, dst, sem):
        copy = pltpu.make_async_copy(src, dst, sem)
        copy.start()
        kept.append(copy)

    sides = [(x_ref, xg, xg_ref, 0), (x_ref, xg, xg_ref, 1), (cot_ref, cots, cots_ref, 0), (cot_ref, cots, cots_ref, 1)]
    opposite = lax.rem(me + 2, 4)
    pieces = [
        (src, dst, out, part)
        for part in (0, 1)
        for src, dst, out in ((w_ref, ws, ws_ref), (wo_ref, wos, wos_ref))
    ]
    cuts = cut_rows(rows)

    def arrived(k, way, step, block):
        _, full, out, part = pieces[k]
        first, size = cuts[part]
        at = span(block * rows + first, size)
        remote(
            full.at[at], full.at[at], ring_send.at[way, k, step], ring_recv.at[way, k, step], ring[way]
        ).wait_recv()
        keep(full.at[at], out.at[at], ring_keep.at[way, k, step])

    def ring_step(step):
        last = step == n // 2 - 1
        for k, (own, full, _, part) in enumerate(pieces):
            first, size = cuts[part]
            for way in (0, 1):
                block = ring_index(lax.rem(pos + (step if way else n - step), n), n)
                here = full.at[span(block * rows + first, size)]
                if step > 0:
                    arrived(k, way, step - 1, block)
                if last and part != way:
                    continue
                src = own.at[pl.ds(first, size)] if step == 0 else here
                go(src, here, ring_send.at[way, k, step], ring_recv.at[way, k, step], ring[way])

    def pass_on(k):
        _, full, out, part = sides[k]
        at = span(opposite * tokens + part * half, half)
        here = full.at[at]
        remote(here, here, over_send.at[k], over_recv.at[k], across).wait_recv()
        go(here, here, pass_send.at[k], pass_recv.at[k], beside)
        keep(here, out.at[at], over_keep.at[k])

    def send_over(k):
        own, full, _, part = sides[k]
        go(
            own.at[pl.ds(part * half, half)], full.at[span(me * tokens + part * half, half)],
            over_send.at[k], over_recv.at[k], across,
        )

    send_over(0)
    send_over(1)
    ring_step(0)
    for k, (own, full) in enumerate(((x_ref, xg), (cot_ref, cots))):
        go(own, full.at[span(me * tokens, tokens)], side_send.at[k], side_recv.at[k], beside)
    mine = ring_index(pos, n)
    keep(x_ref, xg_ref.at[span(me * tokens, tokens)], own_sem.at[0])
    keep(cot_ref, cots_ref.at[span(me * tokens, tokens)], own_sem.at[1])
    keep(w_ref, ws_ref.at[span(mine * rows, rows)], own_sem.at[2])
    keep(wo_ref, wos_ref.at[span(mine * rows, rows)], own_sem.at[3])
    for step in range(1, n // 2):
        ring_step(step)
        if step == 1:
            pass_on(0)
            pass_on(1)
            send_over(2)
            send_over(3)
    pass_on(2)
    pass_on(3)
    for k, piece in enumerate(pieces):
        arrived(k, piece[3], n // 2 - 1, ring_index(lax.rem(pos + n // 2, n), n))
    next_door = me + 1 - 2 * lax.rem(me, 2)
    far = lax.rem(next_door + 2, 4)
    for k, (full, out) in enumerate(((xg, xg_ref), (cots, cots_ref))):
        at = span(next_door * tokens, tokens)
        here = full.at[at]
        remote(here, here, side_send.at[k], side_recv.at[k], beside).wait_recv()
        keep(here, out.at[at], side_keep.at[k])
    for k, (_, full, out, part) in enumerate(sides):
        at = span(far * tokens + part * half, half)
        here = full.at[at]
        remote(here, here, pass_send.at[k], pass_recv.at[k], beside).wait_recv()
        keep(here, out.at[at], pass_keep.at[k])
    for copy in kept:
        copy.wait()
    for copy in started:
        copy.wait_send()


def gather_all(n, x, cot, w, wo):
    tokens, rows = x.shape[0], w.shape[0]
    dma = pltpu.SemaphoreType.DMA
    anywhere = pl.BlockSpec(memory_space=pl.ANY)
    inside = pl.BlockSpec(memory_space=pltpu.VMEM)
    shapes = [(a.shape[0] * k, a.shape[1]) for a, k in ((x, 4), (cot, 4), (w, n), (wo, n))]
    return pl.pallas_call(
        functools.partial(gather_body, n, rows, tokens),
        in_specs=[inside] * 4,
        out_specs=[anywhere] * 4,
        out_shape=[jax.ShapeDtypeStruct(shape, bf16) for shape in shapes],
        scratch_shapes=[
            *(pltpu.VMEM(shape, bf16) for shape in shapes),
            dma((4,)), dma((2, 4, n // 2)), dma((4,)), dma((2,)),
            dma((2, 4, n // 2)), dma((2, 4, n // 2)), dma((4,)), dma((4,)),
            dma((2,)), dma((2,)), dma((4,)), dma((4,)), dma((4,)),
        ],
        compiler_params=pltpu.CompilerParams(
            collective_id=0, has_side_effects=True, vmem_limit_bytes=48 * 2**20
        ),
        name="gather_all",
    )(x, cot, w, wo)


def reduce_body(
    n, rows, tokens, starts,
    gc_ref, go_ref, branch_ref, back_ref, small_ref,
    oc_ref, oo_ref, obranch_ref, oback_ref, bc_ref, osmall_ref,
    gc, go_, slots, held, near, over, smalls, tens, bc_slot,
    load_sem, ring_send, ring_recv, near_send, near_recv, over_send, over_recv,
    small_send, small_recv, ten_send, ten_recv, bc_send, bc_recv,
):
    pos, ring, me, across, beside = neighbours(n)
    enter((*ring, across, beside))
    cuts = cut_rows(rows)
    started = []

    def go(*args):
        copy = remote(*args)
        copy.start()
        started.append(copy)
        return copy

    core = lax.rem(me, 2)
    opposite = lax.rem(me + 2, 4)
    next_door = me + 1 - 2 * core
    far = lax.rem(next_door + 2, 4)
    half = tokens // 2
    items = [(gc_ref, gc, oc_ref, lo, hi) for lo, hi in starts] + [(go_ref, go_, oo_ref, 0, go_.shape[1])]

    def block_at(way, steps):
        return ring_index(lax.rem(pos + (steps if way else n - steps), n), n)

    for k, (src, _, _, lo, hi) in enumerate(items):
        for way in (0, 1):
            first, size = cuts[way]
            go(
                src.at[span(block_at(way, 1) * rows + first, size), pl.ds(lo, hi - lo)],
                slots[way][k].at[0],
                ring_send.at[way, k, 0], ring_recv.at[way, k, 0], ring[way],
            )
    sides = [(branch_ref, 0), (back_ref, 1)]
    for turn, target in ((0, far), (1, next_door)):
        for src, k in sides:
            for part in (0, 1):
                go(
                    src.at[span(target * tokens + part * half, half)],
                    near.at[k, turn, part],
                    near_send.at[k, turn, part], near_recv.at[k, turn, part], beside,
                )
    loads = {}
    for turn, target in ((0, opposite), (1, me)):
        for src, k in sides:
            for part in (0, 1):
                copy = pltpu.make_async_copy(
                    src.at[span(target * tokens + part * half, half)],
                    held.at[k, turn, part], load_sem.at[4 * turn + 2 * k + part],
                )
                copy.start()
                loads[k, turn, part] = copy
    for k, (src, dst) in enumerate(((gc_ref, gc), (go_ref, go_))):
        copy = pltpu.make_async_copy(src, dst, load_sem.at[8 + k])
        copy.start()
        loads["ring", k] = copy
    small_load = pltpu.make_async_copy(small_ref, smalls.at[pos], load_sem.at[10])
    small_load.start()

    def add_side(k, turn, part, dst):
        def some(i, _):
            at = span(i * 16, 16)
            total = held[k, turn, part, at, :].astype(f32) + near[k, turn, part, at, :].astype(f32)
            if dst is None:
                held[k, turn, part, at, :] = total.astype(bf16)
            else:
                dst[span(part * half + i * 16, 16), :] = total
            return 0

        lax.fori_loop(0, half // 16, some, 0)

    def near_ready(k, turn, part):
        loads[k, turn, part].wait()
        remote(
            near.at[k, turn, part], near.at[k, turn, part],
            near_send.at[k, turn, part], near_recv.at[k, turn, part], beside,
        ).wait_recv()

    for k in (0, 1):
        for part in (0, 1):
            near_ready(k, 0, part)
            add_side(k, 0, part, None)
            go(held.at[k, 0, part], over.at[k, part], over_send.at[k, part], over_recv.at[k, part], across)

    small_load.wait()
    loads["ring", 0].wait()
    loads["ring", 1].wait()
    outs = (obranch_ref, oback_ref)
    todo = [(k, part) for k in (0, 1) for part in (0, 1)]

    for step in range(n - 1):
        here = smalls.at[lax.rem(pos + n - step, n)]
        go(here, here, small_send.at[step], small_recv.at[step], ring[0])
        for k, (_, own, out, lo, hi) in enumerate(items):
            for way in (0, 1):
                first, size = cuts[way]
                slot = slots[way][k].at[step]
                remote(
                    slot, slot, ring_send.at[way, k, step], ring_recv.at[way, k, step], ring[way]
                ).wait_recv()
                block = block_at(way, 2 + step) if step < n - 2 else block_at(way, 0)

                def some(i, _, way=way, k=k, step=step, own=own, out=out, lo=lo, hi=hi, first=first, block=block):
                    total = slots[way][k][step, span(i * 16, 16), :].astype(f32)
                    total = total + own[span(block * rows + first + i * 16, 16), lo:hi].astype(f32)
                    if step < n - 2:
                        slots[way][k][step, span(i * 16, 16), :] = total.astype(bf16)
                    else:
                        out[span(first + i * 16, 16), lo:hi] = total
                    return 0

                lax.fori_loop(0, size // 16, some, 0)
                if step < n - 2:
                    go(
                        slot, slots[way][k].at[step + 1],
                        ring_send.at[way, k, step + 1], ring_recv.at[way, k, step + 1], ring[way],
                    )
            if step == n - 2 and k == 0:
                bc_slot[0] = oc_ref[:, starts[0][0] : starts[0][0] + 2 * NS]
                go(bc_slot.at[0], bc_slot.at[1], bc_send.at[0], bc_recv.at[0], beside)
        here = smalls.at[lax.rem(pos + 2 * n - step - 1, n)]
        remote(here, here, small_send.at[step], small_recv.at[step], ring[0]).wait_recv()
        if todo and step >= 1:
            k, part = todo.pop(0)
            near_ready(k, 1, part)
            add_side(k, 1, part, outs[k])
    for k, part in todo:
        near_ready(k, 1, part)
        add_side(k, 1, part, outs[k])

    total = smalls[0]
    for i in range(1, n):
        total = total + smalls[i]
    tens[me] = total
    go(tens.at[me], tens.at[me], ten_send.at[0], ten_recv.at[0], beside)
    remote(bc_slot.at[1], bc_slot.at[1], bc_send.at[0], bc_recv.at[0], beside).wait_recv()
    bc_slot[2] = bc_slot[0] + bc_slot[1]
    go(bc_slot.at[2], bc_slot.at[3], bc_send.at[1], bc_recv.at[1], across)
    here = tens.at[next_door]
    remote(here, here, ten_send.at[0], ten_recv.at[0], beside).wait_recv()
    for k, target in ((0, me), (1, next_door)):
        here = tens.at[target]
        go(here, here, ten_send.at[1 + k], ten_recv.at[1 + k], across)
    for k in (0, 1):
        for part in (0, 1):
            slot = over.at[k, part]
            remote(slot, slot, over_send.at[k, part], over_recv.at[k, part], across).wait_recv()

            def some(i, _, k=k, part=part):
                at = span(part * half + i * 16, 16)
                outs[k][at, :] = outs[k][at, :] + over[k, part, span(i * 16, 16), :].astype(f32)
                return 0

            lax.fori_loop(0, half // 16, some, 0)
    for k, target in ((0, opposite), (1, far)):
        here = tens.at[target]
        remote(here, here, ten_send.at[1 + k], ten_recv.at[1 + k], across).wait_recv()
    osmall_ref[...] = tens[...]
    remote(bc_slot.at[3], bc_slot.at[3], bc_send.at[1], bc_recv.at[1], across).wait_recv()
    bc_ref[...] = bc_slot[2] + bc_slot[3]
    for copy in started:
        copy.wait_send()


def reduce_all(n, grad_cat, grad_out, branch, back, small):
    rows, tokens = grad_cat.shape[0] // n, branch.shape[0] // 4
    wide, width = grad_cat.shape[1], grad_out.shape[1]
    starts = ((2 * width, wide), (0, 2 * width))
    widths = [hi - lo for lo, hi in starts] + [width]
    sizes = [size for _, size in cut_rows(rows)]
    half = tokens // 2
    dma, vm = pltpu.SemaphoreType.DMA, pltpu.VMEM
    anywhere = pl.BlockSpec(memory_space=pl.ANY)
    inside = pl.BlockSpec(memory_space=pltpu.VMEM)
    return pl.pallas_call(
        functools.partial(reduce_body, n, rows, tokens, starts),
        in_specs=[anywhere] * 5,
        out_specs=[inside] * 6,
        out_shape=[
            jax.ShapeDtypeStruct((rows, wide), f32),
            jax.ShapeDtypeStruct((rows, width), f32),
            jax.ShapeDtypeStruct((tokens, D), f32),
            jax.ShapeDtypeStruct((tokens, D), f32),
            jax.ShapeDtypeStruct((rows, 2 * NS), f32),
            jax.ShapeDtypeStruct((4, *small.shape), f32),
        ],
        scratch_shapes=[
            vm(grad_cat.shape, bf16), vm(grad_out.shape, bf16),
            [[vm((n - 1, size, w), bf16) for w in widths] for size in sizes],
            vm((2, 2, 2, half, D), bf16), vm((2, 2, 2, half, D), bf16), vm((2, 2, half, D), bf16),
            vm((n, *small.shape), f32), vm((4, *small.shape), f32), vm((4, rows, 2 * NS), f32),
            dma((11,)), dma((2, 3, n - 1)), dma((2, 3, n - 1)), dma((2, 2, 2)), dma((2, 2, 2)),
            dma((2, 2)), dma((2, 2)), dma((n - 1,)), dma((n - 1,)), dma((3,)), dma((3,)), dma((2,)), dma((2,)),
        ],
        compiler_params=pltpu.CompilerParams(
            collective_id=1, has_side_effects=True, vmem_limit_bytes=60 * 2**20
        ),
        name="reduce_all",
    )(grad_cat, grad_out, branch, back, small)


def adamw_step(weight, first, second, grad, rate, decay):
    first_new = beta_first * first + (1.0 - beta_first) * grad
    second_new = beta_second * second + (1.0 - beta_second) * grad * grad
    hat_first = first_new / (1.0 - beta_first**STEP)
    hat_second = second_new / (1.0 - beta_second**STEP)
    weight_new = weight - rate * (hat_first / (jnp.sqrt(hat_second) + adam_eps) + decay * weight)
    return (weight_new, first_new, second_new)


def local(
    layer_input,
    out_grad,
    small_params,
    small_first,
    small_second,
    w_zx,
    zx_first,
    zx_second,
    w_bc,
    bc_first,
    bc_second,
    w_dt,
    dt_first,
    dt_second,
    w_out,
    out_first,
    out_second,
):
    tensor_index = lax.axis_index("tensor")
    local_in = layer_input.astype(f32)
    gain_in, gate_gain, conv_x, bias_x, conv_bc, bias_bc, dt_bias, a_log, d_skip = unpack(
        small_params
    )
    rows_own = w_zx.shape[0]
    width = w_zx.shape[2]
    heads = w_dt.shape[1]
    chan_start = tensor_index * width
    head_start = tensor_index * heads
    gate_local = lax.dynamic_slice_in_dim(gate_gain, chan_start, width, 0)
    conv_local = lax.dynamic_slice_in_dim(conv_x, chan_start, width, 1)
    bias_local = lax.dynamic_slice_in_dim(bias_x, chan_start, width, 0)
    dtb_local = lax.dynamic_slice_in_dim(dt_bias, head_start, heads, 0)
    a_local = -jnp.exp(lax.dynamic_slice_in_dim(a_log, head_start, heads, 0))
    dskip_local = lax.dynamic_slice_in_dim(d_skip, head_start, heads, 0)
    taps = jnp.concatenate(
        [
            jnp.concatenate([conv_local, conv_bc], axis=1),
            jnp.concatenate([bias_local, bias_bc])[None, :],
            jnp.zeros((8 - CONV - 1, width + 2 * NS), f32),
        ],
        axis=0,
    )
    lanes = lambda v: jnp.pad(v, (0, LANES - heads))
    head = jnp.pad(jnp.stack([lanes(dtb_local), lanes(a_local)]), ((0, 6), (0, 0)))
    chan = jnp.pad(jnp.stack([gate_local, jnp.repeat(dskip_local, P_SIZE)]), ((0, 6), (0, 0)))
    pick = jnp.asarray(
        (jnp.arange(width)[:, None] // P_SIZE == jnp.arange(LANES)[None, :]), bf16
    )

    inv_in = lax.rsqrt(jnp.mean(local_in * local_in, axis=-1, keepdims=True) + norm_eps)
    normed_in = local_in * inv_in * gain_in[None, :]
    w_cat = jnp.concatenate(
        [
            w_zx.reshape(rows_own, 2 * width).astype(bf16),
            w_bc.astype(bf16),
            jnp.pad(w_dt, ((0, 0), (0, LANES - heads))).astype(bf16),
        ],
        axis=1,
    )
    n = lax.axis_size("dp")
    xg, cot_all, w_all, wo_all = gather_all(
        n, normed_in.astype(bf16), out_grad, w_cat, w_out.astype(bf16)
    )

    z, v, xc, dr, y, dn, st, red = ssd_forward(xg, w_all, cot_all, wo_all, taps, head, chan)
    sums = lax.psum(red[::8], "tensor")
    red = jnp.repeat(sums, 8, axis=0)
    normed_low, d_cat, acc, hacc = ssd_backward(z, v, xc, dr, y, dn, st, red, taps, head, chan, pick)

    branch = mm(normed_low, wo_all, NT).astype(bf16)
    grad_out = mm(cot_all, normed_low, TN).astype(bf16)
    back = mm(d_cat, w_all, NT)
    gain_part = jnp.sum(xg.astype(f32) * back, axis=0) / gain_in
    grad_cat = mm(xg, d_cat, TN).astype(bf16)
    acc = jnp.sum(acc, axis=1)
    hacc = jnp.sum(hacc, axis=1)
    skip_part = jnp.sum(acc[CONV + 2, :width].reshape(heads, P_SIZE), axis=1)
    small = jnp.concatenate(
        [
            acc[: CONV + 1].reshape(-1), acc[CONV + 1, :width], hacc[0], hacc[1],
            gain_part, jnp.pad(skip_part, (0, 4 * LANES - heads)),
        ]
    ).reshape(8, width + 2 * NS)
    owner_cat, owner_out, own_branch, d_normed_in, owner_bc, tens = reduce_all(
        n, grad_cat, grad_out, branch, back.astype(bf16), small
    )
    layer_output = (local_in + own_branch).astype(bf16)
    owner_zx = owner_cat[:, : 2 * width].reshape(rows_own, 2, width)
    owner_dt = owner_cat[:, 2 * width + 2 * NS : 2 * width + 2 * NS + heads]

    inner_in = jnp.sum(local_in * gain_in[None, :] * d_normed_in, axis=-1, keepdims=True)
    input_grad = (
        out_grad.astype(f32)
        + inv_in * gain_in[None, :] * d_normed_in
        - local_in * (inv_in * inv_in * inv_in * inner_in / D)
    )
    gain_sum = jnp.sum(tens[:, 6:8], axis=0).reshape(-1)[:D]
    bc_sum = jnp.sum(tens[:, : CONV + 1, width:], axis=0)
    small_grad = jnp.concatenate(
        [
            gain_sum,
            tens[:, CONV + 1, :width].reshape(-1),
            jnp.moveaxis(tens[:, :CONV, :width], 0, 1).reshape(-1),
            tens[:, CONV, :width].reshape(-1),
            bc_sum.reshape(-1),
            tens[:, CONV + 1, width : width + heads].reshape(-1),
            tens[:, CONV + 1, width + LANES : width + LANES + heads].reshape(-1) * -jnp.exp(a_log),
            tens[:, 7, 512 : 512 + heads].reshape(-1),
        ]
    )
    small_new, small_first_new, small_second_new = adamw_step(
        small_params, small_first, small_second, small_grad, small_rate, 0.0
    )
    zx_new, zx_first_new, zx_second_new = adamw_step(
        w_zx, zx_first, zx_second, owner_zx, matrix_rate, matrix_decay
    )
    bc_new, bc_first_new, bc_second_new = adamw_step(
        w_bc, bc_first, bc_second, owner_bc, matrix_rate, matrix_decay
    )
    dt_new, dt_first_new, dt_second_new = adamw_step(
        w_dt, dt_first, dt_second, owner_dt, matrix_rate, matrix_decay
    )
    out_new, out_first_new, out_second_new = adamw_step(
        w_out, out_first, out_second, owner_out, matrix_rate, matrix_decay
    )
    return (
        layer_output,
        input_grad,
        small_new,
        small_first_new,
        small_second_new,
        zx_new,
        zx_first_new,
        zx_second_new,
        bc_new,
        bc_first_new,
        bc_second_new,
        dt_new,
        dt_first_new,
        dt_second_new,
        out_new,
        out_first_new,
        out_second_new,
    )


def solution(mesh):
    return jax.shard_map(
        local,
        mesh=mesh,
        in_specs=(
            P(("dp", "tensor"), None),
            P(("dp", "tensor"), None),
            P(),
            P(),
            P(),
            P("dp", None, "tensor"),
            P("dp", None, "tensor"),
            P("dp", None, "tensor"),
            P("dp", None),
            P("dp", None),
            P("dp", None),
            P("dp", "tensor"),
            P("dp", "tensor"),
            P("dp", "tensor"),
            P("dp", "tensor"),
            P("dp", "tensor"),
            P("dp", "tensor"),
        ),
        out_specs=(
            P(("dp", "tensor"), None),
            P(("dp", "tensor"), None),
            P(),
            P(),
            P(),
            P("dp", None, "tensor"),
            P("dp", None, "tensor"),
            P("dp", None, "tensor"),
            P("dp", None),
            P("dp", None),
            P("dp", None),
            P("dp", "tensor"),
            P("dp", "tensor"),
            P("dp", "tensor"),
            P("dp", "tensor"),
            P("dp", "tensor"),
            P("dp", "tensor"),
        ),
        check_vma=False,
    )
```

```python
import functools

import jax
import jax.numpy as jnp
from jax import lax
from jax.experimental import pallas as pl
from jax.experimental.pallas import tpu as pltpu
from jax.sharding import PartitionSpec as P

D = 1536
DI = 3072
H = 48
NS = 128
P_SIZE = 64
CONV = 4
LEN = 2048
STEP = 10

T = 128
ROWS = 256
LANES = 128

norm_eps = 1e-05
adam_eps = 1e-08
beta_first = 0.9
beta_second = 0.95
matrix_rate = 0.01
small_rate = 0.1
matrix_decay = 0.1

f32 = jnp.float32
bf16 = jnp.bfloat16
NN = (((1,), (0,)), ((), ()))
NT = (((1,), (1,)), ((), ()))
TN = (((0,), (0,)), ((), ()))
HIGHEST = lax.Precision.HIGHEST


def unpack(flat):
    gain_in = flat[:D]
    cursor = D
    gate_gain = flat[cursor : cursor + DI]
    cursor = cursor + DI
    conv_x = flat[cursor : cursor + CONV * DI].reshape(CONV, DI)
    cursor = cursor + CONV * DI
    bias_x = flat[cursor : cursor + DI]
    cursor = cursor + DI
    conv_bc = flat[cursor : cursor + CONV * 2 * NS].reshape(CONV, 2 * NS)
    cursor = cursor + CONV * 2 * NS
    bias_bc = flat[cursor : cursor + 2 * NS]
    cursor = cursor + 2 * NS
    dt_bias = flat[cursor : cursor + H]
    a_log = flat[cursor + H : cursor + 2 * H]
    d_skip = flat[cursor + 2 * H : cursor + 3 * H]
    return (gain_in, gate_gain, conv_x, bias_x, conv_bc, bias_bc, dt_bias, a_log, d_skip)


def mm(a, b, dims=NN):
    return lax.dot_general(a, b, dims, preferred_element_type=f32)


def mm_exact(a, b, dims=NN):
    return lax.dot_general(a, b, dims, preferred_element_type=f32, precision=HIGHEST)


def sigmoid(v):
    return 0.5 * jnp.tanh(0.5 * v) + 0.5


def softplus(v):
    return jnp.maximum(v, 0.0) + jnp.log1p(jnp.exp(-jnp.abs(v)))


def spread(col):
    return jnp.broadcast_to(col, (T, LANES))


def block_iota(axis):
    return lax.broadcasted_iota(jnp.int32, (T, LANES), axis)


def head_rows(dr_ref, head_ref, rows):
    raw = dr_ref[rows, :] + head_ref[0:1, :]
    dt = softplus(raw)
    low_tri = jnp.where(block_iota(0) >= block_iota(1), 1.0, 0.0).astype(f32)
    decay = mm_exact(low_tri, dt * head_ref[1:2, :])
    return raw, dt, decay


def ring_place(n):
    me = lax.axis_index("dp")
    z, x = lax.div(me, 2), lax.rem(me, 2)
    return z + x * (n - 1 - 2 * z)


def ring_index(pos, n):
    back = lax.div(pos, n // 2)
    return 2 * pos + back * (2 * n - 1 - 4 * pos)


def neighbours(n):
    pos = ring_place(n)
    right = ring_index(lax.rem(pos + 1, n), n)
    left = ring_index(lax.rem(pos + n - 1, n), n)
    me = lax.axis_index("tensor")
    y, core = lax.div(me, 2), lax.rem(me, 2)
    across = 2 * (1 - y) + core
    beside = 2 * y + 1 - core
    return pos, ({"dp": right}, {"dp": left}), me, {"tensor": across}, {"tensor": beside}


def enter(peers):
    barrier = pltpu.get_barrier_semaphore()
    for peer in peers:
        pl.semaphore_signal(barrier, inc=1, device_id=peer, device_id_type=pl.DeviceIdType.MESH)
    pl.semaphore_wait(barrier, len(peers))


def remote(src, dst, send_sem, recv_sem, peer):
    return pltpu.make_async_remote_copy(
        src_ref=src, dst_ref=dst, send_sem=send_sem, recv_sem=recv_sem,
        device_id=peer, device_id_type=pl.DeviceIdType.MESH,
    )


def span(start, size):
    return pl.ds(pl.multiple_of(start, 16), size)


def cut_rows(rows):
    top = rows // 32 * 16
    return ((0, top), (top, rows - top))


def forward_body(
    n, rows, tokens, width,
    xg_ref, w_ref, taps_ref, head_ref, chan_ref, cot_ref, wo_ref,
    z_ref, v_ref, xc_ref, dr_ref, y_ref, dn_ref, st_ref, red_ref, cots_ref, wos_ref,
    halo, state, gated_all, cots, wos, sums,
    own_keep, ring_keep, over_keep, side_keep, pass_keep, ring_send, ring_recv, over_send, over_recv,
    side_send, side_recv, pass_send, pass_recv, sum_send, sum_recv,
):
    pairs = width // LANES
    wide = width + 2 * NS
    step = pl.program_id(0)
    steps = LEN // ROWS
    pos, ring, me, across, beside = neighbours(n)
    opposite = lax.rem(me + 2, 4)
    next_door = me + 1 - 2 * lax.rem(me, 2)
    far = lax.rem(next_door + 2, 4)
    half = tokens // 2
    hops = n // 2
    cuts = cut_rows(rows)
    mine = ring_index(pos, n)

    def hop(part, way, h):
        first, size = cuts[part]
        block = ring_index(lax.rem(pos + (h if way else n - h), n), n)
        here = wos.at[span(block * rows + first, size)]
        src = wo_ref.at[pl.ds(first, size)] if h == 0 else here
        return remote(src, here, ring_send.at[way, part, h], ring_recv.at[way, part, h], ring[way])

    def hop_lands(part, way, h):
        first, size = cuts[part]
        block = ring_index(lax.rem(pos + (h + 1 if way else n - h - 1), n), n)
        return span(block * rows + first, size)

    def hop_arrival(part, way, h):
        here = wos.at[hop_lands(part, way, h)]
        return remote(here, here, ring_send.at[way, part, h], ring_recv.at[way, part, h], ring[way])

    def hop_keep(part, way, h):
        at = hop_lands(part, way, h)
        return pltpu.make_async_copy(wos.at[at], wos_ref.at[at], ring_keep.at[way, part, h])

    def hop_ways(h):
        return [(part, way) for part in (0, 1) for way in (0, 1) if h < hops - 1 or part == way]

    def over(k):
        return remote(
            cot_ref.at[pl.ds(k * half, half)], cots.at[span(me * tokens + k * half, half)],
            over_send.at[k], over_recv.at[k], across,
        )

    def landed(full, start, size, send, recv, peer):
        here = full.at[span(start, size)]
        return remote(here, here, send, recv, peer)

    def over_arrival(k):
        start = opposite * tokens + k * half
        return landed(cots, start, half, over_send.at[k], over_recv.at[k], across)

    def passing(k):
        start = opposite * tokens + k * half
        return landed(cots, start, half, pass_send.at[k], pass_recv.at[k], beside)

    def pass_arrival(k):
        return landed(cots, far * tokens + k * half, half, pass_send.at[k], pass_recv.at[k], beside)

    def side():
        return remote(cot_ref, cots.at[span(me * tokens, tokens)], side_send.at[0], side_recv.at[0], beside)

    def side_arrival():
        return landed(cots, next_door * tokens, tokens, side_send.at[0], side_recv.at[0], beside)

    def keep(start, size, sem):
        return pltpu.make_async_copy(cots.at[span(start, size)], cots_ref.at[span(start, size)], sem)

    def own_keeps():
        return (
            pltpu.make_async_copy(cot_ref, cots_ref.at[span(me * tokens, tokens)], own_keep.at[0]),
            pltpu.make_async_copy(wo_ref, wos_ref.at[span(mine * rows, rows)], own_keep.at[1]),
            pltpu.make_async_copy(cot_ref, cots.at[span(me * tokens, tokens)], own_keep.at[2]),
            pltpu.make_async_copy(wo_ref, wos.at[span(mine * rows, rows)], own_keep.at[3]),
        )

    @pl.when(step == 0)
    def _():
        enter((*ring, across, beside))
        over(0).start()
        over(1).start()
        for part, way in hop_ways(0):
            hop(part, way, 0).start()
        side().start()
        for copy in own_keeps():
            copy.start()
        halo[0:8, :] = jnp.zeros((8, wide), f32)
        state[...] = jnp.zeros_like(state)

    for h in range(1, hops):

        @pl.when(step == min(2 * h, steps - 1))
        def _(h=h):
            for part, way in hop_ways(h - 1):
                hop_arrival(part, way, h - 1).wait_recv()
                hop_keep(part, way, h - 1).start()
                if (part, way) in hop_ways(h):
                    hop(part, way, h).start()

    @pl.when(step == steps - 1)
    def _():
        for k in (0, 1):
            over_arrival(k).wait_recv()
            passing(k).start()
            keep(opposite * tokens + k * half, half, over_keep.at[k]).start()

    @pl.when(step == steps)
    def _():
        for part, way in hop_ways(hops - 1):
            hop_arrival(part, way, hops - 1).wait_recv()
            hop_keep(part, way, hops - 1).start()
        side_arrival().wait_recv()
        keep(next_door * tokens, tokens, side_keep.at[0]).start()
        for k in (0, 1):
            pass_arrival(k).wait_recv()
            keep(far * tokens + k * half, half, pass_keep.at[k]).start()
        for copy in own_keeps():
            copy.wait()

    @pl.when(step < steps)
    def _():
        scan_step(
            width, step, xg_ref, w_ref, taps_ref, head_ref, chan_ref,
            z_ref, v_ref, xc_ref, dr_ref, y_ref, st_ref, halo, state, gated_all, sums,
        )

    @pl.when(step >= steps)
    def _():
        at = span((step - steps) * ROWS, ROWS)
        dn_ref[...] = mm(cots[at, :], wos[...])
        inner = jnp.zeros((ROWS, LANES), f32)
        for p in range(pairs):
            cols = slice(p * LANES, (p + 1) * LANES)
            inner = inner + gated_all[at, cols] * chan_ref[0:1, cols] * dn_ref[:, cols]
        lanes = pl.ds(pl.multiple_of((step - steps) * ROWS, ROWS), ROWS)
        sums[0, 4:8, lanes] = mm_exact(jnp.ones((8, LANES), f32), inner, NT)[4:8]

    @pl.when(step == 2 * steps - 1)
    def _():
        first = remote(sums.at[0], sums.at[1], sum_send.at[0], sum_recv.at[0], beside)
        first.start()
        first.wait_recv()
        sums[2] = sums[0] + sums[1]
        second = remote(sums.at[2], sums.at[3], sum_send.at[1], sum_recv.at[1], across)
        second.start()
        for h in range(hops):
            for part, way in hop_ways(h):
                hop(part, way, h).wait_send()
                hop_keep(part, way, h).wait()
        side().wait_send()
        keep(next_door * tokens, tokens, side_keep.at[0]).wait()
        for k in (0, 1):
            over(k).wait_send()
            passing(k).wait_send()
            keep(opposite * tokens + k * half, half, over_keep.at[k]).wait()
            keep(far * tokens + k * half, half, pass_keep.at[k]).wait()
        first.wait_send()
        second.wait()
        red_ref[...] = sums[2] + sums[3]


def scan_step(
    width, step, xg_ref, w_ref, taps_ref, head_ref, chan_ref,
    z_ref, v_ref, xc_ref, dr_ref, y_ref, st_ref, halo, state, gated_all, sums,
):
    pairs = width // LANES
    wide = width + 2 * NS
    dr_ref[...] = mm(xg_ref[...], w_ref[:, width + wide :])
    halo[8 : 8 + ROWS, :] = mm(xg_ref[...], w_ref[:, width : width + wide])
    z_ref[...] = mm(xg_ref[...], w_ref[:, :width])
    low_half = block_iota(1) < P_SIZE
    causal = block_iota(0) >= block_iota(1)

    def convolved(sub, block):
        cols = slice(block * LANES, (block + 1) * LANES)
        total = taps_ref[CONV : CONV + 1, cols]
        for k in range(CONV):
            first = 8 - (CONV - 1) + k + sub * T
            total = total + taps_ref[k : k + 1, cols] * halo[first : first + T, cols]
        rows = slice(sub * T, (sub + 1) * T)
        xc_ref[rows, cols] = total
        v_ref[rows, cols] = halo[8 + sub * T : 8 + (sub + 1) * T, cols].astype(bf16)
        return total * sigmoid(total)

    for sub in range(ROWS // T):
        rows = slice(sub * T, (sub + 1) * T)
        raw, dt, decay = head_rows(dr_ref, head_ref, rows)
        decay_t = decay.T
        b_low = convolved(sub, pairs).astype(bf16)
        c_low = convolved(sub, pairs + 1).astype(bf16)
        b_t = b_low.T
        scores = jnp.where(causal, mm(c_low, b_low, NT), 0.0)
        squares = jnp.zeros((T, LANES), f32)
        st_ref[sub] = state[...].astype(bf16)
        for p in range(pairs):
            cols = slice(p * LANES, (p + 1) * LANES)
            x = convolved(sub, p)
            l1, l2 = spread(decay[:, 2 * p : 2 * p + 1]), spread(decay[:, 2 * p + 1 : 2 * p + 2])
            both = jnp.where(low_half, l1, l2)
            dtb = jnp.where(
                low_half, spread(dt[:, 2 * p : 2 * p + 1]), spread(dt[:, 2 * p + 1 : 2 * p + 2])
            )
            u = x * dtb
            m1 = scores * jnp.exp(jnp.minimum(l1 - decay_t[2 * p : 2 * p + 1, :], 0.0))
            m2 = scores * jnp.exp(jnp.minimum(l2 - decay_t[2 * p + 1 : 2 * p + 2, :], 0.0))
            mixing = jnp.concatenate([m1.astype(bf16), m2.astype(bf16)], axis=1)
            parts = jnp.concatenate(
                [jnp.where(low_half, u, 0.0).astype(bf16), jnp.where(low_half, 0.0, u).astype(bf16)],
                axis=0,
            )
            last = both[T - 1 : T, :]
            entering = st_ref[sub, :, cols]
            y = mm(mixing, parts) + jnp.exp(both) * mm(c_low, entering) + chan_ref[1:2, cols] * x
            tail = (u * jnp.exp(last - both)).astype(bf16)
            state[:, cols] = jnp.exp(last) * state[:, cols] + mm(b_t, tail)
            y_ref[rows, cols] = y
            z = z_ref[rows, cols]
            gated = y * (z * sigmoid(z))
            gated_all[span(step * ROWS + sub * T, T), cols] = gated
            squares = squares + gated * gated
        lanes = pl.ds(pl.multiple_of(step * ROWS + sub * T, T), T)
        sums[0, 0:4, lanes] = mm_exact(jnp.ones((8, LANES), f32), squares, NT)[0:4]
    halo[0:8, :] = halo[ROWS : ROWS + 8, :]


def ssd_forward(n, xg, w_cat, taps, head, chan, cot, wo):
    length = xg.shape[0]
    rows, width = wo.shape
    tokens = cot.shape[0]
    wide = width + 2 * NS
    steps = length // ROWS
    subs = ROWS // T
    assert length == LEN
    early = lambda i: jnp.minimum(i, steps - 1)
    row = lambda m: pl.BlockSpec((ROWS, m), lambda i: (early(i), 0))
    whole = lambda a: pl.BlockSpec(a.shape, lambda i: (0,) * a.ndim, pipeline_mode=pl.Buffered(1))
    anywhere = pl.BlockSpec(memory_space=pl.ANY)
    vm, dma = pltpu.VMEM, pltpu.SemaphoreType.DMA
    hops = dma((2, 2, n // 2))
    return pl.pallas_call(
        functools.partial(forward_body, n, rows, tokens, width),
        grid=(2 * steps,),
        in_specs=[row(D), whole(w_cat), whole(taps), whole(head), whole(chan), whole(cot), whole(wo)],
        out_specs=[
            row(width), row(wide), row(wide), row(LANES), row(width),
            pl.BlockSpec((ROWS, width), lambda i: (jnp.maximum(i - steps, 0), 0)),
            pl.BlockSpec((subs, NS, width), lambda i: (early(i), 0, 0)),
            pl.BlockSpec((8, length), lambda i: (0, 0)),
            anywhere, anywhere,
        ],
        out_shape=[
            jax.ShapeDtypeStruct((length, width), f32),
            jax.ShapeDtypeStruct((length, wide), bf16),
            jax.ShapeDtypeStruct((length, wide), f32),
            jax.ShapeDtypeStruct((length, LANES), f32),
            jax.ShapeDtypeStruct((length, width), f32),
            jax.ShapeDtypeStruct((length, width), f32),
            jax.ShapeDtypeStruct((length // T, NS, width), bf16),
            jax.ShapeDtypeStruct((8, length), f32),
            jax.ShapeDtypeStruct((4 * tokens, D), bf16),
            jax.ShapeDtypeStruct((n * rows, width), bf16),
        ],
        scratch_shapes=[
            vm((ROWS + 8, wide), f32), vm((NS, width), f32), vm((length, width), f32),
            vm((4 * tokens, D), bf16), vm((n * rows, width), bf16), vm((4, 8, length), f32),
            dma((4,)), hops, dma((2,)), dma((1,)), dma((2,)), hops, hops, dma((2,)), dma((2,)),
            dma((1,)), dma((1,)), dma((2,)), dma((2,)), dma((2,)), dma((2,)),
        ],
        compiler_params=pltpu.CompilerParams(
            collective_id=2, has_side_effects=True, vmem_limit_bytes=58 * 2**20
        ),
        name="layer_forward",
    )(xg, w_cat, taps, head, chan, cot, wo)


def backward_body(
    width,
    z_ref, v_ref, xc_ref, dr_ref, y_ref, dn_ref, st_ref, red_ref, taps_ref, head_ref, chan_ref, pick_ref,
    nl_ref, d_ref, acc_ref, hacc_ref,
    dxh, dstate, yst, bds, dyeb, utb, gin, gout, xdu, turn,
):
    pairs = width // LANES
    wide = width + 2 * NS
    step = pl.program_id(0)

    @pl.when(step == 0)
    def _():
        dxh[T : T + 8, :] = jnp.zeros((8, wide), f32)
        dstate[...] = jnp.zeros_like(dstate)
        acc_ref[...] = jnp.zeros_like(acc_ref)
        hacc_ref[...] = jnp.zeros_like(hacc_ref)
        turn[...] = jnp.zeros_like(turn)

    low_half = block_iota(1) < P_SIZE
    row_at, col_at = block_iota(0), block_iota(1)
    until = row_at <= col_at
    before = row_at < col_at
    upper = jnp.where(until, 1.0, 0.0).astype(f32)
    strict = jnp.where(before, 1.0, 0.0).astype(f32)
    low_tri = jnp.where(row_at >= col_at, 1.0, 0.0).astype(bf16)

    def add(index, cols, value):
        acc_ref[index, :, cols] += jnp.sum(value.reshape(T // 8, 8, LANES), axis=0)

    def conv_back(rows, block, d_act, xc, s, act):
        cols = slice(block * LANES, (block + 1) * LANES)
        dxh[0:T, cols] = d_act * (s + act * (1.0 - s))
        v = v_ref[rows, cols].astype(f32)
        total = None
        for m in range(CONV):
            moved = dxh[m : m + T, cols]
            if m == 0:
                add(CONV, cols, moved)
            add(CONV - 1 - m, cols, v * moved)
            term = taps_ref[CONV - 1 - m : CONV - m, cols] * moved
            total = term if total is None else total + term
        d_ref[rows, width + block * LANES : width + (block + 1) * LANES] = total.astype(bf16)

    for sub in reversed(range(ROWS // T)):
        rows = slice(sub * T, (sub + 1) * T)
        raw, dt, decay = head_rows(dr_ref, head_ref, rows)
        decay_t = decay.T
        sums = red_ref[:, rows]
        q_row = lax.rsqrt(sums[0:4] / DI + norm_eps)
        k_row = q_row * q_row * q_row * sums[4:8] / DI
        turned = jnp.concatenate([q_row, k_row], axis=0).T
        q = spread(turned[:, 0:1])
        kk = spread(turned[:, 4:5])
        b_cols = slice(width, width + NS)
        c_cols = slice(width + NS, width + 2 * NS)
        b_xc, c_xc = xc_ref[rows, b_cols], xc_ref[rows, c_cols]
        b_s, c_s = sigmoid(b_xc), sigmoid(c_xc)
        b_act, c_act = b_xc * b_s, c_xc * c_s
        b_low, c_low = b_act.astype(bf16), c_act.astype(bf16)
        c_t = c_low.T
        scores_t = jnp.where(until, mm(b_low, c_low, NT), 0.0)
        ds_low = dstate[...].astype(bf16)
        yst[...] = mm(c_low, st_ref[sub])
        bds[...] = mm(b_low, ds_low)
        d_scores = jnp.zeros((T, LANES), f32)
        for p in range(pairs):
            cols = slice(p * LANES, (p + 1) * LANES)
            z, y, dn = z_ref[rows, cols], y_ref[rows, cols], dn_ref[rows, cols]
            gain = chan_ref[0:1, cols]
            s = sigmoid(z)
            sz = z * s
            gated = y * sz
            gq = gated * q
            dg = q * gain * dn - gated * kk
            add(CONV + 1, cols, gq * dn)
            nl_ref[rows, cols] = (gq * gain).astype(bf16)
            d_ref[rows, cols] = (dg * y * (s + sz * (1.0 - s))).astype(bf16)
            dy = dg * sz
            xc = xc_ref[rows, cols]
            xs = sigmoid(xc)
            x = xc * xs
            l1, l2 = spread(decay[:, 2 * p : 2 * p + 1]), spread(decay[:, 2 * p + 1 : 2 * p + 2])
            both = jnp.where(low_half, l1, l2)
            dtb = jnp.where(
                low_half, spread(dt[:, 2 * p : 2 * p + 1]), spread(dt[:, 2 * p + 1 : 2 * p + 2])
            )
            u = x * dtb
            last = both[T - 1 : T, :]
            e1 = jnp.exp(jnp.minimum(decay_t[2 * p : 2 * p + 1, :] - l1, 0.0))
            e2 = jnp.exp(jnp.minimum(decay_t[2 * p + 1 : 2 * p + 2, :] - l2, 0.0))
            dy_low = dy.astype(bf16)
            zero = jnp.zeros_like(dy_low)
            u_low = u.astype(bf16)
            du_in = mm(
                jnp.concatenate([(scores_t * e1).astype(bf16), (scores_t * e2).astype(bf16)], axis=1),
                jnp.concatenate(
                    [jnp.where(low_half, dy_low, zero), jnp.where(low_half, zero, dy_low)], axis=0
                ),
            )
            d_mix = mm(
                jnp.concatenate(
                    [jnp.where(low_half, u_low, zero), jnp.where(low_half, zero, u_low)], axis=0
                ),
                dy_low,
                NT,
            )
            d1, d2 = d_mix[:T] * e1, d_mix[T:] * e2
            d_scores = d_scores + d1 + d2
            reach = mm(
                jnp.concatenate([(d1 * scores_t).astype(bf16), (d2 * scores_t).astype(bf16)], axis=0),
                low_tri,
            )
            turn[2 * p : 2 * p + 1, :] = jnp.sum(jnp.where(before, reach[:T], 0.0), axis=0, keepdims=True)
            turn[2 * p + 1 : 2 * p + 2, :] = jnp.sum(
                jnp.where(before, reach[T:], 0.0), axis=0, keepdims=True
            )
            tail = jnp.exp(last - both)
            dye = dy * jnp.exp(both)
            du_out = tail * bds[:, cols]
            du = du_in + du_out
            gin[:, cols] = (dye * yst[:, cols]).astype(bf16)
            gout[:, cols] = (u * du_out).astype(bf16)
            xdu[:, cols] = (x * du).astype(bf16)
            dyeb[:, cols] = dye.astype(bf16)
            utb[:, cols] = (u * tail).astype(bf16)
            add(CONV + 2, cols, dy * x)
            conv_back(rows, p, dtb * du + chan_ref[1:2, cols] * dy, xc, xs, x)
        d_scores = jnp.where(until, d_scores, 0.0).astype(bf16)
        d_b = mm(d_scores, c_low) + mm(utb[...], ds_low, NT)
        d_c = mm(d_scores, b_low, TN) + mm(dyeb[...], st_ref[sub], NT)
        conv_back(rows, pairs, d_b, b_xc, b_s, b_act)
        conv_back(rows, pairs + 1, d_c, c_xc, c_s, c_act)
        ended = jnp.zeros((1, LANES), f32)
        for p in range(pairs):
            cols = slice(p * LANES, (p + 1) * LANES)
            last = jnp.where(
                low_half[0:1], decay[T - 1 : T, 2 * p : 2 * p + 1], decay[T - 1 : T, 2 * p + 1 : 2 * p + 2]
            )
            fade = jnp.exp(last)
            before_ds = dstate[:, cols]
            through = jnp.sum(before_ds * st_ref[sub, :, cols].astype(f32), axis=0, keepdims=True) * fade
            ended = ended + mm_exact(through, pick_ref[cols, :].astype(f32))
            dstate[:, cols] = fade * before_ds + mm(c_t, dyeb[:, cols])
        gin_heads = mm(gin[...], pick_ref[...])
        gout_heads = mm(gout[...], pick_ref[...])
        reached = (
            turn[...].T
            + mm_exact(upper, gin_heads)
            + mm_exact(strict, gout_heads, TN)
            + ended
        )
        d_raw = (head_ref[1:2, :] * reached + mm(xdu[...], pick_ref[...])) * sigmoid(raw)
        d_ref[rows, width + wide :] = d_raw.astype(bf16)
        hacc_ref[0] += jnp.sum(d_raw.reshape(T // 8, 8, LANES), axis=0)
        hacc_ref[1] += jnp.sum((dt * reached).reshape(T // 8, 8, LANES), axis=0)
        dxh[T : T + 8, :] = dxh[0:8, :]


def ssd_backward(z, v, xc, dr, y, dn, st, red, taps, head, chan, pick):
    tokens, width = z.shape
    wide = width + 2 * NS
    steps = tokens // ROWS
    subs = ROWS // T
    row = lambda n: pl.BlockSpec((ROWS, n), lambda i: (steps - 1 - i, 0))
    whole = lambda a: pl.BlockSpec(a.shape, lambda i: (0,) * a.ndim, pipeline_mode=pl.Buffered(1))
    total = width + wide + LANES
    vm = pltpu.VMEM
    return pl.pallas_call(
        functools.partial(backward_body, width),
        grid=(steps,),
        in_specs=[
            row(width), row(wide), row(wide), row(LANES), row(width), row(width),
            pl.BlockSpec((subs, NS, width), lambda i: (steps - 1 - i, 0, 0)),
            pl.BlockSpec((8, ROWS), lambda i: (0, steps - 1 - i)),
            whole(taps), whole(head), whole(chan), whole(pick),
        ],
        out_specs=[
            row(width), row(total),
            pl.BlockSpec((CONV + 3, 8, wide), lambda i: (0, 0, 0)),
            pl.BlockSpec((2, 8, LANES), lambda i: (0, 0, 0)),
        ],
        out_shape=[
            jax.ShapeDtypeStruct((tokens, width), bf16),
            jax.ShapeDtypeStruct((tokens, total), bf16),
            jax.ShapeDtypeStruct((CONV + 3, 8, wide), f32),
            jax.ShapeDtypeStruct((2, 8, LANES), f32),
        ],
        scratch_shapes=[
            vm((T + 8, wide), f32), vm((NS, width), f32), vm((T, width), f32), vm((T, width), f32),
            vm((T, width), bf16), vm((T, width), bf16), vm((T, width), bf16), vm((T, width), bf16),
            vm((T, width), bf16), vm((T, LANES), f32),
        ],
        compiler_params=pltpu.CompilerParams(vmem_limit_bytes=56 * 2**20),
        name="layer_backward",
    )(z, v, xc, dr, y, dn, st, red, taps, head, chan, pick)


def gather_body(
    n, rows, tokens,
    x_ref, w_ref, xg_ref, ws_ref, xg, ws,
    keep_sem, ring_keep, ring_send, ring_recv, over_send, over_recv, side_send, side_recv, pass_send, pass_recv,
):
    pos, ring, me, across, beside = neighbours(n)
    enter((*ring, across, beside))
    half = tokens // 2
    started, kept = [], []

    def go(*args):
        copy = remote(*args)
        copy.start()
        started.append(copy)

    def keep(src, dst, sem):
        copy = pltpu.make_async_copy(src, dst, sem)
        copy.start()
        kept.append(copy)

    opposite = lax.rem(me + 2, 4)
    next_door = me + 1 - 2 * lax.rem(me, 2)
    far = lax.rem(next_door + 2, 4)
    cuts = cut_rows(rows)

    def arrived(part, way, step, block):
        first, size = cuts[part]
        at = span(block * rows + first, size)
        remote(
            ws.at[at], ws.at[at], ring_send.at[way, part, step], ring_recv.at[way, part, step], ring[way]
        ).wait_recv()
        keep(ws.at[at], ws_ref.at[at], ring_keep.at[way, part, step])

    def ring_step(step):
        last = step == n // 2 - 1
        for part, (first, size) in enumerate(cuts):
            for way in (0, 1):
                block = ring_index(lax.rem(pos + (step if way else n - step), n), n)
                here = ws.at[span(block * rows + first, size)]
                if step > 0:
                    arrived(part, way, step - 1, block)
                if last and part != way:
                    continue
                src = w_ref.at[pl.ds(first, size)] if step == 0 else here
                go(src, here, ring_send.at[way, part, step], ring_recv.at[way, part, step], ring[way])

    def pass_on(k):
        at = span(opposite * tokens + k * half, half)
        here = xg.at[at]
        remote(here, here, over_send.at[k], over_recv.at[k], across).wait_recv()
        go(here, here, pass_send.at[k], pass_recv.at[k], beside)
        keep(here, xg_ref.at[at], keep_sem.at[k])

    ring_step(0)
    for k in (0, 1):
        go(
            x_ref.at[pl.ds(k * half, half)], xg.at[span(me * tokens + k * half, half)],
            over_send.at[k], over_recv.at[k], across,
        )
    go(x_ref, xg.at[span(me * tokens, tokens)], side_send.at[0], side_recv.at[0], beside)
    mine = ring_index(pos, n)
    keep(x_ref, xg_ref.at[span(me * tokens, tokens)], keep_sem.at[2])
    keep(w_ref, ws_ref.at[span(mine * rows, rows)], keep_sem.at[3])
    for step in range(1, n // 2):
        ring_step(step)
        if step == n // 2 - 2:
            pass_on(0)
            pass_on(1)
    at = span(next_door * tokens, tokens)
    remote(xg.at[at], xg.at[at], side_send.at[0], side_recv.at[0], beside).wait_recv()
    keep(xg.at[at], xg_ref.at[at], keep_sem.at[4])
    for k in (0, 1):
        at = span(far * tokens + k * half, half)
        remote(xg.at[at], xg.at[at], pass_send.at[k], pass_recv.at[k], beside).wait_recv()
        keep(xg.at[at], xg_ref.at[at], keep_sem.at[5 + k])
    for part in (0, 1):
        arrived(part, part, n // 2 - 1, ring_index(lax.rem(pos + n // 2, n), n))
    for copy in kept:
        copy.wait()
    for copy in started:
        copy.wait_send()


def gather_all(n, x, w):
    tokens, rows = x.shape[0], w.shape[0]
    dma = pltpu.SemaphoreType.DMA
    anywhere = pl.BlockSpec(memory_space=pl.ANY)
    inside = pl.BlockSpec(memory_space=pltpu.VMEM)
    shapes = [(a.shape[0] * k, a.shape[1]) for a, k in ((x, 4), (w, n))]
    hops = dma((2, 2, n // 2))
    return pl.pallas_call(
        functools.partial(gather_body, n, rows, tokens),
        in_specs=[inside] * 2,
        out_specs=[anywhere] * 2,
        out_shape=[jax.ShapeDtypeStruct(shape, bf16) for shape in shapes],
        scratch_shapes=[
            *(pltpu.VMEM(shape, bf16) for shape in shapes),
            dma((7,)), hops, hops, hops, dma((2,)), dma((2,)), dma((1,)), dma((1,)), dma((2,)), dma((2,)),
        ],
        compiler_params=pltpu.CompilerParams(
            collective_id=0, has_side_effects=True, vmem_limit_bytes=40 * 2**20
        ),
        name="gather_all",
    )(x, w)


def reduce_body(
    n, rows, tokens, starts,
    gc_ref, go_ref, branch_ref, back_ref, small_ref,
    oc_ref, oo_ref, obranch_ref, oback_ref, bc_ref, osmall_ref,
    gc, go_, slots, held, near, over, smalls, tens, bc_slot,
    load_sem, ring_send, ring_recv, near_send, near_recv, over_send, over_recv,
    small_send, small_recv, ten_send, ten_recv, bc_send, bc_recv,
):
    pos, ring, me, across, beside = neighbours(n)
    enter((*ring, across, beside))
    cuts = cut_rows(rows)
    started = []

    def go(*args):
        copy = remote(*args)
        copy.start()
        started.append(copy)
        return copy

    core = lax.rem(me, 2)
    opposite = lax.rem(me + 2, 4)
    next_door = me + 1 - 2 * core
    far = lax.rem(next_door + 2, 4)
    half = tokens // 2
    items = [(gc_ref, gc, oc_ref, lo, hi) for lo, hi in starts] + [(go_ref, go_, oo_ref, 0, go_.shape[1])]

    def block_at(way, steps):
        return ring_index(lax.rem(pos + (steps if way else n - steps), n), n)

    for k, (src, _, _, lo, hi) in enumerate(items):
        for way in (0, 1):
            first, size = cuts[way]
            go(
                src.at[span(block_at(way, 1) * rows + first, size), pl.ds(lo, hi - lo)],
                slots[way][k].at[0],
                ring_send.at[way, k, 0], ring_recv.at[way, k, 0], ring[way],
            )
    sides = [(branch_ref, 0), (back_ref, 1)]
    for turn, target in ((0, far), (1, next_door)):
        for src, k in sides:
            for part in (0, 1):
                go(
                    src.at[span(target * tokens + part * half, half)],
                    near.at[k, turn, part],
                    near_send.at[k, turn, part], near_recv.at[k, turn, part], beside,
                )
    loads = {}
    for turn, target in ((0, opposite), (1, me)):
        for src, k in sides:
            for part in (0, 1):
                copy = pltpu.make_async_copy(
                    src.at[span(target * tokens + part * half, half)],
                    held.at[k, turn, part], load_sem.at[4 * turn + 2 * k + part],
                )
                copy.start()
                loads[k, turn, part] = copy
    for k, (src, dst) in enumerate(((gc_ref, gc), (go_ref, go_))):
        copy = pltpu.make_async_copy(src, dst, load_sem.at[8 + k])
        copy.start()
        loads["ring", k] = copy
    small_load = pltpu.make_async_copy(small_ref, smalls.at[pos], load_sem.at[10])
    small_load.start()

    def add_side(k, turn, part, dst):
        def some(i, _):
            at = span(i * 16, 16)
            total = held[k, turn, part, at, :].astype(f32) + near[k, turn, part, at, :].astype(f32)
            if dst is None:
                held[k, turn, part, at, :] = total.astype(bf16)
            else:
                dst[span(part * half + i * 16, 16), :] = total
            return 0

        lax.fori_loop(0, half // 16, some, 0)

    def near_ready(k, turn, part):
        loads[k, turn, part].wait()
        remote(
            near.at[k, turn, part], near.at[k, turn, part],
            near_send.at[k, turn, part], near_recv.at[k, turn, part], beside,
        ).wait_recv()

    for k in (0, 1):
        for part in (0, 1):
            near_ready(k, 0, part)
            add_side(k, 0, part, None)
            go(held.at[k, 0, part], over.at[k, part], over_send.at[k, part], over_recv.at[k, part], across)

    small_load.wait()
    loads["ring", 0].wait()
    loads["ring", 1].wait()
    outs = (obranch_ref, oback_ref)
    todo = [(k, part) for k in (0, 1) for part in (0, 1)]

    for step in range(n - 1):
        here = smalls.at[lax.rem(pos + n - step, n)]
        go(here, here, small_send.at[step], small_recv.at[step], ring[0])
        for k, (_, own, out, lo, hi) in enumerate(items):
            for way in (0, 1):
                first, size = cuts[way]
                slot = slots[way][k].at[step]
                remote(
                    slot, slot, ring_send.at[way, k, step], ring_recv.at[way, k, step], ring[way]
                ).wait_recv()
                block = block_at(way, 2 + step) if step < n - 2 else block_at(way, 0)

                def some(i, _, way=way, k=k, step=step, own=own, out=out, lo=lo, hi=hi, first=first, block=block):
                    total = slots[way][k][step, span(i * 16, 16), :].astype(f32)
                    total = total + own[span(block * rows + first + i * 16, 16), lo:hi].astype(f32)
                    if step < n - 2:
                        slots[way][k][step, span(i * 16, 16), :] = total.astype(bf16)
                    else:
                        out[span(first + i * 16, 16), lo:hi] = total
                    return 0

                lax.fori_loop(0, size // 16, some, 0)
                if step < n - 2:
                    go(
                        slot, slots[way][k].at[step + 1],
                        ring_send.at[way, k, step + 1], ring_recv.at[way, k, step + 1], ring[way],
                    )
            if step == n - 2 and k == 0:
                bc_slot[0] = oc_ref[:, starts[0][0] : starts[0][0] + 2 * NS]
                go(bc_slot.at[0], bc_slot.at[1], bc_send.at[0], bc_recv.at[0], beside)
        here = smalls.at[lax.rem(pos + 2 * n - step - 1, n)]
        remote(here, here, small_send.at[step], small_recv.at[step], ring[0]).wait_recv()
        if todo and step >= 1:
            k, part = todo.pop(0)
            near_ready(k, 1, part)
            add_side(k, 1, part, outs[k])
    for k, part in todo:
        near_ready(k, 1, part)
        add_side(k, 1, part, outs[k])

    total = smalls[0]
    for i in range(1, n):
        total = total + smalls[i]
    tens[me] = total
    go(tens.at[me], tens.at[me], ten_send.at[0], ten_recv.at[0], beside)
    remote(bc_slot.at[1], bc_slot.at[1], bc_send.at[0], bc_recv.at[0], beside).wait_recv()
    bc_slot[2] = bc_slot[0] + bc_slot[1]
    go(bc_slot.at[2], bc_slot.at[3], bc_send.at[1], bc_recv.at[1], across)
    here = tens.at[next_door]
    remote(here, here, ten_send.at[0], ten_recv.at[0], beside).wait_recv()
    for k, target in ((0, me), (1, next_door)):
        here = tens.at[target]
        go(here, here, ten_send.at[1 + k], ten_recv.at[1 + k], across)
    for k in (0, 1):
        for part in (0, 1):
            slot = over.at[k, part]
            remote(slot, slot, over_send.at[k, part], over_recv.at[k, part], across).wait_recv()

            def some(i, _, k=k, part=part):
                at = span(part * half + i * 16, 16)
                outs[k][at, :] = outs[k][at, :] + over[k, part, span(i * 16, 16), :].astype(f32)
                return 0

            lax.fori_loop(0, half // 16, some, 0)
    for k, target in ((0, opposite), (1, far)):
        here = tens.at[target]
        remote(here, here, ten_send.at[1 + k], ten_recv.at[1 + k], across).wait_recv()
    osmall_ref[...] = tens[...]
    remote(bc_slot.at[3], bc_slot.at[3], bc_send.at[1], bc_recv.at[1], across).wait_recv()
    bc_ref[...] = bc_slot[2] + bc_slot[3]
    for copy in started:
        copy.wait_send()


def reduce_all(n, grad_cat, grad_out, branch, back, small):
    rows, tokens = grad_cat.shape[0] // n, branch.shape[0] // 4
    wide, width = grad_cat.shape[1], grad_out.shape[1]
    starts = ((2 * width, wide), (0, 2 * width))
    widths = [hi - lo for lo, hi in starts] + [width]
    sizes = [size for _, size in cut_rows(rows)]
    half = tokens // 2
    dma, vm = pltpu.SemaphoreType.DMA, pltpu.VMEM
    anywhere = pl.BlockSpec(memory_space=pl.ANY)
    inside = pl.BlockSpec(memory_space=pltpu.VMEM)
    return pl.pallas_call(
        functools.partial(reduce_body, n, rows, tokens, starts),
        in_specs=[anywhere] * 5,
        out_specs=[inside] * 6,
        out_shape=[
            jax.ShapeDtypeStruct((rows, wide), f32),
            jax.ShapeDtypeStruct((rows, width), f32),
            jax.ShapeDtypeStruct((tokens, D), f32),
            jax.ShapeDtypeStruct((tokens, D), f32),
            jax.ShapeDtypeStruct((rows, 2 * NS), f32),
            jax.ShapeDtypeStruct((4, *small.shape), f32),
        ],
        scratch_shapes=[
            vm(grad_cat.shape, bf16), vm(grad_out.shape, bf16),
            [[vm((n - 1, size, w), bf16) for w in widths] for size in sizes],
            vm((2, 2, 2, half, D), bf16), vm((2, 2, 2, half, D), bf16), vm((2, 2, half, D), bf16),
            vm((n, *small.shape), f32), vm((4, *small.shape), f32), vm((4, rows, 2 * NS), f32),
            dma((11,)), dma((2, 3, n - 1)), dma((2, 3, n - 1)), dma((2, 2, 2)), dma((2, 2, 2)),
            dma((2, 2)), dma((2, 2)), dma((n - 1,)), dma((n - 1,)), dma((3,)), dma((3,)), dma((2,)), dma((2,)),
        ],
        compiler_params=pltpu.CompilerParams(
            collective_id=1, has_side_effects=True, vmem_limit_bytes=60 * 2**20
        ),
        name="reduce_all",
    )(grad_cat, grad_out, branch, back, small)


def adamw_step(weight, first, second, grad, rate, decay):
    first_new = beta_first * first + (1.0 - beta_first) * grad
    second_new = beta_second * second + (1.0 - beta_second) * grad * grad
    hat_first = first_new / (1.0 - beta_first**STEP)
    hat_second = second_new / (1.0 - beta_second**STEP)
    weight_new = weight - rate * (hat_first / (jnp.sqrt(hat_second) + adam_eps) + decay * weight)
    return (weight_new, first_new, second_new)


def local(
    layer_input,
    out_grad,
    small_params,
    small_first,
    small_second,
    w_zx,
    zx_first,
    zx_second,
    w_bc,
    bc_first,
    bc_second,
    w_dt,
    dt_first,
    dt_second,
    w_out,
    out_first,
    out_second,
):
    tensor_index = lax.axis_index("tensor")
    local_in = layer_input.astype(f32)
    gain_in, gate_gain, conv_x, bias_x, conv_bc, bias_bc, dt_bias, a_log, d_skip = unpack(
        small_params
    )
    rows_own = w_zx.shape[0]
    width = w_zx.shape[2]
    heads = w_dt.shape[1]
    chan_start = tensor_index * width
    head_start = tensor_index * heads
    gate_local = lax.dynamic_slice_in_dim(gate_gain, chan_start, width, 0)
    conv_local = lax.dynamic_slice_in_dim(conv_x, chan_start, width, 1)
    bias_local = lax.dynamic_slice_in_dim(bias_x, chan_start, width, 0)
    dtb_local = lax.dynamic_slice_in_dim(dt_bias, head_start, heads, 0)
    a_local = -jnp.exp(lax.dynamic_slice_in_dim(a_log, head_start, heads, 0))
    dskip_local = lax.dynamic_slice_in_dim(d_skip, head_start, heads, 0)
    taps = jnp.concatenate(
        [
            jnp.concatenate([conv_local, conv_bc], axis=1),
            jnp.concatenate([bias_local, bias_bc])[None, :],
            jnp.zeros((8 - CONV - 1, width + 2 * NS), f32),
        ],
        axis=0,
    )
    lanes = lambda v: jnp.pad(v, (0, LANES - heads))
    head = jnp.pad(jnp.stack([lanes(dtb_local), lanes(a_local)]), ((0, 6), (0, 0)))
    chan = jnp.pad(jnp.stack([gate_local, jnp.repeat(dskip_local, P_SIZE)]), ((0, 6), (0, 0)))
    pick = jnp.asarray(
        (jnp.arange(width)[:, None] // P_SIZE == jnp.arange(LANES)[None, :]), bf16
    )

    inv_in = lax.rsqrt(jnp.mean(local_in * local_in, axis=-1, keepdims=True) + norm_eps)
    normed_in = local_in * inv_in * gain_in[None, :]
    w_cat = jnp.concatenate(
        [
            w_zx.reshape(rows_own, 2 * width).astype(bf16),
            w_bc.astype(bf16),
            jnp.pad(w_dt, ((0, 0), (0, LANES - heads))).astype(bf16),
        ],
        axis=1,
    )
    n = lax.axis_size("dp")
    xg, w_all = gather_all(n, normed_in.astype(bf16), w_cat)
    z, v, xc, dr, y, dn, st, red, cot_all, wo_all = ssd_forward(
        n, xg, w_all, taps, head, chan, out_grad, w_out.astype(bf16)
    )
    normed_low, d_cat, acc, hacc = ssd_backward(z, v, xc, dr, y, dn, st, red, taps, head, chan, pick)

    branch = mm(normed_low, wo_all, NT).astype(bf16)
    grad_out = mm(cot_all, normed_low, TN).astype(bf16)
    back = mm(d_cat, w_all, NT)
    gain_part = jnp.sum(xg.astype(f32) * back, axis=0) / gain_in
    grad_cat = mm(xg, d_cat, TN).astype(bf16)
    acc = jnp.sum(acc, axis=1)
    hacc = jnp.sum(hacc, axis=1)
    skip_part = jnp.sum(acc[CONV + 2, :width].reshape(heads, P_SIZE), axis=1)
    small = jnp.concatenate(
        [
            acc[: CONV + 1].reshape(-1), acc[CONV + 1, :width], hacc[0], hacc[1],
            gain_part, jnp.pad(skip_part, (0, 4 * LANES - heads)),
        ]
    ).reshape(8, width + 2 * NS)
    owner_cat, owner_out, own_branch, d_normed_in, owner_bc, tens = reduce_all(
        n, grad_cat, grad_out, branch, back.astype(bf16), small
    )
    layer_output = (local_in + own_branch).astype(bf16)
    owner_zx = owner_cat[:, : 2 * width].reshape(rows_own, 2, width)
    owner_dt = owner_cat[:, 2 * width + 2 * NS : 2 * width + 2 * NS + heads]

    inner_in = jnp.sum(local_in * gain_in[None, :] * d_normed_in, axis=-1, keepdims=True)
    input_grad = (
        out_grad.astype(f32)
        + inv_in * gain_in[None, :] * d_normed_in
        - local_in * (inv_in * inv_in * inv_in * inner_in / D)
    )
    gain_sum = jnp.sum(tens[:, 6:8], axis=0).reshape(-1)[:D]
    bc_sum = jnp.sum(tens[:, : CONV + 1, width:], axis=0)
    small_grad = jnp.concatenate(
        [
            gain_sum,
            tens[:, CONV + 1, :width].reshape(-1),
            jnp.moveaxis(tens[:, :CONV, :width], 0, 1).reshape(-1),
            tens[:, CONV, :width].reshape(-1),
            bc_sum.reshape(-1),
            tens[:, CONV + 1, width : width + heads].reshape(-1),
            tens[:, CONV + 1, width + LANES : width + LANES + heads].reshape(-1) * -jnp.exp(a_log),
            tens[:, 7, 512 : 512 + heads].reshape(-1),
        ]
    )
    small_new, small_first_new, small_second_new = adamw_step(
        small_params, small_first, small_second, small_grad, small_rate, 0.0
    )
    zx_new, zx_first_new, zx_second_new = adamw_step(
        w_zx, zx_first, zx_second, owner_zx, matrix_rate, matrix_decay
    )
    bc_new, bc_first_new, bc_second_new = adamw_step(
        w_bc, bc_first, bc_second, owner_bc, matrix_rate, matrix_decay
    )
    dt_new, dt_first_new, dt_second_new = adamw_step(
        w_dt, dt_first, dt_second, owner_dt, matrix_rate, matrix_decay
    )
    out_new, out_first_new, out_second_new = adamw_step(
        w_out, out_first, out_second, owner_out, matrix_rate, matrix_decay
    )
    return (
        layer_output,
        input_grad,
        small_new,
        small_first_new,
        small_second_new,
        zx_new,
        zx_first_new,
        zx_second_new,
        bc_new,
        bc_first_new,
        bc_second_new,
        dt_new,
        dt_first_new,
        dt_second_new,
        out_new,
        out_first_new,
        out_second_new,
    )


def solution(mesh):
    return jax.shard_map(
        local,
        mesh=mesh,
        in_specs=(
            P(("dp", "tensor"), None),
            P(("dp", "tensor"), None),
            P(),
            P(),
            P(),
            P("dp", None, "tensor"),
            P("dp", None, "tensor"),
            P("dp", None, "tensor"),
            P("dp", None),
            P("dp", None),
            P("dp", None),
            P("dp", "tensor"),
            P("dp", "tensor"),
            P("dp", "tensor"),
            P("dp", "tensor"),
            P("dp", "tensor"),
            P("dp", "tensor"),
        ),
        out_specs=(
            P(("dp", "tensor"), None),
            P(("dp", "tensor"), None),
            P(),
            P(),
            P(),
            P("dp", None, "tensor"),
            P("dp", None, "tensor"),
            P("dp", None, "tensor"),
            P("dp", None),
            P("dp", None),
            P("dp", None),
            P("dp", "tensor"),
            P("dp", "tensor"),
            P("dp", "tensor"),
            P("dp", "tensor"),
            P("dp", "tensor"),
            P("dp", "tensor"),
        ),
        check_vma=False,
    )
```

```python
import functools

import jax
import jax.numpy as jnp
from jax import lax
from jax.experimental import pallas as pl
from jax.experimental.pallas import tpu as pltpu
from jax.sharding import PartitionSpec as P

D = 1536
DI = 3072
H = 48
NS = 128
P_SIZE = 64
CONV = 4
LEN = 2048
STEP = 10

T = 128
ROWS = 256
LANES = 128

norm_eps = 1e-05
adam_eps = 1e-08
beta_first = 0.9
beta_second = 0.95
matrix_rate = 0.01
small_rate = 0.1
matrix_decay = 0.1

f32 = jnp.float32
bf16 = jnp.bfloat16
NN = (((1,), (0,)), ((), ()))
NT = (((1,), (1,)), ((), ()))
TN = (((0,), (0,)), ((), ()))
HIGHEST = lax.Precision.HIGHEST


def unpack(flat):
    gain_in = flat[:D]
    cursor = D
    gate_gain = flat[cursor : cursor + DI]
    cursor = cursor + DI
    conv_x = flat[cursor : cursor + CONV * DI].reshape(CONV, DI)
    cursor = cursor + CONV * DI
    bias_x = flat[cursor : cursor + DI]
    cursor = cursor + DI
    conv_bc = flat[cursor : cursor + CONV * 2 * NS].reshape(CONV, 2 * NS)
    cursor = cursor + CONV * 2 * NS
    bias_bc = flat[cursor : cursor + 2 * NS]
    cursor = cursor + 2 * NS
    dt_bias = flat[cursor : cursor + H]
    a_log = flat[cursor + H : cursor + 2 * H]
    d_skip = flat[cursor + 2 * H : cursor + 3 * H]
    return (gain_in, gate_gain, conv_x, bias_x, conv_bc, bias_bc, dt_bias, a_log, d_skip)


def mm(a, b, dims=NN):
    return lax.dot_general(a, b, dims, preferred_element_type=f32)


def mm_exact(a, b, dims=NN):
    return lax.dot_general(a, b, dims, preferred_element_type=f32, precision=HIGHEST)


def sigmoid(v):
    return 0.5 * jnp.tanh(0.5 * v) + 0.5


def softplus(v):
    return jnp.maximum(v, 0.0) + jnp.log1p(jnp.exp(-jnp.abs(v)))


def spread(col):
    return jnp.broadcast_to(col, (T, LANES))


def block_iota(axis):
    return lax.broadcasted_iota(jnp.int32, (T, LANES), axis)


def head_rows(dr_ref, head_ref, rows):
    raw = dr_ref[rows, :] + head_ref[0:1, :]
    dt = softplus(raw)
    low_tri = jnp.where(block_iota(0) >= block_iota(1), 1.0, 0.0).astype(f32)
    decay = mm_exact(low_tri, dt * head_ref[1:2, :])
    return raw, dt, decay


def ring_place(n):
    me = lax.axis_index("dp")
    z, x = lax.div(me, 2), lax.rem(me, 2)
    return z + x * (n - 1 - 2 * z)


def ring_index(pos, n):
    back = lax.div(pos, n // 2)
    return 2 * pos + back * (2 * n - 1 - 4 * pos)


def neighbours(n):
    pos = ring_place(n)
    right = ring_index(lax.rem(pos + 1, n), n)
    left = ring_index(lax.rem(pos + n - 1, n), n)
    me = lax.axis_index("tensor")
    y, core = lax.div(me, 2), lax.rem(me, 2)
    across = 2 * (1 - y) + core
    beside = 2 * y + 1 - core
    return pos, ({"dp": right}, {"dp": left}), me, {"tensor": across}, {"tensor": beside}


def enter(peers):
    barrier = pltpu.get_barrier_semaphore()
    for peer in peers:
        pl.semaphore_signal(barrier, inc=1, device_id=peer, device_id_type=pl.DeviceIdType.MESH)
    pl.semaphore_wait(barrier, len(peers))


def remote(src, dst, send_sem, recv_sem, peer):
    return pltpu.make_async_remote_copy(
        src_ref=src, dst_ref=dst, send_sem=send_sem, recv_sem=recv_sem,
        device_id=peer, device_id_type=pl.DeviceIdType.MESH,
    )


def span(start, size):
    return pl.ds(pl.multiple_of(start, 16), size)


def cut_rows(rows):
    top = rows // 32 * 16
    return ((0, top), (top, rows - top))


def forward_body(
    n, rows, tokens, width,
    xg_ref, w_ref, taps_ref, head_ref, chan_ref, cot_ref, wo_ref,
    z_ref, v_ref, xc_ref, dr_ref, y_ref, dn_ref, st_ref, red_ref, cots_ref, wos_ref,
    halo, state, gated_all, cots, wos, sums,
    own_keep, ring_keep, over_keep, side_keep, pass_keep, ring_send, ring_recv, over_send, over_recv,
    side_send, side_recv, pass_send, pass_recv, sum_send, sum_recv,
):
    pairs = width // LANES
    wide = width + 2 * NS
    step = pl.program_id(0)
    steps = LEN // ROWS
    pos, ring, me, across, beside = neighbours(n)
    opposite = lax.rem(me + 2, 4)
    next_door = me + 1 - 2 * lax.rem(me, 2)
    far = lax.rem(next_door + 2, 4)
    half = tokens // 2
    hops = n // 2
    cuts = cut_rows(rows)
    mine = ring_index(pos, n)

    def hop(part, way, h):
        first, size = cuts[part]
        block = ring_index(lax.rem(pos + (h if way else n - h), n), n)
        here = wos.at[span(block * rows + first, size)]
        src = wo_ref.at[pl.ds(first, size)] if h == 0 else here
        return remote(src, here, ring_send.at[way, part, h], ring_recv.at[way, part, h], ring[way])

    def hop_lands(part, way, h):
        first, size = cuts[part]
        block = ring_index(lax.rem(pos + (h + 1 if way else n - h - 1), n), n)
        return span(block * rows + first, size)

    def hop_arrival(part, way, h):
        here = wos.at[hop_lands(part, way, h)]
        return remote(here, here, ring_send.at[way, part, h], ring_recv.at[way, part, h], ring[way])

    def hop_keep(part, way, h):
        at = hop_lands(part, way, h)
        return pltpu.make_async_copy(wos.at[at], wos_ref.at[at], ring_keep.at[way, part, h])

    def hop_ways(h):
        return [(part, way) for part in (0, 1) for way in (0, 1) if h < hops - 1 or part == way]

    def over(k):
        return remote(
            cot_ref.at[pl.ds(k * half, half)], cots.at[span(me * tokens + k * half, half)],
            over_send.at[k], over_recv.at[k], across,
        )

    def landed(full, start, size, send, recv, peer):
        here = full.at[span(start, size)]
        return remote(here, here, send, recv, peer)

    def over_arrival(k):
        start = opposite * tokens + k * half
        return landed(cots, start, half, over_send.at[k], over_recv.at[k], across)

    def passing(k):
        start = opposite * tokens + k * half
        return landed(cots, start, half, pass_send.at[k], pass_recv.at[k], beside)

    def pass_arrival(k):
        return landed(cots, far * tokens + k * half, half, pass_send.at[k], pass_recv.at[k], beside)

    def side():
        return remote(cot_ref, cots.at[span(me * tokens, tokens)], side_send.at[0], side_recv.at[0], beside)

    def side_arrival():
        return landed(cots, next_door * tokens, tokens, side_send.at[0], side_recv.at[0], beside)

    def keep(start, size, sem):
        return pltpu.make_async_copy(cots.at[span(start, size)], cots_ref.at[span(start, size)], sem)

    def own_keeps():
        return (
            pltpu.make_async_copy(cot_ref, cots_ref.at[span(me * tokens, tokens)], own_keep.at[0]),
            pltpu.make_async_copy(wo_ref, wos_ref.at[span(mine * rows, rows)], own_keep.at[1]),
            pltpu.make_async_copy(cot_ref, cots.at[span(me * tokens, tokens)], own_keep.at[2]),
            pltpu.make_async_copy(wo_ref, wos.at[span(mine * rows, rows)], own_keep.at[3]),
        )

    @pl.when(step == 0)
    def _():
        enter((*ring, across, beside))
        over(0).start()
        over(1).start()
        for part, way in hop_ways(0):
            hop(part, way, 0).start()
        side().start()
        for copy in own_keeps():
            copy.start()
        halo[0:8, :] = jnp.zeros((8, wide), f32)
        state[...] = jnp.zeros_like(state)

    for h in range(1, hops):

        @pl.when(step == min(2 * h, steps - 1))
        def _(h=h):
            for part, way in hop_ways(h - 1):
                hop_arrival(part, way, h - 1).wait_recv()
                hop_keep(part, way, h - 1).start()
                if (part, way) in hop_ways(h):
                    hop(part, way, h).start()

    @pl.when(step == steps - 1)
    def _():
        for k in (0, 1):
            over_arrival(k).wait_recv()
            passing(k).start()
            keep(opposite * tokens + k * half, half, over_keep.at[k]).start()

    @pl.when(step == steps)
    def _():
        for part, way in hop_ways(hops - 1):
            hop_arrival(part, way, hops - 1).wait_recv()
            hop_keep(part, way, hops - 1).start()
        side_arrival().wait_recv()
        keep(next_door * tokens, tokens, side_keep.at[0]).start()
        for k in (0, 1):
            pass_arrival(k).wait_recv()
            keep(far * tokens + k * half, half, pass_keep.at[k]).start()
        for copy in own_keeps():
            copy.wait()

    @pl.when(step < steps)
    def _():
        scan_step(
            width, step, xg_ref, w_ref, taps_ref, head_ref, chan_ref,
            z_ref, v_ref, xc_ref, dr_ref, y_ref, st_ref, halo, state, gated_all, sums,
        )

    @pl.when(step >= steps)
    def _():
        at = span((step - steps) * ROWS, ROWS)
        dn_ref[...] = mm(cots[at, :], wos[...])
        inner = jnp.zeros((ROWS, LANES), f32)
        for p in range(pairs):
            cols = slice(p * LANES, (p + 1) * LANES)
            inner = inner + gated_all[at, cols] * chan_ref[0:1, cols] * dn_ref[:, cols]
        lanes = pl.ds(pl.multiple_of((step - steps) * ROWS, ROWS), ROWS)
        sums[0, 4:8, lanes] = mm_exact(jnp.ones((8, LANES), f32), inner, NT)[4:8]

    @pl.when(step == 2 * steps - 1)
    def _():
        first = remote(sums.at[0], sums.at[1], sum_send.at[0], sum_recv.at[0], beside)
        first.start()
        first.wait_recv()
        sums[2] = sums[0] + sums[1]
        second = remote(sums.at[2], sums.at[3], sum_send.at[1], sum_recv.at[1], across)
        second.start()
        for h in range(hops):
            for part, way in hop_ways(h):
                hop(part, way, h).wait_send()
                hop_keep(part, way, h).wait()
        side().wait_send()
        keep(next_door * tokens, tokens, side_keep.at[0]).wait()
        for k in (0, 1):
            over(k).wait_send()
            passing(k).wait_send()
            keep(opposite * tokens + k * half, half, over_keep.at[k]).wait()
            keep(far * tokens + k * half, half, pass_keep.at[k]).wait()
        first.wait_send()
        second.wait()
        red_ref[...] = sums[2] + sums[3]


def scan_step(
    width, step, xg_ref, w_ref, taps_ref, head_ref, chan_ref,
    z_ref, v_ref, xc_ref, dr_ref, y_ref, st_ref, halo, state, gated_all, sums,
):
    pairs = width // LANES
    wide = width + 2 * NS
    dr_ref[...] = mm(xg_ref[...], w_ref[:, width + wide :])
    halo[8 : 8 + ROWS, :] = mm(xg_ref[...], w_ref[:, width : width + wide])
    z_ref[...] = mm(xg_ref[...], w_ref[:, :width])
    low_half = block_iota(1) < P_SIZE
    causal = block_iota(0) >= block_iota(1)

    def convolved(sub, block):
        cols = slice(block * LANES, (block + 1) * LANES)
        total = taps_ref[CONV : CONV + 1, cols]
        for k in range(CONV):
            first = 8 - (CONV - 1) + k + sub * T
            total = total + taps_ref[k : k + 1, cols] * halo[first : first + T, cols]
        rows = slice(sub * T, (sub + 1) * T)
        xc_ref[rows, cols] = total
        v_ref[rows, cols] = halo[8 + sub * T : 8 + (sub + 1) * T, cols].astype(bf16)
        return total * sigmoid(total)

    for sub in range(ROWS // T):
        rows = slice(sub * T, (sub + 1) * T)
        raw, dt, decay = head_rows(dr_ref, head_ref, rows)
        decay_t = decay.T
        b_low = convolved(sub, pairs).astype(bf16)
        c_low = convolved(sub, pairs + 1).astype(bf16)
        b_t = b_low.T
        scores = jnp.where(causal, mm(c_low, b_low, NT), 0.0)
        squares = jnp.zeros((T, LANES), f32)
        st_ref[sub] = state[...].astype(bf16)
        for p in range(pairs):
            cols = slice(p * LANES, (p + 1) * LANES)
            x = convolved(sub, p)
            l1, l2 = spread(decay[:, 2 * p : 2 * p + 1]), spread(decay[:, 2 * p + 1 : 2 * p + 2])
            both = jnp.where(low_half, l1, l2)
            dtb = jnp.where(
                low_half, spread(dt[:, 2 * p : 2 * p + 1]), spread(dt[:, 2 * p + 1 : 2 * p + 2])
            )
            u = x * dtb
            m1 = scores * jnp.exp(jnp.minimum(l1 - decay_t[2 * p : 2 * p + 1, :], 0.0))
            m2 = scores * jnp.exp(jnp.minimum(l2 - decay_t[2 * p + 1 : 2 * p + 2, :], 0.0))
            mixing = jnp.concatenate([m1.astype(bf16), m2.astype(bf16)], axis=1)
            parts = jnp.concatenate(
                [jnp.where(low_half, u, 0.0).astype(bf16), jnp.where(low_half, 0.0, u).astype(bf16)],
                axis=0,
            )
            last = both[T - 1 : T, :]
            entering = st_ref[sub, :, cols]
            y = mm(mixing, parts) + jnp.exp(both) * mm(c_low, entering) + chan_ref[1:2, cols] * x
            tail = (u * jnp.exp(last - both)).astype(bf16)
            state[:, cols] = jnp.exp(last) * state[:, cols] + mm(b_t, tail)
            y_ref[rows, cols] = y
            z = z_ref[rows, cols]
            gated = y * (z * sigmoid(z))
            gated_all[span(step * ROWS + sub * T, T), cols] = gated
            squares = squares + gated * gated
        lanes = pl.ds(pl.multiple_of(step * ROWS + sub * T, T), T)
        sums[0, 0:4, lanes] = mm_exact(jnp.ones((8, LANES), f32), squares, NT)[0:4]
    halo[0:8, :] = halo[ROWS : ROWS + 8, :]


def ssd_forward(n, xg, w_cat, taps, head, chan, cot, wo):
    length = xg.shape[0]
    rows, width = wo.shape
    tokens = cot.shape[0]
    wide = width + 2 * NS
    steps = length // ROWS
    subs = ROWS // T
    assert length == LEN
    early = lambda i: jnp.minimum(i, steps - 1)
    row = lambda m: pl.BlockSpec((ROWS, m), lambda i: (early(i), 0))
    whole = lambda a: pl.BlockSpec(a.shape, lambda i: (0,) * a.ndim, pipeline_mode=pl.Buffered(1))
    anywhere = pl.BlockSpec(memory_space=pl.ANY)
    vm, dma = pltpu.VMEM, pltpu.SemaphoreType.DMA
    hops = dma((2, 2, n // 2))
    return pl.pallas_call(
        functools.partial(forward_body, n, rows, tokens, width),
        grid=(2 * steps,),
        in_specs=[row(D), whole(w_cat), whole(taps), whole(head), whole(chan), whole(cot), whole(wo)],
        out_specs=[
            row(width), row(wide), row(wide), row(LANES), row(width),
            pl.BlockSpec((ROWS, width), lambda i: (jnp.maximum(i - steps, 0), 0)),
            pl.BlockSpec((subs, NS, width), lambda i: (early(i), 0, 0)),
            pl.BlockSpec((8, length), lambda i: (0, 0)),
            anywhere, anywhere,
        ],
        out_shape=[
            jax.ShapeDtypeStruct((length, width), f32),
            jax.ShapeDtypeStruct((length, wide), bf16),
            jax.ShapeDtypeStruct((length, wide), f32),
            jax.ShapeDtypeStruct((length, LANES), f32),
            jax.ShapeDtypeStruct((length, width), f32),
            jax.ShapeDtypeStruct((length, width), f32),
            jax.ShapeDtypeStruct((length // T, NS, width), bf16),
            jax.ShapeDtypeStruct((8, length), f32),
            jax.ShapeDtypeStruct((4 * tokens, D), bf16),
            jax.ShapeDtypeStruct((n * rows, width), bf16),
        ],
        scratch_shapes=[
            vm((ROWS + 8, wide), f32), vm((NS, width), f32), vm((length, width), f32),
            vm((4 * tokens, D), bf16), vm((n * rows, width), bf16), vm((4, 8, length), f32),
            dma((4,)), hops, dma((2,)), dma((1,)), dma((2,)), hops, hops, dma((2,)), dma((2,)),
            dma((1,)), dma((1,)), dma((2,)), dma((2,)), dma((2,)), dma((2,)),
        ],
        compiler_params=pltpu.CompilerParams(
            collective_id=2, has_side_effects=True, vmem_limit_bytes=58 * 2**20
        ),
        name="layer_forward",
    )(xg, w_cat, taps, head, chan, cot, wo)


def gather_body(
    n, rows, tokens,
    x_ref, w_ref, xg_ref, ws_ref, xg, ws,
    keep_sem, ring_keep, ring_send, ring_recv, over_send, over_recv, side_send, side_recv, pass_send, pass_recv,
):
    pos, ring, me, across, beside = neighbours(n)
    enter((*ring, across, beside))
    half = tokens // 2
    started, kept = [], []

    def go(*args):
        copy = remote(*args)
        copy.start()
        started.append(copy)

    def keep(src, dst, sem):
        copy = pltpu.make_async_copy(src, dst, sem)
        copy.start()
        kept.append(copy)

    opposite = lax.rem(me + 2, 4)
    next_door = me + 1 - 2 * lax.rem(me, 2)
    far = lax.rem(next_door + 2, 4)
    cuts = cut_rows(rows)

    def arrived(part, way, step, block):
        first, size = cuts[part]
        at = span(block * rows + first, size)
        remote(
            ws.at[at], ws.at[at], ring_send.at[way, part, step], ring_recv.at[way, part, step], ring[way]
        ).wait_recv()
        keep(ws.at[at], ws_ref.at[at], ring_keep.at[way, part, step])

    def ring_step(step):
        last = step == n // 2 - 1
        for part, (first, size) in enumerate(cuts):
            for way in (0, 1):
                block = ring_index(lax.rem(pos + (step if way else n - step), n), n)
                here = ws.at[span(block * rows + first, size)]
                if step > 0:
                    arrived(part, way, step - 1, block)
                if last and part != way:
                    continue
                src = w_ref.at[pl.ds(first, size)] if step == 0 else here
                go(src, here, ring_send.at[way, part, step], ring_recv.at[way, part, step], ring[way])

    def pass_on(k):
        at = span(opposite * tokens + k * half, half)
        here = xg.at[at]
        remote(here, here, over_send.at[k], over_recv.at[k], across).wait_recv()
        go(here, here, pass_send.at[k], pass_recv.at[k], beside)
        keep(here, xg_ref.at[at], keep_sem.at[k])

    ring_step(0)
    for k in (0, 1):
        go(
            x_ref.at[pl.ds(k * half, half)], xg.at[span(me * tokens + k * half, half)],
            over_send.at[k], over_recv.at[k], across,
        )
    go(x_ref, xg.at[span(me * tokens, tokens)], side_send.at[0], side_recv.at[0], beside)
    mine = ring_index(pos, n)
    keep(x_ref, xg_ref.at[span(me * tokens, tokens)], keep_sem.at[2])
    keep(w_ref, ws_ref.at[span(mine * rows, rows)], keep_sem.at[3])
    for step in range(1, n // 2):
        ring_step(step)
        if step == n // 2 - 2:
            pass_on(0)
            pass_on(1)
    at = span(next_door * tokens, tokens)
    remote(xg.at[at], xg.at[at], side_send.at[0], side_recv.at[0], beside).wait_recv()
    keep(xg.at[at], xg_ref.at[at], keep_sem.at[4])
    for k in (0, 1):
        at = span(far * tokens + k * half, half)
        remote(xg.at[at], xg.at[at], pass_send.at[k], pass_recv.at[k], beside).wait_recv()
        keep(xg.at[at], xg_ref.at[at], keep_sem.at[5 + k])
    for part in (0, 1):
        arrived(part, part, n // 2 - 1, ring_index(lax.rem(pos + n // 2, n), n))
    for copy in kept:
        copy.wait()
    for copy in started:
        copy.wait_send()


def gather_all(n, x, w):
    tokens, rows = x.shape[0], w.shape[0]
    dma = pltpu.SemaphoreType.DMA
    anywhere = pl.BlockSpec(memory_space=pl.ANY)
    inside = pl.BlockSpec(memory_space=pltpu.VMEM)
    shapes = [(a.shape[0] * k, a.shape[1]) for a, k in ((x, 4), (w, n))]
    hops = dma((2, 2, n // 2))
    return pl.pallas_call(
        functools.partial(gather_body, n, rows, tokens),
        in_specs=[inside] * 2,
        out_specs=[anywhere] * 2,
        out_shape=[jax.ShapeDtypeStruct(shape, bf16) for shape in shapes],
        scratch_shapes=[
            *(pltpu.VMEM(shape, bf16) for shape in shapes),
            dma((7,)), hops, hops, hops, dma((2,)), dma((2,)), dma((1,)), dma((1,)), dma((2,)), dma((2,)),
        ],
        compiler_params=pltpu.CompilerParams(
            collective_id=0, has_side_effects=True, vmem_limit_bytes=40 * 2**20
        ),
        name="gather_all",
    )(x, w)


def gradient_body(
    width,
    z_ref, y_ref, dn_ref, red_ref, wo_ref, chan_ref, xg_ref, cot_ref,
    dy_ref, dz_ref, branch_ref, early_ref, gate_ref,
    nl, dz_all,
):
    step = pl.program_id(0)
    steps = LEN // ROWS

    @pl.when(step == 0)
    def _():
        gate_ref[...] = jnp.zeros_like(gate_ref)

    @pl.when(step < steps)
    def _():
        q_row = lax.rsqrt(red_ref[0:4, :] / DI + norm_eps)
        k_row = q_row * q_row * q_row * red_ref[4:8, :] / DI
        turned = jnp.concatenate([q_row, k_row], axis=0).T
        for sub in range(ROWS // T):
            rows = slice(sub * T, (sub + 1) * T)
            at = span(step * ROWS + sub * T, T)
            q, kk = spread(turned[rows, 0:1]), spread(turned[rows, 4:5])
            for p in range(width // LANES):
                cols = slice(p * LANES, (p + 1) * LANES)
                z, y, dn = z_ref[rows, cols], y_ref[rows, cols], dn_ref[rows, cols]
                gain = chan_ref[0:1, cols]
                s = sigmoid(z)
                sz = z * s
                gated = y * sz
                gq = gated * q
                dg = q * gain * dn - gated * kk
                gate_ref[:, cols] += jnp.sum((gq * dn).reshape(T // 8, 8, LANES), axis=0)
                nl[at, cols] = (gq * gain).astype(bf16)
                dz = (dg * y * (s + sz * (1.0 - s))).astype(bf16)
                dz_all[at, cols] = dz
                dz_ref[rows, cols] = dz
                dy_ref[rows, cols] = dg * sz
        branch_ref[...] = mm(nl[span(step * ROWS, ROWS), :], wo_ref[...], NT).astype(bf16)

    @pl.when(step >= steps)
    def _():
        early_ref[:, :width] = mm(xg_ref[...], dz_all[...], TN).astype(bf16)
        early_ref[:, width:] = mm(cot_ref[...], nl[...], TN).astype(bf16)


def early_gradients(z, y, dn, red, wo, chan, xg, cot):
    length, width = z.shape
    steps = length // ROWS
    deep = 2 * LANES
    early = lambda i: jnp.minimum(i, steps - 1)
    late = lambda i: jnp.maximum(i - steps, 0)
    row = lambda m: pl.BlockSpec((ROWS, m), lambda i: (early(i), 0))
    column = pl.BlockSpec((length, deep), lambda i: (0, late(i)))
    whole = lambda a: pl.BlockSpec(a.shape, lambda i: (0,) * a.ndim, pipeline_mode=pl.Buffered(1))
    return pl.pallas_call(
        functools.partial(gradient_body, width),
        grid=(steps + D // deep,),
        in_specs=[
            row(width), row(width), row(width), pl.BlockSpec((8, ROWS), lambda i: (0, early(i))),
            whole(wo), whole(chan), column, column,
        ],
        out_specs=[
            row(width), row(width), row(D), pl.BlockSpec((deep, 2 * width), lambda i: (late(i), 0)),
            pl.BlockSpec((8, width), lambda i: (0, 0)),
        ],
        out_shape=[
            jax.ShapeDtypeStruct((length, width), f32),
            jax.ShapeDtypeStruct((length, width), bf16),
            jax.ShapeDtypeStruct((length, D), bf16),
            jax.ShapeDtypeStruct((D, 2 * width), bf16),
            jax.ShapeDtypeStruct((8, width), f32),
        ],
        scratch_shapes=[pltpu.VMEM((length, width), bf16), pltpu.VMEM((length, width), bf16)],
        compiler_params=pltpu.CompilerParams(vmem_limit_bytes=48 * 2**20),
        name="early_gradients",
    )(z, y, dn, red, wo, chan, xg, cot)


def backward_body(
    n, own_rows, tokens, width,
    dy_ref, v_ref, xc_ref, dr_ref, st_ref, gate_ref, taps_ref, head_ref, chan_ref, pick_ref, early_ref, branch_ref,
    d_ref, small_ref, oearly_ref, obranch_ref,
    dxh, dstate, yst, bds, dyeb, utb, gin, gout, xdu, turn, acc, hacc,
    own, slots, near, held, over_slot,
    load_sem, ring_send, ring_recv, near_send, near_recv, over_send, over_recv,
):
    pairs = width // LANES
    wide = width + 2 * NS
    step = pl.program_id(0)
    steps = LEN // ROWS
    pos, ring, me, across, beside = neighbours(n)
    opposite = lax.rem(me + 2, 4)
    next_door = me + 1 - 2 * lax.rem(me, 2)
    far = lax.rem(next_door + 2, 4)
    half = tokens // 2
    cuts = cut_rows(own_rows)

    def block_at(way, count):
        return ring_index(lax.rem(pos + (count if way else n - count), n), n)

    def hop(k, way, h):
        first, size = cuts[way]
        if h == 0:
            src = early_ref.at[span(block_at(way, 1) * own_rows + first, size), pl.ds(k * width, width)]
        else:
            src = slots[way][k].at[h - 1]
        return remote(
            src, slots[way][k].at[h], ring_send.at[way, k, h], ring_recv.at[way, k, h], ring[way]
        )

    def near_copy(turned, part):
        start = (next_door if turned else far) * tokens + part * half
        return remote(
            branch_ref.at[span(start, half)], near.at[turned, part],
            near_send.at[turned, part], near_recv.at[turned, part], beside,
        )

    def held_copy(turned, part):
        start = (me if turned else opposite) * tokens + part * half
        return pltpu.make_async_copy(
            branch_ref.at[span(start, half)], held.at[turned, part], load_sem.at[2 * turned + part]
        )

    def over_copy(part):
        return remote(held.at[0, part], over_slot.at[part], over_send.at[part], over_recv.at[part], across)

    def own_copy():
        return pltpu.make_async_copy(early_ref, own, load_sem.at[4])

    def ring_turn(k, h):
        for way in (0, 1):
            first, size = cuts[way]
            hop(k, way, h).wait_recv()
            block = block_at(way, 2 + h) if h < n - 2 else block_at(way, 0)

            def some(i, _, way=way, first=first, block=block):
                cols = slice(k * width, (k + 1) * width)
                total = slots[way][k][h, span(i * 16, 16), :].astype(f32)
                total = total + own[span(block * own_rows + first + i * 16, 16), cols].astype(f32)
                if h < n - 2:
                    slots[way][k][h, span(i * 16, 16), :] = total.astype(bf16)
                else:
                    oearly_ref[span(first + i * 16, 16), cols] = total
                return 0

            lax.fori_loop(0, size // 16, some, 0)
            if h < n - 2:
                hop(k, way, h + 1).start()

    def ring_poll(k):
        for h in range(n - 1):
            pl.when(step == min(h + 1, steps - 1))(functools.partial(ring_turn, k, h))

    def add_near(turned):
        for part in (0, 1):
            held_copy(turned, part).wait()
            near_copy(turned, part).wait_recv()

            def some(i, _, part=part):
                at = span(i * 16, 16)
                total = held[turned, part, at, :].astype(f32) + near[turned, part, at, :].astype(f32)
                if turned:
                    obranch_ref[span(part * half + i * 16, 16), :] = total
                else:
                    held[0, part, at, :] = total.astype(bf16)
                return 0

            lax.fori_loop(0, half // 16, some, 0)
            if not turned:
                over_copy(part).start()

    @pl.when(step == 0)
    def _():
        enter((*ring, across, beside))
        for k in (0, 1):
            for way in (0, 1):
                hop(k, way, 0).start()
        for turned in (0, 1):
            for part in (0, 1):
                near_copy(turned, part).start()
                held_copy(turned, part).start()
        own_copy().start()
        dxh[T : T + 8, :] = jnp.zeros((8, wide), f32)
        dstate[...] = jnp.zeros_like(dstate)
        acc[...] = jnp.zeros_like(acc)
        hacc[...] = jnp.zeros_like(hacc)
        turn[...] = jnp.zeros_like(turn)

    @pl.when(step == 1)
    def _():
        own_copy().wait()
        add_near(0)

    pl.when(step == 2)(functools.partial(add_near, 1))
    ring_poll(0)

    low_half = block_iota(1) < P_SIZE
    row_at, col_at = block_iota(0), block_iota(1)
    until = row_at <= col_at
    before = row_at < col_at
    upper = jnp.where(until, 1.0, 0.0).astype(f32)
    strict = jnp.where(before, 1.0, 0.0).astype(f32)
    low_tri = jnp.where(row_at >= col_at, 1.0, 0.0).astype(bf16)

    def add(index, cols, value):
        acc[index, :, cols] += jnp.sum(value.reshape(T // 8, 8, LANES), axis=0)

    def conv_back(rows, block, d_act, xc, s, act):
        cols = slice(block * LANES, (block + 1) * LANES)
        dxh[0:T, cols] = d_act * (s + act * (1.0 - s))
        v = v_ref[rows, cols].astype(f32)
        total = None
        for m in range(CONV):
            moved = dxh[m : m + T, cols]
            if m == 0:
                add(CONV, cols, moved)
            add(CONV - 1 - m, cols, v * moved)
            term = taps_ref[CONV - 1 - m : CONV - m, cols] * moved
            total = term if total is None else total + term
        d_ref[rows, cols] = total.astype(bf16)

    for sub in reversed(range(ROWS // T)):
        rows = slice(sub * T, (sub + 1) * T)
        raw, dt, decay = head_rows(dr_ref, head_ref, rows)
        decay_t = decay.T
        b_cols = slice(width, width + NS)
        c_cols = slice(width + NS, width + 2 * NS)
        b_xc, c_xc = xc_ref[rows, b_cols], xc_ref[rows, c_cols]
        b_s, c_s = sigmoid(b_xc), sigmoid(c_xc)
        b_act, c_act = b_xc * b_s, c_xc * c_s
        b_low, c_low = b_act.astype(bf16), c_act.astype(bf16)
        c_t = c_low.T
        scores_t = jnp.where(until, mm(b_low, c_low, NT), 0.0)
        ds_low = dstate[...].astype(bf16)
        yst[...] = mm(c_low, st_ref[sub])
        bds[...] = mm(b_low, ds_low)
        d_scores = jnp.zeros((T, LANES), f32)
        for p in range(pairs):
            cols = slice(p * LANES, (p + 1) * LANES)
            dy = dy_ref[rows, cols]
            xc = xc_ref[rows, cols]
            xs = sigmoid(xc)
            x = xc * xs
            l1, l2 = spread(decay[:, 2 * p : 2 * p + 1]), spread(decay[:, 2 * p + 1 : 2 * p + 2])
            both = jnp.where(low_half, l1, l2)
            dtb = jnp.where(
                low_half, spread(dt[:, 2 * p : 2 * p + 1]), spread(dt[:, 2 * p + 1 : 2 * p + 2])
            )
            u = x * dtb
            last = both[T - 1 : T, :]
            e1 = jnp.exp(jnp.minimum(decay_t[2 * p : 2 * p + 1, :] - l1, 0.0))
            e2 = jnp.exp(jnp.minimum(decay_t[2 * p + 1 : 2 * p + 2, :] - l2, 0.0))
            dy_low = dy.astype(bf16)
            zero = jnp.zeros_like(dy_low)
            u_low = u.astype(bf16)
            du_in = mm(
                jnp.concatenate([(scores_t * e1).astype(bf16), (scores_t * e2).astype(bf16)], axis=1),
                jnp.concatenate(
                    [jnp.where(low_half, dy_low, zero), jnp.where(low_half, zero, dy_low)], axis=0
                ),
            )
            d_mix = mm(
                jnp.concatenate(
                    [jnp.where(low_half, u_low, zero), jnp.where(low_half, zero, u_low)], axis=0
                ),
                dy_low,
                NT,
            )
            d1, d2 = d_mix[:T] * e1, d_mix[T:] * e2
            d_scores = d_scores + d1 + d2
            reach = mm(
                jnp.concatenate([(d1 * scores_t).astype(bf16), (d2 * scores_t).astype(bf16)], axis=0),
                low_tri,
            )
            turn[2 * p : 2 * p + 1, :] = jnp.sum(jnp.where(before, reach[:T], 0.0), axis=0, keepdims=True)
            turn[2 * p + 1 : 2 * p + 2, :] = jnp.sum(
                jnp.where(before, reach[T:], 0.0), axis=0, keepdims=True
            )
            tail = jnp.exp(last - both)
            dye = dy * jnp.exp(both)
            du_out = tail * bds[:, cols]
            du = du_in + du_out
            gin[:, cols] = (dye * yst[:, cols]).astype(bf16)
            gout[:, cols] = (u * du_out).astype(bf16)
            xdu[:, cols] = (x * du).astype(bf16)
            dyeb[:, cols] = dye.astype(bf16)
            utb[:, cols] = (u * tail).astype(bf16)
            add(CONV + 1, cols, dy * x)
            conv_back(rows, p, dtb * du + chan_ref[1:2, cols] * dy, xc, xs, x)
        d_scores = jnp.where(until, d_scores, 0.0).astype(bf16)
        d_b = mm(d_scores, c_low) + mm(utb[...], ds_low, NT)
        d_c = mm(d_scores, b_low, TN) + mm(dyeb[...], st_ref[sub], NT)
        conv_back(rows, pairs, d_b, b_xc, b_s, b_act)
        conv_back(rows, pairs + 1, d_c, c_xc, c_s, c_act)
        ended = jnp.zeros((1, LANES), f32)
        for p in range(pairs):
            cols = slice(p * LANES, (p + 1) * LANES)
            last = jnp.where(
                low_half[0:1], decay[T - 1 : T, 2 * p : 2 * p + 1], decay[T - 1 : T, 2 * p + 1 : 2 * p + 2]
            )
            fade = jnp.exp(last)
            before_ds = dstate[:, cols]
            through = jnp.sum(before_ds * st_ref[sub, :, cols].astype(f32), axis=0, keepdims=True) * fade
            ended = ended + mm_exact(through, pick_ref[cols, :].astype(f32))
            dstate[:, cols] = fade * before_ds + mm(c_t, dyeb[:, cols])
        gin_heads = mm(gin[...], pick_ref[...])
        gout_heads = mm(gout[...], pick_ref[...])
        reached = (
            turn[...].T
            + mm_exact(upper, gin_heads)
            + mm_exact(strict, gout_heads, TN)
            + ended
        )
        d_raw = (head_ref[1:2, :] * reached + mm(xdu[...], pick_ref[...])) * sigmoid(raw)
        d_ref[rows, wide:] = d_raw.astype(bf16)
        hacc[0] += jnp.sum(d_raw.reshape(T // 8, 8, LANES), axis=0)
        hacc[1] += jnp.sum((dt * reached).reshape(T // 8, 8, LANES), axis=0)
        dxh[T : T + 8, :] = dxh[0:8, :]
        if sub == 1:
            ring_poll(1)

    @pl.when(step == steps - 1)
    def _():
        total = lambda a: jnp.sum(a, axis=0, keepdims=True)
        for k in range(CONV + 1):
            small_ref[k : k + 1, :] = total(acc[k])
        small_ref[CONV + 1 : CONV + 2, :width] = total(gate_ref[...])
        small_ref[CONV + 1 : CONV + 2, width : width + LANES] = total(hacc[0])
        small_ref[CONV + 1 : CONV + 2, width + LANES :] = total(hacc[1])
        small_ref[CONV + 2 :, :] = jnp.zeros((2, wide), f32)
        skip = mm_exact(acc[CONV + 1, :, :width], pick_ref[...].astype(f32))
        small_ref[CONV + 3 : CONV + 4, 512 : 512 + LANES] = total(skip)
        for part in (0, 1):
            over_copy(part).wait_recv()

            def some(i, _, part=part):
                at = span(part * half + i * 16, 16)
                obranch_ref[at, :] = obranch_ref[at, :] + over_slot[part, span(i * 16, 16), :].astype(f32)
                return 0

            lax.fori_loop(0, half // 16, some, 0)
        for part in (0, 1):
            over_copy(part).wait_send()
            for turned in (0, 1):
                near_copy(turned, part).wait_send()
        for h in range(n - 1):
            for k in (0, 1):
                for way in (0, 1):
                    hop(k, way, h).wait_send()


def ssd_backward(n, dy, v, xc, dr, st, gate, taps, head, chan, pick, early, branch):
    length, width = dy.shape
    wide = width + 2 * NS
    steps = length // ROWS
    subs = ROWS // T
    own_rows, tokens = D // n, length // 4
    half = tokens // 2
    row = lambda m: pl.BlockSpec((ROWS, m), lambda i: (steps - 1 - i, 0))
    whole = lambda a: pl.BlockSpec(a.shape, lambda i: (0,) * a.ndim, pipeline_mode=pl.Buffered(1))
    fixed = lambda *shape: pl.BlockSpec(shape, lambda i: (0,) * len(shape))
    anywhere = pl.BlockSpec(memory_space=pl.ANY)
    vm, dma = pltpu.VMEM, pltpu.SemaphoreType.DMA
    return pl.pallas_call(
        functools.partial(backward_body, n, own_rows, tokens, width),
        grid=(steps,),
        in_specs=[
            row(width), row(wide), row(wide), row(LANES),
            pl.BlockSpec((subs, NS, width), lambda i: (steps - 1 - i, 0, 0)),
            whole(gate), whole(taps), whole(head), whole(chan), whole(pick), anywhere, anywhere,
        ],
        out_specs=[
            row(wide + LANES), fixed(8, wide), fixed(own_rows, 2 * width), fixed(tokens, D),
        ],
        out_shape=[
            jax.ShapeDtypeStruct((length, wide + LANES), bf16),
            jax.ShapeDtypeStruct((8, wide), f32),
            jax.ShapeDtypeStruct((own_rows, 2 * width), f32),
            jax.ShapeDtypeStruct((tokens, D), f32),
        ],
        scratch_shapes=[
            vm((T + 8, wide), f32), vm((NS, width), f32), vm((T, width), f32), vm((T, width), f32),
            vm((T, width), bf16), vm((T, width), bf16), vm((T, width), bf16), vm((T, width), bf16),
            vm((T, width), bf16), vm((T, LANES), f32), vm((CONV + 2, 8, wide), f32), vm((2, 8, LANES), f32),
            vm((D, 2 * width), bf16),
            [[vm((n - 1, size, width), bf16) for _ in (0, 1)] for _, size in cut_rows(own_rows)],
            vm((2, 2, half, D), bf16), vm((2, 2, half, D), bf16), vm((2, half, D), bf16),
            dma((5,)), dma((2, 2, n - 1)), dma((2, 2, n - 1)), dma((2, 2)), dma((2, 2)), dma((2,)), dma((2,)),
        ],
        compiler_params=pltpu.CompilerParams(
            collective_id=3, has_side_effects=True, vmem_limit_bytes=58 * 2**20
        ),
        name="layer_backward",
    )(dy, v, xc, dr, st, gate, taps, head, chan, pick, early, branch)


def reduce_body(
    n, rows, tokens, starts,
    xg_ref, d_ref, dz_ref, w_ref, small_ref,
    oxs_ref, oback_ref, bc_ref, osmall_ref,
    xg, d, dz, w, grads, slots, staged, near, over, gains, smalls, tens, bc_slot,
    load_sem, ring_send, ring_recv, near_send, near_recv, over_send, over_recv,
    small_send, small_recv, ten_send, ten_recv, bc_send, bc_recv,
):
    pos, ring, me, across, beside = neighbours(n)
    cuts = cut_rows(rows)
    core = lax.rem(me, 2)
    opposite = lax.rem(me + 2, 4)
    next_door = me + 1 - 2 * core
    far = lax.rem(next_door + 2, 4)
    half = tokens // 2
    wide = d.shape[1]
    width = dz.shape[1]
    loads = []
    for k, (src, dst) in enumerate(
        ((xg_ref, xg), (d_ref, d), (dz_ref, dz), (w_ref, w), (small_ref, smalls.at[pos]))
    ):
        loads.append(pltpu.make_async_copy(src, dst, load_sem.at[k]))
        loads[-1].start()
    enter((*ring, across, beside))
    started = []

    def go(*args):
        copy = remote(*args)
        copy.start()
        started.append(copy)

    def block_at(way, count):
        return ring_index(lax.rem(pos + (count if way else n - count), n), n)

    def product(k):
        lo, hi = starts[k]

        def some(i, _):
            at = pl.ds(pl.multiple_of(i * 2 * LANES, 2 * LANES), 2 * LANES)
            grads[at, lo:hi] = mm(xg[:, at], d[:, lo:hi], TN).astype(bf16)
            return 0

        lax.fori_loop(0, D // (2 * LANES), some, 0)
        for way in (0, 1):
            first, size = cuts[way]
            go(
                grads.at[span(block_at(way, 1) * rows + first, size), pl.ds(lo, hi - lo)],
                slots[way][k].at[0], ring_send.at[way, k, 0], ring_recv.at[way, k, 0], ring[way],
            )

    def back(target, part):
        at = span(target * tokens + part * half, half)
        total = mm(dz[at, :], w[:, :width], NT) + mm(d[at, :], w[:, width:], NT)
        gains[...] += jnp.sum((total * xg[at, :].astype(f32)).reshape(half // 8, 8, D), axis=0)
        return total

    def near_copy(turned, part):
        return remote(
            staged.at[turned, part], near.at[turned, part],
            near_send.at[turned, part], near_recv.at[turned, part], beside,
        )

    def over_copy(part):
        return remote(near.at[0, part], over.at[part], over_send.at[part], over_recv.at[part], across)

    def give(turned):
        def some(part, _):
            staged[turned, part] = back(next_door if turned else far, part).astype(bf16)
            near_copy(turned, part).start()
            return 0

        lax.fori_loop(0, 2, some, 0)

    def take(turned):
        def some(part, _):
            total = back(me if turned else opposite, part)
            near_copy(turned, part).wait_recv()
            total = total + near[turned, part].astype(f32)
            if turned:
                oback_ref[span(part * half, half), :] = total
            else:
                near[0, part] = total.astype(bf16)
                over_copy(part).start()
            return 0

        lax.fori_loop(0, 2, some, 0)

    def ring_turn(k, h):
        lo, hi = starts[k]
        for way in (0, 1):
            first, size = cuts[way]
            slot = slots[way][k].at[h]
            remote(slot, slot, ring_send.at[way, k, h], ring_recv.at[way, k, h], ring[way]).wait_recv()
            block = block_at(way, 2 + h) if h < n - 2 else block_at(way, 0)

            def some(i, _, way=way, first=first, block=block):
                total = slots[way][k][h, span(i * 16, 16), :].astype(f32)
                total = total + grads[span(block * rows + first + i * 16, 16), lo:hi].astype(f32)
                if h < n - 2:
                    slots[way][k][h, span(i * 16, 16), :] = total.astype(bf16)
                else:
                    oxs_ref[span(first + i * 16, 16), lo:hi] = total
                return 0

            lax.fori_loop(0, size // 16, some, 0)
            if h < n - 2:
                go(
                    slot, slots[way][k].at[h + 1],
                    ring_send.at[way, k, h + 1], ring_recv.at[way, k, h + 1], ring[way],
                )

    def small_hop(way, h):
        here = smalls.at[lax.rem(pos + (h if way else n - h), n)]
        go(here, here, small_send.at[way, h], small_recv.at[way, h], ring[way])

    def small_lands(way, h):
        here = smalls.at[lax.rem(pos + (h + 1 if way else n - h - 1), n)]
        remote(here, here, small_send.at[way, h], small_recv.at[way, h], ring[way]).wait_recv()

    gains[...] = jnp.zeros_like(gains)
    loads[0].wait()
    loads[1].wait()
    product(0)
    loads[2].wait()
    loads[3].wait()
    give(0)
    product(1)
    take(0)
    ring_turn(0, 0)
    give(1)
    ring_turn(1, 0)
    ring_turn(0, 1)
    take(1)
    ring_turn(1, 1)
    loads[4].wait()
    gain = jnp.sum(gains[...], axis=0, keepdims=True)
    smalls[pos, 6:7, :] = gain[:, :1024]
    smalls[pos, 7:8, 0:512] = gain[:, 1024:]
    for h in range(2, n - 1):
        s = h - 2
        if s < n // 2:
            for way in (0, 1):
                if s > 0 and (way == 0 or s < n // 2):
                    small_lands(way, s - 1)
                if way == 0 or s < n // 2 - 1:
                    small_hop(way, s)
        for k in (0, 1):
            ring_turn(k, h)
            if h == n - 2 and k == 0:
                bc_slot[0] = oxs_ref[:, starts[0][0] : starts[0][0] + 2 * NS]
                go(bc_slot.at[0], bc_slot.at[1], bc_send.at[0], bc_recv.at[0], beside)
    for s in range(n - 3, n // 2):
        for way in (0, 1):
            if s > 0:
                small_lands(way, s - 1)
            if way == 0 or s < n // 2 - 1:
                small_hop(way, s)
    small_lands(0, n // 2 - 1)

    total = smalls[0]
    for i in range(1, n):
        total = total + smalls[i]
    tens[me] = total
    go(tens.at[me], tens.at[me], ten_send.at[0], ten_recv.at[0], beside)
    remote(bc_slot.at[1], bc_slot.at[1], bc_send.at[0], bc_recv.at[0], beside).wait_recv()
    bc_slot[2] = bc_slot[0] + bc_slot[1]
    go(bc_slot.at[2], bc_slot.at[3], bc_send.at[1], bc_recv.at[1], across)
    here = tens.at[next_door]
    remote(here, here, ten_send.at[0], ten_recv.at[0], beside).wait_recv()
    for k, target in ((0, me), (1, next_door)):
        here = tens.at[target]
        go(here, here, ten_send.at[1 + k], ten_recv.at[1 + k], across)
    for part in (0, 1):
        over_copy(part).wait_recv()

        def some(i, _, part=part):
            at = span(part * half + i * 16, 16)
            oback_ref[at, :] = oback_ref[at, :] + over[part, span(i * 16, 16), :].astype(f32)
            return 0

        lax.fori_loop(0, half // 16, some, 0)
    for k, target in ((0, opposite), (1, far)):
        here = tens.at[target]
        remote(here, here, ten_send.at[1 + k], ten_recv.at[1 + k], across).wait_recv()
    osmall_ref[...] = tens[...]
    remote(bc_slot.at[3], bc_slot.at[3], bc_send.at[1], bc_recv.at[1], across).wait_recv()
    bc_ref[...] = bc_slot[2] + bc_slot[3]
    for part in (0, 1):
        over_copy(part).wait_send()
        for turned in (0, 1):
            near_copy(turned, part).wait_send()
    for copy in started:
        copy.wait_send()


def reduce_all(n, xg, d, dz, w, small):
    rows, tokens = D // n, xg.shape[0] // 4
    width, late = dz.shape[1], d.shape[1]
    starts = ((width, late), (0, width))
    half = tokens // 2
    dma, vm = pltpu.SemaphoreType.DMA, pltpu.VMEM
    anywhere = pl.BlockSpec(memory_space=pl.ANY)
    inside = pl.BlockSpec(memory_space=pltpu.VMEM)
    return pl.pallas_call(
        functools.partial(reduce_body, n, rows, tokens, starts),
        in_specs=[anywhere] * 5,
        out_specs=[inside] * 4,
        out_shape=[
            jax.ShapeDtypeStruct((rows, late), f32),
            jax.ShapeDtypeStruct((tokens, D), f32),
            jax.ShapeDtypeStruct((rows, 2 * NS), f32),
            jax.ShapeDtypeStruct((4, *small.shape), f32),
        ],
        scratch_shapes=[
            vm(xg.shape, bf16), vm(d.shape, bf16), vm(dz.shape, bf16), vm(w.shape, bf16), vm((D, late), bf16),
            [[vm((n - 1, size, hi - lo), bf16) for lo, hi in starts] for _, size in cut_rows(rows)],
            vm((2, 2, half, D), bf16), vm((2, 2, half, D), bf16), vm((2, half, D), bf16), vm((8, D), f32),
            vm((n, *small.shape), f32), vm((4, *small.shape), f32), vm((4, rows, 2 * NS), f32),
            dma((5,)), dma((2, 2, n - 1)), dma((2, 2, n - 1)), dma((2, 2)), dma((2, 2)), dma((2,)), dma((2,)),
            dma((2, n // 2)), dma((2, n // 2)), dma((3,)), dma((3,)), dma((2,)), dma((2,)),
        ],
        compiler_params=pltpu.CompilerParams(
            collective_id=1, has_side_effects=True, vmem_limit_bytes=60 * 2**20
        ),
        name="reduce_all",
    )(xg, d, dz, w, small)


def adamw_step(weight, first, second, grad, rate, decay):
    first_new = beta_first * first + (1.0 - beta_first) * grad
    second_new = beta_second * second + (1.0 - beta_second) * grad * grad
    hat_first = first_new / (1.0 - beta_first**STEP)
    hat_second = second_new / (1.0 - beta_second**STEP)
    weight_new = weight - rate * (hat_first / (jnp.sqrt(hat_second) + adam_eps) + decay * weight)
    return (weight_new, first_new, second_new)


def local(
    layer_input,
    out_grad,
    small_params,
    small_first,
    small_second,
    w_zx,
    zx_first,
    zx_second,
    w_bc,
    bc_first,
    bc_second,
    w_dt,
    dt_first,
    dt_second,
    w_out,
    out_first,
    out_second,
):
    tensor_index = lax.axis_index("tensor")
    local_in = layer_input.astype(f32)
    gain_in, gate_gain, conv_x, bias_x, conv_bc, bias_bc, dt_bias, a_log, d_skip = unpack(
        small_params
    )
    rows_own = w_zx.shape[0]
    width = w_zx.shape[2]
    heads = w_dt.shape[1]
    chan_start = tensor_index * width
    head_start = tensor_index * heads
    gate_local = lax.dynamic_slice_in_dim(gate_gain, chan_start, width, 0)
    conv_local = lax.dynamic_slice_in_dim(conv_x, chan_start, width, 1)
    bias_local = lax.dynamic_slice_in_dim(bias_x, chan_start, width, 0)
    dtb_local = lax.dynamic_slice_in_dim(dt_bias, head_start, heads, 0)
    a_local = -jnp.exp(lax.dynamic_slice_in_dim(a_log, head_start, heads, 0))
    dskip_local = lax.dynamic_slice_in_dim(d_skip, head_start, heads, 0)
    taps = jnp.concatenate(
        [
            jnp.concatenate([conv_local, conv_bc], axis=1),
            jnp.concatenate([bias_local, bias_bc])[None, :],
            jnp.zeros((8 - CONV - 1, width + 2 * NS), f32),
        ],
        axis=0,
    )
    lanes = lambda v: jnp.pad(v, (0, LANES - heads))
    head = jnp.pad(jnp.stack([lanes(dtb_local), lanes(a_local)]), ((0, 6), (0, 0)))
    chan = jnp.pad(jnp.stack([gate_local, jnp.repeat(dskip_local, P_SIZE)]), ((0, 6), (0, 0)))
    pick = jnp.asarray(
        (jnp.arange(width)[:, None] // P_SIZE == jnp.arange(LANES)[None, :]), bf16
    )

    inv_in = lax.rsqrt(jnp.mean(local_in * local_in, axis=-1, keepdims=True) + norm_eps)
    normed_in = local_in * inv_in * gain_in[None, :]
    w_cat = jnp.concatenate(
        [
            w_zx.reshape(rows_own, 2 * width).astype(bf16),
            w_bc.astype(bf16),
            jnp.pad(w_dt, ((0, 0), (0, LANES - heads))).astype(bf16),
        ],
        axis=1,
    )
    n = lax.axis_size("dp")
    xg, w_all = gather_all(n, normed_in.astype(bf16), w_cat)
    z, v, xc, dr, y, dn, st, red, cot_all, wo_all = ssd_forward(
        n, xg, w_all, taps, head, chan, out_grad, w_out.astype(bf16)
    )
    dy, dz, branch, early, gate = early_gradients(z, y, dn, red, wo_all, chan, xg, cot_all)
    d_late, small, owner_early, own_branch = ssd_backward(
        n, dy, v, xc, dr, st, gate, taps, head, chan, pick, early, branch
    )
    owner_late, d_normed_in, owner_bc, tens = reduce_all(n, xg, d_late, dz, w_all, small)
    layer_output = (local_in + own_branch).astype(bf16)
    owner_zx = jnp.stack([owner_early[:, :width], owner_late[:, :width]], axis=1)
    owner_out = owner_early[:, width:]
    owner_dt = owner_late[:, width + 2 * NS : width + 2 * NS + heads]

    inner_in = jnp.sum(local_in * gain_in[None, :] * d_normed_in, axis=-1, keepdims=True)
    input_grad = (
        out_grad.astype(f32)
        + inv_in * gain_in[None, :] * d_normed_in
        - local_in * (inv_in * inv_in * inv_in * inner_in / D)
    )
    gain_sum = jnp.sum(tens[:, 6:8], axis=0).reshape(-1)[:D] / gain_in
    bc_sum = jnp.sum(tens[:, : CONV + 1, width:], axis=0)
    small_grad = jnp.concatenate(
        [
            gain_sum,
            tens[:, CONV + 1, :width].reshape(-1),
            jnp.moveaxis(tens[:, :CONV, :width], 0, 1).reshape(-1),
            tens[:, CONV, :width].reshape(-1),
            bc_sum.reshape(-1),
            tens[:, CONV + 1, width : width + heads].reshape(-1),
            tens[:, CONV + 1, width + LANES : width + LANES + heads].reshape(-1) * -jnp.exp(a_log),
            tens[:, 7, 512 : 512 + heads].reshape(-1),
        ]
    )
    small_new, small_first_new, small_second_new = adamw_step(
        small_params, small_first, small_second, small_grad, small_rate, 0.0
    )
    zx_new, zx_first_new, zx_second_new = adamw_step(
        w_zx, zx_first, zx_second, owner_zx, matrix_rate, matrix_decay
    )
    bc_new, bc_first_new, bc_second_new = adamw_step(
        w_bc, bc_first, bc_second, owner_bc, matrix_rate, matrix_decay
    )
    dt_new, dt_first_new, dt_second_new = adamw_step(
        w_dt, dt_first, dt_second, owner_dt, matrix_rate, matrix_decay
    )
    out_new, out_first_new, out_second_new = adamw_step(
        w_out, out_first, out_second, owner_out, matrix_rate, matrix_decay
    )
    return (
        layer_output,
        input_grad,
        small_new,
        small_first_new,
        small_second_new,
        zx_new,
        zx_first_new,
        zx_second_new,
        bc_new,
        bc_first_new,
        bc_second_new,
        dt_new,
        dt_first_new,
        dt_second_new,
        out_new,
        out_first_new,
        out_second_new,
    )


def solution(mesh):
    return jax.shard_map(
        local,
        mesh=mesh,
        in_specs=(
            P(("dp", "tensor"), None),
            P(("dp", "tensor"), None),
            P(),
            P(),
            P(),
            P("dp", None, "tensor"),
            P("dp", None, "tensor"),
            P("dp", None, "tensor"),
            P("dp", None),
            P("dp", None),
            P("dp", None),
            P("dp", "tensor"),
            P("dp", "tensor"),
            P("dp", "tensor"),
            P("dp", "tensor"),
            P("dp", "tensor"),
            P("dp", "tensor"),
        ),
        out_specs=(
            P(("dp", "tensor"), None),
            P(("dp", "tensor"), None),
            P(),
            P(),
            P(),
            P("dp", None, "tensor"),
            P("dp", None, "tensor"),
            P("dp", None, "tensor"),
            P("dp", None),
            P("dp", None),
            P("dp", None),
            P("dp", "tensor"),
            P("dp", "tensor"),
            P("dp", "tensor"),
            P("dp", "tensor"),
            P("dp", "tensor"),
            P("dp", "tensor"),
        ),
        check_vma=False,
    )
```

```python
import functools

import jax
import jax.numpy as jnp
from jax import lax
from jax.experimental import pallas as pl
from jax.experimental.pallas import tpu as pltpu
from jax.sharding import PartitionSpec as P

D = 1536
DI = 3072
H = 48
NS = 128
P_SIZE = 64
CONV = 4
LEN = 2048
STEP = 10

T = 128
ROWS = 256
LANES = 128
ROOM = 60 * 2**20

norm_eps = 1e-05
adam_eps = 1e-08
beta_first = 0.9
beta_second = 0.95
matrix_rate = 0.01
small_rate = 0.1
matrix_decay = 0.1

f32 = jnp.float32
bf16 = jnp.bfloat16
NN = (((1,), (0,)), ((), ()))
NT = (((1,), (1,)), ((), ()))
TN = (((0,), (0,)), ((), ()))
HIGHEST = lax.Precision.HIGHEST


def unpack(flat):
    gain_in = flat[:D]
    cursor = D
    gate_gain = flat[cursor : cursor + DI]
    cursor = cursor + DI
    conv_x = flat[cursor : cursor + CONV * DI].reshape(CONV, DI)
    cursor = cursor + CONV * DI
    bias_x = flat[cursor : cursor + DI]
    cursor = cursor + DI
    conv_bc = flat[cursor : cursor + CONV * 2 * NS].reshape(CONV, 2 * NS)
    cursor = cursor + CONV * 2 * NS
    bias_bc = flat[cursor : cursor + 2 * NS]
    cursor = cursor + 2 * NS
    dt_bias = flat[cursor : cursor + H]
    a_log = flat[cursor + H : cursor + 2 * H]
    d_skip = flat[cursor + 2 * H : cursor + 3 * H]
    return (gain_in, gate_gain, conv_x, bias_x, conv_bc, bias_bc, dt_bias, a_log, d_skip)


def mm(a, b, dims=NN):
    return lax.dot_general(a, b, dims, preferred_element_type=f32)


def mm_exact(a, b, dims=NN):
    return lax.dot_general(a, b, dims, preferred_element_type=f32, precision=HIGHEST)


def sigmoid(v):
    return 0.5 * jnp.tanh(0.5 * v) + 0.5


def softplus(v):
    return jnp.maximum(v, 0.0) + jnp.log1p(jnp.exp(-jnp.abs(v)))


def spread(col):
    return jnp.broadcast_to(col, (T, LANES))


def block_iota(axis):
    return lax.broadcasted_iota(jnp.int32, (T, LANES), axis)


def head_rows(dr_ref, head_ref, rows):
    raw = dr_ref[rows, :] + head_ref[0:1, :]
    dt = softplus(raw)
    low_tri = jnp.where(block_iota(0) >= block_iota(1), 1.0, 0.0).astype(f32)
    decay = mm_exact(low_tri, dt * head_ref[1:2, :])
    return raw, dt, decay


def ring_place(n):
    me = lax.axis_index("dp")
    z, x = lax.div(me, 2), lax.rem(me, 2)
    return z + x * (n - 1 - 2 * z)


def ring_index(pos, n):
    back = lax.div(pos, n // 2)
    return 2 * pos + back * (2 * n - 1 - 4 * pos)


def neighbours(n):
    pos = ring_place(n)
    right = ring_index(lax.rem(pos + 1, n), n)
    left = ring_index(lax.rem(pos + n - 1, n), n)
    me = lax.axis_index("tensor")
    y, core = lax.div(me, 2), lax.rem(me, 2)
    across = 2 * (1 - y) + core
    beside = 2 * y + 1 - core
    return pos, ({"dp": right}, {"dp": left}), me, {"tensor": across}, {"tensor": beside}


def enter(peers):
    barrier = pltpu.get_barrier_semaphore()
    for peer in peers:
        pl.semaphore_signal(barrier, inc=1, device_id=peer, device_id_type=pl.DeviceIdType.MESH)
    pl.semaphore_wait(barrier, len(peers))


def remote(src, dst, send_sem, recv_sem, peer):
    return pltpu.make_async_remote_copy(
        src_ref=src, dst_ref=dst, send_sem=send_sem, recv_sem=recv_sem,
        device_id=peer, device_id_type=pl.DeviceIdType.MESH,
    )


def span(start, size):
    return pl.ds(pl.multiple_of(start, 16), size)


def strip(rows):
    return next(size for size in (48, 32, 16) if rows % size == 0)


def cut_rows(rows):
    top = rows // 32 * 16
    return ((0, top), (top, rows - top))


def forward_body(
    n, rows, tokens, width,
    xg_ref, tall_ref, w_ref, taps_ref, head_ref, chan_ref, cot_ref, wp_ref,
    z_ref, v_ref, xc_ref, dr_ref, y_ref, dn_ref, st_ref, red_ref, cots_ref, wps_ref,
    halo, state, y_all, cots, wps, sums,
    own_keep, ring_keep, over_keep, side_keep, pass_keep, ring_send, ring_recv, over_send, over_recv,
    side_send, side_recv, pass_send, pass_recv, sum_send, sum_recv,
):
    pairs = width // LANES
    wide = width + 2 * NS
    step = pl.program_id(0)
    steps = LEN // ROWS
    tall = 2 * ROWS
    gating, norming = steps, steps + LEN // tall
    last_step = norming + LEN // tall - 1
    pos, ring, me, across, beside = neighbours(n)
    opposite = lax.rem(me + 2, 4)
    next_door = me + 1 - 2 * lax.rem(me, 2)
    far = lax.rem(next_door + 2, 4)
    half = tokens // 2
    hops = n // 2
    cuts = cut_rows(rows)
    mine = ring_index(pos, n)

    def hop(k, part, way, h):
        first, size = cuts[part]
        cols = pl.ds(k * width, width)
        block = ring_index(lax.rem(pos + (h if way else n - h), n), n)
        here = wps.at[span(block * rows + first, size), cols]
        src = wp_ref.at[pl.ds(first, size), cols] if h == 0 else here
        return remote(src, here, ring_send.at[way, part, k, h], ring_recv.at[way, part, k, h], ring[way])

    def hop_lands(k, part, way, h):
        first, size = cuts[part]
        block = ring_index(lax.rem(pos + (h + 1 if way else n - h - 1), n), n)
        return span(block * rows + first, size), pl.ds(k * width, width)

    def hop_arrival(k, part, way, h):
        here = wps.at[hop_lands(k, part, way, h)]
        return remote(here, here, ring_send.at[way, part, k, h], ring_recv.at[way, part, k, h], ring[way])

    def hop_keep(k, part, way, h):
        at = hop_lands(k, part, way, h)
        return pltpu.make_async_copy(wps.at[at], wps_ref.at[at], ring_keep.at[way, part, k, h])

    def hop_ways(h):
        return [(part, way) for part in (0, 1) for way in (0, 1) if h < hops - 1 or part == way]

    def hop_on(k, h):
        for part, way in hop_ways(h - 1) if h > 0 else ():
            hop_arrival(k, part, way, h - 1).wait_recv()
            hop_keep(k, part, way, h - 1).start()
            if h < hops and (part, way) in hop_ways(h):
                hop(k, part, way, h).start()
        if h == 0:
            for part, way in hop_ways(0):
                hop(k, part, way, 0).start()

    def over(k):
        return remote(
            cot_ref.at[pl.ds(k * half, half)], cots.at[span(me * tokens + k * half, half)],
            over_send.at[k], over_recv.at[k], across,
        )

    def landed(full, start, size, send, recv, peer):
        here = full.at[span(start, size)]
        return remote(here, here, send, recv, peer)

    def over_arrival(k):
        start = opposite * tokens + k * half
        return landed(cots, start, half, over_send.at[k], over_recv.at[k], across)

    def passing(k):
        start = opposite * tokens + k * half
        return landed(cots, start, half, pass_send.at[k], pass_recv.at[k], beside)

    def pass_arrival(k):
        return landed(cots, far * tokens + k * half, half, pass_send.at[k], pass_recv.at[k], beside)

    def side():
        return remote(cot_ref, cots.at[span(me * tokens, tokens)], side_send.at[0], side_recv.at[0], beside)

    def side_arrival():
        return landed(cots, next_door * tokens, tokens, side_send.at[0], side_recv.at[0], beside)

    def keep(start, size, sem):
        return pltpu.make_async_copy(cots.at[span(start, size)], cots_ref.at[span(start, size)], sem)

    def own_keeps():
        return (
            pltpu.make_async_copy(cot_ref, cots_ref.at[span(me * tokens, tokens)], own_keep.at[0]),
            pltpu.make_async_copy(wp_ref, wps_ref.at[span(mine * rows, rows)], own_keep.at[1]),
            pltpu.make_async_copy(cot_ref, cots.at[span(me * tokens, tokens)], own_keep.at[2]),
            pltpu.make_async_copy(wp_ref, wps.at[span(mine * rows, rows)], own_keep.at[3]),
        )

    @pl.when(step == 0)
    def _():
        enter((*ring, across, beside))
        hop_on(0, 0)
        over(0).start()
        over(1).start()
        side().start()
        for copy in own_keeps():
            copy.start()
        halo[0:8, :] = jnp.zeros((8, wide), f32)
        state[...] = jnp.zeros_like(state)

    for h in range(1, hops + 1):
        pl.when(step == (gating if h == hops else min(2 * h, gating)))(functools.partial(hop_on, 0, h))
    for h in range(hops + 1):
        at = (3, 6, gating)[h] if h < 3 else min(gating + 2 * (h - 2), norming)
        pl.when(step == (norming if h == hops else at))(functools.partial(hop_on, 1, h))

    @pl.when(step == gating)
    def _():
        for k in (0, 1):
            over_arrival(k).wait_recv()
            passing(k).start()
            keep(opposite * tokens + k * half, half, over_keep.at[k]).start()
        for copy in own_keeps():
            copy.wait()

    @pl.when(step == norming)
    def _():
        side_arrival().wait_recv()
        keep(next_door * tokens, tokens, side_keep.at[0]).start()
        for k in (0, 1):
            pass_arrival(k).wait_recv()
            keep(far * tokens + k * half, half, pass_keep.at[k]).start()

    @pl.when(step < gating)
    def _():
        scan_step(
            width, step, xg_ref, w_ref, taps_ref, head_ref, chan_ref,
            v_ref, xc_ref, dr_ref, y_ref, st_ref, halo, state, y_all,
        )

    def token_sum(row, first, value):
        lanes = pl.ds(pl.multiple_of(first, tall), tall)
        sums[0, row : row + 4, lanes] = mm_exact(jnp.ones((8, LANES), f32), value, NT)[0:4]

    @pl.when((step >= gating) & (step < norming))
    def _():
        first = (step - gating) * tall
        z_ref[...] = mm(tall_ref[...], wps[:, :width])
        squares = jnp.zeros((tall, LANES), f32)
        for p in range(pairs):
            cols = slice(p * LANES, (p + 1) * LANES)
            z = z_ref[:, cols]
            gated = y_all[span(first, tall), cols] * (z * sigmoid(z))
            y_all[span(first, tall), cols] = gated
            squares = squares + gated * gated
        token_sum(0, first, squares)

    @pl.when(step >= norming)
    def _():
        first = (step - norming) * tall
        dn_ref[...] = mm(cots[span(first, tall), :], wps[:, width:])
        inner = jnp.zeros((tall, LANES), f32)
        for p in range(pairs):
            cols = slice(p * LANES, (p + 1) * LANES)
            inner = inner + y_all[span(first, tall), cols] * chan_ref[0:1, cols] * dn_ref[:, cols]
        token_sum(4, first, inner)

    @pl.when(step == last_step)
    def _():
        first = remote(sums.at[0], sums.at[1], sum_send.at[0], sum_recv.at[0], beside)
        first.start()
        first.wait_recv()
        sums[2] = sums[0] + sums[1]
        second = remote(sums.at[2], sums.at[3], sum_send.at[1], sum_recv.at[1], across)
        second.start()
        for h in range(hops):
            for part, way in hop_ways(h):
                for k in (0, 1):
                    hop(k, part, way, h).wait_send()
                    hop_keep(k, part, way, h).wait()
        side().wait_send()
        keep(next_door * tokens, tokens, side_keep.at[0]).wait()
        for k in (0, 1):
            over(k).wait_send()
            passing(k).wait_send()
            keep(opposite * tokens + k * half, half, over_keep.at[k]).wait()
            keep(far * tokens + k * half, half, pass_keep.at[k]).wait()
        first.wait_send()
        second.wait()
        red_ref[...] = sums[2] + sums[3]


def scan_step(
    width, step, xg_ref, w_ref, taps_ref, head_ref, chan_ref,
    v_ref, xc_ref, dr_ref, y_ref, st_ref, halo, state, y_all,
):
    pairs = width // LANES
    wide = width + 2 * NS
    dr_ref[...] = mm(xg_ref[...], w_ref[:, wide:])
    halo[8 : 8 + ROWS, :] = mm(xg_ref[...], w_ref[:, :wide])
    low_half = block_iota(1) < P_SIZE
    causal = block_iota(0) >= block_iota(1)

    def convolved(sub, block):
        cols = slice(block * LANES, (block + 1) * LANES)
        total = taps_ref[CONV : CONV + 1, cols]
        for k in range(CONV):
            first = 8 - (CONV - 1) + k + sub * T
            total = total + taps_ref[k : k + 1, cols] * halo[first : first + T, cols]
        rows = slice(sub * T, (sub + 1) * T)
        xc_ref[rows, cols] = total
        v_ref[rows, cols] = halo[8 + sub * T : 8 + (sub + 1) * T, cols].astype(bf16)
        return total * sigmoid(total)

    for sub in range(ROWS // T):
        rows = slice(sub * T, (sub + 1) * T)
        raw, dt, decay = head_rows(dr_ref, head_ref, rows)
        decay_t = decay.T
        b_low = convolved(sub, pairs).astype(bf16)
        c_low = convolved(sub, pairs + 1).astype(bf16)
        b_t = b_low.T
        scores = jnp.where(causal, mm(c_low, b_low, NT), 0.0)
        st_ref[sub] = state[...].astype(bf16)
        for p in range(pairs):
            cols = slice(p * LANES, (p + 1) * LANES)
            x = convolved(sub, p)
            l1, l2 = spread(decay[:, 2 * p : 2 * p + 1]), spread(decay[:, 2 * p + 1 : 2 * p + 2])
            both = jnp.where(low_half, l1, l2)
            dtb = jnp.where(
                low_half, spread(dt[:, 2 * p : 2 * p + 1]), spread(dt[:, 2 * p + 1 : 2 * p + 2])
            )
            u = x * dtb
            m1 = scores * jnp.exp(jnp.minimum(l1 - decay_t[2 * p : 2 * p + 1, :], 0.0))
            m2 = scores * jnp.exp(jnp.minimum(l2 - decay_t[2 * p + 1 : 2 * p + 2, :], 0.0))
            mixing = jnp.concatenate([m1.astype(bf16), m2.astype(bf16)], axis=1)
            parts = jnp.concatenate(
                [jnp.where(low_half, u, 0.0).astype(bf16), jnp.where(low_half, 0.0, u).astype(bf16)],
                axis=0,
            )
            last = both[T - 1 : T, :]
            entering = st_ref[sub, :, cols]
            y = mm(mixing, parts) + jnp.exp(both) * mm(c_low, entering) + chan_ref[1:2, cols] * x
            tail = (u * jnp.exp(last - both)).astype(bf16)
            state[:, cols] = jnp.exp(last) * state[:, cols] + mm(b_t, tail)
            y_ref[rows, cols] = y
            y_all[span(step * ROWS + sub * T, T), cols] = y
    halo[0:8, :] = halo[ROWS : ROWS + 8, :]


def ssd_forward(n, xg, w, taps, head, chan, cot, wp):
    length = xg.shape[0]
    rows, width = wp.shape[0], wp.shape[1] // 2
    tokens = cot.shape[0]
    wide = width + 2 * NS
    steps = length // ROWS
    tall = 2 * ROWS
    more = length // tall
    subs = ROWS // T
    assert length == LEN
    early = lambda i: jnp.minimum(i, steps - 1)
    middle = lambda i: jnp.clip(i - steps, 0, more - 1)
    row = lambda m: pl.BlockSpec((ROWS, m), lambda i: (early(i), 0))
    whole = lambda a: pl.BlockSpec(a.shape, lambda i: (0,) * a.ndim, pipeline_mode=pl.Buffered(1))
    anywhere = pl.BlockSpec(memory_space=pl.ANY)
    vm, dma = pltpu.VMEM, pltpu.SemaphoreType.DMA
    hops = dma((2, 2, 2, n // 2))
    return pl.pallas_call(
        functools.partial(forward_body, n, rows, tokens, width),
        grid=(steps + 2 * more,),
        in_specs=[
            row(D), pl.BlockSpec((tall, D), lambda i: (middle(i), 0)),
            whole(w), whole(taps), whole(head), whole(chan), whole(cot), whole(wp),
        ],
        out_specs=[
            pl.BlockSpec((tall, width), lambda i: (middle(i), 0)),
            row(wide), row(wide), row(LANES), row(width),
            pl.BlockSpec((tall, width), lambda i: (jnp.maximum(i - steps - more, 0), 0)),
            pl.BlockSpec((subs, NS, width), lambda i: (early(i), 0, 0)),
            pl.BlockSpec((8, length), lambda i: (0, 0)),
            anywhere, anywhere,
        ],
        out_shape=[
            jax.ShapeDtypeStruct((length, width), f32),
            jax.ShapeDtypeStruct((length, wide), bf16),
            jax.ShapeDtypeStruct((length, wide), f32),
            jax.ShapeDtypeStruct((length, LANES), f32),
            jax.ShapeDtypeStruct((length, width), f32),
            jax.ShapeDtypeStruct((length, width), f32),
            jax.ShapeDtypeStruct((length // T, NS, width), bf16),
            jax.ShapeDtypeStruct((8, length), f32),
            jax.ShapeDtypeStruct((4 * tokens, D), bf16),
            jax.ShapeDtypeStruct((n * rows, 2 * width), bf16),
        ],
        scratch_shapes=[
            vm((ROWS + 8, wide), f32), vm((NS, width), f32), vm((length, width), f32),
            vm((4 * tokens, D), bf16), vm((n * rows, 2 * width), bf16), vm((4, 8, length), f32),
            dma((4,)), hops, dma((2,)), dma((1,)), dma((2,)), hops, hops, dma((2,)), dma((2,)),
            dma((1,)), dma((1,)), dma((2,)), dma((2,)), dma((2,)), dma((2,)),
        ],
        compiler_params=pltpu.CompilerParams(collective_id=2, has_side_effects=True, vmem_limit_bytes=ROOM),
        name="layer_forward",
    )(xg, xg, w, taps, head, chan, cot, wp)


def gather_body(
    n, rows, tokens,
    x_ref, w_ref, xg_ref, ws_ref, xg, ws,
    keep_sem, ring_keep, ring_send, ring_recv, over_send, over_recv, side_send, side_recv, pass_send, pass_recv,
):
    pos, ring, me, across, beside = neighbours(n)
    enter((*ring, across, beside))
    half = tokens // 2
    started, kept = [], []

    def go(*args):
        copy = remote(*args)
        copy.start()
        started.append(copy)

    def keep(src, dst, sem):
        copy = pltpu.make_async_copy(src, dst, sem)
        copy.start()
        kept.append(copy)

    opposite = lax.rem(me + 2, 4)
    next_door = me + 1 - 2 * lax.rem(me, 2)
    far = lax.rem(next_door + 2, 4)
    cuts = cut_rows(rows)

    def arrived(part, way, step, block):
        first, size = cuts[part]
        at = span(block * rows + first, size)
        remote(
            ws.at[at], ws.at[at], ring_send.at[way, part, step], ring_recv.at[way, part, step], ring[way]
        ).wait_recv()
        keep(ws.at[at], ws_ref.at[at], ring_keep.at[way, part, step])

    def ring_step(step):
        last = step == n // 2 - 1
        for part, (first, size) in enumerate(cuts):
            for way in (0, 1):
                block = ring_index(lax.rem(pos + (step if way else n - step), n), n)
                here = ws.at[span(block * rows + first, size)]
                if step > 0:
                    arrived(part, way, step - 1, block)
                if last and part != way:
                    continue
                src = w_ref.at[pl.ds(first, size)] if step == 0 else here
                go(src, here, ring_send.at[way, part, step], ring_recv.at[way, part, step], ring[way])

    def pass_on(k):
        at = span(opposite * tokens + k * half, half)
        here = xg.at[at]
        remote(here, here, over_send.at[k], over_recv.at[k], across).wait_recv()
        go(here, here, pass_send.at[k], pass_recv.at[k], beside)
        keep(here, xg_ref.at[at], keep_sem.at[k])

    ring_step(0)
    for k in (0, 1):
        go(
            x_ref.at[pl.ds(k * half, half)], xg.at[span(me * tokens + k * half, half)],
            over_send.at[k], over_recv.at[k], across,
        )
    go(x_ref, xg.at[span(me * tokens, tokens)], side_send.at[0], side_recv.at[0], beside)
    mine = ring_index(pos, n)
    keep(x_ref, xg_ref.at[span(me * tokens, tokens)], keep_sem.at[2])
    keep(w_ref, ws_ref.at[span(mine * rows, rows)], keep_sem.at[3])
    for step in range(1, n // 2):
        ring_step(step)
        if step == n // 2 - 2:
            pass_on(0)
            pass_on(1)
    at = span(next_door * tokens, tokens)
    remote(xg.at[at], xg.at[at], side_send.at[0], side_recv.at[0], beside).wait_recv()
    keep(xg.at[at], xg_ref.at[at], keep_sem.at[4])
    for k in (0, 1):
        at = span(far * tokens + k * half, half)
        remote(xg.at[at], xg.at[at], pass_send.at[k], pass_recv.at[k], beside).wait_recv()
        keep(xg.at[at], xg_ref.at[at], keep_sem.at[5 + k])
    for part in (0, 1):
        arrived(part, part, n // 2 - 1, ring_index(lax.rem(pos + n // 2, n), n))
    for copy in kept:
        copy.wait()
    for copy in started:
        copy.wait_send()


def gather_all(n, x, w):
    tokens, rows = x.shape[0], w.shape[0]
    dma = pltpu.SemaphoreType.DMA
    anywhere = pl.BlockSpec(memory_space=pl.ANY)
    inside = pl.BlockSpec(memory_space=pltpu.VMEM)
    shapes = [(a.shape[0] * k, a.shape[1]) for a, k in ((x, 4), (w, n))]
    hops = dma((2, 2, n // 2))
    return pl.pallas_call(
        functools.partial(gather_body, n, rows, tokens),
        in_specs=[inside] * 2,
        out_specs=[anywhere] * 2,
        out_shape=[jax.ShapeDtypeStruct(shape, bf16) for shape in shapes],
        scratch_shapes=[
            *(pltpu.VMEM(shape, bf16) for shape in shapes),
            dma((7,)), hops, hops, hops, dma((2,)), dma((2,)), dma((1,)), dma((1,)), dma((2,)), dma((2,)),
        ],
        compiler_params=pltpu.CompilerParams(
            collective_id=0, has_side_effects=True, vmem_limit_bytes=ROOM
        ),
        name="gather_all",
    )(x, w)


def gradient_body(
    width,
    z_ref, y_ref, dn_ref, red_ref, wo_ref, chan_ref, xg_ref, cot_ref,
    dy_ref, dz_ref, branch_ref, early_ref, gate_ref,
    nl, dz_all,
):
    step = pl.program_id(0)
    steps = LEN // ROWS

    @pl.when(step == 0)
    def _():
        gate_ref[...] = jnp.zeros_like(gate_ref)

    @pl.when(step < steps)
    def _():
        q_row = lax.rsqrt(red_ref[0:4, :] / DI + norm_eps)
        k_row = q_row * q_row * q_row * red_ref[4:8, :] / DI
        turned = jnp.concatenate([q_row, k_row], axis=0).T
        for sub in range(ROWS // T):
            rows = slice(sub * T, (sub + 1) * T)
            at = span(step * ROWS + sub * T, T)
            q, kk = spread(turned[rows, 0:1]), spread(turned[rows, 4:5])
            for p in range(width // LANES):
                cols = slice(p * LANES, (p + 1) * LANES)
                z, y, dn = z_ref[rows, cols], y_ref[rows, cols], dn_ref[rows, cols]
                gain = chan_ref[0:1, cols]
                s = sigmoid(z)
                sz = z * s
                gated = y * sz
                gq = gated * q
                dg = q * gain * dn - gated * kk
                gate_ref[:, cols] += jnp.sum((gq * dn).reshape(T // 8, 8, LANES), axis=0)
                nl[at, cols] = (gq * gain).astype(bf16)
                dz = (dg * y * (s + sz * (1.0 - s))).astype(bf16)
                dz_all[at, cols] = dz
                dz_ref[rows, cols] = dz
                dy_ref[rows, cols] = dg * sz
        branch_ref[...] = mm(nl[span(step * ROWS, ROWS), :], wo_ref[...], NT).astype(bf16)

    @pl.when(step >= steps)
    def _():
        early_ref[:, :width] = mm(xg_ref[...], dz_all[...], TN).astype(bf16)
        early_ref[:, width:] = mm(cot_ref[...], nl[...], TN).astype(bf16)


def early_gradients(z, y, dn, red, wp, chan, xg, cot):
    length, width = z.shape
    steps = length // ROWS
    deep = 2 * LANES
    early = lambda i: jnp.minimum(i, steps - 1)
    late = lambda i: jnp.maximum(i - steps, 0)
    row = lambda m: pl.BlockSpec((ROWS, m), lambda i: (early(i), 0))
    column = pl.BlockSpec((length, deep), lambda i: (0, late(i)))
    whole = lambda a: pl.BlockSpec(a.shape, lambda i: (0,) * a.ndim, pipeline_mode=pl.Buffered(1))
    return pl.pallas_call(
        functools.partial(gradient_body, width),
        grid=(steps + D // deep,),
        in_specs=[
            row(width), row(width), row(width), pl.BlockSpec((8, ROWS), lambda i: (0, early(i))),
            pl.BlockSpec((D, width), lambda i: (0, 1), pipeline_mode=pl.Buffered(1)),
            whole(chan), column, column,
        ],
        out_specs=[
            row(width), row(width), row(D), pl.BlockSpec((deep, 2 * width), lambda i: (late(i), 0)),
            pl.BlockSpec((8, width), lambda i: (0, 0)),
        ],
        out_shape=[
            jax.ShapeDtypeStruct((length, width), f32),
            jax.ShapeDtypeStruct((length, width), bf16),
            jax.ShapeDtypeStruct((length, D), bf16),
            jax.ShapeDtypeStruct((D, 2 * width), bf16),
            jax.ShapeDtypeStruct((8, width), f32),
        ],
        scratch_shapes=[pltpu.VMEM((length, width), bf16), pltpu.VMEM((length, width), bf16)],
        compiler_params=pltpu.CompilerParams(vmem_limit_bytes=ROOM),
        name="early_gradients",
    )(z, y, dn, red, wp, chan, xg, cot)


def backward_body(
    n, own_rows, tokens, width,
    dy_ref, v_ref, xc_ref, dr_ref, st_ref, gate_ref, taps_ref, head_ref, chan_ref, pick_ref, early_ref, branch_ref,
    d_ref, small_ref, oearly_ref, obranch_ref,
    dxh, dstate, yst, bds, dyeb, utb, gin, gout, xdu, turn, acc, hacc,
    own, slots, near, held, over_slot,
    load_sem, ring_send, ring_recv, near_send, near_recv, over_send, over_recv,
):
    pairs = width // LANES
    wide = width + 2 * NS
    step = pl.program_id(0)
    steps = LEN // ROWS
    pos, ring, me, across, beside = neighbours(n)
    opposite = lax.rem(me + 2, 4)
    next_door = me + 1 - 2 * lax.rem(me, 2)
    far = lax.rem(next_door + 2, 4)
    half = tokens // 2
    cuts = cut_rows(own_rows)

    def block_at(way, count):
        return ring_index(lax.rem(pos + (count if way else n - count), n), n)

    def hop(k, way, h):
        first, size = cuts[way]
        if h == 0:
            src = early_ref.at[span(block_at(way, 1) * own_rows + first, size), pl.ds(k * width, width)]
        else:
            src = slots[way][k].at[h - 1]
        return remote(
            src, slots[way][k].at[h], ring_send.at[way, k, h], ring_recv.at[way, k, h], ring[way]
        )

    def near_copy(turned, part):
        start = (next_door if turned else far) * tokens + part * half
        return remote(
            branch_ref.at[span(start, half)], near.at[turned, part],
            near_send.at[turned, part], near_recv.at[turned, part], beside,
        )

    def held_copy(turned, part):
        start = (me if turned else opposite) * tokens + part * half
        return pltpu.make_async_copy(
            branch_ref.at[span(start, half)], held.at[turned, part], load_sem.at[2 * turned + part]
        )

    def over_copy(part):
        return remote(held.at[0, part], over_slot.at[part], over_send.at[part], over_recv.at[part], across)

    def own_copy():
        return pltpu.make_async_copy(early_ref, own, load_sem.at[4])

    def ring_turn(k, h):
        for way in (0, 1):
            first, size = cuts[way]
            hop(k, way, h).wait_recv()
            block = block_at(way, 2 + h) if h < n - 2 else block_at(way, 0)

            tile = strip(size)

            def some(i, _, way=way, first=first, block=block, tile=tile):
                cols = slice(k * width, (k + 1) * width)
                came = slots[way][k][h, span(i * tile, tile), :]
                mine = own[span(block * own_rows + first + i * tile, tile), cols]
                if h < n - 2:
                    slots[way][k][h, span(i * tile, tile), :] = came + mine
                else:
                    oearly_ref[span(first + i * tile, tile), cols] = came.astype(f32) + mine.astype(f32)
                return 0

            lax.fori_loop(0, size // tile, some, 0)
            if h < n - 2:
                hop(k, way, h + 1).start()

    def ring_poll(k):
        for h in range(n - 1):
            pl.when(step == min(h + 1, steps - 1))(functools.partial(ring_turn, k, h))

    def add_near(turned):
        for part in (0, 1):
            held_copy(turned, part).wait()
            near_copy(turned, part).wait_recv()

            def some(i, _, part=part):
                at = span(i * 32, 32)
                if turned:
                    total = held[1, part, at, :].astype(f32) + near[1, part, at, :].astype(f32)
                    obranch_ref[span(part * half + i * 32, 32), :] = total
                else:
                    held[0, part, at, :] = held[0, part, at, :] + near[0, part, at, :]
                return 0

            lax.fori_loop(0, half // 32, some, 0)
            if not turned:
                over_copy(part).start()

    @pl.when(step == 0)
    def _():
        enter((*ring, across, beside))
        for k in (0, 1):
            for way in (0, 1):
                hop(k, way, 0).start()
        for turned in (0, 1):
            for part in (0, 1):
                near_copy(turned, part).start()
                held_copy(turned, part).start()
        own_copy().start()
        dxh[T : T + 8, :] = jnp.zeros((8, wide), f32)
        dstate[...] = jnp.zeros_like(dstate)
        acc[...] = jnp.zeros_like(acc)
        hacc[...] = jnp.zeros_like(hacc)
        turn[...] = jnp.zeros_like(turn)

    @pl.when(step == 1)
    def _():
        own_copy().wait()
        add_near(0)

    pl.when(step == 2)(functools.partial(add_near, 1))
    ring_poll(0)

    low_half = block_iota(1) < P_SIZE
    row_at, col_at = block_iota(0), block_iota(1)
    until = row_at <= col_at
    before = row_at < col_at
    upper = jnp.where(until, 1.0, 0.0).astype(f32)
    strict = jnp.where(before, 1.0, 0.0).astype(f32)
    low_tri = jnp.where(row_at >= col_at, 1.0, 0.0).astype(bf16)

    def add(index, cols, value):
        acc[index, :, cols] += jnp.sum(value.reshape(T // 8, 8, LANES), axis=0)

    def conv_back(rows, block, d_act, xc, s, act):
        cols = slice(block * LANES, (block + 1) * LANES)
        dxh[0:T, cols] = d_act * (s + act * (1.0 - s))
        v = v_ref[rows, cols].astype(f32)
        total = None
        for m in range(CONV):
            moved = dxh[m : m + T, cols]
            if m == 0:
                add(CONV, cols, moved)
            add(CONV - 1 - m, cols, v * moved)
            term = taps_ref[CONV - 1 - m : CONV - m, cols] * moved
            total = term if total is None else total + term
        d_ref[rows, cols] = total.astype(bf16)

    for sub in reversed(range(ROWS // T)):
        rows = slice(sub * T, (sub + 1) * T)
        raw, dt, decay = head_rows(dr_ref, head_ref, rows)
        decay_t = decay.T
        b_cols = slice(width, width + NS)
        c_cols = slice(width + NS, width + 2 * NS)
        b_xc, c_xc = xc_ref[rows, b_cols], xc_ref[rows, c_cols]
        b_s, c_s = sigmoid(b_xc), sigmoid(c_xc)
        b_act, c_act = b_xc * b_s, c_xc * c_s
        b_low, c_low = b_act.astype(bf16), c_act.astype(bf16)
        c_t = c_low.T
        scores_t = jnp.where(until, mm(b_low, c_low, NT), 0.0)
        ds_low = dstate[...].astype(bf16)
        yst[...] = mm(c_low, st_ref[sub])
        bds[...] = mm(b_low, ds_low)
        d_scores = jnp.zeros((T, LANES), f32)
        for p in range(pairs):
            cols = slice(p * LANES, (p + 1) * LANES)
            dy = dy_ref[rows, cols]
            xc = xc_ref[rows, cols]
            xs = sigmoid(xc)
            x = xc * xs
            l1, l2 = spread(decay[:, 2 * p : 2 * p + 1]), spread(decay[:, 2 * p + 1 : 2 * p + 2])
            both = jnp.where(low_half, l1, l2)
            dtb = jnp.where(
                low_half, spread(dt[:, 2 * p : 2 * p + 1]), spread(dt[:, 2 * p + 1 : 2 * p + 2])
            )
            u = x * dtb
            last = both[T - 1 : T, :]
            e1 = jnp.exp(jnp.minimum(decay_t[2 * p : 2 * p + 1, :] - l1, 0.0))
            e2 = jnp.exp(jnp.minimum(decay_t[2 * p + 1 : 2 * p + 2, :] - l2, 0.0))
            dy_low = dy.astype(bf16)
            zero = jnp.zeros_like(dy_low)
            u_low = u.astype(bf16)
            du_in = mm(
                jnp.concatenate([(scores_t * e1).astype(bf16), (scores_t * e2).astype(bf16)], axis=1),
                jnp.concatenate(
                    [jnp.where(low_half, dy_low, zero), jnp.where(low_half, zero, dy_low)], axis=0
                ),
            )
            d_mix = mm(
                jnp.concatenate(
                    [jnp.where(low_half, u_low, zero), jnp.where(low_half, zero, u_low)], axis=0
                ),
                dy_low,
                NT,
            )
            d1, d2 = d_mix[:T] * e1, d_mix[T:] * e2
            d_scores = d_scores + d1 + d2
            reach = mm(
                jnp.concatenate([(d1 * scores_t).astype(bf16), (d2 * scores_t).astype(bf16)], axis=0),
                low_tri,
            )
            turn[2 * p : 2 * p + 1, :] = jnp.sum(jnp.where(before, reach[:T], 0.0), axis=0, keepdims=True)
            turn[2 * p + 1 : 2 * p + 2, :] = jnp.sum(
                jnp.where(before, reach[T:], 0.0), axis=0, keepdims=True
            )
            tail = jnp.exp(last - both)
            dye = dy * jnp.exp(both)
            du_out = tail * bds[:, cols]
            du = du_in + du_out
            gin[:, cols] = (dye * yst[:, cols]).astype(bf16)
            gout[:, cols] = (u * du_out).astype(bf16)
            xdu[:, cols] = (x * du).astype(bf16)
            dyeb[:, cols] = dye.astype(bf16)
            utb[:, cols] = (u * tail).astype(bf16)
            add(CONV + 1, cols, dy * x)
            conv_back(rows, p, dtb * du + chan_ref[1:2, cols] * dy, xc, xs, x)
        d_scores = jnp.where(until, d_scores, 0.0).astype(bf16)
        d_b = mm(d_scores, c_low) + mm(utb[...], ds_low, NT)
        d_c = mm(d_scores, b_low, TN) + mm(dyeb[...], st_ref[sub], NT)
        conv_back(rows, pairs, d_b, b_xc, b_s, b_act)
        conv_back(rows, pairs + 1, d_c, c_xc, c_s, c_act)
        ended = jnp.zeros((1, LANES), f32)
        for p in range(pairs):
            cols = slice(p * LANES, (p + 1) * LANES)
            last = jnp.where(
                low_half[0:1], decay[T - 1 : T, 2 * p : 2 * p + 1], decay[T - 1 : T, 2 * p + 1 : 2 * p + 2]
            )
            fade = jnp.exp(last)
            before_ds = dstate[:, cols]
            through = jnp.sum(before_ds * st_ref[sub, :, cols].astype(f32), axis=0, keepdims=True) * fade
            ended = ended + mm_exact(through, pick_ref[cols, :].astype(f32))
            dstate[:, cols] = fade * before_ds + mm(c_t, dyeb[:, cols])
        gin_heads = mm(gin[...], pick_ref[...])
        gout_heads = mm(gout[...], pick_ref[...])
        reached = (
            turn[...].T
            + mm_exact(upper, gin_heads)
            + mm_exact(strict, gout_heads, TN)
            + ended
        )
        d_raw = (head_ref[1:2, :] * reached + mm(xdu[...], pick_ref[...])) * sigmoid(raw)
        d_ref[rows, wide:] = d_raw.astype(bf16)
        hacc[0] += jnp.sum(d_raw.reshape(T // 8, 8, LANES), axis=0)
        hacc[1] += jnp.sum((dt * reached).reshape(T // 8, 8, LANES), axis=0)
        dxh[T : T + 8, :] = dxh[0:8, :]
        if sub == 1:
            ring_poll(1)

    @pl.when(step == steps - 1)
    def _():
        total = lambda a: jnp.sum(a, axis=0, keepdims=True)
        for k in range(CONV + 1):
            small_ref[k : k + 1, :] = total(acc[k])
        small_ref[CONV + 1 : CONV + 2, :width] = total(gate_ref[...])
        small_ref[CONV + 1 : CONV + 2, width : width + LANES] = total(hacc[0])
        small_ref[CONV + 1 : CONV + 2, width + LANES :] = total(hacc[1])
        small_ref[CONV + 2 :, :] = jnp.zeros((2, wide), f32)
        skip = mm_exact(acc[CONV + 1, :, :width], pick_ref[...].astype(f32))
        small_ref[CONV + 3 : CONV + 4, 512 : 512 + LANES] = total(skip)
        for part in (0, 1):
            over_copy(part).wait_recv()

            def some(i, _, part=part):
                at = span(part * half + i * 32, 32)
                obranch_ref[at, :] = obranch_ref[at, :] + over_slot[part, span(i * 32, 32), :].astype(f32)
                return 0

            lax.fori_loop(0, half // 32, some, 0)
        for part in (0, 1):
            over_copy(part).wait_send()
            for turned in (0, 1):
                near_copy(turned, part).wait_send()
        for h in range(n - 1):
            for k in (0, 1):
                for way in (0, 1):
                    hop(k, way, h).wait_send()


def ssd_backward(n, dy, v, xc, dr, st, gate, taps, head, chan, pick, early, branch):
    length, width = dy.shape
    wide = width + 2 * NS
    steps = length // ROWS
    subs = ROWS // T
    own_rows, tokens = D // n, length // 4
    half = tokens // 2
    row = lambda m: pl.BlockSpec((ROWS, m), lambda i: (steps - 1 - i, 0))
    whole = lambda a: pl.BlockSpec(a.shape, lambda i: (0,) * a.ndim, pipeline_mode=pl.Buffered(1))
    fixed = lambda *shape: pl.BlockSpec(shape, lambda i: (0,) * len(shape))
    anywhere = pl.BlockSpec(memory_space=pl.ANY)
    vm, dma = pltpu.VMEM, pltpu.SemaphoreType.DMA
    return pl.pallas_call(
        functools.partial(backward_body, n, own_rows, tokens, width),
        grid=(steps,),
        in_specs=[
            row(width), row(wide), row(wide), row(LANES),
            pl.BlockSpec((subs, NS, width), lambda i: (steps - 1 - i, 0, 0)),
            whole(gate), whole(taps), whole(head), whole(chan), whole(pick), anywhere, anywhere,
        ],
        out_specs=[
            row(wide + LANES), fixed(8, wide), fixed(own_rows, 2 * width), fixed(tokens, D),
        ],
        out_shape=[
            jax.ShapeDtypeStruct((length, wide + LANES), bf16),
            jax.ShapeDtypeStruct((8, wide), f32),
            jax.ShapeDtypeStruct((own_rows, 2 * width), f32),
            jax.ShapeDtypeStruct((tokens, D), f32),
        ],
        scratch_shapes=[
            vm((T + 8, wide), f32), vm((NS, width), f32), vm((T, width), f32), vm((T, width), f32),
            vm((T, width), bf16), vm((T, width), bf16), vm((T, width), bf16), vm((T, width), bf16),
            vm((T, width), bf16), vm((T, LANES), f32), vm((CONV + 2, 8, wide), f32), vm((2, 8, LANES), f32),
            vm((D, 2 * width), bf16),
            [[vm((n - 1, size, width), bf16) for _ in (0, 1)] for _, size in cut_rows(own_rows)],
            vm((2, 2, half, D), bf16), vm((2, 2, half, D), bf16), vm((2, half, D), bf16),
            dma((5,)), dma((2, 2, n - 1)), dma((2, 2, n - 1)), dma((2, 2)), dma((2, 2)), dma((2,)), dma((2,)),
        ],
        compiler_params=pltpu.CompilerParams(
            collective_id=3, has_side_effects=True, vmem_limit_bytes=ROOM
        ),
        name="layer_backward",
    )(dy, v, xc, dr, st, gate, taps, head, chan, pick, early, branch)


def reduce_body(
    n, rows, tokens, starts,
    xg_ref, d_ref, dz_ref, wp_ref, w_ref, small_ref,
    oxs_ref, oback_ref, bc_ref, osmall_ref,
    xg, d, dz, wz, w, grads, slots, staged, near, over, gains, smalls, tens, bc_slot,
    load_sem, ring_send, ring_recv, near_send, near_recv, over_send, over_recv,
    small_send, small_recv, ten_send, ten_recv, bc_send, bc_recv,
):
    pos, ring, me, across, beside = neighbours(n)
    cuts = cut_rows(rows)
    core = lax.rem(me, 2)
    opposite = lax.rem(me + 2, 4)
    next_door = me + 1 - 2 * core
    far = lax.rem(next_door + 2, 4)
    half = tokens // 2
    wide = d.shape[1]
    width = dz.shape[1]
    loads = []
    for k, (src, dst) in enumerate(
        (
            (d_ref, d), (xg_ref, xg), (dz_ref, dz), (w_ref, w), (small_ref, smalls.at[pos]),
            (wp_ref.at[:, pl.ds(0, width)], wz),
        )
    ):
        loads.append(pltpu.make_async_copy(src, dst, load_sem.at[k]))
        loads[-1].start()
    enter((*ring, across, beside))
    started = []

    def go(*args):
        copy = remote(*args)
        copy.start()
        started.append(copy)

    def block_at(way, count):
        return ring_index(lax.rem(pos + (count if way else n - count), n), n)

    def product(k):
        lo, hi = starts[k]

        def some(i, _):
            at = pl.ds(pl.multiple_of(i * 2 * LANES, 2 * LANES), 2 * LANES)
            grads[at, lo:hi] = mm(xg[:, at], d[:, lo:hi], TN).astype(bf16)
            return 0

        lax.fori_loop(0, D // (2 * LANES), some, 0)
        for way in (0, 1):
            first, size = cuts[way]
            go(
                grads.at[span(block_at(way, 1) * rows + first, size), pl.ds(lo, hi - lo)],
                slots[way][k].at[0], ring_send.at[way, k, 0], ring_recv.at[way, k, 0], ring[way],
            )

    def back(target, part):
        at = span(target * tokens + part * half, half)
        total = mm(dz[at, :], wz[...], NT) + mm(d[at, :], w[...], NT)
        gains[...] += jnp.sum((total * xg[at, :].astype(f32)).reshape(half // 8, 8, D), axis=0)
        return total

    def near_copy(turned, part):
        return remote(
            staged.at[turned, part], near.at[turned, part],
            near_send.at[turned, part], near_recv.at[turned, part], beside,
        )

    def over_copy(part):
        return remote(near.at[0, part], over.at[part], over_send.at[part], over_recv.at[part], across)

    def give(turned, part):
        staged[turned, part] = back(next_door if turned else far, part).astype(bf16)
        near_copy(turned, part).start()

    def take(turned, part):
        total = back(me if turned else opposite, part)
        near_copy(turned, part).wait_recv()
        total = total + near[turned, part].astype(f32)
        if turned:
            oback_ref[span(part * half, half), :] = total
        else:
            near[0, part] = total.astype(bf16)
            over_copy(part).start()

    def ring_turn(k, h):
        lo, hi = starts[k]
        for way in (0, 1):
            first, size = cuts[way]
            slot = slots[way][k].at[h]
            remote(slot, slot, ring_send.at[way, k, h], ring_recv.at[way, k, h], ring[way]).wait_recv()
            block = block_at(way, 2 + h) if h < n - 2 else block_at(way, 0)

            tile = strip(size)

            def some(i, _, way=way, first=first, block=block, tile=tile):
                came = slots[way][k][h, span(i * tile, tile), :]
                mine = grads[span(block * rows + first + i * tile, tile), lo:hi]
                if h < n - 2:
                    slots[way][k][h, span(i * tile, tile), :] = came + mine
                else:
                    oxs_ref[span(first + i * tile, tile), lo:hi] = came.astype(f32) + mine.astype(f32)
                return 0

            lax.fori_loop(0, size // tile, some, 0)
            if h < n - 2:
                go(
                    slot, slots[way][k].at[h + 1],
                    ring_send.at[way, k, h + 1], ring_recv.at[way, k, h + 1], ring[way],
                )

    def small_hop(way, h):
        here = smalls.at[lax.rem(pos + (h if way else n - h), n)]
        go(here, here, small_send.at[way, h], small_recv.at[way, h], ring[way])

    def small_lands(way, h):
        here = smalls.at[lax.rem(pos + (h + 1 if way else n - h - 1), n)]
        remote(here, here, small_send.at[way, h], small_recv.at[way, h], ring[way]).wait_recv()

    gains[...] = jnp.zeros_like(gains)
    loads[0].wait()
    loads[1].wait()
    product(0)
    product(1)
    for k in (2, 3, 5):
        loads[k].wait()
    give(0, 0)
    ring_turn(0, 0)
    give(0, 1)
    ring_turn(1, 0)
    take(0, 0)
    ring_turn(0, 1)
    take(0, 1)
    ring_turn(1, 1)
    give(1, 0)
    give(1, 1)
    ring_turn(0, 2)
    take(1, 0)
    ring_turn(1, 2)
    take(1, 1)
    loads[4].wait()
    gain = jnp.sum(gains[...], axis=0, keepdims=True)
    smalls[pos, 6:7, :] = gain[:, :1024]
    smalls[pos, 7:8, 0:512] = gain[:, 1024:]
    for h in range(3, n - 1):
        s = h - 3
        if s < n // 2:
            for way in (0, 1):
                if s > 0 and (way == 0 or s < n // 2):
                    small_lands(way, s - 1)
                if way == 0 or s < n // 2 - 1:
                    small_hop(way, s)
        for k in (0, 1):
            ring_turn(k, h)
            if h == n - 2 and k == 0:
                bc_slot[0] = oxs_ref[:, starts[0][0] : starts[0][0] + 2 * NS]
                go(bc_slot.at[0], bc_slot.at[1], bc_send.at[0], bc_recv.at[0], beside)
    for s in range(n - 4, n // 2):
        for way in (0, 1):
            if s > 0:
                small_lands(way, s - 1)
            if way == 0 or s < n // 2 - 1:
                small_hop(way, s)
    small_lands(0, n // 2 - 1)

    total = smalls[0]
    for i in range(1, n):
        total = total + smalls[i]
    tens[me] = total
    go(tens.at[me], tens.at[me], ten_send.at[0], ten_recv.at[0], beside)
    remote(bc_slot.at[1], bc_slot.at[1], bc_send.at[0], bc_recv.at[0], beside).wait_recv()
    bc_slot[2] = bc_slot[0] + bc_slot[1]
    go(bc_slot.at[2], bc_slot.at[3], bc_send.at[1], bc_recv.at[1], across)
    here = tens.at[next_door]
    remote(here, here, ten_send.at[0], ten_recv.at[0], beside).wait_recv()
    for k, target in ((0, me), (1, next_door)):
        here = tens.at[target]
        go(here, here, ten_send.at[1 + k], ten_recv.at[1 + k], across)
    for part in (0, 1):
        over_copy(part).wait_recv()

        def some(i, _, part=part):
            at = span(part * half + i * 32, 32)
            oback_ref[at, :] = oback_ref[at, :] + over[part, span(i * 32, 32), :].astype(f32)
            return 0

        lax.fori_loop(0, half // 32, some, 0)
    for k, target in ((0, opposite), (1, far)):
        here = tens.at[target]
        remote(here, here, ten_send.at[1 + k], ten_recv.at[1 + k], across).wait_recv()
    osmall_ref[...] = tens[...]
    remote(bc_slot.at[3], bc_slot.at[3], bc_send.at[1], bc_recv.at[1], across).wait_recv()
    bc_ref[...] = bc_slot[2] + bc_slot[3]
    for part in (0, 1):
        over_copy(part).wait_send()
        for turned in (0, 1):
            near_copy(turned, part).wait_send()
    for copy in started:
        copy.wait_send()


def reduce_all(n, xg, d, dz, wp, w, small):
    rows, tokens = D // n, xg.shape[0] // 4
    width, late = dz.shape[1], d.shape[1]
    starts = ((width, late), (0, width))
    half = tokens // 2
    dma, vm = pltpu.SemaphoreType.DMA, pltpu.VMEM
    anywhere = pl.BlockSpec(memory_space=pl.ANY)
    inside = pl.BlockSpec(memory_space=pltpu.VMEM)
    return pl.pallas_call(
        functools.partial(reduce_body, n, rows, tokens, starts),
        in_specs=[anywhere] * 6,
        out_specs=[inside] * 4,
        out_shape=[
            jax.ShapeDtypeStruct((rows, late), f32),
            jax.ShapeDtypeStruct((tokens, D), f32),
            jax.ShapeDtypeStruct((rows, 2 * NS), f32),
            jax.ShapeDtypeStruct((4, *small.shape), f32),
        ],
        scratch_shapes=[
            vm(xg.shape, bf16), vm(d.shape, bf16), vm(dz.shape, bf16), vm((D, width), bf16), vm(w.shape, bf16),
            vm((D, late), bf16),
            [[vm((n - 1, size, hi - lo), bf16) for lo, hi in starts] for _, size in cut_rows(rows)],
            vm((2, 2, half, D), bf16), vm((2, 2, half, D), bf16), vm((2, half, D), bf16), vm((8, D), f32),
            vm((n, *small.shape), f32), vm((4, *small.shape), f32), vm((4, rows, 2 * NS), f32),
            dma((6,)), dma((2, 2, n - 1)), dma((2, 2, n - 1)), dma((2, 2)), dma((2, 2)), dma((2,)), dma((2,)),
            dma((2, n // 2)), dma((2, n // 2)), dma((3,)), dma((3,)), dma((2,)), dma((2,)),
        ],
        compiler_params=pltpu.CompilerParams(
            collective_id=1, has_side_effects=True, vmem_limit_bytes=ROOM
        ),
        name="reduce_all",
    )(xg, d, dz, wp, w, small)


def adamw_step(weight, first, second, grad, rate, decay):
    first_new = beta_first * first + (1.0 - beta_first) * grad
    second_new = beta_second * second + (1.0 - beta_second) * grad * grad
    hat_first = first_new / (1.0 - beta_first**STEP)
    hat_second = second_new / (1.0 - beta_second**STEP)
    weight_new = weight - rate * (hat_first / (jnp.sqrt(hat_second) + adam_eps) + decay * weight)
    return (weight_new, first_new, second_new)


def local(
    layer_input,
    out_grad,
    small_params,
    small_first,
    small_second,
    w_zx,
    zx_first,
    zx_second,
    w_bc,
    bc_first,
    bc_second,
    w_dt,
    dt_first,
    dt_second,
    w_out,
    out_first,
    out_second,
):
    tensor_index = lax.axis_index("tensor")
    local_in = layer_input.astype(f32)
    gain_in, gate_gain, conv_x, bias_x, conv_bc, bias_bc, dt_bias, a_log, d_skip = unpack(
        small_params
    )
    rows_own = w_zx.shape[0]
    width = w_zx.shape[2]
    heads = w_dt.shape[1]
    chan_start = tensor_index * width
    head_start = tensor_index * heads
    gate_local = lax.dynamic_slice_in_dim(gate_gain, chan_start, width, 0)
    conv_local = lax.dynamic_slice_in_dim(conv_x, chan_start, width, 1)
    bias_local = lax.dynamic_slice_in_dim(bias_x, chan_start, width, 0)
    dtb_local = lax.dynamic_slice_in_dim(dt_bias, head_start, heads, 0)
    a_local = -jnp.exp(lax.dynamic_slice_in_dim(a_log, head_start, heads, 0))
    dskip_local = lax.dynamic_slice_in_dim(d_skip, head_start, heads, 0)
    taps = jnp.concatenate(
        [
            jnp.concatenate([conv_local, conv_bc], axis=1),
            jnp.concatenate([bias_local, bias_bc])[None, :],
            jnp.zeros((8 - CONV - 1, width + 2 * NS), f32),
        ],
        axis=0,
    )
    lanes = lambda v: jnp.pad(v, (0, LANES - heads))
    head = jnp.pad(jnp.stack([lanes(dtb_local), lanes(a_local)]), ((0, 6), (0, 0)))
    chan = jnp.pad(jnp.stack([gate_local, jnp.repeat(dskip_local, P_SIZE)]), ((0, 6), (0, 0)))
    pick = jnp.asarray(
        (jnp.arange(width)[:, None] // P_SIZE == jnp.arange(LANES)[None, :]), bf16
    )

    inv_in = lax.rsqrt(jnp.mean(local_in * local_in, axis=-1, keepdims=True) + norm_eps)
    normed_in = local_in * inv_in * gain_in[None, :]
    low = lambda a: a.astype(bf16)
    w_late = jnp.concatenate(
        [low(w_zx[:, 1]), low(w_bc), low(jnp.pad(w_dt, ((0, 0), (0, LANES - heads))))], axis=1
    )
    w_pair = jnp.concatenate([low(w_zx[:, 0]), low(w_out)], axis=1)
    n = lax.axis_size("dp")
    xg, w_all = gather_all(n, normed_in.astype(bf16), w_late)
    z, v, xc, dr, y, dn, st, red, cot_all, pair_all = ssd_forward(
        n, xg, w_all, taps, head, chan, out_grad, w_pair
    )
    dy, dz, branch, early, gate = early_gradients(z, y, dn, red, pair_all, chan, xg, cot_all)
    d_late, small, owner_early, own_branch = ssd_backward(
        n, dy, v, xc, dr, st, gate, taps, head, chan, pick, early, branch
    )
    owner_late, d_normed_in, owner_bc, tens = reduce_all(n, xg, d_late, dz, pair_all, w_all, small)
    layer_output = (local_in + own_branch).astype(bf16)
    owner_zx = jnp.stack([owner_early[:, :width], owner_late[:, :width]], axis=1)
    owner_out = owner_early[:, width:]
    owner_dt = owner_late[:, width + 2 * NS : width + 2 * NS + heads]

    inner_in = jnp.sum(local_in * gain_in[None, :] * d_normed_in, axis=-1, keepdims=True)
    input_grad = (
        out_grad.astype(f32)
        + inv_in * gain_in[None, :] * d_normed_in
        - local_in * (inv_in * inv_in * inv_in * inner_in / D)
    )
    gain_sum = jnp.sum(tens[:, 6:8], axis=0).reshape(-1)[:D] / gain_in
    bc_sum = jnp.sum(tens[:, : CONV + 1, width:], axis=0)
    small_grad = jnp.concatenate(
        [
            gain_sum,
            tens[:, CONV + 1, :width].reshape(-1),
            jnp.moveaxis(tens[:, :CONV, :width], 0, 1).reshape(-1),
            tens[:, CONV, :width].reshape(-1),
            bc_sum.reshape(-1),
            tens[:, CONV + 1, width : width + heads].reshape(-1),
            tens[:, CONV + 1, width + LANES : width + LANES + heads].reshape(-1) * -jnp.exp(a_log),
            tens[:, 7, 512 : 512 + heads].reshape(-1),
        ]
    )
    small_new, small_first_new, small_second_new = adamw_step(
        small_params, small_first, small_second, small_grad, small_rate, 0.0
    )
    zx_new, zx_first_new, zx_second_new = adamw_step(
        w_zx, zx_first, zx_second, owner_zx, matrix_rate, matrix_decay
    )
    bc_new, bc_first_new, bc_second_new = adamw_step(
        w_bc, bc_first, bc_second, owner_bc, matrix_rate, matrix_decay
    )
    dt_new, dt_first_new, dt_second_new = adamw_step(
        w_dt, dt_first, dt_second, owner_dt, matrix_rate, matrix_decay
    )
    out_new, out_first_new, out_second_new = adamw_step(
        w_out, out_first, out_second, owner_out, matrix_rate, matrix_decay
    )
    return (
        layer_output,
        input_grad,
        small_new,
        small_first_new,
        small_second_new,
        zx_new,
        zx_first_new,
        zx_second_new,
        bc_new,
        bc_first_new,
        bc_second_new,
        dt_new,
        dt_first_new,
        dt_second_new,
        out_new,
        out_first_new,
        out_second_new,
    )


def solution(mesh):
    return jax.shard_map(
        local,
        mesh=mesh,
        in_specs=(
            P(("dp", "tensor"), None),
            P(("dp", "tensor"), None),
            P(),
            P(),
            P(),
            P("dp", None, "tensor"),
            P("dp", None, "tensor"),
            P("dp", None, "tensor"),
            P("dp", None),
            P("dp", None),
            P("dp", None),
            P("dp", "tensor"),
            P("dp", "tensor"),
            P("dp", "tensor"),
            P("dp", "tensor"),
            P("dp", "tensor"),
            P("dp", "tensor"),
        ),
        out_specs=(
            P(("dp", "tensor"), None),
            P(("dp", "tensor"), None),
            P(),
            P(),
            P(),
            P("dp", None, "tensor"),
            P("dp", None, "tensor"),
            P("dp", None, "tensor"),
            P("dp", None),
            P("dp", None),
            P("dp", None),
            P("dp", "tensor"),
            P("dp", "tensor"),
            P("dp", "tensor"),
            P("dp", "tensor"),
            P("dp", "tensor"),
            P("dp", "tensor"),
        ),
        check_vma=False,
    )
```

```python
import functools

import jax
import jax.numpy as jnp
from jax import lax
from jax.experimental import pallas as pl
from jax.experimental.pallas import tpu as pltpu
from jax.sharding import PartitionSpec as P

D = 1536
DI = 3072
H = 48
NS = 128
P_SIZE = 64
CONV = 4
LEN = 2048
STEP = 10

T = 128
ROWS = 256
LANES = 128
ROOM = 60 * 2**20

norm_eps = 1e-05
adam_eps = 1e-08
beta_first = 0.9
beta_second = 0.95
matrix_rate = 0.01
small_rate = 0.1
matrix_decay = 0.1

f32 = jnp.float32
bf16 = jnp.bfloat16
NN = (((1,), (0,)), ((), ()))
NT = (((1,), (1,)), ((), ()))
TN = (((0,), (0,)), ((), ()))
HIGHEST = lax.Precision.HIGHEST


def unpack(flat):
    gain_in = flat[:D]
    cursor = D
    gate_gain = flat[cursor : cursor + DI]
    cursor = cursor + DI
    conv_x = flat[cursor : cursor + CONV * DI].reshape(CONV, DI)
    cursor = cursor + CONV * DI
    bias_x = flat[cursor : cursor + DI]
    cursor = cursor + DI
    conv_bc = flat[cursor : cursor + CONV * 2 * NS].reshape(CONV, 2 * NS)
    cursor = cursor + CONV * 2 * NS
    bias_bc = flat[cursor : cursor + 2 * NS]
    cursor = cursor + 2 * NS
    dt_bias = flat[cursor : cursor + H]
    a_log = flat[cursor + H : cursor + 2 * H]
    d_skip = flat[cursor + 2 * H : cursor + 3 * H]
    return (gain_in, gate_gain, conv_x, bias_x, conv_bc, bias_bc, dt_bias, a_log, d_skip)


def mm(a, b, dims=NN):
    return lax.dot_general(a, b, dims, preferred_element_type=f32)


def mm_exact(a, b, dims=NN):
    return lax.dot_general(a, b, dims, preferred_element_type=f32, precision=HIGHEST)


def sigmoid(v):
    return 0.5 * jnp.tanh(0.5 * v) + 0.5


def softplus(v):
    return jnp.maximum(v, 0.0) + jnp.log1p(jnp.exp(-jnp.abs(v)))


def spread(col):
    return jnp.broadcast_to(col, (T, LANES))


def block_iota(axis):
    return lax.broadcasted_iota(jnp.int32, (T, LANES), axis)


def head_rows(dr_ref, head_ref, rows):
    raw = dr_ref[rows, :] + head_ref[0:1, :]
    dt = softplus(raw)
    low_tri = jnp.where(block_iota(0) >= block_iota(1), 1.0, 0.0).astype(f32)
    decay = mm_exact(low_tri, dt * head_ref[1:2, :])
    return raw, dt, decay


def ring_place(n):
    me = lax.axis_index("dp")
    z, x = lax.div(me, 2), lax.rem(me, 2)
    return z + x * (n - 1 - 2 * z)


def ring_index(pos, n):
    back = lax.div(pos, n // 2)
    return 2 * pos + back * (2 * n - 1 - 4 * pos)


def neighbours(n):
    pos = ring_place(n)
    right = ring_index(lax.rem(pos + 1, n), n)
    left = ring_index(lax.rem(pos + n - 1, n), n)
    me = lax.axis_index("tensor")
    y, core = lax.div(me, 2), lax.rem(me, 2)
    across = 2 * (1 - y) + core
    beside = 2 * y + 1 - core
    return pos, ({"dp": right}, {"dp": left}), me, {"tensor": across}, {"tensor": beside}


def enter(peers):
    barrier = pltpu.get_barrier_semaphore()
    for peer in peers:
        pl.semaphore_signal(barrier, inc=1, device_id=peer, device_id_type=pl.DeviceIdType.MESH)
    pl.semaphore_wait(barrier, len(peers))


def remote(src, dst, send_sem, recv_sem, peer):
    return pltpu.make_async_remote_copy(
        src_ref=src, dst_ref=dst, send_sem=send_sem, recv_sem=recv_sem,
        device_id=peer, device_id_type=pl.DeviceIdType.MESH,
    )


def span(start, size):
    return pl.ds(pl.multiple_of(start, 16), size)


def strip(rows):
    return next(size for size in (48, 32, 16) if rows % size == 0)


def cut_rows(rows):
    top = rows // 32 * 16
    return ((0, top), (top, rows - top))


def forward_body(
    n, rows, tokens, width,
    xg_ref, tall_ref, w_ref, taps_ref, head_ref, chan_ref, cot_ref, wp_ref,
    z_ref, v_ref, xc_ref, dr_ref, y_ref, dn_ref, st_ref, red_ref, cots_ref, wps_ref,
    halo, state, y_all, cots, wps, sums,
    own_keep, ring_keep, over_keep, side_keep, pass_keep, ring_send, ring_recv, over_send, over_recv,
    side_send, side_recv, pass_send, pass_recv, sum_send, sum_recv,
):
    pairs = width // LANES
    wide = width + 2 * NS
    step = pl.program_id(0)
    steps = LEN // ROWS
    tall = 2 * ROWS
    gating, norming = steps, steps + LEN // tall
    last_step = norming + LEN // tall - 1
    pos, ring, me, across, beside = neighbours(n)
    opposite = lax.rem(me + 2, 4)
    next_door = me + 1 - 2 * lax.rem(me, 2)
    far = lax.rem(next_door + 2, 4)
    half = tokens // 2
    hops = n // 2
    cuts = cut_rows(rows)
    mine = ring_index(pos, n)

    def hop(k, part, way, h):
        first, size = cuts[part]
        cols = pl.ds(k * width, width)
        block = ring_index(lax.rem(pos + (h if way else n - h), n), n)
        here = wps.at[span(block * rows + first, size), cols]
        src = wp_ref.at[pl.ds(first, size), cols] if h == 0 else here
        return remote(src, here, ring_send.at[way, part, k, h], ring_recv.at[way, part, k, h], ring[way])

    def hop_lands(k, part, way, h):
        first, size = cuts[part]
        block = ring_index(lax.rem(pos + (h + 1 if way else n - h - 1), n), n)
        return span(block * rows + first, size), pl.ds(k * width, width)

    def hop_arrival(k, part, way, h):
        here = wps.at[hop_lands(k, part, way, h)]
        return remote(here, here, ring_send.at[way, part, k, h], ring_recv.at[way, part, k, h], ring[way])

    def hop_keep(k, part, way, h):
        at = hop_lands(k, part, way, h)
        return pltpu.make_async_copy(wps.at[at], wps_ref.at[at], ring_keep.at[way, part, k, h])

    def hop_ways(h):
        return [(part, way) for part in (0, 1) for way in (0, 1) if h < hops - 1 or part == way]

    def hop_on(k, h):
        for part, way in hop_ways(h - 1) if h > 0 else ():
            hop_arrival(k, part, way, h - 1).wait_recv()
            hop_keep(k, part, way, h - 1).start()
            if h < hops and (part, way) in hop_ways(h):
                hop(k, part, way, h).start()
        if h == 0:
            for part, way in hop_ways(0):
                hop(k, part, way, 0).start()

    def over(k):
        return remote(
            cot_ref.at[pl.ds(k * half, half)], cots.at[span(me * tokens + k * half, half)],
            over_send.at[k], over_recv.at[k], across,
        )

    def landed(full, start, size, send, recv, peer):
        here = full.at[span(start, size)]
        return remote(here, here, send, recv, peer)

    def over_arrival(k):
        start = opposite * tokens + k * half
        return landed(cots, start, half, over_send.at[k], over_recv.at[k], across)

    def passing(k):
        start = opposite * tokens + k * half
        return landed(cots, start, half, pass_send.at[k], pass_recv.at[k], beside)

    def pass_arrival(k):
        return landed(cots, far * tokens + k * half, half, pass_send.at[k], pass_recv.at[k], beside)

    def side():
        return remote(cot_ref, cots.at[span(me * tokens, tokens)], side_send.at[0], side_recv.at[0], beside)

    def side_arrival():
        return landed(cots, next_door * tokens, tokens, side_send.at[0], side_recv.at[0], beside)

    def keep(start, size, sem):
        return pltpu.make_async_copy(cots.at[span(start, size)], cots_ref.at[span(start, size)], sem)

    def own_keeps():
        return (
            pltpu.make_async_copy(cot_ref, cots_ref.at[span(me * tokens, tokens)], own_keep.at[0]),
            pltpu.make_async_copy(wp_ref, wps_ref.at[span(mine * rows, rows)], own_keep.at[1]),
            pltpu.make_async_copy(cot_ref, cots.at[span(me * tokens, tokens)], own_keep.at[2]),
            pltpu.make_async_copy(wp_ref, wps.at[span(mine * rows, rows)], own_keep.at[3]),
        )

    @pl.when(step == 0)
    def _():
        enter((*ring, across, beside))
        hop_on(0, 0)
        over(0).start()
        over(1).start()
        side().start()
        for copy in own_keeps():
            copy.start()
        halo[0:8, :] = jnp.zeros((8, wide), f32)
        state[...] = jnp.zeros_like(state)

    for h in range(1, hops):
        at = (2, 5, gating)[h - 1] if h < 4 else gating
        pl.when(step == at)(functools.partial(hop_on, 0, h))
    for h in range(hops):
        at = (1, 4, 7, gating)[h] if h < 4 else norming
        pl.when(step == at)(functools.partial(hop_on, 1, h))
    pl.when(step == gating)(functools.partial(hop_on, 0, hops))
    pl.when(step == norming)(functools.partial(hop_on, 1, hops))

    @pl.when(step == gating)
    def _():
        for k in (0, 1):
            over_arrival(k).wait_recv()
            passing(k).start()
            keep(opposite * tokens + k * half, half, over_keep.at[k]).start()
        for copy in own_keeps():
            copy.wait()

    @pl.when(step == norming)
    def _():
        side_arrival().wait_recv()
        keep(next_door * tokens, tokens, side_keep.at[0]).start()
        for k in (0, 1):
            pass_arrival(k).wait_recv()
            keep(far * tokens + k * half, half, pass_keep.at[k]).start()

    @pl.when(step < gating)
    def _():
        scan_step(
            width, step, xg_ref, w_ref, taps_ref, head_ref, chan_ref,
            v_ref, xc_ref, dr_ref, y_ref, st_ref, halo, state, y_all,
        )

    def token_sum(row, first, value):
        lanes = pl.ds(pl.multiple_of(first, tall), tall)
        sums[0, row : row + 4, lanes] = mm_exact(jnp.ones((8, LANES), f32), value, NT)[0:4]

    @pl.when((step >= gating) & (step < norming))
    def _():
        first = (step - gating) * tall
        z_ref[...] = mm(tall_ref[...], wps[:, :width])
        squares = jnp.zeros((tall, LANES), f32)
        for p in range(pairs):
            cols = slice(p * LANES, (p + 1) * LANES)
            z = z_ref[:, cols]
            gated = y_all[span(first, tall), cols] * (z * sigmoid(z))
            y_all[span(first, tall), cols] = gated
            squares = squares + gated * gated
        token_sum(0, first, squares)

    @pl.when(step >= norming)
    def _():
        first = (step - norming) * tall
        dn_ref[...] = mm(cots[span(first, tall), :], wps[:, width:])
        inner = jnp.zeros((tall, LANES), f32)
        for p in range(pairs):
            cols = slice(p * LANES, (p + 1) * LANES)
            inner = inner + y_all[span(first, tall), cols] * chan_ref[0:1, cols] * dn_ref[:, cols]
        token_sum(4, first, inner)

    @pl.when(step == last_step)
    def _():
        first = remote(sums.at[0], sums.at[1], sum_send.at[0], sum_recv.at[0], beside)
        first.start()
        first.wait_recv()
        sums[2] = sums[0] + sums[1]
        second = remote(sums.at[2], sums.at[3], sum_send.at[1], sum_recv.at[1], across)
        second.start()
        for h in range(hops):
            for part, way in hop_ways(h):
                for k in (0, 1):
                    hop(k, part, way, h).wait_send()
                    hop_keep(k, part, way, h).wait()
        side().wait_send()
        keep(next_door * tokens, tokens, side_keep.at[0]).wait()
        for k in (0, 1):
            over(k).wait_send()
            passing(k).wait_send()
            keep(opposite * tokens + k * half, half, over_keep.at[k]).wait()
            keep(far * tokens + k * half, half, pass_keep.at[k]).wait()
        first.wait_send()
        second.wait()
        red_ref[...] = sums[2] + sums[3]


def scan_step(
    width, step, xg_ref, w_ref, taps_ref, head_ref, chan_ref,
    v_ref, xc_ref, dr_ref, y_ref, st_ref, halo, state, y_all,
):
    pairs = width // LANES
    wide = width + 2 * NS
    dr_ref[...] = mm(xg_ref[...], w_ref[:, wide:])
    halo[8 : 8 + ROWS, :] = mm(xg_ref[...], w_ref[:, :wide])
    low_half = block_iota(1) < P_SIZE
    causal = block_iota(0) >= block_iota(1)

    def convolved(sub, block):
        cols = slice(block * LANES, (block + 1) * LANES)
        total = taps_ref[CONV : CONV + 1, cols]
        for k in range(CONV):
            first = 8 - (CONV - 1) + k + sub * T
            total = total + taps_ref[k : k + 1, cols] * halo[first : first + T, cols]
        rows = slice(sub * T, (sub + 1) * T)
        xc_ref[rows, cols] = total
        v_ref[rows, cols] = halo[8 + sub * T : 8 + (sub + 1) * T, cols].astype(bf16)
        return total * sigmoid(total)

    for sub in range(ROWS // T):
        rows = slice(sub * T, (sub + 1) * T)
        raw, dt, decay = head_rows(dr_ref, head_ref, rows)
        decay_t = decay.T
        b_low = convolved(sub, pairs).astype(bf16)
        c_low = convolved(sub, pairs + 1).astype(bf16)
        b_t = b_low.T
        scores = jnp.where(causal, mm(c_low, b_low, NT), 0.0)
        st_ref[sub] = state[...].astype(bf16)
        for p in range(pairs):
            cols = slice(p * LANES, (p + 1) * LANES)
            x = convolved(sub, p)
            l1, l2 = spread(decay[:, 2 * p : 2 * p + 1]), spread(decay[:, 2 * p + 1 : 2 * p + 2])
            both = jnp.where(low_half, l1, l2)
            dtb = jnp.where(
                low_half, spread(dt[:, 2 * p : 2 * p + 1]), spread(dt[:, 2 * p + 1 : 2 * p + 2])
            )
            u = x * dtb
            m1 = scores * jnp.exp(jnp.minimum(l1 - decay_t[2 * p : 2 * p + 1, :], 0.0))
            m2 = scores * jnp.exp(jnp.minimum(l2 - decay_t[2 * p + 1 : 2 * p + 2, :], 0.0))
            mixing = jnp.concatenate([m1.astype(bf16), m2.astype(bf16)], axis=1)
            parts = jnp.concatenate(
                [jnp.where(low_half, u, 0.0).astype(bf16), jnp.where(low_half, 0.0, u).astype(bf16)],
                axis=0,
            )
            last = both[T - 1 : T, :]
            entering = st_ref[sub, :, cols]
            y = mm(mixing, parts) + jnp.exp(both) * mm(c_low, entering) + chan_ref[1:2, cols] * x
            tail = (u * jnp.exp(last - both)).astype(bf16)
            state[:, cols] = jnp.exp(last) * state[:, cols] + mm(b_t, tail)
            y_ref[rows, cols] = y
            y_all[span(step * ROWS + sub * T, T), cols] = y
    halo[0:8, :] = halo[ROWS : ROWS + 8, :]


def ssd_forward(n, xg, w, taps, head, chan, cot, wp):
    length = xg.shape[0]
    rows, width = wp.shape[0], wp.shape[1] // 2
    tokens = cot.shape[0]
    wide = width + 2 * NS
    steps = length // ROWS
    tall = 2 * ROWS
    more = length // tall
    subs = ROWS // T
    assert length == LEN
    early = lambda i: jnp.minimum(i, steps - 1)
    middle = lambda i: jnp.clip(i - steps, 0, more - 1)
    row = lambda m: pl.BlockSpec((ROWS, m), lambda i: (early(i), 0))
    whole = lambda a: pl.BlockSpec(a.shape, lambda i: (0,) * a.ndim, pipeline_mode=pl.Buffered(1))
    anywhere = pl.BlockSpec(memory_space=pl.ANY)
    vm, dma = pltpu.VMEM, pltpu.SemaphoreType.DMA
    hops = dma((2, 2, 2, n // 2))
    return pl.pallas_call(
        functools.partial(forward_body, n, rows, tokens, width),
        grid=(steps + 2 * more,),
        in_specs=[
            row(D), pl.BlockSpec((tall, D), lambda i: (middle(i), 0)),
            whole(w), whole(taps), whole(head), whole(chan), whole(cot), whole(wp),
        ],
        out_specs=[
            pl.BlockSpec((tall, width), lambda i: (middle(i), 0)),
            row(wide), row(wide), row(LANES), row(width),
            pl.BlockSpec((tall, width), lambda i: (jnp.maximum(i - steps - more, 0), 0)),
            pl.BlockSpec((subs, NS, width), lambda i: (early(i), 0, 0)),
            pl.BlockSpec((8, length), lambda i: (0, 0)),
            anywhere, anywhere,
        ],
        out_shape=[
            jax.ShapeDtypeStruct((length, width), f32),
            jax.ShapeDtypeStruct((length, wide), bf16),
            jax.ShapeDtypeStruct((length, wide), f32),
            jax.ShapeDtypeStruct((length, LANES), f32),
            jax.ShapeDtypeStruct((length, width), f32),
            jax.ShapeDtypeStruct((length, width), f32),
            jax.ShapeDtypeStruct((length // T, NS, width), bf16),
            jax.ShapeDtypeStruct((8, length), f32),
            jax.ShapeDtypeStruct((4 * tokens, D), bf16),
            jax.ShapeDtypeStruct((n * rows, 2 * width), bf16),
        ],
        scratch_shapes=[
            vm((ROWS + 8, wide), f32), vm((NS, width), f32), vm((length, width), f32),
            vm((4 * tokens, D), bf16), vm((n * rows, 2 * width), bf16), vm((4, 8, length), f32),
            dma((4,)), hops, dma((2,)), dma((1,)), dma((2,)), hops, hops, dma((2,)), dma((2,)),
            dma((1,)), dma((1,)), dma((2,)), dma((2,)), dma((2,)), dma((2,)),
        ],
        compiler_params=pltpu.CompilerParams(collective_id=2, has_side_effects=True, vmem_limit_bytes=ROOM),
        name="layer_forward",
    )(xg, xg, w, taps, head, chan, cot, wp)


def gather_body(
    n, rows, tokens,
    x_ref, w_ref, xg_ref, ws_ref, xg, ws,
    keep_sem, ring_keep, ring_send, ring_recv, over_send, over_recv, side_send, side_recv, pass_send, pass_recv,
):
    pos, ring, me, across, beside = neighbours(n)
    enter((*ring, across, beside))
    half = tokens // 2
    started, kept = [], []

    def go(*args):
        copy = remote(*args)
        copy.start()
        started.append(copy)
        return copy

    def keep(src, dst, sem):
        copy = pltpu.make_async_copy(src, dst, sem)
        copy.start()
        kept.append(copy)

    opposite = lax.rem(me + 2, 4)
    next_door = me + 1 - 2 * lax.rem(me, 2)
    far = lax.rem(next_door + 2, 4)
    cuts = cut_rows(rows)

    def arrived(part, way, step, block):
        first, size = cuts[part]
        at = span(block * rows + first, size)
        remote(
            ws.at[at], ws.at[at], ring_send.at[way, part, step], ring_recv.at[way, part, step], ring[way]
        ).wait_recv()
        keep(ws.at[at], ws_ref.at[at], ring_keep.at[way, part, step])

    def ring_step(step, parts=(0, 1)):
        last = step == n // 2 - 1
        for part in parts:
            first, size = cuts[part]
            for way in (0, 1):
                block = ring_index(lax.rem(pos + (step if way else n - step), n), n)
                here = ws.at[span(block * rows + first, size)]
                if step > 0:
                    arrived(part, way, step - 1, block)
                if last and part != way:
                    continue
                src = w_ref.at[pl.ds(first, size)] if step == 0 else here
                go(src, here, ring_send.at[way, part, step], ring_recv.at[way, part, step], ring[way])

    def pass_on(k):
        at = span(opposite * tokens + k * half, half)
        here = xg.at[at]
        remote(here, here, over_send.at[k], over_recv.at[k], across).wait_recv()
        go(here, here, pass_send.at[k], pass_recv.at[k], beside)
        keep(here, xg_ref.at[at], keep_sem.at[k])

    ring_step(0, (0,))
    leading = list(started)
    for k in (0, 1):
        go(
            x_ref.at[pl.ds(k * half, half)], xg.at[span(me * tokens + k * half, half)],
            over_send.at[k], over_recv.at[k], across,
        )
    go(x_ref, xg.at[span(me * tokens, tokens)], side_send.at[0], side_recv.at[0], beside)
    mine = ring_index(pos, n)
    keep(x_ref, xg_ref.at[span(me * tokens, tokens)], keep_sem.at[2])
    keep(w_ref, ws_ref.at[span(mine * rows, rows)], keep_sem.at[3])
    for copy in leading:
        copy.wait_send()
        started.remove(copy)
    ring_step(0, (1,))
    for step in range(1, n // 2):
        ring_step(step)
        if step == n // 2 - 2:
            pass_on(0)
            pass_on(1)
    at = span(next_door * tokens, tokens)
    remote(xg.at[at], xg.at[at], side_send.at[0], side_recv.at[0], beside).wait_recv()
    keep(xg.at[at], xg_ref.at[at], keep_sem.at[4])
    for k in (0, 1):
        at = span(far * tokens + k * half, half)
        remote(xg.at[at], xg.at[at], pass_send.at[k], pass_recv.at[k], beside).wait_recv()
        keep(xg.at[at], xg_ref.at[at], keep_sem.at[5 + k])
    for part in (0, 1):
        arrived(part, part, n // 2 - 1, ring_index(lax.rem(pos + n // 2, n), n))
    for copy in kept:
        copy.wait()
    for copy in started:
        copy.wait_send()


def gather_all(n, x, w):
    tokens, rows = x.shape[0], w.shape[0]
    dma = pltpu.SemaphoreType.DMA
    anywhere = pl.BlockSpec(memory_space=pl.ANY)
    inside = pl.BlockSpec(memory_space=pltpu.VMEM)
    shapes = [(a.shape[0] * k, a.shape[1]) for a, k in ((x, 4), (w, n))]
    hops = dma((2, 2, n // 2))
    return pl.pallas_call(
        functools.partial(gather_body, n, rows, tokens),
        in_specs=[inside] * 2,
        out_specs=[anywhere] * 2,
        out_shape=[jax.ShapeDtypeStruct(shape, bf16) for shape in shapes],
        scratch_shapes=[
            *(pltpu.VMEM(shape, bf16) for shape in shapes),
            dma((7,)), hops, hops, hops, dma((2,)), dma((2,)), dma((1,)), dma((1,)), dma((2,)), dma((2,)),
        ],
        compiler_params=pltpu.CompilerParams(
            collective_id=0, has_side_effects=True, vmem_limit_bytes=ROOM
        ),
        name="gather_all",
    )(x, w)


def gradient_body(
    width,
    z_ref, y_ref, dn_ref, red_ref, wo_ref, chan_ref, xg_ref, cot_ref,
    dy_ref, dz_ref, branch_ref, early_ref, gate_ref,
    nl, dz_all, fresh, hold,
):
    step = pl.program_id(0)
    steps = LEN // ROWS
    slab = D // (width // LANES)

    def multiply(p):
        at = slice(p * slab, (p + 1) * slab)
        branch_ref[:, at] = mm(hold[...], wo_ref[at, :], NT).astype(bf16)

    @pl.when(step == 0)
    def _():
        gate_ref[...] = jnp.zeros_like(gate_ref)
        hold[...] = jnp.zeros_like(hold)

    @pl.when(step < steps)
    def _():
        q_row = lax.rsqrt(red_ref[0:4, :] / DI + norm_eps)
        k_row = q_row * q_row * q_row * red_ref[4:8, :] / DI
        turned = jnp.concatenate([q_row, k_row], axis=0).T
        for p in range(width // LANES):
            cols = slice(p * LANES, (p + 1) * LANES)
            multiply(p)
            for sub in range(ROWS // T):
                rows = slice(sub * T, (sub + 1) * T)
                q, kk = spread(turned[rows, 0:1]), spread(turned[rows, 4:5])
                z, y, dn = z_ref[rows, cols], y_ref[rows, cols], dn_ref[rows, cols]
                gain = chan_ref[0:1, cols]
                s = sigmoid(z)
                sz = z * s
                gated = y * sz
                gq = gated * q
                dg = q * gain * dn - gated * kk
                gate_ref[:, cols] += jnp.sum((gq * dn).reshape(T // 8, 8, LANES), axis=0)
                fresh[rows, cols] = (gq * gain).astype(bf16)
                dz_ref[rows, cols] = (dg * y * (s + sz * (1.0 - s))).astype(bf16)
                dy_ref[rows, cols] = dg * sz
        at = span(step * ROWS, ROWS)
        hold[...] = fresh[...]
        nl[at, :] = fresh[...]
        dz_all[at, :] = dz_ref[...]

    @pl.when(step == steps)
    def _():
        for p in range(width // LANES):
            multiply(p)

    @pl.when(step >= steps)
    def _():
        early_ref[:, :width] = mm(xg_ref[...], dz_all[...], TN).astype(bf16)
        early_ref[:, width:] = mm(cot_ref[...], nl[...], TN).astype(bf16)


def early_gradients(z, y, dn, red, wp, chan, xg, cot):
    length, width = z.shape
    steps = length // ROWS
    deep = 2 * LANES
    early = lambda i: jnp.minimum(i, steps - 1)
    late = lambda i: jnp.maximum(i - steps, 0)
    row = lambda m: pl.BlockSpec((ROWS, m), lambda i: (early(i), 0))
    column = pl.BlockSpec((length, deep), lambda i: (0, late(i)))
    whole = lambda a: pl.BlockSpec(a.shape, lambda i: (0,) * a.ndim, pipeline_mode=pl.Buffered(1))
    return pl.pallas_call(
        functools.partial(gradient_body, width),
        grid=(steps + D // deep,),
        in_specs=[
            row(width), row(width), row(width), pl.BlockSpec((8, ROWS), lambda i: (0, early(i))),
            pl.BlockSpec((D, width), lambda i: (0, 1), pipeline_mode=pl.Buffered(1)),
            whole(chan), column, column,
        ],
        out_specs=[
            row(width), row(width), pl.BlockSpec((ROWS, D), lambda i: (jnp.clip(i - 1, 0, steps - 1), 0)),
            pl.BlockSpec((deep, 2 * width), lambda i: (late(i), 0)),
            pl.BlockSpec((8, width), lambda i: (0, 0)),
        ],
        out_shape=[
            jax.ShapeDtypeStruct((length, width), f32),
            jax.ShapeDtypeStruct((length, width), bf16),
            jax.ShapeDtypeStruct((length, D), bf16),
            jax.ShapeDtypeStruct((D, 2 * width), bf16),
            jax.ShapeDtypeStruct((8, width), f32),
        ],
        scratch_shapes=[pltpu.VMEM((rows, width), bf16) for rows in (length, length, ROWS, ROWS)],
        compiler_params=pltpu.CompilerParams(vmem_limit_bytes=ROOM),
        name="early_gradients",
    )(z, y, dn, red, wp, chan, xg, cot)


def backward_body(
    n, own_rows, tokens, width,
    dy_ref, v_ref, xc_ref, dr_ref, st_ref, gate_ref, taps_ref, head_ref, chan_ref, pick_ref, early_ref, branch_ref,
    d_ref, small_ref, oearly_ref, obranch_ref,
    dxh, dstate, yst, bds, dyeb, utb, gin, gout, xdu, turn, acc, hacc,
    own, slots, near, held, over_slot,
    load_sem, ring_send, ring_recv, near_send, near_recv, over_send, over_recv,
):
    pairs = width // LANES
    wide = width + 2 * NS
    step = pl.program_id(0)
    steps = LEN // ROWS
    pos, ring, me, across, beside = neighbours(n)
    opposite = lax.rem(me + 2, 4)
    next_door = me + 1 - 2 * lax.rem(me, 2)
    far = lax.rem(next_door + 2, 4)
    half = tokens // 2
    cuts = cut_rows(own_rows)

    def block_at(way, count):
        return ring_index(lax.rem(pos + (count if way else n - count), n), n)

    def hop(k, way, h):
        first, size = cuts[way]
        if h == 0:
            src = early_ref.at[span(block_at(way, 1) * own_rows + first, size), pl.ds(k * width, width)]
        else:
            src = slots[way][k].at[h - 1]
        return remote(
            src, slots[way][k].at[h], ring_send.at[way, k, h], ring_recv.at[way, k, h], ring[way]
        )

    def near_copy(turned, part):
        start = (next_door if turned else far) * tokens + part * half
        return remote(
            branch_ref.at[span(start, half)], near.at[turned, part],
            near_send.at[turned, part], near_recv.at[turned, part], beside,
        )

    def held_copy(turned, part):
        start = (me if turned else opposite) * tokens + part * half
        return pltpu.make_async_copy(
            branch_ref.at[span(start, half)], held.at[turned, part], load_sem.at[2 * turned + part]
        )

    def over_copy(part):
        return remote(held.at[0, part], over_slot.at[part], over_send.at[part], over_recv.at[part], across)

    def own_copy():
        return pltpu.make_async_copy(early_ref, own, load_sem.at[4])

    def ring_turn(k, h):
        for way in (0, 1):
            first, size = cuts[way]
            hop(k, way, h).wait_recv()
            block = block_at(way, 2 + h) if h < n - 2 else block_at(way, 0)

            tile = strip(size)

            def some(i, _, way=way, first=first, block=block, tile=tile):
                cols = slice(k * width, (k + 1) * width)
                came = slots[way][k][h, span(i * tile, tile), :]
                mine = own[span(block * own_rows + first + i * tile, tile), cols]
                if h < n - 2:
                    slots[way][k][h, span(i * tile, tile), :] = came + mine
                else:
                    oearly_ref[span(first + i * tile, tile), cols] = came.astype(f32) + mine.astype(f32)
                return 0

            lax.fori_loop(0, size // tile, some, 0)
            if h < n - 2:
                hop(k, way, h + 1).start()

    def ring_poll(k):
        for h in range(n - 1):
            pl.when(step == min(h + 1, steps - 1))(functools.partial(ring_turn, k, h))

    def add_near(turned):
        for part in (0, 1):
            held_copy(turned, part).wait()
            near_copy(turned, part).wait_recv()

            def some(i, _, part=part):
                at = span(i * 32, 32)
                if turned:
                    total = held[1, part, at, :].astype(f32) + near[1, part, at, :].astype(f32)
                    obranch_ref[span(part * half + i * 32, 32), :] = total
                else:
                    held[0, part, at, :] = held[0, part, at, :] + near[0, part, at, :]
                return 0

            lax.fori_loop(0, half // 32, some, 0)
            if not turned:
                over_copy(part).start()

    @pl.when(step == 0)
    def _():
        enter((*ring, across, beside))
        for way in (0, 1):
            hop(0, way, 0).start()
        for turned in (0, 1):
            for part in (0, 1):
                near_copy(turned, part).start()
                held_copy(turned, part).start()
        own_copy().start()
        dxh[T : T + 8, :] = jnp.zeros((8, wide), f32)
        dstate[...] = jnp.zeros_like(dstate)
        acc[...] = jnp.zeros_like(acc)
        hacc[...] = jnp.zeros_like(hacc)
        turn[...] = jnp.zeros_like(turn)

    @pl.when(step == 1)
    def _():
        own_copy().wait()
        add_near(0)

    pl.when(step == 2)(functools.partial(add_near, 1))
    ring_poll(0)

    low_half = block_iota(1) < P_SIZE
    row_at, col_at = block_iota(0), block_iota(1)
    until = row_at <= col_at
    before = row_at < col_at
    upper = jnp.where(until, 1.0, 0.0).astype(f32)
    strict = jnp.where(before, 1.0, 0.0).astype(f32)
    low_tri = jnp.where(row_at >= col_at, 1.0, 0.0).astype(bf16)

    def add(index, cols, value):
        acc[index, :, cols] += jnp.sum(value.reshape(T // 8, 8, LANES), axis=0)

    def conv_back(rows, block, d_act, xc, s, act):
        cols = slice(block * LANES, (block + 1) * LANES)
        dxh[0:T, cols] = d_act * (s + act * (1.0 - s))
        v = v_ref[rows, cols].astype(f32)
        total = None
        for m in range(CONV):
            moved = dxh[m : m + T, cols]
            if m == 0:
                add(CONV, cols, moved)
            add(CONV - 1 - m, cols, v * moved)
            term = taps_ref[CONV - 1 - m : CONV - m, cols] * moved
            total = term if total is None else total + term
        d_ref[rows, cols] = total.astype(bf16)

    for sub in reversed(range(ROWS // T)):
        rows = slice(sub * T, (sub + 1) * T)
        raw, dt, decay = head_rows(dr_ref, head_ref, rows)
        decay_t = decay.T
        b_cols = slice(width, width + NS)
        c_cols = slice(width + NS, width + 2 * NS)
        b_xc, c_xc = xc_ref[rows, b_cols], xc_ref[rows, c_cols]
        b_s, c_s = sigmoid(b_xc), sigmoid(c_xc)
        b_act, c_act = b_xc * b_s, c_xc * c_s
        b_low, c_low = b_act.astype(bf16), c_act.astype(bf16)
        c_t = c_low.T
        scores_t = jnp.where(until, mm(b_low, c_low, NT), 0.0)
        ds_low = dstate[...].astype(bf16)
        yst[...] = mm(c_low, st_ref[sub])
        bds[...] = mm(b_low, ds_low)
        d_scores = jnp.zeros((T, LANES), f32)
        for p in range(pairs):
            cols = slice(p * LANES, (p + 1) * LANES)
            dy = dy_ref[rows, cols]
            xc = xc_ref[rows, cols]
            xs = sigmoid(xc)
            x = xc * xs
            l1, l2 = spread(decay[:, 2 * p : 2 * p + 1]), spread(decay[:, 2 * p + 1 : 2 * p + 2])
            both = jnp.where(low_half, l1, l2)
            dtb = jnp.where(
                low_half, spread(dt[:, 2 * p : 2 * p + 1]), spread(dt[:, 2 * p + 1 : 2 * p + 2])
            )
            u = x * dtb
            last = both[T - 1 : T, :]
            e1 = jnp.exp(jnp.minimum(decay_t[2 * p : 2 * p + 1, :] - l1, 0.0))
            e2 = jnp.exp(jnp.minimum(decay_t[2 * p + 1 : 2 * p + 2, :] - l2, 0.0))
            dy_low = dy.astype(bf16)
            zero = jnp.zeros_like(dy_low)
            u_low = u.astype(bf16)
            du_in = mm(
                jnp.concatenate([(scores_t * e1).astype(bf16), (scores_t * e2).astype(bf16)], axis=1),
                jnp.concatenate(
                    [jnp.where(low_half, dy_low, zero), jnp.where(low_half, zero, dy_low)], axis=0
                ),
            )
            d_mix = mm(
                jnp.concatenate(
                    [jnp.where(low_half, u_low, zero), jnp.where(low_half, zero, u_low)], axis=0
                ),
                dy_low,
                NT,
            )
            d1, d2 = d_mix[:T] * e1, d_mix[T:] * e2
            d_scores = d_scores + d1 + d2
            reach = mm(
                jnp.concatenate([(d1 * scores_t).astype(bf16), (d2 * scores_t).astype(bf16)], axis=0),
                low_tri,
            )
            turn[2 * p : 2 * p + 1, :] = jnp.sum(jnp.where(before, reach[:T], 0.0), axis=0, keepdims=True)
            turn[2 * p + 1 : 2 * p + 2, :] = jnp.sum(
                jnp.where(before, reach[T:], 0.0), axis=0, keepdims=True
            )
            tail = jnp.exp(last - both)
            dye = dy * jnp.exp(both)
            du_out = tail * bds[:, cols]
            du = du_in + du_out
            gin[:, cols] = (dye * yst[:, cols]).astype(bf16)
            gout[:, cols] = (u * du_out).astype(bf16)
            xdu[:, cols] = (x * du).astype(bf16)
            dyeb[:, cols] = dye.astype(bf16)
            utb[:, cols] = (u * tail).astype(bf16)
            add(CONV + 1, cols, dy * x)
            conv_back(rows, p, dtb * du + chan_ref[1:2, cols] * dy, xc, xs, x)
        d_scores = jnp.where(until, d_scores, 0.0).astype(bf16)
        d_b = mm(d_scores, c_low) + mm(utb[...], ds_low, NT)
        d_c = mm(d_scores, b_low, TN) + mm(dyeb[...], st_ref[sub], NT)
        conv_back(rows, pairs, d_b, b_xc, b_s, b_act)
        conv_back(rows, pairs + 1, d_c, c_xc, c_s, c_act)
        ended = jnp.zeros((1, LANES), f32)
        for p in range(pairs):
            cols = slice(p * LANES, (p + 1) * LANES)
            last = jnp.where(
                low_half[0:1], decay[T - 1 : T, 2 * p : 2 * p + 1], decay[T - 1 : T, 2 * p + 1 : 2 * p + 2]
            )
            fade = jnp.exp(last)
            before_ds = dstate[:, cols]
            through = jnp.sum(before_ds * st_ref[sub, :, cols].astype(f32), axis=0, keepdims=True) * fade
            ended = ended + mm_exact(through, pick_ref[cols, :].astype(f32))
            dstate[:, cols] = fade * before_ds + mm(c_t, dyeb[:, cols])
        gin_heads = mm(gin[...], pick_ref[...])
        gout_heads = mm(gout[...], pick_ref[...])
        reached = (
            turn[...].T
            + mm_exact(upper, gin_heads)
            + mm_exact(strict, gout_heads, TN)
            + ended
        )
        d_raw = (head_ref[1:2, :] * reached + mm(xdu[...], pick_ref[...])) * sigmoid(raw)
        d_ref[rows, wide:] = d_raw.astype(bf16)
        hacc[0] += jnp.sum(d_raw.reshape(T // 8, 8, LANES), axis=0)
        hacc[1] += jnp.sum((dt * reached).reshape(T // 8, 8, LANES), axis=0)
        dxh[T : T + 8, :] = dxh[0:8, :]
        if sub == 1:
            @pl.when(step == 0)
            def _():
                for way in (0, 1):
                    hop(1, way, 0).start()

            ring_poll(1)

    @pl.when(step == steps - 1)
    def _():
        total = lambda a: jnp.sum(a, axis=0, keepdims=True)
        for k in range(CONV + 1):
            small_ref[k : k + 1, :] = total(acc[k])
        small_ref[CONV + 1 : CONV + 2, :width] = total(gate_ref[...])
        small_ref[CONV + 1 : CONV + 2, width : width + LANES] = total(hacc[0])
        small_ref[CONV + 1 : CONV + 2, width + LANES :] = total(hacc[1])
        small_ref[CONV + 2 :, :] = jnp.zeros((2, wide), f32)
        skip = mm_exact(acc[CONV + 1, :, :width], pick_ref[...].astype(f32))
        small_ref[CONV + 3 : CONV + 4, 512 : 512 + LANES] = total(skip)
        for part in (0, 1):
            over_copy(part).wait_recv()

            def some(i, _, part=part):
                at = span(part * half + i * 32, 32)
                obranch_ref[at, :] = obranch_ref[at, :] + over_slot[part, span(i * 32, 32), :].astype(f32)
                return 0

            lax.fori_loop(0, half // 32, some, 0)
        for part in (0, 1):
            over_copy(part).wait_send()
            for turned in (0, 1):
                near_copy(turned, part).wait_send()
        for h in range(n - 1):
            for k in (0, 1):
                for way in (0, 1):
                    hop(k, way, h).wait_send()


def ssd_backward(n, dy, v, xc, dr, st, gate, taps, head, chan, pick, early, branch):
    length, width = dy.shape
    wide = width + 2 * NS
    steps = length // ROWS
    subs = ROWS // T
    own_rows, tokens = D // n, length // 4
    half = tokens // 2
    row = lambda m: pl.BlockSpec((ROWS, m), lambda i: (steps - 1 - i, 0))
    whole = lambda a: pl.BlockSpec(a.shape, lambda i: (0,) * a.ndim, pipeline_mode=pl.Buffered(1))
    fixed = lambda *shape: pl.BlockSpec(shape, lambda i: (0,) * len(shape))
    anywhere = pl.BlockSpec(memory_space=pl.ANY)
    vm, dma = pltpu.VMEM, pltpu.SemaphoreType.DMA
    return pl.pallas_call(
        functools.partial(backward_body, n, own_rows, tokens, width),
        grid=(steps,),
        in_specs=[
            row(width), row(wide), row(wide), row(LANES),
            pl.BlockSpec((subs, NS, width), lambda i: (steps - 1 - i, 0, 0)),
            whole(gate), whole(taps), whole(head), whole(chan), whole(pick), anywhere, anywhere,
        ],
        out_specs=[
            row(wide + LANES), fixed(8, wide), fixed(own_rows, 2 * width), fixed(tokens, D),
        ],
        out_shape=[
            jax.ShapeDtypeStruct((length, wide + LANES), bf16),
            jax.ShapeDtypeStruct((8, wide), f32),
            jax.ShapeDtypeStruct((own_rows, 2 * width), f32),
            jax.ShapeDtypeStruct((tokens, D), f32),
        ],
        scratch_shapes=[
            vm((T + 8, wide), f32), vm((NS, width), f32), vm((T, width), f32), vm((T, width), f32),
            vm((T, width), bf16), vm((T, width), bf16), vm((T, width), bf16), vm((T, width), bf16),
            vm((T, width), bf16), vm((T, LANES), f32), vm((CONV + 2, 8, wide), f32), vm((2, 8, LANES), f32),
            vm((D, 2 * width), bf16),
            [[vm((n - 1, size, width), bf16) for _ in (0, 1)] for _, size in cut_rows(own_rows)],
            vm((2, 2, half, D), bf16), vm((2, 2, half, D), bf16), vm((2, half, D), bf16),
            dma((5,)), dma((2, 2, n - 1)), dma((2, 2, n - 1)), dma((2, 2)), dma((2, 2)), dma((2,)), dma((2,)),
        ],
        compiler_params=pltpu.CompilerParams(
            collective_id=3, has_side_effects=True, vmem_limit_bytes=ROOM
        ),
        name="layer_backward",
    )(dy, v, xc, dr, st, gate, taps, head, chan, pick, early, branch)


def reduce_body(
    n, rows, tokens, starts,
    xg_ref, d_ref, dz_ref, wp_ref, w_ref, small_ref,
    oxs_ref, oback_ref, bc_ref, osmall_ref,
    xg, d, dz, wz, w, work, grads, slots, staged, near, over, gains, smalls, tens, bc_slot,
    load_sem, ring_send, ring_recv, near_send, near_recv, over_send, over_recv,
    small_send, small_recv, ten_send, ten_recv, bc_send, bc_recv,
):
    pos, ring, me, across, beside = neighbours(n)
    cuts = cut_rows(rows)
    core = lax.rem(me, 2)
    opposite = lax.rem(me + 2, 4)
    next_door = me + 1 - 2 * core
    far = lax.rem(next_door + 2, 4)
    half = tokens // 2
    wide = d.shape[1]
    width = dz.shape[1]
    loads = []
    for k, (src, dst) in enumerate(
        (
            (d_ref, d), (xg_ref, xg), (dz_ref, dz), (w_ref, w), (small_ref, smalls.at[pos]),
            (wp_ref.at[:, pl.ds(0, width)], wz),
        )
    ):
        loads.append(pltpu.make_async_copy(src, dst, load_sem.at[k]))
        loads[-1].start()
    enter((*ring, across, beside))
    started = []

    def go(*args):
        copy = remote(*args)
        copy.start()
        started.append(copy)

    def block_at(way, count):
        return ring_index(lax.rem(pos + (count if way else n - count), n), n)

    def hop(k, way, h):
        lo, hi = starts[k]
        first, size = cuts[way]
        if h == 0:
            src = grads.at[span(block_at(way, 1) * rows + first, size), pl.ds(lo, hi - lo)]
        else:
            src = slots[way][k].at[h - 1]
        return remote(
            src, slots[way][k].at[h], ring_send.at[way, k, h], ring_recv.at[way, k, h], ring[way]
        )

    def product(k):
        lo, hi = starts[k]

        def some(i, _):
            at = pl.ds(pl.multiple_of(i * 2 * LANES, 2 * LANES), 2 * LANES)
            grads[at, lo:hi] = mm(xg[:, at], d[:, lo:hi], TN).astype(bf16)
            return 0

        lax.fori_loop(0, D // (2 * LANES), some, 0)
        for way in (0, 1):
            hop(k, way, 0).start()

    def near_copy(turned, part):
        return remote(
            staged.at[turned, part], near.at[turned, part],
            near_send.at[turned, part], near_recv.at[turned, part], beside,
        )

    def over_copy(part):
        return remote(near.at[0, part], over.at[part], over_send.at[part], over_recv.at[part], across)

    def ring_turn(k, h):
        lo, hi = starts[k]
        for way in (0, 1):
            first, size = cuts[way]
            slot = slots[way][k].at[h]
            remote(slot, slot, ring_send.at[way, k, h], ring_recv.at[way, k, h], ring[way]).wait_recv()
            block = block_at(way, 2 + h) if h < n - 2 else block_at(way, 0)

            tile = strip(size)

            def some(i, _, way=way, first=first, block=block, tile=tile):
                came = slots[way][k][h, span(i * tile, tile), :]
                mine = grads[span(block * rows + first + i * tile, tile), lo:hi]
                if h < n - 2:
                    slots[way][k][h, span(i * tile, tile), :] = came + mine
                else:
                    oxs_ref[span(first + i * tile, tile), lo:hi] = came.astype(f32) + mine.astype(f32)
                return 0

            lax.fori_loop(0, size // tile, some, 0)
            if h < n - 2:
                hop(k, way, h + 1).start()

    def small_hop(way, h):
        here = smalls.at[lax.rem(pos + (h if way else n - h), n)]
        go(here, here, small_send.at[way, h], small_recv.at[way, h], ring[way])

    def small_lands(way, h):
        here = smalls.at[lax.rem(pos + (h + 1 if way else n - h - 1), n)]
        remote(here, here, small_send.at[way, h], small_recv.at[way, h], ring[way]).wait_recv()

    gains[...] = jnp.zeros_like(gains)
    loads[0].wait()
    loads[1].wait()
    product(0)
    for k in (2, 3, 5):
        loads[k].wait()
    turns = {1: [(0, 0)], 2: [(0, 1)], 3: [(1, 0)], 4: [(0, 2), (1, 1)], 5: [(0, 3), (2, 0)], 6: [(1, 2)], 7: [(0, 4), (2, 1)]}
    taken = [sum(k == group for some in turns.values() for k, _ in some) for group in range(3)]

    def block(i, _):
        pl.when(i == 2)(functools.partial(product, 1))
        pl.when(i == 4)(functools.partial(product, 2))
        which, part = lax.div(i, 2), lax.rem(i, 2)
        own = lax.rem(which, 2)
        turned = lax.div(which, 2)
        target = lax.rem(next_door + own * (me - next_door) + 2 * (1 - turned), 4)
        at = span(target * tokens + part * half, half)
        total = mm(dz[at, :], wz[...], NT) + mm(d[at, :], w[...], NT)
        gains[...] += jnp.sum((total * xg[at, :].astype(f32)).reshape(half // 8, 8, D), axis=0)
        work[...] = total

        @pl.when(own == 0)
        def _():
            staged[turned, part] = work[...].astype(bf16)
            near_copy(turned, part).start()

        @pl.when(own == 1)
        def _():
            near_copy(turned, part).wait_recv()

        @pl.when(which == 1)
        def _():
            near[0, part] = (work[...] + near[0, part].astype(f32)).astype(bf16)
            over_copy(part).start()

        @pl.when(which == 3)
        def _():
            oback_ref[span(part * half, half), :] = work[...] + near[1, part].astype(f32)

        for at_block, some in turns.items():

            @pl.when(i == at_block)
            def _(some=some):
                for k, h in some:
                    ring_turn(k, h)

        return 0

    lax.fori_loop(0, 8, block, 0)
    loads[4].wait()
    gain = jnp.sum(gains[...], axis=0, keepdims=True)
    smalls[pos, 6:7, :] = gain[:, :1024]
    smalls[pos, 7:8, 0:512] = gain[:, 1024:]

    rest = [(k, h) for h in range(n - 1) for k in (1, 2, 0) if h >= taken[k]]
    rest.sort(key=lambda turn: turn[1] - taken[turn[0]])

    def small_step(s):
        for way in (0, 1):
            if s > 0 and (way == 0 or s < n // 2):
                small_lands(way, s - 1)
            if s < n // 2 - way:
                small_hop(way, s)

    small_step(0)
    steps_done = 1
    for at, (k, h) in enumerate(rest):
        ring_turn(k, h)
        if (k, h) == (0, n - 2):
            bc_slot[0] = oxs_ref[:, starts[0][0] : starts[0][0] + 2 * NS]
            go(bc_slot.at[0], bc_slot.at[1], bc_send.at[0], bc_recv.at[0], beside)
        if at % 2 == 1 and steps_done < n // 2:
            small_step(steps_done)
            steps_done += 1
    for s in range(steps_done, n // 2):
        small_step(s)
    small_lands(0, n // 2 - 1)

    total = smalls[0]
    for i in range(1, n):
        total = total + smalls[i]
    tens[me] = total
    go(tens.at[me], tens.at[me], ten_send.at[0], ten_recv.at[0], beside)
    remote(bc_slot.at[1], bc_slot.at[1], bc_send.at[0], bc_recv.at[0], beside).wait_recv()
    bc_slot[2] = bc_slot[0] + bc_slot[1]
    go(bc_slot.at[2], bc_slot.at[3], bc_send.at[1], bc_recv.at[1], across)
    here = tens.at[next_door]
    remote(here, here, ten_send.at[0], ten_recv.at[0], beside).wait_recv()
    for k, target in ((0, me), (1, next_door)):
        here = tens.at[target]
        go(here, here, ten_send.at[1 + k], ten_recv.at[1 + k], across)
    for part in (0, 1):
        over_copy(part).wait_recv()

        def some(i, _, part=part):
            at = span(part * half + i * 32, 32)
            oback_ref[at, :] = oback_ref[at, :] + over[part, span(i * 32, 32), :].astype(f32)
            return 0

        lax.fori_loop(0, half // 32, some, 0)
    for k, target in ((0, opposite), (1, far)):
        here = tens.at[target]
        remote(here, here, ten_send.at[1 + k], ten_recv.at[1 + k], across).wait_recv()
    osmall_ref[...] = tens[...]
    remote(bc_slot.at[3], bc_slot.at[3], bc_send.at[1], bc_recv.at[1], across).wait_recv()
    bc_ref[...] = bc_slot[2] + bc_slot[3]
    for part in (0, 1):
        over_copy(part).wait_send()
        for turned in (0, 1):
            near_copy(turned, part).wait_send()
    for k in range(len(starts)):
        for way in (0, 1):
            for h in range(n - 1):
                hop(k, way, h).wait_send()
    for copy in started:
        copy.wait_send()


def reduce_all(n, xg, d, dz, wp, w, small):
    rows, tokens = D // n, xg.shape[0] // 4
    width, late = dz.shape[1], d.shape[1]
    starts = ((width, late), (0, width // 2), (width // 2, width))
    half = tokens // 2
    dma, vm = pltpu.SemaphoreType.DMA, pltpu.VMEM
    anywhere = pl.BlockSpec(memory_space=pl.ANY)
    inside = pl.BlockSpec(memory_space=pltpu.VMEM)
    return pl.pallas_call(
        functools.partial(reduce_body, n, rows, tokens, starts),
        in_specs=[anywhere] * 6,
        out_specs=[inside] * 4,
        out_shape=[
            jax.ShapeDtypeStruct((rows, late), f32),
            jax.ShapeDtypeStruct((tokens, D), f32),
            jax.ShapeDtypeStruct((rows, 2 * NS), f32),
            jax.ShapeDtypeStruct((4, *small.shape), f32),
        ],
        scratch_shapes=[
            vm(xg.shape, bf16), vm(d.shape, bf16), vm(dz.shape, bf16), vm((D, width), bf16), vm(w.shape, bf16),
            vm((half, D), f32), vm((D, late), bf16),
            [[vm((n - 1, size, hi - lo), bf16) for lo, hi in starts] for _, size in cut_rows(rows)],
            vm((2, 2, half, D), bf16), vm((2, 2, half, D), bf16), vm((2, half, D), bf16), vm((8, D), f32),
            vm((n, *small.shape), f32), vm((4, *small.shape), f32), vm((4, rows, 2 * NS), f32),
            dma((6,)), dma((2, 3, n - 1)), dma((2, 3, n - 1)), dma((2, 2)), dma((2, 2)), dma((2,)), dma((2,)),
            dma((2, n // 2)), dma((2, n // 2)), dma((3,)), dma((3,)), dma((2,)), dma((2,)),
        ],
        compiler_params=pltpu.CompilerParams(
            collective_id=1, has_side_effects=True, vmem_limit_bytes=ROOM
        ),
        name="reduce_all",
    )(xg, d, dz, wp, w, small)


def adamw_step(weight, first, second, grad, rate, decay):
    first_new = beta_first * first + (1.0 - beta_first) * grad
    second_new = beta_second * second + (1.0 - beta_second) * grad * grad
    hat_first = first_new / (1.0 - beta_first**STEP)
    hat_second = second_new / (1.0 - beta_second**STEP)
    weight_new = weight - rate * (hat_first / (jnp.sqrt(hat_second) + adam_eps) + decay * weight)
    return (weight_new, first_new, second_new)


def local(
    layer_input,
    out_grad,
    small_params,
    small_first,
    small_second,
    w_zx,
    zx_first,
    zx_second,
    w_bc,
    bc_first,
    bc_second,
    w_dt,
    dt_first,
    dt_second,
    w_out,
    out_first,
    out_second,
):
    tensor_index = lax.axis_index("tensor")
    local_in = layer_input.astype(f32)
    gain_in, gate_gain, conv_x, bias_x, conv_bc, bias_bc, dt_bias, a_log, d_skip = unpack(
        small_params
    )
    rows_own = w_zx.shape[0]
    width = w_zx.shape[2]
    heads = w_dt.shape[1]
    chan_start = tensor_index * width
    head_start = tensor_index * heads
    gate_local = lax.dynamic_slice_in_dim(gate_gain, chan_start, width, 0)
    conv_local = lax.dynamic_slice_in_dim(conv_x, chan_start, width, 1)
    bias_local = lax.dynamic_slice_in_dim(bias_x, chan_start, width, 0)
    dtb_local = lax.dynamic_slice_in_dim(dt_bias, head_start, heads, 0)
    a_local = -jnp.exp(lax.dynamic_slice_in_dim(a_log, head_start, heads, 0))
    dskip_local = lax.dynamic_slice_in_dim(d_skip, head_start, heads, 0)
    taps = jnp.concatenate(
        [
            jnp.concatenate([conv_local, conv_bc], axis=1),
            jnp.concatenate([bias_local, bias_bc])[None, :],
            jnp.zeros((8 - CONV - 1, width + 2 * NS), f32),
        ],
        axis=0,
    )
    lanes = lambda v: jnp.pad(v, (0, LANES - heads))
    head = jnp.pad(jnp.stack([lanes(dtb_local), lanes(a_local)]), ((0, 6), (0, 0)))
    chan = jnp.pad(jnp.stack([gate_local, jnp.repeat(dskip_local, P_SIZE)]), ((0, 6), (0, 0)))
    pick = jnp.asarray(
        (jnp.arange(width)[:, None] // P_SIZE == jnp.arange(LANES)[None, :]), bf16
    )

    inv_in = lax.rsqrt(jnp.mean(local_in * local_in, axis=-1, keepdims=True) + norm_eps)
    normed_in = local_in * inv_in * gain_in[None, :]
    low = lambda a: a.astype(bf16)
    w_late = jnp.concatenate(
        [low(w_zx[:, 1]), low(w_bc), low(jnp.pad(w_dt, ((0, 0), (0, LANES - heads))))], axis=1
    )
    w_pair = jnp.concatenate([low(w_zx[:, 0]), low(w_out)], axis=1)
    n = lax.axis_size("dp")
    xg, w_all = gather_all(n, normed_in.astype(bf16), w_late)
    z, v, xc, dr, y, dn, st, red, cot_all, pair_all = ssd_forward(
        n, xg, w_all, taps, head, chan, out_grad, w_pair
    )
    dy, dz, branch, early, gate = early_gradients(z, y, dn, red, pair_all, chan, xg, cot_all)
    d_late, small, owner_early, own_branch = ssd_backward(
        n, dy, v, xc, dr, st, gate, taps, head, chan, pick, early, branch
    )
    owner_late, d_normed_in, owner_bc, tens = reduce_all(n, xg, d_late, dz, pair_all, w_all, small)
    layer_output = (local_in + own_branch).astype(bf16)
    owner_zx = jnp.stack([owner_early[:, :width], owner_late[:, :width]], axis=1)
    owner_out = owner_early[:, width:]
    owner_dt = owner_late[:, width + 2 * NS : width + 2 * NS + heads]

    inner_in = jnp.sum(local_in * gain_in[None, :] * d_normed_in, axis=-1, keepdims=True)
    input_grad = (
        out_grad.astype(f32)
        + inv_in * gain_in[None, :] * d_normed_in
        - local_in * (inv_in * inv_in * inv_in * inner_in / D)
    )
    gain_sum = jnp.sum(tens[:, 6:8], axis=0).reshape(-1)[:D] / gain_in
    bc_sum = jnp.sum(tens[:, : CONV + 1, width:], axis=0)
    small_grad = jnp.concatenate(
        [
            gain_sum,
            tens[:, CONV + 1, :width].reshape(-1),
            jnp.moveaxis(tens[:, :CONV, :width], 0, 1).reshape(-1),
            tens[:, CONV, :width].reshape(-1),
            bc_sum.reshape(-1),
            tens[:, CONV + 1, width : width + heads].reshape(-1),
            tens[:, CONV + 1, width + LANES : width + LANES + heads].reshape(-1) * -jnp.exp(a_log),
            tens[:, 7, 512 : 512 + heads].reshape(-1),
        ]
    )
    small_new, small_first_new, small_second_new = adamw_step(
        small_params, small_first, small_second, small_grad, small_rate, 0.0
    )
    zx_new, zx_first_new, zx_second_new = adamw_step(
        w_zx, zx_first, zx_second, owner_zx, matrix_rate, matrix_decay
    )
    bc_new, bc_first_new, bc_second_new = adamw_step(
        w_bc, bc_first, bc_second, owner_bc, matrix_rate, matrix_decay
    )
    dt_new, dt_first_new, dt_second_new = adamw_step(
        w_dt, dt_first, dt_second, owner_dt, matrix_rate, matrix_decay
    )
    out_new, out_first_new, out_second_new = adamw_step(
        w_out, out_first, out_second, owner_out, matrix_rate, matrix_decay
    )
    return (
        layer_output,
        input_grad,
        small_new,
        small_first_new,
        small_second_new,
        zx_new,
        zx_first_new,
        zx_second_new,
        bc_new,
        bc_first_new,
        bc_second_new,
        dt_new,
        dt_first_new,
        dt_second_new,
        out_new,
        out_first_new,
        out_second_new,
    )


def solution(mesh):
    return jax.shard_map(
        local,
        mesh=mesh,
        in_specs=(
            P(("dp", "tensor"), None),
            P(("dp", "tensor"), None),
            P(),
            P(),
            P(),
            P("dp", None, "tensor"),
            P("dp", None, "tensor"),
            P("dp", None, "tensor"),
            P("dp", None),
            P("dp", None),
            P("dp", None),
            P("dp", "tensor"),
            P("dp", "tensor"),
            P("dp", "tensor"),
            P("dp", "tensor"),
            P("dp", "tensor"),
            P("dp", "tensor"),
        ),
        out_specs=(
            P(("dp", "tensor"), None),
            P(("dp", "tensor"), None),
            P(),
            P(),
            P(),
            P("dp", None, "tensor"),
            P("dp", None, "tensor"),
            P("dp", None, "tensor"),
            P("dp", None),
            P("dp", None),
            P("dp", None),
            P("dp", "tensor"),
            P("dp", "tensor"),
            P("dp", "tensor"),
            P("dp", "tensor"),
            P("dp", "tensor"),
            P("dp", "tensor"),
        ),
        check_vma=False,
    )
```

```python
import functools

import jax
import jax.numpy as jnp
from jax import lax
from jax.experimental import pallas as pl
from jax.experimental.pallas import tpu as pltpu
from jax.sharding import PartitionSpec as P

D = 1536
DI = 3072
H = 48
NS = 128
P_SIZE = 64
CONV = 4
LEN = 2048
STEP = 10

T = 128
ROWS = 256
LANES = 128
ROOM = 60 * 2**20

norm_eps = 1e-05
adam_eps = 1e-08
beta_first = 0.9
beta_second = 0.95
matrix_rate = 0.01
small_rate = 0.1
matrix_decay = 0.1

f32 = jnp.float32
bf16 = jnp.bfloat16
NN = (((1,), (0,)), ((), ()))
NT = (((1,), (1,)), ((), ()))
TN = (((0,), (0,)), ((), ()))
HIGHEST = lax.Precision.HIGHEST


GATE_ROW, TAPS_ROW, BIAS_ROW, TAPS_BC_ROW, BIAS_BC_ROW, HEAD_ROW, FLAT_ROWS = 12, 36, 132, 156, 164, 166, 168


def mm(a, b, dims=NN):
    return lax.dot_general(a, b, dims, preferred_element_type=f32)


def mm_exact(a, b, dims=NN):
    return lax.dot_general(a, b, dims, preferred_element_type=f32, precision=HIGHEST)


def sigmoid(v):
    return 0.5 * jnp.tanh(0.5 * v) + 0.5


def softplus(v):
    return jnp.maximum(v, 0.0) + jnp.log1p(jnp.exp(-jnp.abs(v)))


def spread(col):
    return jnp.broadcast_to(col, (T, LANES))


def block_iota(axis):
    return lax.broadcasted_iota(jnp.int32, (T, LANES), axis)


def head_rows(dr_ref, head_ref, rows):
    raw = dr_ref[rows, :] + head_ref[0:1, :]
    dt = softplus(raw)
    low_tri = jnp.where(block_iota(0) >= block_iota(1), 1.0, 0.0).astype(f32)
    decay = mm_exact(low_tri, dt * head_ref[1:2, :])
    return raw, dt, decay


def ring_place(n):
    me = lax.axis_index("dp")
    z, x = lax.div(me, 2), lax.rem(me, 2)
    return z + x * (n - 1 - 2 * z)


def ring_index(pos, n):
    back = lax.div(pos, n // 2)
    return 2 * pos + back * (2 * n - 1 - 4 * pos)


def neighbours(n):
    pos = ring_place(n)
    right = ring_index(lax.rem(pos + 1, n), n)
    left = ring_index(lax.rem(pos + n - 1, n), n)
    me = lax.axis_index("tensor")
    y, core = lax.div(me, 2), lax.rem(me, 2)
    across = 2 * (1 - y) + core
    beside = 2 * y + 1 - core
    return pos, ({"dp": right}, {"dp": left}), me, {"tensor": across}, {"tensor": beside}


def greet(peers):
    barrier = pltpu.get_barrier_semaphore()
    for peer in peers:
        pl.semaphore_signal(barrier, inc=1, device_id=peer, device_id_type=pl.DeviceIdType.MESH)


def enter(peers):
    greet(peers)
    pl.semaphore_wait(pltpu.get_barrier_semaphore(), len(peers))


def remote(src, dst, send_sem, recv_sem, peer):
    return pltpu.make_async_remote_copy(
        src_ref=src, dst_ref=dst, send_sem=send_sem, recv_sem=recv_sem,
        device_id=peer, device_id_type=pl.DeviceIdType.MESH,
    )


def span(start, size):
    return pl.ds(pl.multiple_of(start, 16), size)


def strip(rows):
    return next(size for size in (48, 32, 16) if rows % size == 0)


def cut_rows(rows):
    top = rows // 32 * 16
    return ((0, top), (top, rows - top))


def forward_body(
    n, rows, tokens, width,
    xg_ref, tall_ref, w_ref, flat_ref, cot_ref, wp_ref,
    z_ref, v_ref, xc_ref, dr_ref, y_ref, dn_ref, st_ref, red_ref, cots_ref, wps_ref, taps_ref, head_ref, chan_ref,
    halo, state, y_all, cots, wps, sums,
    own_keep, ring_keep, over_keep, side_keep, pass_keep, ring_send, ring_recv, over_send, over_recv,
    side_send, side_recv, pass_send, pass_recv, sum_send, sum_recv,
):
    pairs = width // LANES
    wide = width + 2 * NS
    step = pl.program_id(0)
    steps = LEN // ROWS
    tall = 2 * ROWS
    gating, norming = steps, steps + LEN // tall
    last_step = norming + LEN // tall - 1
    pos, ring, me, across, beside = neighbours(n)
    opposite = lax.rem(me + 2, 4)
    next_door = me + 1 - 2 * lax.rem(me, 2)
    far = lax.rem(next_door + 2, 4)
    half = tokens // 2
    hops = n // 2
    cuts = cut_rows(rows)
    mine = ring_index(pos, n)

    def hop(k, part, way, h):
        first, size = cuts[part]
        cols = pl.ds(k * width, width)
        block = ring_index(lax.rem(pos + (h if way else n - h), n), n)
        here = wps.at[span(block * rows + first, size), cols]
        src = wp_ref.at[pl.ds(first, size), cols] if h == 0 else here
        return remote(src, here, ring_send.at[way, part, k, h], ring_recv.at[way, part, k, h], ring[way])

    def hop_lands(k, part, way, h):
        first, size = cuts[part]
        block = ring_index(lax.rem(pos + (h + 1 if way else n - h - 1), n), n)
        return span(block * rows + first, size), pl.ds(k * width, width)

    def hop_arrival(k, part, way, h):
        here = wps.at[hop_lands(k, part, way, h)]
        return remote(here, here, ring_send.at[way, part, k, h], ring_recv.at[way, part, k, h], ring[way])

    def hop_keep(k, part, way, h):
        at = hop_lands(k, part, way, h)
        return pltpu.make_async_copy(wps.at[at], wps_ref.at[at], ring_keep.at[way, part, k, h])

    def hop_ways(h):
        return [(part, way) for part in (0, 1) for way in (0, 1) if h < hops - 1 or part == way]

    def hop_on(k, h):
        for part, way in hop_ways(h - 1) if h > 0 else ():
            hop_arrival(k, part, way, h - 1).wait_recv()
            hop_keep(k, part, way, h - 1).start()
            if h < hops and (part, way) in hop_ways(h):
                hop(k, part, way, h).start()
        if h == 0:
            for part, way in hop_ways(0):
                hop(k, part, way, 0).start()

    def over(k):
        return remote(
            cot_ref.at[pl.ds(k * half, half)], cots.at[span(me * tokens + k * half, half)],
            over_send.at[k], over_recv.at[k], across,
        )

    def landed(full, start, size, send, recv, peer):
        here = full.at[span(start, size)]
        return remote(here, here, send, recv, peer)

    def over_arrival(k):
        start = opposite * tokens + k * half
        return landed(cots, start, half, over_send.at[k], over_recv.at[k], across)

    def passing(k):
        start = opposite * tokens + k * half
        return landed(cots, start, half, pass_send.at[k], pass_recv.at[k], beside)

    def pass_arrival(k):
        return landed(cots, far * tokens + k * half, half, pass_send.at[k], pass_recv.at[k], beside)

    def side():
        return remote(cot_ref, cots.at[span(me * tokens, tokens)], side_send.at[0], side_recv.at[0], beside)

    def side_arrival():
        return landed(cots, next_door * tokens, tokens, side_send.at[0], side_recv.at[0], beside)

    def keep(start, size, sem):
        return pltpu.make_async_copy(cots.at[span(start, size)], cots_ref.at[span(start, size)], sem)

    def own_keeps():
        return (
            pltpu.make_async_copy(cot_ref, cots_ref.at[span(me * tokens, tokens)], own_keep.at[0]),
            pltpu.make_async_copy(wp_ref, wps_ref.at[span(mine * rows, rows)], own_keep.at[1]),
            pltpu.make_async_copy(cot_ref, cots.at[span(me * tokens, tokens)], own_keep.at[2]),
            pltpu.make_async_copy(wp_ref, wps.at[span(mine * rows, rows)], own_keep.at[3]),
        )

    @pl.when(step == 0)
    def _():
        enter((*ring, across, beside))
        hop_on(0, 0)
        over(0).start()
        over(1).start()
        side().start()
        for copy in own_keeps():
            copy.start()
        halo[0:8, :] = jnp.zeros((8, wide), f32)
        state[...] = jnp.zeros_like(state)
        parameter_rows(me, width, flat_ref, taps_ref, head_ref, chan_ref)

    for h in range(1, hops):
        at = (2, 5, gating)[h - 1] if h < 4 else gating
        pl.when(step == at)(functools.partial(hop_on, 0, h))
    for h in range(hops):
        at = (1, 4, 7, gating)[h] if h < 4 else norming
        pl.when(step == at)(functools.partial(hop_on, 1, h))
    pl.when(step == gating)(functools.partial(hop_on, 0, hops))
    pl.when(step == norming)(functools.partial(hop_on, 1, hops))

    @pl.when(step == gating)
    def _():
        for k in (0, 1):
            over_arrival(k).wait_recv()
            passing(k).start()
            keep(opposite * tokens + k * half, half, over_keep.at[k]).start()
        for copy in own_keeps():
            copy.wait()

    @pl.when(step == norming)
    def _():
        side_arrival().wait_recv()
        keep(next_door * tokens, tokens, side_keep.at[0]).start()
        for k in (0, 1):
            pass_arrival(k).wait_recv()
            keep(far * tokens + k * half, half, pass_keep.at[k]).start()

    @pl.when(step < gating)
    def _():
        scan_step(
            width, step, xg_ref, w_ref, taps_ref, head_ref, chan_ref,
            v_ref, xc_ref, dr_ref, y_ref, st_ref, halo, state, y_all,
        )

    def token_sum(row, first, value):
        lanes = pl.ds(pl.multiple_of(first, tall), tall)
        sums[0, row : row + 4, lanes] = mm_exact(jnp.ones((8, LANES), f32), value, NT)[0:4]

    @pl.when((step >= gating) & (step < norming))
    def _():
        first = (step - gating) * tall
        z_ref[...] = mm(tall_ref[...], wps[:, :width])
        squares = jnp.zeros((tall, LANES), f32)
        for p in range(pairs):
            cols = slice(p * LANES, (p + 1) * LANES)
            z = z_ref[:, cols]
            gated = y_all[span(first, tall), cols] * (z * sigmoid(z))
            y_all[span(first, tall), cols] = gated
            squares = squares + gated * gated
        token_sum(0, first, squares)

    @pl.when(step >= norming)
    def _():
        first = (step - norming) * tall
        dn_ref[...] = mm(cots[span(first, tall), :], wps[:, width:])
        inner = jnp.zeros((tall, LANES), f32)
        for p in range(pairs):
            cols = slice(p * LANES, (p + 1) * LANES)
            inner = inner + y_all[span(first, tall), cols] * chan_ref[0:1, cols] * dn_ref[:, cols]
        token_sum(4, first, inner)

    @pl.when(step == last_step)
    def _():
        first = remote(sums.at[0], sums.at[1], sum_send.at[0], sum_recv.at[0], beside)
        first.start()
        first.wait_recv()
        sums[2] = sums[0] + sums[1]
        second = remote(sums.at[2], sums.at[3], sum_send.at[1], sum_recv.at[1], across)
        second.start()
        for h in range(hops):
            for part, way in hop_ways(h):
                for k in (0, 1):
                    hop(k, part, way, h).wait_send()
                    hop_keep(k, part, way, h).wait()
        side().wait_send()
        keep(next_door * tokens, tokens, side_keep.at[0]).wait()
        for k in (0, 1):
            over(k).wait_send()
            passing(k).wait_send()
            keep(opposite * tokens + k * half, half, over_keep.at[k]).wait()
            keep(far * tokens + k * half, half, pass_keep.at[k]).wait()
        first.wait_send()
        second.wait()
        red_ref[...] = sums[2] + sums[3]


def parameter_rows(me, width, flat_ref, taps_ref, head_ref, chan_ref):
    pairs = width // LANES
    heads = width // P_SIZE
    taps_ref[...] = jnp.zeros_like(taps_ref)
    chan_ref[...] = jnp.zeros_like(chan_ref)
    for c in range(pairs):
        cols = slice(c * LANES, (c + 1) * LANES)
        chan_ref[0:1, cols] = flat_ref[pl.ds(GATE_ROW + pairs * me + c, 1), :]
        taps_ref[CONV : CONV + 1, cols] = flat_ref[pl.ds(BIAS_ROW + pairs * me + c, 1), :]
        for k in range(CONV):
            taps_ref[k : k + 1, cols] = flat_ref[pl.ds(TAPS_ROW + 4 * pairs * k + pairs * me + c, 1), :]
    for c in range(2):
        cols = slice(width + c * LANES, width + (c + 1) * LANES)
        taps_ref[CONV : CONV + 1, cols] = flat_ref[BIAS_BC_ROW + c : BIAS_BC_ROW + c + 1, :]
        for k in range(CONV):
            row = TAPS_BC_ROW + 2 * k + c
            taps_ref[k : k + 1, cols] = flat_ref[row : row + 1, :]
    both = jnp.concatenate([flat_ref[HEAD_ROW : HEAD_ROW + 1, :], flat_ref[HEAD_ROW + 1 : HEAD_ROW + 2, :]], axis=1)
    both = jnp.broadcast_to(both, (8, 2 * LANES))
    lane = lax.broadcasted_iota(jnp.int32, (2 * LANES, LANES), 0)
    head = lax.broadcasted_iota(jnp.int32, (2 * LANES, LANES), 1)

    def take(kind):
        match = (lane == 4 * heads * kind + heads * me + head) & (head < heads)
        return mm_exact(both, jnp.where(match, 1.0, 0.0).astype(f32))

    valid = lax.broadcasted_iota(jnp.int32, (8, LANES), 1) < heads
    row = lax.broadcasted_iota(jnp.int32, (8, LANES), 0)
    rates = jnp.where(valid, -jnp.exp(take(1)), 0.0)
    head_ref[...] = jnp.where(row == 0, take(0), jnp.where(row == 1, rates, 0.0))
    skip = mm_exact(take(2), picked(width).astype(f32), NT)
    chan_ref[1:2, :] = skip[0:1]


def picked(width):
    channel = lax.broadcasted_iota(jnp.int32, (width, LANES), 0)
    head = lax.broadcasted_iota(jnp.int32, (width, LANES), 1)
    return jnp.where((channel >= head * P_SIZE) & (channel < (head + 1) * P_SIZE), 1.0, 0.0).astype(bf16)


def scan_step(
    width, step, xg_ref, w_ref, taps_ref, head_ref, chan_ref,
    v_ref, xc_ref, dr_ref, y_ref, st_ref, halo, state, y_all,
):
    pairs = width // LANES
    wide = width + 2 * NS
    dr_ref[...] = mm(xg_ref[...], w_ref[:, wide:])
    halo[8 : 8 + ROWS, :] = mm(xg_ref[...], w_ref[:, :wide])
    low_half = block_iota(1) < P_SIZE
    causal = block_iota(0) >= block_iota(1)

    def convolved(sub, block):
        cols = slice(block * LANES, (block + 1) * LANES)
        total = taps_ref[CONV : CONV + 1, cols]
        for k in range(CONV):
            first = 8 - (CONV - 1) + k + sub * T
            total = total + taps_ref[k : k + 1, cols] * halo[first : first + T, cols]
        rows = slice(sub * T, (sub + 1) * T)
        xc_ref[rows, cols] = total
        v_ref[rows, cols] = halo[8 + sub * T : 8 + (sub + 1) * T, cols].astype(bf16)
        return total * sigmoid(total)

    for sub in range(ROWS // T):
        rows = slice(sub * T, (sub + 1) * T)
        raw, dt, decay = head_rows(dr_ref, head_ref, rows)
        decay_t = decay.T
        b_low = convolved(sub, pairs).astype(bf16)
        c_low = convolved(sub, pairs + 1).astype(bf16)
        b_t = b_low.T
        scores = jnp.where(causal, mm(c_low, b_low, NT), 0.0)
        st_ref[sub] = state[...].astype(bf16)
        for p in range(pairs):
            cols = slice(p * LANES, (p + 1) * LANES)
            x = convolved(sub, p)
            l1, l2 = spread(decay[:, 2 * p : 2 * p + 1]), spread(decay[:, 2 * p + 1 : 2 * p + 2])
            both = jnp.where(low_half, l1, l2)
            dtb = jnp.where(
                low_half, spread(dt[:, 2 * p : 2 * p + 1]), spread(dt[:, 2 * p + 1 : 2 * p + 2])
            )
            u = x * dtb
            m1 = scores * jnp.exp(jnp.minimum(l1 - decay_t[2 * p : 2 * p + 1, :], 0.0))
            m2 = scores * jnp.exp(jnp.minimum(l2 - decay_t[2 * p + 1 : 2 * p + 2, :], 0.0))
            mixing = jnp.concatenate([m1.astype(bf16), m2.astype(bf16)], axis=1)
            parts = jnp.concatenate(
                [jnp.where(low_half, u, 0.0).astype(bf16), jnp.where(low_half, 0.0, u).astype(bf16)],
                axis=0,
            )
            last = both[T - 1 : T, :]
            entering = st_ref[sub, :, cols]
            y = mm(mixing, parts) + jnp.exp(both) * mm(c_low, entering) + chan_ref[1:2, cols] * x
            tail = (u * jnp.exp(last - both)).astype(bf16)
            state[:, cols] = jnp.exp(last) * state[:, cols] + mm(b_t, tail)
            y_ref[rows, cols] = y
            y_all[span(step * ROWS + sub * T, T), cols] = y
    halo[0:8, :] = halo[ROWS : ROWS + 8, :]


def ssd_forward(n, xg, w, flat, cot, wp):
    length = xg.shape[0]
    rows, width = wp.shape[0], wp.shape[1] // 2
    tokens = cot.shape[0]
    wide = width + 2 * NS
    steps = length // ROWS
    tall = 2 * ROWS
    more = length // tall
    subs = ROWS // T
    assert length == LEN
    early = lambda i: jnp.minimum(i, steps - 1)
    middle = lambda i: jnp.clip(i - steps, 0, more - 1)
    row = lambda m: pl.BlockSpec((ROWS, m), lambda i: (early(i), 0))
    whole = lambda a: pl.BlockSpec(a.shape, lambda i: (0,) * a.ndim, pipeline_mode=pl.Buffered(1))
    anywhere = pl.BlockSpec(memory_space=pl.ANY)
    vm, dma = pltpu.VMEM, pltpu.SemaphoreType.DMA
    hops = dma((2, 2, 2, n // 2))
    return pl.pallas_call(
        functools.partial(forward_body, n, rows, tokens, width),
        grid=(steps + 2 * more,),
        in_specs=[
            row(D), pl.BlockSpec((tall, D), lambda i: (middle(i), 0)),
            whole(w), whole(flat), whole(cot), whole(wp),
        ],
        out_specs=[
            pl.BlockSpec((tall, width), lambda i: (middle(i), 0)),
            row(wide), row(wide), row(LANES), row(width),
            pl.BlockSpec((tall, width), lambda i: (jnp.maximum(i - steps - more, 0), 0)),
            pl.BlockSpec((subs, NS, width), lambda i: (early(i), 0, 0)),
            pl.BlockSpec((8, length), lambda i: (0, 0)),
            anywhere, anywhere,
            *(pl.BlockSpec((8, m), lambda i: (0, 0)) for m in (wide, LANES, width)),
        ],
        out_shape=[
            jax.ShapeDtypeStruct((length, width), f32),
            jax.ShapeDtypeStruct((length, wide), bf16),
            jax.ShapeDtypeStruct((length, wide), f32),
            jax.ShapeDtypeStruct((length, LANES), f32),
            jax.ShapeDtypeStruct((length, width), f32),
            jax.ShapeDtypeStruct((length, width), f32),
            jax.ShapeDtypeStruct((length // T, NS, width), bf16),
            jax.ShapeDtypeStruct((8, length), f32),
            jax.ShapeDtypeStruct((4 * tokens, D), bf16),
            jax.ShapeDtypeStruct((n * rows, 2 * width), bf16),
            *(jax.ShapeDtypeStruct((8, m), f32) for m in (wide, LANES, width)),
        ],
        scratch_shapes=[
            vm((ROWS + 8, wide), f32), vm((NS, width), f32), vm((length, width), f32),
            vm((4 * tokens, D), bf16), vm((n * rows, 2 * width), bf16), vm((4, 8, length), f32),
            dma((4,)), hops, dma((2,)), dma((1,)), dma((2,)), hops, hops, dma((2,)), dma((2,)),
            dma((1,)), dma((1,)), dma((2,)), dma((2,)), dma((2,)), dma((2,)),
        ],
        compiler_params=pltpu.CompilerParams(collective_id=2, has_side_effects=True, vmem_limit_bytes=ROOM),
        name="layer_forward",
    )(xg, xg, w, flat, cot, wp)


def gather_body(
    n, rows, tokens,
    in_ref, flat_ref, wzx_ref, wbc_ref, wdt_ref, wout_ref, xg_ref, ws_ref, wp_ref, x_ref, w_ref, xg, ws,
    keep_sem, ring_keep, ring_send, ring_recv, over_send, over_recv, side_send, side_recv, pass_send, pass_recv,
):
    pos, ring, me, across, beside = neighbours(n)
    greet((*ring, across, beside))
    half = tokens // 2
    width = wout_ref.shape[1]
    heads = wdt_ref.shape[0]
    w_ref[:, :width] = wzx_ref[:, 1, :].astype(bf16)
    w_ref[:, width : width + 2 * NS] = wbc_ref[...].astype(bf16)
    unit = jnp.where(
        lax.broadcasted_iota(jnp.int32, (16, LANES), 0) == lax.broadcasted_iota(jnp.int32, (16, LANES), 1), 1.0, 0.0
    ).astype(bf16)
    steps_w = jnp.concatenate([wdt_ref[...], jnp.zeros((16 - heads, rows), f32)], axis=0).astype(bf16)
    w_ref[:, width + 2 * NS :] = mm(steps_w, unit, TN).astype(bf16)

    def normalize(k):
        def some(i, _):
            at = span(k * half + i * 64, 64)
            squares = jnp.zeros((64, LANES), f32)
            for c in range(D // LANES):
                x = in_ref[at, c * LANES : (c + 1) * LANES].astype(f32)
                squares = squares + x * x
            inverse = lax.rsqrt(jnp.sum(squares, axis=-1, keepdims=True) / D + norm_eps)
            inverse = jnp.broadcast_to(inverse, (64, LANES))
            for c in range(D // LANES):
                cols = slice(c * LANES, (c + 1) * LANES)
                x_ref[at, cols] = (in_ref[at, cols].astype(f32) * inverse * flat_ref[c : c + 1, :]).astype(bf16)
            return 0

        lax.fori_loop(0, half // 64, some, 0)

    normalize(0)
    pl.semaphore_wait(pltpu.get_barrier_semaphore(), 4)
    started, kept = [], []

    def go(*args):
        copy = remote(*args)
        copy.start()
        started.append(copy)
        return copy

    def keep(src, dst, sem):
        copy = pltpu.make_async_copy(src, dst, sem)
        copy.start()
        kept.append(copy)

    opposite = lax.rem(me + 2, 4)
    next_door = me + 1 - 2 * lax.rem(me, 2)
    far = lax.rem(next_door + 2, 4)
    cuts = cut_rows(rows)

    def arrived(part, way, step, block):
        first, size = cuts[part]
        at = span(block * rows + first, size)
        remote(
            ws.at[at], ws.at[at], ring_send.at[way, part, step], ring_recv.at[way, part, step], ring[way]
        ).wait_recv()
        keep(ws.at[at], ws_ref.at[at], ring_keep.at[way, part, step])

    def ring_step(step, parts=(0, 1)):
        last = step == n // 2 - 1
        for part in parts:
            first, size = cuts[part]
            for way in (0, 1):
                block = ring_index(lax.rem(pos + (step if way else n - step), n), n)
                here = ws.at[span(block * rows + first, size)]
                if step > 0:
                    arrived(part, way, step - 1, block)
                if last and part != way:
                    continue
                src = w_ref.at[pl.ds(first, size)] if step == 0 else here
                go(src, here, ring_send.at[way, part, step], ring_recv.at[way, part, step], ring[way])

    def pass_on(k):
        at = span(opposite * tokens + k * half, half)
        here = xg.at[at]
        remote(here, here, over_send.at[k], over_recv.at[k], across).wait_recv()
        go(here, here, pass_send.at[k], pass_recv.at[k], beside)
        keep(here, xg_ref.at[at], keep_sem.at[k])

    ring_step(0, (0,))
    leading = list(started)
    for k in (0, 1):
        if k == 1:
            normalize(1)
        go(
            x_ref.at[pl.ds(k * half, half)], xg.at[span(me * tokens + k * half, half)],
            over_send.at[k], over_recv.at[k], across,
        )
    go(x_ref, xg.at[span(me * tokens, tokens)], side_send.at[0], side_recv.at[0], beside)
    mine = ring_index(pos, n)
    keep(x_ref, xg_ref.at[span(me * tokens, tokens)], keep_sem.at[2])
    keep(w_ref, ws_ref.at[span(mine * rows, rows)], keep_sem.at[3])
    wp_ref[:, :width] = wzx_ref[:, 0, :].astype(bf16)
    wp_ref[:, width:] = wout_ref[...].astype(bf16)
    for copy in leading:
        copy.wait_send()
        started.remove(copy)
    ring_step(0, (1,))
    for step in range(1, n // 2):
        ring_step(step)
        if step == n // 2 - 2:
            pass_on(0)
            pass_on(1)
    at = span(next_door * tokens, tokens)
    remote(xg.at[at], xg.at[at], side_send.at[0], side_recv.at[0], beside).wait_recv()
    keep(xg.at[at], xg_ref.at[at], keep_sem.at[4])
    for k in (0, 1):
        at = span(far * tokens + k * half, half)
        remote(xg.at[at], xg.at[at], pass_send.at[k], pass_recv.at[k], beside).wait_recv()
        keep(xg.at[at], xg_ref.at[at], keep_sem.at[5 + k])
    for part in (0, 1):
        arrived(part, part, n // 2 - 1, ring_index(lax.rem(pos + n // 2, n), n))
    for copy in kept:
        copy.wait()
    for copy in started:
        copy.wait_send()


def gather_all(n, layer_input, flat, w_zx, w_bc, w_dt, w_out):
    tokens, rows, width = layer_input.shape[0], w_bc.shape[0], w_out.shape[1]
    late = width + 2 * NS + LANES
    dma = pltpu.SemaphoreType.DMA
    anywhere = pl.BlockSpec(memory_space=pl.ANY)
    inside = pl.BlockSpec(memory_space=pltpu.VMEM)
    own = ((tokens, D), (rows, late))
    full = ((4 * tokens, D), (n * rows, late))
    hops = dma((2, 2, n // 2))
    return pl.pallas_call(
        functools.partial(gather_body, n, rows, tokens),
        in_specs=[inside] * 6,
        out_specs=[anywhere, anywhere, inside],
        out_shape=[jax.ShapeDtypeStruct(shape, bf16) for shape in (*full, (rows, 2 * width))],
        scratch_shapes=[
            *(pltpu.VMEM(shape, bf16) for shape in (*own, *full)),
            dma((7,)), hops, hops, hops, dma((2,)), dma((2,)), dma((1,)), dma((1,)), dma((2,)), dma((2,)),
        ],
        compiler_params=pltpu.CompilerParams(collective_id=0, has_side_effects=True, vmem_limit_bytes=ROOM),
        name="gather_all",
    )(layer_input, flat, w_zx, w_bc, w_dt, w_out)


def gradient_body(
    width,
    z_ref, y_ref, dn_ref, red_ref, wo_ref, chan_ref, xg_ref, cot_ref,
    dy_ref, dz_ref, branch_ref, early_ref, gate_ref,
    nl, dz_all, fresh, hold,
):
    step = pl.program_id(0)
    steps = LEN // ROWS
    slab = D // (width // LANES)

    def multiply(p):
        at = slice(p * slab, (p + 1) * slab)
        branch_ref[:, at] = mm(hold[...], wo_ref[at, :], NT).astype(bf16)

    @pl.when(step == 0)
    def _():
        gate_ref[...] = jnp.zeros_like(gate_ref)
        hold[...] = jnp.zeros_like(hold)

    @pl.when(step < steps)
    def _():
        q_row = lax.rsqrt(red_ref[0:4, :] / DI + norm_eps)
        k_row = q_row * q_row * q_row * red_ref[4:8, :] / DI
        turned = jnp.concatenate([q_row, k_row], axis=0).T
        for p in range(width // LANES):
            cols = slice(p * LANES, (p + 1) * LANES)
            multiply(p)
            for sub in range(ROWS // T):
                rows = slice(sub * T, (sub + 1) * T)
                q, kk = spread(turned[rows, 0:1]), spread(turned[rows, 4:5])
                z, y, dn = z_ref[rows, cols], y_ref[rows, cols], dn_ref[rows, cols]
                gain = chan_ref[0:1, cols]
                s = sigmoid(z)
                sz = z * s
                gated = y * sz
                gq = gated * q
                dg = q * gain * dn - gated * kk
                gate_ref[:, cols] += jnp.sum((gq * dn).reshape(T // 8, 8, LANES), axis=0)
                fresh[rows, cols] = (gq * gain).astype(bf16)
                dz_ref[rows, cols] = (dg * y * (s + sz * (1.0 - s))).astype(bf16)
                dy_ref[rows, cols] = dg * sz
        at = span(step * ROWS, ROWS)
        hold[...] = fresh[...]
        nl[at, :] = fresh[...]
        dz_all[at, :] = dz_ref[...]

    @pl.when(step == steps)
    def _():
        for p in range(width // LANES):
            multiply(p)

    @pl.when(step >= steps)
    def _():
        early_ref[:, :width] = mm(xg_ref[...], dz_all[...], TN).astype(bf16)
        early_ref[:, width:] = mm(cot_ref[...], nl[...], TN).astype(bf16)


def early_gradients(z, y, dn, red, wp, chan, xg, cot):
    length, width = z.shape
    steps = length // ROWS
    deep = 2 * LANES
    early = lambda i: jnp.minimum(i, steps - 1)
    late = lambda i: jnp.maximum(i - steps, 0)
    row = lambda m: pl.BlockSpec((ROWS, m), lambda i: (early(i), 0))
    column = pl.BlockSpec((length, deep), lambda i: (0, late(i)))
    whole = lambda a: pl.BlockSpec(a.shape, lambda i: (0,) * a.ndim, pipeline_mode=pl.Buffered(1))
    return pl.pallas_call(
        functools.partial(gradient_body, width),
        grid=(steps + D // deep,),
        in_specs=[
            row(width), row(width), row(width), pl.BlockSpec((8, ROWS), lambda i: (0, early(i))),
            pl.BlockSpec((D, width), lambda i: (0, 1), pipeline_mode=pl.Buffered(1)),
            whole(chan), column, column,
        ],
        out_specs=[
            row(width), row(width), pl.BlockSpec((ROWS, D), lambda i: (jnp.clip(i - 1, 0, steps - 1), 0)),
            pl.BlockSpec((deep, 2 * width), lambda i: (late(i), 0)),
            pl.BlockSpec((8, width), lambda i: (0, 0)),
        ],
        out_shape=[
            jax.ShapeDtypeStruct((length, width), f32),
            jax.ShapeDtypeStruct((length, width), bf16),
            jax.ShapeDtypeStruct((length, D), bf16),
            jax.ShapeDtypeStruct((D, 2 * width), bf16),
            jax.ShapeDtypeStruct((8, width), f32),
        ],
        scratch_shapes=[pltpu.VMEM((rows, width), bf16) for rows in (length, length, ROWS, ROWS)],
        compiler_params=pltpu.CompilerParams(vmem_limit_bytes=ROOM),
        name="early_gradients",
    )(z, y, dn, red, wp, chan, xg, cot)


def backward_body(
    n, own_rows, tokens, width,
    dy_ref, v_ref, xc_ref, dr_ref, st_ref, gate_ref, taps_ref, head_ref, chan_ref, early_ref, branch_ref,
    d_ref, small_ref, oearly_ref, obranch_ref,
    dxh, dstate, yst, bds, dyeb, utb, gin, gout, xdu, turn, acc, hacc, pick_ref,
    own, slots, near, held, over_slot,
    load_sem, ring_send, ring_recv, near_send, near_recv, over_send, over_recv,
):
    pairs = width // LANES
    wide = width + 2 * NS
    step = pl.program_id(0)
    steps = LEN // ROWS
    pos, ring, me, across, beside = neighbours(n)
    opposite = lax.rem(me + 2, 4)
    next_door = me + 1 - 2 * lax.rem(me, 2)
    far = lax.rem(next_door + 2, 4)
    half = tokens // 2
    cuts = cut_rows(own_rows)

    def block_at(way, count):
        return ring_index(lax.rem(pos + (count if way else n - count), n), n)

    def hop(k, way, h):
        first, size = cuts[way]
        if h == 0:
            src = early_ref.at[span(block_at(way, 1) * own_rows + first, size), pl.ds(k * width, width)]
        else:
            src = slots[way][k].at[h - 1]
        return remote(
            src, slots[way][k].at[h], ring_send.at[way, k, h], ring_recv.at[way, k, h], ring[way]
        )

    def near_copy(turned, part):
        start = (next_door if turned else far) * tokens + part * half
        return remote(
            branch_ref.at[span(start, half)], near.at[turned, part],
            near_send.at[turned, part], near_recv.at[turned, part], beside,
        )

    def held_copy(turned, part):
        start = (me if turned else opposite) * tokens + part * half
        return pltpu.make_async_copy(
            branch_ref.at[span(start, half)], held.at[turned, part], load_sem.at[2 * turned + part]
        )

    def over_copy(part):
        return remote(held.at[0, part], over_slot.at[part], over_send.at[part], over_recv.at[part], across)

    def own_copy():
        return pltpu.make_async_copy(early_ref, own, load_sem.at[4])

    def ring_turn(k, h):
        for way in (0, 1):
            first, size = cuts[way]
            hop(k, way, h).wait_recv()
            block = block_at(way, 2 + h) if h < n - 2 else block_at(way, 0)

            tile = strip(size)

            def some(i, _, way=way, first=first, block=block, tile=tile):
                cols = slice(k * width, (k + 1) * width)
                came = slots[way][k][h, span(i * tile, tile), :]
                mine = own[span(block * own_rows + first + i * tile, tile), cols]
                if h < n - 2:
                    slots[way][k][h, span(i * tile, tile), :] = came + mine
                else:
                    oearly_ref[span(first + i * tile, tile), cols] = came.astype(f32) + mine.astype(f32)
                return 0

            lax.fori_loop(0, size // tile, some, 0)
            if h < n - 2:
                hop(k, way, h + 1).start()

    def ring_poll(k):
        for h in range(n - 1):
            pl.when(step == min(h + 1, steps - 1))(functools.partial(ring_turn, k, h))

    def add_near(turned):
        for part in (0, 1):
            held_copy(turned, part).wait()
            near_copy(turned, part).wait_recv()

            def some(i, _, part=part):
                at = span(i * 32, 32)
                if turned:
                    total = held[1, part, at, :].astype(f32) + near[1, part, at, :].astype(f32)
                    obranch_ref[span(part * half + i * 32, 32), :] = total
                else:
                    held[0, part, at, :] = held[0, part, at, :] + near[0, part, at, :]
                return 0

            lax.fori_loop(0, half // 32, some, 0)
            if not turned:
                over_copy(part).start()

    @pl.when(step == 0)
    def _():
        enter((*ring, across, beside))
        for way in (0, 1):
            hop(0, way, 0).start()
        for turned in (0, 1):
            for part in (0, 1):
                near_copy(turned, part).start()
                held_copy(turned, part).start()
        own_copy().start()
        dxh[T : T + 8, :] = jnp.zeros((8, wide), f32)
        dstate[...] = jnp.zeros_like(dstate)
        acc[...] = jnp.zeros_like(acc)
        hacc[...] = jnp.zeros_like(hacc)
        turn[...] = jnp.zeros_like(turn)
        pick_ref[...] = picked(width)

    @pl.when(step == 1)
    def _():
        own_copy().wait()
        add_near(0)

    pl.when(step == 2)(functools.partial(add_near, 1))
    ring_poll(0)

    low_half = block_iota(1) < P_SIZE
    row_at, col_at = block_iota(0), block_iota(1)
    until = row_at <= col_at
    before = row_at < col_at
    upper = jnp.where(until, 1.0, 0.0).astype(f32)
    strict = jnp.where(before, 1.0, 0.0).astype(f32)
    low_tri = jnp.where(row_at >= col_at, 1.0, 0.0).astype(bf16)

    def add(index, cols, value):
        acc[index, :, cols] += jnp.sum(value.reshape(T // 8, 8, LANES), axis=0)

    def conv_back(rows, block, d_act, xc, s, act):
        cols = slice(block * LANES, (block + 1) * LANES)
        dxh[0:T, cols] = d_act * (s + act * (1.0 - s))
        v = v_ref[rows, cols].astype(f32)
        total = None
        for m in range(CONV):
            moved = dxh[m : m + T, cols]
            if m == 0:
                add(CONV, cols, moved)
            add(CONV - 1 - m, cols, v * moved)
            term = taps_ref[CONV - 1 - m : CONV - m, cols] * moved
            total = term if total is None else total + term
        d_ref[rows, cols] = total.astype(bf16)

    for sub in reversed(range(ROWS // T)):
        rows = slice(sub * T, (sub + 1) * T)
        raw, dt, decay = head_rows(dr_ref, head_ref, rows)
        decay_t = decay.T
        b_cols = slice(width, width + NS)
        c_cols = slice(width + NS, width + 2 * NS)
        b_xc, c_xc = xc_ref[rows, b_cols], xc_ref[rows, c_cols]
        b_s, c_s = sigmoid(b_xc), sigmoid(c_xc)
        b_act, c_act = b_xc * b_s, c_xc * c_s
        b_low, c_low = b_act.astype(bf16), c_act.astype(bf16)
        c_t = c_low.T
        scores_t = jnp.where(until, mm(b_low, c_low, NT), 0.0)
        ds_low = dstate[...].astype(bf16)
        yst[...] = mm(c_low, st_ref[sub])
        bds[...] = mm(b_low, ds_low)
        d_scores = jnp.zeros((T, LANES), f32)
        for p in range(pairs):
            cols = slice(p * LANES, (p + 1) * LANES)
            dy = dy_ref[rows, cols]
            xc = xc_ref[rows, cols]
            xs = sigmoid(xc)
            x = xc * xs
            l1, l2 = spread(decay[:, 2 * p : 2 * p + 1]), spread(decay[:, 2 * p + 1 : 2 * p + 2])
            both = jnp.where(low_half, l1, l2)
            dtb = jnp.where(
                low_half, spread(dt[:, 2 * p : 2 * p + 1]), spread(dt[:, 2 * p + 1 : 2 * p + 2])
            )
            u = x * dtb
            last = both[T - 1 : T, :]
            e1 = jnp.exp(jnp.minimum(decay_t[2 * p : 2 * p + 1, :] - l1, 0.0))
            e2 = jnp.exp(jnp.minimum(decay_t[2 * p + 1 : 2 * p + 2, :] - l2, 0.0))
            dy_low = dy.astype(bf16)
            zero = jnp.zeros_like(dy_low)
            u_low = u.astype(bf16)
            du_in = mm(
                jnp.concatenate([(scores_t * e1).astype(bf16), (scores_t * e2).astype(bf16)], axis=1),
                jnp.concatenate(
                    [jnp.where(low_half, dy_low, zero), jnp.where(low_half, zero, dy_low)], axis=0
                ),
            )
            d_mix = mm(
                jnp.concatenate(
                    [jnp.where(low_half, u_low, zero), jnp.where(low_half, zero, u_low)], axis=0
                ),
                dy_low,
                NT,
            )
            d1, d2 = d_mix[:T] * e1, d_mix[T:] * e2
            d_scores = d_scores + d1 + d2
            reach = mm(
                jnp.concatenate([(d1 * scores_t).astype(bf16), (d2 * scores_t).astype(bf16)], axis=0),
                low_tri,
            )
            turn[2 * p : 2 * p + 1, :] = jnp.sum(jnp.where(before, reach[:T], 0.0), axis=0, keepdims=True)
            turn[2 * p + 1 : 2 * p + 2, :] = jnp.sum(
                jnp.where(before, reach[T:], 0.0), axis=0, keepdims=True
            )
            tail = jnp.exp(last - both)
            dye = dy * jnp.exp(both)
            du_out = tail * bds[:, cols]
            du = du_in + du_out
            gin[:, cols] = (dye * yst[:, cols]).astype(bf16)
            gout[:, cols] = (u * du_out).astype(bf16)
            xdu[:, cols] = (x * du).astype(bf16)
            dyeb[:, cols] = dye.astype(bf16)
            utb[:, cols] = (u * tail).astype(bf16)
            add(CONV + 1, cols, dy * x)
            conv_back(rows, p, dtb * du + chan_ref[1:2, cols] * dy, xc, xs, x)
        d_scores = jnp.where(until, d_scores, 0.0).astype(bf16)
        d_b = mm(d_scores, c_low) + mm(utb[...], ds_low, NT)
        d_c = mm(d_scores, b_low, TN) + mm(dyeb[...], st_ref[sub], NT)
        conv_back(rows, pairs, d_b, b_xc, b_s, b_act)
        conv_back(rows, pairs + 1, d_c, c_xc, c_s, c_act)
        ended = jnp.zeros((1, LANES), f32)
        for p in range(pairs):
            cols = slice(p * LANES, (p + 1) * LANES)
            last = jnp.where(
                low_half[0:1], decay[T - 1 : T, 2 * p : 2 * p + 1], decay[T - 1 : T, 2 * p + 1 : 2 * p + 2]
            )
            fade = jnp.exp(last)
            before_ds = dstate[:, cols]
            through = jnp.sum(before_ds * st_ref[sub, :, cols].astype(f32), axis=0, keepdims=True) * fade
            ended = ended + mm_exact(through, pick_ref[cols, :].astype(f32))
            dstate[:, cols] = fade * before_ds + mm(c_t, dyeb[:, cols])
        gin_heads = mm(gin[...], pick_ref[...])
        gout_heads = mm(gout[...], pick_ref[...])
        reached = (
            turn[...].T
            + mm_exact(upper, gin_heads)
            + mm_exact(strict, gout_heads, TN)
            + ended
        )
        d_raw = (head_ref[1:2, :] * reached + mm(xdu[...], pick_ref[...])) * sigmoid(raw)
        d_ref[rows, wide:] = d_raw.astype(bf16)
        hacc[0] += jnp.sum(d_raw.reshape(T // 8, 8, LANES), axis=0)
        hacc[1] += jnp.sum((dt * reached).reshape(T // 8, 8, LANES), axis=0)
        dxh[T : T + 8, :] = dxh[0:8, :]
        if sub == 1:
            @pl.when(step == 0)
            def _():
                for way in (0, 1):
                    hop(1, way, 0).start()

            ring_poll(1)

    @pl.when(step == steps - 1)
    def _():
        total = lambda a: jnp.sum(a, axis=0, keepdims=True)
        for k in range(CONV + 1):
            small_ref[k : k + 1, :] = total(acc[k])
        small_ref[CONV + 1 : CONV + 2, :width] = total(gate_ref[...])
        small_ref[CONV + 1 : CONV + 2, width : width + LANES] = total(hacc[0])
        small_ref[CONV + 1 : CONV + 2, width + LANES :] = total(hacc[1]) * head_ref[1:2, :]
        small_ref[CONV + 2 :, :] = jnp.zeros((2, wide), f32)
        skip = mm_exact(acc[CONV + 1, :, :width], pick_ref[...].astype(f32))
        small_ref[CONV + 3 : CONV + 4, 512 : 512 + LANES] = total(skip)
        for part in (0, 1):
            over_copy(part).wait_recv()

            def some(i, _, part=part):
                at = span(part * half + i * 32, 32)
                obranch_ref[at, :] = obranch_ref[at, :] + over_slot[part, span(i * 32, 32), :].astype(f32)
                return 0

            lax.fori_loop(0, half // 32, some, 0)
        for part in (0, 1):
            over_copy(part).wait_send()
            for turned in (0, 1):
                near_copy(turned, part).wait_send()
        for h in range(n - 1):
            for k in (0, 1):
                for way in (0, 1):
                    hop(k, way, h).wait_send()


def ssd_backward(n, dy, v, xc, dr, st, gate, taps, head, chan, early, branch):
    length, width = dy.shape
    wide = width + 2 * NS
    steps = length // ROWS
    subs = ROWS // T
    own_rows, tokens = D // n, length // 4
    half = tokens // 2
    row = lambda m: pl.BlockSpec((ROWS, m), lambda i: (steps - 1 - i, 0))
    whole = lambda a: pl.BlockSpec(a.shape, lambda i: (0,) * a.ndim, pipeline_mode=pl.Buffered(1))
    fixed = lambda *shape: pl.BlockSpec(shape, lambda i: (0,) * len(shape))
    anywhere = pl.BlockSpec(memory_space=pl.ANY)
    vm, dma = pltpu.VMEM, pltpu.SemaphoreType.DMA
    return pl.pallas_call(
        functools.partial(backward_body, n, own_rows, tokens, width),
        grid=(steps,),
        in_specs=[
            row(width), row(wide), row(wide), row(LANES),
            pl.BlockSpec((subs, NS, width), lambda i: (steps - 1 - i, 0, 0)),
            whole(gate), whole(taps), whole(head), whole(chan), anywhere, anywhere,
        ],
        out_specs=[
            row(wide + LANES), fixed(8, wide), fixed(own_rows, 2 * width), fixed(tokens, D),
        ],
        out_shape=[
            jax.ShapeDtypeStruct((length, wide + LANES), bf16),
            jax.ShapeDtypeStruct((8, wide), f32),
            jax.ShapeDtypeStruct((own_rows, 2 * width), f32),
            jax.ShapeDtypeStruct((tokens, D), f32),
        ],
        scratch_shapes=[
            vm((T + 8, wide), f32), vm((NS, width), f32), vm((T, width), f32), vm((T, width), f32),
            vm((T, width), bf16), vm((T, width), bf16), vm((T, width), bf16), vm((T, width), bf16),
            vm((T, width), bf16), vm((T, LANES), f32), vm((CONV + 2, 8, wide), f32), vm((2, 8, LANES), f32),
            vm((width, LANES), bf16),
            vm((D, 2 * width), bf16),
            [[vm((n - 1, size, width), bf16) for _ in (0, 1)] for _, size in cut_rows(own_rows)],
            vm((2, 2, half, D), bf16), vm((2, 2, half, D), bf16), vm((2, half, D), bf16),
            dma((5,)), dma((2, 2, n - 1)), dma((2, 2, n - 1)), dma((2, 2)), dma((2, 2)), dma((2,)), dma((2,)),
        ],
        compiler_params=pltpu.CompilerParams(
            collective_id=3, has_side_effects=True, vmem_limit_bytes=ROOM
        ),
        name="layer_backward",
    )(dy, v, xc, dr, st, gate, taps, head, chan, early, branch)


def reduce_body(
    n, rows, tokens, starts,
    xg_ref, d_ref, dz_ref, wp_ref, w_ref, small_ref, flat_ref,
    oxs_ref, oback_ref, bc_ref, oflat_ref,
    xg, d, dz, wz, w, work, grads, slots, staged, near, over, gains, smalls, tens, bc_slot,
    load_sem, ring_send, ring_recv, near_send, near_recv, over_send, over_recv,
    small_send, small_recv, ten_send, ten_recv, bc_send, bc_recv,
):
    pos, ring, me, across, beside = neighbours(n)
    cuts = cut_rows(rows)
    core = lax.rem(me, 2)
    opposite = lax.rem(me + 2, 4)
    next_door = me + 1 - 2 * core
    far = lax.rem(next_door + 2, 4)
    half = tokens // 2
    wide = d.shape[1]
    width = dz.shape[1]
    loads = []
    for k, (src, dst) in enumerate(
        (
            (d_ref, d), (xg_ref, xg), (dz_ref, dz), (w_ref, w), (small_ref, smalls.at[pos]),
            (wp_ref.at[:, pl.ds(0, width)], wz),
        )
    ):
        loads.append(pltpu.make_async_copy(src, dst, load_sem.at[k]))
        loads[-1].start()
    enter((*ring, across, beside))
    started = []

    def go(*args):
        copy = remote(*args)
        copy.start()
        started.append(copy)

    def block_at(way, count):
        return ring_index(lax.rem(pos + (count if way else n - count), n), n)

    def hop(k, way, h):
        lo, hi = starts[k]
        first, size = cuts[way]
        if h == 0:
            src = grads.at[span(block_at(way, 1) * rows + first, size), pl.ds(lo, hi - lo)]
        else:
            src = slots[way][k].at[h - 1]
        return remote(
            src, slots[way][k].at[h], ring_send.at[way, k, h], ring_recv.at[way, k, h], ring[way]
        )

    def product(k):
        lo, hi = starts[k]

        def some(i, _):
            at = pl.ds(pl.multiple_of(i * 2 * LANES, 2 * LANES), 2 * LANES)
            grads[at, lo:hi] = mm(xg[:, at], d[:, lo:hi], TN).astype(bf16)
            return 0

        lax.fori_loop(0, D // (2 * LANES), some, 0)
        for way in (0, 1):
            hop(k, way, 0).start()

    def near_copy(turned, part):
        return remote(
            staged.at[turned, part], near.at[turned, part],
            near_send.at[turned, part], near_recv.at[turned, part], beside,
        )

    def over_copy(part):
        return remote(near.at[0, part], over.at[part], over_send.at[part], over_recv.at[part], across)

    def ring_turn(k, h):
        lo, hi = starts[k]
        for way in (0, 1):
            first, size = cuts[way]
            slot = slots[way][k].at[h]
            remote(slot, slot, ring_send.at[way, k, h], ring_recv.at[way, k, h], ring[way]).wait_recv()
            block = block_at(way, 2 + h) if h < n - 2 else block_at(way, 0)

            tile = strip(size)

            def some(i, _, way=way, first=first, block=block, tile=tile):
                came = slots[way][k][h, span(i * tile, tile), :]
                mine = grads[span(block * rows + first + i * tile, tile), lo:hi]
                if h < n - 2:
                    slots[way][k][h, span(i * tile, tile), :] = came + mine
                else:
                    oxs_ref[span(first + i * tile, tile), lo:hi] = came.astype(f32) + mine.astype(f32)
                return 0

            lax.fori_loop(0, size // tile, some, 0)
            if h < n - 2:
                hop(k, way, h + 1).start()

    def small_hop(way, h):
        here = smalls.at[lax.rem(pos + (h if way else n - h), n)]
        go(here, here, small_send.at[way, h], small_recv.at[way, h], ring[way])

    def small_lands(way, h):
        here = smalls.at[lax.rem(pos + (h + 1 if way else n - h - 1), n)]
        remote(here, here, small_send.at[way, h], small_recv.at[way, h], ring[way]).wait_recv()

    gains[...] = jnp.zeros_like(gains)
    loads[0].wait()
    loads[1].wait()
    product(0)
    product(1)
    for k in (2, 3, 5):
        loads[k].wait()
    turns = {1: [(0, 0), (1, 0)], 2: [(0, 1)], 3: [(1, 1)], 4: [(0, 2)], 5: [(1, 2)], 6: [(0, 3)], 7: [(1, 3)]}
    taken = [sum(k == group for some in turns.values() for k, _ in some) for group in range(len(starts))]

    def block(i, _):
        which, part = lax.div(i, 2), lax.rem(i, 2)
        own = lax.rem(which, 2)
        turned = lax.div(which, 2)
        target = lax.rem(next_door + own * (me - next_door) + 2 * (1 - turned), 4)
        at = span(target * tokens + part * half, half)
        total = mm(dz[at, :], wz[...], NT) + mm(d[at, :], w[...], NT)
        gains[...] += jnp.sum((total * xg[at, :].astype(f32)).reshape(half // 8, 8, D), axis=0)
        work[...] = total

        @pl.when(own == 0)
        def _():
            staged[turned, part] = work[...].astype(bf16)
            near_copy(turned, part).start()

        @pl.when(own == 1)
        def _():
            near_copy(turned, part).wait_recv()

        @pl.when(which == 1)
        def _():
            near[0, part] = (work[...] + near[0, part].astype(f32)).astype(bf16)
            over_copy(part).start()

        @pl.when(which == 3)
        def _():
            oback_ref[span(part * half, half), :] = work[...] + near[1, part].astype(f32)

        for at_block, some in turns.items():

            @pl.when(i == at_block)
            def _(some=some):
                for k, h in some:
                    ring_turn(k, h)

        return 0

    lax.fori_loop(0, 8, block, 0)
    loads[4].wait()
    gain = jnp.sum(gains[...], axis=0, keepdims=True)
    for c in range(D // LANES):
        row, col = 6 + c // 8, (c % 8) * LANES
        smalls[pos, row : row + 1, col : col + LANES] = gain[:, c * LANES : (c + 1) * LANES] / flat_ref[c : c + 1, :]

    rest = [(k, h) for h in range(n - 1) for k in (0, 1) if h >= taken[k]]
    rest.sort(key=lambda turn: turn[1] - taken[turn[0]])

    def small_step(s):
        for way in (0, 1):
            if s > 0 and (way == 0 or s < n // 2):
                small_lands(way, s - 1)
            if s < n // 2 - way:
                small_hop(way, s)

    small_step(0)
    steps_done = 1
    for at, (k, h) in enumerate(rest):
        ring_turn(k, h)
        if (k, h) == (0, n - 2):
            bc_slot[0] = oxs_ref[:, starts[0][0] : starts[0][0] + 2 * NS]
            go(bc_slot.at[0], bc_slot.at[1], bc_send.at[0], bc_recv.at[0], beside)
        if at % 2 == 1 and steps_done < n // 2:
            small_step(steps_done)
            steps_done += 1
    for s in range(steps_done, n // 2):
        small_step(s)
    small_lands(0, n // 2 - 1)

    total = smalls[0]
    for i in range(1, n):
        total = total + smalls[i]
    tens[me] = total
    go(tens.at[me], tens.at[me], ten_send.at[0], ten_recv.at[0], beside)
    remote(bc_slot.at[1], bc_slot.at[1], bc_send.at[0], bc_recv.at[0], beside).wait_recv()
    bc_slot[2] = bc_slot[0] + bc_slot[1]
    go(bc_slot.at[2], bc_slot.at[3], bc_send.at[1], bc_recv.at[1], across)
    here = tens.at[next_door]
    remote(here, here, ten_send.at[0], ten_recv.at[0], beside).wait_recv()
    for k, target in ((0, me), (1, next_door)):
        here = tens.at[target]
        go(here, here, ten_send.at[1 + k], ten_recv.at[1 + k], across)
    for part in (0, 1):
        over_copy(part).wait_recv()

        def some(i, _, part=part):
            at = span(part * half + i * 32, 32)
            oback_ref[at, :] = oback_ref[at, :] + over[part, span(i * 32, 32), :].astype(f32)
            return 0

        lax.fori_loop(0, half // 32, some, 0)
    for k, target in ((0, opposite), (1, far)):
        here = tens.at[target]
        remote(here, here, ten_send.at[1 + k], ten_recv.at[1 + k], across).wait_recv()
    flat_gradients(width, tens, oflat_ref)
    remote(bc_slot.at[3], bc_slot.at[3], bc_send.at[1], bc_recv.at[1], across).wait_recv()
    bc_ref[...] = bc_slot[2] + bc_slot[3]
    for part in (0, 1):
        over_copy(part).wait_send()
        for turned in (0, 1):
            near_copy(turned, part).wait_send()
    for k in range(len(starts)):
        for way in (0, 1):
            for h in range(n - 1):
                hop(k, way, h).wait_send()
    for copy in started:
        copy.wait_send()


def flat_gradients(width, tens, out_ref):
    pairs = width // LANES
    heads = width // P_SIZE

    def sums(row, col):
        total = tens[0, row : row + 1, col : col + LANES]
        for t in range(1, 4):
            total = total + tens[t, row : row + 1, col : col + LANES]
        return total

    def put(row, value):
        out_ref[row : row + 1, :] = value

    for c in range(D // LANES):
        put(c, sums(6 + c // 8, (c % 8) * LANES))
    for t in range(4):
        for c in range(pairs):
            cols = slice(c * LANES, (c + 1) * LANES)
            put(GATE_ROW + pairs * t + c, tens[t, CONV + 1 : CONV + 2, cols])
            put(BIAS_ROW + pairs * t + c, tens[t, CONV : CONV + 1, cols])
            for k in range(CONV):
                put(TAPS_ROW + 4 * pairs * k + pairs * t + c, tens[t, k : k + 1, cols])
    for c in range(2):
        put(BIAS_BC_ROW + c, sums(CONV, width + c * LANES))
        for k in range(CONV):
            put(TAPS_BC_ROW + 2 * k + c, sums(k, width + c * LANES))
    kinds = ((CONV + 1, width), (CONV + 1, width + LANES), (CONV + 3, 512))
    rows = [tens[t, row : row + 1, col : col + LANES] for row, col in kinds for t in range(4)]
    rows = jnp.concatenate(rows + [jnp.zeros((16 - len(rows), LANES), f32)], axis=0)
    lane = lax.broadcasted_iota(jnp.int32, (LANES, 2 * LANES), 1)
    entry = lax.broadcasted_iota(jnp.int32, (LANES, 2 * LANES), 0)
    spread_out = mm_exact(rows, jnp.where(lax.rem(lane, heads) == entry, 1.0, 0.0).astype(f32))
    at = lax.broadcasted_iota(jnp.int32, (16, 2 * LANES), 1)
    source = lax.broadcasted_iota(jnp.int32, (16, 2 * LANES), 0)
    line = jnp.sum(jnp.where(lax.div(at, heads) == source, spread_out, 0.0), axis=0, keepdims=True)
    put(HEAD_ROW, line[:, :LANES])
    put(HEAD_ROW + 1, line[:, LANES:])


def reduce_all(n, xg, d, dz, wp, w, small, flat):
    rows, tokens = D // n, xg.shape[0] // 4
    width, late = dz.shape[1], d.shape[1]
    starts = ((width, late), (0, width))
    half = tokens // 2
    dma, vm = pltpu.SemaphoreType.DMA, pltpu.VMEM
    anywhere = pl.BlockSpec(memory_space=pl.ANY)
    inside = pl.BlockSpec(memory_space=pltpu.VMEM)
    return pl.pallas_call(
        functools.partial(reduce_body, n, rows, tokens, starts),
        in_specs=[anywhere] * 6 + [inside],
        out_specs=[inside] * 4,
        out_shape=[
            jax.ShapeDtypeStruct((rows, late), f32),
            jax.ShapeDtypeStruct((tokens, D), f32),
            jax.ShapeDtypeStruct((rows, 2 * NS), f32),
            jax.ShapeDtypeStruct((FLAT_ROWS, LANES), f32),
        ],
        scratch_shapes=[
            vm(xg.shape, bf16), vm(d.shape, bf16), vm(dz.shape, bf16), vm((D, width), bf16), vm(w.shape, bf16),
            vm((half, D), f32), vm((D, late), bf16),
            [[vm((n - 1, size, hi - lo), bf16) for lo, hi in starts] for _, size in cut_rows(rows)],
            vm((2, 2, half, D), bf16), vm((2, 2, half, D), bf16), vm((2, half, D), bf16), vm((8, D), f32),
            vm((n, *small.shape), f32), vm((4, *small.shape), f32), vm((4, rows, 2 * NS), f32),
            dma((6,)), dma((2, 2, n - 1)), dma((2, 2, n - 1)), dma((2, 2)), dma((2, 2)), dma((2,)), dma((2,)),
            dma((2, n // 2)), dma((2, n // 2)), dma((3,)), dma((3,)), dma((2,)), dma((2,)),
        ],
        compiler_params=pltpu.CompilerParams(
            collective_id=1, has_side_effects=True, vmem_limit_bytes=ROOM
        ),
        name="reduce_all",
    )(xg, d, dz, wp, w, small, flat)


def adamw_step(weight, first, second, grad, rate, decay):
    first_new = beta_first * first + (1.0 - beta_first) * grad
    second_new = beta_second * second + (1.0 - beta_second) * grad * grad
    hat_first = first_new / (1.0 - beta_first**STEP)
    hat_second = second_new / (1.0 - beta_second**STEP)
    weight_new = weight - rate * (hat_first / (jnp.sqrt(hat_second) + adam_eps) + decay * weight)
    return (weight_new, first_new, second_new)


def finish_body(
    width, heads,
    in_ref, cot_ref, branch_ref, back_ref, flat_ref, early_ref, late_ref, bcg_ref,
    zx_ref, zx1_ref, zx2_ref, bc_ref, bc1_ref, bc2_ref, out_ref, out1_ref, out2_ref, late_all_ref, dt_ref, dt1_ref, dt2_ref,
    layer_ref, grad_ref, zxn_ref, zx1n_ref, zx2n_ref, bcn_ref, bc1n_ref, bc2n_ref,
    outn_ref, out1n_ref, out2n_ref, dtn_ref, dt1n_ref, dt2n_ref,
    both,
):
    def update(refs, news, grad):
        fresh = adamw_step(*(ref[...] for ref in refs), grad, matrix_rate, matrix_decay)
        for ref, value in zip(news, fresh):
            ref[...] = value

    both[:, 0, :] = early_ref[:, :width]
    both[:, 1, :] = late_ref[:, :width]
    update((zx_ref, zx1_ref, zx2_ref), (zxn_ref, zx1n_ref, zx2n_ref), both[...])
    update((bc_ref, bc1_ref, bc2_ref), (bcn_ref, bc1n_ref, bc2n_ref), bcg_ref[...])
    update((out_ref, out1_ref, out2_ref), (outn_ref, out1n_ref, out2n_ref), early_ref[:, width:])

    @pl.when(pl.program_id(0) == 0)
    def _():
        unit = jnp.where(
            lax.broadcasted_iota(jnp.int32, (16, LANES), 0) == lax.broadcasted_iota(jnp.int32, (16, LANES), 1), 1.0, 0.0
        ).astype(f32)
        turned = mm_exact(unit, late_all_ref[:, width + 2 * NS :], NT)
        update((dt_ref, dt1_ref, dt2_ref), (dtn_ref, dt1n_ref, dt2n_ref), turned[:heads])

    rows = in_ref.shape[0]
    tile = 64

    def some(i, _):
        at = span(i * tile, tile)
        squares = jnp.zeros((tile, LANES), f32)
        inner = jnp.zeros((tile, LANES), f32)
        for c in range(D // LANES):
            cols = slice(c * LANES, (c + 1) * LANES)
            x = in_ref[at, cols].astype(f32)
            squares = squares + x * x
            inner = inner + x * flat_ref[c : c + 1, :] * back_ref[at, cols]
        r = lax.rsqrt(jnp.sum(squares, axis=-1, keepdims=True) / D + norm_eps)
        k = r * r * r * jnp.sum(inner, axis=-1, keepdims=True) / D
        r, k = jnp.broadcast_to(r, (tile, LANES)), jnp.broadcast_to(k, (tile, LANES))
        for c in range(D // LANES):
            cols = slice(c * LANES, (c + 1) * LANES)
            x = in_ref[at, cols].astype(f32)
            layer_ref[at, cols] = (x + branch_ref[at, cols]).astype(bf16)
            grad_ref[at, cols] = cot_ref[at, cols].astype(f32) + r * flat_ref[c : c + 1, :] * back_ref[at, cols] - x * k
        return 0

    lax.fori_loop(0, rows // tile, some, 0)


def finish(layer_input, out_grad, branch, back, flat, early, late, bcg, zx, bc, out, dt):
    tokens, (rows, _, width), heads = layer_input.shape[0], zx[0].shape, dt[0].shape[0]
    steps = 4 if rows % 32 == 0 else 2
    part = lambda a: pl.BlockSpec((a.shape[0] // steps, *a.shape[1:]), lambda i: (i,) + (0,) * (a.ndim - 1))
    whole = lambda a: pl.BlockSpec(a.shape, lambda i: (0,) * a.ndim)
    like = lambda a, dtype=f32: jax.ShapeDtypeStruct(a.shape, dtype)
    weights = (*zx, *bc, *out)
    return pl.pallas_call(
        functools.partial(finish_body, width, heads),
        grid=(steps,),
        in_specs=[
            *(part(a) for a in (layer_input, out_grad, branch, back)), whole(flat),
            *(part(a) for a in (early, late, bcg, *weights)), whole(late), *(whole(a) for a in dt),
        ],
        out_specs=[part(layer_input), part(back), *(part(a) for a in weights), *(whole(a) for a in dt)],
        out_shape=[like(layer_input, bf16), like(back), *(like(a) for a in weights), *(like(a) for a in dt)],
        scratch_shapes=[pltpu.VMEM((rows // steps, 2, width), f32)],
        compiler_params=pltpu.CompilerParams(vmem_limit_bytes=ROOM),
        name="finish",
    )(layer_input, out_grad, branch, back, flat, early, late, bcg, *weights, late, *dt)


def local(
    layer_input,
    out_grad,
    small_params,
    small_first,
    small_second,
    w_zx,
    zx_first,
    zx_second,
    w_bc,
    bc_first,
    bc_second,
    w_dt,
    dt_first,
    dt_second,
    w_out,
    out_first,
    out_second,
):
    n = lax.axis_size("dp")
    flat = jnp.pad(small_params, (0, FLAT_ROWS * LANES - small_params.shape[0])).reshape(FLAT_ROWS, LANES)
    xg, w_all, w_pair = gather_all(n, layer_input, flat, w_zx, w_bc, w_dt.T, w_out)
    z, v, xc, dr, y, dn, st, red, cot_all, pair_all, taps, head, chan = ssd_forward(
        n, xg, w_all, flat, out_grad, w_pair
    )
    dy, dz, branch, early, gate = early_gradients(z, y, dn, red, pair_all, chan, xg, cot_all)
    d_late, small, owner_early, own_branch = ssd_backward(
        n, dy, v, xc, dr, st, gate, taps, head, chan, early, branch
    )
    owner_late, d_normed_in, owner_bc, flat_grad = reduce_all(
        n, xg, d_late, dz, pair_all, w_all, small, flat
    )
    small_grad = flat_grad.reshape(-1)[: small_params.shape[0]]
    small_new, small_first_new, small_second_new = adamw_step(
        small_params, small_first, small_second, small_grad, small_rate, 0.0
    )
    (
        layer_output, input_grad, zx_new, zx_first_new, zx_second_new, bc_new, bc_first_new, bc_second_new,
        out_new, out_first_new, out_second_new, dt_new, dt_first_new, dt_second_new,
    ) = finish(
        layer_input, out_grad, own_branch, d_normed_in, flat, owner_early, owner_late, owner_bc,
        (w_zx, zx_first, zx_second), (w_bc, bc_first, bc_second), (w_out, out_first, out_second),
        (w_dt.T, dt_first.T, dt_second.T),
    )
    dt_new, dt_first_new, dt_second_new = dt_new.T, dt_first_new.T, dt_second_new.T
    return (
        layer_output,
        input_grad,
        small_new,
        small_first_new,
        small_second_new,
        zx_new,
        zx_first_new,
        zx_second_new,
        bc_new,
        bc_first_new,
        bc_second_new,
        dt_new,
        dt_first_new,
        dt_second_new,
        out_new,
        out_first_new,
        out_second_new,
    )


def solution(mesh):
    return jax.shard_map(
        local,
        mesh=mesh,
        in_specs=(
            P(("dp", "tensor"), None),
            P(("dp", "tensor"), None),
            P(),
            P(),
            P(),
            P("dp", None, "tensor"),
            P("dp", None, "tensor"),
            P("dp", None, "tensor"),
            P("dp", None),
            P("dp", None),
            P("dp", None),
            P("dp", "tensor"),
            P("dp", "tensor"),
            P("dp", "tensor"),
            P("dp", "tensor"),
            P("dp", "tensor"),
            P("dp", "tensor"),
        ),
        out_specs=(
            P(("dp", "tensor"), None),
            P(("dp", "tensor"), None),
            P(),
            P(),
            P(),
            P("dp", None, "tensor"),
            P("dp", None, "tensor"),
            P("dp", None, "tensor"),
            P("dp", None),
            P("dp", None),
            P("dp", None),
            P("dp", "tensor"),
            P("dp", "tensor"),
            P("dp", "tensor"),
            P("dp", "tensor"),
            P("dp", "tensor"),
            P("dp", "tensor"),
        ),
        check_vma=False,
    )
```

```python
import functools

import jax
import jax.numpy as jnp
from jax import lax
from jax.experimental import pallas as pl
from jax.experimental.pallas import tpu as pltpu
from jax.sharding import PartitionSpec as P

D = 1536
DI = 3072
H = 48
NS = 128
P_SIZE = 64
CONV = 4
LEN = 2048
STEP = 10

T = 128
ROWS = 256
LANES = 128
ROOM = 60 * 2**20
Z_EARLY = 256

norm_eps = 1e-05
adam_eps = 1e-08
beta_first = 0.9
beta_second = 0.95
matrix_rate = 0.01
small_rate = 0.1
matrix_decay = 0.1

f32 = jnp.float32
bf16 = jnp.bfloat16
NN = (((1,), (0,)), ((), ()))
NT = (((1,), (1,)), ((), ()))
TN = (((0,), (0,)), ((), ()))
HIGHEST = lax.Precision.HIGHEST


GATE_ROW, TAPS_ROW, BIAS_ROW, TAPS_BC_ROW, BIAS_BC_ROW, HEAD_ROW, FLAT_ROWS = 12, 36, 132, 156, 164, 166, 168


def mm(a, b, dims=NN):
    return lax.dot_general(a, b, dims, preferred_element_type=f32)


def mm_exact(a, b, dims=NN):
    return lax.dot_general(a, b, dims, preferred_element_type=f32, precision=HIGHEST)


def sigmoid(v):
    return 0.5 * jnp.tanh(0.5 * v) + 0.5


def softplus(v):
    return jnp.maximum(v, 0.0) + jnp.log1p(jnp.exp(-jnp.abs(v)))


def spread(col):
    return jnp.broadcast_to(col, (T, LANES))


def block_iota(axis):
    return lax.broadcasted_iota(jnp.int32, (T, LANES), axis)


def head_rows(dr_ref, head_ref, rows):
    raw = dr_ref[rows, :] + head_ref[0:1, :]
    dt = softplus(raw)
    low_tri = jnp.where(block_iota(0) >= block_iota(1), 1.0, 0.0).astype(f32)
    decay = mm_exact(low_tri, dt * head_ref[1:2, :])
    return raw, dt, decay


def ring_place(n):
    me = lax.axis_index("dp")
    z, x = lax.div(me, 2), lax.rem(me, 2)
    return z + x * (n - 1 - 2 * z)


def ring_index(pos, n):
    back = lax.div(pos, n // 2)
    return 2 * pos + back * (2 * n - 1 - 4 * pos)


def neighbours(n):
    pos = ring_place(n)
    right = ring_index(lax.rem(pos + 1, n), n)
    left = ring_index(lax.rem(pos + n - 1, n), n)
    me = lax.axis_index("tensor")
    y, core = lax.div(me, 2), lax.rem(me, 2)
    across = 2 * (1 - y) + core
    beside = 2 * y + 1 - core
    return pos, ({"dp": right}, {"dp": left}), me, {"tensor": across}, {"tensor": beside}


def greet(peers):
    barrier = pltpu.get_barrier_semaphore()
    for peer in peers:
        pl.semaphore_signal(barrier, inc=1, device_id=peer, device_id_type=pl.DeviceIdType.MESH)


def enter(peers):
    greet(peers)
    pl.semaphore_wait(pltpu.get_barrier_semaphore(), len(peers))


def remote(src, dst, send_sem, recv_sem, peer):
    return pltpu.make_async_remote_copy(
        src_ref=src, dst_ref=dst, send_sem=send_sem, recv_sem=recv_sem,
        device_id=peer, device_id_type=pl.DeviceIdType.MESH,
    )


def span(start, size):
    return pl.ds(pl.multiple_of(start, 16), size)


def strip(rows):
    return next(size for size in (48, 32, 16) if rows % size == 0)


def cut_rows(rows):
    top = rows // 32 * 16
    return ((0, top), (top, rows - top))


def forward_body(
    n, rows, tokens, width,
    xg_ref, tall_ref, w_ref, flat_ref, cot_ref, wp_ref,
    z_ref, v_ref, xc_ref, dr_ref, y_ref, dn_ref, st_ref, red_ref, cots_ref, wps_ref, taps_ref, head_ref, chan_ref,
    halo, state, y_all, cots, wps, sums,
    own_keep, ring_keep, over_keep, side_keep, pass_keep, ring_send, ring_recv, over_send, over_recv,
    side_send, side_recv, pass_send, pass_recv, sum_send, sum_recv,
):
    pairs = width // LANES
    wide = width + 2 * NS
    step = pl.program_id(0)
    steps = LEN // ROWS
    tall = 2 * ROWS
    gating, norming = steps, steps + LEN // tall
    last_step = norming + LEN // tall - 1
    pos, ring, me, across, beside = neighbours(n)
    opposite = lax.rem(me + 2, 4)
    next_door = me + 1 - 2 * lax.rem(me, 2)
    far = lax.rem(next_door + 2, 4)
    askew = {"tensor": far}
    half = tokens // 2
    hops = n // 2
    cuts = cut_rows(rows)
    mine = ring_index(pos, n)

    parts_of = ((0, width), (width, width - Z_EARLY))

    def hop(k, part, way, h):
        first, size = cuts[part]
        cols = pl.ds(*parts_of[k])
        block = ring_index(lax.rem(pos + (h if way else n - h), n), n)
        here = wps.at[span(block * rows + first, size), cols]
        src = wp_ref.at[pl.ds(first, size), cols] if h == 0 else here
        return remote(src, here, ring_send.at[way, part, k, h], ring_recv.at[way, part, k, h], ring[way])

    def hop_lands(k, part, way, h):
        first, size = cuts[part]
        block = ring_index(lax.rem(pos + (h + 1 if way else n - h - 1), n), n)
        return span(block * rows + first, size), pl.ds(*parts_of[k])

    def hop_arrival(k, part, way, h):
        here = wps.at[hop_lands(k, part, way, h)]
        return remote(here, here, ring_send.at[way, part, k, h], ring_recv.at[way, part, k, h], ring[way])

    def hop_keep(k, part, way, h):
        at = hop_lands(k, part, way, h)
        return pltpu.make_async_copy(wps.at[at], wps_ref.at[at], ring_keep.at[way, part, k, h])

    def hop_ways(h):
        return [(part, way) for part in (0, 1) for way in (0, 1) if h < hops - 1 or part == way]

    def hop_on(k, h):
        for part, way in hop_ways(h - 1) if h > 0 else ():
            hop_arrival(k, part, way, h - 1).wait_recv()
            hop_keep(k, part, way, h - 1).start()
            if h < hops and (part, way) in hop_ways(h):
                hop(k, part, way, h).start()
        if h == 0:
            for part, way in hop_ways(0):
                hop(k, part, way, 0).start()

    def over(k):
        return remote(
            cot_ref.at[pl.ds(k * half, half)], cots.at[span(me * tokens + k * half, half)],
            over_send.at[k], over_recv.at[k], across,
        )

    def landed(full, start, size, send, recv, peer):
        here = full.at[span(start, size)]
        return remote(here, here, send, recv, peer)

    def over_arrival(k):
        start = opposite * tokens + k * half
        return landed(cots, start, half, over_send.at[k], over_recv.at[k], across)

    def passing(k):
        start = opposite * tokens + k * half
        return landed(cots, start, half, pass_send.at[k], pass_recv.at[k], beside)

    def pass_arrival(k):
        return landed(cots, far * tokens + k * half, half, pass_send.at[k], pass_recv.at[k], beside)

    def side():
        return remote(cot_ref, cots.at[span(me * tokens, tokens)], side_send.at[0], side_recv.at[0], beside)

    def side_arrival():
        return landed(cots, next_door * tokens, tokens, side_send.at[0], side_recv.at[0], beside)

    def keep(start, size, sem):
        return pltpu.make_async_copy(cots.at[span(start, size)], cots_ref.at[span(start, size)], sem)

    def own_keeps():
        return (
            pltpu.make_async_copy(cot_ref, cots_ref.at[span(me * tokens, tokens)], own_keep.at[0]),
            pltpu.make_async_copy(wp_ref, wps_ref.at[span(mine * rows, rows)], own_keep.at[1]),
            pltpu.make_async_copy(cot_ref, cots.at[span(me * tokens, tokens)], own_keep.at[2]),
            pltpu.make_async_copy(wp_ref, wps.at[span(mine * rows, rows)], own_keep.at[3]),
        )

    @pl.when(step == 0)
    def _():
        enter((*ring, across, beside, askew))
        hop_on(0, 0)
        over(0).start()
        over(1).start()
        side().start()
        for copy in own_keeps():
            copy.start()
        halo[0:8, :] = jnp.zeros((8, wide), f32)
        state[...] = jnp.zeros_like(state)
        parameter_rows(me, width, flat_ref, taps_ref, head_ref, chan_ref)

    for h in range(1, hops):
        pl.when(step == min(2 * h, gating))(functools.partial(hop_on, 0, h))
    for h in range(hops):
        pl.when(step == min(2 * h + 1, gating))(functools.partial(hop_on, 1, h))
    for k in (1, 0):
        pl.when(step == gating)(functools.partial(hop_on, k, hops))

    @pl.when(step == gating)
    def _():
        for k in (0, 1):
            over_arrival(k).wait_recv()
            passing(k).start()
            keep(opposite * tokens + k * half, half, over_keep.at[k]).start()
        for copy in own_keeps():
            copy.wait()

    @pl.when(step == norming)
    def _():
        side_arrival().wait_recv()
        keep(next_door * tokens, tokens, side_keep.at[0]).start()
        for k in (0, 1):
            pass_arrival(k).wait_recv()
            keep(far * tokens + k * half, half, pass_keep.at[k]).start()

    @pl.when(step < gating)
    def _():
        scan_step(
            width, step, xg_ref, w_ref, taps_ref, head_ref, chan_ref,
            v_ref, xc_ref, dr_ref, y_ref, st_ref, halo, state, y_all,
        )

    def token_sum(row, first, value):
        lanes = pl.ds(pl.multiple_of(first, tall), tall)
        sums[me, row : row + 4, lanes] = mm_exact(jnp.ones((8, LANES), f32), value, NT)[0:4]

    @pl.when((step >= gating) & (step < norming))
    def _():
        first = (step - gating) * tall
        z_ref[:, :Z_EARLY] = mm(tall_ref[...], w_ref[:, wide + LANES :])
        z_ref[:, Z_EARLY:] = mm(tall_ref[...], wps[:, width:])
        squares = jnp.zeros((tall, LANES), f32)
        for p in range(pairs):
            cols = slice(p * LANES, (p + 1) * LANES)
            z = z_ref[:, cols]
            gated = y_all[span(first, tall), cols] * (z * sigmoid(z))
            y_all[span(first, tall), cols] = gated
            squares = squares + gated * gated
        token_sum(0, first, squares)

    @pl.when(step >= norming)
    def _():
        first = (step - norming) * tall
        dn_ref[...] = mm(cots[span(first, tall), :], wps[:, :width])
        inner = jnp.zeros((tall, LANES), f32)
        for p in range(pairs):
            cols = slice(p * LANES, (p + 1) * LANES)
            inner = inner + y_all[span(first, tall), cols] * chan_ref[0:1, cols] * dn_ref[:, cols]
        token_sum(4, first, inner)

    @pl.when(step == last_step)
    def _():
        peers = ((beside, next_door), (across, opposite), (askew, far))
        for k, (peer, _) in enumerate(peers):
            remote(sums.at[me], sums.at[me], sum_send.at[k], sum_recv.at[k], peer).start()
        for h in range(hops):
            for part, way in hop_ways(h):
                for k in (0, 1):
                    hop(k, part, way, h).wait_send()
                    hop_keep(k, part, way, h).wait()
        side().wait_send()
        keep(next_door * tokens, tokens, side_keep.at[0]).wait()
        for k in (0, 1):
            over(k).wait_send()
            passing(k).wait_send()
            keep(opposite * tokens + k * half, half, over_keep.at[k]).wait()
            keep(far * tokens + k * half, half, pass_keep.at[k]).wait()
        for k, (peer, other) in enumerate(peers):
            remote(sums.at[other], sums.at[other], sum_send.at[k], sum_recv.at[k], peer).wait()
        red_ref[...] = ((sums[0] + sums[1]) + sums[2]) + sums[3]


def parameter_rows(me, width, flat_ref, taps_ref, head_ref, chan_ref):
    pairs = width // LANES
    heads = width // P_SIZE
    taps_ref[...] = jnp.zeros_like(taps_ref)
    chan_ref[...] = jnp.zeros_like(chan_ref)
    for c in range(pairs):
        cols = slice(c * LANES, (c + 1) * LANES)
        chan_ref[0:1, cols] = flat_ref[pl.ds(GATE_ROW + pairs * me + c, 1), :]
        taps_ref[CONV : CONV + 1, cols] = flat_ref[pl.ds(BIAS_ROW + pairs * me + c, 1), :]
        for k in range(CONV):
            taps_ref[k : k + 1, cols] = flat_ref[pl.ds(TAPS_ROW + 4 * pairs * k + pairs * me + c, 1), :]
    for c in range(2):
        cols = slice(width + c * LANES, width + (c + 1) * LANES)
        taps_ref[CONV : CONV + 1, cols] = flat_ref[BIAS_BC_ROW + c : BIAS_BC_ROW + c + 1, :]
        for k in range(CONV):
            row = TAPS_BC_ROW + 2 * k + c
            taps_ref[k : k + 1, cols] = flat_ref[row : row + 1, :]
    both = jnp.concatenate([flat_ref[HEAD_ROW : HEAD_ROW + 1, :], flat_ref[HEAD_ROW + 1 : HEAD_ROW + 2, :]], axis=1)
    both = jnp.broadcast_to(both, (8, 2 * LANES))
    lane = lax.broadcasted_iota(jnp.int32, (2 * LANES, LANES), 0)
    head = lax.broadcasted_iota(jnp.int32, (2 * LANES, LANES), 1)

    def take(kind):
        match = (lane == 4 * heads * kind + heads * me + head) & (head < heads)
        return mm_exact(both, jnp.where(match, 1.0, 0.0).astype(f32))

    valid = lax.broadcasted_iota(jnp.int32, (8, LANES), 1) < heads
    row = lax.broadcasted_iota(jnp.int32, (8, LANES), 0)
    rates = jnp.where(valid, -jnp.exp(take(1)), 0.0)
    head_ref[...] = jnp.where(row == 0, take(0), jnp.where(row == 1, rates, 0.0))
    skip = mm_exact(take(2), picked(width).astype(f32), NT)
    chan_ref[1:2, :] = skip[0:1]


def picked(width):
    channel = lax.broadcasted_iota(jnp.int32, (width, LANES), 0)
    head = lax.broadcasted_iota(jnp.int32, (width, LANES), 1)
    return jnp.where((channel >= head * P_SIZE) & (channel < (head + 1) * P_SIZE), 1.0, 0.0).astype(bf16)


def scan_step(
    width, step, xg_ref, w_ref, taps_ref, head_ref, chan_ref,
    v_ref, xc_ref, dr_ref, y_ref, st_ref, halo, state, y_all,
):
    pairs = width // LANES
    wide = width + 2 * NS
    dr_ref[...] = mm(xg_ref[...], w_ref[:, wide : wide + LANES])
    halo[8 : 8 + ROWS, :] = mm(xg_ref[...], w_ref[:, :wide])
    low_half = block_iota(1) < P_SIZE
    causal = block_iota(0) >= block_iota(1)

    def convolved(sub, block):
        cols = slice(block * LANES, (block + 1) * LANES)
        total = taps_ref[CONV : CONV + 1, cols]
        for k in range(CONV):
            first = 8 - (CONV - 1) + k + sub * T
            total = total + taps_ref[k : k + 1, cols] * halo[first : first + T, cols]
        rows = slice(sub * T, (sub + 1) * T)
        xc_ref[rows, cols] = total
        v_ref[rows, cols] = halo[8 + sub * T : 8 + (sub + 1) * T, cols].astype(bf16)
        return total * sigmoid(total)

    for sub in range(ROWS // T):
        rows = slice(sub * T, (sub + 1) * T)
        raw, dt, decay = head_rows(dr_ref, head_ref, rows)
        decay_t = decay.T
        b_low = convolved(sub, pairs).astype(bf16)
        c_low = convolved(sub, pairs + 1).astype(bf16)
        b_t = b_low.T
        scores = jnp.where(causal, mm(c_low, b_low, NT), 0.0)
        st_ref[sub] = state[...].astype(bf16)
        for p in range(pairs):
            cols = slice(p * LANES, (p + 1) * LANES)
            x = convolved(sub, p)
            l1, l2 = spread(decay[:, 2 * p : 2 * p + 1]), spread(decay[:, 2 * p + 1 : 2 * p + 2])
            both = jnp.where(low_half, l1, l2)
            dtb = jnp.where(
                low_half, spread(dt[:, 2 * p : 2 * p + 1]), spread(dt[:, 2 * p + 1 : 2 * p + 2])
            )
            u = x * dtb
            m1 = scores * jnp.exp(jnp.minimum(l1 - decay_t[2 * p : 2 * p + 1, :], 0.0))
            m2 = scores * jnp.exp(jnp.minimum(l2 - decay_t[2 * p + 1 : 2 * p + 2, :], 0.0))
            mixing = jnp.concatenate([m1.astype(bf16), m2.astype(bf16)], axis=1)
            parts = jnp.concatenate(
                [jnp.where(low_half, u, 0.0).astype(bf16), jnp.where(low_half, 0.0, u).astype(bf16)],
                axis=0,
            )
            last = both[T - 1 : T, :]
            entering = st_ref[sub, :, cols]
            y = mm(mixing, parts) + jnp.exp(both) * mm(c_low, entering) + chan_ref[1:2, cols] * x
            tail = (u * jnp.exp(last - both)).astype(bf16)
            state[:, cols] = jnp.exp(last) * state[:, cols] + mm(b_t, tail)
            y_ref[rows, cols] = y
            y_all[span(step * ROWS + sub * T, T), cols] = y
    halo[0:8, :] = halo[ROWS : ROWS + 8, :]


def ssd_forward(n, xg, w, flat, cot, wp):
    length = xg.shape[0]
    rows, width = wp.shape[0], (wp.shape[1] + Z_EARLY) // 2
    tokens = cot.shape[0]
    wide = width + 2 * NS
    steps = length // ROWS
    tall = 2 * ROWS
    more = length // tall
    subs = ROWS // T
    assert length == LEN
    early = lambda i: jnp.minimum(i, steps - 1)
    middle = lambda i: jnp.clip(i - steps, 0, more - 1)
    row = lambda m: pl.BlockSpec((ROWS, m), lambda i: (early(i), 0))
    whole = lambda a: pl.BlockSpec(a.shape, lambda i: (0,) * a.ndim, pipeline_mode=pl.Buffered(1))
    anywhere = pl.BlockSpec(memory_space=pl.ANY)
    vm, dma = pltpu.VMEM, pltpu.SemaphoreType.DMA
    hops = dma((2, 2, 2, n // 2))
    return pl.pallas_call(
        functools.partial(forward_body, n, rows, tokens, width),
        grid=(steps + 2 * more,),
        in_specs=[
            row(D), pl.BlockSpec((tall, D), lambda i: (middle(i), 0)),
            whole(w), whole(flat), whole(cot), whole(wp),
        ],
        out_specs=[
            pl.BlockSpec((tall, width), lambda i: (middle(i), 0)),
            row(wide), row(wide), row(LANES), row(width),
            pl.BlockSpec((tall, width), lambda i: (jnp.maximum(i - steps - more, 0), 0)),
            pl.BlockSpec((subs, NS, width), lambda i: (early(i), 0, 0)),
            pl.BlockSpec((8, length), lambda i: (0, 0)),
            anywhere, anywhere,
            *(pl.BlockSpec((8, m), lambda i: (0, 0)) for m in (wide, LANES, width)),
        ],
        out_shape=[
            jax.ShapeDtypeStruct((length, width), f32),
            jax.ShapeDtypeStruct((length, wide), bf16),
            jax.ShapeDtypeStruct((length, wide), f32),
            jax.ShapeDtypeStruct((length, LANES), f32),
            jax.ShapeDtypeStruct((length, width), f32),
            jax.ShapeDtypeStruct((length, width), f32),
            jax.ShapeDtypeStruct((length // T, NS, width), bf16),
            jax.ShapeDtypeStruct((8, length), f32),
            jax.ShapeDtypeStruct((4 * tokens, D), bf16),
            jax.ShapeDtypeStruct((n * rows, 2 * width - Z_EARLY), bf16),
            *(jax.ShapeDtypeStruct((8, m), f32) for m in (wide, LANES, width)),
        ],
        scratch_shapes=[
            vm((ROWS + 8, wide), f32), vm((NS, width), f32), vm((length, width), f32),
            vm((4 * tokens, D), bf16), vm((n * rows, 2 * width - Z_EARLY), bf16), vm((4, 8, length), f32),
            dma((4,)), hops, dma((2,)), dma((1,)), dma((2,)), hops, hops, dma((2,)), dma((2,)),
            dma((1,)), dma((1,)), dma((2,)), dma((2,)), dma((3,)), dma((3,)),
        ],
        compiler_params=pltpu.CompilerParams(collective_id=2, has_side_effects=True, vmem_limit_bytes=ROOM),
        name="layer_forward",
    )(xg, xg, w, flat, cot, wp)


def gather_body(
    n, rows, tokens,
    in_ref, flat_ref, wzx_ref, wbc_ref, wdt_ref, wout_ref, xg_ref, xt_ref, ws_ref, wp_ref, x_ref, w_ref, xg, xt, ws,
    keep_sem, turn_sem, ring_keep, ring_send, ring_recv, over_send, over_recv, side_send, side_recv, pass_send, pass_recv,
):
    pos, ring, me, across, beside = neighbours(n)
    greet((*ring, across, beside))
    quarter = tokens // 4
    width = wout_ref.shape[1]
    heads = wdt_ref.shape[0]
    late = width + 2 * NS + LANES
    w_ref[:, :width] = wzx_ref[:, 1, :].astype(bf16)
    w_ref[:, width : width + 2 * NS] = wbc_ref[...].astype(bf16)
    unit = jnp.where(
        lax.broadcasted_iota(jnp.int32, (16, LANES), 0) == lax.broadcasted_iota(jnp.int32, (16, LANES), 1), 1.0, 0.0
    ).astype(bf16)
    steps_w = jnp.concatenate([wdt_ref[...], jnp.zeros((16 - heads, rows), f32)], axis=0).astype(bf16)
    w_ref[:, width + 2 * NS : late] = mm(steps_w, unit, TN).astype(bf16)
    w_ref[:, late:] = wzx_ref[:, 0, :Z_EARLY].astype(bf16)

    def normalize(k):
        def some(i, _):
            at = span(k * quarter + i * 64, 64)
            squares = jnp.zeros((64, LANES), f32)
            for c in range(D // LANES):
                x = in_ref[at, c * LANES : (c + 1) * LANES].astype(f32)
                squares = squares + x * x
            inverse = lax.rsqrt(jnp.sum(squares, axis=-1, keepdims=True) / D + norm_eps)
            inverse = jnp.broadcast_to(inverse, (64, LANES))
            for c in range(D // LANES):
                cols = slice(c * LANES, (c + 1) * LANES)
                x_ref[at, cols] = (in_ref[at, cols].astype(f32) * inverse * flat_ref[c : c + 1, :]).astype(bf16)
            return 0

        lax.fori_loop(0, quarter // 64, some, 0)

    normalize(0)
    pl.semaphore_wait(pltpu.get_barrier_semaphore(), 4)
    started, kept = [], []

    def go(*args):
        copy = remote(*args)
        copy.start()
        started.append(copy)
        return copy

    def keep(src, dst, sem):
        copy = pltpu.make_async_copy(src, dst, sem)
        copy.start()
        kept.append(copy)

    opposite = lax.rem(me + 2, 4)
    next_door = me + 1 - 2 * lax.rem(me, 2)
    far = lax.rem(next_door + 2, 4)
    cuts = cut_rows(rows)

    def turned(src, start, first, size):
        sets = D // (4 * LANES)

        def some(i, _):
            row = first + lax.div(i, sets) * LANES
            at = span(row if src is x_ref else start + row, LANES)
            to = pl.ds(pl.multiple_of(start + row, LANES), LANES)
            for c in range(4):
                cols = pl.ds(pl.multiple_of((lax.rem(i, sets) * 4 + c) * LANES, LANES), LANES)
                xt[cols, to] = src[at, cols].T
            return 0

        lax.fori_loop(0, size // LANES * sets, some, 0)

    def keep_turned(k, block):
        at = pl.ds(pl.multiple_of(block * tokens, LANES), tokens)
        keep(xt.at[:, at], xt_ref.at[:, at], turn_sem.at[k])

    def arrived(part, way, step, block):
        first, size = cuts[part]
        at = span(block * rows + first, size)
        remote(
            ws.at[at], ws.at[at], ring_send.at[way, part, step], ring_recv.at[way, part, step], ring[way]
        ).wait_recv()
        keep(ws.at[at], ws_ref.at[at], ring_keep.at[way, part, step])

    def ring_step(step, parts=(0, 1)):
        last = step == n // 2 - 1
        for part in parts:
            first, size = cuts[part]
            for way in (0, 1):
                block = ring_index(lax.rem(pos + (step if way else n - step), n), n)
                here = ws.at[span(block * rows + first, size)]
                if step > 0:
                    arrived(part, way, step - 1, block)
                if last and part != way:
                    continue
                src = w_ref.at[pl.ds(first, size)] if step == 0 else here
                go(src, here, ring_send.at[way, part, step], ring_recv.at[way, part, step], ring[way])

    def send_over(k):
        go(
            x_ref.at[pl.ds(k * quarter, quarter)], xg.at[span(me * tokens + k * quarter, quarter)],
            over_send.at[k], over_recv.at[k], across,
        )

    def pass_on(k):
        at = span(opposite * tokens + k * quarter, quarter)
        here = xg.at[at]
        remote(here, here, over_send.at[k], over_recv.at[k], across).wait_recv()
        go(here, here, pass_send.at[k], pass_recv.at[k], beside)
        keep(here, xg_ref.at[at], keep_sem.at[k])

    def pass_lands(k):
        at = span(far * tokens + k * quarter, quarter)
        remote(xg.at[at], xg.at[at], pass_send.at[k], pass_recv.at[k], beside).wait_recv()
        keep(xg.at[at], xg_ref.at[at], keep_sem.at[4 + k])
        turned(xg, far * tokens, k * quarter, quarter)

    ring_step(0, (0,))
    leading = list(started)
    send_over(0)
    normalize(1)
    send_over(1)
    normalize(2)
    normalize(3)
    go(x_ref, xg.at[span(me * tokens, tokens)], side_send.at[0], side_recv.at[0], beside)
    wp_ref[:, :width] = wout_ref[...].astype(bf16)
    wp_ref[:, width:] = wzx_ref[:, 0, Z_EARLY:].astype(bf16)
    for copy in leading:
        copy.wait_send()
        started.remove(copy)
    ring_step(0, (1,))
    mine = ring_index(pos, n)
    keep(x_ref, xg_ref.at[span(me * tokens, tokens)], keep_sem.at[8])
    keep(w_ref, ws_ref.at[span(mine * rows, rows)], keep_sem.at[9])
    turned(x_ref, me * tokens, 0, tokens)
    keep_turned(0, me)
    ring_step(1)
    send_over(2)
    at = span(next_door * tokens, tokens)
    remote(xg.at[at], xg.at[at], side_send.at[0], side_recv.at[0], beside).wait_recv()
    keep(xg.at[at], xg_ref.at[at], keep_sem.at[10])
    turned(xg, next_door * tokens, 0, tokens)
    keep_turned(1, next_door)
    send_over(3)
    for step in range(2, n // 2):
        ring_step(step)
        if step == 2:
            pass_on(0)
            pass_on(1)
            turned(xg, opposite * tokens, 0, 2 * quarter)
    pass_on(2)
    pass_lands(0)
    pass_lands(1)
    pass_on(3)
    turned(xg, opposite * tokens, 2 * quarter, 2 * quarter)
    keep_turned(2, opposite)
    for part in (0, 1):
        arrived(part, part, n // 2 - 1, ring_index(lax.rem(pos + n // 2, n), n))
    pass_lands(2)
    pass_lands(3)
    keep_turned(3, far)
    for copy in kept:
        copy.wait()
    for copy in started:
        copy.wait_send()


def gather_all(n, layer_input, flat, w_zx, w_bc, w_dt, w_out):
    tokens, rows, width = layer_input.shape[0], w_bc.shape[0], w_out.shape[1]
    early = width + 2 * NS + LANES + Z_EARLY
    dma = pltpu.SemaphoreType.DMA
    anywhere = pl.BlockSpec(memory_space=pl.ANY)
    inside = pl.BlockSpec(memory_space=pltpu.VMEM)
    own = ((tokens, D), (rows, early))
    full = ((4 * tokens, D), (D, 4 * tokens), (n * rows, early))
    hops = dma((2, 2, n // 2))
    return pl.pallas_call(
        functools.partial(gather_body, n, rows, tokens),
        in_specs=[inside] * 6,
        out_specs=[anywhere, anywhere, anywhere, inside],
        out_shape=[jax.ShapeDtypeStruct(shape, bf16) for shape in (*full, (rows, 2 * width - Z_EARLY))],
        scratch_shapes=[
            *(pltpu.VMEM(shape, bf16) for shape in (*own, *full)),
            dma((11,)), dma((4,)), hops, hops, hops, dma((4,)), dma((4,)), dma((1,)), dma((1,)), dma((4,)), dma((4,)),
        ],
        compiler_params=pltpu.CompilerParams(collective_id=0, has_side_effects=True, vmem_limit_bytes=ROOM),
        name="gather_all",
    )(layer_input, flat, w_zx, w_bc, w_dt, w_out)


def gradient_body(
    width,
    z_ref, y_ref, dn_ref, red_ref, wo_ref, chan_ref, xt_ref, cot_ref,
    dy_ref, dz_ref, branch_ref, early_ref, gate_ref,
    nl, dz_all, fresh, hold,
):
    step = pl.program_id(0)
    steps = LEN // ROWS
    slab = D // (width // LANES)

    def multiply(p):
        at = slice(p * slab, (p + 1) * slab)
        branch_ref[:, at] = mm(hold[...], wo_ref[at, :], NT).astype(bf16)

    @pl.when(step == 0)
    def _():
        gate_ref[...] = jnp.zeros_like(gate_ref)
        hold[...] = jnp.zeros_like(hold)

    @pl.when(step < steps)
    def _():
        q_row = lax.rsqrt(red_ref[0:4, :] / DI + norm_eps)
        k_row = q_row * q_row * q_row * red_ref[4:8, :] / DI
        turned = jnp.concatenate([q_row, k_row], axis=0).T
        for p in range(width // LANES):
            cols = slice(p * LANES, (p + 1) * LANES)
            multiply(p)
            for sub in range(ROWS // T):
                rows = slice(sub * T, (sub + 1) * T)
                q, kk = spread(turned[rows, 0:1]), spread(turned[rows, 4:5])
                z, y, dn = z_ref[rows, cols], y_ref[rows, cols], dn_ref[rows, cols]
                gain = chan_ref[0:1, cols]
                s = sigmoid(z)
                sz = z * s
                gated = y * sz
                gq = gated * q
                dg = q * gain * dn - gated * kk
                gate_ref[:, cols] += jnp.sum((gq * dn).reshape(T // 8, 8, LANES), axis=0)
                fresh[rows, cols] = (gq * gain).astype(bf16)
                dz_ref[rows, cols] = (dg * y * (s + sz * (1.0 - s))).astype(bf16)
                dy_ref[rows, cols] = dg * sz
        at = span(step * ROWS, ROWS)
        hold[...] = fresh[...]
        nl[at, :] = fresh[...]
        dz_all[at, :] = dz_ref[...]

    @pl.when(step == steps)
    def _():
        for p in range(width // LANES):
            multiply(p)

    @pl.when(step >= steps)
    def _():
        early_ref[:, :width] = mm(xt_ref[...], dz_all[...]).astype(bf16)
        early_ref[:, width:] = mm(cot_ref[...], nl[...], TN).astype(bf16)


def early_gradients(z, y, dn, red, wp, chan, xt, cot):
    length, width = z.shape
    steps = length // ROWS
    deep = 2 * LANES
    early = lambda i: jnp.minimum(i, steps - 1)
    late = lambda i: jnp.maximum(i - steps, 0)
    row = lambda m: pl.BlockSpec((ROWS, m), lambda i: (early(i), 0))
    column = pl.BlockSpec((length, deep), lambda i: (0, late(i)))
    whole = lambda a: pl.BlockSpec(a.shape, lambda i: (0,) * a.ndim, pipeline_mode=pl.Buffered(1))
    return pl.pallas_call(
        functools.partial(gradient_body, width),
        grid=(steps + D // deep,),
        in_specs=[
            row(width), row(width), row(width), pl.BlockSpec((8, ROWS), lambda i: (0, early(i))),
            pl.BlockSpec((D, width), lambda i: (0, 0), pipeline_mode=pl.Buffered(1)),
            whole(chan), pl.BlockSpec((deep, length), lambda i: (late(i), 0)), column,
        ],
        out_specs=[
            row(width), row(width), pl.BlockSpec((ROWS, D), lambda i: (jnp.clip(i - 1, 0, steps - 1), 0)),
            pl.BlockSpec((deep, 2 * width), lambda i: (late(i), 0)),
            pl.BlockSpec((8, width), lambda i: (0, 0)),
        ],
        out_shape=[
            jax.ShapeDtypeStruct((length, width), f32),
            jax.ShapeDtypeStruct((length, width), bf16),
            jax.ShapeDtypeStruct((length, D), bf16),
            jax.ShapeDtypeStruct((D, 2 * width), bf16),
            jax.ShapeDtypeStruct((8, width), f32),
        ],
        scratch_shapes=[pltpu.VMEM((rows, width), bf16) for rows in (length, length, ROWS, ROWS)],
        compiler_params=pltpu.CompilerParams(vmem_limit_bytes=ROOM),
        name="early_gradients",
    )(z, y, dn, red, wp, chan, xt, cot)


def backward_body(
    n, own_rows, tokens, width,
    dy_ref, v_ref, xc_ref, dr_ref, st_ref, gate_ref, taps_ref, head_ref, chan_ref, early_ref, branch_ref,
    d_ref, small_ref, oearly_ref, obranch_ref,
    dxh, dstate, yst, bds, dyeb, utb, gin, gout, xdu, turn, acc, hacc, pick_ref,
    own, slots, near, held, over_slot,
    load_sem, ring_send, ring_recv, near_send, near_recv, over_send, over_recv,
):
    pairs = width // LANES
    wide = width + 2 * NS
    step = pl.program_id(0)
    steps = LEN // ROWS
    pos, ring, me, across, beside = neighbours(n)
    opposite = lax.rem(me + 2, 4)
    next_door = me + 1 - 2 * lax.rem(me, 2)
    far = lax.rem(next_door + 2, 4)
    half = tokens // 2
    cuts = cut_rows(own_rows)

    def block_at(way, count):
        return ring_index(lax.rem(pos + (count if way else n - count), n), n)

    def hop(k, way, h):
        first, size = cuts[way]
        if h == 0:
            src = early_ref.at[span(block_at(way, 1) * own_rows + first, size), pl.ds(k * width, width)]
        else:
            src = slots[way][k].at[h - 1]
        return remote(
            src, slots[way][k].at[h], ring_send.at[way, k, h], ring_recv.at[way, k, h], ring[way]
        )

    def near_copy(turned, part):
        start = (next_door if turned else far) * tokens + part * half
        return remote(
            branch_ref.at[span(start, half)], near.at[turned, part],
            near_send.at[turned, part], near_recv.at[turned, part], beside,
        )

    def held_copy(turned, part):
        start = (me if turned else opposite) * tokens + part * half
        return pltpu.make_async_copy(
            branch_ref.at[span(start, half)], held.at[turned, part], load_sem.at[2 * turned + part]
        )

    def over_copy(part):
        return remote(held.at[0, part], over_slot.at[part], over_send.at[part], over_recv.at[part], across)

    def own_copy():
        return pltpu.make_async_copy(early_ref, own, load_sem.at[4])

    def ring_turn(k, h):
        for way in (0, 1):
            first, size = cuts[way]
            hop(k, way, h).wait_recv()
            block = block_at(way, 2 + h) if h < n - 2 else block_at(way, 0)

            tile = strip(size)

            def some(i, _, way=way, first=first, block=block, tile=tile):
                cols = slice(k * width, (k + 1) * width)
                came = slots[way][k][h, span(i * tile, tile), :]
                mine = own[span(block * own_rows + first + i * tile, tile), cols]
                if h < n - 2:
                    slots[way][k][h, span(i * tile, tile), :] = came + mine
                else:
                    oearly_ref[span(first + i * tile, tile), cols] = came.astype(f32) + mine.astype(f32)
                return 0

            lax.fori_loop(0, size // tile, some, 0)
            if h < n - 2:
                hop(k, way, h + 1).start()

    def ring_poll(k):
        for h in range(n - 1):
            pl.when(step == min(h + 1, steps - 1))(functools.partial(ring_turn, k, h))

    def add_near(turned):
        for part in (0, 1):
            held_copy(turned, part).wait()
            near_copy(turned, part).wait_recv()

            def some(i, _, part=part):
                at = span(i * 32, 32)
                if turned:
                    total = held[1, part, at, :].astype(f32) + near[1, part, at, :].astype(f32)
                    obranch_ref[span(part * half + i * 32, 32), :] = total
                else:
                    held[0, part, at, :] = held[0, part, at, :] + near[0, part, at, :]
                return 0

            lax.fori_loop(0, half // 32, some, 0)
            if not turned:
                over_copy(part).start()

    @pl.when(step == 0)
    def _():
        enter((*ring, across, beside))
        for way in (0, 1):
            hop(0, way, 0).start()
        for turned in (0, 1):
            for part in (0, 1):
                near_copy(turned, part).start()
                held_copy(turned, part).start()
        own_copy().start()
        dxh[T : T + 8, :] = jnp.zeros((8, wide), f32)
        dstate[...] = jnp.zeros_like(dstate)
        acc[...] = jnp.zeros_like(acc)
        hacc[...] = jnp.zeros_like(hacc)
        turn[...] = jnp.zeros_like(turn)
        pick_ref[...] = picked(width)

    @pl.when(step == 1)
    def _():
        own_copy().wait()
        add_near(0)

    pl.when(step == 2)(functools.partial(add_near, 1))
    ring_poll(0)

    low_half = block_iota(1) < P_SIZE
    row_at, col_at = block_iota(0), block_iota(1)
    until = row_at <= col_at
    before = row_at < col_at
    upper = jnp.where(until, 1.0, 0.0).astype(f32)
    strict = jnp.where(before, 1.0, 0.0).astype(f32)
    low_tri = jnp.where(row_at >= col_at, 1.0, 0.0).astype(bf16)

    def add(index, cols, value):
        acc[index, :, cols] += jnp.sum(value.reshape(T // 8, 8, LANES), axis=0)

    def conv_back(rows, block, d_act, xc, s, act):
        cols = slice(block * LANES, (block + 1) * LANES)
        dxh[0:T, cols] = d_act * (s + act * (1.0 - s))
        v = v_ref[rows, cols].astype(f32)
        total = None
        for m in range(CONV):
            moved = dxh[m : m + T, cols]
            if m == 0:
                add(CONV, cols, moved)
            add(CONV - 1 - m, cols, v * moved)
            term = taps_ref[CONV - 1 - m : CONV - m, cols] * moved
            total = term if total is None else total + term
        d_ref[rows, cols] = total.astype(bf16)

    for sub in reversed(range(ROWS // T)):
        rows = slice(sub * T, (sub + 1) * T)
        raw, dt, decay = head_rows(dr_ref, head_ref, rows)
        decay_t = decay.T
        b_cols = slice(width, width + NS)
        c_cols = slice(width + NS, width + 2 * NS)
        b_xc, c_xc = xc_ref[rows, b_cols], xc_ref[rows, c_cols]
        b_s, c_s = sigmoid(b_xc), sigmoid(c_xc)
        b_act, c_act = b_xc * b_s, c_xc * c_s
        b_low, c_low = b_act.astype(bf16), c_act.astype(bf16)
        c_t = c_low.T
        scores_t = jnp.where(until, mm(b_low, c_low, NT), 0.0)
        ds_low = dstate[...].astype(bf16)
        yst[...] = mm(c_low, st_ref[sub])
        bds[...] = mm(b_low, ds_low)
        d_scores = jnp.zeros((T, LANES), f32)
        for p in range(pairs):
            cols = slice(p * LANES, (p + 1) * LANES)
            dy = dy_ref[rows, cols]
            xc = xc_ref[rows, cols]
            xs = sigmoid(xc)
            x = xc * xs
            l1, l2 = spread(decay[:, 2 * p : 2 * p + 1]), spread(decay[:, 2 * p + 1 : 2 * p + 2])
            both = jnp.where(low_half, l1, l2)
            dtb = jnp.where(
                low_half, spread(dt[:, 2 * p : 2 * p + 1]), spread(dt[:, 2 * p + 1 : 2 * p + 2])
            )
            u = x * dtb
            last = both[T - 1 : T, :]
            e1 = jnp.exp(jnp.minimum(decay_t[2 * p : 2 * p + 1, :] - l1, 0.0))
            e2 = jnp.exp(jnp.minimum(decay_t[2 * p + 1 : 2 * p + 2, :] - l2, 0.0))
            dy_low = dy.astype(bf16)
            zero = jnp.zeros_like(dy_low)
            u_low = u.astype(bf16)
            du_in = mm(
                jnp.concatenate([(scores_t * e1).astype(bf16), (scores_t * e2).astype(bf16)], axis=1),
                jnp.concatenate(
                    [jnp.where(low_half, dy_low, zero), jnp.where(low_half, zero, dy_low)], axis=0
                ),
            )
            d_mix = mm(
                jnp.concatenate(
                    [jnp.where(low_half, u_low, zero), jnp.where(low_half, zero, u_low)], axis=0
                ),
                dy_low,
                NT,
            )
            d1, d2 = d_mix[:T] * e1, d_mix[T:] * e2
            d_scores = d_scores + d1 + d2
            reach = mm(
                jnp.concatenate([(d1 * scores_t).astype(bf16), (d2 * scores_t).astype(bf16)], axis=0),
                low_tri,
            )
            turn[2 * p : 2 * p + 1, :] = jnp.sum(jnp.where(before, reach[:T], 0.0), axis=0, keepdims=True)
            turn[2 * p + 1 : 2 * p + 2, :] = jnp.sum(
                jnp.where(before, reach[T:], 0.0), axis=0, keepdims=True
            )
            tail = jnp.exp(last - both)
            dye = dy * jnp.exp(both)
            du_out = tail * bds[:, cols]
            du = du_in + du_out
            gin[:, cols] = (dye * yst[:, cols]).astype(bf16)
            gout[:, cols] = (u * du_out).astype(bf16)
            xdu[:, cols] = (x * du).astype(bf16)
            dyeb[:, cols] = dye.astype(bf16)
            utb[:, cols] = (u * tail).astype(bf16)
            add(CONV + 1, cols, dy * x)
            conv_back(rows, p, dtb * du + chan_ref[1:2, cols] * dy, xc, xs, x)
        d_scores = jnp.where(until, d_scores, 0.0).astype(bf16)
        d_b = mm(d_scores, c_low) + mm(utb[...], ds_low, NT)
        d_c = mm(d_scores, b_low, TN) + mm(dyeb[...], st_ref[sub], NT)
        conv_back(rows, pairs, d_b, b_xc, b_s, b_act)
        conv_back(rows, pairs + 1, d_c, c_xc, c_s, c_act)
        ended = jnp.zeros((1, LANES), f32)
        for p in range(pairs):
            cols = slice(p * LANES, (p + 1) * LANES)
            last = jnp.where(
                low_half[0:1], decay[T - 1 : T, 2 * p : 2 * p + 1], decay[T - 1 : T, 2 * p + 1 : 2 * p + 2]
            )
            fade = jnp.exp(last)
            before_ds = dstate[:, cols]
            through = jnp.sum(before_ds * st_ref[sub, :, cols].astype(f32), axis=0, keepdims=True) * fade
            ended = ended + mm_exact(through, pick_ref[cols, :].astype(f32))
            dstate[:, cols] = fade * before_ds + mm(c_t, dyeb[:, cols])
        gin_heads = mm(gin[...], pick_ref[...])
        gout_heads = mm(gout[...], pick_ref[...])
        reached = (
            turn[...].T
            + mm_exact(upper, gin_heads)
            + mm_exact(strict, gout_heads, TN)
            + ended
        )
        d_raw = (head_ref[1:2, :] * reached + mm(xdu[...], pick_ref[...])) * sigmoid(raw)
        d_ref[rows, wide:] = d_raw.astype(bf16)
        hacc[0] += jnp.sum(d_raw.reshape(T // 8, 8, LANES), axis=0)
        hacc[1] += jnp.sum((dt * reached).reshape(T // 8, 8, LANES), axis=0)
        dxh[T : T + 8, :] = dxh[0:8, :]
        if sub == 1:
            @pl.when(step == 0)
            def _():
                for way in (0, 1):
                    hop(1, way, 0).start()

            ring_poll(1)

    @pl.when(step == steps - 1)
    def _():
        total = lambda a: jnp.sum(a, axis=0, keepdims=True)
        for k in range(CONV + 1):
            small_ref[k : k + 1, :] = total(acc[k])
        small_ref[CONV + 1 : CONV + 2, :width] = total(gate_ref[...])
        small_ref[CONV + 1 : CONV + 2, width : width + LANES] = total(hacc[0])
        small_ref[CONV + 1 : CONV + 2, width + LANES :] = total(hacc[1]) * head_ref[1:2, :]
        small_ref[CONV + 2 :, :] = jnp.zeros((2, wide), f32)
        skip = mm_exact(acc[CONV + 1, :, :width], pick_ref[...].astype(f32))
        small_ref[CONV + 3 : CONV + 4, 512 : 512 + LANES] = total(skip)
        for part in (0, 1):
            over_copy(part).wait_recv()

            def some(i, _, part=part):
                at = span(part * half + i * 32, 32)
                obranch_ref[at, :] = obranch_ref[at, :] + over_slot[part, span(i * 32, 32), :].astype(f32)
                return 0

            lax.fori_loop(0, half // 32, some, 0)
        for part in (0, 1):
            over_copy(part).wait_send()
            for turned in (0, 1):
                near_copy(turned, part).wait_send()
        for h in range(n - 1):
            for k in (0, 1):
                for way in (0, 1):
                    hop(k, way, h).wait_send()


def ssd_backward(n, dy, v, xc, dr, st, gate, taps, head, chan, early, branch):
    length, width = dy.shape
    wide = width + 2 * NS
    steps = length // ROWS
    subs = ROWS // T
    own_rows, tokens = D // n, length // 4
    half = tokens // 2
    row = lambda m: pl.BlockSpec((ROWS, m), lambda i: (steps - 1 - i, 0))
    whole = lambda a: pl.BlockSpec(a.shape, lambda i: (0,) * a.ndim, pipeline_mode=pl.Buffered(1))
    fixed = lambda *shape: pl.BlockSpec(shape, lambda i: (0,) * len(shape))
    anywhere = pl.BlockSpec(memory_space=pl.ANY)
    vm, dma = pltpu.VMEM, pltpu.SemaphoreType.DMA
    return pl.pallas_call(
        functools.partial(backward_body, n, own_rows, tokens, width),
        grid=(steps,),
        in_specs=[
            row(width), row(wide), row(wide), row(LANES),
            pl.BlockSpec((subs, NS, width), lambda i: (steps - 1 - i, 0, 0)),
            whole(gate), whole(taps), whole(head), whole(chan), anywhere, anywhere,
        ],
        out_specs=[
            row(wide + LANES), fixed(8, wide), fixed(own_rows, 2 * width), fixed(tokens, D),
        ],
        out_shape=[
            jax.ShapeDtypeStruct((length, wide + LANES), bf16),
            jax.ShapeDtypeStruct((8, wide), f32),
            jax.ShapeDtypeStruct((own_rows, 2 * width), f32),
            jax.ShapeDtypeStruct((tokens, D), f32),
        ],
        scratch_shapes=[
            vm((T + 8, wide), f32), vm((NS, width), f32), vm((T, width), f32), vm((T, width), f32),
            vm((T, width), bf16), vm((T, width), bf16), vm((T, width), bf16), vm((T, width), bf16),
            vm((T, width), bf16), vm((T, LANES), f32), vm((CONV + 2, 8, wide), f32), vm((2, 8, LANES), f32),
            vm((width, LANES), bf16),
            vm((D, 2 * width), bf16),
            [[vm((n - 1, size, width), bf16) for _ in (0, 1)] for _, size in cut_rows(own_rows)],
            vm((2, 2, half, D), bf16), vm((2, 2, half, D), bf16), vm((2, half, D), bf16),
            dma((5,)), dma((2, 2, n - 1)), dma((2, 2, n - 1)), dma((2, 2)), dma((2, 2)), dma((2,)), dma((2,)),
        ],
        compiler_params=pltpu.CompilerParams(
            collective_id=3, has_side_effects=True, vmem_limit_bytes=ROOM
        ),
        name="layer_backward",
    )(dy, v, xc, dr, st, gate, taps, head, chan, early, branch)


def reduce_body(
    n, rows, tokens, starts,
    xg_ref, xt_ref, d_ref, dz_ref, wp_ref, w_ref, small_ref, flat_ref,
    oxs_ref, oback_ref, bc_ref, oflat_ref,
    xg, xt, d, dz, wz, w, work, grads, slots, staged, near, over, gains, smalls, tens, bc_slot,
    load_sem, ring_send, ring_recv, near_send, near_recv, over_send, over_recv,
    small_send, small_recv, ten_send, ten_recv, bc_send, bc_recv,
):
    pos, ring, me, across, beside = neighbours(n)
    cuts = cut_rows(rows)
    core = lax.rem(me, 2)
    opposite = lax.rem(me + 2, 4)
    next_door = me + 1 - 2 * core
    far = lax.rem(next_door + 2, 4)
    half = tokens // 2
    late = d.shape[1]
    width = dz.shape[1]
    loads = []
    rest_of_z = width - Z_EARLY
    for k, (src, dst) in enumerate(
        (
            (d_ref, d), (xt_ref, xt), (dz_ref, dz), (w_ref.at[:, pl.ds(0, late)], w),
            (w_ref.at[:, pl.ds(late, Z_EARLY)], wz.at[:, pl.ds(0, Z_EARLY)]),
            (wp_ref.at[:, pl.ds(width, rest_of_z)], wz.at[:, pl.ds(Z_EARLY, rest_of_z)]),
            (xg_ref, xg), (small_ref, smalls.at[pos]),
        )
    ):
        loads.append(pltpu.make_async_copy(src, dst, load_sem.at[k]))
        loads[-1].start()
    enter((*ring, across, beside))
    started = []

    def go(*args):
        copy = remote(*args)
        copy.start()
        started.append(copy)

    def block_at(way, count):
        return ring_index(lax.rem(pos + (count if way else n - count), n), n)

    def hop(k, way, h):
        lo, hi = starts[k]
        first, size = cuts[way]
        if h == 0:
            src = grads.at[span(block_at(way, 1) * rows + first, size), pl.ds(lo, hi - lo)]
        else:
            src = slots[way][k].at[h - 1]
        return remote(
            src, slots[way][k].at[h], ring_send.at[way, k, h], ring_recv.at[way, k, h], ring[way]
        )

    def product(k):
        lo, hi = starts[k]

        def some(i, _):
            at = pl.ds(pl.multiple_of(i * 2 * LANES, 2 * LANES), 2 * LANES)
            grads[at, lo:hi] = mm(xt[at, :], d[:, lo:hi]).astype(bf16)
            return 0

        lax.fori_loop(0, D // (2 * LANES), some, 0)
        for way in (0, 1):
            hop(k, way, 0).start()

    def near_copy(turned, part):
        return remote(
            staged.at[turned, part], near.at[turned, part],
            near_send.at[turned, part], near_recv.at[turned, part], beside,
        )

    def over_copy(part):
        return remote(near.at[0, part], over.at[part], over_send.at[part], over_recv.at[part], across)

    def ring_turn(k, h):
        lo, hi = starts[k]
        for way in (0, 1):
            first, size = cuts[way]
            slot = slots[way][k].at[h]
            remote(slot, slot, ring_send.at[way, k, h], ring_recv.at[way, k, h], ring[way]).wait_recv()
            block = block_at(way, 2 + h) if h < n - 2 else block_at(way, 0)

            tile = strip(size)

            def some(i, _, way=way, first=first, block=block, tile=tile):
                came = slots[way][k][h, span(i * tile, tile), :]
                mine = grads[span(block * rows + first + i * tile, tile), lo:hi]
                if h < n - 2:
                    slots[way][k][h, span(i * tile, tile), :] = came + mine
                else:
                    oxs_ref[span(first + i * tile, tile), lo:hi] = came.astype(f32) + mine.astype(f32)
                return 0

            lax.fori_loop(0, size // tile, some, 0)
            if h < n - 2:
                hop(k, way, h + 1).start()

    def small_hop(way, h):
        here = smalls.at[lax.rem(pos + (h if way else n - h), n)]
        go(here, here, small_send.at[way, h], small_recv.at[way, h], ring[way])

    def small_lands(way, h):
        here = smalls.at[lax.rem(pos + (h + 1 if way else n - h - 1), n)]
        remote(here, here, small_send.at[way, h], small_recv.at[way, h], ring[way]).wait_recv()

    gains[...] = jnp.zeros_like(gains)
    loads[0].wait()
    loads[1].wait()
    product(0)
    for k in (2, 3, 4, 5, 6):
        loads[k].wait()
    turns = {1: [(0, 0)], 2: [(0, 1), (1, 0)], 3: [(2, 0)], 4: [(0, 2), (1, 1)], 5: [(2, 1)], 6: [(0, 3), (1, 2)], 7: [(2, 2)]}
    taken = [sum(k == group for some in turns.values() for k, _ in some) for group in range(len(starts))]

    def block(i, _):
        @pl.when(i == 2)
        def _():
            product(1)
            product(2)

        which, part = lax.div(i, 2), lax.rem(i, 2)
        own = lax.rem(which, 2)
        turned = lax.div(which, 2)
        target = lax.rem(next_door + own * (me - next_door) + 2 * (1 - turned), 4)
        at = span(target * tokens + part * half, half)
        total = mm(dz[at, :], wz[...], NT) + mm(d[at, :], w[...], NT)
        gains[...] += jnp.sum((total * xg[at, :].astype(f32)).reshape(half // 8, 8, D), axis=0)
        work[...] = total

        @pl.when(own == 0)
        def _():
            staged[turned, part] = work[...].astype(bf16)
            near_copy(turned, part).start()

        @pl.when(own == 1)
        def _():
            near_copy(turned, part).wait_recv()

        @pl.when(which == 1)
        def _():
            near[0, part] = (work[...] + near[0, part].astype(f32)).astype(bf16)
            over_copy(part).start()

        @pl.when(which == 3)
        def _():
            oback_ref[span(part * half, half), :] = work[...] + near[1, part].astype(f32)

        for at_block, some in turns.items():

            @pl.when(i == at_block)
            def _(some=some):
                for k, h in some:
                    ring_turn(k, h)

        return 0

    lax.fori_loop(0, 8, block, 0)
    loads[7].wait()
    gain = jnp.sum(gains[...], axis=0, keepdims=True)
    for c in range(D // LANES):
        row, col = 6 + c // 8, (c % 8) * LANES
        smalls[pos, row : row + 1, col : col + LANES] = gain[:, c * LANES : (c + 1) * LANES] / flat_ref[c : c + 1, :]

    rest = [(k, h) for h in range(n - 1) for k in (0, 1, 2) if h >= taken[k]]
    rest.sort(key=lambda turn: turn[1] - taken[turn[0]])

    def small_step(s):
        for way in (0, 1):
            if s > 0 and (way == 0 or s < n // 2):
                small_lands(way, s - 1)
            if s < n // 2 - way:
                small_hop(way, s)

    small_step(0)
    steps_done = 1
    for at, (k, h) in enumerate(rest):
        ring_turn(k, h)
        if (k, h) == (0, n - 2):
            bc_slot[0] = oxs_ref[:, starts[0][0] : starts[0][0] + 2 * NS]
            go(bc_slot.at[0], bc_slot.at[1], bc_send.at[0], bc_recv.at[0], beside)
        if at % 2 == 1 and steps_done < n // 2:
            small_step(steps_done)
            steps_done += 1
    for s in range(steps_done, n // 2):
        small_step(s)
    small_lands(0, n // 2 - 1)

    total = smalls[0]
    for i in range(1, n):
        total = total + smalls[i]
    tens[me] = total
    go(tens.at[me], tens.at[me], ten_send.at[0], ten_recv.at[0], beside)
    remote(bc_slot.at[1], bc_slot.at[1], bc_send.at[0], bc_recv.at[0], beside).wait_recv()
    bc_slot[2] = bc_slot[0] + bc_slot[1]
    go(bc_slot.at[2], bc_slot.at[3], bc_send.at[1], bc_recv.at[1], across)
    here = tens.at[next_door]
    remote(here, here, ten_send.at[0], ten_recv.at[0], beside).wait_recv()
    for k, target in ((0, me), (1, next_door)):
        here = tens.at[target]
        go(here, here, ten_send.at[1 + k], ten_recv.at[1 + k], across)
    for part in (0, 1):
        over_copy(part).wait_recv()

        def some(i, _, part=part):
            at = span(part * half + i * 32, 32)
            oback_ref[at, :] = oback_ref[at, :] + over[part, span(i * 32, 32), :].astype(f32)
            return 0

        lax.fori_loop(0, half // 32, some, 0)
    for k, target in ((0, opposite), (1, far)):
        here = tens.at[target]
        remote(here, here, ten_send.at[1 + k], ten_recv.at[1 + k], across).wait_recv()
    flat_gradients(width, tens, oflat_ref)
    remote(bc_slot.at[3], bc_slot.at[3], bc_send.at[1], bc_recv.at[1], across).wait_recv()
    bc_ref[...] = bc_slot[2] + bc_slot[3]
    for part in (0, 1):
        over_copy(part).wait_send()
        for turned in (0, 1):
            near_copy(turned, part).wait_send()
    for k in range(len(starts)):
        for way in (0, 1):
            for h in range(n - 1):
                hop(k, way, h).wait_send()
    for copy in started:
        copy.wait_send()


def flat_gradients(width, tens, out_ref):
    pairs = width // LANES
    heads = width // P_SIZE

    def sums(row, col):
        total = tens[0, row : row + 1, col : col + LANES]
        for t in range(1, 4):
            total = total + tens[t, row : row + 1, col : col + LANES]
        return total

    def put(row, value):
        out_ref[row : row + 1, :] = value

    for c in range(D // LANES):
        put(c, sums(6 + c // 8, (c % 8) * LANES))
    for t in range(4):
        for c in range(pairs):
            cols = slice(c * LANES, (c + 1) * LANES)
            put(GATE_ROW + pairs * t + c, tens[t, CONV + 1 : CONV + 2, cols])
            put(BIAS_ROW + pairs * t + c, tens[t, CONV : CONV + 1, cols])
            for k in range(CONV):
                put(TAPS_ROW + 4 * pairs * k + pairs * t + c, tens[t, k : k + 1, cols])
    for c in range(2):
        put(BIAS_BC_ROW + c, sums(CONV, width + c * LANES))
        for k in range(CONV):
            put(TAPS_BC_ROW + 2 * k + c, sums(k, width + c * LANES))
    kinds = ((CONV + 1, width), (CONV + 1, width + LANES), (CONV + 3, 512))
    rows = [tens[t, row : row + 1, col : col + LANES] for row, col in kinds for t in range(4)]
    rows = jnp.concatenate(rows + [jnp.zeros((16 - len(rows), LANES), f32)], axis=0)
    lane = lax.broadcasted_iota(jnp.int32, (LANES, 2 * LANES), 1)
    entry = lax.broadcasted_iota(jnp.int32, (LANES, 2 * LANES), 0)
    spread_out = mm_exact(rows, jnp.where(lax.rem(lane, heads) == entry, 1.0, 0.0).astype(f32))
    at = lax.broadcasted_iota(jnp.int32, (16, 2 * LANES), 1)
    source = lax.broadcasted_iota(jnp.int32, (16, 2 * LANES), 0)
    line = jnp.sum(jnp.where(lax.div(at, heads) == source, spread_out, 0.0), axis=0, keepdims=True)
    put(HEAD_ROW, line[:, :LANES])
    put(HEAD_ROW + 1, line[:, LANES:])


def reduce_all(n, xg, xt, d, dz, wp, w, small, flat):
    rows, tokens = D // n, xg.shape[0] // 4
    width, late = dz.shape[1], d.shape[1]
    starts = ((width, late), (0, width // 2), (width // 2, width))
    half = tokens // 2
    dma, vm = pltpu.SemaphoreType.DMA, pltpu.VMEM
    anywhere = pl.BlockSpec(memory_space=pl.ANY)
    inside = pl.BlockSpec(memory_space=pltpu.VMEM)
    return pl.pallas_call(
        functools.partial(reduce_body, n, rows, tokens, starts),
        in_specs=[anywhere] * 7 + [inside],
        out_specs=[inside] * 4,
        out_shape=[
            jax.ShapeDtypeStruct((rows, late), f32),
            jax.ShapeDtypeStruct((tokens, D), f32),
            jax.ShapeDtypeStruct((rows, 2 * NS), f32),
            jax.ShapeDtypeStruct((FLAT_ROWS, LANES), f32),
        ],
        scratch_shapes=[
            vm(xg.shape, bf16), vm(xt.shape, bf16), vm(d.shape, bf16), vm(dz.shape, bf16), vm((D, width), bf16),
            vm((D, late), bf16),
            vm((half, D), f32), vm((D, late), bf16),
            [[vm((n - 1, size, hi - lo), bf16) for lo, hi in starts] for _, size in cut_rows(rows)],
            vm((2, 2, half, D), bf16), vm((2, 2, half, D), bf16), vm((2, half, D), bf16), vm((8, D), f32),
            vm((n, *small.shape), f32), vm((4, *small.shape), f32), vm((4, rows, 2 * NS), f32),
            dma((8,)), dma((2, 3, n - 1)), dma((2, 3, n - 1)), dma((2, 2)), dma((2, 2)), dma((2,)), dma((2,)),
            dma((2, n // 2)), dma((2, n // 2)), dma((3,)), dma((3,)), dma((2,)), dma((2,)),
        ],
        compiler_params=pltpu.CompilerParams(
            collective_id=1, has_side_effects=True, vmem_limit_bytes=ROOM
        ),
        name="reduce_all",
    )(xg, xt, d, dz, wp, w, small, flat)


def adamw_step(weight, first, second, grad, rate, decay):
    first_new = beta_first * first + (1.0 - beta_first) * grad
    second_new = beta_second * second + (1.0 - beta_second) * grad * grad
    hat_first = first_new / (1.0 - beta_first**STEP)
    hat_second = second_new / (1.0 - beta_second**STEP)
    weight_new = weight - rate * (hat_first / (jnp.sqrt(hat_second) + adam_eps) + decay * weight)
    return (weight_new, first_new, second_new)


def finish_body(
    width, heads,
    in_ref, cot_ref, branch_ref, back_ref, flat_ref, early_ref, late_ref, bcg_ref,
    zx_ref, zx1_ref, zx2_ref, bc_ref, bc1_ref, bc2_ref, out_ref, out1_ref, out2_ref, late_all_ref, dt_ref, dt1_ref, dt2_ref,
    layer_ref, grad_ref, zxn_ref, zx1n_ref, zx2n_ref, bcn_ref, bc1n_ref, bc2n_ref,
    outn_ref, out1n_ref, out2n_ref, dtn_ref, dt1n_ref, dt2n_ref,
):
    def update(refs, news, grad):
        fresh = adamw_step(*(ref[...] for ref in refs), grad, matrix_rate, matrix_decay)
        for ref, value in zip(news, fresh):
            ref[...] = value

    for k, grad in ((0, early_ref), (1, late_ref)):
        fresh = adamw_step(
            *(ref[:, k, :] for ref in (zx_ref, zx1_ref, zx2_ref)), grad[:, :width], matrix_rate, matrix_decay
        )
        for ref, value in zip((zxn_ref, zx1n_ref, zx2n_ref), fresh):
            ref[:, k, :] = value
    update((bc_ref, bc1_ref, bc2_ref), (bcn_ref, bc1n_ref, bc2n_ref), bcg_ref[...])
    update((out_ref, out1_ref, out2_ref), (outn_ref, out1n_ref, out2n_ref), early_ref[:, width:])

    @pl.when(pl.program_id(0) == 0)
    def _():
        unit = jnp.where(
            lax.broadcasted_iota(jnp.int32, (16, LANES), 0) == lax.broadcasted_iota(jnp.int32, (16, LANES), 1), 1.0, 0.0
        ).astype(f32)
        turned = mm_exact(unit, late_all_ref[:, width + 2 * NS :], NT)
        update((dt_ref, dt1_ref, dt2_ref), (dtn_ref, dt1n_ref, dt2n_ref), turned[:heads])

    rows = in_ref.shape[0]
    tile = 64

    def some(i, _):
        at = span(i * tile, tile)
        squares = jnp.zeros((tile, LANES), f32)
        inner = jnp.zeros((tile, LANES), f32)
        for c in range(D // LANES):
            cols = slice(c * LANES, (c + 1) * LANES)
            x = in_ref[at, cols].astype(f32)
            squares = squares + x * x
            inner = inner + x * flat_ref[c : c + 1, :] * back_ref[at, cols]
        r = lax.rsqrt(jnp.sum(squares, axis=-1, keepdims=True) / D + norm_eps)
        k = r * r * r * jnp.sum(inner, axis=-1, keepdims=True) / D
        r, k = jnp.broadcast_to(r, (tile, LANES)), jnp.broadcast_to(k, (tile, LANES))
        for c in range(D // LANES):
            cols = slice(c * LANES, (c + 1) * LANES)
            x = in_ref[at, cols].astype(f32)
            layer_ref[at, cols] = (x + branch_ref[at, cols]).astype(bf16)
            grad_ref[at, cols] = cot_ref[at, cols].astype(f32) + r * flat_ref[c : c + 1, :] * back_ref[at, cols] - x * k
        return 0

    lax.fori_loop(0, rows // tile, some, 0)


def finish(layer_input, out_grad, branch, back, flat, early, late, bcg, zx, bc, out, dt):
    (rows, width), heads = out[0].shape, dt[0].shape[0]
    steps = 4 if rows % 32 == 0 else 2
    part = lambda a: pl.BlockSpec((a.shape[0] // steps, *a.shape[1:]), lambda i: (i,) + (0,) * (a.ndim - 1))
    whole = lambda a: pl.BlockSpec(a.shape, lambda i: (0,) * a.ndim)
    like = lambda a, dtype=f32: jax.ShapeDtypeStruct(a.shape, dtype)
    weights = (*zx, *bc, *out)
    return pl.pallas_call(
        functools.partial(finish_body, width, heads),
        grid=(steps,),
        in_specs=[
            *(part(a) for a in (layer_input, out_grad, branch, back)), whole(flat),
            *(part(a) for a in (early, late, bcg, *weights)), whole(late), *(whole(a) for a in dt),
        ],
        out_specs=[part(layer_input), part(back), *(part(a) for a in weights), *(whole(a) for a in dt)],
        out_shape=[like(layer_input, bf16), like(back), *(like(a) for a in weights), *(like(a) for a in dt)],
        compiler_params=pltpu.CompilerParams(vmem_limit_bytes=ROOM),
        name="finish",
    )(layer_input, out_grad, branch, back, flat, early, late, bcg, *weights, late, *dt)


def local(
    layer_input,
    out_grad,
    small_params,
    small_first,
    small_second,
    w_zx,
    zx_first,
    zx_second,
    w_bc,
    bc_first,
    bc_second,
    w_dt,
    dt_first,
    dt_second,
    w_out,
    out_first,
    out_second,
):
    n = lax.axis_size("dp")
    flat = jnp.pad(small_params, (0, FLAT_ROWS * LANES - small_params.shape[0])).reshape(FLAT_ROWS, LANES)
    xg, xt, w_all, w_pair = gather_all(n, layer_input, flat, w_zx, w_bc, w_dt.T, w_out)
    z, v, xc, dr, y, dn, st, red, cot_all, pair_all, taps, head, chan = ssd_forward(
        n, xg, w_all, flat, out_grad, w_pair
    )
    dy, dz, branch, early, gate = early_gradients(z, y, dn, red, pair_all, chan, xt, cot_all)
    d_late, small, owner_early, own_branch = ssd_backward(
        n, dy, v, xc, dr, st, gate, taps, head, chan, early, branch
    )
    owner_late, d_normed_in, owner_bc, flat_grad = reduce_all(
        n, xg, xt, d_late, dz, pair_all, w_all, small, flat
    )
    small_grad = flat_grad.reshape(-1)[: small_params.shape[0]]
    small_new, small_first_new, small_second_new = adamw_step(
        small_params, small_first, small_second, small_grad, small_rate, 0.0
    )
    (
        layer_output, input_grad, zx_new, zx_first_new, zx_second_new, bc_new, bc_first_new, bc_second_new,
        out_new, out_first_new, out_second_new, dt_new, dt_first_new, dt_second_new,
    ) = finish(
        layer_input, out_grad, own_branch, d_normed_in, flat, owner_early, owner_late, owner_bc,
        (w_zx, zx_first, zx_second), (w_bc, bc_first, bc_second), (w_out, out_first, out_second),
        (w_dt.T, dt_first.T, dt_second.T),
    )
    dt_new, dt_first_new, dt_second_new = dt_new.T, dt_first_new.T, dt_second_new.T
    return (
        layer_output,
        input_grad,
        small_new,
        small_first_new,
        small_second_new,
        zx_new,
        zx_first_new,
        zx_second_new,
        bc_new,
        bc_first_new,
        bc_second_new,
        dt_new,
        dt_first_new,
        dt_second_new,
        out_new,
        out_first_new,
        out_second_new,
    )


def solution(mesh):
    return jax.shard_map(
        local,
        mesh=mesh,
        in_specs=(
            P(("dp", "tensor"), None),
            P(("dp", "tensor"), None),
            P(),
            P(),
            P(),
            P("dp", None, "tensor"),
            P("dp", None, "tensor"),
            P("dp", None, "tensor"),
            P("dp", None),
            P("dp", None),
            P("dp", None),
            P("dp", "tensor"),
            P("dp", "tensor"),
            P("dp", "tensor"),
            P("dp", "tensor"),
            P("dp", "tensor"),
            P("dp", "tensor"),
        ),
        out_specs=(
            P(("dp", "tensor"), None),
            P(("dp", "tensor"), None),
            P(),
            P(),
            P(),
            P("dp", None, "tensor"),
            P("dp", None, "tensor"),
            P("dp", None, "tensor"),
            P("dp", None),
            P("dp", None),
            P("dp", None),
            P("dp", "tensor"),
            P("dp", "tensor"),
            P("dp", "tensor"),
            P("dp", "tensor"),
            P("dp", "tensor"),
            P("dp", "tensor"),
        ),
        check_vma=False,
    )
```

```python
import functools

import jax
import jax.numpy as jnp
from jax import lax
from jax.experimental import pallas as pl
from jax.experimental.pallas import tpu as pltpu
from jax.sharding import PartitionSpec as P

D = 1536
DI = 3072
H = 48
NS = 128
P_SIZE = 64
CONV = 4
LEN = 2048
STEP = 10

T = 128
ROWS = 256
LANES = 128
ROOM = 60 * 2**20
Z_EARLY = 256

norm_eps = 1e-05
adam_eps = 1e-08
beta_first = 0.9
beta_second = 0.95
matrix_rate = 0.01
small_rate = 0.1
matrix_decay = 0.1

f32 = jnp.float32
bf16 = jnp.bfloat16
NN = (((1,), (0,)), ((), ()))
NT = (((1,), (1,)), ((), ()))
TN = (((0,), (0,)), ((), ()))
HIGHEST = lax.Precision.HIGHEST


GATE_ROW, TAPS_ROW, BIAS_ROW, TAPS_BC_ROW, BIAS_BC_ROW, HEAD_ROW, FLAT_ROWS = 12, 36, 132, 156, 164, 166, 168


def mm(a, b, dims=NN):
    return lax.dot_general(a, b, dims, preferred_element_type=f32)


def mm_exact(a, b, dims=NN):
    return lax.dot_general(a, b, dims, preferred_element_type=f32, precision=HIGHEST)


def sigmoid(v):
    return 0.5 * jnp.tanh(0.5 * v) + 0.5


def softplus(v):
    return jnp.maximum(v, 0.0) + jnp.log1p(jnp.exp(-jnp.abs(v)))


def spread(col):
    return jnp.broadcast_to(col, (T, LANES))


def block_iota(axis):
    return lax.broadcasted_iota(jnp.int32, (T, LANES), axis)


def head_rows(dr_ref, head_ref, rows):
    raw = dr_ref[rows, :] + head_ref[0:1, :]
    dt = softplus(raw)
    low_tri = jnp.where(block_iota(0) >= block_iota(1), 1.0, 0.0).astype(f32)
    decay = mm_exact(low_tri, dt * head_ref[1:2, :])
    return raw, dt, decay


def ring_place(n):
    me = lax.axis_index("dp")
    z, x = lax.div(me, 2), lax.rem(me, 2)
    return z + x * (n - 1 - 2 * z)


def ring_index(pos, n):
    back = lax.div(pos, n // 2)
    return 2 * pos + back * (2 * n - 1 - 4 * pos)


def neighbours(n):
    pos = ring_place(n)
    right = ring_index(lax.rem(pos + 1, n), n)
    left = ring_index(lax.rem(pos + n - 1, n), n)
    me = lax.axis_index("tensor")
    y, core = lax.div(me, 2), lax.rem(me, 2)
    across = 2 * (1 - y) + core
    beside = 2 * y + 1 - core
    return pos, ({"dp": right}, {"dp": left}), me, {"tensor": across}, {"tensor": beside}


def greet(peers):
    barrier = pltpu.get_barrier_semaphore()
    for peer in peers:
        pl.semaphore_signal(barrier, inc=1, device_id=peer, device_id_type=pl.DeviceIdType.MESH)


def enter(peers):
    greet(peers)
    pl.semaphore_wait(pltpu.get_barrier_semaphore(), len(peers))


def remote(src, dst, send_sem, recv_sem, peer):
    return pltpu.make_async_remote_copy(
        src_ref=src, dst_ref=dst, send_sem=send_sem, recv_sem=recv_sem,
        device_id=peer, device_id_type=pl.DeviceIdType.MESH,
    )


def span(start, size):
    return pl.ds(pl.multiple_of(start, 16), size)


def strip(rows):
    return next(size for size in (48, 32, 16) if rows % size == 0)


def cut_rows(rows):
    top = rows // 32 * 16
    return ((0, top), (top, rows - top))


def forward_body(
    n, rows, tokens, width,
    tall_ref, xt_ref, w_ref, flat_ref, cot_ref, wp_ref,
    v_ref, xc_ref, dr_ref, st_ref, dy_ref, dz_ref, branch_ref, early_ref, gate_ref, gain_ref, wps_ref,
    taps_ref, head_ref, chan_ref,
    halo, state, y_all, z_all, dn_all, nl_all, dz_all, cots, wps, sums, red,
    own_keep, ring_keep, ring_send, ring_recv, over_send, over_recv,
    side_send, side_recv, pass_send, pass_recv, sum_send, sum_recv,
):
    pairs = width // LANES
    wide = width + 2 * NS
    step = pl.program_id(0)
    steps = LEN // ROWS
    tall = 2 * ROWS
    gating = steps
    forming = gating + LEN // tall
    products = forming + steps
    last_step = products + D // ROWS - 1
    pos, ring, me, across, beside = neighbours(n)
    opposite = lax.rem(me + 2, 4)
    next_door = me + 1 - 2 * lax.rem(me, 2)
    far = lax.rem(next_door + 2, 4)
    askew = {"tensor": far}
    quarter = tokens // 4
    hops = n // 2
    cuts = cut_rows(rows)
    mine = ring_index(pos, n)

    parts_of = ((0, width), (width, width - Z_EARLY))

    def hop(k, part, way, h):
        first, size = cuts[part]
        cols = pl.ds(*parts_of[k])
        block = ring_index(lax.rem(pos + (h if way else n - h), n), n)
        here = wps.at[span(block * rows + first, size), cols]
        src = wp_ref.at[pl.ds(first, size), cols] if h == 0 else here
        return remote(src, here, ring_send.at[way, part, k, h], ring_recv.at[way, part, k, h], ring[way])

    def hop_lands(k, part, way, h):
        first, size = cuts[part]
        block = ring_index(lax.rem(pos + (h + 1 if way else n - h - 1), n), n)
        return span(block * rows + first, size), pl.ds(*parts_of[k])

    def hop_arrival(k, part, way, h):
        here = wps.at[hop_lands(k, part, way, h)]
        return remote(here, here, ring_send.at[way, part, k, h], ring_recv.at[way, part, k, h], ring[way])

    def hop_keep(part, way, h):
        at = hop_lands(1, part, way, h)
        return pltpu.make_async_copy(wps.at[at], wps_ref.at[at], ring_keep.at[way, part, h])

    def hop_ways(h):
        return [(part, way) for part in (0, 1) for way in (0, 1) if h < hops - 1 or part == way]

    def hop_on(k, h):
        for part, way in hop_ways(h - 1) if h > 0 else ():
            hop_arrival(k, part, way, h - 1).wait_recv()
            if k == 1:
                hop_keep(part, way, h - 1).start()
            if h < hops and (part, way) in hop_ways(h):
                hop(k, part, way, h).start()
        if h == 0:
            for part, way in hop_ways(0):
                hop(k, part, way, 0).start()

    def over(k):
        return remote(
            cot_ref.at[pl.ds(k * quarter, quarter)], cots.at[span(me * tokens + k * quarter, quarter)],
            over_send.at[k], over_recv.at[k], across,
        )

    def landed(start, size, send, recv, peer):
        here = cots.at[span(start, size)]
        return remote(here, here, send, recv, peer)

    def over_arrival(k):
        return landed(opposite * tokens + k * quarter, quarter, over_send.at[k], over_recv.at[k], across)

    def passing(k):
        return landed(opposite * tokens + k * quarter, quarter, pass_send.at[k], pass_recv.at[k], beside)

    def pass_arrival(k):
        return landed(far * tokens + k * quarter, quarter, pass_send.at[k], pass_recv.at[k], beside)

    def side():
        return remote(cot_ref, cots.at[span(me * tokens, tokens)], side_send.at[0], side_recv.at[0], beside)

    def side_arrival():
        return landed(next_door * tokens, tokens, side_send.at[0], side_recv.at[0], beside)

    def own_keeps():
        z_cols = pl.ds(*parts_of[1])
        return (
            pltpu.make_async_copy(cot_ref, cots.at[span(me * tokens, tokens)], own_keep.at[0]),
            pltpu.make_async_copy(wp_ref, wps.at[span(mine * rows, rows)], own_keep.at[1]),
            pltpu.make_async_copy(wp_ref.at[:, z_cols], wps_ref.at[span(mine * rows, rows), z_cols], own_keep.at[2]),
        )

    def pass_on(*pieces):
        for k in pieces:
            over_arrival(k).wait_recv()
            passing(k).start()

    @pl.when(step == 0)
    def _():
        enter((*ring, across, beside, askew))
        hop_on(0, 0)
        over(0).start()
        over(1).start()
        side().start()
        for copy in own_keeps():
            copy.start()
        halo[0:8, :] = jnp.zeros((8, wide), f32)
        state[...] = jnp.zeros_like(state)
        parameter_rows(me, width, flat_ref, taps_ref, head_ref, chan_ref)
        gate_ref[...] = jnp.zeros_like(gate_ref)

    for h in range(1, hops):
        pl.when(step == min(2 * h, gating))(functools.partial(hop_on, 0, h))
    for h in range(hops):
        pl.when(step == min(2 * h + 1, gating))(functools.partial(hop_on, 1, h))
    for k in (1, 0):
        pl.when(step == gating)(functools.partial(hop_on, k, hops))

    @pl.when(step == 3)
    def _():
        over(2).start()

    @pl.when(step == 5)
    def _():
        over(3).start()
        pass_on(0, 1)

    pl.when(step == steps - 1)(functools.partial(pass_on, 2))

    @pl.when(step < gating)
    def _():
        scan_step(
            width, step, tall_ref, w_ref, taps_ref, head_ref, chan_ref,
            v_ref, xc_ref, dr_ref, st_ref, halo, state, y_all, functools.partial(pass_on, 3),
        )

    @pl.when(step == gating)
    def _():
        side_arrival().wait_recv()
        for k in range(4):
            pass_arrival(k).wait_recv()
        for copy in own_keeps():
            copy.wait()

    @pl.when((step >= gating) & (step < forming))
    def _():
        first = (step - gating) * tall
        at = span(first, tall)
        z_all[at, :Z_EARLY] = mm(tall_ref[...], w_ref[:, wide + LANES :])
        z_all[at, Z_EARLY:] = mm(tall_ref[...], wps[:, width:])
        dn_all[at, :] = mm(cots[at, :], wps[:, :width])
        ones = jnp.ones((8, LANES), f32)
        for sub in range(tall // T):
            rows_at = span(first + sub * T, T)
            squares = jnp.zeros((T, LANES), f32)
            inner = jnp.zeros((T, LANES), f32)
            for p in range(pairs):
                cols = slice(p * LANES, (p + 1) * LANES)
                z = z_all[rows_at, cols]
                gated = y_all[rows_at, cols] * (z * sigmoid(z))
                squares = squares + gated * gated
                inner = inner + gated * chan_ref[0:1, cols] * dn_all[rows_at, cols]
            lanes = pl.ds(pl.multiple_of(first + sub * T, T), T)
            sums[me, 0:4, lanes] = mm_exact(ones, squares, NT)[0:4]
            sums[me, 4:8, lanes] = mm_exact(ones, inner, NT)[4:8]

    @pl.when(step == forming - 1)
    def _():
        peers = ((beside, next_door), (across, opposite), (askew, far))
        for k, (peer, _) in enumerate(peers):
            remote(sums.at[me], sums.at[me], sum_send.at[k], sum_recv.at[k], peer).start()
        for h in range(hops):
            for part, way in hop_ways(h):
                for k in (0, 1):
                    hop(k, part, way, h).wait_send()
                hop_keep(part, way, h).wait()
        side().wait_send()
        for k in range(4):
            over(k).wait_send()
            passing(k).wait_send()
        for k, (peer, other) in enumerate(peers):
            remote(sums.at[other], sums.at[other], sum_send.at[k], sum_recv.at[k], peer).wait()
        red[...] = ((sums[0] + sums[1]) + sums[2]) + sums[3]

    @pl.when((step >= forming) & (step < products))
    def _():
        first = (step - forming) * ROWS
        lanes = pl.ds(pl.multiple_of(first, ROWS), ROWS)
        q_row = lax.rsqrt(red[0:4, lanes] / DI + norm_eps)
        k_row = q_row * q_row * q_row * red[4:8, lanes] / DI
        turned = jnp.concatenate([q_row, k_row], axis=0).T
        for sub in range(ROWS // T):
            rows_at = slice(sub * T, (sub + 1) * T)
            at = span(first + sub * T, T)
            q, kk = spread(turned[rows_at, 0:1]), spread(turned[rows_at, 4:5])
            for p in range(pairs):
                cols = slice(p * LANES, (p + 1) * LANES)
                z, y, dn = z_all[at, cols], y_all[at, cols], dn_all[at, cols]
                gain = chan_ref[0:1, cols]
                s = sigmoid(z)
                sz = z * s
                gated = y * sz
                gq = gated * q
                dg = q * gain * dn - gated * kk
                gate_ref[:, cols] += jnp.sum((gq * dn).reshape(T // 8, 8, LANES), axis=0)
                nl_all[at, cols] = (gq * gain).astype(bf16)
                dz = (dg * y * (s + sz * (1.0 - s))).astype(bf16)
                dz_all[at, cols] = dz
                dz_ref[rows_at, cols] = dz
                dy_ref[rows_at, cols] = (dg * sz).astype(bf16)
        branch_ref[...] = mm(nl_all[span(first, ROWS), :], wps[:, :width], NT).astype(bf16)

    @pl.when(step >= products)
    def _():
        first = (step - products) * ROWS
        at = span(first, ROWS)
        lanes = pl.ds(pl.multiple_of(first, ROWS), ROWS)
        grad = mm(xt_ref[...], dz_all[...])
        early_ref[:, :width] = grad.astype(bf16)
        share = jnp.zeros((ROWS, LANES), f32)
        for p in range(pairs):
            cols = slice(p * LANES, (p + 1) * LANES)
            if p < Z_EARLY // LANES:
                w = w_ref[at, wide + (p + 1) * LANES : wide + (p + 2) * LANES]
            else:
                w = wps[at, width + p * LANES - Z_EARLY : width + (p + 1) * LANES - Z_EARLY]
            share = share + grad[:, cols] * w.astype(f32)
        gain_ref[:, lanes] = mm_exact(jnp.ones((8, LANES), f32), share, NT)
        early_ref[:, width:] = mm(cots[:, lanes], nl_all[...], TN).astype(bf16)


def parameter_rows(me, width, flat_ref, taps_ref, head_ref, chan_ref):
    pairs = width // LANES
    heads = width // P_SIZE
    taps_ref[...] = jnp.zeros_like(taps_ref)
    chan_ref[...] = jnp.zeros_like(chan_ref)
    for c in range(pairs):
        cols = slice(c * LANES, (c + 1) * LANES)
        chan_ref[0:1, cols] = flat_ref[pl.ds(GATE_ROW + pairs * me + c, 1), :]
        taps_ref[CONV : CONV + 1, cols] = flat_ref[pl.ds(BIAS_ROW + pairs * me + c, 1), :]
        for k in range(CONV):
            taps_ref[k : k + 1, cols] = flat_ref[pl.ds(TAPS_ROW + 4 * pairs * k + pairs * me + c, 1), :]
    for c in range(2):
        cols = slice(width + c * LANES, width + (c + 1) * LANES)
        taps_ref[CONV : CONV + 1, cols] = flat_ref[BIAS_BC_ROW + c : BIAS_BC_ROW + c + 1, :]
        for k in range(CONV):
            row = TAPS_BC_ROW + 2 * k + c
            taps_ref[k : k + 1, cols] = flat_ref[row : row + 1, :]
    both = jnp.concatenate([flat_ref[HEAD_ROW : HEAD_ROW + 1, :], flat_ref[HEAD_ROW + 1 : HEAD_ROW + 2, :]], axis=1)
    both = jnp.broadcast_to(both, (8, 2 * LANES))
    lane = lax.broadcasted_iota(jnp.int32, (2 * LANES, LANES), 0)
    head = lax.broadcasted_iota(jnp.int32, (2 * LANES, LANES), 1)

    def take(kind):
        match = (lane == 4 * heads * kind + heads * me + head) & (head < heads)
        return mm_exact(both, jnp.where(match, 1.0, 0.0).astype(f32))

    valid = lax.broadcasted_iota(jnp.int32, (8, LANES), 1) < heads
    row = lax.broadcasted_iota(jnp.int32, (8, LANES), 0)
    rates = jnp.where(valid, -jnp.exp(take(1)), 0.0)
    head_ref[...] = jnp.where(row == 0, take(0), jnp.where(row == 1, rates, 0.0))
    skip = mm_exact(take(2), picked(width).astype(f32), NT)
    chan_ref[1:2, :] = skip[0:1]


def picked(width):
    channel = lax.broadcasted_iota(jnp.int32, (width, LANES), 0)
    head = lax.broadcasted_iota(jnp.int32, (width, LANES), 1)
    return jnp.where((channel >= head * P_SIZE) & (channel < (head + 1) * P_SIZE), 1.0, 0.0).astype(bf16)


def scan_step(
    width, step, tall_ref, w_ref, taps_ref, head_ref, chan_ref,
    v_ref, xc_ref, dr_ref, st_ref, halo, state, y_all, late_turn,
):
    pairs = width // LANES
    wide = width + 2 * NS
    mine = span(lax.rem(step, 2) * ROWS, ROWS)
    dr_ref[...] = mm(tall_ref[mine, :], w_ref[:, wide : wide + LANES])
    halo[8 : 8 + ROWS, :] = mm(tall_ref[mine, :], w_ref[:, :wide])
    low_half = block_iota(1) < P_SIZE
    causal = block_iota(0) >= block_iota(1)

    def convolved(sub, block):
        cols = slice(block * LANES, (block + 1) * LANES)
        total = taps_ref[CONV : CONV + 1, cols]
        for k in range(CONV):
            first = 8 - (CONV - 1) + k + sub * T
            total = total + taps_ref[k : k + 1, cols] * halo[first : first + T, cols]
        rows = slice(sub * T, (sub + 1) * T)
        xc_ref[rows, cols] = total.astype(bf16)
        v_ref[rows, cols] = halo[8 + sub * T : 8 + (sub + 1) * T, cols].astype(bf16)
        return total * sigmoid(total)

    for sub in range(ROWS // T):
        rows = slice(sub * T, (sub + 1) * T)
        raw, dt, decay = head_rows(dr_ref, head_ref, rows)
        decay_t = decay.T
        b_low = convolved(sub, pairs).astype(bf16)
        c_low = convolved(sub, pairs + 1).astype(bf16)
        b_t = b_low.T
        scores = jnp.where(causal, mm(c_low, b_low, NT), 0.0)
        st_ref[sub] = state[...].astype(bf16)
        for p in range(pairs):
            cols = slice(p * LANES, (p + 1) * LANES)
            x = convolved(sub, p)
            l1, l2 = spread(decay[:, 2 * p : 2 * p + 1]), spread(decay[:, 2 * p + 1 : 2 * p + 2])
            both = jnp.where(low_half, l1, l2)
            dtb = jnp.where(
                low_half, spread(dt[:, 2 * p : 2 * p + 1]), spread(dt[:, 2 * p + 1 : 2 * p + 2])
            )
            u = x * dtb
            m1 = scores * jnp.exp(jnp.minimum(l1 - decay_t[2 * p : 2 * p + 1, :], 0.0))
            m2 = scores * jnp.exp(jnp.minimum(l2 - decay_t[2 * p + 1 : 2 * p + 2, :], 0.0))
            mixing = jnp.concatenate([m1.astype(bf16), m2.astype(bf16)], axis=1)
            parts = jnp.concatenate(
                [jnp.where(low_half, u, 0.0).astype(bf16), jnp.where(low_half, 0.0, u).astype(bf16)],
                axis=0,
            )
            last = both[T - 1 : T, :]
            entering = st_ref[sub, :, cols]
            y = mm(mixing, parts) + jnp.exp(both) * mm(c_low, entering) + chan_ref[1:2, cols] * x
            tail = (u * jnp.exp(last - both)).astype(bf16)
            state[:, cols] = jnp.exp(last) * state[:, cols] + mm(b_t, tail)
            y_all[span(step * ROWS + sub * T, T), cols] = y
        if sub == 0:
            pl.when(step == LEN // ROWS - 1)(late_turn)
    halo[0:8, :] = halo[ROWS : ROWS + 8, :]


def ssd_forward(n, xg, xt, w, flat, cot, wp):
    length = xg.shape[0]
    rows, width = wp.shape[0], (wp.shape[1] + Z_EARLY) // 2
    tokens = cot.shape[0]
    wide = width + 2 * NS
    steps = length // ROWS
    tall = 2 * ROWS
    forming = steps + length // tall
    products = forming + steps
    subs = ROWS // T
    assert length == LEN
    early = lambda i: jnp.minimum(i, steps - 1)
    formed = lambda i: jnp.clip(i - forming, 0, steps - 1)
    late = lambda i: jnp.maximum(i - products, 0)
    tall_at = lambda i: jnp.where(i < steps, lax.div(i, 2), jnp.minimum(i - steps, length // tall - 1))
    row = lambda m: pl.BlockSpec((ROWS, m), lambda i: (early(i), 0))
    form = lambda m: pl.BlockSpec((ROWS, m), lambda i: (formed(i), 0))
    whole = lambda a: pl.BlockSpec(a.shape, lambda i: (0,) * a.ndim, pipeline_mode=pl.Buffered(1))
    fixed = lambda m: pl.BlockSpec((8, m), lambda i: (0, 0))
    anywhere = pl.BlockSpec(memory_space=pl.ANY)
    vm, dma = pltpu.VMEM, pltpu.SemaphoreType.DMA
    hops = dma((2, 2, 2, n // 2))
    shape = lambda dims, dtype: jax.ShapeDtypeStruct(dims, dtype)
    return pl.pallas_call(
        functools.partial(forward_body, n, rows, tokens, width),
        grid=(products + D // ROWS,),
        in_specs=[
            pl.BlockSpec((tall, D), lambda i: (tall_at(i), 0)),
            pl.BlockSpec((ROWS, length), lambda i: (late(i), 0)),
            whole(w), whole(flat), whole(cot), whole(wp),
        ],
        out_specs=[
            row(wide), row(wide), row(LANES), pl.BlockSpec((subs, NS, width), lambda i: (early(i), 0, 0)),
            form(width), form(width), form(D), pl.BlockSpec((ROWS, 2 * width), lambda i: (late(i), 0)),
            fixed(width), fixed(D), anywhere, *(fixed(m) for m in (wide, LANES, width)),
        ],
        out_shape=[
            shape((length, wide), bf16), shape((length, wide), bf16), shape((length, LANES), f32),
            shape((length // T, NS, width), bf16), shape((length, width), bf16), shape((length, width), bf16),
            shape((length, D), bf16), shape((D, 2 * width), bf16), shape((8, width), f32), shape((8, D), f32),
            shape((n * rows, 2 * width - Z_EARLY), bf16), *(shape((8, m), f32) for m in (wide, LANES, width)),
        ],
        scratch_shapes=[
            vm((ROWS + 8, wide), f32), vm((NS, width), f32), *(vm((length, width), f32) for _ in range(3)),
            vm((length, width), bf16), vm((length, width), bf16),
            vm((4 * tokens, D), bf16), vm((n * rows, 2 * width - Z_EARLY), bf16), vm((4, 8, length), f32),
            vm((8, length), f32),
            dma((3,)), dma((2, 2, n // 2)), hops, hops, dma((4,)), dma((4,)),
            dma((1,)), dma((1,)), dma((4,)), dma((4,)), dma((3,)), dma((3,)),
        ],
        compiler_params=pltpu.CompilerParams(collective_id=2, has_side_effects=True, vmem_limit_bytes=ROOM),
        name="layer_forward",
    )(xg, xt, w, flat, cot, wp)


def gather_body(
    n, rows, tokens,
    in_ref, flat_ref, wzx_ref, wbc_ref, wdt_ref, wout_ref, xg_ref, xt_ref, ws_ref, wp_ref, x_ref, w_ref, xg, xt, ws,
    keep_sem, turn_sem, ring_keep, ring_send, ring_recv, over_send, over_recv, side_send, side_recv, pass_send, pass_recv,
):
    pos, ring, me, across, beside = neighbours(n)
    greet((*ring, across, beside))
    quarter = tokens // 4
    width = wout_ref.shape[1]
    heads = wdt_ref.shape[0]
    late = width + 2 * NS + LANES
    w_ref[:, :width] = wzx_ref[:, 1, :].astype(bf16)
    w_ref[:, width : width + 2 * NS] = wbc_ref[...].astype(bf16)
    unit = jnp.where(
        lax.broadcasted_iota(jnp.int32, (16, LANES), 0) == lax.broadcasted_iota(jnp.int32, (16, LANES), 1), 1.0, 0.0
    ).astype(bf16)
    steps_w = jnp.concatenate([wdt_ref[...], jnp.zeros((16 - heads, rows), f32)], axis=0).astype(bf16)
    w_ref[:, width + 2 * NS : late] = mm(steps_w, unit, TN).astype(bf16)
    w_ref[:, late:] = wzx_ref[:, 0, :Z_EARLY].astype(bf16)

    def normalize(k):
        def some(i, _):
            at = span(k * quarter + i * 64, 64)
            squares = jnp.zeros((64, LANES), f32)
            for c in range(D // LANES):
                x = in_ref[at, c * LANES : (c + 1) * LANES].astype(f32)
                squares = squares + x * x
            inverse = lax.rsqrt(jnp.sum(squares, axis=-1, keepdims=True) / D + norm_eps)
            inverse = jnp.broadcast_to(inverse, (64, LANES))
            for c in range(D // LANES):
                cols = slice(c * LANES, (c + 1) * LANES)
                x_ref[at, cols] = (in_ref[at, cols].astype(f32) * inverse * flat_ref[c : c + 1, :]).astype(bf16)
            return 0

        lax.fori_loop(0, quarter // 64, some, 0)

    normalize(0)
    pl.semaphore_wait(pltpu.get_barrier_semaphore(), 4)
    started, kept = [], []

    def go(*args):
        copy = remote(*args)
        copy.start()
        started.append(copy)
        return copy

    def keep(src, dst, sem):
        copy = pltpu.make_async_copy(src, dst, sem)
        copy.start()
        kept.append(copy)

    opposite = lax.rem(me + 2, 4)
    next_door = me + 1 - 2 * lax.rem(me, 2)
    far = lax.rem(next_door + 2, 4)
    cuts = cut_rows(rows)

    def turned(src, start, first, size):
        sets = D // (4 * LANES)

        def some(i, _):
            row = first + lax.div(i, sets) * LANES
            at = span(row if src is x_ref else start + row, LANES)
            to = pl.ds(pl.multiple_of(start + row, LANES), LANES)
            for c in range(4):
                cols = pl.ds(pl.multiple_of((lax.rem(i, sets) * 4 + c) * LANES, LANES), LANES)
                xt[cols, to] = src[at, cols].T
            return 0

        lax.fori_loop(0, size // LANES * sets, some, 0)

    def keep_turned(k, block):
        at = pl.ds(pl.multiple_of(block * tokens, LANES), tokens)
        keep(xt.at[:, at], xt_ref.at[:, at], turn_sem.at[k])

    def arrived(part, way, step, block):
        first, size = cuts[part]
        at = span(block * rows + first, size)
        remote(
            ws.at[at], ws.at[at], ring_send.at[way, part, step], ring_recv.at[way, part, step], ring[way]
        ).wait_recv()
        keep(ws.at[at], ws_ref.at[at], ring_keep.at[way, part, step])

    def ring_step(step, parts=(0, 1)):
        last = step == n // 2 - 1
        for part in parts:
            first, size = cuts[part]
            for way in (0, 1):
                block = ring_index(lax.rem(pos + (step if way else n - step), n), n)
                here = ws.at[span(block * rows + first, size)]
                if step > 0:
                    arrived(part, way, step - 1, block)
                if last and part != way:
                    continue
                src = w_ref.at[pl.ds(first, size)] if step == 0 else here
                go(src, here, ring_send.at[way, part, step], ring_recv.at[way, part, step], ring[way])

    def send_over(k):
        go(
            x_ref.at[pl.ds(k * quarter, quarter)], xg.at[span(me * tokens + k * quarter, quarter)],
            over_send.at[k], over_recv.at[k], across,
        )

    def pass_on(k):
        at = span(opposite * tokens + k * quarter, quarter)
        here = xg.at[at]
        remote(here, here, over_send.at[k], over_recv.at[k], across).wait_recv()
        go(here, here, pass_send.at[k], pass_recv.at[k], beside)
        keep(here, xg_ref.at[at], keep_sem.at[k])

    def pass_lands(k):
        at = span(far * tokens + k * quarter, quarter)
        remote(xg.at[at], xg.at[at], pass_send.at[k], pass_recv.at[k], beside).wait_recv()
        keep(xg.at[at], xg_ref.at[at], keep_sem.at[4 + k])
        turned(xg, far * tokens, k * quarter, quarter)

    ring_step(0, (0,))
    leading = list(started)
    send_over(0)
    normalize(1)
    send_over(1)
    normalize(2)
    normalize(3)
    go(x_ref, xg.at[span(me * tokens, tokens)], side_send.at[0], side_recv.at[0], beside)
    wp_ref[:, :width] = wout_ref[...].astype(bf16)
    wp_ref[:, width:] = wzx_ref[:, 0, Z_EARLY:].astype(bf16)
    for copy in leading:
        copy.wait_send()
        started.remove(copy)
    ring_step(0, (1,))
    mine = ring_index(pos, n)
    keep(x_ref, xg_ref.at[span(me * tokens, tokens)], keep_sem.at[8])
    keep(w_ref, ws_ref.at[span(mine * rows, rows)], keep_sem.at[9])
    turned(x_ref, me * tokens, 0, tokens)
    keep_turned(0, me)
    ring_step(1)
    send_over(2)
    at = span(next_door * tokens, tokens)
    remote(xg.at[at], xg.at[at], side_send.at[0], side_recv.at[0], beside).wait_recv()
    keep(xg.at[at], xg_ref.at[at], keep_sem.at[10])
    turned(xg, next_door * tokens, 0, tokens)
    keep_turned(1, next_door)
    send_over(3)
    for step in range(2, n // 2):
        ring_step(step)
        if step == 2:
            pass_on(0)
            pass_on(1)
            turned(xg, opposite * tokens, 0, 2 * quarter)
    pass_on(2)
    pass_lands(0)
    pass_lands(1)
    pass_on(3)
    turned(xg, opposite * tokens, 2 * quarter, 2 * quarter)
    keep_turned(2, opposite)
    for part in (0, 1):
        arrived(part, part, n // 2 - 1, ring_index(lax.rem(pos + n // 2, n), n))
    pass_lands(2)
    pass_lands(3)
    keep_turned(3, far)
    for copy in kept:
        copy.wait()
    for copy in started:
        copy.wait_send()


def gather_all(n, layer_input, flat, w_zx, w_bc, w_dt, w_out):
    tokens, rows, width = layer_input.shape[0], w_bc.shape[0], w_out.shape[1]
    early = width + 2 * NS + LANES + Z_EARLY
    dma = pltpu.SemaphoreType.DMA
    anywhere = pl.BlockSpec(memory_space=pl.ANY)
    inside = pl.BlockSpec(memory_space=pltpu.VMEM)
    own = ((tokens, D), (rows, early))
    full = ((4 * tokens, D), (D, 4 * tokens), (n * rows, early))
    hops = dma((2, 2, n // 2))
    return pl.pallas_call(
        functools.partial(gather_body, n, rows, tokens),
        in_specs=[inside] * 6,
        out_specs=[anywhere, anywhere, anywhere, inside],
        out_shape=[jax.ShapeDtypeStruct(shape, bf16) for shape in (*full, (rows, 2 * width - Z_EARLY))],
        scratch_shapes=[
            *(pltpu.VMEM(shape, bf16) for shape in (*own, *full)),
            dma((11,)), dma((4,)), hops, hops, hops, dma((4,)), dma((4,)), dma((1,)), dma((1,)), dma((4,)), dma((4,)),
        ],
        compiler_params=pltpu.CompilerParams(collective_id=0, has_side_effects=True, vmem_limit_bytes=ROOM),
        name="gather_all",
    )(layer_input, flat, w_zx, w_bc, w_dt, w_out)


def backward_body(
    n, own_rows, tokens, width,
    dy_ref, v_ref, xc_ref, dr_ref, st_ref, gate_ref, taps_ref, head_ref, chan_ref, early_ref, branch_ref,
    d_ref, small_ref, oearly_ref, obranch_ref,
    dxh, dstate, yst, bds, dyeb, utb, gin, gout, xdu, turn, acc, hacc, pick_ref,
    own, slots, near, held, over_slot,
    load_sem, ring_send, ring_recv, near_send, near_recv, over_send, over_recv,
):
    pairs = width // LANES
    wide = width + 2 * NS
    step = pl.program_id(0)
    steps = LEN // ROWS
    pos, ring, me, across, beside = neighbours(n)
    opposite = lax.rem(me + 2, 4)
    next_door = me + 1 - 2 * lax.rem(me, 2)
    far = lax.rem(next_door + 2, 4)
    half = tokens // 2
    cuts = cut_rows(own_rows)

    def block_at(way, count):
        return ring_index(lax.rem(pos + (count if way else n - count), n), n)

    def hop(k, way, h):
        first, size = cuts[way]
        if h == 0:
            src = early_ref.at[span(block_at(way, 1) * own_rows + first, size), pl.ds(k * width, width)]
        else:
            src = slots[way][k].at[h - 1]
        return remote(
            src, slots[way][k].at[h], ring_send.at[way, k, h], ring_recv.at[way, k, h], ring[way]
        )

    def near_copy(turned, part):
        start = (next_door if turned else far) * tokens + part * half
        return remote(
            branch_ref.at[span(start, half)], near.at[turned, part],
            near_send.at[turned, part], near_recv.at[turned, part], beside,
        )

    def held_copy(turned, part):
        start = (me if turned else opposite) * tokens + part * half
        return pltpu.make_async_copy(
            branch_ref.at[span(start, half)], held.at[turned, part], load_sem.at[2 * turned + part]
        )

    def over_copy(part):
        return remote(held.at[0, part], over_slot.at[part], over_send.at[part], over_recv.at[part], across)

    def own_copy():
        return pltpu.make_async_copy(early_ref, own, load_sem.at[4])

    def ring_turn(k, h):
        for way in (0, 1):
            first, size = cuts[way]
            hop(k, way, h).wait_recv()
            block = block_at(way, 2 + h) if h < n - 2 else block_at(way, 0)

            tile = strip(size)

            def some(i, _, way=way, first=first, block=block, tile=tile):
                cols = slice(k * width, (k + 1) * width)
                came = slots[way][k][h, span(i * tile, tile), :]
                mine = own[span(block * own_rows + first + i * tile, tile), cols]
                if h < n - 2:
                    slots[way][k][h, span(i * tile, tile), :] = came + mine
                else:
                    oearly_ref[span(first + i * tile, tile), cols] = came.astype(f32) + mine.astype(f32)
                return 0

            lax.fori_loop(0, size // tile, some, 0)
            if h < n - 2:
                hop(k, way, h + 1).start()

    def ring_poll(k):
        for h in range(n - 1):
            pl.when(step == min(h + 1, steps - 1))(functools.partial(ring_turn, k, h))

    def add_near(turned):
        for part in (0, 1):
            held_copy(turned, part).wait()
            near_copy(turned, part).wait_recv()

            def some(i, _, part=part):
                at = span(i * 32, 32)
                if turned:
                    total = held[1, part, at, :].astype(f32) + near[1, part, at, :].astype(f32)
                    obranch_ref[span(part * half + i * 32, 32), :] = total
                else:
                    held[0, part, at, :] = held[0, part, at, :] + near[0, part, at, :]
                return 0

            lax.fori_loop(0, half // 32, some, 0)
            if not turned:
                over_copy(part).start()

    @pl.when(step == 0)
    def _():
        enter((*ring, across, beside))
        for way in (0, 1):
            hop(0, way, 0).start()
        for turned in (0, 1):
            for part in (0, 1):
                near_copy(turned, part).start()
                held_copy(turned, part).start()
        own_copy().start()
        dxh[T : T + 8, :] = jnp.zeros((8, wide), f32)
        dstate[...] = jnp.zeros_like(dstate)
        acc[...] = jnp.zeros_like(acc)
        hacc[...] = jnp.zeros_like(hacc)
        turn[...] = jnp.zeros_like(turn)
        pick_ref[...] = picked(width)

    @pl.when(step == 1)
    def _():
        own_copy().wait()
        add_near(0)

    pl.when(step == 2)(functools.partial(add_near, 1))
    ring_poll(0)

    low_half = block_iota(1) < P_SIZE
    row_at, col_at = block_iota(0), block_iota(1)
    until = row_at <= col_at
    before = row_at < col_at
    upper = jnp.where(until, 1.0, 0.0).astype(f32)
    strict = jnp.where(before, 1.0, 0.0).astype(f32)
    low_tri = jnp.where(row_at >= col_at, 1.0, 0.0).astype(bf16)

    def add(index, cols, value):
        acc[index, :, cols] += jnp.sum(value.reshape(T // 8, 8, LANES), axis=0)

    def conv_back(rows, block, d_act, xc, s, act):
        cols = slice(block * LANES, (block + 1) * LANES)
        dxh[0:T, cols] = d_act * (s + act * (1.0 - s))
        v = v_ref[rows, cols].astype(f32)
        total = None
        for m in range(CONV):
            moved = dxh[m : m + T, cols]
            if m == 0:
                add(CONV, cols, moved)
            add(CONV - 1 - m, cols, v * moved)
            term = taps_ref[CONV - 1 - m : CONV - m, cols] * moved
            total = term if total is None else total + term
        d_ref[rows, cols] = total.astype(bf16)

    for sub in reversed(range(ROWS // T)):
        rows = slice(sub * T, (sub + 1) * T)
        raw, dt, decay = head_rows(dr_ref, head_ref, rows)
        decay_t = decay.T
        b_cols = slice(width, width + NS)
        c_cols = slice(width + NS, width + 2 * NS)
        b_xc, c_xc = xc_ref[rows, b_cols].astype(f32), xc_ref[rows, c_cols].astype(f32)
        b_s, c_s = sigmoid(b_xc), sigmoid(c_xc)
        b_act, c_act = b_xc * b_s, c_xc * c_s
        b_low, c_low = b_act.astype(bf16), c_act.astype(bf16)
        c_t = c_low.T
        scores_t = jnp.where(until, mm(b_low, c_low, NT), 0.0)
        ds_low = dstate[...].astype(bf16)
        yst[...] = mm(c_low, st_ref[sub])
        bds[...] = mm(b_low, ds_low)
        d_scores = jnp.zeros((T, LANES), f32)
        for p in range(pairs):
            cols = slice(p * LANES, (p + 1) * LANES)
            dy_low = dy_ref[rows, cols]
            dy = dy_low.astype(f32)
            xc = xc_ref[rows, cols].astype(f32)
            xs = sigmoid(xc)
            x = xc * xs
            l1, l2 = spread(decay[:, 2 * p : 2 * p + 1]), spread(decay[:, 2 * p + 1 : 2 * p + 2])
            both = jnp.where(low_half, l1, l2)
            dtb = jnp.where(
                low_half, spread(dt[:, 2 * p : 2 * p + 1]), spread(dt[:, 2 * p + 1 : 2 * p + 2])
            )
            u = x * dtb
            last = both[T - 1 : T, :]
            e1 = jnp.exp(jnp.minimum(decay_t[2 * p : 2 * p + 1, :] - l1, 0.0))
            e2 = jnp.exp(jnp.minimum(decay_t[2 * p + 1 : 2 * p + 2, :] - l2, 0.0))
            zero = jnp.zeros_like(dy_low)
            u_low = u.astype(bf16)
            du_in = mm(
                jnp.concatenate([(scores_t * e1).astype(bf16), (scores_t * e2).astype(bf16)], axis=1),
                jnp.concatenate(
                    [jnp.where(low_half, dy_low, zero), jnp.where(low_half, zero, dy_low)], axis=0
                ),
            )
            d_mix = mm(
                jnp.concatenate(
                    [jnp.where(low_half, u_low, zero), jnp.where(low_half, zero, u_low)], axis=0
                ),
                dy_low,
                NT,
            )
            d1, d2 = d_mix[:T] * e1, d_mix[T:] * e2
            d_scores = d_scores + d1 + d2
            reach = mm(
                jnp.concatenate([(d1 * scores_t).astype(bf16), (d2 * scores_t).astype(bf16)], axis=0),
                low_tri,
            )
            turn[2 * p : 2 * p + 1, :] = jnp.sum(jnp.where(before, reach[:T], 0.0), axis=0, keepdims=True)
            turn[2 * p + 1 : 2 * p + 2, :] = jnp.sum(
                jnp.where(before, reach[T:], 0.0), axis=0, keepdims=True
            )
            tail = jnp.exp(last - both)
            dye = dy * jnp.exp(both)
            du_out = tail * bds[:, cols]
            du = du_in + du_out
            gin[:, cols] = (dye * yst[:, cols]).astype(bf16)
            gout[:, cols] = (u * du_out).astype(bf16)
            xdu[:, cols] = (x * du).astype(bf16)
            dyeb[:, cols] = dye.astype(bf16)
            utb[:, cols] = (u * tail).astype(bf16)
            add(CONV + 1, cols, dy * x)
            conv_back(rows, p, dtb * du + chan_ref[1:2, cols] * dy, xc, xs, x)
        d_scores = jnp.where(until, d_scores, 0.0).astype(bf16)
        d_b = mm(d_scores, c_low) + mm(utb[...], ds_low, NT)
        d_c = mm(d_scores, b_low, TN) + mm(dyeb[...], st_ref[sub], NT)
        conv_back(rows, pairs, d_b, b_xc, b_s, b_act)
        conv_back(rows, pairs + 1, d_c, c_xc, c_s, c_act)
        ended = jnp.zeros((1, LANES), f32)
        for p in range(pairs):
            cols = slice(p * LANES, (p + 1) * LANES)
            last = jnp.where(
                low_half[0:1], decay[T - 1 : T, 2 * p : 2 * p + 1], decay[T - 1 : T, 2 * p + 1 : 2 * p + 2]
            )
            fade = jnp.exp(last)
            before_ds = dstate[:, cols]
            through = jnp.sum(before_ds * st_ref[sub, :, cols].astype(f32), axis=0, keepdims=True) * fade
            ended = ended + mm_exact(through, pick_ref[cols, :].astype(f32))
            dstate[:, cols] = fade * before_ds + mm(c_t, dyeb[:, cols])
        gin_heads = mm(gin[...], pick_ref[...])
        gout_heads = mm(gout[...], pick_ref[...])
        reached = (
            turn[...].T
            + mm_exact(upper, gin_heads)
            + mm_exact(strict, gout_heads, TN)
            + ended
        )
        d_raw = (head_ref[1:2, :] * reached + mm(xdu[...], pick_ref[...])) * sigmoid(raw)
        d_ref[rows, wide:] = d_raw.astype(bf16)
        hacc[0] += jnp.sum(d_raw.reshape(T // 8, 8, LANES), axis=0)
        hacc[1] += jnp.sum((dt * reached).reshape(T // 8, 8, LANES), axis=0)
        dxh[T : T + 8, :] = dxh[0:8, :]
        if sub == 1:
            @pl.when(step == 0)
            def _():
                for way in (0, 1):
                    hop(1, way, 0).start()

            ring_poll(1)

    @pl.when(step == steps - 1)
    def _():
        total = lambda a: jnp.sum(a, axis=0, keepdims=True)
        for k in range(CONV + 1):
            small_ref[k : k + 1, :] = total(acc[k])
        small_ref[CONV + 1 : CONV + 2, :width] = total(gate_ref[...])
        small_ref[CONV + 1 : CONV + 2, width : width + LANES] = total(hacc[0])
        small_ref[CONV + 1 : CONV + 2, width + LANES :] = total(hacc[1]) * head_ref[1:2, :]
        small_ref[CONV + 2 :, :] = jnp.zeros((2, wide), f32)
        skip = mm_exact(acc[CONV + 1, :, :width], pick_ref[...].astype(f32))
        small_ref[CONV + 3 : CONV + 4, 512 : 512 + LANES] = total(skip)
        for part in (0, 1):
            over_copy(part).wait_recv()

            def some(i, _, part=part):
                at = span(part * half + i * 32, 32)
                obranch_ref[at, :] = obranch_ref[at, :] + over_slot[part, span(i * 32, 32), :].astype(f32)
                return 0

            lax.fori_loop(0, half // 32, some, 0)
        for part in (0, 1):
            over_copy(part).wait_send()
            for turned in (0, 1):
                near_copy(turned, part).wait_send()
        for h in range(n - 1):
            for k in (0, 1):
                for way in (0, 1):
                    hop(k, way, h).wait_send()


def ssd_backward(n, dy, v, xc, dr, st, gate, taps, head, chan, early, branch):
    length, width = dy.shape
    wide = width + 2 * NS
    steps = length // ROWS
    subs = ROWS // T
    own_rows, tokens = D // n, length // 4
    half = tokens // 2
    row = lambda m: pl.BlockSpec((ROWS, m), lambda i: (steps - 1 - i, 0))
    whole = lambda a: pl.BlockSpec(a.shape, lambda i: (0,) * a.ndim, pipeline_mode=pl.Buffered(1))
    fixed = lambda *shape: pl.BlockSpec(shape, lambda i: (0,) * len(shape))
    anywhere = pl.BlockSpec(memory_space=pl.ANY)
    vm, dma = pltpu.VMEM, pltpu.SemaphoreType.DMA
    return pl.pallas_call(
        functools.partial(backward_body, n, own_rows, tokens, width),
        grid=(steps,),
        in_specs=[
            row(width), row(wide), row(wide), row(LANES),
            pl.BlockSpec((subs, NS, width), lambda i: (steps - 1 - i, 0, 0)),
            whole(gate), whole(taps), whole(head), whole(chan), anywhere, anywhere,
        ],
        out_specs=[
            row(wide + LANES), fixed(8, wide), fixed(own_rows, 2 * width), fixed(tokens, D),
        ],
        out_shape=[
            jax.ShapeDtypeStruct((length, wide + LANES), bf16),
            jax.ShapeDtypeStruct((8, wide), f32),
            jax.ShapeDtypeStruct((own_rows, 2 * width), f32),
            jax.ShapeDtypeStruct((tokens, D), f32),
        ],
        scratch_shapes=[
            vm((T + 8, wide), f32), vm((NS, width), f32), vm((T, width), f32), vm((T, width), f32),
            vm((T, width), bf16), vm((T, width), bf16), vm((T, width), bf16), vm((T, width), bf16),
            vm((T, width), bf16), vm((T, LANES), f32), vm((CONV + 2, 8, wide), f32), vm((2, 8, LANES), f32),
            vm((width, LANES), bf16),
            vm((D, 2 * width), bf16),
            [[vm((n - 1, size, width), bf16) for _ in (0, 1)] for _, size in cut_rows(own_rows)],
            vm((2, 2, half, D), bf16), vm((2, 2, half, D), bf16), vm((2, half, D), bf16),
            dma((5,)), dma((2, 2, n - 1)), dma((2, 2, n - 1)), dma((2, 2)), dma((2, 2)), dma((2,)), dma((2,)),
        ],
        compiler_params=pltpu.CompilerParams(
            collective_id=3, has_side_effects=True, vmem_limit_bytes=ROOM
        ),
        name="layer_backward",
    )(dy, v, xc, dr, st, gate, taps, head, chan, early, branch)


def reduce_body(
    n, rows, tokens, starts,
    xt_ref, d_ref, dz_ref, wp_ref, w_ref, small_ref, flat_ref, gain_ref,
    oxs_ref, oback_ref, bc_ref, oflat_ref,
    xt, d, dz, wz, w, work, grads, slots, staged, near, over, smalls, tens, bc_slot,
    load_sem, ring_send, ring_recv, near_send, near_recv, over_send, over_recv,
    small_send, small_recv, ten_send, ten_recv, bc_send, bc_recv,
):
    pos, ring, me, across, beside = neighbours(n)
    cuts = cut_rows(rows)
    core = lax.rem(me, 2)
    opposite = lax.rem(me + 2, 4)
    next_door = me + 1 - 2 * core
    far = lax.rem(next_door + 2, 4)
    half = tokens // 2
    late = d.shape[1]
    width = dz.shape[1]
    rest_of_z = width - Z_EARLY
    tile = 2 * LANES
    tiles = D // tile
    columns = [pl.ds(lo, hi - lo) for lo, hi in starts]
    sources = [(d_ref.at[:, columns[0]], d.at[:, columns[0]])]
    sources += [(xt_ref.at[pl.ds(i * tile, tile)], xt.at[pl.ds(i * tile, tile)]) for i in range(tiles)]
    sources += [(d_ref.at[:, some], d.at[:, some]) for some in columns[1:]]
    sources += [
        (dz_ref, dz), (w_ref.at[:, pl.ds(0, late)], w),
        (w_ref.at[:, pl.ds(late, Z_EARLY)], wz.at[:, pl.ds(0, Z_EARLY)]),
        (wp_ref.at[:, pl.ds(width, rest_of_z)], wz.at[:, pl.ds(Z_EARLY, rest_of_z)]),
        (small_ref, smalls.at[pos]),
    ]
    loads = [pltpu.make_async_copy(src, dst, load_sem.at[k]) for k, (src, dst) in enumerate(sources)]
    for load in loads:
        load.start()
    enter((*ring, across, beside))
    started = []

    def go(*args):
        copy = remote(*args)
        copy.start()
        started.append(copy)

    def block_at(way, count):
        return ring_index(lax.rem(pos + (count if way else n - count), n), n)

    def hop(k, way, h):
        lo, hi = starts[k]
        first, size = cuts[way]
        if h == 0:
            src = grads.at[span(block_at(way, 1) * rows + first, size), pl.ds(lo, hi - lo)]
        else:
            src = slots[way][k].at[h - 1]
        return remote(
            src, slots[way][k].at[h], ring_send.at[way, k, h], ring_recv.at[way, k, h], ring[way]
        )

    def product(k):
        lo, hi = starts[k]

        def some(i, _):
            if k == 0:
                rows_at = span(i * tile, tile)
                pltpu.make_async_copy(xt_ref.at[rows_at], xt.at[rows_at], load_sem.at[1 + i]).wait()
            at = span(i * tile, tile)
            grads[at, lo:hi] = mm(xt[at, :], d[:, lo:hi]).astype(bf16)
            return 0

        loads[0 if k == 0 else tiles + k].wait()
        lax.fori_loop(0, tiles, some, 0)
        for way in (0, 1):
            hop(k, way, 0).start()

    def near_copy(turned, part):
        return remote(
            staged.at[turned, part], near.at[turned, part],
            near_send.at[turned, part], near_recv.at[turned, part], beside,
        )

    def over_copy(part):
        return remote(near.at[0, part], over.at[part], over_send.at[part], over_recv.at[part], across)

    def ring_turn(k, h):
        lo, hi = starts[k]
        for way in (0, 1):
            first, size = cuts[way]
            slot = slots[way][k].at[h]
            remote(slot, slot, ring_send.at[way, k, h], ring_recv.at[way, k, h], ring[way]).wait_recv()
            block = block_at(way, 2 + h) if h < n - 2 else block_at(way, 0)

            tile = strip(size)

            def some(i, _, way=way, first=first, block=block, tile=tile):
                came = slots[way][k][h, span(i * tile, tile), :]
                mine = grads[span(block * rows + first + i * tile, tile), lo:hi]
                if h < n - 2:
                    slots[way][k][h, span(i * tile, tile), :] = came + mine
                else:
                    oxs_ref[span(first + i * tile, tile), lo:hi] = came.astype(f32) + mine.astype(f32)
                return 0

            lax.fori_loop(0, size // tile, some, 0)
            if h < n - 2:
                hop(k, way, h + 1).start()

    def small_hop(way, h):
        here = smalls.at[lax.rem(pos + (h if way else n - h), n)]
        go(here, here, small_send.at[way, h], small_recv.at[way, h], ring[way])

    def small_lands(way, h):
        here = smalls.at[lax.rem(pos + (h + 1 if way else n - h - 1), n)]
        remote(here, here, small_send.at[way, h], small_recv.at[way, h], ring[way]).wait_recv()

    for k in range(len(starts)):
        product(k)
    for load in loads[tiles + len(starts) :]:
        load.wait()
    turns = {0: [(0, 0)], 1: [(1, 0), (2, 0)], 2: [(0, 1)], 3: [(1, 1), (2, 1)], 4: [(0, 2)], 5: [(1, 2), (2, 2)], 6: [(0, 3)], 7: [(1, 3), (2, 3)]}
    taken = [sum(k == group for some in turns.values() for k, _ in some) for group in range(len(starts))]

    def block(i, _):
        which, part = lax.div(i, 2), lax.rem(i, 2)
        own = lax.rem(which, 2)
        turned = lax.div(which, 2)
        target = lax.rem(next_door + own * (me - next_door) + 2 * (1 - turned), 4)
        at = span(target * tokens + part * half, half)
        total = mm(dz[at, :], wz[...], NT) + mm(d[at, :], w[...], NT)
        work[...] = total

        @pl.when(own == 0)
        def _():
            staged[turned, part] = work[...].astype(bf16)
            near_copy(turned, part).start()

        @pl.when(own == 1)
        def _():
            near_copy(turned, part).wait_recv()

        @pl.when(which == 1)
        def _():
            near[0, part] = (work[...] + near[0, part].astype(f32)).astype(bf16)
            over_copy(part).start()

        @pl.when(which == 3)
        def _():
            oback_ref[span(part * half, half), :] = work[...] + near[1, part].astype(f32)

        for at_block, some in turns.items():

            @pl.when(i == at_block)
            def _(some=some):
                for k, h in some:
                    ring_turn(k, h)

        return 0

    lax.fori_loop(0, 8, block, 0)
    for i in range(tiles):
        share = jnp.zeros((tile, LANES), f32)
        for c in range(late // LANES):
            cols = slice(c * LANES, (c + 1) * LANES)
            at = slice(i * tile, (i + 1) * tile)
            share = share + grads[at, cols].astype(f32) * w[at, cols].astype(f32)
        total = mm_exact(jnp.ones((8, LANES), f32), share, NT)[0:1] + gain_ref[0:1, i * tile : (i + 1) * tile]
        for c in range(2 * i, 2 * i + 2):
            row, col = 6 + c // 8, (c % 8) * LANES
            part = total[:, (c - 2 * i) * LANES : (c - 2 * i + 1) * LANES]
            smalls[pos, row : row + 1, col : col + LANES] = part / flat_ref[c : c + 1, :]

    rest = [(k, h) for h in range(n - 1) for k in (0, 1, 2) if h >= taken[k]]
    rest.sort(key=lambda turn: turn[1] - taken[turn[0]])

    def small_step(s):
        for way in (0, 1):
            if s > 0 and (way == 0 or s < n // 2):
                small_lands(way, s - 1)
            if s < n // 2 - way:
                small_hop(way, s)

    small_step(0)
    steps_done = 1
    for at, (k, h) in enumerate(rest):
        ring_turn(k, h)
        if (k, h) == (0, n - 2):
            bc_slot[0] = oxs_ref[:, starts[0][0] : starts[0][0] + 2 * NS]
            go(bc_slot.at[0], bc_slot.at[1], bc_send.at[0], bc_recv.at[0], beside)
        if at % 2 == 1 and steps_done < n // 2:
            small_step(steps_done)
            steps_done += 1
    for s in range(steps_done, n // 2):
        small_step(s)
    small_lands(0, n // 2 - 1)

    total = smalls[0]
    for i in range(1, n):
        total = total + smalls[i]
    tens[me] = total
    go(tens.at[me], tens.at[me], ten_send.at[0], ten_recv.at[0], beside)
    remote(bc_slot.at[1], bc_slot.at[1], bc_send.at[0], bc_recv.at[0], beside).wait_recv()
    bc_slot[2] = bc_slot[0] + bc_slot[1]
    go(bc_slot.at[2], bc_slot.at[3], bc_send.at[1], bc_recv.at[1], across)
    here = tens.at[next_door]
    remote(here, here, ten_send.at[0], ten_recv.at[0], beside).wait_recv()
    for k, target in ((0, me), (1, next_door)):
        here = tens.at[target]
        go(here, here, ten_send.at[1 + k], ten_recv.at[1 + k], across)
    for part in (0, 1):
        over_copy(part).wait_recv()

        def some(i, _, part=part):
            at = span(part * half + i * 32, 32)
            oback_ref[at, :] = oback_ref[at, :] + over[part, span(i * 32, 32), :].astype(f32)
            return 0

        lax.fori_loop(0, half // 32, some, 0)
    for k, target in ((0, opposite), (1, far)):
        here = tens.at[target]
        remote(here, here, ten_send.at[1 + k], ten_recv.at[1 + k], across).wait_recv()
    flat_gradients(width, tens, oflat_ref)
    remote(bc_slot.at[3], bc_slot.at[3], bc_send.at[1], bc_recv.at[1], across).wait_recv()
    bc_ref[...] = bc_slot[2] + bc_slot[3]
    for part in (0, 1):
        over_copy(part).wait_send()
        for turned in (0, 1):
            near_copy(turned, part).wait_send()
    for k in range(len(starts)):
        for way in (0, 1):
            for h in range(n - 1):
                hop(k, way, h).wait_send()
    for copy in started:
        copy.wait_send()


def flat_gradients(width, tens, out_ref):
    pairs = width // LANES
    heads = width // P_SIZE

    def sums(row, col):
        total = tens[0, row : row + 1, col : col + LANES]
        for t in range(1, 4):
            total = total + tens[t, row : row + 1, col : col + LANES]
        return total

    def put(row, value):
        out_ref[row : row + 1, :] = value

    for c in range(D // LANES):
        put(c, sums(6 + c // 8, (c % 8) * LANES))
    for t in range(4):
        for c in range(pairs):
            cols = slice(c * LANES, (c + 1) * LANES)
            put(GATE_ROW + pairs * t + c, tens[t, CONV + 1 : CONV + 2, cols])
            put(BIAS_ROW + pairs * t + c, tens[t, CONV : CONV + 1, cols])
            for k in range(CONV):
                put(TAPS_ROW + 4 * pairs * k + pairs * t + c, tens[t, k : k + 1, cols])
    for c in range(2):
        put(BIAS_BC_ROW + c, sums(CONV, width + c * LANES))
        for k in range(CONV):
            put(TAPS_BC_ROW + 2 * k + c, sums(k, width + c * LANES))
    kinds = ((CONV + 1, width), (CONV + 1, width + LANES), (CONV + 3, 512))
    rows = [tens[t, row : row + 1, col : col + LANES] for row, col in kinds for t in range(4)]
    rows = jnp.concatenate(rows + [jnp.zeros((16 - len(rows), LANES), f32)], axis=0)
    lane = lax.broadcasted_iota(jnp.int32, (LANES, 2 * LANES), 1)
    entry = lax.broadcasted_iota(jnp.int32, (LANES, 2 * LANES), 0)
    spread_out = mm_exact(rows, jnp.where(lax.rem(lane, heads) == entry, 1.0, 0.0).astype(f32))
    at = lax.broadcasted_iota(jnp.int32, (16, 2 * LANES), 1)
    source = lax.broadcasted_iota(jnp.int32, (16, 2 * LANES), 0)
    line = jnp.sum(jnp.where(lax.div(at, heads) == source, spread_out, 0.0), axis=0, keepdims=True)
    put(HEAD_ROW, line[:, :LANES])
    put(HEAD_ROW + 1, line[:, LANES:])


def reduce_all(n, xt, d, dz, wp, w, small, flat, gain):
    rows, tokens = D // n, dz.shape[0] // 4
    width, late = dz.shape[1], d.shape[1]
    starts = ((width, late), (0, width // 2), (width // 2, width))
    half = tokens // 2
    dma, vm = pltpu.SemaphoreType.DMA, pltpu.VMEM
    anywhere = pl.BlockSpec(memory_space=pl.ANY)
    inside = pl.BlockSpec(memory_space=pltpu.VMEM)
    return pl.pallas_call(
        functools.partial(reduce_body, n, rows, tokens, starts),
        in_specs=[anywhere] * 6 + [inside] * 2,
        out_specs=[inside] * 4,
        out_shape=[
            jax.ShapeDtypeStruct((rows, late), f32),
            jax.ShapeDtypeStruct((tokens, D), f32),
            jax.ShapeDtypeStruct((rows, 2 * NS), f32),
            jax.ShapeDtypeStruct((FLAT_ROWS, LANES), f32),
        ],
        scratch_shapes=[
            vm(xt.shape, bf16), vm(d.shape, bf16), vm(dz.shape, bf16), vm((D, width), bf16),
            vm((D, late), bf16),
            vm((half, D), f32), vm((D, late), bf16),
            [[vm((n - 1, size, hi - lo), bf16) for lo, hi in starts] for _, size in cut_rows(rows)],
            vm((2, 2, half, D), bf16), vm((2, 2, half, D), bf16), vm((2, half, D), bf16),
            vm((n, *small.shape), f32), vm((4, *small.shape), f32), vm((4, rows, 2 * NS), f32),
            dma((14,)), dma((2, 3, n - 1)), dma((2, 3, n - 1)), dma((2, 2)), dma((2, 2)), dma((2,)), dma((2,)),
            dma((2, n // 2)), dma((2, n // 2)), dma((3,)), dma((3,)), dma((2,)), dma((2,)),
        ],
        compiler_params=pltpu.CompilerParams(
            collective_id=1, has_side_effects=True, vmem_limit_bytes=ROOM
        ),
        name="reduce_all",
    )(xt, d, dz, wp, w, small, flat, gain)


def adamw_step(weight, first, second, grad, rate, decay):
    first_new = beta_first * first + (1.0 - beta_first) * grad
    second_new = beta_second * second + (1.0 - beta_second) * grad * grad
    hat_first = first_new / (1.0 - beta_first**STEP)
    hat_second = second_new / (1.0 - beta_second**STEP)
    weight_new = weight - rate * (hat_first / (jnp.sqrt(hat_second) + adam_eps) + decay * weight)
    return (weight_new, first_new, second_new)


def finish_body(
    width, heads,
    in_ref, cot_ref, branch_ref, back_ref, flat_ref, early_ref, late_ref, bcg_ref,
    zx_ref, zx1_ref, zx2_ref, bc_ref, bc1_ref, bc2_ref, out_ref, out1_ref, out2_ref, late_all_ref, dt_ref, dt1_ref, dt2_ref,
    layer_ref, grad_ref, zxn_ref, zx1n_ref, zx2n_ref, bcn_ref, bc1n_ref, bc2n_ref,
    outn_ref, out1n_ref, out2n_ref, dtn_ref, dt1n_ref, dt2n_ref,
):
    def update(refs, news, grad):
        fresh = adamw_step(*(ref[...] for ref in refs), grad, matrix_rate, matrix_decay)
        for ref, value in zip(news, fresh):
            ref[...] = value

    for k, grad in ((0, early_ref), (1, late_ref)):
        fresh = adamw_step(
            *(ref[:, k, :] for ref in (zx_ref, zx1_ref, zx2_ref)), grad[:, :width], matrix_rate, matrix_decay
        )
        for ref, value in zip((zxn_ref, zx1n_ref, zx2n_ref), fresh):
            ref[:, k, :] = value
    update((bc_ref, bc1_ref, bc2_ref), (bcn_ref, bc1n_ref, bc2n_ref), bcg_ref[...])
    update((out_ref, out1_ref, out2_ref), (outn_ref, out1n_ref, out2n_ref), early_ref[:, width:])

    @pl.when(pl.program_id(0) == 0)
    def _():
        unit = jnp.where(
            lax.broadcasted_iota(jnp.int32, (16, LANES), 0) == lax.broadcasted_iota(jnp.int32, (16, LANES), 1), 1.0, 0.0
        ).astype(f32)
        turned = mm_exact(unit, late_all_ref[:, width + 2 * NS :], NT)
        update((dt_ref, dt1_ref, dt2_ref), (dtn_ref, dt1n_ref, dt2n_ref), turned[:heads])

    rows = in_ref.shape[0]
    tile = 64

    def some(i, _):
        at = span(i * tile, tile)
        squares = jnp.zeros((tile, LANES), f32)
        inner = jnp.zeros((tile, LANES), f32)
        for c in range(D // LANES):
            cols = slice(c * LANES, (c + 1) * LANES)
            x = in_ref[at, cols].astype(f32)
            squares = squares + x * x
            inner = inner + x * flat_ref[c : c + 1, :] * back_ref[at, cols]
        r = lax.rsqrt(jnp.sum(squares, axis=-1, keepdims=True) / D + norm_eps)
        k = r * r * r * jnp.sum(inner, axis=-1, keepdims=True) / D
        r, k = jnp.broadcast_to(r, (tile, LANES)), jnp.broadcast_to(k, (tile, LANES))
        for c in range(D // LANES):
            cols = slice(c * LANES, (c + 1) * LANES)
            x = in_ref[at, cols].astype(f32)
            layer_ref[at, cols] = (x + branch_ref[at, cols]).astype(bf16)
            grad_ref[at, cols] = cot_ref[at, cols].astype(f32) + r * flat_ref[c : c + 1, :] * back_ref[at, cols] - x * k
        return 0

    lax.fori_loop(0, rows // tile, some, 0)


def finish(layer_input, out_grad, branch, back, flat, early, late, bcg, zx, bc, out, dt):
    (rows, width), heads = out[0].shape, dt[0].shape[0]
    steps = 4 if rows % 32 == 0 else 2
    part = lambda a: pl.BlockSpec((a.shape[0] // steps, *a.shape[1:]), lambda i: (i,) + (0,) * (a.ndim - 1))
    whole = lambda a: pl.BlockSpec(a.shape, lambda i: (0,) * a.ndim)
    like = lambda a, dtype=f32: jax.ShapeDtypeStruct(a.shape, dtype)
    weights = (*zx, *bc, *out)
    return pl.pallas_call(
        functools.partial(finish_body, width, heads),
        grid=(steps,),
        in_specs=[
            *(part(a) for a in (layer_input, out_grad, branch, back)), whole(flat),
            *(part(a) for a in (early, late, bcg, *weights)), whole(late), *(whole(a) for a in dt),
        ],
        out_specs=[part(layer_input), part(back), *(part(a) for a in weights), *(whole(a) for a in dt)],
        out_shape=[like(layer_input, bf16), like(back), *(like(a) for a in weights), *(like(a) for a in dt)],
        compiler_params=pltpu.CompilerParams(vmem_limit_bytes=ROOM),
        name="finish",
    )(layer_input, out_grad, branch, back, flat, early, late, bcg, *weights, late, *dt)


def local(
    layer_input,
    out_grad,
    small_params,
    small_first,
    small_second,
    w_zx,
    zx_first,
    zx_second,
    w_bc,
    bc_first,
    bc_second,
    w_dt,
    dt_first,
    dt_second,
    w_out,
    out_first,
    out_second,
):
    n = lax.axis_size("dp")
    flat = jnp.pad(small_params, (0, FLAT_ROWS * LANES - small_params.shape[0])).reshape(FLAT_ROWS, LANES)
    xg, xt, w_all, w_pair = gather_all(n, layer_input, flat, w_zx, w_bc, w_dt.T, w_out)
    v, xc, dr, st, dy, dz, branch, early, gate, gain, pair_all, taps, head, chan = ssd_forward(
        n, xg, xt, w_all, flat, out_grad, w_pair
    )
    d_late, small, owner_early, own_branch = ssd_backward(
        n, dy, v, xc, dr, st, gate, taps, head, chan, early, branch
    )
    owner_late, d_normed_in, owner_bc, flat_grad = reduce_all(
        n, xt, d_late, dz, pair_all, w_all, small, flat, gain
    )
    small_grad = flat_grad.reshape(-1)[: small_params.shape[0]]
    small_new, small_first_new, small_second_new = adamw_step(
        small_params, small_first, small_second, small_grad, small_rate, 0.0
    )
    (
        layer_output, input_grad, zx_new, zx_first_new, zx_second_new, bc_new, bc_first_new, bc_second_new,
        out_new, out_first_new, out_second_new, dt_new, dt_first_new, dt_second_new,
    ) = finish(
        layer_input, out_grad, own_branch, d_normed_in, flat, owner_early, owner_late, owner_bc,
        (w_zx, zx_first, zx_second), (w_bc, bc_first, bc_second), (w_out, out_first, out_second),
        (w_dt.T, dt_first.T, dt_second.T),
    )
    dt_new, dt_first_new, dt_second_new = dt_new.T, dt_first_new.T, dt_second_new.T
    return (
        layer_output,
        input_grad,
        small_new,
        small_first_new,
        small_second_new,
        zx_new,
        zx_first_new,
        zx_second_new,
        bc_new,
        bc_first_new,
        bc_second_new,
        dt_new,
        dt_first_new,
        dt_second_new,
        out_new,
        out_first_new,
        out_second_new,
    )


def solution(mesh):
    return jax.shard_map(
        local,
        mesh=mesh,
        in_specs=(
            P(("dp", "tensor"), None),
            P(("dp", "tensor"), None),
            P(),
            P(),
            P(),
            P("dp", None, "tensor"),
            P("dp", None, "tensor"),
            P("dp", None, "tensor"),
            P("dp", None),
            P("dp", None),
            P("dp", None),
            P("dp", "tensor"),
            P("dp", "tensor"),
            P("dp", "tensor"),
            P("dp", "tensor"),
            P("dp", "tensor"),
            P("dp", "tensor"),
        ),
        out_specs=(
            P(("dp", "tensor"), None),
            P(("dp", "tensor"), None),
            P(),
            P(),
            P(),
            P("dp", None, "tensor"),
            P("dp", None, "tensor"),
            P("dp", None, "tensor"),
            P("dp", None),
            P("dp", None),
            P("dp", None),
            P("dp", "tensor"),
            P("dp", "tensor"),
            P("dp", "tensor"),
            P("dp", "tensor"),
            P("dp", "tensor"),
            P("dp", "tensor"),
        ),
        check_vma=False,
    )
```

```python
import functools

import jax
import jax.numpy as jnp
from jax import lax
from jax.experimental import pallas as pl
from jax.experimental.pallas import tpu as pltpu
from jax.sharding import PartitionSpec as P

D = 1536
DI = 3072
H = 48
NS = 128
P_SIZE = 64
CONV = 4
LEN = 2048
STEP = 10

T = 128
ROWS = 256
LANES = 128
ROOM = 60 * 2**20
Z_EARLY = 256

norm_eps = 1e-05
adam_eps = 1e-08
beta_first = 0.9
beta_second = 0.95
matrix_rate = 0.01
small_rate = 0.1
matrix_decay = 0.1

f32 = jnp.float32
bf16 = jnp.bfloat16
NN = (((1,), (0,)), ((), ()))
NT = (((1,), (1,)), ((), ()))
TN = (((0,), (0,)), ((), ()))
HIGHEST = lax.Precision.HIGHEST


GATE_ROW, TAPS_ROW, BIAS_ROW, TAPS_BC_ROW, BIAS_BC_ROW, HEAD_ROW, FLAT_ROWS = 12, 36, 132, 156, 164, 166, 168


def mm(a, b, dims=NN):
    return lax.dot_general(a, b, dims, preferred_element_type=f32)


def mm_exact(a, b, dims=NN):
    return lax.dot_general(a, b, dims, preferred_element_type=f32, precision=HIGHEST)


def sigmoid(v):
    return 0.5 * jnp.tanh(0.5 * v) + 0.5


def softplus(v):
    return jnp.maximum(v, 0.0) + jnp.log1p(jnp.exp(-jnp.abs(v)))


def spread(col):
    return jnp.broadcast_to(col, (T, LANES))


def block_iota(axis):
    return lax.broadcasted_iota(jnp.int32, (T, LANES), axis)


HEADS = 16
LOG2_E = 1.4426950408889634


def pieces(value, count):
    parts = []
    for k in range(count):
        part = value.astype(bf16)
        parts.append(part)
        if k < count - 1:
            value = value - part.astype(f32)
    return jnp.concatenate(parts, axis=1)


def columns_of(rows):
    return jnp.concatenate([rows, jnp.zeros((LANES - HEADS, T), f32)], axis=0).T


def set_heads(head_ref, head_t, until):
    turned = jnp.concatenate([head_ref[...], jnp.zeros((LANES - 8, LANES), f32)], axis=0).T
    head_t[0] = spread(turned[:, 0:1])[:HEADS]
    head_t[1] = spread(turned[:, 1:2])[:HEADS]
    matrix = jnp.where(block_iota(0) <= block_iota(1), 1.0, 0.0).astype(bf16)
    for k in range(3):
        until[k * T : (k + 1) * T, :] = matrix


def head_rows(dr_ref, head_t, until, rows):
    raw = dr_ref[rows, :].T[:HEADS] + head_t[0]
    dt = softplus(raw)
    decay = mm(pieces(dt * (head_t[1] * LOG2_E), 3), until[...])
    return raw, dt, decay, columns_of(dt), columns_of(decay)


def ring_place(n):
    me = lax.axis_index("dp")
    z, x = lax.div(me, 2), lax.rem(me, 2)
    return z + x * (n - 1 - 2 * z)


def ring_index(pos, n):
    back = lax.div(pos, n // 2)
    return 2 * pos + back * (2 * n - 1 - 4 * pos)


def neighbours(n):
    pos = ring_place(n)
    right = ring_index(lax.rem(pos + 1, n), n)
    left = ring_index(lax.rem(pos + n - 1, n), n)
    me = lax.axis_index("tensor")
    y, core = lax.div(me, 2), lax.rem(me, 2)
    across = 2 * (1 - y) + core
    beside = 2 * y + 1 - core
    return pos, ({"dp": right}, {"dp": left}), me, {"tensor": across}, {"tensor": beside}


def greet(peers):
    barrier = pltpu.get_barrier_semaphore()
    for peer in peers:
        pl.semaphore_signal(barrier, inc=1, device_id=peer, device_id_type=pl.DeviceIdType.MESH)


def enter(peers):
    greet(peers)
    pl.semaphore_wait(pltpu.get_barrier_semaphore(), len(peers))


def remote(src, dst, send_sem, recv_sem, peer):
    return pltpu.make_async_remote_copy(
        src_ref=src, dst_ref=dst, send_sem=send_sem, recv_sem=recv_sem,
        device_id=peer, device_id_type=pl.DeviceIdType.MESH,
    )


def span(start, size):
    return pl.ds(pl.multiple_of(start, 16), size)


def strip(rows):
    return next(size for size in (48, 32, 16) if rows % size == 0)


def cut_rows(rows):
    top = rows // 32 * 16
    return ((0, top), (top, rows - top))


def forward_body(
    n, rows, tokens, width,
    tall_ref, xt_ref, w_ref, flat_ref, cot_ref, wp_ref,
    v_ref, xc_ref, dr_ref, st_ref, dy_ref, dz_ref, branch_ref, early_ref, gate_ref, gain_ref, wps_ref,
    taps_ref, head_ref, chan_ref,
    halo, state, y_all, z_all, dn_all, nl_all, dz_all, cots, wps, sums, red, head_t, until, across_state, tails,
    own_keep, ring_keep, ring_send, ring_recv, over_send, over_recv,
    side_send, side_recv, pass_send, pass_recv, sum_send, sum_recv,
):
    pairs = width // LANES
    wide = width + 2 * NS
    step = pl.program_id(0)
    steps = LEN // ROWS
    tall = 2 * ROWS
    gating = steps
    forming = gating + LEN // tall
    products = forming + steps
    last_step = products + D // ROWS - 1
    pos, ring, me, across, beside = neighbours(n)
    opposite = lax.rem(me + 2, 4)
    next_door = me + 1 - 2 * lax.rem(me, 2)
    far = lax.rem(next_door + 2, 4)
    askew = {"tensor": far}
    quarter = tokens // 4
    hops = n // 2
    cuts = cut_rows(rows)
    mine = ring_index(pos, n)

    parts_of = ((0, width), (width, width - Z_EARLY))

    def hop(k, part, way, h):
        first, size = cuts[part]
        cols = pl.ds(*parts_of[k])
        block = ring_index(lax.rem(pos + (h if way else n - h), n), n)
        here = wps.at[span(block * rows + first, size), cols]
        src = wp_ref.at[pl.ds(first, size), cols] if h == 0 else here
        return remote(src, here, ring_send.at[way, part, k, h], ring_recv.at[way, part, k, h], ring[way])

    def hop_lands(k, part, way, h):
        first, size = cuts[part]
        block = ring_index(lax.rem(pos + (h + 1 if way else n - h - 1), n), n)
        return span(block * rows + first, size), pl.ds(*parts_of[k])

    def hop_arrival(k, part, way, h):
        here = wps.at[hop_lands(k, part, way, h)]
        return remote(here, here, ring_send.at[way, part, k, h], ring_recv.at[way, part, k, h], ring[way])

    def hop_keep(part, way, h):
        at = hop_lands(1, part, way, h)
        return pltpu.make_async_copy(wps.at[at], wps_ref.at[at], ring_keep.at[way, part, h])

    def hop_ways(h):
        return [(part, way) for part in (0, 1) for way in (0, 1) if h < hops - 1 or part == way]

    def hop_on(k, h):
        for part, way in hop_ways(h - 1) if h > 0 else ():
            hop_arrival(k, part, way, h - 1).wait_recv()
            if k == 1:
                hop_keep(part, way, h - 1).start()
            if h < hops and (part, way) in hop_ways(h):
                hop(k, part, way, h).start()
        if h == 0:
            for part, way in hop_ways(0):
                hop(k, part, way, 0).start()

    def over(k):
        return remote(
            cot_ref.at[pl.ds(k * quarter, quarter)], cots.at[span(me * tokens + k * quarter, quarter)],
            over_send.at[k], over_recv.at[k], across,
        )

    def landed(start, size, send, recv, peer):
        here = cots.at[span(start, size)]
        return remote(here, here, send, recv, peer)

    def over_arrival(k):
        return landed(opposite * tokens + k * quarter, quarter, over_send.at[k], over_recv.at[k], across)

    def passing(k):
        return landed(opposite * tokens + k * quarter, quarter, pass_send.at[k], pass_recv.at[k], beside)

    def pass_arrival(k):
        return landed(far * tokens + k * quarter, quarter, pass_send.at[k], pass_recv.at[k], beside)

    def side():
        return remote(cot_ref, cots.at[span(me * tokens, tokens)], side_send.at[0], side_recv.at[0], beside)

    def side_arrival():
        return landed(next_door * tokens, tokens, side_send.at[0], side_recv.at[0], beside)

    def own_keeps():
        z_cols = pl.ds(*parts_of[1])
        return (
            pltpu.make_async_copy(cot_ref, cots.at[span(me * tokens, tokens)], own_keep.at[0]),
            pltpu.make_async_copy(wp_ref, wps.at[span(mine * rows, rows)], own_keep.at[1]),
            pltpu.make_async_copy(wp_ref.at[:, z_cols], wps_ref.at[span(mine * rows, rows), z_cols], own_keep.at[2]),
        )

    def pass_on(*pieces):
        for k in pieces:
            over_arrival(k).wait_recv()
            passing(k).start()

    @pl.when(step == 0)
    def _():
        enter((*ring, across, beside, askew))
        hop_on(0, 0)
        over(0).start()
        over(1).start()
        side().start()
        for copy in own_keeps():
            copy.start()
        halo[0:8, :] = jnp.zeros((8, wide), f32)
        state[...] = jnp.zeros_like(state)
        parameter_rows(me, width, flat_ref, taps_ref, head_ref, chan_ref)
        set_heads(head_ref, head_t, until)
        gate_ref[...] = jnp.zeros_like(gate_ref)

    for h in range(1, hops):
        pl.when(step == min(2 * h, gating))(functools.partial(hop_on, 0, h))
    for h in range(hops):
        pl.when(step == min(2 * h + 1, gating))(functools.partial(hop_on, 1, h))
    for k in (1, 0):
        pl.when(step == gating)(functools.partial(hop_on, k, hops))

    @pl.when(step == 3)
    def _():
        over(2).start()

    @pl.when(step == 5)
    def _():
        over(3).start()
        pass_on(0, 1)

    pl.when(step == steps - 1)(functools.partial(pass_on, 2))

    @pl.when(step < gating)
    def _():
        scan_step(
            width, step, tall_ref, w_ref, taps_ref, head_ref, chan_ref,
            v_ref, xc_ref, dr_ref, st_ref, halo, state, y_all, head_t, until, across_state, tails,
            functools.partial(pass_on, 3),
        )

    @pl.when(step == gating)
    def _():
        side_arrival().wait_recv()
        for k in range(4):
            pass_arrival(k).wait_recv()
        for copy in own_keeps():
            copy.wait()

    @pl.when((step >= gating) & (step < forming))
    def _():
        first = (step - gating) * tall
        at = span(first, tall)
        z_all[at, :Z_EARLY] = mm(tall_ref[...], w_ref[:, wide + LANES :])
        z_all[at, Z_EARLY:] = mm(tall_ref[...], wps[:, width:])
        dn_all[at, :] = mm(cots[at, :], wps[:, :width])
        ones = jnp.ones((8, LANES), f32)
        for sub in range(tall // T):
            rows_at = span(first + sub * T, T)
            squares = jnp.zeros((T, LANES), f32)
            inner = jnp.zeros((T, LANES), f32)
            for p in range(pairs):
                cols = slice(p * LANES, (p + 1) * LANES)
                z = z_all[rows_at, cols]
                gated = y_all[rows_at, cols] * (z * sigmoid(z))
                squares = squares + gated * gated
                inner = inner + gated * chan_ref[0:1, cols] * dn_all[rows_at, cols]
            lanes = pl.ds(pl.multiple_of(first + sub * T, T), T)
            sums[me, 0:4, lanes] = mm_exact(ones, squares, NT)[0:4]
            sums[me, 4:8, lanes] = mm_exact(ones, inner, NT)[4:8]

    @pl.when(step == forming - 1)
    def _():
        peers = ((beside, next_door), (across, opposite), (askew, far))
        for k, (peer, _) in enumerate(peers):
            remote(sums.at[me], sums.at[me], sum_send.at[k], sum_recv.at[k], peer).start()
        for h in range(hops):
            for part, way in hop_ways(h):
                for k in (0, 1):
                    hop(k, part, way, h).wait_send()
                hop_keep(part, way, h).wait()
        side().wait_send()
        for k in range(4):
            over(k).wait_send()
            passing(k).wait_send()
        for k, (peer, other) in enumerate(peers):
            remote(sums.at[other], sums.at[other], sum_send.at[k], sum_recv.at[k], peer).wait()
        red[...] = ((sums[0] + sums[1]) + sums[2]) + sums[3]

    @pl.when((step >= forming) & (step < products))
    def _():
        first = (step - forming) * ROWS
        lanes = pl.ds(pl.multiple_of(first, ROWS), ROWS)
        q_row = lax.rsqrt(red[0:4, lanes] / DI + norm_eps)
        k_row = q_row * q_row * q_row * red[4:8, lanes] / DI
        turned = jnp.concatenate([q_row, k_row], axis=0).T
        for sub in range(ROWS // T):
            rows_at = slice(sub * T, (sub + 1) * T)
            at = span(first + sub * T, T)
            q, kk = spread(turned[rows_at, 0:1]), spread(turned[rows_at, 4:5])
            for p in range(pairs):
                cols = slice(p * LANES, (p + 1) * LANES)
                z, y, dn = z_all[at, cols], y_all[at, cols], dn_all[at, cols]
                gain = chan_ref[0:1, cols]
                s = sigmoid(z)
                sz = z * s
                gated = y * sz
                gq = gated * q
                dg = q * gain * dn - gated * kk
                gate_ref[:, cols] += jnp.sum((gq * dn).reshape(T // 8, 8, LANES), axis=0)
                nl_all[at, cols] = (gq * gain).astype(bf16)
                dz = (dg * y * (s + sz * (1.0 - s))).astype(bf16)
                dz_all[at, cols] = dz
                dz_ref[rows_at, cols] = dz
                dy_ref[rows_at, cols] = (dg * sz).astype(bf16)
        branch_ref[...] = mm(nl_all[span(first, ROWS), :], wps[:, :width], NT).astype(bf16)

    @pl.when(step >= products)
    def _():
        first = (step - products) * ROWS
        at = span(first, ROWS)
        lanes = pl.ds(pl.multiple_of(first, ROWS), ROWS)
        grad = mm(xt_ref[...], dz_all[...])
        early_ref[:, :width] = grad.astype(bf16)
        share = jnp.zeros((ROWS, LANES), f32)
        for p in range(pairs):
            cols = slice(p * LANES, (p + 1) * LANES)
            if p < Z_EARLY // LANES:
                w = w_ref[at, wide + (p + 1) * LANES : wide + (p + 2) * LANES]
            else:
                w = wps[at, width + p * LANES - Z_EARLY : width + (p + 1) * LANES - Z_EARLY]
            share = share + grad[:, cols] * w.astype(f32)
        gain_ref[:, lanes] = mm_exact(jnp.ones((8, LANES), f32), share, NT)
        early_ref[:, width:] = mm(cots[:, lanes], nl_all[...], TN).astype(bf16)


def parameter_rows(me, width, flat_ref, taps_ref, head_ref, chan_ref):
    pairs = width // LANES
    heads = width // P_SIZE
    taps_ref[...] = jnp.zeros_like(taps_ref)
    chan_ref[...] = jnp.zeros_like(chan_ref)
    for c in range(pairs):
        cols = slice(c * LANES, (c + 1) * LANES)
        chan_ref[0:1, cols] = flat_ref[pl.ds(GATE_ROW + pairs * me + c, 1), :]
        taps_ref[CONV : CONV + 1, cols] = flat_ref[pl.ds(BIAS_ROW + pairs * me + c, 1), :]
        for k in range(CONV):
            taps_ref[k : k + 1, cols] = flat_ref[pl.ds(TAPS_ROW + 4 * pairs * k + pairs * me + c, 1), :]
    for c in range(2):
        cols = slice(width + c * LANES, width + (c + 1) * LANES)
        taps_ref[CONV : CONV + 1, cols] = flat_ref[BIAS_BC_ROW + c : BIAS_BC_ROW + c + 1, :]
        for k in range(CONV):
            row = TAPS_BC_ROW + 2 * k + c
            taps_ref[k : k + 1, cols] = flat_ref[row : row + 1, :]
    both = jnp.concatenate([flat_ref[HEAD_ROW : HEAD_ROW + 1, :], flat_ref[HEAD_ROW + 1 : HEAD_ROW + 2, :]], axis=1)
    both = jnp.broadcast_to(both, (8, 2 * LANES))
    lane = lax.broadcasted_iota(jnp.int32, (2 * LANES, LANES), 0)
    head = lax.broadcasted_iota(jnp.int32, (2 * LANES, LANES), 1)

    def take(kind):
        match = (lane == 4 * heads * kind + heads * me + head) & (head < heads)
        return mm_exact(both, jnp.where(match, 1.0, 0.0).astype(f32))

    valid = lax.broadcasted_iota(jnp.int32, (8, LANES), 1) < heads
    row = lax.broadcasted_iota(jnp.int32, (8, LANES), 0)
    rates = jnp.where(valid, -jnp.exp(take(1)), 0.0)
    head_ref[...] = jnp.where(row == 0, take(0), jnp.where(row == 1, rates, 0.0))
    skip = mm_exact(take(2), picked(width).astype(f32), NT)
    chan_ref[1:2, :] = skip[0:1]


def picked(width):
    channel = lax.broadcasted_iota(jnp.int32, (width, LANES), 0)
    head = lax.broadcasted_iota(jnp.int32, (width, LANES), 1)
    return jnp.where((channel >= head * P_SIZE) & (channel < (head + 1) * P_SIZE), 1.0, 0.0).astype(bf16)


def scan_step(
    width, step, tall_ref, w_ref, taps_ref, head_ref, chan_ref,
    v_ref, xc_ref, dr_ref, st_ref, halo, state, y_all, head_t, until, across_state, tails, late_turn,
):
    pairs = width // LANES
    wide = width + 2 * NS
    mine = span(lax.rem(step, 2) * ROWS, ROWS)
    dr_ref[...] = mm(tall_ref[mine, :], w_ref[:, wide : wide + LANES])
    halo[8 : 8 + ROWS, :] = mm(tall_ref[mine, :], w_ref[:, :wide])
    low_half = block_iota(1) < P_SIZE
    causal = block_iota(0) >= block_iota(1)

    def convolved(sub, block):
        cols = slice(block * LANES, (block + 1) * LANES)
        total = taps_ref[CONV : CONV + 1, cols]
        for k in range(CONV):
            first = 8 - (CONV - 1) + k + sub * T
            total = total + taps_ref[k : k + 1, cols] * halo[first : first + T, cols]
        rows = slice(sub * T, (sub + 1) * T)
        xc_ref[rows, cols] = total.astype(bf16)
        v_ref[rows, cols] = halo[8 + sub * T : 8 + (sub + 1) * T, cols].astype(bf16)
        return total * sigmoid(total)

    for sub in range(ROWS // T):
        rows = slice(sub * T, (sub + 1) * T)
        _, _, decay_t, dt, decay = head_rows(dr_ref, head_t, until, rows)
        b_low = convolved(sub, pairs).astype(bf16)
        c_low = convolved(sub, pairs + 1).astype(bf16)
        b_t = b_low.T
        scores = jnp.where(causal, mm(c_low, b_low, NT), 0.0)
        st_ref[sub] = state[...].astype(bf16)
        across_state[...] = mm(c_low, st_ref[sub])
        for p in range(pairs):
            cols = slice(p * LANES, (p + 1) * LANES)
            x = convolved(sub, p)
            l1, l2 = spread(decay[:, 2 * p : 2 * p + 1]), spread(decay[:, 2 * p + 1 : 2 * p + 2])
            both = jnp.where(low_half, l1, l2)
            dtb = jnp.where(
                low_half, spread(dt[:, 2 * p : 2 * p + 1]), spread(dt[:, 2 * p + 1 : 2 * p + 2])
            )
            u = x * dtb
            m1 = scores * jnp.exp2(jnp.minimum(l1 - decay_t[2 * p : 2 * p + 1, :], 0.0))
            m2 = scores * jnp.exp2(jnp.minimum(l2 - decay_t[2 * p + 1 : 2 * p + 2, :], 0.0))
            mixing = jnp.concatenate([m1.astype(bf16), m2.astype(bf16)], axis=1)
            u_low = u.astype(bf16)
            zero = jnp.zeros_like(u_low)
            parts = jnp.concatenate(
                [jnp.where(low_half, u_low, zero), jnp.where(low_half, zero, u_low)], axis=0
            )
            last = both[T - 1 : T, :]
            y = mm(mixing, parts) + jnp.exp2(both) * across_state[:, cols] + chan_ref[1:2, cols] * x
            tails[:, cols] = (u * jnp.exp2(last - both)).astype(bf16)
            state[:, cols] = jnp.exp2(last) * state[:, cols]
            y_all[span(step * ROWS + sub * T, T), cols] = y
        state[...] = state[...] + mm(b_t, tails[...])
        if sub == 0:
            pl.when(step == LEN // ROWS - 1)(late_turn)
    halo[0:8, :] = halo[ROWS : ROWS + 8, :]


def ssd_forward(n, xg, xt, w, flat, cot, wp):
    length = xg.shape[0]
    rows, width = wp.shape[0], (wp.shape[1] + Z_EARLY) // 2
    tokens = cot.shape[0]
    wide = width + 2 * NS
    steps = length // ROWS
    tall = 2 * ROWS
    forming = steps + length // tall
    products = forming + steps
    subs = ROWS // T
    assert length == LEN
    early = lambda i: jnp.minimum(i, steps - 1)
    formed = lambda i: jnp.clip(i - forming, 0, steps - 1)
    late = lambda i: jnp.maximum(i - products, 0)
    tall_at = lambda i: jnp.where(i < steps, lax.div(i, 2), jnp.minimum(i - steps, length // tall - 1))
    row = lambda m: pl.BlockSpec((ROWS, m), lambda i: (early(i), 0))
    form = lambda m: pl.BlockSpec((ROWS, m), lambda i: (formed(i), 0))
    whole = lambda a: pl.BlockSpec(a.shape, lambda i: (0,) * a.ndim, pipeline_mode=pl.Buffered(1))
    fixed = lambda m: pl.BlockSpec((8, m), lambda i: (0, 0))
    anywhere = pl.BlockSpec(memory_space=pl.ANY)
    vm, dma = pltpu.VMEM, pltpu.SemaphoreType.DMA
    hops = dma((2, 2, 2, n // 2))
    shape = lambda dims, dtype: jax.ShapeDtypeStruct(dims, dtype)
    return pl.pallas_call(
        functools.partial(forward_body, n, rows, tokens, width),
        grid=(products + D // ROWS,),
        in_specs=[
            pl.BlockSpec((tall, D), lambda i: (tall_at(i), 0)),
            pl.BlockSpec((ROWS, length), lambda i: (late(i), 0)),
            whole(w), whole(flat), whole(cot), whole(wp),
        ],
        out_specs=[
            row(wide), row(wide), row(LANES), pl.BlockSpec((subs, NS, width), lambda i: (early(i), 0, 0)),
            form(width), form(width), form(D), pl.BlockSpec((ROWS, 2 * width), lambda i: (late(i), 0)),
            fixed(width), fixed(D), anywhere, *(fixed(m) for m in (wide, LANES, width)),
        ],
        out_shape=[
            shape((length, wide), bf16), shape((length, wide), bf16), shape((length, LANES), f32),
            shape((length // T, NS, width), bf16), shape((length, width), bf16), shape((length, width), bf16),
            shape((length, D), bf16), shape((D, 2 * width), bf16), shape((8, width), f32), shape((8, D), f32),
            shape((n * rows, 2 * width - Z_EARLY), bf16), *(shape((8, m), f32) for m in (wide, LANES, width)),
        ],
        scratch_shapes=[
            vm((ROWS + 8, wide), f32), vm((NS, width), f32), *(vm((length, width), f32) for _ in range(3)),
            vm((length, width), bf16), vm((length, width), bf16),
            vm((4 * tokens, D), bf16), vm((n * rows, 2 * width - Z_EARLY), bf16), vm((4, 8, length), f32),
            vm((8, length), f32), vm((2, HEADS, LANES), f32), vm((3 * T, LANES), bf16),
            vm((T, width), f32), vm((T, width), bf16),
            dma((3,)), dma((2, 2, n // 2)), hops, hops, dma((4,)), dma((4,)),
            dma((1,)), dma((1,)), dma((4,)), dma((4,)), dma((3,)), dma((3,)),
        ],
        compiler_params=pltpu.CompilerParams(collective_id=2, has_side_effects=True, vmem_limit_bytes=ROOM),
        name="layer_forward",
    )(xg, xt, w, flat, cot, wp)


def gather_body(
    n, rows, tokens,
    in_ref, flat_ref, wzx_ref, wbc_ref, wdt_ref, wout_ref, xg_ref, xt_ref, ws_ref, wp_ref, x_ref, w_ref, xg, xt, ws,
    keep_sem, turn_sem, ring_keep, ring_send, ring_recv, over_send, over_recv, side_send, side_recv, pass_send, pass_recv,
):
    pos, ring, me, across, beside = neighbours(n)
    greet((*ring, across, beside))
    quarter = tokens // 4
    width = wout_ref.shape[1]
    heads = wdt_ref.shape[0]
    late = width + 2 * NS + LANES
    w_ref[:, :width] = wzx_ref[:, 1, :].astype(bf16)
    w_ref[:, width : width + 2 * NS] = wbc_ref[...].astype(bf16)
    unit = jnp.where(
        lax.broadcasted_iota(jnp.int32, (16, LANES), 0) == lax.broadcasted_iota(jnp.int32, (16, LANES), 1), 1.0, 0.0
    ).astype(bf16)
    steps_w = jnp.concatenate([wdt_ref[...], jnp.zeros((16 - heads, rows), f32)], axis=0).astype(bf16)
    w_ref[:, width + 2 * NS : late] = mm(steps_w, unit, TN).astype(bf16)
    w_ref[:, late:] = wzx_ref[:, 0, :Z_EARLY].astype(bf16)

    def normalize(k):
        def some(i, _):
            at = span(k * quarter + i * 64, 64)
            squares = jnp.zeros((64, LANES), f32)
            for c in range(D // LANES):
                x = in_ref[at, c * LANES : (c + 1) * LANES].astype(f32)
                squares = squares + x * x
            inverse = lax.rsqrt(jnp.sum(squares, axis=-1, keepdims=True) / D + norm_eps)
            inverse = jnp.broadcast_to(inverse, (64, LANES))
            for c in range(D // LANES):
                cols = slice(c * LANES, (c + 1) * LANES)
                x_ref[at, cols] = (in_ref[at, cols].astype(f32) * inverse * flat_ref[c : c + 1, :]).astype(bf16)
            return 0

        lax.fori_loop(0, quarter // 64, some, 0)

    normalize(0)
    pl.semaphore_wait(pltpu.get_barrier_semaphore(), 4)
    started, kept = [], []

    def go(*args):
        copy = remote(*args)
        copy.start()
        started.append(copy)
        return copy

    def keep(src, dst, sem):
        copy = pltpu.make_async_copy(src, dst, sem)
        copy.start()
        kept.append(copy)

    opposite = lax.rem(me + 2, 4)
    next_door = me + 1 - 2 * lax.rem(me, 2)
    far = lax.rem(next_door + 2, 4)
    cuts = cut_rows(rows)

    def turned(src, start, first, size):
        sets = D // (4 * LANES)

        def some(i, _):
            row = first + lax.div(i, sets) * LANES
            at = span(row if src is x_ref else start + row, LANES)
            to = pl.ds(pl.multiple_of(start + row, LANES), LANES)
            for c in range(4):
                cols = pl.ds(pl.multiple_of((lax.rem(i, sets) * 4 + c) * LANES, LANES), LANES)
                xt[cols, to] = src[at, cols].T
            return 0

        lax.fori_loop(0, size // LANES * sets, some, 0)

    def keep_turned(k, block):
        at = pl.ds(pl.multiple_of(block * tokens, LANES), tokens)
        keep(xt.at[:, at], xt_ref.at[:, at], turn_sem.at[k])

    def arrived(part, way, step, block):
        first, size = cuts[part]
        at = span(block * rows + first, size)
        remote(
            ws.at[at], ws.at[at], ring_send.at[way, part, step], ring_recv.at[way, part, step], ring[way]
        ).wait_recv()
        keep(ws.at[at], ws_ref.at[at], ring_keep.at[way, part, step])

    def ring_step(step, parts=(0, 1)):
        last = step == n // 2 - 1
        for part in parts:
            first, size = cuts[part]
            for way in (0, 1):
                block = ring_index(lax.rem(pos + (step if way else n - step), n), n)
                here = ws.at[span(block * rows + first, size)]
                if step > 0:
                    arrived(part, way, step - 1, block)
                if last and part != way:
                    continue
                src = w_ref.at[pl.ds(first, size)] if step == 0 else here
                go(src, here, ring_send.at[way, part, step], ring_recv.at[way, part, step], ring[way])

    def send_over(k):
        go(
            x_ref.at[pl.ds(k * quarter, quarter)], xg.at[span(me * tokens + k * quarter, quarter)],
            over_send.at[k], over_recv.at[k], across,
        )

    def pass_on(k):
        at = span(opposite * tokens + k * quarter, quarter)
        here = xg.at[at]
        remote(here, here, over_send.at[k], over_recv.at[k], across).wait_recv()
        go(here, here, pass_send.at[k], pass_recv.at[k], beside)
        keep(here, xg_ref.at[at], keep_sem.at[k])

    def pass_lands(k):
        at = span(far * tokens + k * quarter, quarter)
        remote(xg.at[at], xg.at[at], pass_send.at[k], pass_recv.at[k], beside).wait_recv()
        keep(xg.at[at], xg_ref.at[at], keep_sem.at[4 + k])
        turned(xg, far * tokens, k * quarter, quarter)

    ring_step(0, (0,))
    leading = list(started)
    send_over(0)
    normalize(1)
    send_over(1)
    normalize(2)
    normalize(3)
    go(x_ref, xg.at[span(me * tokens, tokens)], side_send.at[0], side_recv.at[0], beside)
    wp_ref[:, :width] = wout_ref[...].astype(bf16)
    wp_ref[:, width:] = wzx_ref[:, 0, Z_EARLY:].astype(bf16)
    for copy in leading:
        copy.wait_send()
        started.remove(copy)
    ring_step(0, (1,))
    mine = ring_index(pos, n)
    keep(x_ref, xg_ref.at[span(me * tokens, tokens)], keep_sem.at[8])
    keep(w_ref, ws_ref.at[span(mine * rows, rows)], keep_sem.at[9])
    turned(x_ref, me * tokens, 0, tokens)
    keep_turned(0, me)
    ring_step(1)
    send_over(2)
    at = span(next_door * tokens, tokens)
    remote(xg.at[at], xg.at[at], side_send.at[0], side_recv.at[0], beside).wait_recv()
    keep(xg.at[at], xg_ref.at[at], keep_sem.at[10])
    turned(xg, next_door * tokens, 0, tokens)
    keep_turned(1, next_door)
    send_over(3)
    for step in range(2, n // 2):
        ring_step(step)
        if step == 2:
            pass_on(0)
            pass_on(1)
            turned(xg, opposite * tokens, 0, 2 * quarter)
    pass_on(2)
    pass_lands(0)
    pass_lands(1)
    pass_on(3)
    turned(xg, opposite * tokens, 2 * quarter, 2 * quarter)
    keep_turned(2, opposite)
    for part in (0, 1):
        arrived(part, part, n // 2 - 1, ring_index(lax.rem(pos + n // 2, n), n))
    pass_lands(2)
    pass_lands(3)
    keep_turned(3, far)
    for copy in kept:
        copy.wait()
    for copy in started:
        copy.wait_send()


def gather_all(n, layer_input, flat, w_zx, w_bc, w_dt, w_out):
    tokens, rows, width = layer_input.shape[0], w_bc.shape[0], w_out.shape[1]
    early = width + 2 * NS + LANES + Z_EARLY
    dma = pltpu.SemaphoreType.DMA
    anywhere = pl.BlockSpec(memory_space=pl.ANY)
    inside = pl.BlockSpec(memory_space=pltpu.VMEM)
    own = ((tokens, D), (rows, early))
    full = ((4 * tokens, D), (D, 4 * tokens), (n * rows, early))
    hops = dma((2, 2, n // 2))
    return pl.pallas_call(
        functools.partial(gather_body, n, rows, tokens),
        in_specs=[inside] * 6,
        out_specs=[anywhere, anywhere, anywhere, inside],
        out_shape=[jax.ShapeDtypeStruct(shape, bf16) for shape in (*full, (rows, 2 * width - Z_EARLY))],
        scratch_shapes=[
            *(pltpu.VMEM(shape, bf16) for shape in (*own, *full)),
            dma((11,)), dma((4,)), hops, hops, hops, dma((4,)), dma((4,)), dma((1,)), dma((1,)), dma((4,)), dma((4,)),
        ],
        compiler_params=pltpu.CompilerParams(collective_id=0, has_side_effects=True, vmem_limit_bytes=ROOM),
        name="gather_all",
    )(layer_input, flat, w_zx, w_bc, w_dt, w_out)


def backward_body(
    n, own_rows, tokens, width,
    dy_ref, v_ref, xc_ref, dr_ref, st_ref, gate_ref, taps_ref, head_ref, chan_ref, early_ref, branch_ref,
    d_ref, small_ref, oearly_ref, obranch_ref,
    dxh, dstate, yst, bds, dyeb, utb, products, turn, acc, hacc, pick_ref, pick_t, fades, head_t, until_ref, reach_ref,
    own, slots, near, held, over_slot,
    load_sem, ring_send, ring_recv, near_send, near_recv, over_send, over_recv,
):
    pairs = width // LANES
    wide = width + 2 * NS
    step = pl.program_id(0)
    steps = LEN // ROWS
    pos, ring, me, across, beside = neighbours(n)
    opposite = lax.rem(me + 2, 4)
    next_door = me + 1 - 2 * lax.rem(me, 2)
    far = lax.rem(next_door + 2, 4)
    half = tokens // 2
    cuts = cut_rows(own_rows)

    def block_at(way, count):
        return ring_index(lax.rem(pos + (count if way else n - count), n), n)

    def hop(k, way, h):
        first, size = cuts[way]
        if h == 0:
            src = early_ref.at[span(block_at(way, 1) * own_rows + first, size), pl.ds(k * width, width)]
        else:
            src = slots[way][k].at[h - 1]
        return remote(
            src, slots[way][k].at[h], ring_send.at[way, k, h], ring_recv.at[way, k, h], ring[way]
        )

    def near_copy(turned, part):
        start = (next_door if turned else far) * tokens + part * half
        return remote(
            branch_ref.at[span(start, half)], near.at[turned, part],
            near_send.at[turned, part], near_recv.at[turned, part], beside,
        )

    def held_copy(turned, part):
        start = (me if turned else opposite) * tokens + part * half
        return pltpu.make_async_copy(
            branch_ref.at[span(start, half)], held.at[turned, part], load_sem.at[2 * turned + part]
        )

    def over_copy(part):
        return remote(held.at[0, part], over_slot.at[part], over_send.at[part], over_recv.at[part], across)

    def own_copy():
        return pltpu.make_async_copy(early_ref, own, load_sem.at[4])

    def ring_turn(k, h):
        for way in (0, 1):
            first, size = cuts[way]
            hop(k, way, h).wait_recv()
            block = block_at(way, 2 + h) if h < n - 2 else block_at(way, 0)

            tile = strip(size)

            def some(i, _, way=way, first=first, block=block, tile=tile):
                cols = slice(k * width, (k + 1) * width)
                came = slots[way][k][h, span(i * tile, tile), :]
                mine = own[span(block * own_rows + first + i * tile, tile), cols]
                if h < n - 2:
                    slots[way][k][h, span(i * tile, tile), :] = came + mine
                else:
                    oearly_ref[span(first + i * tile, tile), cols] = came.astype(f32) + mine.astype(f32)
                return 0

            lax.fori_loop(0, size // tile, some, 0)
            if h < n - 2:
                hop(k, way, h + 1).start()

    def ring_poll(k):
        for h in range(n - 1):
            pl.when(step == min(h + 1, steps - 1))(functools.partial(ring_turn, k, h))

    def add_near(turned):
        for part in (0, 1):
            held_copy(turned, part).wait()
            near_copy(turned, part).wait_recv()

            def some(i, _, part=part):
                at = span(i * 32, 32)
                if turned:
                    total = held[1, part, at, :].astype(f32) + near[1, part, at, :].astype(f32)
                    obranch_ref[span(part * half + i * 32, 32), :] = total
                else:
                    held[0, part, at, :] = held[0, part, at, :] + near[0, part, at, :]
                return 0

            lax.fori_loop(0, half // 32, some, 0)
            if not turned:
                over_copy(part).start()

    @pl.when(step == 0)
    def _():
        enter((*ring, across, beside))
        for way in (0, 1):
            hop(0, way, 0).start()
        for turned in (0, 1):
            for part in (0, 1):
                near_copy(turned, part).start()
                held_copy(turned, part).start()
        own_copy().start()
        dxh[T : T + 8, :] = jnp.zeros((8, wide), f32)
        dstate[...] = jnp.zeros_like(dstate)
        acc[...] = jnp.zeros_like(acc)
        hacc[...] = jnp.zeros_like(hacc)
        turn[...] = jnp.zeros_like(turn)
        pick_ref[...] = picked(width)
        channel = lax.broadcasted_iota(jnp.int32, (HEADS, width), 1)
        head = lax.broadcasted_iota(jnp.int32, (HEADS, width), 0)
        mine = (channel >= head * P_SIZE) & (channel < (head + 1) * P_SIZE)
        pick_t[...] = jnp.where(mine, 1.0, 0.0).astype(bf16)
        set_heads(head_ref, head_t, until_ref)
        from_here = jnp.where(block_iota(0) >= block_iota(1), 1.0, 0.0).astype(bf16)
        after = jnp.where(block_iota(0) < block_iota(1), 1.0, 0.0).astype(bf16)
        for k, matrix in enumerate((from_here, from_here, after, after)):
            reach_ref[k * T : (k + 1) * T, :] = matrix
        products[3 * T :, :] = jnp.zeros((HEADS, width), bf16)

    @pl.when(step == 1)
    def _():
        own_copy().wait()
        add_near(0)

    pl.when(step == 2)(functools.partial(add_near, 1))
    ring_poll(0)

    low_half = block_iota(1) < P_SIZE
    row_at, col_at = block_iota(0), block_iota(1)
    until = row_at <= col_at
    pair_lane = lax.broadcasted_iota(jnp.int32, (8, 2 * T), 1)
    pair_row = lax.broadcasted_iota(jnp.int32, (8, 2 * T), 0)
    each = jnp.where(lax.div(pair_lane, T) == pair_row, 1.0, 0.0).astype(bf16)
    ones = jnp.ones((8, T), bf16)

    def add(index, cols, value):
        acc[index, :, cols] += jnp.sum(value.reshape(T // 8, 8, LANES), axis=0)

    def conv_back(rows, block, d_act, xc, s, act):
        cols = slice(block * LANES, (block + 1) * LANES)
        dxh[0:T, cols] = d_act * (s + act * (1.0 - s))
        v = v_ref[rows, cols].astype(f32)
        total = None
        for m in range(CONV):
            moved = dxh[m : m + T, cols]
            if m == 0:
                add(CONV, cols, moved)
            add(CONV - 1 - m, cols, v * moved)
            term = taps_ref[CONV - 1 - m : CONV - m, cols] * moved
            total = term if total is None else total + term
        d_ref[rows, cols] = total.astype(bf16)

    for sub in reversed(range(ROWS // T)):
        rows = slice(sub * T, (sub + 1) * T)
        raw_t, dt_t, decay_t, dt, decay = head_rows(dr_ref, head_t, until_ref, rows)
        b_cols = slice(width, width + NS)
        c_cols = slice(width + NS, width + 2 * NS)
        b_xc, c_xc = xc_ref[rows, b_cols].astype(f32), xc_ref[rows, c_cols].astype(f32)
        b_s, c_s = sigmoid(b_xc), sigmoid(c_xc)
        b_act, c_act = b_xc * b_s, c_xc * c_s
        b_low, c_low = b_act.astype(bf16), c_act.astype(bf16)
        c_t = c_low.T
        scores_t = jnp.where(until, mm(b_low, c_low, NT), 0.0)
        ds_low = dstate[...].astype(bf16)
        yst[...] = mm(c_low, st_ref[sub])
        bds[...] = mm(b_low, ds_low)
        d_scores = jnp.zeros((T, LANES), f32)
        for p in range(pairs):
            cols = slice(p * LANES, (p + 1) * LANES)
            dy_low = dy_ref[rows, cols]
            dy = dy_low.astype(f32)
            xc = xc_ref[rows, cols].astype(f32)
            xs = sigmoid(xc)
            x = xc * xs
            l1, l2 = spread(decay[:, 2 * p : 2 * p + 1]), spread(decay[:, 2 * p + 1 : 2 * p + 2])
            both = jnp.where(low_half, l1, l2)
            dtb = jnp.where(
                low_half, spread(dt[:, 2 * p : 2 * p + 1]), spread(dt[:, 2 * p + 1 : 2 * p + 2])
            )
            u = x * dtb
            last = both[T - 1 : T, :]
            e1 = jnp.exp2(jnp.minimum(decay_t[2 * p : 2 * p + 1, :] - l1, 0.0))
            e2 = jnp.exp2(jnp.minimum(decay_t[2 * p + 1 : 2 * p + 2, :] - l2, 0.0))
            zero = jnp.zeros_like(dy_low)
            dy_parts = jnp.concatenate(
                [jnp.where(low_half, dy_low, zero), jnp.where(low_half, zero, dy_low)], axis=0
            )
            du_in = mm(
                jnp.concatenate([(scores_t * e1).astype(bf16), (scores_t * e2).astype(bf16)], axis=1), dy_parts
            )
            d_mix = mm(u.astype(bf16), dy_parts, NT)
            d1, d2 = d_mix[:, :T] * e1, d_mix[:, T:] * e2
            d_scores = d_scores + d1 + d2
            held_pairs = jnp.concatenate([(d1 * scores_t).astype(bf16), (d2 * scores_t).astype(bf16)], axis=1)
            reached_by = mm(ones, held_pairs)
            leaving = mm(each, held_pairs, NT)
            turn[2 * p : 2 * p + 1, :] = reached_by[0:1, :T] - leaving[0:1]
            turn[2 * p + 1 : 2 * p + 2, :] = reached_by[0:1, T:] - leaving[1:2]
            tail = jnp.exp2(last - both)
            fades[0:1, cols] = jnp.exp2(last)
            dye = dy * jnp.exp2(both)
            du_out = tail * bds[:, cols]
            du = du_in + du_out
            products[0:T, cols] = (dye * yst[:, cols]).astype(bf16)
            products[T : 2 * T, cols] = (u * du_out).astype(bf16)
            products[2 * T : 3 * T, cols] = (x * du).astype(bf16)
            dyeb[:, cols] = dye.astype(bf16)
            utb[:, cols] = (u * tail).astype(bf16)
            add(CONV + 1, cols, dy * x)
            conv_back(rows, p, dtb * du + chan_ref[1:2, cols] * dy, xc, xs, x)
        d_scores = jnp.where(until, d_scores, 0.0).astype(bf16)
        d_b = mm(d_scores, c_low) + mm(utb[...], ds_low, NT)
        d_c = mm(d_scores, b_low, TN) + mm(dyeb[...], st_ref[sub], NT)
        conv_back(rows, pairs, d_b, b_xc, b_s, b_act)
        conv_back(rows, pairs + 1, d_c, c_xc, c_s, c_act)
        fade = fades[0:1, :]
        before_ds = dstate[...]
        through = jnp.sum(before_ds * st_ref[sub].astype(f32), axis=0, keepdims=True) * fade
        products[3 * T : 3 * T + HEADS, :] = jnp.broadcast_to(through, (HEADS, width)).astype(bf16)
        dstate[...] = fade * before_ds + mm(c_t, dyeb[...])
        by_head = mm(pick_t[...], products[...], NT)
        inside = pieces(turn[...] + by_head[:, :T], 2)
        outside = pieces(by_head[:, T : 2 * T], 2)
        reached = mm(jnp.concatenate([inside, outside], axis=1), reach_ref[...])
        reached = reached + jnp.broadcast_to(by_head[:, 3 * T : 3 * T + 1], (HEADS, T))
        d_raw = (head_t[1] * reached + by_head[:, 2 * T : 3 * T]) * sigmoid(raw_t)
        d_ref[rows, wide:] = columns_of(d_raw).astype(bf16)
        hacc[0] += d_raw
        hacc[1] += dt_t * reached
        dxh[T : T + 8, :] = dxh[0:8, :]
        if sub == 1:
            @pl.when(step == 0)
            def _():
                for way in (0, 1):
                    hop(1, way, 0).start()

            ring_poll(1)

    @pl.when(step == steps - 1)
    def _():
        total = lambda a: jnp.sum(a, axis=0, keepdims=True)
        for k in range(CONV + 1):
            small_ref[k : k + 1, :] = total(acc[k])
        small_ref[CONV + 1 : CONV + 2, :width] = total(gate_ref[...])
        small_ref[CONV + 1 : CONV + 2, width : width + LANES] = total(columns_of(hacc[0]))
        small_ref[CONV + 1 : CONV + 2, width + LANES :] = total(columns_of(hacc[1])) * head_ref[1:2, :]
        small_ref[CONV + 2 :, :] = jnp.zeros((2, wide), f32)
        skip = mm_exact(acc[CONV + 1, :, :width], pick_ref[...].astype(f32))
        small_ref[CONV + 3 : CONV + 4, 512 : 512 + LANES] = total(skip)
        for part in (0, 1):
            over_copy(part).wait_recv()

            def some(i, _, part=part):
                at = span(part * half + i * 32, 32)
                obranch_ref[at, :] = obranch_ref[at, :] + over_slot[part, span(i * 32, 32), :].astype(f32)
                return 0

            lax.fori_loop(0, half // 32, some, 0)
        for part in (0, 1):
            over_copy(part).wait_send()
            for turned in (0, 1):
                near_copy(turned, part).wait_send()
        for h in range(n - 1):
            for k in (0, 1):
                for way in (0, 1):
                    hop(k, way, h).wait_send()


def ssd_backward(n, dy, v, xc, dr, st, gate, taps, head, chan, early, branch):
    length, width = dy.shape
    wide = width + 2 * NS
    steps = length // ROWS
    subs = ROWS // T
    own_rows, tokens = D // n, length // 4
    half = tokens // 2
    row = lambda m: pl.BlockSpec((ROWS, m), lambda i: (steps - 1 - i, 0))
    whole = lambda a: pl.BlockSpec(a.shape, lambda i: (0,) * a.ndim, pipeline_mode=pl.Buffered(1))
    fixed = lambda *shape: pl.BlockSpec(shape, lambda i: (0,) * len(shape))
    anywhere = pl.BlockSpec(memory_space=pl.ANY)
    vm, dma = pltpu.VMEM, pltpu.SemaphoreType.DMA
    return pl.pallas_call(
        functools.partial(backward_body, n, own_rows, tokens, width),
        grid=(steps,),
        in_specs=[
            row(width), row(wide), row(wide), row(LANES),
            pl.BlockSpec((subs, NS, width), lambda i: (steps - 1 - i, 0, 0)),
            whole(gate), whole(taps), whole(head), whole(chan), anywhere, anywhere,
        ],
        out_specs=[
            row(wide + LANES), fixed(8, wide), fixed(own_rows, 2 * width), fixed(tokens, D),
        ],
        out_shape=[
            jax.ShapeDtypeStruct((length, wide + LANES), bf16),
            jax.ShapeDtypeStruct((8, wide), f32),
            jax.ShapeDtypeStruct((own_rows, 2 * width), f32),
            jax.ShapeDtypeStruct((tokens, D), f32),
        ],
        scratch_shapes=[
            vm((T + 8, wide), f32), vm((NS, width), f32), vm((T, width), f32), vm((T, width), f32),
            vm((T, width), bf16), vm((T, width), bf16), vm((3 * T + HEADS, width), bf16),
            vm((HEADS, T), f32), vm((CONV + 2, 8, wide), f32), vm((2, HEADS, T), f32),
            vm((width, LANES), bf16), vm((HEADS, width), bf16), vm((8, width), f32), vm((2, HEADS, LANES), f32),
            vm((3 * T, LANES), bf16), vm((4 * T, LANES), bf16),
            vm((D, 2 * width), bf16),
            [[vm((n - 1, size, width), bf16) for _ in (0, 1)] for _, size in cut_rows(own_rows)],
            vm((2, 2, half, D), bf16), vm((2, 2, half, D), bf16), vm((2, half, D), bf16),
            dma((5,)), dma((2, 2, n - 1)), dma((2, 2, n - 1)), dma((2, 2)), dma((2, 2)), dma((2,)), dma((2,)),
        ],
        compiler_params=pltpu.CompilerParams(
            collective_id=3, has_side_effects=True, vmem_limit_bytes=ROOM
        ),
        name="layer_backward",
    )(dy, v, xc, dr, st, gate, taps, head, chan, early, branch)


def reduce_body(
    n, rows, tokens, starts,
    xt_ref, d_ref, dz_ref, wp_ref, w_ref, small_ref, flat_ref, gain_ref,
    oxs_ref, oback_ref, bc_ref, oflat_ref,
    xt, d, dz, wz, w, work, grads, slots, staged, near, over, smalls, tens, bc_slot,
    load_sem, ring_send, ring_recv, near_send, near_recv, over_send, over_recv,
    small_send, small_recv, ten_send, ten_recv, bc_send, bc_recv,
):
    pos, ring, me, across, beside = neighbours(n)
    cuts = cut_rows(rows)
    core = lax.rem(me, 2)
    opposite = lax.rem(me + 2, 4)
    next_door = me + 1 - 2 * core
    far = lax.rem(next_door + 2, 4)
    half = tokens // 2
    late = d.shape[1]
    width = dz.shape[1]
    rest_of_z = width - Z_EARLY
    tile = 2 * LANES
    tiles = D // tile
    columns = [pl.ds(lo, hi - lo) for lo, hi in starts]
    sources = [(d_ref.at[:, columns[0]], d.at[:, columns[0]])]
    sources += [(xt_ref.at[pl.ds(i * tile, tile)], xt.at[pl.ds(i * tile, tile)]) for i in range(tiles)]
    sources += [(d_ref.at[:, some], d.at[:, some]) for some in columns[1:]]
    sources += [
        (dz_ref, dz), (w_ref.at[:, pl.ds(0, late)], w),
        (w_ref.at[:, pl.ds(late, Z_EARLY)], wz.at[:, pl.ds(0, Z_EARLY)]),
        (wp_ref.at[:, pl.ds(width, rest_of_z)], wz.at[:, pl.ds(Z_EARLY, rest_of_z)]),
        (small_ref, smalls.at[pos]),
    ]
    loads = [pltpu.make_async_copy(src, dst, load_sem.at[k]) for k, (src, dst) in enumerate(sources)]
    for load in loads:
        load.start()
    enter((*ring, across, beside))
    started = []

    def go(*args):
        copy = remote(*args)
        copy.start()
        started.append(copy)

    def block_at(way, count):
        return ring_index(lax.rem(pos + (count if way else n - count), n), n)

    def hop(k, way, h):
        lo, hi = starts[k]
        first, size = cuts[way]
        if h == 0:
            src = grads.at[span(block_at(way, 1) * rows + first, size), pl.ds(lo, hi - lo)]
        else:
            src = slots[way][k].at[h - 1]
        return remote(
            src, slots[way][k].at[h], ring_send.at[way, k, h], ring_recv.at[way, k, h], ring[way]
        )

    def product(k):
        lo, hi = starts[k]

        def some(i, _):
            if k == 0:
                rows_at = span(i * tile, tile)
                pltpu.make_async_copy(xt_ref.at[rows_at], xt.at[rows_at], load_sem.at[1 + i]).wait()
            at = span(i * tile, tile)
            grads[at, lo:hi] = mm(xt[at, :], d[:, lo:hi]).astype(bf16)
            return 0

        loads[0 if k == 0 else tiles + k].wait()
        lax.fori_loop(0, tiles, some, 0)
        for way in (0, 1):
            hop(k, way, 0).start()

    def near_copy(turned, part):
        return remote(
            staged.at[turned, part], near.at[turned, part],
            near_send.at[turned, part], near_recv.at[turned, part], beside,
        )

    def over_copy(part):
        return remote(near.at[0, part], over.at[part], over_send.at[part], over_recv.at[part], across)

    def ring_turn(k, h):
        lo, hi = starts[k]
        for way in (0, 1):
            first, size = cuts[way]
            slot = slots[way][k].at[h]
            remote(slot, slot, ring_send.at[way, k, h], ring_recv.at[way, k, h], ring[way]).wait_recv()
            block = block_at(way, 2 + h) if h < n - 2 else block_at(way, 0)

            tile = strip(size)

            def some(i, _, way=way, first=first, block=block, tile=tile):
                came = slots[way][k][h, span(i * tile, tile), :]
                mine = grads[span(block * rows + first + i * tile, tile), lo:hi]
                if h < n - 2:
                    slots[way][k][h, span(i * tile, tile), :] = came + mine
                else:
                    oxs_ref[span(first + i * tile, tile), lo:hi] = came.astype(f32) + mine.astype(f32)
                return 0

            lax.fori_loop(0, size // tile, some, 0)
            if h < n - 2:
                hop(k, way, h + 1).start()

    def small_hop(way, h):
        here = smalls.at[lax.rem(pos + (h if way else n - h), n)]
        go(here, here, small_send.at[way, h], small_recv.at[way, h], ring[way])

    def small_lands(way, h):
        here = smalls.at[lax.rem(pos + (h + 1 if way else n - h - 1), n)]
        remote(here, here, small_send.at[way, h], small_recv.at[way, h], ring[way]).wait_recv()

    for k in range(len(starts)):
        product(k)
    for load in loads[tiles + len(starts) :]:
        load.wait()
    turns = {0: [(0, 0)], 1: [(1, 0), (2, 0)], 2: [(0, 1)], 3: [(1, 1), (2, 1)], 4: [(0, 2)], 5: [(1, 2), (2, 2)], 6: [(0, 3)], 7: [(1, 3), (2, 3)]}
    taken = [sum(k == group for some in turns.values() for k, _ in some) for group in range(len(starts))]

    def block(i, _):
        which, part = lax.div(i, 2), lax.rem(i, 2)
        own = lax.rem(which, 2)
        turned = lax.div(which, 2)
        target = lax.rem(next_door + own * (me - next_door) + 2 * (1 - turned), 4)
        at = span(target * tokens + part * half, half)
        total = mm(dz[at, :], wz[...], NT) + mm(d[at, :], w[...], NT)
        work[...] = total

        @pl.when(own == 0)
        def _():
            staged[turned, part] = work[...].astype(bf16)
            near_copy(turned, part).start()

        @pl.when(own == 1)
        def _():
            near_copy(turned, part).wait_recv()

        @pl.when(which == 1)
        def _():
            near[0, part] = (work[...] + near[0, part].astype(f32)).astype(bf16)
            over_copy(part).start()

        @pl.when(which == 3)
        def _():
            oback_ref[span(part * half, half), :] = work[...] + near[1, part].astype(f32)

        for at_block, some in turns.items():

            @pl.when(i == at_block)
            def _(some=some):
                for k, h in some:
                    ring_turn(k, h)

        return 0

    lax.fori_loop(0, 8, block, 0)
    for i in range(tiles):
        share = jnp.zeros((tile, LANES), f32)
        for c in range(late // LANES):
            cols = slice(c * LANES, (c + 1) * LANES)
            at = slice(i * tile, (i + 1) * tile)
            share = share + grads[at, cols].astype(f32) * w[at, cols].astype(f32)
        total = mm_exact(jnp.ones((8, LANES), f32), share, NT)[0:1] + gain_ref[0:1, i * tile : (i + 1) * tile]
        for c in range(2 * i, 2 * i + 2):
            row, col = 6 + c // 8, (c % 8) * LANES
            part = total[:, (c - 2 * i) * LANES : (c - 2 * i + 1) * LANES]
            smalls[pos, row : row + 1, col : col + LANES] = part / flat_ref[c : c + 1, :]

    rest = [(k, h) for h in range(n - 1) for k in (0, 1, 2) if h >= taken[k]]
    rest.sort(key=lambda turn: turn[1] - taken[turn[0]])

    def small_step(s):
        for way in (0, 1):
            if s > 0 and (way == 0 or s < n // 2):
                small_lands(way, s - 1)
            if s < n // 2 - way:
                small_hop(way, s)

    small_step(0)
    steps_done = 1
    for at, (k, h) in enumerate(rest):
        ring_turn(k, h)
        if (k, h) == (0, n - 2):
            bc_slot[0] = oxs_ref[:, starts[0][0] : starts[0][0] + 2 * NS]
            go(bc_slot.at[0], bc_slot.at[1], bc_send.at[0], bc_recv.at[0], beside)
        if at % 2 == 1 and steps_done < n // 2:
            small_step(steps_done)
            steps_done += 1
    for s in range(steps_done, n // 2):
        small_step(s)
    small_lands(0, n // 2 - 1)

    total = smalls[0]
    for i in range(1, n):
        total = total + smalls[i]
    tens[me] = total
    go(tens.at[me], tens.at[me], ten_send.at[0], ten_recv.at[0], beside)
    remote(bc_slot.at[1], bc_slot.at[1], bc_send.at[0], bc_recv.at[0], beside).wait_recv()
    bc_slot[2] = bc_slot[0] + bc_slot[1]
    go(bc_slot.at[2], bc_slot.at[3], bc_send.at[1], bc_recv.at[1], across)
    here = tens.at[next_door]
    remote(here, here, ten_send.at[0], ten_recv.at[0], beside).wait_recv()
    for k, target in ((0, me), (1, next_door)):
        here = tens.at[target]
        go(here, here, ten_send.at[1 + k], ten_recv.at[1 + k], across)
    for part in (0, 1):
        over_copy(part).wait_recv()

        def some(i, _, part=part):
            at = span(part * half + i * 32, 32)
            oback_ref[at, :] = oback_ref[at, :] + over[part, span(i * 32, 32), :].astype(f32)
            return 0

        lax.fori_loop(0, half // 32, some, 0)
    for k, target in ((0, opposite), (1, far)):
        here = tens.at[target]
        remote(here, here, ten_send.at[1 + k], ten_recv.at[1 + k], across).wait_recv()
    flat_gradients(width, tens, oflat_ref)
    remote(bc_slot.at[3], bc_slot.at[3], bc_send.at[1], bc_recv.at[1], across).wait_recv()
    bc_ref[...] = bc_slot[2] + bc_slot[3]
    for part in (0, 1):
        over_copy(part).wait_send()
        for turned in (0, 1):
            near_copy(turned, part).wait_send()
    for k in range(len(starts)):
        for way in (0, 1):
            for h in range(n - 1):
                hop(k, way, h).wait_send()
    for copy in started:
        copy.wait_send()


def flat_gradients(width, tens, out_ref):
    pairs = width // LANES
    heads = width // P_SIZE

    def sums(row, col):
        total = tens[0, row : row + 1, col : col + LANES]
        for t in range(1, 4):
            total = total + tens[t, row : row + 1, col : col + LANES]
        return total

    def put(row, value):
        out_ref[row : row + 1, :] = value

    for c in range(D // LANES):
        put(c, sums(6 + c // 8, (c % 8) * LANES))
    for t in range(4):
        for c in range(pairs):
            cols = slice(c * LANES, (c + 1) * LANES)
            put(GATE_ROW + pairs * t + c, tens[t, CONV + 1 : CONV + 2, cols])
            put(BIAS_ROW + pairs * t + c, tens[t, CONV : CONV + 1, cols])
            for k in range(CONV):
                put(TAPS_ROW + 4 * pairs * k + pairs * t + c, tens[t, k : k + 1, cols])
    for c in range(2):
        put(BIAS_BC_ROW + c, sums(CONV, width + c * LANES))
        for k in range(CONV):
            put(TAPS_BC_ROW + 2 * k + c, sums(k, width + c * LANES))
    kinds = ((CONV + 1, width), (CONV + 1, width + LANES), (CONV + 3, 512))
    rows = [tens[t, row : row + 1, col : col + LANES] for row, col in kinds for t in range(4)]
    rows = jnp.concatenate(rows + [jnp.zeros((16 - len(rows), LANES), f32)], axis=0)
    lane = lax.broadcasted_iota(jnp.int32, (LANES, 2 * LANES), 1)
    entry = lax.broadcasted_iota(jnp.int32, (LANES, 2 * LANES), 0)
    spread_out = mm_exact(rows, jnp.where(lax.rem(lane, heads) == entry, 1.0, 0.0).astype(f32))
    at = lax.broadcasted_iota(jnp.int32, (16, 2 * LANES), 1)
    source = lax.broadcasted_iota(jnp.int32, (16, 2 * LANES), 0)
    line = jnp.sum(jnp.where(lax.div(at, heads) == source, spread_out, 0.0), axis=0, keepdims=True)
    put(HEAD_ROW, line[:, :LANES])
    put(HEAD_ROW + 1, line[:, LANES:])


def reduce_all(n, xt, d, dz, wp, w, small, flat, gain):
    rows, tokens = D // n, dz.shape[0] // 4
    width, late = dz.shape[1], d.shape[1]
    starts = ((width, late), (0, width // 2), (width // 2, width))
    half = tokens // 2
    dma, vm = pltpu.SemaphoreType.DMA, pltpu.VMEM
    anywhere = pl.BlockSpec(memory_space=pl.ANY)
    inside = pl.BlockSpec(memory_space=pltpu.VMEM)
    return pl.pallas_call(
        functools.partial(reduce_body, n, rows, tokens, starts),
        in_specs=[anywhere] * 6 + [inside] * 2,
        out_specs=[inside] * 4,
        out_shape=[
            jax.ShapeDtypeStruct((rows, late), f32),
            jax.ShapeDtypeStruct((tokens, D), f32),
            jax.ShapeDtypeStruct((rows, 2 * NS), f32),
            jax.ShapeDtypeStruct((FLAT_ROWS, LANES), f32),
        ],
        scratch_shapes=[
            vm(xt.shape, bf16), vm(d.shape, bf16), vm(dz.shape, bf16), vm((D, width), bf16),
            vm((D, late), bf16),
            vm((half, D), f32), vm((D, late), bf16),
            [[vm((n - 1, size, hi - lo), bf16) for lo, hi in starts] for _, size in cut_rows(rows)],
            vm((2, 2, half, D), bf16), vm((2, 2, half, D), bf16), vm((2, half, D), bf16),
            vm((n, *small.shape), f32), vm((4, *small.shape), f32), vm((4, rows, 2 * NS), f32),
            dma((14,)), dma((2, 3, n - 1)), dma((2, 3, n - 1)), dma((2, 2)), dma((2, 2)), dma((2,)), dma((2,)),
            dma((2, n // 2)), dma((2, n // 2)), dma((3,)), dma((3,)), dma((2,)), dma((2,)),
        ],
        compiler_params=pltpu.CompilerParams(
            collective_id=1, has_side_effects=True, vmem_limit_bytes=ROOM
        ),
        name="reduce_all",
    )(xt, d, dz, wp, w, small, flat, gain)


def adamw_step(weight, first, second, grad, rate, decay):
    first_new = beta_first * first + (1.0 - beta_first) * grad
    second_new = beta_second * second + (1.0 - beta_second) * grad * grad
    hat_first = first_new * (1.0 / (1.0 - beta_first**STEP))
    hat_second = second_new * (1.0 / (1.0 - beta_second**STEP))
    weight_new = weight - rate * (hat_first / (jnp.sqrt(hat_second) + adam_eps) + decay * weight)
    return (weight_new, first_new, second_new)


def finish_body(
    width, heads,
    in_ref, cot_ref, branch_ref, back_ref, flat_ref, early_ref, late_ref, bcg_ref,
    zx_ref, zx1_ref, zx2_ref, bc_ref, bc1_ref, bc2_ref, out_ref, out1_ref, out2_ref, late_all_ref, dt_ref, dt1_ref, dt2_ref,
    layer_ref, grad_ref, zxn_ref, zx1n_ref, zx2n_ref, bcn_ref, bc1n_ref, bc2n_ref,
    outn_ref, out1n_ref, out2n_ref, dtn_ref, dt1n_ref, dt2n_ref,
):
    def update(refs, news, grad):
        fresh = adamw_step(*(ref[...] for ref in refs), grad, matrix_rate, matrix_decay)
        for ref, value in zip(news, fresh):
            ref[...] = value

    for k, grad in ((0, early_ref), (1, late_ref)):
        fresh = adamw_step(
            *(ref[:, k, :] for ref in (zx_ref, zx1_ref, zx2_ref)), grad[:, :width], matrix_rate, matrix_decay
        )
        for ref, value in zip((zxn_ref, zx1n_ref, zx2n_ref), fresh):
            ref[:, k, :] = value
    update((bc_ref, bc1_ref, bc2_ref), (bcn_ref, bc1n_ref, bc2n_ref), bcg_ref[...])
    update((out_ref, out1_ref, out2_ref), (outn_ref, out1n_ref, out2n_ref), early_ref[:, width:])

    @pl.when(pl.program_id(0) == 0)
    def _():
        unit = jnp.where(
            lax.broadcasted_iota(jnp.int32, (16, LANES), 0) == lax.broadcasted_iota(jnp.int32, (16, LANES), 1), 1.0, 0.0
        ).astype(f32)
        turned = mm_exact(unit, late_all_ref[:, width + 2 * NS :], NT)
        update((dt_ref, dt1_ref, dt2_ref), (dtn_ref, dt1n_ref, dt2n_ref), turned[:heads])

    rows = in_ref.shape[0]
    tile = 64

    def some(i, _):
        at = span(i * tile, tile)
        squares = jnp.zeros((tile, LANES), f32)
        inner = jnp.zeros((tile, LANES), f32)
        for c in range(D // LANES):
            cols = slice(c * LANES, (c + 1) * LANES)
            x = in_ref[at, cols].astype(f32)
            squares = squares + x * x
            inner = inner + x * flat_ref[c : c + 1, :] * back_ref[at, cols]
        r = lax.rsqrt(jnp.sum(squares, axis=-1, keepdims=True) / D + norm_eps)
        k = r * r * r * jnp.sum(inner, axis=-1, keepdims=True) / D
        r, k = jnp.broadcast_to(r, (tile, LANES)), jnp.broadcast_to(k, (tile, LANES))
        for c in range(D // LANES):
            cols = slice(c * LANES, (c + 1) * LANES)
            x = in_ref[at, cols].astype(f32)
            layer_ref[at, cols] = (x + branch_ref[at, cols]).astype(bf16)
            grad_ref[at, cols] = cot_ref[at, cols].astype(f32) + r * flat_ref[c : c + 1, :] * back_ref[at, cols] - x * k
        return 0

    lax.fori_loop(0, rows // tile, some, 0)


def finish(layer_input, out_grad, branch, back, flat, early, late, bcg, zx, bc, out, dt):
    (rows, width), heads = out[0].shape, dt[0].shape[0]
    steps = 4 if rows % 32 == 0 else 2
    part = lambda a: pl.BlockSpec((a.shape[0] // steps, *a.shape[1:]), lambda i: (i,) + (0,) * (a.ndim - 1))
    whole = lambda a: pl.BlockSpec(a.shape, lambda i: (0,) * a.ndim)
    like = lambda a, dtype=f32: jax.ShapeDtypeStruct(a.shape, dtype)
    weights = (*zx, *bc, *out)
    return pl.pallas_call(
        functools.partial(finish_body, width, heads),
        grid=(steps,),
        in_specs=[
            *(part(a) for a in (layer_input, out_grad, branch, back)), whole(flat),
            *(part(a) for a in (early, late, bcg, *weights)), whole(late), *(whole(a) for a in dt),
        ],
        out_specs=[part(layer_input), part(back), *(part(a) for a in weights), *(whole(a) for a in dt)],
        out_shape=[like(layer_input, bf16), like(back), *(like(a) for a in weights), *(like(a) for a in dt)],
        compiler_params=pltpu.CompilerParams(vmem_limit_bytes=ROOM),
        name="finish",
    )(layer_input, out_grad, branch, back, flat, early, late, bcg, *weights, late, *dt)


def local(
    layer_input,
    out_grad,
    small_params,
    small_first,
    small_second,
    w_zx,
    zx_first,
    zx_second,
    w_bc,
    bc_first,
    bc_second,
    w_dt,
    dt_first,
    dt_second,
    w_out,
    out_first,
    out_second,
):
    n = lax.axis_size("dp")
    flat = jnp.pad(small_params, (0, FLAT_ROWS * LANES - small_params.shape[0])).reshape(FLAT_ROWS, LANES)
    xg, xt, w_all, w_pair = gather_all(n, layer_input, flat, w_zx, w_bc, w_dt.T, w_out)
    v, xc, dr, st, dy, dz, branch, early, gate, gain, pair_all, taps, head, chan = ssd_forward(
        n, xg, xt, w_all, flat, out_grad, w_pair
    )
    d_late, small, owner_early, own_branch = ssd_backward(
        n, dy, v, xc, dr, st, gate, taps, head, chan, early, branch
    )
    owner_late, d_normed_in, owner_bc, flat_grad = reduce_all(
        n, xt, d_late, dz, pair_all, w_all, small, flat, gain
    )
    small_grad = flat_grad.reshape(-1)[: small_params.shape[0]]
    small_new, small_first_new, small_second_new = adamw_step(
        small_params, small_first, small_second, small_grad, small_rate, 0.0
    )
    (
        layer_output, input_grad, zx_new, zx_first_new, zx_second_new, bc_new, bc_first_new, bc_second_new,
        out_new, out_first_new, out_second_new, dt_new, dt_first_new, dt_second_new,
    ) = finish(
        layer_input, out_grad, own_branch, d_normed_in, flat, owner_early, owner_late, owner_bc,
        (w_zx, zx_first, zx_second), (w_bc, bc_first, bc_second), (w_out, out_first, out_second),
        (w_dt.T, dt_first.T, dt_second.T),
    )
    dt_new, dt_first_new, dt_second_new = dt_new.T, dt_first_new.T, dt_second_new.T
    return (
        layer_output,
        input_grad,
        small_new,
        small_first_new,
        small_second_new,
        zx_new,
        zx_first_new,
        zx_second_new,
        bc_new,
        bc_first_new,
        bc_second_new,
        dt_new,
        dt_first_new,
        dt_second_new,
        out_new,
        out_first_new,
        out_second_new,
    )


def solution(mesh):
    return jax.shard_map(
        local,
        mesh=mesh,
        in_specs=(
            P(("dp", "tensor"), None),
            P(("dp", "tensor"), None),
            P(),
            P(),
            P(),
            P("dp", None, "tensor"),
            P("dp", None, "tensor"),
            P("dp", None, "tensor"),
            P("dp", None),
            P("dp", None),
            P("dp", None),
            P("dp", "tensor"),
            P("dp", "tensor"),
            P("dp", "tensor"),
            P("dp", "tensor"),
            P("dp", "tensor"),
            P("dp", "tensor"),
        ),
        out_specs=(
            P(("dp", "tensor"), None),
            P(("dp", "tensor"), None),
            P(),
            P(),
            P(),
            P("dp", None, "tensor"),
            P("dp", None, "tensor"),
            P("dp", None, "tensor"),
            P("dp", None),
            P("dp", None),
            P("dp", None),
            P("dp", "tensor"),
            P("dp", "tensor"),
            P("dp", "tensor"),
            P("dp", "tensor"),
            P("dp", "tensor"),
            P("dp", "tensor"),
        ),
        check_vma=False,
    )
```

```python
import functools

import jax
import jax.numpy as jnp
from jax import lax
from jax.experimental import pallas as pl
from jax.experimental.pallas import tpu as pltpu
from jax.sharding import PartitionSpec as P

D = 1536
DI = 3072
H = 48
NS = 128
P_SIZE = 64
CONV = 4
LEN = 2048
STEP = 10

T = 128
ROWS = 256
LANES = 128
ROOM = 60 * 2**20

norm_eps = 1e-05
adam_eps = 1e-08
beta_first = 0.9
beta_second = 0.95
matrix_rate = 0.01
small_rate = 0.1
matrix_decay = 0.1

f32 = jnp.float32
bf16 = jnp.bfloat16
NN = (((1,), (0,)), ((), ()))
NT = (((1,), (1,)), ((), ()))
TN = (((0,), (0,)), ((), ()))
HIGHEST = lax.Precision.HIGHEST


GATE_ROW, TAPS_ROW, BIAS_ROW, TAPS_BC_ROW, BIAS_BC_ROW, HEAD_ROW, FLAT_ROWS = 12, 36, 132, 156, 164, 166, 168


def mm(a, b, dims=NN):
    return lax.dot_general(a, b, dims, preferred_element_type=f32)


def mm_exact(a, b, dims=NN):
    return lax.dot_general(a, b, dims, preferred_element_type=f32, precision=HIGHEST)


def sigmoid(v):
    return 0.5 * jnp.tanh(0.5 * v) + 0.5


def softplus(v):
    return jnp.maximum(v, 0.0) + jnp.log1p(jnp.exp(-jnp.abs(v)))


def spread(col):
    return jnp.broadcast_to(col, (T, LANES))


def block_iota(axis):
    return lax.broadcasted_iota(jnp.int32, (T, LANES), axis)


HEADS = 16
LOG2_E = 1.4426950408889634


def pieces(value, count):
    parts = []
    for k in range(count):
        part = value.astype(bf16)
        parts.append(part)
        if k < count - 1:
            value = value - part.astype(f32)
    return jnp.concatenate(parts, axis=1)


def columns_of(rows):
    return jnp.concatenate([rows, jnp.zeros((LANES - HEADS, T), f32)], axis=0).T


def set_heads(head_ref, head_t, until):
    turned = jnp.concatenate([head_ref[...], jnp.zeros((LANES - 8, LANES), f32)], axis=0).T
    head_t[0] = spread(turned[:, 0:1])[:HEADS]
    head_t[1] = spread(turned[:, 1:2])[:HEADS]
    matrix = jnp.where(block_iota(0) <= block_iota(1), 1.0, 0.0).astype(bf16)
    for k in range(3):
        until[k * T : (k + 1) * T, :] = matrix


def head_rows(dr_ref, head_t, until, rows):
    raw = dr_ref[rows, :].T[:HEADS] + head_t[0]
    dt = softplus(raw)
    decay = mm(pieces(dt * (head_t[1] * LOG2_E), 3), until[...])
    return raw, dt, decay, columns_of(dt), columns_of(decay)


def ring_place(n):
    me = lax.axis_index("dp")
    z, x = lax.div(me, 2), lax.rem(me, 2)
    return z + x * (n - 1 - 2 * z)


def ring_index(pos, n):
    back = lax.div(pos, n // 2)
    return 2 * pos + back * (2 * n - 1 - 4 * pos)


def neighbours(n):
    pos = ring_place(n)
    right = ring_index(lax.rem(pos + 1, n), n)
    left = ring_index(lax.rem(pos + n - 1, n), n)
    me = lax.axis_index("tensor")
    y, core = lax.div(me, 2), lax.rem(me, 2)
    across = 2 * (1 - y) + core
    beside = 2 * y + 1 - core
    return pos, ({"dp": right}, {"dp": left}), me, {"tensor": across}, {"tensor": beside}


def greet(peers):
    barrier = pltpu.get_barrier_semaphore()
    for peer in peers:
        pl.semaphore_signal(barrier, inc=1, device_id=peer, device_id_type=pl.DeviceIdType.MESH)


def enter(peers):
    greet(peers)
    pl.semaphore_wait(pltpu.get_barrier_semaphore(), len(peers))


def remote(src, dst, send_sem, recv_sem, peer):
    return pltpu.make_async_remote_copy(
        src_ref=src, dst_ref=dst, send_sem=send_sem, recv_sem=recv_sem,
        device_id=peer, device_id_type=pl.DeviceIdType.MESH,
    )


def span(start, size):
    return pl.ds(pl.multiple_of(start, 16), size)


def strip(rows):
    return next(size for size in (48, 32, 16) if rows % size == 0)


def cut_rows(rows):
    top = rows // 32 * 16
    return ((0, top), (top, rows - top))


def forward_body(
    n, rows, tokens, width,
    in_ref, cot_ref, flat_ref, wzx_ref, wbc_ref, wdt_ref, wout_ref,
    v_ref, xc_ref, dr_ref, st_ref, dy_ref, dz_ref, branch_ref, early_ref, gate_ref, gain_ref,
    xg_ref, ws_ref, wps_ref, taps_ref, head_ref, chan_ref,
    halo, state, y_all, z_all, dn_all, nl_all, dz_all, xg, cots, ws, wps, sums, red, head_t, until, across_state, tails, work,
    own_keep, lead_keep, lead_send, lead_recv, x_keep, x_over_send, x_over_recv, x_side_send, x_side_recv,
    x_pass_send, x_pass_recv, ring_keep, ring_send, ring_recv, over_send, over_recv,
    side_send, side_recv, pass_send, pass_recv, sum_send, sum_recv,
):
    pairs = width // LANES
    wide = width + 2 * NS
    step = pl.program_id(0)
    steps = LEN // ROWS
    tall = 2 * ROWS
    gating = steps
    forming = gating + LEN // tall
    products = forming + steps
    last_step = products + D // ROWS - 1
    pos, ring, me, across, beside = neighbours(n)
    opposite = lax.rem(me + 2, 4)
    next_door = me + 1 - 2 * lax.rem(me, 2)
    far = lax.rem(next_door + 2, 4)
    askew = {"tensor": far}
    quarter = tokens // 4
    hops = n // 2
    cuts = cut_rows(rows)
    mine = ring_index(pos, n)

    late = wide + LANES
    parts_of = ((0, width), (width, width))

    def hop(k, part, way, h):
        first, size = cuts[part]
        cols = pl.ds(*parts_of[k])
        block = ring_index(lax.rem(pos + (h if way else n - h), n), n)
        here = wps.at[span(block * rows + first, size), cols]
        return remote(here, here, ring_send.at[way, part, k, h], ring_recv.at[way, part, k, h], ring[way])

    def hop_lands(k, part, way, h):
        first, size = cuts[part]
        block = ring_index(lax.rem(pos + (h + 1 if way else n - h - 1), n), n)
        return span(block * rows + first, size), pl.ds(*parts_of[k])

    def hop_arrival(k, part, way, h):
        here = wps.at[hop_lands(k, part, way, h)]
        return remote(here, here, ring_send.at[way, part, k, h], ring_recv.at[way, part, k, h], ring[way])

    def hop_keep(part, way, h):
        at = hop_lands(1, part, way, h)
        return pltpu.make_async_copy(wps.at[at], wps_ref.at[at], ring_keep.at[way, part, h])

    def hop_ways(h):
        return [(part, way) for part in (0, 1) for way in (0, 1) if h < hops - 1 or part == way]

    def hop_on(k, h):
        for part, way in hop_ways(h - 1) if h > 0 else ():
            hop_arrival(k, part, way, h - 1).wait_recv()
            if k == 1:
                hop_keep(part, way, h - 1).start()
            if h < hops and (part, way) in hop_ways(h):
                hop(k, part, way, h).start()
        if h == 0:
            for part, way in hop_ways(0):
                hop(k, part, way, 0).start()

    def over(k):
        return remote(
            cot_ref.at[pl.ds(k * quarter, quarter)], cots.at[span(me * tokens + k * quarter, quarter)],
            over_send.at[k], over_recv.at[k], across,
        )

    def landed(start, size, send, recv, peer):
        here = cots.at[span(start, size)]
        return remote(here, here, send, recv, peer)

    def over_arrival(k):
        return landed(opposite * tokens + k * quarter, quarter, over_send.at[k], over_recv.at[k], across)

    def passing(k):
        return landed(opposite * tokens + k * quarter, quarter, pass_send.at[k], pass_recv.at[k], beside)

    def pass_arrival(k):
        return landed(far * tokens + k * quarter, quarter, pass_send.at[k], pass_recv.at[k], beside)

    def side():
        return remote(cot_ref, cots.at[span(me * tokens, tokens)], side_send.at[0], side_recv.at[0], beside)

    def side_arrival():
        return landed(next_door * tokens, tokens, side_send.at[0], side_recv.at[0], beside)

    def own_cot():
        return pltpu.make_async_copy(cot_ref, cots.at[span(me * tokens, tokens)], own_keep.at[0])

    def own_z():
        at = span(mine * rows, rows), pl.ds(*parts_of[1])
        return pltpu.make_async_copy(wps.at[at], wps_ref.at[at], own_keep.at[1])

    def pass_on(*pieces):
        for k in pieces:
            over_arrival(k).wait_recv()
            passing(k).start()

    def normalize(k):
        def some(i, _):
            at = span(me * tokens + k * quarter + i * 64, 64)
            squares = jnp.zeros((64, LANES), f32)
            for c in range(D // LANES):
                x = xg[at, c * LANES : (c + 1) * LANES].astype(f32)
                squares = squares + x * x
            inverse = lax.rsqrt(jnp.sum(squares, axis=-1, keepdims=True) / D + norm_eps)
            inverse = jnp.broadcast_to(inverse, (64, LANES))
            for c in range(D // LANES):
                cols = slice(c * LANES, (c + 1) * LANES)
                xg[at, cols] = (xg[at, cols].astype(f32) * inverse * flat_ref[c : c + 1, :]).astype(bf16)
            return 0

        lax.fori_loop(0, quarter // 64, some, 0)

    @pl.when(step == 0)
    def _():
        own_rows = span(me * tokens, tokens)
        greet((*ring, across, beside, askew))
        load = pltpu.make_async_copy(in_ref, xg.at[own_rows], own_keep.at[2])
        load.start()
        own_cot().start()
        mine_at = span(mine * rows, rows)
        ws[mine_at, :width] = wzx_ref[:, 1, :].astype(bf16)
        ws[mine_at, width:wide] = wbc_ref[...].astype(bf16)
        heads = wdt_ref.shape[0]
        unit = jnp.where(
            lax.broadcasted_iota(jnp.int32, (16, LANES), 0) == lax.broadcasted_iota(jnp.int32, (16, LANES), 1), 1.0, 0.0
        ).astype(bf16)
        steps_w = jnp.concatenate([wdt_ref[...], jnp.zeros((16 - heads, rows), f32)], axis=0).astype(bf16)
        ws[mine_at, wide:] = mm(steps_w, unit, TN).astype(bf16)
        load.wait()
        normalize(0)
        pl.semaphore_wait(pltpu.get_barrier_semaphore(), 5)
        started, kept = [], []

        def go(*args):
            copy = remote(*args)
            copy.start()
            started.append(copy)

        def keep(src, dst, sem):
            copy = pltpu.make_async_copy(src, dst, sem)
            copy.start()
            kept.append(copy)

        def arrived(part, way, h, block):
            first, size = cuts[part]
            at = span(block * rows + first, size)
            remote(
                ws.at[at], ws.at[at], lead_send.at[way, part, h], lead_recv.at[way, part, h], ring[way]
            ).wait_recv()
            keep(ws.at[at], ws_ref.at[at], lead_keep.at[way, part, h])

        def lead(h, parts=(0, 1)):
            for part in parts:
                first, size = cuts[part]
                for way in (0, 1):
                    block = ring_index(lax.rem(pos + (h if way else n - h), n), n)
                    here = ws.at[span(block * rows + first, size)]
                    if h > 0:
                        arrived(part, way, h - 1, block)
                    if h == hops - 1 and part != way:
                        continue
                    go(here, here, lead_send.at[way, part, h], lead_recv.at[way, part, h], ring[way])

        def x_over(k):
            at = span(me * tokens + k * quarter, quarter)
            go(xg.at[at], xg.at[at], x_over_send.at[k], x_over_recv.at[k], across)

        def x_pass(k):
            at = span(opposite * tokens + k * quarter, quarter)
            here = xg.at[at]
            remote(here, here, x_over_send.at[k], x_over_recv.at[k], across).wait_recv()
            go(here, here, x_pass_send.at[k], x_pass_recv.at[k], beside)
            keep(here, xg_ref.at[at], x_keep.at[k])

        def x_pass_lands(k):
            at = span(far * tokens + k * quarter, quarter)
            remote(xg.at[at], xg.at[at], x_pass_send.at[k], x_pass_recv.at[k], beside).wait_recv()
            keep(xg.at[at], xg_ref.at[at], x_keep.at[4 + k])

        lead(0, (0,))
        leading = list(started)
        x_over(0)
        for k in (1, 2, 3):
            normalize(k)
            if k == 1:
                x_over(1)
        go(xg.at[own_rows], xg.at[own_rows], x_side_send.at[0], x_side_recv.at[0], beside)
        keep(xg.at[own_rows], xg_ref.at[own_rows], x_keep.at[8])
        wps[mine_at, :width] = wout_ref[...].astype(bf16)
        wps[mine_at, width:] = wzx_ref[:, 0, :].astype(bf16)
        for copy in leading:
            copy.wait_send()
            started.remove(copy)
        lead(0, (1,))
        keep(ws.at[mine_at], ws_ref.at[mine_at], x_keep.at[9])
        own_z().start()
        halo[0:8, :] = jnp.zeros((8, wide), f32)
        state[...] = jnp.zeros_like(state)
        gate_ref[...] = jnp.zeros_like(gate_ref)
        parameter_rows(me, width, flat_ref, taps_ref, head_ref, chan_ref)
        set_heads(head_ref, head_t, until)
        lead(1)
        x_over(2)
        at = span(next_door * tokens, tokens)
        remote(xg.at[at], xg.at[at], x_side_send.at[0], x_side_recv.at[0], beside).wait_recv()
        keep(xg.at[at], xg_ref.at[at], x_keep.at[10])
        side().start()
        lead(2)
        x_over(3)
        x_pass(0)
        x_pass(1)
        for h in range(3, hops):
            lead(h)
        hop_on(0, 0)
        x_pass(2)
        over(0).start()
        x_pass_lands(0)
        x_pass_lands(1)
        x_pass(3)
        for part in (0, 1):
            arrived(part, part, hops - 1, ring_index(lax.rem(pos + n // 2, n), n))
        hop_on(1, 0)
        over(1).start()
        x_pass_lands(2)
        x_pass_lands(3)
        for copy in kept:
            copy.wait()
        for copy in started:
            copy.wait_send()

    for k, times in enumerate(((1, 4, 6), (2, 5, 7))):
        for h in range(1, hops):
            at = times[h - 1] if h <= len(times) else gating
            pl.when(step == at)(functools.partial(hop_on, k, h))
    for k in (0, 1):
        pl.when(step == gating)(functools.partial(hop_on, k, hops))

    @pl.when(step == 2)
    def _():
        over(2).start()

    @pl.when(step == 4)
    def _():
        over(3).start()
        pass_on(0, 1)

    pl.when(step == steps - 1)(functools.partial(pass_on, 2))

    @pl.when(step < gating)
    def _():
        scan_step(
            width, step, xg, ws, taps_ref, head_ref, chan_ref,
            v_ref, xc_ref, dr_ref, st_ref, halo, state, y_all, head_t, until, across_state, tails,
            functools.partial(pass_on, 3),
        )

    @pl.when(step == gating)
    def _():
        side_arrival().wait_recv()
        for k in range(4):
            pass_arrival(k).wait_recv()
        own_cot().wait()
        own_z().wait()

    @pl.when((step >= gating) & (step < forming))
    def _():
        first = (step - gating) * tall
        at = span(first, tall)
        z_all[at, :] = mm(xg[at, :], wps[:, width:])
        work[...] = mm(cots[at, :], wps[:, :width])
        dn_all[at, :] = work[...].astype(bf16)
        ones = jnp.ones((8, LANES), f32)
        for sub in range(tall // T):
            rows_at = span(first + sub * T, T)
            squares = jnp.zeros((T, LANES), f32)
            inner = jnp.zeros((T, LANES), f32)
            for p in range(pairs):
                cols = slice(p * LANES, (p + 1) * LANES)
                z = z_all[rows_at, cols]
                gated = y_all[rows_at, cols] * (z * sigmoid(z))
                squares = squares + gated * gated
                inner = inner + gated * chan_ref[0:1, cols] * work[sub * T : (sub + 1) * T, cols]
            lanes = pl.ds(pl.multiple_of(first + sub * T, T), T)
            sums[me, 0:4, lanes] = mm_exact(ones, squares, NT)[0:4]
            sums[me, 4:8, lanes] = mm_exact(ones, inner, NT)[4:8]

    @pl.when(step == forming - 1)
    def _():
        peers = ((beside, next_door), (across, opposite), (askew, far))
        for k, (peer, _) in enumerate(peers):
            remote(sums.at[me], sums.at[me], sum_send.at[k], sum_recv.at[k], peer).start()
        for h in range(hops):
            for part, way in hop_ways(h):
                for k in (0, 1):
                    hop(k, part, way, h).wait_send()
                hop_keep(part, way, h).wait()
        side().wait_send()
        for k in range(4):
            over(k).wait_send()
            passing(k).wait_send()
        for k, (peer, other) in enumerate(peers):
            remote(sums.at[other], sums.at[other], sum_send.at[k], sum_recv.at[k], peer).wait()
        red[...] = ((sums[0] + sums[1]) + sums[2]) + sums[3]

    @pl.when((step >= forming) & (step < products))
    def _():
        first = (step - forming) * ROWS
        lanes = pl.ds(pl.multiple_of(first, ROWS), ROWS)
        q_row = lax.rsqrt(red[0:4, lanes] / DI + norm_eps)
        k_row = q_row * q_row * q_row * red[4:8, lanes] / DI
        turned = jnp.concatenate([q_row, k_row], axis=0).T
        for sub in range(ROWS // T):
            rows_at = slice(sub * T, (sub + 1) * T)
            at = span(first + sub * T, T)
            q, kk = spread(turned[rows_at, 0:1]), spread(turned[rows_at, 4:5])
            for p in range(pairs):
                cols = slice(p * LANES, (p + 1) * LANES)
                z, y, dn = z_all[at, cols], y_all[at, cols], dn_all[at, cols].astype(f32)
                gain = chan_ref[0:1, cols]
                s = sigmoid(z)
                sz = z * s
                gated = y * sz
                gq = gated * q
                dg = q * gain * dn - gated * kk
                gate_ref[:, cols] += jnp.sum((gq * dn).reshape(T // 8, 8, LANES), axis=0)
                nl_all[at, cols] = (gq * gain).astype(bf16)
                dz = (dg * y * (s + sz * (1.0 - s))).astype(bf16)
                dz_all[at, cols] = dz
                dz_ref[rows_at, cols] = dz
                dy_ref[rows_at, cols] = (dg * sz).astype(bf16)
        branch_ref[...] = mm(nl_all[span(first, ROWS), :], wps[:, :width], NT).astype(bf16)

    @pl.when(step >= products)
    def _():
        first = (step - products) * ROWS
        at = span(first, ROWS)
        lanes = pl.ds(pl.multiple_of(first, ROWS), ROWS)
        grad = mm(xg[:, lanes], dz_all[...], TN)
        early_ref[:, :width] = grad.astype(bf16)
        share = jnp.zeros((ROWS, LANES), f32)
        for p in range(pairs):
            cols = slice(p * LANES, (p + 1) * LANES)
            w = wps[at, width + p * LANES : width + (p + 1) * LANES]
            share = share + grad[:, cols] * w.astype(f32)
        gain_ref[:, lanes] = mm_exact(jnp.ones((8, LANES), f32), share, NT)
        early_ref[:, width:] = mm(cots[:, lanes], nl_all[...], TN).astype(bf16)


def parameter_rows(me, width, flat_ref, taps_ref, head_ref, chan_ref):
    pairs = width // LANES
    heads = width // P_SIZE
    taps_ref[...] = jnp.zeros_like(taps_ref)
    chan_ref[...] = jnp.zeros_like(chan_ref)
    for c in range(pairs):
        cols = slice(c * LANES, (c + 1) * LANES)
        chan_ref[0:1, cols] = flat_ref[pl.ds(GATE_ROW + pairs * me + c, 1), :]
        taps_ref[CONV : CONV + 1, cols] = flat_ref[pl.ds(BIAS_ROW + pairs * me + c, 1), :]
        for k in range(CONV):
            taps_ref[k : k + 1, cols] = flat_ref[pl.ds(TAPS_ROW + 4 * pairs * k + pairs * me + c, 1), :]
    for c in range(2):
        cols = slice(width + c * LANES, width + (c + 1) * LANES)
        taps_ref[CONV : CONV + 1, cols] = flat_ref[BIAS_BC_ROW + c : BIAS_BC_ROW + c + 1, :]
        for k in range(CONV):
            row = TAPS_BC_ROW + 2 * k + c
            taps_ref[k : k + 1, cols] = flat_ref[row : row + 1, :]
    both = jnp.concatenate([flat_ref[HEAD_ROW : HEAD_ROW + 1, :], flat_ref[HEAD_ROW + 1 : HEAD_ROW + 2, :]], axis=1)
    both = jnp.broadcast_to(both, (8, 2 * LANES))
    lane = lax.broadcasted_iota(jnp.int32, (2 * LANES, LANES), 0)
    head = lax.broadcasted_iota(jnp.int32, (2 * LANES, LANES), 1)

    def take(kind):
        match = (lane == 4 * heads * kind + heads * me + head) & (head < heads)
        return mm_exact(both, jnp.where(match, 1.0, 0.0).astype(f32))

    valid = lax.broadcasted_iota(jnp.int32, (8, LANES), 1) < heads
    row = lax.broadcasted_iota(jnp.int32, (8, LANES), 0)
    rates = jnp.where(valid, -jnp.exp(take(1)), 0.0)
    head_ref[...] = jnp.where(row == 0, take(0), jnp.where(row == 1, rates, 0.0))
    skip = mm_exact(take(2), picked(width).astype(f32), NT)
    chan_ref[1:2, :] = skip[0:1]


def picked(width):
    channel = lax.broadcasted_iota(jnp.int32, (width, LANES), 0)
    head = lax.broadcasted_iota(jnp.int32, (width, LANES), 1)
    return jnp.where((channel >= head * P_SIZE) & (channel < (head + 1) * P_SIZE), 1.0, 0.0).astype(bf16)


def scan_step(
    width, step, xg, w_ref, taps_ref, head_ref, chan_ref,
    v_ref, xc_ref, dr_ref, st_ref, halo, state, y_all, head_t, until, across_state, tails, late_turn,
):
    pairs = width // LANES
    wide = width + 2 * NS
    mine = span(step * ROWS, ROWS)
    dr_ref[...] = mm(xg[mine, :], w_ref[:, wide:])
    halo[8 : 8 + ROWS, :] = mm(xg[mine, :], w_ref[:, :wide])
    low_half = block_iota(1) < P_SIZE
    causal = block_iota(0) >= block_iota(1)

    def convolved(sub, block):
        cols = slice(block * LANES, (block + 1) * LANES)
        total = taps_ref[CONV : CONV + 1, cols]
        for k in range(CONV):
            first = 8 - (CONV - 1) + k + sub * T
            total = total + taps_ref[k : k + 1, cols] * halo[first : first + T, cols]
        rows = slice(sub * T, (sub + 1) * T)
        xc_ref[rows, cols] = total.astype(bf16)
        v_ref[rows, cols] = halo[8 + sub * T : 8 + (sub + 1) * T, cols].astype(bf16)
        return total * sigmoid(total)

    for sub in range(ROWS // T):
        rows = slice(sub * T, (sub + 1) * T)
        _, _, decay_t, dt, decay = head_rows(dr_ref, head_t, until, rows)
        b_low = convolved(sub, pairs).astype(bf16)
        c_low = convolved(sub, pairs + 1).astype(bf16)
        b_t = b_low.T
        scores = jnp.where(causal, mm(c_low, b_low, NT), 0.0)
        st_ref[sub] = state[...].astype(bf16)
        across_state[...] = mm(c_low, st_ref[sub])
        for p in range(pairs):
            cols = slice(p * LANES, (p + 1) * LANES)
            x = convolved(sub, p)
            l1, l2 = spread(decay[:, 2 * p : 2 * p + 1]), spread(decay[:, 2 * p + 1 : 2 * p + 2])
            both = jnp.where(low_half, l1, l2)
            dtb = jnp.where(
                low_half, spread(dt[:, 2 * p : 2 * p + 1]), spread(dt[:, 2 * p + 1 : 2 * p + 2])
            )
            u = x * dtb
            m1 = scores * jnp.exp2(jnp.minimum(l1 - decay_t[2 * p : 2 * p + 1, :], 0.0))
            m2 = scores * jnp.exp2(jnp.minimum(l2 - decay_t[2 * p + 1 : 2 * p + 2, :], 0.0))
            mixing = jnp.concatenate([m1.astype(bf16), m2.astype(bf16)], axis=1)
            u_low = u.astype(bf16)
            zero = jnp.zeros_like(u_low)
            parts = jnp.concatenate(
                [jnp.where(low_half, u_low, zero), jnp.where(low_half, zero, u_low)], axis=0
            )
            last = both[T - 1 : T, :]
            y = mm(mixing, parts) + jnp.exp2(both) * across_state[:, cols] + chan_ref[1:2, cols] * x
            tails[:, cols] = (u * jnp.exp2(last - both)).astype(bf16)
            state[:, cols] = jnp.exp2(last) * state[:, cols]
            y_all[span(step * ROWS + sub * T, T), cols] = y
        state[...] = state[...] + mm(b_t, tails[...])
        if sub == 0:
            pl.when(step == LEN // ROWS - 1)(late_turn)
    halo[0:8, :] = halo[ROWS : ROWS + 8, :]


def ssd_forward(n, layer_input, out_grad, flat, w_zx, w_bc, w_dt, w_out):
    rows, width = w_out.shape
    tokens = layer_input.shape[0]
    length = 4 * tokens
    wide = width + 2 * NS
    steps = length // ROWS
    tall = 2 * ROWS
    forming = steps + length // tall
    products = forming + steps
    subs = ROWS // T
    assert length == LEN
    early = lambda i: jnp.minimum(i, steps - 1)
    formed = lambda i: jnp.clip(i - forming, 0, steps - 1)
    late = lambda i: jnp.maximum(i - products, 0)
    row = lambda m: pl.BlockSpec((ROWS, m), lambda i: (early(i), 0))
    form = lambda m: pl.BlockSpec((ROWS, m), lambda i: (formed(i), 0))
    whole = lambda a: pl.BlockSpec(a.shape, lambda i: (0,) * a.ndim, pipeline_mode=pl.Buffered(1))
    fixed = lambda m: pl.BlockSpec((8, m), lambda i: (0, 0))
    anywhere = pl.BlockSpec(memory_space=pl.ANY)
    vm, dma = pltpu.VMEM, pltpu.SemaphoreType.DMA
    hops, lead = dma((2, 2, 2, n // 2)), dma((2, 2, n // 2))
    shape = lambda dims, dtype: jax.ShapeDtypeStruct(dims, dtype)
    return pl.pallas_call(
        functools.partial(forward_body, n, rows, tokens, width),
        grid=(products + D // ROWS,),
        in_specs=[anywhere, anywhere, *(whole(a) for a in (flat, w_zx, w_bc, w_dt, w_out))],
        out_specs=[
            row(wide), row(wide), row(LANES), pl.BlockSpec((subs, NS, width), lambda i: (early(i), 0, 0)),
            form(width), form(width), form(D), pl.BlockSpec((ROWS, 2 * width), lambda i: (late(i), 0)),
            fixed(width), fixed(D), anywhere, anywhere, anywhere, *(fixed(m) for m in (wide, LANES, width)),
        ],
        out_shape=[
            shape((length, wide), bf16), shape((length, wide), bf16), shape((length, LANES), f32),
            shape((length // T, NS, width), bf16), shape((length, width), bf16), shape((length, width), bf16),
            shape((length, D), bf16), shape((D, 2 * width), bf16), shape((8, width), f32), shape((8, D), f32),
            shape((length, D), bf16), shape((D, wide + LANES), bf16), shape((D, 2 * width), bf16),
            *(shape((8, m), f32) for m in (wide, LANES, width)),
        ],
        scratch_shapes=[
            vm((ROWS + 8, wide), f32), vm((NS, width), f32), vm((length, width), f32), vm((length, width), f32),
            *(vm((length, width), bf16) for _ in range(3)),
            vm((length, D), bf16), vm((length, D), bf16), vm((D, wide + LANES), bf16), vm((D, 2 * width), bf16),
            vm((4, 8, length), f32), vm((8, length), f32), vm((2, HEADS, LANES), f32), vm((3 * T, LANES), bf16),
            vm((T, width), f32), vm((T, width), bf16), vm((tall, width), f32),
            dma((3,)), lead, lead, lead, dma((11,)), dma((4,)), dma((4,)), dma((1,)), dma((1,)),
            dma((4,)), dma((4,)), lead, hops, hops, dma((4,)), dma((4,)),
            dma((1,)), dma((1,)), dma((4,)), dma((4,)), dma((3,)), dma((3,)),
        ],
        compiler_params=pltpu.CompilerParams(collective_id=2, has_side_effects=True, vmem_limit_bytes=ROOM),
        name="layer_forward",
    )(layer_input, out_grad, flat, w_zx, w_bc, w_dt, w_out)


def backward_body(
    n, own_rows, tokens, width,
    dy_ref, v_ref, xc_ref, dr_ref, st_ref, gate_ref, taps_ref, head_ref, chan_ref, early_ref, branch_ref,
    d_ref, small_ref, oearly_ref, obranch_ref,
    dxh, dstate, yst, bds, dyeb, utb, products, turn, acc, hacc, pick_ref, pick_t, fades, head_t, until_ref, reach_ref,
    own, slots, near, held, over_slot,
    load_sem, ring_send, ring_recv, near_send, near_recv, over_send, over_recv,
):
    pairs = width // LANES
    wide = width + 2 * NS
    step = pl.program_id(0)
    steps = LEN // ROWS
    pos, ring, me, across, beside = neighbours(n)
    opposite = lax.rem(me + 2, 4)
    next_door = me + 1 - 2 * lax.rem(me, 2)
    far = lax.rem(next_door + 2, 4)
    half = tokens // 2
    cuts = cut_rows(own_rows)

    def block_at(way, count):
        return ring_index(lax.rem(pos + (count if way else n - count), n), n)

    def hop(k, way, h):
        first, size = cuts[way]
        if h == 0:
            src = early_ref.at[span(block_at(way, 1) * own_rows + first, size), pl.ds(k * width, width)]
        else:
            src = slots[way][k].at[h - 1]
        return remote(
            src, slots[way][k].at[h], ring_send.at[way, k, h], ring_recv.at[way, k, h], ring[way]
        )

    def near_copy(turned, part):
        start = (next_door if turned else far) * tokens + part * half
        return remote(
            branch_ref.at[span(start, half)], near.at[turned, part],
            near_send.at[turned, part], near_recv.at[turned, part], beside,
        )

    def held_copy(turned, part):
        start = (me if turned else opposite) * tokens + part * half
        return pltpu.make_async_copy(
            branch_ref.at[span(start, half)], held.at[turned, part], load_sem.at[2 * turned + part]
        )

    def over_copy(part):
        return remote(held.at[0, part], over_slot.at[part], over_send.at[part], over_recv.at[part], across)

    def own_copy():
        return pltpu.make_async_copy(early_ref, own, load_sem.at[4])

    def ring_turn(k, h):
        for way in (0, 1):
            first, size = cuts[way]
            hop(k, way, h).wait_recv()
            block = block_at(way, 2 + h) if h < n - 2 else block_at(way, 0)

            tile = strip(size)

            def some(i, _, way=way, first=first, block=block, tile=tile):
                cols = slice(k * width, (k + 1) * width)
                came = slots[way][k][h, span(i * tile, tile), :]
                mine = own[span(block * own_rows + first + i * tile, tile), cols]
                if h < n - 2:
                    slots[way][k][h, span(i * tile, tile), :] = came + mine
                else:
                    oearly_ref[span(first + i * tile, tile), cols] = came.astype(f32) + mine.astype(f32)
                return 0

            lax.fori_loop(0, size // tile, some, 0)
            if h < n - 2:
                hop(k, way, h + 1).start()

    def ring_poll(k):
        for h in range(n - 1):
            pl.when(step == min(h + 1, steps - 1))(functools.partial(ring_turn, k, h))

    def add_near(turned):
        for part in (0, 1):
            held_copy(turned, part).wait()
            near_copy(turned, part).wait_recv()

            def some(i, _, part=part):
                at = span(i * 32, 32)
                if turned:
                    total = held[1, part, at, :].astype(f32) + near[1, part, at, :].astype(f32)
                    obranch_ref[span(part * half + i * 32, 32), :] = total
                else:
                    held[0, part, at, :] = held[0, part, at, :] + near[0, part, at, :]
                return 0

            lax.fori_loop(0, half // 32, some, 0)
            if not turned:
                over_copy(part).start()

    @pl.when(step == 0)
    def _():
        enter((*ring, across, beside))
        for way in (0, 1):
            hop(0, way, 0).start()
        for turned in (0, 1):
            for part in (0, 1):
                near_copy(turned, part).start()
                held_copy(turned, part).start()
        own_copy().start()
        dxh[T : T + 8, :] = jnp.zeros((8, wide), f32)
        dstate[...] = jnp.zeros_like(dstate)
        acc[...] = jnp.zeros_like(acc)
        hacc[...] = jnp.zeros_like(hacc)
        turn[...] = jnp.zeros_like(turn)
        pick_ref[...] = picked(width)
        channel = lax.broadcasted_iota(jnp.int32, (HEADS, width), 1)
        head = lax.broadcasted_iota(jnp.int32, (HEADS, width), 0)
        mine = (channel >= head * P_SIZE) & (channel < (head + 1) * P_SIZE)
        pick_t[...] = jnp.where(mine, 1.0, 0.0).astype(bf16)
        set_heads(head_ref, head_t, until_ref)
        from_here = jnp.where(block_iota(0) >= block_iota(1), 1.0, 0.0).astype(bf16)
        after = jnp.where(block_iota(0) < block_iota(1), 1.0, 0.0).astype(bf16)
        for k, matrix in enumerate((from_here, from_here, after, after)):
            reach_ref[k * T : (k + 1) * T, :] = matrix
        products[3 * T :, :] = jnp.zeros((HEADS, width), bf16)

    @pl.when(step == 1)
    def _():
        own_copy().wait()
        add_near(0)

    pl.when(step == 2)(functools.partial(add_near, 1))
    ring_poll(0)

    low_half = block_iota(1) < P_SIZE
    row_at, col_at = block_iota(0), block_iota(1)
    until = row_at <= col_at
    pair_lane = lax.broadcasted_iota(jnp.int32, (8, 2 * T), 1)
    pair_row = lax.broadcasted_iota(jnp.int32, (8, 2 * T), 0)
    each = jnp.where(lax.div(pair_lane, T) == pair_row, 1.0, 0.0).astype(bf16)
    ones = jnp.ones((8, T), bf16)

    def add(index, cols, value):
        acc[index, :, cols] += jnp.sum(value.reshape(T // 8, 8, LANES), axis=0)

    def conv_back(rows, block, d_act, xc, s, act):
        cols = slice(block * LANES, (block + 1) * LANES)
        dxh[0:T, cols] = d_act * (s + act * (1.0 - s))
        v = v_ref[rows, cols].astype(f32)
        total = None
        for m in range(CONV):
            moved = dxh[m : m + T, cols]
            if m == 0:
                add(CONV, cols, moved)
            add(CONV - 1 - m, cols, v * moved)
            term = taps_ref[CONV - 1 - m : CONV - m, cols] * moved
            total = term if total is None else total + term
        d_ref[rows, cols] = total.astype(bf16)

    for sub in reversed(range(ROWS // T)):
        rows = slice(sub * T, (sub + 1) * T)
        raw_t, dt_t, decay_t, dt, decay = head_rows(dr_ref, head_t, until_ref, rows)
        b_cols = slice(width, width + NS)
        c_cols = slice(width + NS, width + 2 * NS)
        b_xc, c_xc = xc_ref[rows, b_cols].astype(f32), xc_ref[rows, c_cols].astype(f32)
        b_s, c_s = sigmoid(b_xc), sigmoid(c_xc)
        b_act, c_act = b_xc * b_s, c_xc * c_s
        b_low, c_low = b_act.astype(bf16), c_act.astype(bf16)
        c_t = c_low.T
        scores_t = jnp.where(until, mm(b_low, c_low, NT), 0.0)
        ds_low = dstate[...].astype(bf16)
        yst[...] = mm(c_low, st_ref[sub])
        bds[...] = mm(b_low, ds_low)
        d_scores = jnp.zeros((T, LANES), f32)
        for p in range(pairs):
            cols = slice(p * LANES, (p + 1) * LANES)
            dy_low = dy_ref[rows, cols]
            dy = dy_low.astype(f32)
            xc = xc_ref[rows, cols].astype(f32)
            xs = sigmoid(xc)
            x = xc * xs
            l1, l2 = spread(decay[:, 2 * p : 2 * p + 1]), spread(decay[:, 2 * p + 1 : 2 * p + 2])
            both = jnp.where(low_half, l1, l2)
            dtb = jnp.where(
                low_half, spread(dt[:, 2 * p : 2 * p + 1]), spread(dt[:, 2 * p + 1 : 2 * p + 2])
            )
            u = x * dtb
            last = both[T - 1 : T, :]
            e1 = jnp.exp2(jnp.minimum(decay_t[2 * p : 2 * p + 1, :] - l1, 0.0))
            e2 = jnp.exp2(jnp.minimum(decay_t[2 * p + 1 : 2 * p + 2, :] - l2, 0.0))
            zero = jnp.zeros_like(dy_low)
            dy_parts = jnp.concatenate(
                [jnp.where(low_half, dy_low, zero), jnp.where(low_half, zero, dy_low)], axis=0
            )
            du_in = mm(
                jnp.concatenate([(scores_t * e1).astype(bf16), (scores_t * e2).astype(bf16)], axis=1), dy_parts
            )
            d_mix = mm(u.astype(bf16), dy_parts, NT)
            d1, d2 = d_mix[:, :T] * e1, d_mix[:, T:] * e2
            d_scores = d_scores + d1 + d2
            held_pairs = jnp.concatenate([(d1 * scores_t).astype(bf16), (d2 * scores_t).astype(bf16)], axis=1)
            reached_by = mm(ones, held_pairs)
            leaving = mm(each, held_pairs, NT)
            turn[2 * p : 2 * p + 1, :] = reached_by[0:1, :T] - leaving[0:1]
            turn[2 * p + 1 : 2 * p + 2, :] = reached_by[0:1, T:] - leaving[1:2]
            tail = jnp.exp2(last - both)
            fades[0:1, cols] = jnp.exp2(last)
            dye = dy * jnp.exp2(both)
            du_out = tail * bds[:, cols]
            du = du_in + du_out
            products[0:T, cols] = (dye * yst[:, cols]).astype(bf16)
            products[T : 2 * T, cols] = (u * du_out).astype(bf16)
            products[2 * T : 3 * T, cols] = (x * du).astype(bf16)
            dyeb[:, cols] = dye.astype(bf16)
            utb[:, cols] = (u * tail).astype(bf16)
            add(CONV + 1, cols, dy * x)
            conv_back(rows, p, dtb * du + chan_ref[1:2, cols] * dy, xc, xs, x)
        d_scores = jnp.where(until, d_scores, 0.0).astype(bf16)
        d_b = mm(d_scores, c_low) + mm(utb[...], ds_low, NT)
        d_c = mm(d_scores, b_low, TN) + mm(dyeb[...], st_ref[sub], NT)
        conv_back(rows, pairs, d_b, b_xc, b_s, b_act)
        conv_back(rows, pairs + 1, d_c, c_xc, c_s, c_act)
        fade = fades[0:1, :]
        before_ds = dstate[...]
        through = jnp.sum(before_ds * st_ref[sub].astype(f32), axis=0, keepdims=True) * fade
        products[3 * T : 3 * T + HEADS, :] = jnp.broadcast_to(through, (HEADS, width)).astype(bf16)
        dstate[...] = fade * before_ds + mm(c_t, dyeb[...])
        by_head = mm(pick_t[...], products[...], NT)
        inside = pieces(turn[...] + by_head[:, :T], 2)
        outside = pieces(by_head[:, T : 2 * T], 2)
        reached = mm(jnp.concatenate([inside, outside], axis=1), reach_ref[...])
        reached = reached + jnp.broadcast_to(by_head[:, 3 * T : 3 * T + 1], (HEADS, T))
        d_raw = (head_t[1] * reached + by_head[:, 2 * T : 3 * T]) * sigmoid(raw_t)
        d_ref[rows, wide:] = columns_of(d_raw).astype(bf16)
        hacc[0] += d_raw
        hacc[1] += dt_t * reached
        dxh[T : T + 8, :] = dxh[0:8, :]
        if sub == 1:
            @pl.when(step == 0)
            def _():
                for way in (0, 1):
                    hop(1, way, 0).start()

            ring_poll(1)

    @pl.when(step == steps - 1)
    def _():
        total = lambda a: jnp.sum(a, axis=0, keepdims=True)
        for k in range(CONV + 1):
            small_ref[k : k + 1, :] = total(acc[k])
        small_ref[CONV + 1 : CONV + 2, :width] = total(gate_ref[...])
        small_ref[CONV + 1 : CONV + 2, width : width + LANES] = total(columns_of(hacc[0]))
        small_ref[CONV + 1 : CONV + 2, width + LANES :] = total(columns_of(hacc[1])) * head_ref[1:2, :]
        small_ref[CONV + 2 :, :] = jnp.zeros((2, wide), f32)
        skip = mm_exact(acc[CONV + 1, :, :width], pick_ref[...].astype(f32))
        small_ref[CONV + 3 : CONV + 4, 512 : 512 + LANES] = total(skip)
        for part in (0, 1):
            over_copy(part).wait_recv()

            def some(i, _, part=part):
                at = span(part * half + i * 32, 32)
                obranch_ref[at, :] = obranch_ref[at, :] + over_slot[part, span(i * 32, 32), :].astype(f32)
                return 0

            lax.fori_loop(0, half // 32, some, 0)
        for part in (0, 1):
            over_copy(part).wait_send()
            for turned in (0, 1):
                near_copy(turned, part).wait_send()
        for h in range(n - 1):
            for k in (0, 1):
                for way in (0, 1):
                    hop(k, way, h).wait_send()


def ssd_backward(n, dy, v, xc, dr, st, gate, taps, head, chan, early, branch):
    length, width = dy.shape
    wide = width + 2 * NS
    steps = length // ROWS
    subs = ROWS // T
    own_rows, tokens = D // n, length // 4
    half = tokens // 2
    row = lambda m: pl.BlockSpec((ROWS, m), lambda i: (steps - 1 - i, 0))
    whole = lambda a: pl.BlockSpec(a.shape, lambda i: (0,) * a.ndim, pipeline_mode=pl.Buffered(1))
    fixed = lambda *shape: pl.BlockSpec(shape, lambda i: (0,) * len(shape))
    anywhere = pl.BlockSpec(memory_space=pl.ANY)
    vm, dma = pltpu.VMEM, pltpu.SemaphoreType.DMA
    return pl.pallas_call(
        functools.partial(backward_body, n, own_rows, tokens, width),
        grid=(steps,),
        in_specs=[
            row(width), row(wide), row(wide), row(LANES),
            pl.BlockSpec((subs, NS, width), lambda i: (steps - 1 - i, 0, 0)),
            whole(gate), whole(taps), whole(head), whole(chan), anywhere, anywhere,
        ],
        out_specs=[
            row(wide + LANES), fixed(8, wide), fixed(own_rows, 2 * width), fixed(tokens, D),
        ],
        out_shape=[
            jax.ShapeDtypeStruct((length, wide + LANES), bf16),
            jax.ShapeDtypeStruct((8, wide), f32),
            jax.ShapeDtypeStruct((own_rows, 2 * width), f32),
            jax.ShapeDtypeStruct((tokens, D), f32),
        ],
        scratch_shapes=[
            vm((T + 8, wide), f32), vm((NS, width), f32), vm((T, width), f32), vm((T, width), f32),
            vm((T, width), bf16), vm((T, width), bf16), vm((3 * T + HEADS, width), bf16),
            vm((HEADS, T), f32), vm((CONV + 2, 8, wide), f32), vm((2, HEADS, T), f32),
            vm((width, LANES), bf16), vm((HEADS, width), bf16), vm((8, width), f32), vm((2, HEADS, LANES), f32),
            vm((3 * T, LANES), bf16), vm((4 * T, LANES), bf16),
            vm((D, 2 * width), bf16),
            [[vm((n - 1, size, width), bf16) for _ in (0, 1)] for _, size in cut_rows(own_rows)],
            vm((2, 2, half, D), bf16), vm((2, 2, half, D), bf16), vm((2, half, D), bf16),
            dma((5,)), dma((2, 2, n - 1)), dma((2, 2, n - 1)), dma((2, 2)), dma((2, 2)), dma((2,)), dma((2,)),
        ],
        compiler_params=pltpu.CompilerParams(
            collective_id=3, has_side_effects=True, vmem_limit_bytes=ROOM
        ),
        name="layer_backward",
    )(dy, v, xc, dr, st, gate, taps, head, chan, early, branch)


def reduce_body(
    n, rows, tokens, starts,
    xg_ref, d_ref, dz_ref, wp_ref, w_ref, small_ref, flat_ref, gain_ref,
    oxs_ref, oback_ref, bc_ref, oflat_ref,
    xg, d, dz, wz, w, work, grads, slots, staged, near, over, smalls, tens, bc_slot,
    load_sem, ring_send, ring_recv, near_send, near_recv, over_send, over_recv,
    small_send, small_recv, ten_send, ten_recv, bc_send, bc_recv,
):
    pos, ring, me, across, beside = neighbours(n)
    cuts = cut_rows(rows)
    core = lax.rem(me, 2)
    opposite = lax.rem(me + 2, 4)
    next_door = me + 1 - 2 * core
    far = lax.rem(next_door + 2, 4)
    half = tokens // 2
    late = d.shape[1]
    width = dz.shape[1]
    tile = 2 * LANES
    tiles = D // tile
    columns = [pl.ds(lo, hi - lo) for lo, hi in starts]
    sources = [(d_ref.at[:, columns[0]], d.at[:, columns[0]])]
    sources += [(xg_ref.at[:, pl.ds(i * tile, tile)], xg.at[:, pl.ds(i * tile, tile)]) for i in range(tiles)]
    sources += [(d_ref.at[:, some], d.at[:, some]) for some in columns[1:]]
    sources += [
        (dz_ref, dz), (w_ref, w), (wp_ref.at[:, pl.ds(width, width)], wz), (small_ref, smalls.at[pos]),
    ]
    loads = [pltpu.make_async_copy(src, dst, load_sem.at[k]) for k, (src, dst) in enumerate(sources)]
    for load in loads:
        load.start()
    enter((*ring, across, beside))
    started = []

    def go(*args):
        copy = remote(*args)
        copy.start()
        started.append(copy)

    def block_at(way, count):
        return ring_index(lax.rem(pos + (count if way else n - count), n), n)

    def hop(k, way, h):
        lo, hi = starts[k]
        first, size = cuts[way]
        if h == 0:
            src = grads.at[span(block_at(way, 1) * rows + first, size), pl.ds(lo, hi - lo)]
        else:
            src = slots[way][k].at[h - 1]
        return remote(
            src, slots[way][k].at[h], ring_send.at[way, k, h], ring_recv.at[way, k, h], ring[way]
        )

    def product(k):
        lo, hi = starts[k]

        def some(i, _):
            at = pl.ds(pl.multiple_of(i * tile, tile), tile)
            if k == 0:
                pltpu.make_async_copy(xg_ref.at[:, at], xg.at[:, at], load_sem.at[1 + i]).wait()
            grads[at, lo:hi] = mm(xg[:, at], d[:, lo:hi], TN).astype(bf16)
            return 0

        loads[0 if k == 0 else tiles + k].wait()
        lax.fori_loop(0, tiles, some, 0)
        for way in (0, 1):
            hop(k, way, 0).start()

    def near_copy(turned, part):
        return remote(
            staged.at[turned, part], near.at[turned, part],
            near_send.at[turned, part], near_recv.at[turned, part], beside,
        )

    def over_copy(part):
        return remote(near.at[0, part], over.at[part], over_send.at[part], over_recv.at[part], across)

    def ring_turn(k, h):
        lo, hi = starts[k]
        for way in (0, 1):
            first, size = cuts[way]
            slot = slots[way][k].at[h]
            remote(slot, slot, ring_send.at[way, k, h], ring_recv.at[way, k, h], ring[way]).wait_recv()
            block = block_at(way, 2 + h) if h < n - 2 else block_at(way, 0)

            tile = strip(size)

            def some(i, _, way=way, first=first, block=block, tile=tile):
                came = slots[way][k][h, span(i * tile, tile), :]
                mine = grads[span(block * rows + first + i * tile, tile), lo:hi]
                if h < n - 2:
                    slots[way][k][h, span(i * tile, tile), :] = came + mine
                else:
                    oxs_ref[span(first + i * tile, tile), lo:hi] = came.astype(f32) + mine.astype(f32)
                return 0

            lax.fori_loop(0, size // tile, some, 0)
            if h < n - 2:
                hop(k, way, h + 1).start()

    def small_hop(way, h):
        here = smalls.at[lax.rem(pos + (h if way else n - h), n)]
        go(here, here, small_send.at[way, h], small_recv.at[way, h], ring[way])

    def small_lands(way, h):
        here = smalls.at[lax.rem(pos + (h + 1 if way else n - h - 1), n)]
        remote(here, here, small_send.at[way, h], small_recv.at[way, h], ring[way]).wait_recv()

    for k in range(len(starts)):
        product(k)
    for load in loads[tiles + len(starts) :]:
        load.wait()
    turns = {0: [(0, 0)], 1: [(1, 0), (2, 0)], 2: [(0, 1)], 3: [(1, 1), (2, 1)], 4: [(0, 2)], 5: [(1, 2), (2, 2)], 6: [(0, 3)], 7: [(1, 3), (2, 3)]}
    taken = [sum(k == group for some in turns.values() for k, _ in some) for group in range(len(starts))]

    def block(i, _):
        which, part = lax.div(i, 2), lax.rem(i, 2)
        own = lax.rem(which, 2)
        turned = lax.div(which, 2)
        target = lax.rem(next_door + own * (me - next_door) + 2 * (1 - turned), 4)
        at = span(target * tokens + part * half, half)
        total = mm(dz[at, :], wz[...], NT) + mm(d[at, :], w[...], NT)
        work[...] = total

        @pl.when(own == 0)
        def _():
            staged[turned, part] = work[...].astype(bf16)
            near_copy(turned, part).start()

        @pl.when(own == 1)
        def _():
            near_copy(turned, part).wait_recv()

        @pl.when(which == 1)
        def _():
            near[0, part] = (work[...] + near[0, part].astype(f32)).astype(bf16)
            over_copy(part).start()

        @pl.when(which == 3)
        def _():
            oback_ref[span(part * half, half), :] = work[...] + near[1, part].astype(f32)

        for at_block, some in turns.items():

            @pl.when(i == at_block)
            def _(some=some):
                for k, h in some:
                    ring_turn(k, h)

        return 0

    lax.fori_loop(0, 8, block, 0)
    for i in range(tiles):
        share = jnp.zeros((tile, LANES), f32)
        for c in range(late // LANES):
            cols = slice(c * LANES, (c + 1) * LANES)
            at = slice(i * tile, (i + 1) * tile)
            share = share + grads[at, cols].astype(f32) * w[at, cols].astype(f32)
        total = mm_exact(jnp.ones((8, LANES), f32), share, NT)[0:1] + gain_ref[0:1, i * tile : (i + 1) * tile]
        for c in range(2 * i, 2 * i + 2):
            row, col = 6 + c // 8, (c % 8) * LANES
            part = total[:, (c - 2 * i) * LANES : (c - 2 * i + 1) * LANES]
            smalls[pos, row : row + 1, col : col + LANES] = part / flat_ref[c : c + 1, :]

    rest = [(k, h) for h in range(n - 1) for k in (0, 1, 2) if h >= taken[k]]
    rest.sort(key=lambda turn: turn[1] - taken[turn[0]])

    def small_step(s):
        for way in (0, 1):
            if s > 0 and (way == 0 or s < n // 2):
                small_lands(way, s - 1)
            if s < n // 2 - way:
                small_hop(way, s)

    small_step(0)
    steps_done = 1
    for at, (k, h) in enumerate(rest):
        ring_turn(k, h)
        if (k, h) == (0, n - 2):
            bc_slot[0] = oxs_ref[:, starts[0][0] : starts[0][0] + 2 * NS]
            go(bc_slot.at[0], bc_slot.at[1], bc_send.at[0], bc_recv.at[0], beside)
        if at % 2 == 1 and steps_done < n // 2:
            small_step(steps_done)
            steps_done += 1
    for s in range(steps_done, n // 2):
        small_step(s)
    small_lands(0, n // 2 - 1)

    total = smalls[0]
    for i in range(1, n):
        total = total + smalls[i]
    tens[me] = total
    go(tens.at[me], tens.at[me], ten_send.at[0], ten_recv.at[0], beside)
    remote(bc_slot.at[1], bc_slot.at[1], bc_send.at[0], bc_recv.at[0], beside).wait_recv()
    bc_slot[2] = bc_slot[0] + bc_slot[1]
    go(bc_slot.at[2], bc_slot.at[3], bc_send.at[1], bc_recv.at[1], across)
    here = tens.at[next_door]
    remote(here, here, ten_send.at[0], ten_recv.at[0], beside).wait_recv()
    for k, target in ((0, me), (1, next_door)):
        here = tens.at[target]
        go(here, here, ten_send.at[1 + k], ten_recv.at[1 + k], across)
    for part in (0, 1):
        over_copy(part).wait_recv()

        def some(i, _, part=part):
            at = span(part * half + i * 32, 32)
            oback_ref[at, :] = oback_ref[at, :] + over[part, span(i * 32, 32), :].astype(f32)
            return 0

        lax.fori_loop(0, half // 32, some, 0)
    for k, target in ((0, opposite), (1, far)):
        here = tens.at[target]
        remote(here, here, ten_send.at[1 + k], ten_recv.at[1 + k], across).wait_recv()
    flat_gradients(width, tens, oflat_ref)
    remote(bc_slot.at[3], bc_slot.at[3], bc_send.at[1], bc_recv.at[1], across).wait_recv()
    bc_ref[...] = bc_slot[2] + bc_slot[3]
    for part in (0, 1):
        over_copy(part).wait_send()
        for turned in (0, 1):
            near_copy(turned, part).wait_send()
    for k in range(len(starts)):
        for way in (0, 1):
            for h in range(n - 1):
                hop(k, way, h).wait_send()
    for copy in started:
        copy.wait_send()


def flat_gradients(width, tens, out_ref):
    pairs = width // LANES
    heads = width // P_SIZE

    def sums(row, col):
        total = tens[0, row : row + 1, col : col + LANES]
        for t in range(1, 4):
            total = total + tens[t, row : row + 1, col : col + LANES]
        return total

    def put(row, value):
        out_ref[row : row + 1, :] = value

    for c in range(D // LANES):
        put(c, sums(6 + c // 8, (c % 8) * LANES))
    for t in range(4):
        for c in range(pairs):
            cols = slice(c * LANES, (c + 1) * LANES)
            put(GATE_ROW + pairs * t + c, tens[t, CONV + 1 : CONV + 2, cols])
            put(BIAS_ROW + pairs * t + c, tens[t, CONV : CONV + 1, cols])
            for k in range(CONV):
                put(TAPS_ROW + 4 * pairs * k + pairs * t + c, tens[t, k : k + 1, cols])
    for c in range(2):
        put(BIAS_BC_ROW + c, sums(CONV, width + c * LANES))
        for k in range(CONV):
            put(TAPS_BC_ROW + 2 * k + c, sums(k, width + c * LANES))
    kinds = ((CONV + 1, width), (CONV + 1, width + LANES), (CONV + 3, 512))
    rows = [tens[t, row : row + 1, col : col + LANES] for row, col in kinds for t in range(4)]
    rows = jnp.concatenate(rows + [jnp.zeros((16 - len(rows), LANES), f32)], axis=0)
    lane = lax.broadcasted_iota(jnp.int32, (LANES, 2 * LANES), 1)
    entry = lax.broadcasted_iota(jnp.int32, (LANES, 2 * LANES), 0)
    spread_out = mm_exact(rows, jnp.where(lax.rem(lane, heads) == entry, 1.0, 0.0).astype(f32))
    at = lax.broadcasted_iota(jnp.int32, (16, 2 * LANES), 1)
    source = lax.broadcasted_iota(jnp.int32, (16, 2 * LANES), 0)
    line = jnp.sum(jnp.where(lax.div(at, heads) == source, spread_out, 0.0), axis=0, keepdims=True)
    put(HEAD_ROW, line[:, :LANES])
    put(HEAD_ROW + 1, line[:, LANES:])


def reduce_all(n, xg, d, dz, wp, w, small, flat, gain):
    rows, tokens = D // n, dz.shape[0] // 4
    width, late = dz.shape[1], d.shape[1]
    starts = ((width, late), (0, width // 2), (width // 2, width))
    half = tokens // 2
    dma, vm = pltpu.SemaphoreType.DMA, pltpu.VMEM
    anywhere = pl.BlockSpec(memory_space=pl.ANY)
    inside = pl.BlockSpec(memory_space=pltpu.VMEM)
    return pl.pallas_call(
        functools.partial(reduce_body, n, rows, tokens, starts),
        in_specs=[anywhere] * 6 + [inside] * 2,
        out_specs=[inside] * 4,
        out_shape=[
            jax.ShapeDtypeStruct((rows, late), f32),
            jax.ShapeDtypeStruct((tokens, D), f32),
            jax.ShapeDtypeStruct((rows, 2 * NS), f32),
            jax.ShapeDtypeStruct((FLAT_ROWS, LANES), f32),
        ],
        scratch_shapes=[
            vm(xg.shape, bf16), vm(d.shape, bf16), vm(dz.shape, bf16), vm((D, width), bf16),
            vm((D, late), bf16),
            vm((half, D), f32), vm((D, late), bf16),
            [[vm((n - 1, size, hi - lo), bf16) for lo, hi in starts] for _, size in cut_rows(rows)],
            vm((2, 2, half, D), bf16), vm((2, 2, half, D), bf16), vm((2, half, D), bf16),
            vm((n, *small.shape), f32), vm((4, *small.shape), f32), vm((4, rows, 2 * NS), f32),
            dma((13,)), dma((2, 3, n - 1)), dma((2, 3, n - 1)), dma((2, 2)), dma((2, 2)), dma((2,)), dma((2,)),
            dma((2, n // 2)), dma((2, n // 2)), dma((3,)), dma((3,)), dma((2,)), dma((2,)),
        ],
        compiler_params=pltpu.CompilerParams(
            collective_id=1, has_side_effects=True, vmem_limit_bytes=ROOM
        ),
        name="reduce_all",
    )(xg, d, dz, wp, w, small, flat, gain)


def adamw_step(weight, first, second, grad, rate, decay):
    first_new = beta_first * first + (1.0 - beta_first) * grad
    second_new = beta_second * second + (1.0 - beta_second) * grad * grad
    hat_first = first_new * (1.0 / (1.0 - beta_first**STEP))
    hat_second = second_new * (1.0 / (1.0 - beta_second**STEP))
    weight_new = weight - rate * (hat_first / (jnp.sqrt(hat_second) + adam_eps) + decay * weight)
    return (weight_new, first_new, second_new)


def finish_body(
    width, heads,
    in_ref, cot_ref, branch_ref, back_ref, flat_ref, early_ref, late_ref, bcg_ref,
    zx_ref, zx1_ref, zx2_ref, bc_ref, bc1_ref, bc2_ref, out_ref, out1_ref, out2_ref, late_all_ref, dt_ref, dt1_ref, dt2_ref,
    layer_ref, grad_ref, zxn_ref, zx1n_ref, zx2n_ref, bcn_ref, bc1n_ref, bc2n_ref,
    outn_ref, out1n_ref, out2n_ref, dtn_ref, dt1n_ref, dt2n_ref,
):
    def update(refs, news, grad):
        fresh = adamw_step(*(ref[...] for ref in refs), grad, matrix_rate, matrix_decay)
        for ref, value in zip(news, fresh):
            ref[...] = value

    for k, grad in ((0, early_ref), (1, late_ref)):
        fresh = adamw_step(
            *(ref[:, k, :] for ref in (zx_ref, zx1_ref, zx2_ref)), grad[:, :width], matrix_rate, matrix_decay
        )
        for ref, value in zip((zxn_ref, zx1n_ref, zx2n_ref), fresh):
            ref[:, k, :] = value
    update((bc_ref, bc1_ref, bc2_ref), (bcn_ref, bc1n_ref, bc2n_ref), bcg_ref[...])
    update((out_ref, out1_ref, out2_ref), (outn_ref, out1n_ref, out2n_ref), early_ref[:, width:])

    @pl.when(pl.program_id(0) == 0)
    def _():
        unit = jnp.where(
            lax.broadcasted_iota(jnp.int32, (16, LANES), 0) == lax.broadcasted_iota(jnp.int32, (16, LANES), 1), 1.0, 0.0
        ).astype(f32)
        turned = mm_exact(unit, late_all_ref[:, width + 2 * NS :], NT)
        update((dt_ref, dt1_ref, dt2_ref), (dtn_ref, dt1n_ref, dt2n_ref), turned[:heads])

    rows = in_ref.shape[0]
    tile = 64

    def some(i, _):
        at = span(i * tile, tile)
        squares = jnp.zeros((tile, LANES), f32)
        inner = jnp.zeros((tile, LANES), f32)
        for c in range(D // LANES):
            cols = slice(c * LANES, (c + 1) * LANES)
            x = in_ref[at, cols].astype(f32)
            squares = squares + x * x
            inner = inner + x * flat_ref[c : c + 1, :] * back_ref[at, cols]
        r = lax.rsqrt(jnp.sum(squares, axis=-1, keepdims=True) / D + norm_eps)
        k = r * r * r * jnp.sum(inner, axis=-1, keepdims=True) / D
        r, k = jnp.broadcast_to(r, (tile, LANES)), jnp.broadcast_to(k, (tile, LANES))
        for c in range(D // LANES):
            cols = slice(c * LANES, (c + 1) * LANES)
            x = in_ref[at, cols].astype(f32)
            layer_ref[at, cols] = (x + branch_ref[at, cols]).astype(bf16)
            grad_ref[at, cols] = cot_ref[at, cols].astype(f32) + r * flat_ref[c : c + 1, :] * back_ref[at, cols] - x * k
        return 0

    lax.fori_loop(0, rows // tile, some, 0)


def finish(layer_input, out_grad, branch, back, flat, early, late, bcg, zx, bc, out, dt):
    (rows, width), heads = out[0].shape, dt[0].shape[0]
    steps = 4 if rows % 32 == 0 else 2
    part = lambda a: pl.BlockSpec((a.shape[0] // steps, *a.shape[1:]), lambda i: (i,) + (0,) * (a.ndim - 1))
    whole = lambda a: pl.BlockSpec(a.shape, lambda i: (0,) * a.ndim)
    like = lambda a, dtype=f32: jax.ShapeDtypeStruct(a.shape, dtype)
    weights = (*zx, *bc, *out)
    return pl.pallas_call(
        functools.partial(finish_body, width, heads),
        grid=(steps,),
        in_specs=[
            *(part(a) for a in (layer_input, out_grad, branch, back)), whole(flat),
            *(part(a) for a in (early, late, bcg, *weights)), whole(late), *(whole(a) for a in dt),
        ],
        out_specs=[part(layer_input), part(back), *(part(a) for a in weights), *(whole(a) for a in dt)],
        out_shape=[like(layer_input, bf16), like(back), *(like(a) for a in weights), *(like(a) for a in dt)],
        compiler_params=pltpu.CompilerParams(vmem_limit_bytes=ROOM),
        name="finish",
    )(layer_input, out_grad, branch, back, flat, early, late, bcg, *weights, late, *dt)


def local(
    layer_input,
    out_grad,
    small_params,
    small_first,
    small_second,
    w_zx,
    zx_first,
    zx_second,
    w_bc,
    bc_first,
    bc_second,
    w_dt,
    dt_first,
    dt_second,
    w_out,
    out_first,
    out_second,
):
    n = lax.axis_size("dp")
    flat = jnp.pad(small_params, (0, FLAT_ROWS * LANES - small_params.shape[0])).reshape(FLAT_ROWS, LANES)
    v, xc, dr, st, dy, dz, branch, early, gate, gain, xg, w_all, pair_all, taps, head, chan = ssd_forward(
        n, layer_input, out_grad, flat, w_zx, w_bc, w_dt.T, w_out
    )
    d_late, small, owner_early, own_branch = ssd_backward(
        n, dy, v, xc, dr, st, gate, taps, head, chan, early, branch
    )
    owner_late, d_normed_in, owner_bc, flat_grad = reduce_all(
        n, xg, d_late, dz, pair_all, w_all, small, flat, gain
    )
    small_grad = flat_grad.reshape(-1)[: small_params.shape[0]]
    small_new, small_first_new, small_second_new = adamw_step(
        small_params, small_first, small_second, small_grad, small_rate, 0.0
    )
    (
        layer_output, input_grad, zx_new, zx_first_new, zx_second_new, bc_new, bc_first_new, bc_second_new,
        out_new, out_first_new, out_second_new, dt_new, dt_first_new, dt_second_new,
    ) = finish(
        layer_input, out_grad, own_branch, d_normed_in, flat, owner_early, owner_late, owner_bc,
        (w_zx, zx_first, zx_second), (w_bc, bc_first, bc_second), (w_out, out_first, out_second),
        (w_dt.T, dt_first.T, dt_second.T),
    )
    dt_new, dt_first_new, dt_second_new = dt_new.T, dt_first_new.T, dt_second_new.T
    return (
        layer_output,
        input_grad,
        small_new,
        small_first_new,
        small_second_new,
        zx_new,
        zx_first_new,
        zx_second_new,
        bc_new,
        bc_first_new,
        bc_second_new,
        dt_new,
        dt_first_new,
        dt_second_new,
        out_new,
        out_first_new,
        out_second_new,
    )


def solution(mesh):
    return jax.shard_map(
        local,
        mesh=mesh,
        in_specs=(
            P(("dp", "tensor"), None),
            P(("dp", "tensor"), None),
            P(),
            P(),
            P(),
            P("dp", None, "tensor"),
            P("dp", None, "tensor"),
            P("dp", None, "tensor"),
            P("dp", None),
            P("dp", None),
            P("dp", None),
            P("dp", "tensor"),
            P("dp", "tensor"),
            P("dp", "tensor"),
            P("dp", "tensor"),
            P("dp", "tensor"),
            P("dp", "tensor"),
        ),
        out_specs=(
            P(("dp", "tensor"), None),
            P(("dp", "tensor"), None),
            P(),
            P(),
            P(),
            P("dp", None, "tensor"),
            P("dp", None, "tensor"),
            P("dp", None, "tensor"),
            P("dp", None),
            P("dp", None),
            P("dp", None),
            P("dp", "tensor"),
            P("dp", "tensor"),
            P("dp", "tensor"),
            P("dp", "tensor"),
            P("dp", "tensor"),
            P("dp", "tensor"),
        ),
        check_vma=False,
    )
```

```python
import functools

import jax
import jax.numpy as jnp
from jax import lax
from jax.experimental import pallas as pl
from jax.experimental.pallas import tpu as pltpu
from jax.sharding import PartitionSpec as P

D = 1536
DI = 3072
H = 48
NS = 128
P_SIZE = 64
CONV = 4
LEN = 2048
STEP = 10

T = 128
ROWS = 256
LANES = 128
ROOM = 60 * 2**20
EARLY_HOPS = 3

norm_eps = 1e-05
adam_eps = 1e-08
beta_first = 0.9
beta_second = 0.95
matrix_rate = 0.01
small_rate = 0.1
matrix_decay = 0.1

f32 = jnp.float32
bf16 = jnp.bfloat16
NN = (((1,), (0,)), ((), ()))
NT = (((1,), (1,)), ((), ()))
TN = (((0,), (0,)), ((), ()))
HIGHEST = lax.Precision.HIGHEST


GATE_ROW, TAPS_ROW, BIAS_ROW, TAPS_BC_ROW, BIAS_BC_ROW, HEAD_ROW, FLAT_ROWS = 12, 36, 132, 156, 164, 166, 168


def mm(a, b, dims=NN):
    return lax.dot_general(a, b, dims, preferred_element_type=f32)


def mm_exact(a, b, dims=NN):
    return lax.dot_general(a, b, dims, preferred_element_type=f32, precision=HIGHEST)


def sigmoid(v):
    return 0.5 * jnp.tanh(0.5 * v) + 0.5


def softplus(v):
    return jnp.maximum(v, 0.0) + jnp.log1p(jnp.exp(-jnp.abs(v)))


def spread(col):
    return jnp.broadcast_to(col, (T, LANES))


def block_iota(axis):
    return lax.broadcasted_iota(jnp.int32, (T, LANES), axis)


HEADS = 16
LOG2_E = 1.4426950408889634


def pieces(value, count):
    parts = []
    for k in range(count):
        part = value.astype(bf16)
        parts.append(part)
        if k < count - 1:
            value = value - part.astype(f32)
    return jnp.concatenate(parts, axis=1)


def columns_of(rows):
    return jnp.concatenate([rows, jnp.zeros((LANES - HEADS, T), f32)], axis=0).T


def set_heads(head_ref, head_t, until):
    turned = jnp.concatenate([head_ref[...], jnp.zeros((LANES - 8, LANES), f32)], axis=0).T
    head_t[0] = spread(turned[:, 0:1])[:HEADS]
    head_t[1] = spread(turned[:, 1:2])[:HEADS]
    matrix = jnp.where(block_iota(0) <= block_iota(1), 1.0, 0.0).astype(bf16)
    for k in range(3):
        until[k * T : (k + 1) * T, :] = matrix


def head_rows(dr_ref, head_t, until, rows):
    raw = dr_ref[rows, :].T[:HEADS] + head_t[0]
    dt = softplus(raw)
    decay = mm(pieces(dt * (head_t[1] * LOG2_E), 3), until[...])
    return raw, dt, decay, columns_of(dt), columns_of(decay)


def ring_place(n):
    me = lax.axis_index("dp")
    z, x = lax.div(me, 2), lax.rem(me, 2)
    return z + x * (n - 1 - 2 * z)


def ring_index(pos, n):
    back = lax.div(pos, n // 2)
    return 2 * pos + back * (2 * n - 1 - 4 * pos)


def neighbours(n):
    pos = ring_place(n)
    right = ring_index(lax.rem(pos + 1, n), n)
    left = ring_index(lax.rem(pos + n - 1, n), n)
    me = lax.axis_index("tensor")
    y, core = lax.div(me, 2), lax.rem(me, 2)
    across = 2 * (1 - y) + core
    beside = 2 * y + 1 - core
    return pos, ({"dp": right}, {"dp": left}), me, {"tensor": across}, {"tensor": beside}


def greet(peers):
    barrier = pltpu.get_barrier_semaphore()
    for peer in peers:
        pl.semaphore_signal(barrier, inc=1, device_id=peer, device_id_type=pl.DeviceIdType.MESH)


def enter(peers):
    greet(peers)
    pl.semaphore_wait(pltpu.get_barrier_semaphore(), len(peers))


def remote(src, dst, send_sem, recv_sem, peer):
    return pltpu.make_async_remote_copy(
        src_ref=src, dst_ref=dst, send_sem=send_sem, recv_sem=recv_sem,
        device_id=peer, device_id_type=pl.DeviceIdType.MESH,
    )


def span(start, size):
    return pl.ds(pl.multiple_of(start, 16), size)


def strip(rows):
    return next(size for size in (48, 32, 16) if rows % size == 0)


def cut_rows(rows):
    top = rows // 32 * 16
    return ((0, top), (top, rows - top))


def forward_body(
    n, rows, tokens, width,
    in_ref, cot_ref, flat_ref, wzx_ref, wbc_ref, wdt_ref, wout_ref,
    v_ref, xc_ref, dr_ref, st_ref, dy_ref, dz_ref, branch_ref, gz_ref, go_ref, carry_ref, gate_ref, gain_ref,
    xg_ref, ws_ref, wps_ref, taps_ref, head_ref, chan_ref,
    halo, state, y_all, z_all, dn_all, nl_all, dz_all, xg, cots, ws, wps, sums, red, head_t, until, across_state, tails, first_slots,
    own_keep, lead_keep, lead_send, lead_recv, x_keep, x_over_send, x_over_recv, x_side_send, x_side_recv,
    x_pass_send, x_pass_recv, ring_keep, ring_send, ring_recv, over_send, over_recv,
    side_send, side_recv, pass_send, pass_recv, sum_send, sum_recv, first_send, first_recv,
):
    pairs = width // LANES
    wide = width + 2 * NS
    step = pl.program_id(0)
    steps = LEN // ROWS
    tall = 2 * ROWS
    norming = steps
    gating = norming + LEN // tall
    forming = gating + LEN // tall
    go_from = forming + steps
    gz_from = go_from + D // ROWS
    branching = gz_from + D // ROWS
    last_step = branching + LEN // tall - 1
    pos, ring, me, across, beside = neighbours(n)
    opposite = lax.rem(me + 2, 4)
    next_door = me + 1 - 2 * lax.rem(me, 2)
    far = lax.rem(next_door + 2, 4)
    askew = {"tensor": far}
    quarter = tokens // 4
    hops = n // 2
    cuts = cut_rows(rows)
    mine = ring_index(pos, n)

    late = wide + LANES
    parts_of = ((0, width), (width, width))

    def hop(k, part, way, h):
        first, size = cuts[part]
        cols = pl.ds(*parts_of[k])
        block = ring_index(lax.rem(pos + (h if way else n - h), n), n)
        here = wps.at[span(block * rows + first, size), cols]
        return remote(here, here, ring_send.at[way, part, k, h], ring_recv.at[way, part, k, h], ring[way])

    def hop_lands(k, part, way, h):
        first, size = cuts[part]
        block = ring_index(lax.rem(pos + (h + 1 if way else n - h - 1), n), n)
        return span(block * rows + first, size), pl.ds(*parts_of[k])

    def hop_arrival(k, part, way, h):
        here = wps.at[hop_lands(k, part, way, h)]
        return remote(here, here, ring_send.at[way, part, k, h], ring_recv.at[way, part, k, h], ring[way])

    def hop_keep(part, way, h):
        at = hop_lands(1, part, way, h)
        return pltpu.make_async_copy(wps.at[at], wps_ref.at[at], ring_keep.at[way, part, h])

    def hop_ways(h):
        return [(part, way) for part in (0, 1) for way in (0, 1) if h < hops - 1 or part == way]

    def hop_on(k, h):
        for part, way in hop_ways(h - 1) if h > 0 else ():
            hop_arrival(k, part, way, h - 1).wait_recv()
            if k == 1:
                hop_keep(part, way, h - 1).start()
            if h < hops and (part, way) in hop_ways(h):
                hop(k, part, way, h).start()
        if h == 0:
            for part, way in hop_ways(0):
                hop(k, part, way, 0).start()

    def over(k):
        return remote(
            cot_ref.at[pl.ds(k * quarter, quarter)], cots.at[span(me * tokens + k * quarter, quarter)],
            over_send.at[k], over_recv.at[k], across,
        )

    def landed(start, size, send, recv, peer):
        here = cots.at[span(start, size)]
        return remote(here, here, send, recv, peer)

    def over_arrival(k):
        return landed(opposite * tokens + k * quarter, quarter, over_send.at[k], over_recv.at[k], across)

    def passing(k):
        return landed(opposite * tokens + k * quarter, quarter, pass_send.at[k], pass_recv.at[k], beside)

    def pass_arrival(k):
        return landed(far * tokens + k * quarter, quarter, pass_send.at[k], pass_recv.at[k], beside)

    def side():
        return remote(cot_ref, cots.at[span(me * tokens, tokens)], side_send.at[0], side_recv.at[0], beside)

    def side_arrival():
        return landed(next_door * tokens, tokens, side_send.at[0], side_recv.at[0], beside)

    def own_cot():
        return pltpu.make_async_copy(cot_ref, cots.at[span(me * tokens, tokens)], own_keep.at[0])

    def own_z():
        at = span(mine * rows, rows), pl.ds(*parts_of[1])
        return pltpu.make_async_copy(wps.at[at], wps_ref.at[at], own_keep.at[1])

    def pass_on(*pieces):
        for k in pieces:
            over_arrival(k).wait_recv()
            passing(k).start()

    def normalize(k):
        def some(i, _):
            at = span(me * tokens + k * quarter + i * 64, 64)
            squares = jnp.zeros((64, LANES), f32)
            for c in range(D // LANES):
                x = xg[at, c * LANES : (c + 1) * LANES].astype(f32)
                squares = squares + x * x
            inverse = lax.rsqrt(jnp.sum(squares, axis=-1, keepdims=True) / D + norm_eps)
            inverse = jnp.broadcast_to(inverse, (64, LANES))
            for c in range(D // LANES):
                cols = slice(c * LANES, (c + 1) * LANES)
                xg[at, cols] = (xg[at, cols].astype(f32) * inverse * flat_ref[c : c + 1, :]).astype(bf16)
            return 0

        lax.fori_loop(0, quarter // 64, some, 0)

    @pl.when(step == 0)
    def _():
        own_rows = span(me * tokens, tokens)
        greet((*ring, across, beside, askew))
        load = pltpu.make_async_copy(in_ref, xg.at[own_rows], own_keep.at[2])
        load.start()
        own_cot().start()
        mine_at = span(mine * rows, rows)
        ws[mine_at, :width] = wzx_ref[:, 1, :].astype(bf16)
        ws[mine_at, width:wide] = wbc_ref[...].astype(bf16)
        heads = wdt_ref.shape[0]
        unit = jnp.where(
            lax.broadcasted_iota(jnp.int32, (16, LANES), 0) == lax.broadcasted_iota(jnp.int32, (16, LANES), 1), 1.0, 0.0
        ).astype(bf16)
        steps_w = jnp.concatenate([wdt_ref[...], jnp.zeros((16 - heads, rows), f32)], axis=0).astype(bf16)
        ws[mine_at, wide:] = mm(steps_w, unit, TN).astype(bf16)
        load.wait()
        normalize(0)
        pl.semaphore_wait(pltpu.get_barrier_semaphore(), 5)
        started, kept = [], []

        def go(*args):
            copy = remote(*args)
            copy.start()
            started.append(copy)

        def keep(src, dst, sem):
            copy = pltpu.make_async_copy(src, dst, sem)
            copy.start()
            kept.append(copy)

        def arrived(part, way, h, block):
            first, size = cuts[part]
            at = span(block * rows + first, size)
            remote(
                ws.at[at], ws.at[at], lead_send.at[way, part, h], lead_recv.at[way, part, h], ring[way]
            ).wait_recv()
            keep(ws.at[at], ws_ref.at[at], lead_keep.at[way, part, h])

        def lead(h, parts=(0, 1)):
            for part in parts:
                first, size = cuts[part]
                for way in (0, 1):
                    block = ring_index(lax.rem(pos + (h if way else n - h), n), n)
                    here = ws.at[span(block * rows + first, size)]
                    if h > 0:
                        arrived(part, way, h - 1, block)
                    if h == hops - 1 and part != way:
                        continue
                    go(here, here, lead_send.at[way, part, h], lead_recv.at[way, part, h], ring[way])

        def x_over(k):
            at = span(me * tokens + k * quarter, quarter)
            go(xg.at[at], xg.at[at], x_over_send.at[k], x_over_recv.at[k], across)

        def x_pass(k):
            at = span(opposite * tokens + k * quarter, quarter)
            here = xg.at[at]
            remote(here, here, x_over_send.at[k], x_over_recv.at[k], across).wait_recv()
            go(here, here, x_pass_send.at[k], x_pass_recv.at[k], beside)
            keep(here, xg_ref.at[at], x_keep.at[k])

        def x_pass_lands(k):
            at = span(far * tokens + k * quarter, quarter)
            remote(xg.at[at], xg.at[at], x_pass_send.at[k], x_pass_recv.at[k], beside).wait_recv()
            keep(xg.at[at], xg_ref.at[at], x_keep.at[4 + k])

        lead(0, (0,))
        leading = list(started)
        x_over(0)
        for k in (1, 2, 3):
            normalize(k)
            if k == 1:
                x_over(1)
        go(xg.at[own_rows], xg.at[own_rows], x_side_send.at[0], x_side_recv.at[0], beside)
        keep(xg.at[own_rows], xg_ref.at[own_rows], x_keep.at[8])
        wps[mine_at, :width] = wout_ref[...].astype(bf16)
        wps[mine_at, width:] = wzx_ref[:, 0, :].astype(bf16)
        for copy in leading:
            copy.wait_send()
            started.remove(copy)
        lead(0, (1,))
        keep(ws.at[mine_at], ws_ref.at[mine_at], x_keep.at[9])
        own_z().start()
        halo[0:8, :] = jnp.zeros((8, wide), f32)
        state[...] = jnp.zeros_like(state)
        gate_ref[...] = jnp.zeros_like(gate_ref)
        parameter_rows(me, width, flat_ref, taps_ref, head_ref, chan_ref)
        set_heads(head_ref, head_t, until)
        lead(1)
        x_over(2)
        at = span(next_door * tokens, tokens)
        remote(xg.at[at], xg.at[at], x_side_send.at[0], x_side_recv.at[0], beside).wait_recv()
        keep(xg.at[at], xg_ref.at[at], x_keep.at[10])
        side().start()
        lead(2)
        x_over(3)
        x_pass(0)
        x_pass(1)
        for h in range(3, hops):
            lead(h)
        hop_on(0, 0)
        x_pass(2)
        over(0).start()
        x_pass_lands(0)
        x_pass_lands(1)
        x_pass(3)
        for part in (0, 1):
            arrived(part, part, hops - 1, ring_index(lax.rem(pos + n // 2, n), n))
        over(1).start()
        x_pass_lands(2)
        x_pass_lands(3)
        for copy in kept:
            copy.wait()
        for copy in started:
            copy.wait_send()

    for h in range(1, hops):
        pl.when(step == min(2 * h - 1, norming - 1))(functools.partial(hop_on, 0, h))
    pl.when(step == norming - 1)(functools.partial(hop_on, 0, hops))
    for h in range(hops):
        pl.when(step == min(2 * h + 2, norming))(functools.partial(hop_on, 1, h))
    pl.when(step == gating)(functools.partial(hop_on, 1, hops))

    @pl.when(step == 2)
    def _():
        over(2).start()

    @pl.when(step == 4)
    def _():
        over(3).start()
        pass_on(0, 1)

    pl.when(step == steps - 1)(functools.partial(pass_on, 2))

    @pl.when(step < norming)
    def _():
        scan_step(
            width, step, xg, ws, taps_ref, head_ref, chan_ref,
            v_ref, xc_ref, dr_ref, st_ref, halo, state, y_all, head_t, until, across_state, tails,
            functools.partial(pass_on, 3),
        )

    @pl.when(step == norming)
    def _():
        side_arrival().wait_recv()
        for k in range(4):
            pass_arrival(k).wait_recv()
        own_cot().wait()
        own_z().wait()

    @pl.when((step >= norming) & (step < gating))
    def _():
        at = span((step - norming) * tall, tall)
        dn_all[at, :] = mm(cots[at, :], wps[:, :width]).astype(bf16)

    @pl.when((step >= gating) & (step < forming))
    def _():
        first = (step - gating) * tall
        at = span(first, tall)
        z_all[at, :] = mm(xg[at, :], wps[:, width:])
        ones = jnp.ones((8, LANES), f32)
        for sub in range(tall // T):
            rows_at = span(first + sub * T, T)
            squares = jnp.zeros((T, LANES), f32)
            inner = jnp.zeros((T, LANES), f32)
            for p in range(pairs):
                cols = slice(p * LANES, (p + 1) * LANES)
                z = z_all[rows_at, cols]
                gated = y_all[rows_at, cols] * (z * sigmoid(z))
                squares = squares + gated * gated
                inner = inner + gated * chan_ref[0:1, cols] * dn_all[rows_at, cols].astype(f32)
            lanes = pl.ds(pl.multiple_of(first + sub * T, T), T)
            sums[me, 0:4, lanes] = mm_exact(ones, squares, NT)[0:4]
            sums[me, 4:8, lanes] = mm_exact(ones, inner, NT)[4:8]

    @pl.when(step == forming - 1)
    def _():
        peers = ((beside, next_door), (across, opposite), (askew, far))
        for k, (peer, _) in enumerate(peers):
            remote(sums.at[me], sums.at[me], sum_send.at[k], sum_recv.at[k], peer).start()
        for h in range(hops):
            for part, way in hop_ways(h):
                for k in (0, 1):
                    hop(k, part, way, h).wait_send()
                hop_keep(part, way, h).wait()
        side().wait_send()
        for k in range(4):
            over(k).wait_send()
            passing(k).wait_send()
        for k, (peer, other) in enumerate(peers):
            remote(sums.at[other], sums.at[other], sum_send.at[k], sum_recv.at[k], peer).wait()
        red[...] = ((sums[0] + sums[1]) + sums[2]) + sums[3]

    @pl.when((step >= forming) & (step < go_from))
    def _():
        first = (step - forming) * ROWS
        lanes = pl.ds(pl.multiple_of(first, ROWS), ROWS)
        q_row = lax.rsqrt(red[0:4, lanes] / DI + norm_eps)
        k_row = q_row * q_row * q_row * red[4:8, lanes] / DI
        turned = jnp.concatenate([q_row, k_row], axis=0).T
        for sub in range(ROWS // T):
            rows_at = slice(sub * T, (sub + 1) * T)
            at = span(first + sub * T, T)
            q, kk = spread(turned[rows_at, 0:1]), spread(turned[rows_at, 4:5])
            for p in range(pairs):
                cols = slice(p * LANES, (p + 1) * LANES)
                z, y, dn = z_all[at, cols], y_all[at, cols], dn_all[at, cols].astype(f32)
                gain = chan_ref[0:1, cols]
                s = sigmoid(z)
                sz = z * s
                gated = y * sz
                gq = gated * q
                dg = q * gain * dn - gated * kk
                gate_ref[:, cols] += jnp.sum((gq * dn).reshape(T // 8, 8, LANES), axis=0)
                nl_all[at, cols] = (gq * gain).astype(bf16)
                dz = (dg * y * (s + sz * (1.0 - s))).astype(bf16)
                dz_all[at, cols] = dz
                dz_ref[rows_at, cols] = dz
                dy_ref[rows_at, cols] = (dg * sz).astype(bf16)

    def block_at(way, count):
        return ring_index(lax.rem(pos + (count if way else n - count), n), n)

    def first_hop(way, h):
        first, size = cuts[way]
        src = ws.at[span(block_at(way, 1) * rows + first, size), pl.ds(0, width)] if h == 0 else first_slots[way].at[h - 1]
        return remote(src, first_slots[way].at[h], first_send.at[way, h], first_recv.at[way, h], ring[way])

    def first_turn(h):
        for way in (0, 1):
            first, size = cuts[way]
            first_hop(way, h).wait_recv()
            block = block_at(way, 2 + h)
            tile = strip(size)

            def some(i, _, way=way, first=first, block=block, tile=tile):
                at = span(i * tile, tile)
                total = first_slots[way][h, at, :] + ws[span(block * rows + first + i * tile, tile), :width]
                if h < EARLY_HOPS - 1:
                    first_slots[way][h, at, :] = total
                else:
                    carry_ref[span(first + i * tile, tile), :] = total
                return 0

            lax.fori_loop(0, size // tile, some, 0)
            if h < EARLY_HOPS - 1:
                first_hop(way, h + 1).start()

    @pl.when((step >= go_from) & (step < gz_from))
    def _():
        first = (step - go_from) * ROWS
        lanes = pl.ds(pl.multiple_of(first, ROWS), ROWS)
        grad = mm(cots[:, lanes], nl_all[...], TN).astype(bf16)
        go_ref[...] = grad
        ws[span(first, ROWS), :width] = grad

    @pl.when(step == gz_from)
    def _():
        for way in (0, 1):
            first_hop(way, 0).start()

    pl.when(step == gz_from + 4)(functools.partial(first_turn, 0))
    pl.when(step == branching + 1)(functools.partial(first_turn, 1))

    @pl.when((step >= gz_from) & (step < branching))
    def _():
        first = (step - gz_from) * ROWS
        at = span(first, ROWS)
        lanes = pl.ds(pl.multiple_of(first, ROWS), ROWS)
        grad = mm(xg[:, lanes], dz_all[...], TN)
        gz_ref[...] = grad.astype(bf16)
        share = jnp.zeros((ROWS, LANES), f32)
        for p in range(pairs):
            cols = slice(p * LANES, (p + 1) * LANES)
            w = wps[at, width + p * LANES : width + (p + 1) * LANES]
            share = share + grad[:, cols] * w.astype(f32)
        gain_ref[:, lanes] = mm_exact(jnp.ones((8, LANES), f32), share, NT)

    @pl.when(step >= branching)
    def _():
        branch_ref[...] = mm(nl_all[span((step - branching) * tall, tall), :], wps[:, :width], NT).astype(bf16)

    @pl.when(step == last_step)
    def _():
        first_turn(EARLY_HOPS - 1)
        for way in (0, 1):
            for h in range(EARLY_HOPS):
                first_hop(way, h).wait_send()


def parameter_rows(me, width, flat_ref, taps_ref, head_ref, chan_ref):
    pairs = width // LANES
    heads = width // P_SIZE
    taps_ref[...] = jnp.zeros_like(taps_ref)
    chan_ref[...] = jnp.zeros_like(chan_ref)
    for c in range(pairs):
        cols = slice(c * LANES, (c + 1) * LANES)
        chan_ref[0:1, cols] = flat_ref[pl.ds(GATE_ROW + pairs * me + c, 1), :]
        taps_ref[CONV : CONV + 1, cols] = flat_ref[pl.ds(BIAS_ROW + pairs * me + c, 1), :]
        for k in range(CONV):
            taps_ref[k : k + 1, cols] = flat_ref[pl.ds(TAPS_ROW + 4 * pairs * k + pairs * me + c, 1), :]
    for c in range(2):
        cols = slice(width + c * LANES, width + (c + 1) * LANES)
        taps_ref[CONV : CONV + 1, cols] = flat_ref[BIAS_BC_ROW + c : BIAS_BC_ROW + c + 1, :]
        for k in range(CONV):
            row = TAPS_BC_ROW + 2 * k + c
            taps_ref[k : k + 1, cols] = flat_ref[row : row + 1, :]
    both = jnp.concatenate([flat_ref[HEAD_ROW : HEAD_ROW + 1, :], flat_ref[HEAD_ROW + 1 : HEAD_ROW + 2, :]], axis=1)
    both = jnp.broadcast_to(both, (8, 2 * LANES))
    lane = lax.broadcasted_iota(jnp.int32, (2 * LANES, LANES), 0)
    head = lax.broadcasted_iota(jnp.int32, (2 * LANES, LANES), 1)

    def take(kind):
        match = (lane == 4 * heads * kind + heads * me + head) & (head < heads)
        return mm_exact(both, jnp.where(match, 1.0, 0.0).astype(f32))

    valid = lax.broadcasted_iota(jnp.int32, (8, LANES), 1) < heads
    row = lax.broadcasted_iota(jnp.int32, (8, LANES), 0)
    rates = jnp.where(valid, -jnp.exp(take(1)), 0.0)
    head_ref[...] = jnp.where(row == 0, take(0), jnp.where(row == 1, rates, 0.0))
    skip = mm_exact(take(2), picked(width).astype(f32), NT)
    chan_ref[1:2, :] = skip[0:1]


def picked(width):
    channel = lax.broadcasted_iota(jnp.int32, (width, LANES), 0)
    head = lax.broadcasted_iota(jnp.int32, (width, LANES), 1)
    return jnp.where((channel >= head * P_SIZE) & (channel < (head + 1) * P_SIZE), 1.0, 0.0).astype(bf16)


def scan_step(
    width, step, xg, w_ref, taps_ref, head_ref, chan_ref,
    v_ref, xc_ref, dr_ref, st_ref, halo, state, y_all, head_t, until, across_state, tails, late_turn,
):
    pairs = width // LANES
    wide = width + 2 * NS
    mine = span(step * ROWS, ROWS)
    dr_ref[...] = mm(xg[mine, :], w_ref[:, wide:])
    halo[8 : 8 + ROWS, :] = mm(xg[mine, :], w_ref[:, :wide])
    low_half = block_iota(1) < P_SIZE
    causal = block_iota(0) >= block_iota(1)

    def convolved(sub, block):
        cols = slice(block * LANES, (block + 1) * LANES)
        total = taps_ref[CONV : CONV + 1, cols]
        for k in range(CONV):
            first = 8 - (CONV - 1) + k + sub * T
            total = total + taps_ref[k : k + 1, cols] * halo[first : first + T, cols]
        rows = slice(sub * T, (sub + 1) * T)
        xc_ref[rows, cols] = total.astype(bf16)
        v_ref[rows, cols] = halo[8 + sub * T : 8 + (sub + 1) * T, cols].astype(bf16)
        return total * sigmoid(total)

    for sub in range(ROWS // T):
        rows = slice(sub * T, (sub + 1) * T)
        _, _, decay_t, dt, decay = head_rows(dr_ref, head_t, until, rows)
        b_low = convolved(sub, pairs).astype(bf16)
        c_low = convolved(sub, pairs + 1).astype(bf16)
        b_t = b_low.T
        scores = jnp.where(causal, mm(c_low, b_low, NT), 0.0)
        st_ref[sub] = state[...].astype(bf16)
        across_state[...] = mm(c_low, st_ref[sub])
        for p in range(pairs):
            cols = slice(p * LANES, (p + 1) * LANES)
            x = convolved(sub, p)
            l1, l2 = spread(decay[:, 2 * p : 2 * p + 1]), spread(decay[:, 2 * p + 1 : 2 * p + 2])
            both = jnp.where(low_half, l1, l2)
            dtb = jnp.where(
                low_half, spread(dt[:, 2 * p : 2 * p + 1]), spread(dt[:, 2 * p + 1 : 2 * p + 2])
            )
            u = x * dtb
            m1 = scores * jnp.exp2(jnp.minimum(l1 - decay_t[2 * p : 2 * p + 1, :], 0.0))
            m2 = scores * jnp.exp2(jnp.minimum(l2 - decay_t[2 * p + 1 : 2 * p + 2, :], 0.0))
            mixing = jnp.concatenate([m1.astype(bf16), m2.astype(bf16)], axis=1)
            u_low = u.astype(bf16)
            zero = jnp.zeros_like(u_low)
            parts = jnp.concatenate(
                [jnp.where(low_half, u_low, zero), jnp.where(low_half, zero, u_low)], axis=0
            )
            last = both[T - 1 : T, :]
            y = mm(mixing, parts) + jnp.exp2(both) * across_state[:, cols] + chan_ref[1:2, cols] * x
            tails[:, cols] = (u * jnp.exp2(last - both)).astype(bf16)
            state[:, cols] = jnp.exp2(last) * state[:, cols]
            y_all[span(step * ROWS + sub * T, T), cols] = y
        state[...] = state[...] + mm(b_t, tails[...])
        if sub == 0:
            pl.when(step == LEN // ROWS - 1)(late_turn)
    halo[0:8, :] = halo[ROWS : ROWS + 8, :]


def ssd_forward(n, layer_input, out_grad, flat, w_zx, w_bc, w_dt, w_out):
    rows, width = w_out.shape
    tokens = layer_input.shape[0]
    length = 4 * tokens
    wide = width + 2 * NS
    steps = length // ROWS
    tall = 2 * ROWS
    forming = steps + 2 * (length // tall)
    go_from = forming + steps
    gz_from = go_from + D // ROWS
    branching = gz_from + D // ROWS
    subs = ROWS // T
    assert length == LEN
    early = lambda i: jnp.minimum(i, steps - 1)
    formed = lambda i: jnp.clip(i - forming, 0, steps - 1)
    of = lambda start, m: pl.BlockSpec((ROWS, m), lambda i: (jnp.clip(i - start, 0, D // ROWS - 1), 0))
    row = lambda m: pl.BlockSpec((ROWS, m), lambda i: (early(i), 0))
    form = lambda m: pl.BlockSpec((ROWS, m), lambda i: (formed(i), 0))
    whole = lambda a: pl.BlockSpec(a.shape, lambda i: (0,) * a.ndim, pipeline_mode=pl.Buffered(1))
    fixed = lambda m: pl.BlockSpec((8, m), lambda i: (0, 0))
    anywhere = pl.BlockSpec(memory_space=pl.ANY)
    vm, dma = pltpu.VMEM, pltpu.SemaphoreType.DMA
    hops, lead = dma((2, 2, 2, n // 2)), dma((2, 2, n // 2))
    shape = lambda dims, dtype: jax.ShapeDtypeStruct(dims, dtype)
    return pl.pallas_call(
        functools.partial(forward_body, n, rows, tokens, width),
        grid=(branching + length // tall,),
        in_specs=[anywhere, anywhere, *(whole(a) for a in (flat, w_zx, w_bc, w_dt, w_out))],
        out_specs=[
            row(wide), row(wide), row(LANES), pl.BlockSpec((subs, NS, width), lambda i: (early(i), 0, 0)),
            form(width), form(width), pl.BlockSpec((tall, D), lambda i: (jnp.maximum(i - branching, 0), 0)),
            of(gz_from, width), of(go_from, width), pl.BlockSpec((rows, width), lambda i: (0, 0)),
            fixed(width), fixed(D), anywhere, anywhere, anywhere, *(fixed(m) for m in (wide, LANES, width)),
        ],
        out_shape=[
            shape((length, wide), bf16), shape((length, wide), bf16), shape((length, LANES), f32),
            shape((length // T, NS, width), bf16), shape((length, width), bf16), shape((length, width), bf16),
            shape((length, D), bf16), shape((D, width), bf16), shape((D, width), bf16), shape((rows, width), bf16),
            shape((8, width), f32), shape((8, D), f32),
            shape((length, D), bf16), shape((D, wide + LANES), bf16), shape((D, 2 * width), bf16),
            *(shape((8, m), f32) for m in (wide, LANES, width)),
        ],
        scratch_shapes=[
            vm((ROWS + 8, wide), f32), vm((NS, width), f32), vm((length, width), f32), vm((length, width), f32),
            *(vm((length, width), bf16) for _ in range(3)),
            vm((length, D), bf16), vm((length, D), bf16), vm((D, wide + LANES), bf16), vm((D, 2 * width), bf16),
            vm((4, 8, length), f32), vm((8, length), f32), vm((2, HEADS, LANES), f32), vm((3 * T, LANES), bf16),
            vm((T, width), f32), vm((T, width), bf16),
            [vm((EARLY_HOPS, size, width), bf16) for _, size in cut_rows(rows)],
            dma((3,)), lead, lead, lead, dma((11,)), dma((4,)), dma((4,)), dma((1,)), dma((1,)),
            dma((4,)), dma((4,)), lead, hops, hops, dma((4,)), dma((4,)),
            dma((1,)), dma((1,)), dma((4,)), dma((4,)), dma((3,)), dma((3,)),
            dma((2, EARLY_HOPS)), dma((2, EARLY_HOPS)),
        ],
        compiler_params=pltpu.CompilerParams(collective_id=2, has_side_effects=True, vmem_limit_bytes=ROOM),
        name="layer_forward",
    )(layer_input, out_grad, flat, w_zx, w_bc, w_dt, w_out)


def backward_body(
    n, own_rows, tokens, width,
    dy_ref, v_ref, xc_ref, dr_ref, st_ref, gate_ref, taps_ref, head_ref, chan_ref, carry_ref, gz_ref, go_ref, branch_ref,
    d_ref, small_ref, oearly_ref, obranch_ref,
    dxh, dstate, yst, bds, dyeb, utb, products, turn, acc, hacc, pick_ref, pick_t, fades, head_t, until_ref, reach_ref,
    own, slots, near, held, over_slot,
    load_sem, ring_send, ring_recv, near_send, near_recv, over_send, over_recv,
):
    pairs = width // LANES
    wide = width + 2 * NS
    step = pl.program_id(0)
    steps = LEN // ROWS
    pos, ring, me, across, beside = neighbours(n)
    opposite = lax.rem(me + 2, 4)
    next_door = me + 1 - 2 * lax.rem(me, 2)
    far = lax.rem(next_door + 2, 4)
    half = tokens // 2
    cuts = cut_rows(own_rows)

    def block_at(way, count):
        return ring_index(lax.rem(pos + (count if way else n - count), n), n)

    def hop(k, way, h):
        first, size = cuts[way]
        done = k * EARLY_HOPS
        if h > done:
            src = slots[way][k].at[h - 1 - done]
        elif k == 0:
            src = gz_ref.at[span(block_at(way, 1) * own_rows + first, size)]
        else:
            src = carry_ref.at[pl.ds(first, size)]
        return remote(
            src, slots[way][k].at[h - done], ring_send.at[way, k, h], ring_recv.at[way, k, h], ring[way]
        )

    def near_copy(turned, part):
        start = (next_door if turned else far) * tokens + part * half
        return remote(
            branch_ref.at[span(start, half)], near.at[turned, part],
            near_send.at[turned, part], near_recv.at[turned, part], beside,
        )

    def held_copy(turned, part):
        start = (me if turned else opposite) * tokens + part * half
        return pltpu.make_async_copy(
            branch_ref.at[span(start, half)], held.at[turned, part], load_sem.at[2 * turned + part]
        )

    def over_copy(part):
        return remote(held.at[0, part], over_slot.at[part], over_send.at[part], over_recv.at[part], across)

    def own_copies():
        return [
            pltpu.make_async_copy(src, own.at[:, pl.ds(k * width, width)], load_sem.at[4 + k])
            for k, src in enumerate((gz_ref, go_ref))
        ]

    def ring_turn(k, h):
        for way in (0, 1):
            first, size = cuts[way]
            hop(k, way, h).wait_recv()
            block = block_at(way, 2 + h) if h < n - 2 else block_at(way, 0)

            tile = strip(size)

            def some(i, _, way=way, first=first, block=block, tile=tile):
                cols = slice(k * width, (k + 1) * width)
                came = slots[way][k][h - k * EARLY_HOPS, span(i * tile, tile), :]
                mine = own[span(block * own_rows + first + i * tile, tile), cols]
                if h < n - 2:
                    slots[way][k][h - k * EARLY_HOPS, span(i * tile, tile), :] = came + mine
                else:
                    oearly_ref[span(first + i * tile, tile), cols] = came.astype(f32) + mine.astype(f32)
                return 0

            lax.fori_loop(0, size // tile, some, 0)
            if h < n - 2:
                hop(k, way, h + 1).start()

    def ring_poll(k):
        for h in range(k * EARLY_HOPS, n - 1):
            at = (1, 3, 4, 6)[min(h - EARLY_HOPS, 3)] if k else min(h + 1, steps - 1)
            pl.when(step == at)(functools.partial(ring_turn, k, h))

    def add_near(turned):
        for part in (0, 1):
            held_copy(turned, part).wait()
            near_copy(turned, part).wait_recv()

            def some(i, _, part=part):
                at = span(i * 32, 32)
                held[turned, part, at, :] = held[turned, part, at, :] + near[turned, part, at, :]
                return 0

            lax.fori_loop(0, half // 32, some, 0)
            if not turned:
                over_copy(part).start()

    @pl.when(step == 0)
    def _():
        enter((*ring, across, beside))
        for way in (0, 1):
            hop(0, way, 0).start()
        for turned in (0, 1):
            for part in (0, 1):
                near_copy(turned, part).start()
                held_copy(turned, part).start()
        for copy in own_copies():
            copy.start()
        dxh[T : T + 8, :] = jnp.zeros((8, wide), f32)
        dstate[...] = jnp.zeros_like(dstate)
        acc[...] = jnp.zeros_like(acc)
        hacc[...] = jnp.zeros_like(hacc)
        turn[...] = jnp.zeros_like(turn)
        pick_ref[...] = picked(width)
        channel = lax.broadcasted_iota(jnp.int32, (HEADS, width), 1)
        head = lax.broadcasted_iota(jnp.int32, (HEADS, width), 0)
        mine = (channel >= head * P_SIZE) & (channel < (head + 1) * P_SIZE)
        pick_t[...] = jnp.where(mine, 1.0, 0.0).astype(bf16)
        set_heads(head_ref, head_t, until_ref)
        from_here = jnp.where(block_iota(0) >= block_iota(1), 1.0, 0.0).astype(bf16)
        after = jnp.where(block_iota(0) < block_iota(1), 1.0, 0.0).astype(bf16)
        for k, matrix in enumerate((from_here, from_here, after, after)):
            reach_ref[k * T : (k + 1) * T, :] = matrix
        products[3 * T :, :] = jnp.zeros((HEADS, width), bf16)

    @pl.when(step == 1)
    def _():
        for copy in own_copies():
            copy.wait()
        add_near(0)

    pl.when(step == 2)(functools.partial(add_near, 1))
    ring_poll(0)

    low_half = block_iota(1) < P_SIZE
    row_at, col_at = block_iota(0), block_iota(1)
    until = row_at <= col_at
    pair_lane = lax.broadcasted_iota(jnp.int32, (8, 2 * T), 1)
    pair_row = lax.broadcasted_iota(jnp.int32, (8, 2 * T), 0)
    each = jnp.where(lax.div(pair_lane, T) == pair_row, 1.0, 0.0).astype(bf16)
    ones = jnp.ones((8, T), bf16)

    def add(index, cols, value):
        acc[index, :, cols] += jnp.sum(value.reshape(T // 8, 8, LANES), axis=0)

    def conv_back(rows, block, d_act, xc, s, act):
        cols = slice(block * LANES, (block + 1) * LANES)
        dxh[0:T, cols] = d_act * (s + act * (1.0 - s))
        v = v_ref[rows, cols].astype(f32)
        total = None
        for m in range(CONV):
            moved = dxh[m : m + T, cols]
            if m == 0:
                add(CONV, cols, moved)
            add(CONV - 1 - m, cols, v * moved)
            term = taps_ref[CONV - 1 - m : CONV - m, cols] * moved
            total = term if total is None else total + term
        d_ref[rows, cols] = total.astype(bf16)

    for sub in reversed(range(ROWS // T)):
        rows = slice(sub * T, (sub + 1) * T)
        raw_t, dt_t, decay_t, dt, decay = head_rows(dr_ref, head_t, until_ref, rows)
        b_cols = slice(width, width + NS)
        c_cols = slice(width + NS, width + 2 * NS)
        b_xc, c_xc = xc_ref[rows, b_cols].astype(f32), xc_ref[rows, c_cols].astype(f32)
        b_s, c_s = sigmoid(b_xc), sigmoid(c_xc)
        b_act, c_act = b_xc * b_s, c_xc * c_s
        b_low, c_low = b_act.astype(bf16), c_act.astype(bf16)
        c_t = c_low.T
        scores_t = jnp.where(until, mm(b_low, c_low, NT), 0.0)
        ds_low = dstate[...].astype(bf16)
        yst[...] = mm(c_low, st_ref[sub])
        bds[...] = mm(b_low, ds_low)
        d_scores = jnp.zeros((T, LANES), f32)
        for p in range(pairs):
            cols = slice(p * LANES, (p + 1) * LANES)
            dy_low = dy_ref[rows, cols]
            dy = dy_low.astype(f32)
            xc = xc_ref[rows, cols].astype(f32)
            xs = sigmoid(xc)
            x = xc * xs
            l1, l2 = spread(decay[:, 2 * p : 2 * p + 1]), spread(decay[:, 2 * p + 1 : 2 * p + 2])
            both = jnp.where(low_half, l1, l2)
            dtb = jnp.where(
                low_half, spread(dt[:, 2 * p : 2 * p + 1]), spread(dt[:, 2 * p + 1 : 2 * p + 2])
            )
            u = x * dtb
            last = both[T - 1 : T, :]
            e1 = jnp.exp2(jnp.minimum(decay_t[2 * p : 2 * p + 1, :] - l1, 0.0))
            e2 = jnp.exp2(jnp.minimum(decay_t[2 * p + 1 : 2 * p + 2, :] - l2, 0.0))
            zero = jnp.zeros_like(dy_low)
            dy_parts = jnp.concatenate(
                [jnp.where(low_half, dy_low, zero), jnp.where(low_half, zero, dy_low)], axis=0
            )
            du_in = mm(
                jnp.concatenate([(scores_t * e1).astype(bf16), (scores_t * e2).astype(bf16)], axis=1), dy_parts
            )
            d_mix = mm(u.astype(bf16), dy_parts, NT)
            d1, d2 = d_mix[:, :T] * e1, d_mix[:, T:] * e2
            d_scores = d_scores + d1 + d2
            held_pairs = jnp.concatenate([(d1 * scores_t).astype(bf16), (d2 * scores_t).astype(bf16)], axis=1)
            reached_by = mm(ones, held_pairs)
            leaving = mm(each, held_pairs, NT)
            turn[2 * p : 2 * p + 1, :] = reached_by[0:1, :T] - leaving[0:1]
            turn[2 * p + 1 : 2 * p + 2, :] = reached_by[0:1, T:] - leaving[1:2]
            tail = jnp.exp2(last - both)
            fades[0:1, cols] = jnp.exp2(last)
            dye = dy * jnp.exp2(both)
            du_out = tail * bds[:, cols]
            du = du_in + du_out
            products[0:T, cols] = (dye * yst[:, cols]).astype(bf16)
            products[T : 2 * T, cols] = (u * du_out).astype(bf16)
            products[2 * T : 3 * T, cols] = (x * du).astype(bf16)
            dyeb[:, cols] = dye.astype(bf16)
            utb[:, cols] = (u * tail).astype(bf16)
            add(CONV + 1, cols, dy * x)
            conv_back(rows, p, dtb * du + chan_ref[1:2, cols] * dy, xc, xs, x)
        d_scores = jnp.where(until, d_scores, 0.0).astype(bf16)
        d_b = mm(d_scores, c_low) + mm(utb[...], ds_low, NT)
        d_c = mm(d_scores, b_low, TN) + mm(dyeb[...], st_ref[sub], NT)
        conv_back(rows, pairs, d_b, b_xc, b_s, b_act)
        conv_back(rows, pairs + 1, d_c, c_xc, c_s, c_act)
        fade = fades[0:1, :]
        before_ds = dstate[...]
        through = jnp.sum(before_ds * st_ref[sub].astype(f32), axis=0, keepdims=True) * fade
        products[3 * T : 3 * T + HEADS, :] = jnp.broadcast_to(through, (HEADS, width)).astype(bf16)
        dstate[...] = fade * before_ds + mm(c_t, dyeb[...])
        by_head = mm(pick_t[...], products[...], NT)
        inside = pieces(turn[...] + by_head[:, :T], 2)
        outside = pieces(by_head[:, T : 2 * T], 2)
        reached = mm(jnp.concatenate([inside, outside], axis=1), reach_ref[...])
        reached = reached + jnp.broadcast_to(by_head[:, 3 * T : 3 * T + 1], (HEADS, T))
        d_raw = (head_t[1] * reached + by_head[:, 2 * T : 3 * T]) * sigmoid(raw_t)
        d_ref[rows, wide:] = columns_of(d_raw).astype(bf16)
        hacc[0] += d_raw
        hacc[1] += dt_t * reached
        dxh[T : T + 8, :] = dxh[0:8, :]
        if sub == 1:
            @pl.when(step == 0)
            def _():
                for way in (0, 1):
                    hop(1, way, EARLY_HOPS).start()

            ring_poll(1)

    @pl.when(step == steps - 1)
    def _():
        total = lambda a: jnp.sum(a, axis=0, keepdims=True)
        for k in range(CONV + 1):
            small_ref[k : k + 1, :] = total(acc[k])
        small_ref[CONV + 1 : CONV + 2, :width] = total(gate_ref[...])
        small_ref[CONV + 1 : CONV + 2, width : width + LANES] = total(columns_of(hacc[0]))
        small_ref[CONV + 1 : CONV + 2, width + LANES :] = total(columns_of(hacc[1])) * head_ref[1:2, :]
        small_ref[CONV + 2 :, :] = jnp.zeros((2, wide), f32)
        skip = mm_exact(acc[CONV + 1, :, :width], pick_ref[...].astype(f32))
        small_ref[CONV + 3 : CONV + 4, 512 : 512 + LANES] = total(skip)
        for part in (0, 1):
            over_copy(part).wait_recv()

            def some(i, _, part=part):
                at = span(part * half + i * 32, 32)
                here = span(i * 32, 32)
                total = held[1, part, here, :].astype(f32) + over_slot[part, here, :].astype(f32)
                obranch_ref[at, :] = total.astype(bf16)
                return 0

            lax.fori_loop(0, half // 32, some, 0)
        for part in (0, 1):
            over_copy(part).wait_send()
            for turned in (0, 1):
                near_copy(turned, part).wait_send()
        for k in (0, 1):
            for h in range(k * EARLY_HOPS, n - 1):
                for way in (0, 1):
                    hop(k, way, h).wait_send()


def ssd_backward(n, dy, v, xc, dr, st, gate, taps, head, chan, carry, gz, go, branch):
    length, width = dy.shape
    wide = width + 2 * NS
    steps = length // ROWS
    subs = ROWS // T
    own_rows, tokens = D // n, length // 4
    half = tokens // 2
    row = lambda m: pl.BlockSpec((ROWS, m), lambda i: (steps - 1 - i, 0))
    whole = lambda a: pl.BlockSpec(a.shape, lambda i: (0,) * a.ndim, pipeline_mode=pl.Buffered(1))
    fixed = lambda *shape: pl.BlockSpec(shape, lambda i: (0,) * len(shape))
    anywhere = pl.BlockSpec(memory_space=pl.ANY)
    vm, dma = pltpu.VMEM, pltpu.SemaphoreType.DMA
    return pl.pallas_call(
        functools.partial(backward_body, n, own_rows, tokens, width),
        grid=(steps,),
        in_specs=[
            row(width), row(wide), row(wide), row(LANES),
            pl.BlockSpec((subs, NS, width), lambda i: (steps - 1 - i, 0, 0)),
            whole(gate), whole(taps), whole(head), whole(chan), whole(carry), anywhere, anywhere, anywhere,
        ],
        out_specs=[
            row(wide + LANES), fixed(8, wide), fixed(own_rows, 2 * width), fixed(tokens, D),
        ],
        out_shape=[
            jax.ShapeDtypeStruct((length, wide + LANES), bf16),
            jax.ShapeDtypeStruct((8, wide), f32),
            jax.ShapeDtypeStruct((own_rows, 2 * width), f32),
            jax.ShapeDtypeStruct((tokens, D), bf16),
        ],
        scratch_shapes=[
            vm((T + 8, wide), f32), vm((NS, width), f32), vm((T, width), f32), vm((T, width), f32),
            vm((T, width), bf16), vm((T, width), bf16), vm((3 * T + HEADS, width), bf16),
            vm((HEADS, T), f32), vm((CONV + 2, 8, wide), f32), vm((2, HEADS, T), f32),
            vm((width, LANES), bf16), vm((HEADS, width), bf16), vm((8, width), f32), vm((2, HEADS, LANES), f32),
            vm((3 * T, LANES), bf16), vm((4 * T, LANES), bf16),
            vm((D, 2 * width), bf16),
            [[vm((n - 1 - k * EARLY_HOPS, size, width), bf16) for k in (0, 1)] for _, size in cut_rows(own_rows)],
            vm((2, 2, half, D), bf16), vm((2, 2, half, D), bf16), vm((2, half, D), bf16),
            dma((6,)), dma((2, 2, n - 1)), dma((2, 2, n - 1)), dma((2, 2)), dma((2, 2)), dma((2,)), dma((2,)),
        ],
        compiler_params=pltpu.CompilerParams(
            collective_id=3, has_side_effects=True, vmem_limit_bytes=ROOM
        ),
        name="layer_backward",
    )(dy, v, xc, dr, st, gate, taps, head, chan, carry, gz, go, branch)


def reduce_body(
    n, rows, tokens, starts,
    xg_ref, d_ref, dz_ref, wp_ref, w_ref, small_ref, flat_ref, gain_ref,
    oxs_ref, oback_ref, bc_ref, oflat_ref,
    xg, d, dz, wz, w, work, grads, slots, staged, near, over, smalls, tens, bc_slot,
    load_sem, ring_send, ring_recv, near_send, near_recv, over_send, over_recv,
    small_send, small_recv, ten_send, ten_recv, bc_send, bc_recv,
):
    pos, ring, me, across, beside = neighbours(n)
    cuts = cut_rows(rows)
    core = lax.rem(me, 2)
    opposite = lax.rem(me + 2, 4)
    next_door = me + 1 - 2 * core
    far = lax.rem(next_door + 2, 4)
    half = tokens // 2
    late = d.shape[1]
    width = dz.shape[1]
    tile = 2 * LANES
    tiles = D // tile
    columns = [pl.ds(lo, hi - lo) for lo, hi in starts]
    sources = [(d_ref.at[:, columns[0]], d.at[:, columns[0]])]
    sources += [(xg_ref.at[:, pl.ds(i * tile, tile)], xg.at[:, pl.ds(i * tile, tile)]) for i in range(tiles)]
    sources += [(d_ref.at[:, some], d.at[:, some]) for some in columns[1:]]
    sources += [
        (dz_ref, dz), (w_ref, w), (wp_ref.at[:, pl.ds(width, width)], wz), (small_ref, smalls.at[pos]),
    ]
    loads = [pltpu.make_async_copy(src, dst, load_sem.at[k]) for k, (src, dst) in enumerate(sources)]
    for load in loads:
        load.start()
    enter((*ring, across, beside))
    started = []

    def go(*args):
        copy = remote(*args)
        copy.start()
        started.append(copy)

    def block_at(way, count):
        return ring_index(lax.rem(pos + (count if way else n - count), n), n)

    def hop(k, way, h):
        lo, hi = starts[k]
        first, size = cuts[way]
        if h == 0:
            src = grads.at[span(block_at(way, 1) * rows + first, size), pl.ds(lo, hi - lo)]
        else:
            src = slots[way][k].at[h - 1]
        return remote(
            src, slots[way][k].at[h], ring_send.at[way, k, h], ring_recv.at[way, k, h], ring[way]
        )

    def product(k):
        lo, hi = starts[k]

        def some(i, _):
            at = pl.ds(pl.multiple_of(i * tile, tile), tile)
            if k == 0:
                pltpu.make_async_copy(xg_ref.at[:, at], xg.at[:, at], load_sem.at[1 + i]).wait()
            grads[at, lo:hi] = mm(xg[:, at], d[:, lo:hi], TN).astype(bf16)
            return 0

        loads[0 if k == 0 else tiles + k].wait()
        lax.fori_loop(0, tiles, some, 0)
        for way in (0, 1):
            hop(k, way, 0).start()

    def near_copy(turned, part):
        return remote(
            staged.at[turned, part], near.at[turned, part],
            near_send.at[turned, part], near_recv.at[turned, part], beside,
        )

    def over_copy(part):
        return remote(near.at[0, part], over.at[part], over_send.at[part], over_recv.at[part], across)

    def ring_turn(k, h):
        lo, hi = starts[k]
        for way in (0, 1):
            first, size = cuts[way]
            slot = slots[way][k].at[h]
            remote(slot, slot, ring_send.at[way, k, h], ring_recv.at[way, k, h], ring[way]).wait_recv()
            block = block_at(way, 2 + h) if h < n - 2 else block_at(way, 0)

            tile = strip(size)

            def some(i, _, way=way, first=first, block=block, tile=tile):
                came = slots[way][k][h, span(i * tile, tile), :]
                mine = grads[span(block * rows + first + i * tile, tile), lo:hi]
                if h < n - 2:
                    slots[way][k][h, span(i * tile, tile), :] = came + mine
                else:
                    oxs_ref[span(first + i * tile, tile), lo:hi] = came.astype(f32) + mine.astype(f32)
                return 0

            lax.fori_loop(0, size // tile, some, 0)
            if h < n - 2:
                hop(k, way, h + 1).start()

    def small_hop(way, h):
        here = smalls.at[lax.rem(pos + (h if way else n - h), n)]
        go(here, here, small_send.at[way, h], small_recv.at[way, h], ring[way])

    def small_lands(way, h):
        here = smalls.at[lax.rem(pos + (h + 1 if way else n - h - 1), n)]
        remote(here, here, small_send.at[way, h], small_recv.at[way, h], ring[way]).wait_recv()

    for k in range(len(starts)):
        product(k)
    for load in loads[tiles + len(starts) :]:
        load.wait()
    turns = {0: [(0, 0)], 1: [(1, 0), (2, 0)], 2: [(0, 1)], 3: [(1, 1), (2, 1)], 4: [(0, 2)], 5: [(1, 2), (2, 2)], 6: [(0, 3)], 7: [(1, 3), (2, 3)]}
    taken = [sum(k == group for some in turns.values() for k, _ in some) for group in range(len(starts))]

    def block(i, _):
        which, part = lax.div(i, 2), lax.rem(i, 2)
        own = lax.rem(which, 2)
        turned = lax.div(which, 2)
        target = lax.rem(next_door + own * (me - next_door) + 2 * (1 - turned), 4)
        at = span(target * tokens + part * half, half)
        total = mm(dz[at, :], wz[...], NT) + mm(d[at, :], w[...], NT)
        work[...] = total

        @pl.when(own == 0)
        def _():
            staged[turned, part] = work[...].astype(bf16)
            near_copy(turned, part).start()

        @pl.when(own == 1)
        def _():
            near_copy(turned, part).wait_recv()

        @pl.when(which == 1)
        def _():
            near[0, part] = (work[...] + near[0, part].astype(f32)).astype(bf16)
            over_copy(part).start()

        @pl.when(which == 3)
        def _():
            near[1, part] = (work[...] + near[1, part].astype(f32)).astype(bf16)

        for at_block, some in turns.items():

            @pl.when(i == at_block)
            def _(some=some):
                for k, h in some:
                    ring_turn(k, h)

        return 0

    lax.fori_loop(0, 8, block, 0)
    for i in range(tiles):
        share = jnp.zeros((tile, LANES), f32)
        for c in range(late // LANES):
            cols = slice(c * LANES, (c + 1) * LANES)
            at = slice(i * tile, (i + 1) * tile)
            share = share + grads[at, cols].astype(f32) * w[at, cols].astype(f32)
        total = mm_exact(jnp.ones((8, LANES), f32), share, NT)[0:1] + gain_ref[0:1, i * tile : (i + 1) * tile]
        for c in range(2 * i, 2 * i + 2):
            row, col = 6 + c // 8, (c % 8) * LANES
            part = total[:, (c - 2 * i) * LANES : (c - 2 * i + 1) * LANES]
            smalls[pos, row : row + 1, col : col + LANES] = part / flat_ref[c : c + 1, :]

    rest = [(k, h) for h in range(n - 1) for k in (0, 1, 2) if h >= taken[k]]
    rest.sort(key=lambda turn: turn[1] - taken[turn[0]])

    def small_step(s):
        for way in (0, 1):
            if s > 0 and (way == 0 or s < n // 2):
                small_lands(way, s - 1)
            if s < n // 2 - way:
                small_hop(way, s)

    small_step(0)
    steps_done = 1
    for at, (k, h) in enumerate(rest):
        ring_turn(k, h)
        if (k, h) == (0, n - 2):
            bc_slot[0] = oxs_ref[:, starts[0][0] : starts[0][0] + 2 * NS]
            go(bc_slot.at[0], bc_slot.at[1], bc_send.at[0], bc_recv.at[0], beside)
        if at % 2 == 1 and steps_done < n // 2:
            small_step(steps_done)
            steps_done += 1
    for s in range(steps_done, n // 2):
        small_step(s)
    small_lands(0, n // 2 - 1)

    total = smalls[0]
    for i in range(1, n):
        total = total + smalls[i]
    tens[me] = total
    go(tens.at[me], tens.at[me], ten_send.at[0], ten_recv.at[0], beside)
    remote(bc_slot.at[1], bc_slot.at[1], bc_send.at[0], bc_recv.at[0], beside).wait_recv()
    bc_slot[2] = bc_slot[0] + bc_slot[1]
    go(bc_slot.at[2], bc_slot.at[3], bc_send.at[1], bc_recv.at[1], across)
    here = tens.at[next_door]
    remote(here, here, ten_send.at[0], ten_recv.at[0], beside).wait_recv()
    for k, target in ((0, me), (1, next_door)):
        here = tens.at[target]
        go(here, here, ten_send.at[1 + k], ten_recv.at[1 + k], across)
    for part in (0, 1):
        over_copy(part).wait_recv()

        def some(i, _, part=part):
            at = span(part * half + i * 32, 32)
            here = span(i * 32, 32)
            oback_ref[at, :] = (near[1, part, here, :].astype(f32) + over[part, here, :].astype(f32)).astype(bf16)
            return 0

        lax.fori_loop(0, half // 32, some, 0)
    for k, target in ((0, opposite), (1, far)):
        here = tens.at[target]
        remote(here, here, ten_send.at[1 + k], ten_recv.at[1 + k], across).wait_recv()
    flat_gradients(width, tens, oflat_ref)
    remote(bc_slot.at[3], bc_slot.at[3], bc_send.at[1], bc_recv.at[1], across).wait_recv()
    bc_ref[...] = bc_slot[2] + bc_slot[3]
    for part in (0, 1):
        over_copy(part).wait_send()
        for turned in (0, 1):
            near_copy(turned, part).wait_send()
    for k in range(len(starts)):
        for way in (0, 1):
            for h in range(n - 1):
                hop(k, way, h).wait_send()
    for copy in started:
        copy.wait_send()


def flat_gradients(width, tens, out_ref):
    pairs = width // LANES
    heads = width // P_SIZE

    def sums(row, col):
        total = tens[0, row : row + 1, col : col + LANES]
        for t in range(1, 4):
            total = total + tens[t, row : row + 1, col : col + LANES]
        return total

    def put(row, value):
        out_ref[row : row + 1, :] = value

    for c in range(D // LANES):
        put(c, sums(6 + c // 8, (c % 8) * LANES))
    for t in range(4):
        for c in range(pairs):
            cols = slice(c * LANES, (c + 1) * LANES)
            put(GATE_ROW + pairs * t + c, tens[t, CONV + 1 : CONV + 2, cols])
            put(BIAS_ROW + pairs * t + c, tens[t, CONV : CONV + 1, cols])
            for k in range(CONV):
                put(TAPS_ROW + 4 * pairs * k + pairs * t + c, tens[t, k : k + 1, cols])
    for c in range(2):
        put(BIAS_BC_ROW + c, sums(CONV, width + c * LANES))
        for k in range(CONV):
            put(TAPS_BC_ROW + 2 * k + c, sums(k, width + c * LANES))
    kinds = ((CONV + 1, width), (CONV + 1, width + LANES), (CONV + 3, 512))
    rows = [tens[t, row : row + 1, col : col + LANES] for row, col in kinds for t in range(4)]
    rows = jnp.concatenate(rows + [jnp.zeros((16 - len(rows), LANES), f32)], axis=0)
    lane = lax.broadcasted_iota(jnp.int32, (LANES, 2 * LANES), 1)
    entry = lax.broadcasted_iota(jnp.int32, (LANES, 2 * LANES), 0)
    spread_out = mm_exact(rows, jnp.where(lax.rem(lane, heads) == entry, 1.0, 0.0).astype(f32))
    at = lax.broadcasted_iota(jnp.int32, (16, 2 * LANES), 1)
    source = lax.broadcasted_iota(jnp.int32, (16, 2 * LANES), 0)
    line = jnp.sum(jnp.where(lax.div(at, heads) == source, spread_out, 0.0), axis=0, keepdims=True)
    put(HEAD_ROW, line[:, :LANES])
    put(HEAD_ROW + 1, line[:, LANES:])


def reduce_all(n, xg, d, dz, wp, w, small, flat, gain):
    rows, tokens = D // n, dz.shape[0] // 4
    width, late = dz.shape[1], d.shape[1]
    starts = ((width, late), (0, width // 2), (width // 2, width))
    half = tokens // 2
    dma, vm = pltpu.SemaphoreType.DMA, pltpu.VMEM
    anywhere = pl.BlockSpec(memory_space=pl.ANY)
    inside = pl.BlockSpec(memory_space=pltpu.VMEM)
    return pl.pallas_call(
        functools.partial(reduce_body, n, rows, tokens, starts),
        in_specs=[anywhere] * 6 + [inside] * 2,
        out_specs=[inside] * 4,
        out_shape=[
            jax.ShapeDtypeStruct((rows, late), f32),
            jax.ShapeDtypeStruct((tokens, D), bf16),
            jax.ShapeDtypeStruct((rows, 2 * NS), f32),
            jax.ShapeDtypeStruct((FLAT_ROWS, LANES), f32),
        ],
        scratch_shapes=[
            vm(xg.shape, bf16), vm(d.shape, bf16), vm(dz.shape, bf16), vm((D, width), bf16),
            vm((D, late), bf16),
            vm((half, D), f32), vm((D, late), bf16),
            [[vm((n - 1, size, hi - lo), bf16) for lo, hi in starts] for _, size in cut_rows(rows)],
            vm((2, 2, half, D), bf16), vm((2, 2, half, D), bf16), vm((2, half, D), bf16),
            vm((n, *small.shape), f32), vm((4, *small.shape), f32), vm((4, rows, 2 * NS), f32),
            dma((13,)), dma((2, 3, n - 1)), dma((2, 3, n - 1)), dma((2, 2)), dma((2, 2)), dma((2,)), dma((2,)),
            dma((2, n // 2)), dma((2, n // 2)), dma((3,)), dma((3,)), dma((2,)), dma((2,)),
        ],
        compiler_params=pltpu.CompilerParams(
            collective_id=1, has_side_effects=True, vmem_limit_bytes=ROOM
        ),
        name="reduce_all",
    )(xg, d, dz, wp, w, small, flat, gain)


def adamw_step(weight, first, second, grad, rate, decay):
    first_new = beta_first * first + (1.0 - beta_first) * grad
    second_new = beta_second * second + (1.0 - beta_second) * grad * grad
    hat_first = first_new * (1.0 / (1.0 - beta_first**STEP))
    hat_second = second_new * (1.0 / (1.0 - beta_second**STEP))
    weight_new = weight - rate * (hat_first / (jnp.sqrt(hat_second) + adam_eps) + decay * weight)
    return (weight_new, first_new, second_new)


def finish_body(
    width, heads,
    in_ref, cot_ref, branch_ref, back_ref, flat_ref, early_ref, late_ref, bcg_ref,
    zx_ref, zx1_ref, zx2_ref, bc_ref, bc1_ref, bc2_ref, out_ref, out1_ref, out2_ref, late_all_ref, dt_ref, dt1_ref, dt2_ref,
    layer_ref, grad_ref, zxn_ref, zx1n_ref, zx2n_ref, bcn_ref, bc1n_ref, bc2n_ref,
    outn_ref, out1n_ref, out2n_ref, dtn_ref, dt1n_ref, dt2n_ref,
):
    def update(refs, news, grad):
        fresh = adamw_step(*(ref[...] for ref in refs), grad, matrix_rate, matrix_decay)
        for ref, value in zip(news, fresh):
            ref[...] = value

    for k, grad in ((0, early_ref), (1, late_ref)):
        fresh = adamw_step(
            *(ref[:, k, :] for ref in (zx_ref, zx1_ref, zx2_ref)), grad[:, :width], matrix_rate, matrix_decay
        )
        for ref, value in zip((zxn_ref, zx1n_ref, zx2n_ref), fresh):
            ref[:, k, :] = value
    update((bc_ref, bc1_ref, bc2_ref), (bcn_ref, bc1n_ref, bc2n_ref), bcg_ref[...])
    update((out_ref, out1_ref, out2_ref), (outn_ref, out1n_ref, out2n_ref), early_ref[:, width:])

    @pl.when(pl.program_id(0) == 0)
    def _():
        unit = jnp.where(
            lax.broadcasted_iota(jnp.int32, (16, LANES), 0) == lax.broadcasted_iota(jnp.int32, (16, LANES), 1), 1.0, 0.0
        ).astype(f32)
        turned = mm_exact(unit, late_all_ref[:, width + 2 * NS :], NT)
        update((dt_ref, dt1_ref, dt2_ref), (dtn_ref, dt1n_ref, dt2n_ref), turned[:heads])

    rows = in_ref.shape[0]
    tile = 64

    def some(i, _):
        at = span(i * tile, tile)
        squares = jnp.zeros((tile, LANES), f32)
        inner = jnp.zeros((tile, LANES), f32)
        for c in range(D // LANES):
            cols = slice(c * LANES, (c + 1) * LANES)
            x = in_ref[at, cols].astype(f32)
            squares = squares + x * x
            inner = inner + x * flat_ref[c : c + 1, :] * back_ref[at, cols].astype(f32)
        r = lax.rsqrt(jnp.sum(squares, axis=-1, keepdims=True) / D + norm_eps)
        k = r * r * r * jnp.sum(inner, axis=-1, keepdims=True) / D
        r, k = jnp.broadcast_to(r, (tile, LANES)), jnp.broadcast_to(k, (tile, LANES))
        for c in range(D // LANES):
            cols = slice(c * LANES, (c + 1) * LANES)
            x = in_ref[at, cols].astype(f32)
            layer_ref[at, cols] = (x + branch_ref[at, cols].astype(f32)).astype(bf16)
            back = back_ref[at, cols].astype(f32)
            grad_ref[at, cols] = cot_ref[at, cols].astype(f32) + r * flat_ref[c : c + 1, :] * back - x * k
        return 0

    lax.fori_loop(0, rows // tile, some, 0)


def finish(layer_input, out_grad, branch, back, flat, early, late, bcg, zx, bc, out, dt):
    (rows, width), heads = out[0].shape, dt[0].shape[0]
    steps = 4 if rows % 32 == 0 else 2
    part = lambda a: pl.BlockSpec((a.shape[0] // steps, *a.shape[1:]), lambda i: (i,) + (0,) * (a.ndim - 1))
    whole = lambda a: pl.BlockSpec(a.shape, lambda i: (0,) * a.ndim)
    like = lambda a, dtype=f32: jax.ShapeDtypeStruct(a.shape, dtype)
    weights = (*zx, *bc, *out)
    return pl.pallas_call(
        functools.partial(finish_body, width, heads),
        grid=(steps,),
        in_specs=[
            *(part(a) for a in (layer_input, out_grad, branch, back)), whole(flat),
            *(part(a) for a in (early, late, bcg, *weights)), whole(late), *(whole(a) for a in dt),
        ],
        out_specs=[part(layer_input), part(back), *(part(a) for a in weights), *(whole(a) for a in dt)],
        out_shape=[like(layer_input, bf16), like(layer_input), *(like(a) for a in weights), *(like(a) for a in dt)],
        compiler_params=pltpu.CompilerParams(vmem_limit_bytes=ROOM),
        name="finish",
    )(layer_input, out_grad, branch, back, flat, early, late, bcg, *weights, late, *dt)


def local(
    layer_input,
    out_grad,
    small_params,
    small_first,
    small_second,
    w_zx,
    zx_first,
    zx_second,
    w_bc,
    bc_first,
    bc_second,
    w_dt,
    dt_first,
    dt_second,
    w_out,
    out_first,
    out_second,
):
    n = lax.axis_size("dp")
    flat = jnp.pad(small_params, (0, FLAT_ROWS * LANES - small_params.shape[0])).reshape(FLAT_ROWS, LANES)
    v, xc, dr, st, dy, dz, branch, gz, go, carry, gate, gain, xg, w_all, pair_all, taps, head, chan = ssd_forward(
        n, layer_input, out_grad, flat, w_zx, w_bc, w_dt.T, w_out
    )
    d_late, small, owner_early, own_branch = ssd_backward(
        n, dy, v, xc, dr, st, gate, taps, head, chan, carry, gz, go, branch
    )
    owner_late, d_normed_in, owner_bc, flat_grad = reduce_all(
        n, xg, d_late, dz, pair_all, w_all, small, flat, gain
    )
    small_grad = flat_grad.reshape(-1)[: small_params.shape[0]]
    small_new, small_first_new, small_second_new = adamw_step(
        small_params, small_first, small_second, small_grad, small_rate, 0.0
    )
    (
        layer_output, input_grad, zx_new, zx_first_new, zx_second_new, bc_new, bc_first_new, bc_second_new,
        out_new, out_first_new, out_second_new, dt_new, dt_first_new, dt_second_new,
    ) = finish(
        layer_input, out_grad, own_branch, d_normed_in, flat, owner_early, owner_late, owner_bc,
        (w_zx, zx_first, zx_second), (w_bc, bc_first, bc_second), (w_out, out_first, out_second),
        (w_dt.T, dt_first.T, dt_second.T),
    )
    dt_new, dt_first_new, dt_second_new = dt_new.T, dt_first_new.T, dt_second_new.T
    return (
        layer_output,
        input_grad,
        small_new,
        small_first_new,
        small_second_new,
        zx_new,
        zx_first_new,
        zx_second_new,
        bc_new,
        bc_first_new,
        bc_second_new,
        dt_new,
        dt_first_new,
        dt_second_new,
        out_new,
        out_first_new,
        out_second_new,
    )


def solution(mesh):
    return jax.shard_map(
        local,
        mesh=mesh,
        in_specs=(
            P(("dp", "tensor"), None),
            P(("dp", "tensor"), None),
            P(),
            P(),
            P(),
            P("dp", None, "tensor"),
            P("dp", None, "tensor"),
            P("dp", None, "tensor"),
            P("dp", None),
            P("dp", None),
            P("dp", None),
            P("dp", "tensor"),
            P("dp", "tensor"),
            P("dp", "tensor"),
            P("dp", "tensor"),
            P("dp", "tensor"),
            P("dp", "tensor"),
        ),
        out_specs=(
            P(("dp", "tensor"), None),
            P(("dp", "tensor"), None),
            P(),
            P(),
            P(),
            P("dp", None, "tensor"),
            P("dp", None, "tensor"),
            P("dp", None, "tensor"),
            P("dp", None),
            P("dp", None),
            P("dp", None),
            P("dp", "tensor"),
            P("dp", "tensor"),
            P("dp", "tensor"),
            P("dp", "tensor"),
            P("dp", "tensor"),
            P("dp", "tensor"),
        ),
        check_vma=False,
    )
```

```python
import functools

import jax
import jax.numpy as jnp
from jax import lax
from jax.experimental import pallas as pl
from jax.experimental.pallas import tpu as pltpu
from jax.sharding import PartitionSpec as P

D = 1536
DI = 3072
H = 48
NS = 128
P_SIZE = 64
CONV = 4
LEN = 2048
STEP = 10

T = 128
ROWS = 256
LANES = 128
ROOM = 60 * 2**20
EARLY_HOPS = 1

norm_eps = 1e-05
adam_eps = 1e-08
beta_first = 0.9
beta_second = 0.95
matrix_rate = 0.01
small_rate = 0.1
matrix_decay = 0.1

f32 = jnp.float32
bf16 = jnp.bfloat16
NN = (((1,), (0,)), ((), ()))
NT = (((1,), (1,)), ((), ()))
TN = (((0,), (0,)), ((), ()))
HIGHEST = lax.Precision.HIGHEST


GATE_ROW, TAPS_ROW, BIAS_ROW, TAPS_BC_ROW, BIAS_BC_ROW, HEAD_ROW, FLAT_ROWS = 12, 36, 132, 156, 164, 166, 168


def mm(a, b, dims=NN):
    return lax.dot_general(a, b, dims, preferred_element_type=f32)


def mm_exact(a, b, dims=NN):
    return lax.dot_general(a, b, dims, preferred_element_type=f32, precision=HIGHEST)


def sigmoid(v):
    return 0.5 * jnp.tanh(0.5 * v) + 0.5


def softplus(v):
    return jnp.maximum(v, 0.0) + jnp.log1p(jnp.exp(-jnp.abs(v)))


def spread(col):
    return jnp.broadcast_to(col, (T, LANES))


def block_iota(axis):
    return lax.broadcasted_iota(jnp.int32, (T, LANES), axis)


HEADS = 16
LOG2_E = 1.4426950408889634


def pieces(value, count):
    parts = []
    for k in range(count):
        part = value.astype(bf16)
        parts.append(part)
        if k < count - 1:
            value = value - part.astype(f32)
    return jnp.concatenate(parts, axis=1)


def columns_of(rows):
    return jnp.concatenate([rows, jnp.zeros((LANES - HEADS, T), f32)], axis=0).T


def set_heads(head_ref, head_t, until):
    turned = jnp.concatenate([head_ref[...], jnp.zeros((LANES - 8, LANES), f32)], axis=0).T
    head_t[0] = spread(turned[:, 0:1])[:HEADS]
    head_t[1] = spread(turned[:, 1:2])[:HEADS]
    matrix = jnp.where(block_iota(0) <= block_iota(1), 1.0, 0.0).astype(bf16)
    for k in range(3):
        until[k * T : (k + 1) * T, :] = matrix


def head_rows(dr_ref, head_t, until, rows):
    raw = dr_ref[rows, :].T[:HEADS] + head_t[0]
    dt = softplus(raw)
    decay = mm(pieces(dt * (head_t[1] * LOG2_E), 3), until[...])
    return raw, dt, decay, columns_of(dt), columns_of(decay)


def ring_place(n):
    me = lax.axis_index("dp")
    z, x = lax.div(me, 2), lax.rem(me, 2)
    return z + x * (n - 1 - 2 * z)


def ring_index(pos, n):
    back = lax.div(pos, n // 2)
    return 2 * pos + back * (2 * n - 1 - 4 * pos)


def neighbours(n):
    pos = ring_place(n)
    right = ring_index(lax.rem(pos + 1, n), n)
    left = ring_index(lax.rem(pos + n - 1, n), n)
    me = lax.axis_index("tensor")
    y, core = lax.div(me, 2), lax.rem(me, 2)
    across = 2 * (1 - y) + core
    beside = 2 * y + 1 - core
    return pos, ({"dp": right}, {"dp": left}), me, {"tensor": across}, {"tensor": beside}


def greet(peers):
    barrier = pltpu.get_barrier_semaphore()
    for peer in peers:
        pl.semaphore_signal(barrier, inc=1, device_id=peer, device_id_type=pl.DeviceIdType.MESH)


def enter(peers):
    greet(peers)
    pl.semaphore_wait(pltpu.get_barrier_semaphore(), len(peers))


def remote(src, dst, send_sem, recv_sem, peer):
    return pltpu.make_async_remote_copy(
        src_ref=src, dst_ref=dst, send_sem=send_sem, recv_sem=recv_sem,
        device_id=peer, device_id_type=pl.DeviceIdType.MESH,
    )


def span(start, size):
    return pl.ds(pl.multiple_of(start, 16), size)


def strip(rows):
    return next(size for size in (48, 32, 16) if rows % size == 0)


def cut_rows(rows):
    top = rows // 32 * 16
    return ((0, top), (top, rows - top))


def forward_body(
    n, rows, tokens, width,
    in_ref, cot_ref, flat_ref, wzx_ref, wbc_ref, wdt_ref, wout_ref,
    v_ref, xc_ref, dr_ref, st_ref, dy_ref, dz_ref, branch_ref, gz_ref, go_ref, carry_ref, gate_ref, gain_ref,
    xg_ref, ws_ref, wps_ref, taps_ref, head_ref, chan_ref,
    halo, state, y_all, z_all, dn_all, nl_all, dz_all, xg, cots, ws, wps, sums, red, head_t, until, across_state, tails, fresh, hold, first_slots,
    own_keep, lead_keep, lead_send, lead_recv, x_keep, x_over_send, x_over_recv, x_side_send, x_side_recv,
    x_pass_send, x_pass_recv, ring_keep, ring_send, ring_recv, over_send, over_recv,
    side_send, side_recv, pass_send, pass_recv, sum_send, sum_recv, first_send, first_recv,
):
    pairs = width // LANES
    wide = width + 2 * NS
    step = pl.program_id(0)
    steps = LEN // ROWS
    tall = 2 * ROWS
    norming = steps
    gating = norming + LEN // tall
    forming = gating + LEN // tall
    go_from = forming + steps
    gz_from = go_from + D // ROWS
    last_step = gz_from + D // ROWS - 1
    pos, ring, me, across, beside = neighbours(n)
    opposite = lax.rem(me + 2, 4)
    next_door = me + 1 - 2 * lax.rem(me, 2)
    far = lax.rem(next_door + 2, 4)
    askew = {"tensor": far}
    quarter = tokens // 4
    hops = n // 2
    cuts = cut_rows(rows)
    mine = ring_index(pos, n)

    late = wide + LANES
    parts_of = ((0, width), (width, width))

    def hop(k, part, way, h):
        first, size = cuts[part]
        cols = pl.ds(*parts_of[k])
        block = ring_index(lax.rem(pos + (h if way else n - h), n), n)
        here = wps.at[span(block * rows + first, size), cols]
        return remote(here, here, ring_send.at[way, part, k, h], ring_recv.at[way, part, k, h], ring[way])

    def hop_lands(k, part, way, h):
        first, size = cuts[part]
        block = ring_index(lax.rem(pos + (h + 1 if way else n - h - 1), n), n)
        return span(block * rows + first, size), pl.ds(*parts_of[k])

    def hop_arrival(k, part, way, h):
        here = wps.at[hop_lands(k, part, way, h)]
        return remote(here, here, ring_send.at[way, part, k, h], ring_recv.at[way, part, k, h], ring[way])

    def hop_keep(part, way, h):
        at = hop_lands(1, part, way, h)
        return pltpu.make_async_copy(wps.at[at], wps_ref.at[at], ring_keep.at[way, part, h])

    def hop_ways(h):
        return [(part, way) for part in (0, 1) for way in (0, 1) if h < hops - 1 or part == way]

    def hop_on(k, h):
        for part, way in hop_ways(h - 1) if h > 0 else ():
            hop_arrival(k, part, way, h - 1).wait_recv()
            if k == 1:
                hop_keep(part, way, h - 1).start()
            if h < hops and (part, way) in hop_ways(h):
                hop(k, part, way, h).start()
        if h == 0:
            for part, way in hop_ways(0):
                hop(k, part, way, 0).start()

    def over(k):
        return remote(
            cot_ref.at[pl.ds(k * quarter, quarter)], cots.at[span(me * tokens + k * quarter, quarter)],
            over_send.at[k], over_recv.at[k], across,
        )

    def landed(start, size, send, recv, peer):
        here = cots.at[span(start, size)]
        return remote(here, here, send, recv, peer)

    def over_arrival(k):
        return landed(opposite * tokens + k * quarter, quarter, over_send.at[k], over_recv.at[k], across)

    def passing(k):
        return landed(opposite * tokens + k * quarter, quarter, pass_send.at[k], pass_recv.at[k], beside)

    def pass_arrival(k):
        return landed(far * tokens + k * quarter, quarter, pass_send.at[k], pass_recv.at[k], beside)

    def side():
        return remote(cot_ref, cots.at[span(me * tokens, tokens)], side_send.at[0], side_recv.at[0], beside)

    def side_arrival():
        return landed(next_door * tokens, tokens, side_send.at[0], side_recv.at[0], beside)

    def own_cot():
        return pltpu.make_async_copy(cot_ref, cots.at[span(me * tokens, tokens)], own_keep.at[0])

    def own_z():
        at = span(mine * rows, rows), pl.ds(*parts_of[1])
        return pltpu.make_async_copy(wps.at[at], wps_ref.at[at], own_keep.at[1])

    def pass_on(*pieces):
        for k in pieces:
            over_arrival(k).wait_recv()
            passing(k).start()

    def normalize(k):
        def some(i, _):
            at = span(me * tokens + k * quarter + i * 64, 64)
            squares = jnp.zeros((64, LANES), f32)
            for c in range(D // LANES):
                x = xg[at, c * LANES : (c + 1) * LANES].astype(f32)
                squares = squares + x * x
            inverse = lax.rsqrt(jnp.sum(squares, axis=-1, keepdims=True) / D + norm_eps)
            inverse = jnp.broadcast_to(inverse, (64, LANES))
            for c in range(D // LANES):
                cols = slice(c * LANES, (c + 1) * LANES)
                xg[at, cols] = (xg[at, cols].astype(f32) * inverse * flat_ref[c : c + 1, :]).astype(bf16)
            return 0

        lax.fori_loop(0, quarter // 64, some, 0)

    @pl.when(step == 0)
    def _():
        own_rows = span(me * tokens, tokens)
        greet((*ring, across, beside, askew))
        load = pltpu.make_async_copy(in_ref, xg.at[own_rows], own_keep.at[2])
        load.start()
        own_cot().start()
        mine_at = span(mine * rows, rows)
        ws[mine_at, :width] = wzx_ref[:, 1, :].astype(bf16)
        ws[mine_at, width:wide] = wbc_ref[...].astype(bf16)
        heads = wdt_ref.shape[0]
        unit = jnp.where(
            lax.broadcasted_iota(jnp.int32, (16, LANES), 0) == lax.broadcasted_iota(jnp.int32, (16, LANES), 1), 1.0, 0.0
        ).astype(bf16)
        steps_w = jnp.concatenate([wdt_ref[...], jnp.zeros((16 - heads, rows), f32)], axis=0).astype(bf16)
        ws[mine_at, wide:] = mm(steps_w, unit, TN).astype(bf16)
        load.wait()
        normalize(0)
        pl.semaphore_wait(pltpu.get_barrier_semaphore(), 5)
        started, kept = [], []

        def go(*args):
            copy = remote(*args)
            copy.start()
            started.append(copy)

        def keep(src, dst, sem):
            copy = pltpu.make_async_copy(src, dst, sem)
            copy.start()
            kept.append(copy)

        def arrived(part, way, h, block):
            first, size = cuts[part]
            at = span(block * rows + first, size)
            remote(
                ws.at[at], ws.at[at], lead_send.at[way, part, h], lead_recv.at[way, part, h], ring[way]
            ).wait_recv()
            keep(ws.at[at], ws_ref.at[at], lead_keep.at[way, part, h])

        def lead(h, parts=(0, 1)):
            for part in parts:
                first, size = cuts[part]
                for way in (0, 1):
                    block = ring_index(lax.rem(pos + (h if way else n - h), n), n)
                    here = ws.at[span(block * rows + first, size)]
                    if h > 0:
                        arrived(part, way, h - 1, block)
                    if h == hops - 1 and part != way:
                        continue
                    go(here, here, lead_send.at[way, part, h], lead_recv.at[way, part, h], ring[way])

        def x_over(k):
            at = span(me * tokens + k * quarter, quarter)
            go(xg.at[at], xg.at[at], x_over_send.at[k], x_over_recv.at[k], across)

        def x_pass(k):
            at = span(opposite * tokens + k * quarter, quarter)
            here = xg.at[at]
            remote(here, here, x_over_send.at[k], x_over_recv.at[k], across).wait_recv()
            go(here, here, x_pass_send.at[k], x_pass_recv.at[k], beside)
            keep(here, xg_ref.at[at], x_keep.at[k])

        def x_pass_lands(k):
            at = span(far * tokens + k * quarter, quarter)
            remote(xg.at[at], xg.at[at], x_pass_send.at[k], x_pass_recv.at[k], beside).wait_recv()
            keep(xg.at[at], xg_ref.at[at], x_keep.at[4 + k])

        lead(0, (0,))
        leading = list(started)
        x_over(0)
        for k in (1, 2, 3):
            normalize(k)
            if k == 1:
                x_over(1)
        go(xg.at[own_rows], xg.at[own_rows], x_side_send.at[0], x_side_recv.at[0], beside)
        keep(xg.at[own_rows], xg_ref.at[own_rows], x_keep.at[8])
        wps[mine_at, :width] = wout_ref[...].astype(bf16)
        wps[mine_at, width:] = wzx_ref[:, 0, :].astype(bf16)
        for copy in leading:
            copy.wait_send()
            started.remove(copy)
        lead(0, (1,))
        keep(ws.at[mine_at], ws_ref.at[mine_at], x_keep.at[9])
        own_z().start()
        halo[0:8, :] = jnp.zeros((8, wide), f32)
        state[...] = jnp.zeros_like(state)
        gate_ref[...] = jnp.zeros_like(gate_ref)
        parameter_rows(me, width, flat_ref, taps_ref, head_ref, chan_ref)
        set_heads(head_ref, head_t, until)
        lead(1)
        x_over(2)
        at = span(next_door * tokens, tokens)
        remote(xg.at[at], xg.at[at], x_side_send.at[0], x_side_recv.at[0], beside).wait_recv()
        keep(xg.at[at], xg_ref.at[at], x_keep.at[10])
        side().start()
        lead(2)
        x_over(3)
        x_pass(0)
        x_pass(1)
        for h in range(3, hops):
            lead(h)
        hop_on(0, 0)
        x_pass(2)
        over(0).start()
        x_pass_lands(0)
        x_pass_lands(1)
        x_pass(3)
        for part in (0, 1):
            arrived(part, part, hops - 1, ring_index(lax.rem(pos + n // 2, n), n))
        hop_on(1, 0)
        over(1).start()
        x_pass_lands(2)
        x_pass_lands(3)
        for copy in kept:
            copy.wait()
        for copy in started:
            copy.wait_send()

    for k, times in enumerate(((1, 4, 6), (2, 5, 7))):
        for h in range(1, hops):
            at = times[h - 1] if h <= len(times) else norming
            pl.when(step == at)(functools.partial(hop_on, k, h))
    pl.when(step == norming)(functools.partial(hop_on, 0, hops))
    pl.when(step == gating)(functools.partial(hop_on, 1, hops))

    @pl.when(step == 2)
    def _():
        over(2).start()

    @pl.when(step == 4)
    def _():
        over(3).start()
        pass_on(0, 1)

    pl.when(step == steps - 1)(functools.partial(pass_on, 2))

    @pl.when(step < norming)
    def _():
        scan_step(
            width, step, xg, ws, taps_ref, head_ref, chan_ref,
            v_ref, xc_ref, dr_ref, st_ref, halo, state, y_all, head_t, until, across_state, tails,
            functools.partial(pass_on, 3),
        )

    @pl.when(step == norming)
    def _():
        side_arrival().wait_recv()
        for k in range(4):
            pass_arrival(k).wait_recv()
        own_cot().wait()
        own_z().wait()

    @pl.when((step >= norming) & (step < gating))
    def _():
        at = span((step - norming) * tall, tall)
        dn_all[at, :] = mm(cots[at, :], wps[:, :width]).astype(bf16)

    @pl.when((step >= gating) & (step < forming))
    def _():
        first = (step - gating) * tall
        at = span(first, tall)
        z_all[at, :] = mm(xg[at, :], wps[:, width:])
        ones = jnp.ones((8, LANES), f32)
        for sub in range(tall // T):
            rows_at = span(first + sub * T, T)
            squares = jnp.zeros((T, LANES), f32)
            inner = jnp.zeros((T, LANES), f32)
            for p in range(pairs):
                cols = slice(p * LANES, (p + 1) * LANES)
                z = z_all[rows_at, cols]
                gated = y_all[rows_at, cols] * (z * sigmoid(z))
                squares = squares + gated * gated
                inner = inner + gated * chan_ref[0:1, cols] * dn_all[rows_at, cols].astype(f32)
            lanes = pl.ds(pl.multiple_of(first + sub * T, T), T)
            sums[me, 0:4, lanes] = mm_exact(ones, squares, NT)[0:4]
            sums[me, 4:8, lanes] = mm_exact(ones, inner, NT)[4:8]

    @pl.when(step == forming - 1)
    def _():
        peers = ((beside, next_door), (across, opposite), (askew, far))
        for k, (peer, _) in enumerate(peers):
            remote(sums.at[me], sums.at[me], sum_send.at[k], sum_recv.at[k], peer).start()
        for h in range(hops):
            for part, way in hop_ways(h):
                for k in (0, 1):
                    hop(k, part, way, h).wait_send()
                hop_keep(part, way, h).wait()
        side().wait_send()
        for k in range(4):
            over(k).wait_send()
            passing(k).wait_send()
        for k, (peer, other) in enumerate(peers):
            remote(sums.at[other], sums.at[other], sum_send.at[k], sum_recv.at[k], peer).wait()
        red[...] = ((sums[0] + sums[1]) + sums[2]) + sums[3]

    slab = D // pairs

    def multiply(p):
        at = slice(p * slab, (p + 1) * slab)
        branch_ref[:, at] = mm(hold[...], wps[at, :width], NT).astype(bf16)

    @pl.when(step == forming)
    def _():
        hold[...] = jnp.zeros_like(hold)

    @pl.when((step >= forming) & (step < go_from))
    def _():
        first = (step - forming) * ROWS
        lanes = pl.ds(pl.multiple_of(first, ROWS), ROWS)
        q_row = lax.rsqrt(red[0:4, lanes] / DI + norm_eps)
        k_row = q_row * q_row * q_row * red[4:8, lanes] / DI
        turned = jnp.concatenate([q_row, k_row], axis=0).T
        for p in range(pairs):
            cols = slice(p * LANES, (p + 1) * LANES)
            gain = chan_ref[0:1, cols]
            multiply(p)
            for sub in range(ROWS // T):
                rows_at = slice(sub * T, (sub + 1) * T)
                at = span(first + sub * T, T)
                q, kk = spread(turned[rows_at, 0:1]), spread(turned[rows_at, 4:5])
                z, y, dn = z_all[at, cols], y_all[at, cols], dn_all[at, cols].astype(f32)
                s = sigmoid(z)
                sz = z * s
                gated = y * sz
                gq = gated * q
                dg = q * gain * dn - gated * kk
                gate_ref[:, cols] += jnp.sum((gq * dn).reshape(T // 8, 8, LANES), axis=0)
                fresh[rows_at, cols] = (gq * gain).astype(bf16)
                dz_ref[rows_at, cols] = (dg * y * (s + sz * (1.0 - s))).astype(bf16)
                dy_ref[rows_at, cols] = (dg * sz).astype(bf16)
        at = span(first, ROWS)
        hold[...] = fresh[...]
        nl_all[at, :] = fresh[...]
        dz_all[at, :] = dz_ref[...]

    @pl.when(step == go_from)
    def _():
        for p in range(pairs):
            multiply(p)

    def block_at(way, count):
        return ring_index(lax.rem(pos + (count if way else n - count), n), n)

    def first_hop(way, h):
        first, size = cuts[way]
        src = ws.at[span(block_at(way, 1) * rows + first, size), pl.ds(0, width)] if h == 0 else first_slots[way].at[h - 1]
        return remote(src, first_slots[way].at[h], first_send.at[way, h], first_recv.at[way, h], ring[way])

    def first_turn(h):
        for way in (0, 1):
            first, size = cuts[way]
            first_hop(way, h).wait_recv()
            block = block_at(way, 2 + h)
            tile = strip(size)

            def some(i, _, way=way, first=first, block=block, tile=tile):
                at = span(i * tile, tile)
                total = first_slots[way][h, at, :] + ws[span(block * rows + first + i * tile, tile), :width]
                if h < EARLY_HOPS - 1:
                    first_slots[way][h, at, :] = total
                else:
                    carry_ref[span(first + i * tile, tile), :] = total
                return 0

            lax.fori_loop(0, size // tile, some, 0)
            if h < EARLY_HOPS - 1:
                first_hop(way, h + 1).start()

    @pl.when((step >= go_from) & (step < gz_from))
    def _():
        first = (step - go_from) * ROWS
        lanes = pl.ds(pl.multiple_of(first, ROWS), ROWS)
        grad = mm(cots[:, lanes], nl_all[...], TN).astype(bf16)
        go_ref[...] = grad
        ws[span(first, ROWS), :width] = grad

    @pl.when(step == gz_from)
    def _():
        for way in (0, 1):
            first_hop(way, 0).start()

    @pl.when(step >= gz_from)
    def _():
        first = (step - gz_from) * ROWS
        at = span(first, ROWS)
        lanes = pl.ds(pl.multiple_of(first, ROWS), ROWS)
        grad = mm(xg[:, lanes], dz_all[...], TN)
        gz_ref[...] = grad.astype(bf16)
        share = jnp.zeros((ROWS, LANES), f32)
        for p in range(pairs):
            cols = slice(p * LANES, (p + 1) * LANES)
            w = wps[at, width + p * LANES : width + (p + 1) * LANES]
            share = share + grad[:, cols] * w.astype(f32)
        gain_ref[:, lanes] = mm_exact(jnp.ones((8, LANES), f32), share, NT)

    @pl.when(step == last_step)
    def _():
        first_turn(EARLY_HOPS - 1)
        for way in (0, 1):
            for h in range(EARLY_HOPS):
                first_hop(way, h).wait_send()


def parameter_rows(me, width, flat_ref, taps_ref, head_ref, chan_ref):
    pairs = width // LANES
    heads = width // P_SIZE
    taps_ref[...] = jnp.zeros_like(taps_ref)
    chan_ref[...] = jnp.zeros_like(chan_ref)
    for c in range(pairs):
        cols = slice(c * LANES, (c + 1) * LANES)
        chan_ref[0:1, cols] = flat_ref[pl.ds(GATE_ROW + pairs * me + c, 1), :]
        taps_ref[CONV : CONV + 1, cols] = flat_ref[pl.ds(BIAS_ROW + pairs * me + c, 1), :]
        for k in range(CONV):
            taps_ref[k : k + 1, cols] = flat_ref[pl.ds(TAPS_ROW + 4 * pairs * k + pairs * me + c, 1), :]
    for c in range(2):
        cols = slice(width + c * LANES, width + (c + 1) * LANES)
        taps_ref[CONV : CONV + 1, cols] = flat_ref[BIAS_BC_ROW + c : BIAS_BC_ROW + c + 1, :]
        for k in range(CONV):
            row = TAPS_BC_ROW + 2 * k + c
            taps_ref[k : k + 1, cols] = flat_ref[row : row + 1, :]
    both = jnp.concatenate([flat_ref[HEAD_ROW : HEAD_ROW + 1, :], flat_ref[HEAD_ROW + 1 : HEAD_ROW + 2, :]], axis=1)
    both = jnp.broadcast_to(both, (8, 2 * LANES))
    lane = lax.broadcasted_iota(jnp.int32, (2 * LANES, LANES), 0)
    head = lax.broadcasted_iota(jnp.int32, (2 * LANES, LANES), 1)

    def take(kind):
        match = (lane == 4 * heads * kind + heads * me + head) & (head < heads)
        return mm_exact(both, jnp.where(match, 1.0, 0.0).astype(f32))

    valid = lax.broadcasted_iota(jnp.int32, (8, LANES), 1) < heads
    row = lax.broadcasted_iota(jnp.int32, (8, LANES), 0)
    rates = jnp.where(valid, -jnp.exp(take(1)), 0.0)
    head_ref[...] = jnp.where(row == 0, take(0), jnp.where(row == 1, rates, 0.0))
    skip = mm_exact(take(2), picked(width).astype(f32), NT)
    chan_ref[1:2, :] = skip[0:1]


def picked(width):
    channel = lax.broadcasted_iota(jnp.int32, (width, LANES), 0)
    head = lax.broadcasted_iota(jnp.int32, (width, LANES), 1)
    return jnp.where((channel >= head * P_SIZE) & (channel < (head + 1) * P_SIZE), 1.0, 0.0).astype(bf16)


def scan_step(
    width, step, xg, w_ref, taps_ref, head_ref, chan_ref,
    v_ref, xc_ref, dr_ref, st_ref, halo, state, y_all, head_t, until, across_state, tails, late_turn,
):
    pairs = width // LANES
    wide = width + 2 * NS
    mine = span(step * ROWS, ROWS)
    dr_ref[...] = mm(xg[mine, :], w_ref[:, wide:])
    halo[8 : 8 + ROWS, :] = mm(xg[mine, :], w_ref[:, :wide])
    low_half = block_iota(1) < P_SIZE
    causal = block_iota(0) >= block_iota(1)

    def convolved(sub, block):
        cols = slice(block * LANES, (block + 1) * LANES)
        total = taps_ref[CONV : CONV + 1, cols]
        for k in range(CONV):
            first = 8 - (CONV - 1) + k + sub * T
            total = total + taps_ref[k : k + 1, cols] * halo[first : first + T, cols]
        rows = slice(sub * T, (sub + 1) * T)
        xc_ref[rows, cols] = total.astype(bf16)
        v_ref[rows, cols] = halo[8 + sub * T : 8 + (sub + 1) * T, cols].astype(bf16)
        return total * sigmoid(total)

    for sub in range(ROWS // T):
        rows = slice(sub * T, (sub + 1) * T)
        _, _, decay_t, dt, decay = head_rows(dr_ref, head_t, until, rows)
        b_low = convolved(sub, pairs).astype(bf16)
        c_low = convolved(sub, pairs + 1).astype(bf16)
        b_t = b_low.T
        scores = jnp.where(causal, mm(c_low, b_low, NT), 0.0)
        st_ref[sub] = state[...].astype(bf16)
        across_state[...] = mm(c_low, st_ref[sub])
        for p in range(pairs):
            cols = slice(p * LANES, (p + 1) * LANES)
            x = convolved(sub, p)
            l1, l2 = spread(decay[:, 2 * p : 2 * p + 1]), spread(decay[:, 2 * p + 1 : 2 * p + 2])
            both = jnp.where(low_half, l1, l2)
            dtb = jnp.where(
                low_half, spread(dt[:, 2 * p : 2 * p + 1]), spread(dt[:, 2 * p + 1 : 2 * p + 2])
            )
            u = x * dtb
            m1 = scores * jnp.exp2(jnp.minimum(l1 - decay_t[2 * p : 2 * p + 1, :], 0.0))
            m2 = scores * jnp.exp2(jnp.minimum(l2 - decay_t[2 * p + 1 : 2 * p + 2, :], 0.0))
            mixing = jnp.concatenate([m1.astype(bf16), m2.astype(bf16)], axis=1)
            u_low = u.astype(bf16)
            zero = jnp.zeros_like(u_low)
            parts = jnp.concatenate(
                [jnp.where(low_half, u_low, zero), jnp.where(low_half, zero, u_low)], axis=0
            )
            last = both[T - 1 : T, :]
            y = mm(mixing, parts) + jnp.exp2(both) * across_state[:, cols] + chan_ref[1:2, cols] * x
            tails[:, cols] = (u * jnp.exp2(last - both)).astype(bf16)
            state[:, cols] = jnp.exp2(last) * state[:, cols]
            y_all[span(step * ROWS + sub * T, T), cols] = y
        state[...] = state[...] + mm(b_t, tails[...])
        if sub == 0:
            pl.when(step == LEN // ROWS - 1)(late_turn)
    halo[0:8, :] = halo[ROWS : ROWS + 8, :]


def ssd_forward(n, layer_input, out_grad, flat, w_zx, w_bc, w_dt, w_out):
    rows, width = w_out.shape
    tokens = layer_input.shape[0]
    length = 4 * tokens
    wide = width + 2 * NS
    steps = length // ROWS
    tall = 2 * ROWS
    forming = steps + 2 * (length // tall)
    go_from = forming + steps
    gz_from = go_from + D // ROWS
    subs = ROWS // T
    assert length == LEN
    early = lambda i: jnp.minimum(i, steps - 1)
    formed = lambda i: jnp.clip(i - forming, 0, steps - 1)
    of = lambda start, m: pl.BlockSpec((ROWS, m), lambda i: (jnp.clip(i - start, 0, D // ROWS - 1), 0))
    row = lambda m: pl.BlockSpec((ROWS, m), lambda i: (early(i), 0))
    form = lambda m: pl.BlockSpec((ROWS, m), lambda i: (formed(i), 0))
    whole = lambda a: pl.BlockSpec(a.shape, lambda i: (0,) * a.ndim, pipeline_mode=pl.Buffered(1))
    fixed = lambda m: pl.BlockSpec((8, m), lambda i: (0, 0))
    anywhere = pl.BlockSpec(memory_space=pl.ANY)
    vm, dma = pltpu.VMEM, pltpu.SemaphoreType.DMA
    hops, lead = dma((2, 2, 2, n // 2)), dma((2, 2, n // 2))
    shape = lambda dims, dtype: jax.ShapeDtypeStruct(dims, dtype)
    return pl.pallas_call(
        functools.partial(forward_body, n, rows, tokens, width),
        grid=(gz_from + D // ROWS,),
        in_specs=[anywhere, anywhere, *(whole(a) for a in (flat, w_zx, w_bc, w_dt, w_out))],
        out_specs=[
            row(wide), row(wide), row(LANES), pl.BlockSpec((subs, NS, width), lambda i: (early(i), 0, 0)),
            form(width), form(width), pl.BlockSpec((ROWS, D), lambda i: (jnp.clip(i - forming - 1, 0, steps - 1), 0)),
            of(gz_from, width), of(go_from, width), pl.BlockSpec((rows, width), lambda i: (0, 0)),
            fixed(width), fixed(D), anywhere, anywhere, anywhere, *(fixed(m) for m in (wide, LANES, width)),
        ],
        out_shape=[
            shape((length, wide), bf16), shape((length, wide), bf16), shape((length, LANES), f32),
            shape((length // T, NS, width), bf16), shape((length, width), bf16), shape((length, width), bf16),
            shape((length, D), bf16), shape((D, width), bf16), shape((D, width), bf16), shape((rows, width), bf16),
            shape((8, width), f32), shape((8, D), f32),
            shape((length, D), bf16), shape((D, wide + LANES), bf16), shape((D, 2 * width), bf16),
            *(shape((8, m), f32) for m in (wide, LANES, width)),
        ],
        scratch_shapes=[
            vm((ROWS + 8, wide), f32), vm((NS, width), f32), vm((length, width), f32), vm((length, width), f32),
            *(vm((length, width), bf16) for _ in range(3)),
            vm((length, D), bf16), vm((length, D), bf16), vm((D, wide + LANES), bf16), vm((D, 2 * width), bf16),
            vm((4, 8, length), f32), vm((8, length), f32), vm((2, HEADS, LANES), f32), vm((3 * T, LANES), bf16),
            vm((T, width), f32), vm((T, width), bf16),
            vm((ROWS, width), bf16), vm((ROWS, width), bf16),
            [vm((EARLY_HOPS, size, width), bf16) for _, size in cut_rows(rows)],
            dma((3,)), lead, lead, lead, dma((11,)), dma((4,)), dma((4,)), dma((1,)), dma((1,)),
            dma((4,)), dma((4,)), lead, hops, hops, dma((4,)), dma((4,)),
            dma((1,)), dma((1,)), dma((4,)), dma((4,)), dma((3,)), dma((3,)),
            dma((2, EARLY_HOPS)), dma((2, EARLY_HOPS)),
        ],
        compiler_params=pltpu.CompilerParams(collective_id=2, has_side_effects=True, vmem_limit_bytes=ROOM),
        name="layer_forward",
    )(layer_input, out_grad, flat, w_zx, w_bc, w_dt, w_out)


def backward_body(
    n, own_rows, tokens, width,
    dy_ref, v_ref, xc_ref, dr_ref, st_ref, gate_ref, taps_ref, head_ref, chan_ref, carry_ref, gz_ref, go_ref, branch_ref,
    d_ref, small_ref, oearly_ref, obranch_ref,
    dxh, dstate, yst, bds, dyeb, utb, products, turn, acc, hacc, pick_ref, pick_t, fades, head_t, until_ref, reach_ref,
    own, slots, near, held, over_slot,
    load_sem, ring_send, ring_recv, near_send, near_recv, over_send, over_recv,
):
    pairs = width // LANES
    wide = width + 2 * NS
    step = pl.program_id(0)
    steps = LEN // ROWS
    pos, ring, me, across, beside = neighbours(n)
    opposite = lax.rem(me + 2, 4)
    next_door = me + 1 - 2 * lax.rem(me, 2)
    far = lax.rem(next_door + 2, 4)
    half = tokens // 2
    cuts = cut_rows(own_rows)

    def block_at(way, count):
        return ring_index(lax.rem(pos + (count if way else n - count), n), n)

    def hop(k, way, h):
        first, size = cuts[way]
        done = k * EARLY_HOPS
        if h > done:
            src = slots[way][k].at[h - 1 - done]
        elif k == 0:
            src = gz_ref.at[span(block_at(way, 1) * own_rows + first, size)]
        else:
            src = carry_ref.at[pl.ds(first, size)]
        return remote(
            src, slots[way][k].at[h - done], ring_send.at[way, k, h], ring_recv.at[way, k, h], ring[way]
        )

    def near_copy(turned, part):
        start = (next_door if turned else far) * tokens + part * half
        return remote(
            branch_ref.at[span(start, half)], near.at[turned, part],
            near_send.at[turned, part], near_recv.at[turned, part], beside,
        )

    def held_copy(turned, part):
        start = (me if turned else opposite) * tokens + part * half
        return pltpu.make_async_copy(
            branch_ref.at[span(start, half)], held.at[turned, part], load_sem.at[2 * turned + part]
        )

    def over_copy(part):
        return remote(held.at[0, part], over_slot.at[part], over_send.at[part], over_recv.at[part], across)

    def own_copies():
        return [
            pltpu.make_async_copy(src, own.at[:, pl.ds(k * width, width)], load_sem.at[4 + k])
            for k, src in enumerate((gz_ref, go_ref))
        ]

    def ring_turn(k, h):
        for way in (0, 1):
            first, size = cuts[way]
            hop(k, way, h).wait_recv()
            block = block_at(way, 2 + h) if h < n - 2 else block_at(way, 0)

            tile = strip(size)

            def some(i, _, way=way, first=first, block=block, tile=tile):
                cols = slice(k * width, (k + 1) * width)
                came = slots[way][k][h - k * EARLY_HOPS, span(i * tile, tile), :]
                mine = own[span(block * own_rows + first + i * tile, tile), cols]
                if h < n - 2:
                    slots[way][k][h - k * EARLY_HOPS, span(i * tile, tile), :] = came + mine
                else:
                    oearly_ref[span(first + i * tile, tile), cols] = came.astype(f32) + mine.astype(f32)
                return 0

            lax.fori_loop(0, size // tile, some, 0)
            if h < n - 2:
                hop(k, way, h + 1).start()

    def ring_poll(k):
        for h in range(k * EARLY_HOPS, n - 1):
            at = min(h + 1 - k * EARLY_HOPS, steps - 1)
            pl.when(step == at)(functools.partial(ring_turn, k, h))

    def add_near(turned):
        for part in (0, 1):
            held_copy(turned, part).wait()
            near_copy(turned, part).wait_recv()

            def some(i, _, part=part):
                at = span(i * 32, 32)
                held[turned, part, at, :] = held[turned, part, at, :] + near[turned, part, at, :]
                return 0

            lax.fori_loop(0, half // 32, some, 0)
            if not turned:
                over_copy(part).start()

    @pl.when(step == 0)
    def _():
        enter((*ring, across, beside))
        for way in (0, 1):
            hop(0, way, 0).start()
        for turned in (0, 1):
            for part in (0, 1):
                near_copy(turned, part).start()
                held_copy(turned, part).start()
        for copy in own_copies():
            copy.start()
        dxh[T : T + 8, :] = jnp.zeros((8, wide), f32)
        dstate[...] = jnp.zeros_like(dstate)
        acc[...] = jnp.zeros_like(acc)
        hacc[...] = jnp.zeros_like(hacc)
        turn[...] = jnp.zeros_like(turn)
        pick_ref[...] = picked(width)
        channel = lax.broadcasted_iota(jnp.int32, (HEADS, width), 1)
        head = lax.broadcasted_iota(jnp.int32, (HEADS, width), 0)
        mine = (channel >= head * P_SIZE) & (channel < (head + 1) * P_SIZE)
        pick_t[...] = jnp.where(mine, 1.0, 0.0).astype(bf16)
        set_heads(head_ref, head_t, until_ref)
        from_here = jnp.where(block_iota(0) >= block_iota(1), 1.0, 0.0).astype(bf16)
        after = jnp.where(block_iota(0) < block_iota(1), 1.0, 0.0).astype(bf16)
        for k, matrix in enumerate((from_here, from_here, after, after)):
            reach_ref[k * T : (k + 1) * T, :] = matrix
        products[3 * T :, :] = jnp.zeros((HEADS, width), bf16)

    @pl.when(step == 1)
    def _():
        for copy in own_copies():
            copy.wait()
        add_near(0)

    pl.when(step == 2)(functools.partial(add_near, 1))
    ring_poll(0)

    low_half = block_iota(1) < P_SIZE
    row_at, col_at = block_iota(0), block_iota(1)
    until = row_at <= col_at
    pair_lane = lax.broadcasted_iota(jnp.int32, (8, 2 * T), 1)
    pair_row = lax.broadcasted_iota(jnp.int32, (8, 2 * T), 0)
    each = jnp.where(lax.div(pair_lane, T) == pair_row, 1.0, 0.0).astype(bf16)
    ones = jnp.ones((8, T), bf16)

    def add(index, cols, value):
        acc[index, :, cols] += jnp.sum(value.reshape(T // 8, 8, LANES), axis=0)

    def conv_back(rows, block, d_act, xc, s, act):
        cols = slice(block * LANES, (block + 1) * LANES)
        dxh[0:T, cols] = d_act * (s + act * (1.0 - s))
        v = v_ref[rows, cols].astype(f32)
        total = None
        for m in range(CONV):
            moved = dxh[m : m + T, cols]
            if m == 0:
                add(CONV, cols, moved)
            add(CONV - 1 - m, cols, v * moved)
            term = taps_ref[CONV - 1 - m : CONV - m, cols] * moved
            total = term if total is None else total + term
        d_ref[rows, cols] = total.astype(bf16)

    for sub in reversed(range(ROWS // T)):
        rows = slice(sub * T, (sub + 1) * T)
        raw_t, dt_t, decay_t, dt, decay = head_rows(dr_ref, head_t, until_ref, rows)
        b_cols = slice(width, width + NS)
        c_cols = slice(width + NS, width + 2 * NS)
        b_xc, c_xc = xc_ref[rows, b_cols].astype(f32), xc_ref[rows, c_cols].astype(f32)
        b_s, c_s = sigmoid(b_xc), sigmoid(c_xc)
        b_act, c_act = b_xc * b_s, c_xc * c_s
        b_low, c_low = b_act.astype(bf16), c_act.astype(bf16)
        c_t = c_low.T
        scores_t = jnp.where(until, mm(b_low, c_low, NT), 0.0)
        ds_low = dstate[...].astype(bf16)
        yst[...] = mm(c_low, st_ref[sub])
        bds[...] = mm(b_low, ds_low)
        d_scores = jnp.zeros((T, LANES), f32)
        for p in range(pairs):
            cols = slice(p * LANES, (p + 1) * LANES)
            dy_low = dy_ref[rows, cols]
            dy = dy_low.astype(f32)
            xc = xc_ref[rows, cols].astype(f32)
            xs = sigmoid(xc)
            x = xc * xs
            l1, l2 = spread(decay[:, 2 * p : 2 * p + 1]), spread(decay[:, 2 * p + 1 : 2 * p + 2])
            both = jnp.where(low_half, l1, l2)
            dtb = jnp.where(
                low_half, spread(dt[:, 2 * p : 2 * p + 1]), spread(dt[:, 2 * p + 1 : 2 * p + 2])
            )
            u = x * dtb
            last = both[T - 1 : T, :]
            e1 = jnp.exp2(jnp.minimum(decay_t[2 * p : 2 * p + 1, :] - l1, 0.0))
            e2 = jnp.exp2(jnp.minimum(decay_t[2 * p + 1 : 2 * p + 2, :] - l2, 0.0))
            zero = jnp.zeros_like(dy_low)
            dy_parts = jnp.concatenate(
                [jnp.where(low_half, dy_low, zero), jnp.where(low_half, zero, dy_low)], axis=0
            )
            du_in = mm(
                jnp.concatenate([(scores_t * e1).astype(bf16), (scores_t * e2).astype(bf16)], axis=1), dy_parts
            )
            d_mix = mm(u.astype(bf16), dy_parts, NT)
            d1, d2 = d_mix[:, :T] * e1, d_mix[:, T:] * e2
            d_scores = d_scores + d1 + d2
            held_pairs = jnp.concatenate([(d1 * scores_t).astype(bf16), (d2 * scores_t).astype(bf16)], axis=1)
            reached_by = mm(ones, held_pairs)
            leaving = mm(each, held_pairs, NT)
            turn[2 * p : 2 * p + 1, :] = reached_by[0:1, :T] - leaving[0:1]
            turn[2 * p + 1 : 2 * p + 2, :] = reached_by[0:1, T:] - leaving[1:2]
            tail = jnp.exp2(last - both)
            fades[0:1, cols] = jnp.exp2(last)
            dye = dy * jnp.exp2(both)
            du_out = tail * bds[:, cols]
            du = du_in + du_out
            products[0:T, cols] = (dye * yst[:, cols]).astype(bf16)
            products[T : 2 * T, cols] = (u * du_out).astype(bf16)
            products[2 * T : 3 * T, cols] = (x * du).astype(bf16)
            dyeb[:, cols] = dye.astype(bf16)
            utb[:, cols] = (u * tail).astype(bf16)
            add(CONV + 1, cols, dy * x)
            conv_back(rows, p, dtb * du + chan_ref[1:2, cols] * dy, xc, xs, x)
        d_scores = jnp.where(until, d_scores, 0.0).astype(bf16)
        d_b = mm(d_scores, c_low) + mm(utb[...], ds_low, NT)
        d_c = mm(d_scores, b_low, TN) + mm(dyeb[...], st_ref[sub], NT)
        conv_back(rows, pairs, d_b, b_xc, b_s, b_act)
        conv_back(rows, pairs + 1, d_c, c_xc, c_s, c_act)
        fade = fades[0:1, :]
        before_ds = dstate[...]
        through = jnp.sum(before_ds * st_ref[sub].astype(f32), axis=0, keepdims=True) * fade
        products[3 * T : 3 * T + HEADS, :] = jnp.broadcast_to(through, (HEADS, width)).astype(bf16)
        dstate[...] = fade * before_ds + mm(c_t, dyeb[...])
        by_head = mm(pick_t[...], products[...], NT)
        inside = pieces(turn[...] + by_head[:, :T], 2)
        outside = pieces(by_head[:, T : 2 * T], 2)
        reached = mm(jnp.concatenate([inside, outside], axis=1), reach_ref[...])
        reached = reached + jnp.broadcast_to(by_head[:, 3 * T : 3 * T + 1], (HEADS, T))
        d_raw = (head_t[1] * reached + by_head[:, 2 * T : 3 * T]) * sigmoid(raw_t)
        d_ref[rows, wide:] = columns_of(d_raw).astype(bf16)
        hacc[0] += d_raw
        hacc[1] += dt_t * reached
        dxh[T : T + 8, :] = dxh[0:8, :]
        if sub == 1:
            @pl.when(step == 0)
            def _():
                for way in (0, 1):
                    hop(1, way, EARLY_HOPS).start()

            ring_poll(1)

    @pl.when(step == steps - 1)
    def _():
        total = lambda a: jnp.sum(a, axis=0, keepdims=True)
        for k in range(CONV + 1):
            small_ref[k : k + 1, :] = total(acc[k])
        small_ref[CONV + 1 : CONV + 2, :width] = total(gate_ref[...])
        small_ref[CONV + 1 : CONV + 2, width : width + LANES] = total(columns_of(hacc[0]))
        small_ref[CONV + 1 : CONV + 2, width + LANES :] = total(columns_of(hacc[1])) * head_ref[1:2, :]
        small_ref[CONV + 2 :, :] = jnp.zeros((2, wide), f32)
        skip = mm_exact(acc[CONV + 1, :, :width], pick_ref[...].astype(f32))
        small_ref[CONV + 3 : CONV + 4, 512 : 512 + LANES] = total(skip)
        for part in (0, 1):
            over_copy(part).wait_recv()

            def some(i, _, part=part):
                at = span(part * half + i * 32, 32)
                here = span(i * 32, 32)
                total = held[1, part, here, :].astype(f32) + over_slot[part, here, :].astype(f32)
                obranch_ref[at, :] = total.astype(bf16)
                return 0

            lax.fori_loop(0, half // 32, some, 0)
        for part in (0, 1):
            over_copy(part).wait_send()
            for turned in (0, 1):
                near_copy(turned, part).wait_send()
        for k in (0, 1):
            for h in range(k * EARLY_HOPS, n - 1):
                for way in (0, 1):
                    hop(k, way, h).wait_send()


def ssd_backward(n, dy, v, xc, dr, st, gate, taps, head, chan, carry, gz, go, branch):
    length, width = dy.shape
    wide = width + 2 * NS
    steps = length // ROWS
    subs = ROWS // T
    own_rows, tokens = D // n, length // 4
    half = tokens // 2
    row = lambda m: pl.BlockSpec((ROWS, m), lambda i: (steps - 1 - i, 0))
    whole = lambda a: pl.BlockSpec(a.shape, lambda i: (0,) * a.ndim, pipeline_mode=pl.Buffered(1))
    fixed = lambda *shape: pl.BlockSpec(shape, lambda i: (0,) * len(shape))
    anywhere = pl.BlockSpec(memory_space=pl.ANY)
    vm, dma = pltpu.VMEM, pltpu.SemaphoreType.DMA
    return pl.pallas_call(
        functools.partial(backward_body, n, own_rows, tokens, width),
        grid=(steps,),
        in_specs=[
            row(width), row(wide), row(wide), row(LANES),
            pl.BlockSpec((subs, NS, width), lambda i: (steps - 1 - i, 0, 0)),
            whole(gate), whole(taps), whole(head), whole(chan), whole(carry), anywhere, anywhere, anywhere,
        ],
        out_specs=[
            row(wide + LANES), fixed(8, wide), fixed(own_rows, 2 * width), fixed(tokens, D),
        ],
        out_shape=[
            jax.ShapeDtypeStruct((length, wide + LANES), bf16),
            jax.ShapeDtypeStruct((8, wide), f32),
            jax.ShapeDtypeStruct((own_rows, 2 * width), f32),
            jax.ShapeDtypeStruct((tokens, D), bf16),
        ],
        scratch_shapes=[
            vm((T + 8, wide), f32), vm((NS, width), f32), vm((T, width), f32), vm((T, width), f32),
            vm((T, width), bf16), vm((T, width), bf16), vm((3 * T + HEADS, width), bf16),
            vm((HEADS, T), f32), vm((CONV + 2, 8, wide), f32), vm((2, HEADS, T), f32),
            vm((width, LANES), bf16), vm((HEADS, width), bf16), vm((8, width), f32), vm((2, HEADS, LANES), f32),
            vm((3 * T, LANES), bf16), vm((4 * T, LANES), bf16),
            vm((D, 2 * width), bf16),
            [[vm((n - 1 - k * EARLY_HOPS, size, width), bf16) for k in (0, 1)] for _, size in cut_rows(own_rows)],
            vm((2, 2, half, D), bf16), vm((2, 2, half, D), bf16), vm((2, half, D), bf16),
            dma((6,)), dma((2, 2, n - 1)), dma((2, 2, n - 1)), dma((2, 2)), dma((2, 2)), dma((2,)), dma((2,)),
        ],
        compiler_params=pltpu.CompilerParams(
            collective_id=3, has_side_effects=True, vmem_limit_bytes=ROOM
        ),
        name="layer_backward",
    )(dy, v, xc, dr, st, gate, taps, head, chan, carry, gz, go, branch)


def reduce_body(
    n, rows, tokens, starts,
    xg_ref, d_ref, dz_ref, wp_ref, w_ref, small_ref, flat_ref, gain_ref,
    oxs_ref, oback_ref, bc_ref, oflat_ref,
    xg, d, dz, wz, w, work, grads, slots, staged, near, over, smalls, tens, bc_slot,
    load_sem, ring_send, ring_recv, near_send, near_recv, over_send, over_recv,
    small_send, small_recv, ten_send, ten_recv, bc_send, bc_recv,
):
    pos, ring, me, across, beside = neighbours(n)
    cuts = cut_rows(rows)
    core = lax.rem(me, 2)
    opposite = lax.rem(me + 2, 4)
    next_door = me + 1 - 2 * core
    far = lax.rem(next_door + 2, 4)
    half = tokens // 2
    late = d.shape[1]
    width = dz.shape[1]
    tile = 2 * LANES
    tiles = D // tile
    columns = [pl.ds(lo, hi - lo) for lo, hi in starts]
    sources = [(d_ref.at[:, columns[0]], d.at[:, columns[0]])]
    sources += [(xg_ref.at[:, pl.ds(i * tile, tile)], xg.at[:, pl.ds(i * tile, tile)]) for i in range(tiles)]
    sources += [(d_ref.at[:, some], d.at[:, some]) for some in columns[1:]]
    sources += [
        (dz_ref, dz), (w_ref, w), (wp_ref.at[:, pl.ds(width, width)], wz), (small_ref, smalls.at[pos]),
    ]
    loads = [pltpu.make_async_copy(src, dst, load_sem.at[k]) for k, (src, dst) in enumerate(sources)]
    for load in loads:
        load.start()
    askew = {"tensor": far}
    enter((*ring, across, beside, askew))
    started = []

    def go(*args):
        copy = remote(*args)
        copy.start()
        started.append(copy)

    def block_at(way, count):
        return ring_index(lax.rem(pos + (count if way else n - count), n), n)

    def hop(k, way, h):
        lo, hi = starts[k]
        first, size = cuts[way]
        if h == 0:
            src = grads.at[span(block_at(way, 1) * rows + first, size), pl.ds(lo, hi - lo)]
        else:
            src = slots[way][k].at[h - 1]
        return remote(
            src, slots[way][k].at[h], ring_send.at[way, k, h], ring_recv.at[way, k, h], ring[way]
        )

    def product(k):
        lo, hi = starts[k]

        def some(i, _):
            at = pl.ds(pl.multiple_of(i * tile, tile), tile)
            if k == 0:
                pltpu.make_async_copy(xg_ref.at[:, at], xg.at[:, at], load_sem.at[1 + i]).wait()
            grads[at, lo:hi] = mm(xg[:, at], d[:, lo:hi], TN).astype(bf16)
            return 0

        loads[0 if k == 0 else tiles + k].wait()
        lax.fori_loop(0, tiles, some, 0)
        for way in (0, 1):
            hop(k, way, 0).start()

    def near_copy(turned, part):
        return remote(
            staged.at[turned, part], near.at[turned, part],
            near_send.at[turned, part], near_recv.at[turned, part], beside,
        )

    def over_copy(part):
        return remote(near.at[0, part], over.at[part], over_send.at[part], over_recv.at[part], across)

    def ring_turn(k, h):
        lo, hi = starts[k]
        for way in (0, 1):
            first, size = cuts[way]
            slot = slots[way][k].at[h]
            remote(slot, slot, ring_send.at[way, k, h], ring_recv.at[way, k, h], ring[way]).wait_recv()
            block = block_at(way, 2 + h) if h < n - 2 else block_at(way, 0)

            tile = strip(size)

            def some(i, _, way=way, first=first, block=block, tile=tile):
                came = slots[way][k][h, span(i * tile, tile), :]
                mine = grads[span(block * rows + first + i * tile, tile), lo:hi]
                if h < n - 2:
                    slots[way][k][h, span(i * tile, tile), :] = came + mine
                else:
                    oxs_ref[span(first + i * tile, tile), lo:hi] = came.astype(f32) + mine.astype(f32)
                return 0

            lax.fori_loop(0, size // tile, some, 0)
            if h < n - 2:
                hop(k, way, h + 1).start()

    def small_hop(way, h):
        here = smalls.at[lax.rem(pos + (h if way else n - h), n)]
        go(here, here, small_send.at[way, h], small_recv.at[way, h], ring[way])

    def small_lands(way, h):
        here = smalls.at[lax.rem(pos + (h + 1 if way else n - h - 1), n)]
        remote(here, here, small_send.at[way, h], small_recv.at[way, h], ring[way]).wait_recv()

    for k in range(len(starts)):
        product(k)
    for load in loads[tiles + len(starts) :]:
        load.wait()
    turns = {0: [(0, 0)], 1: [(1, 0), (2, 0)], 2: [(0, 1)], 3: [(1, 1), (2, 1)], 4: [(0, 2)], 5: [(1, 2), (2, 2)], 6: [(0, 3)], 7: [(1, 3), (2, 3)]}
    taken = [sum(k == group for some in turns.values() for k, _ in some) for group in range(len(starts))]

    def block(i, _):
        which, part = lax.div(i, 2), lax.rem(i, 2)
        own = lax.rem(which, 2)
        turned = lax.div(which, 2)
        target = lax.rem(next_door + own * (me - next_door) + 2 * (1 - turned), 4)
        at = span(target * tokens + part * half, half)
        total = mm(dz[at, :], wz[...], NT) + mm(d[at, :], w[...], NT)
        work[...] = total

        @pl.when(own == 0)
        def _():
            staged[turned, part] = work[...].astype(bf16)
            near_copy(turned, part).start()

        @pl.when(own == 1)
        def _():
            near_copy(turned, part).wait_recv()

        @pl.when(which == 1)
        def _():
            near[0, part] = (work[...] + near[0, part].astype(f32)).astype(bf16)
            over_copy(part).start()

        @pl.when(which == 3)
        def _():
            near[1, part] = (work[...] + near[1, part].astype(f32)).astype(bf16)

        for at_block, some in turns.items():

            @pl.when(i == at_block)
            def _(some=some):
                for k, h in some:
                    ring_turn(k, h)

        return 0

    lax.fori_loop(0, 8, block, 0)
    for i in range(tiles):
        share = jnp.zeros((tile, LANES), f32)
        for c in range(late // LANES):
            cols = slice(c * LANES, (c + 1) * LANES)
            at = slice(i * tile, (i + 1) * tile)
            share = share + grads[at, cols].astype(f32) * w[at, cols].astype(f32)
        total = mm_exact(jnp.ones((8, LANES), f32), share, NT)[0:1] + gain_ref[0:1, i * tile : (i + 1) * tile]
        for c in range(2 * i, 2 * i + 2):
            row, col = 6 + c // 8, (c % 8) * LANES
            part = total[:, (c - 2 * i) * LANES : (c - 2 * i + 1) * LANES]
            smalls[pos, row : row + 1, col : col + LANES] = part / flat_ref[c : c + 1, :]

    rest = [(k, h) for h in range(n - 1) for k in (0, 1, 2) if h >= taken[k]]
    rest.sort(key=lambda turn: turn[1] - taken[turn[0]])

    def small_step(s):
        for way in (0, 1):
            if s > 0 and (way == 0 or s < n // 2):
                small_lands(way, s - 1)
            if s < n // 2 - way:
                small_hop(way, s)

    small_step(0)
    steps_done = 1
    for at, (k, h) in enumerate(rest):
        ring_turn(k, h)
        if (k, h) == (0, n - 2):
            bc_slot[0] = oxs_ref[:, starts[0][0] : starts[0][0] + 2 * NS]
            go(bc_slot.at[0], bc_slot.at[1], bc_send.at[0], bc_recv.at[0], beside)
        if at % 2 == 1 and steps_done < n // 2:
            small_step(steps_done)
            steps_done += 1
    for s in range(steps_done, n // 2):
        small_step(s)
    small_lands(0, n // 2 - 1)

    total = smalls[0]
    for i in range(1, n):
        total = total + smalls[i]
    tens[me] = total
    others = ((beside, next_door), (across, opposite), (askew, far))
    for k, (peer, _) in enumerate(others):
        go(tens.at[me], tens.at[me], ten_send.at[k], ten_recv.at[k], peer)
    remote(bc_slot.at[1], bc_slot.at[1], bc_send.at[0], bc_recv.at[0], beside).wait_recv()
    bc_slot[2] = bc_slot[0] + bc_slot[1]
    go(bc_slot.at[2], bc_slot.at[3], bc_send.at[1], bc_recv.at[1], across)
    for part in (0, 1):
        over_copy(part).wait_recv()

        def some(i, _, part=part):
            at = span(part * half + i * 32, 32)
            here = span(i * 32, 32)
            oback_ref[at, :] = (near[1, part, here, :].astype(f32) + over[part, here, :].astype(f32)).astype(bf16)
            return 0

        lax.fori_loop(0, half // 32, some, 0)
    for k, (peer, target) in enumerate(others):
        here = tens.at[target]
        remote(here, here, ten_send.at[k], ten_recv.at[k], peer).wait_recv()
    flat_gradients(width, tens, oflat_ref)
    remote(bc_slot.at[3], bc_slot.at[3], bc_send.at[1], bc_recv.at[1], across).wait_recv()
    bc_ref[...] = bc_slot[2] + bc_slot[3]
    for part in (0, 1):
        over_copy(part).wait_send()
        for turned in (0, 1):
            near_copy(turned, part).wait_send()
    for k in range(len(starts)):
        for way in (0, 1):
            for h in range(n - 1):
                hop(k, way, h).wait_send()
    for copy in started:
        copy.wait_send()


def flat_gradients(width, tens, out_ref):
    pairs = width // LANES
    heads = width // P_SIZE

    def sums(row, col):
        total = tens[0, row : row + 1, col : col + LANES]
        for t in range(1, 4):
            total = total + tens[t, row : row + 1, col : col + LANES]
        return total

    def put(row, value):
        out_ref[row : row + 1, :] = value

    for c in range(D // LANES):
        put(c, sums(6 + c // 8, (c % 8) * LANES))
    for t in range(4):
        for c in range(pairs):
            cols = slice(c * LANES, (c + 1) * LANES)
            put(GATE_ROW + pairs * t + c, tens[t, CONV + 1 : CONV + 2, cols])
            put(BIAS_ROW + pairs * t + c, tens[t, CONV : CONV + 1, cols])
            for k in range(CONV):
                put(TAPS_ROW + 4 * pairs * k + pairs * t + c, tens[t, k : k + 1, cols])
    for c in range(2):
        put(BIAS_BC_ROW + c, sums(CONV, width + c * LANES))
        for k in range(CONV):
            put(TAPS_BC_ROW + 2 * k + c, sums(k, width + c * LANES))
    kinds = ((CONV + 1, width), (CONV + 1, width + LANES), (CONV + 3, 512))
    rows = [tens[t, row : row + 1, col : col + LANES] for row, col in kinds for t in range(4)]
    rows = jnp.concatenate(rows + [jnp.zeros((16 - len(rows), LANES), f32)], axis=0)
    lane = lax.broadcasted_iota(jnp.int32, (LANES, 2 * LANES), 1)
    entry = lax.broadcasted_iota(jnp.int32, (LANES, 2 * LANES), 0)
    spread_out = mm_exact(rows, jnp.where(lax.rem(lane, heads) == entry, 1.0, 0.0).astype(f32))
    at = lax.broadcasted_iota(jnp.int32, (16, 2 * LANES), 1)
    source = lax.broadcasted_iota(jnp.int32, (16, 2 * LANES), 0)
    line = jnp.sum(jnp.where(lax.div(at, heads) == source, spread_out, 0.0), axis=0, keepdims=True)
    put(HEAD_ROW, line[:, :LANES])
    put(HEAD_ROW + 1, line[:, LANES:])


def reduce_all(n, xg, d, dz, wp, w, small, flat, gain):
    rows, tokens = D // n, dz.shape[0] // 4
    width, late = dz.shape[1], d.shape[1]
    starts = ((width, late), (0, width // 2), (width // 2, width))
    half = tokens // 2
    dma, vm = pltpu.SemaphoreType.DMA, pltpu.VMEM
    anywhere = pl.BlockSpec(memory_space=pl.ANY)
    inside = pl.BlockSpec(memory_space=pltpu.VMEM)
    return pl.pallas_call(
        functools.partial(reduce_body, n, rows, tokens, starts),
        in_specs=[anywhere] * 6 + [inside] * 2,
        out_specs=[inside] * 4,
        out_shape=[
            jax.ShapeDtypeStruct((rows, late), f32),
            jax.ShapeDtypeStruct((tokens, D), bf16),
            jax.ShapeDtypeStruct((rows, 2 * NS), f32),
            jax.ShapeDtypeStruct((FLAT_ROWS, LANES), f32),
        ],
        scratch_shapes=[
            vm(xg.shape, bf16), vm(d.shape, bf16), vm(dz.shape, bf16), vm((D, width), bf16),
            vm((D, late), bf16),
            vm((half, D), f32), vm((D, late), bf16),
            [[vm((n - 1, size, hi - lo), bf16) for lo, hi in starts] for _, size in cut_rows(rows)],
            vm((2, 2, half, D), bf16), vm((2, 2, half, D), bf16), vm((2, half, D), bf16),
            vm((n, *small.shape), f32), vm((4, *small.shape), f32), vm((4, rows, 2 * NS), f32),
            dma((13,)), dma((2, 3, n - 1)), dma((2, 3, n - 1)), dma((2, 2)), dma((2, 2)), dma((2,)), dma((2,)),
            dma((2, n // 2)), dma((2, n // 2)), dma((3,)), dma((3,)), dma((2,)), dma((2,)),
        ],
        compiler_params=pltpu.CompilerParams(
            collective_id=1, has_side_effects=True, vmem_limit_bytes=ROOM
        ),
        name="reduce_all",
    )(xg, d, dz, wp, w, small, flat, gain)


def adamw_step(weight, first, second, grad, rate, decay):
    first_new = beta_first * first + (1.0 - beta_first) * grad
    second_new = beta_second * second + (1.0 - beta_second) * grad * grad
    hat_first = first_new * (1.0 / (1.0 - beta_first**STEP))
    hat_second = second_new * (1.0 / (1.0 - beta_second**STEP))
    weight_new = weight - rate * (hat_first / (jnp.sqrt(hat_second) + adam_eps) + decay * weight)
    return (weight_new, first_new, second_new)


def finish_body(
    width, heads,
    in_ref, cot_ref, branch_ref, back_ref, flat_ref, early_ref, late_ref, bcg_ref,
    zx_ref, zx1_ref, zx2_ref, bc_ref, bc1_ref, bc2_ref, out_ref, out1_ref, out2_ref, late_all_ref, dt_ref, dt1_ref, dt2_ref,
    layer_ref, grad_ref, zxn_ref, zx1n_ref, zx2n_ref, bcn_ref, bc1n_ref, bc2n_ref,
    outn_ref, out1n_ref, out2n_ref, dtn_ref, dt1n_ref, dt2n_ref,
):
    def update(refs, news, grad):
        fresh = adamw_step(*(ref[...] for ref in refs), grad, matrix_rate, matrix_decay)
        for ref, value in zip(news, fresh):
            ref[...] = value

    for k, grad in ((0, early_ref), (1, late_ref)):
        fresh = adamw_step(
            *(ref[:, k, :] for ref in (zx_ref, zx1_ref, zx2_ref)), grad[:, :width], matrix_rate, matrix_decay
        )
        for ref, value in zip((zxn_ref, zx1n_ref, zx2n_ref), fresh):
            ref[:, k, :] = value
    update((bc_ref, bc1_ref, bc2_ref), (bcn_ref, bc1n_ref, bc2n_ref), bcg_ref[...])
    update((out_ref, out1_ref, out2_ref), (outn_ref, out1n_ref, out2n_ref), early_ref[:, width:])

    @pl.when(pl.program_id(0) == 0)
    def _():
        unit = jnp.where(
            lax.broadcasted_iota(jnp.int32, (16, LANES), 0) == lax.broadcasted_iota(jnp.int32, (16, LANES), 1), 1.0, 0.0
        ).astype(f32)
        turned = mm_exact(unit, late_all_ref[:, width + 2 * NS :], NT)
        update((dt_ref, dt1_ref, dt2_ref), (dtn_ref, dt1n_ref, dt2n_ref), turned[:heads])

    rows = in_ref.shape[0]
    tile = 64

    def some(i, _):
        at = span(i * tile, tile)
        squares = jnp.zeros((tile, LANES), f32)
        inner = jnp.zeros((tile, LANES), f32)
        for c in range(D // LANES):
            cols = slice(c * LANES, (c + 1) * LANES)
            x = in_ref[at, cols].astype(f32)
            squares = squares + x * x
            inner = inner + x * flat_ref[c : c + 1, :] * back_ref[at, cols].astype(f32)
        r = lax.rsqrt(jnp.sum(squares, axis=-1, keepdims=True) / D + norm_eps)
        k = r * r * r * jnp.sum(inner, axis=-1, keepdims=True) / D
        r, k = jnp.broadcast_to(r, (tile, LANES)), jnp.broadcast_to(k, (tile, LANES))
        for c in range(D // LANES):
            cols = slice(c * LANES, (c + 1) * LANES)
            x = in_ref[at, cols].astype(f32)
            layer_ref[at, cols] = (x + branch_ref[at, cols].astype(f32)).astype(bf16)
            back = back_ref[at, cols].astype(f32)
            grad_ref[at, cols] = cot_ref[at, cols].astype(f32) + r * flat_ref[c : c + 1, :] * back - x * k
        return 0

    lax.fori_loop(0, rows // tile, some, 0)


def finish(layer_input, out_grad, branch, back, flat, early, late, bcg, zx, bc, out, dt):
    (rows, width), heads = out[0].shape, dt[0].shape[0]
    steps = 4 if rows % 32 == 0 else 2
    part = lambda a: pl.BlockSpec((a.shape[0] // steps, *a.shape[1:]), lambda i: (i,) + (0,) * (a.ndim - 1))
    whole = lambda a: pl.BlockSpec(a.shape, lambda i: (0,) * a.ndim)
    like = lambda a, dtype=f32: jax.ShapeDtypeStruct(a.shape, dtype)
    weights = (*zx, *bc, *out)
    return pl.pallas_call(
        functools.partial(finish_body, width, heads),
        grid=(steps,),
        in_specs=[
            *(part(a) for a in (layer_input, out_grad, branch, back)), whole(flat),
            *(part(a) for a in (early, late, bcg, *weights)), whole(late), *(whole(a) for a in dt),
        ],
        out_specs=[part(layer_input), part(back), *(part(a) for a in weights), *(whole(a) for a in dt)],
        out_shape=[like(layer_input, bf16), like(layer_input), *(like(a) for a in weights), *(like(a) for a in dt)],
        compiler_params=pltpu.CompilerParams(vmem_limit_bytes=ROOM),
        name="finish",
    )(layer_input, out_grad, branch, back, flat, early, late, bcg, *weights, late, *dt)


def local(
    layer_input,
    out_grad,
    small_params,
    small_first,
    small_second,
    w_zx,
    zx_first,
    zx_second,
    w_bc,
    bc_first,
    bc_second,
    w_dt,
    dt_first,
    dt_second,
    w_out,
    out_first,
    out_second,
):
    n = lax.axis_size("dp")
    flat = jnp.pad(small_params, (0, FLAT_ROWS * LANES - small_params.shape[0])).reshape(FLAT_ROWS, LANES)
    v, xc, dr, st, dy, dz, branch, gz, go, carry, gate, gain, xg, w_all, pair_all, taps, head, chan = ssd_forward(
        n, layer_input, out_grad, flat, w_zx, w_bc, w_dt.T, w_out
    )
    d_late, small, owner_early, own_branch = ssd_backward(
        n, dy, v, xc, dr, st, gate, taps, head, chan, carry, gz, go, branch
    )
    owner_late, d_normed_in, owner_bc, flat_grad = reduce_all(
        n, xg, d_late, dz, pair_all, w_all, small, flat, gain
    )
    small_grad = flat_grad.reshape(-1)[: small_params.shape[0]]
    small_new, small_first_new, small_second_new = adamw_step(
        small_params, small_first, small_second, small_grad, small_rate, 0.0
    )
    (
        layer_output, input_grad, zx_new, zx_first_new, zx_second_new, bc_new, bc_first_new, bc_second_new,
        out_new, out_first_new, out_second_new, dt_new, dt_first_new, dt_second_new,
    ) = finish(
        layer_input, out_grad, own_branch, d_normed_in, flat, owner_early, owner_late, owner_bc,
        (w_zx, zx_first, zx_second), (w_bc, bc_first, bc_second), (w_out, out_first, out_second),
        (w_dt.T, dt_first.T, dt_second.T),
    )
    dt_new, dt_first_new, dt_second_new = dt_new.T, dt_first_new.T, dt_second_new.T
    return (
        layer_output,
        input_grad,
        small_new,
        small_first_new,
        small_second_new,
        zx_new,
        zx_first_new,
        zx_second_new,
        bc_new,
        bc_first_new,
        bc_second_new,
        dt_new,
        dt_first_new,
        dt_second_new,
        out_new,
        out_first_new,
        out_second_new,
    )


def solution(mesh):
    return jax.shard_map(
        local,
        mesh=mesh,
        in_specs=(
            P(("dp", "tensor"), None),
            P(("dp", "tensor"), None),
            P(),
            P(),
            P(),
            P("dp", None, "tensor"),
            P("dp", None, "tensor"),
            P("dp", None, "tensor"),
            P("dp", None),
            P("dp", None),
            P("dp", None),
            P("dp", "tensor"),
            P("dp", "tensor"),
            P("dp", "tensor"),
            P("dp", "tensor"),
            P("dp", "tensor"),
            P("dp", "tensor"),
        ),
        out_specs=(
            P(("dp", "tensor"), None),
            P(("dp", "tensor"), None),
            P(),
            P(),
            P(),
            P("dp", None, "tensor"),
            P("dp", None, "tensor"),
            P("dp", None, "tensor"),
            P("dp", None),
            P("dp", None),
            P("dp", None),
            P("dp", "tensor"),
            P("dp", "tensor"),
            P("dp", "tensor"),
            P("dp", "tensor"),
            P("dp", "tensor"),
            P("dp", "tensor"),
        ),
        check_vma=False,
    )
```

```python
import functools

import jax
import jax.numpy as jnp
from jax import lax
from jax.experimental import pallas as pl
from jax.experimental.pallas import tpu as pltpu
from jax.sharding import PartitionSpec as P

D = 1536
DI = 3072
H = 48
NS = 128
P_SIZE = 64
CONV = 4
LEN = 2048
STEP = 10

T = 128
ROWS = 256
LANES = 128
ROOM = 60 * 2**20

norm_eps = 1e-05
adam_eps = 1e-08
beta_first = 0.9
beta_second = 0.95
matrix_rate = 0.01
small_rate = 0.1
matrix_decay = 0.1

f32 = jnp.float32
bf16 = jnp.bfloat16
NN = (((1,), (0,)), ((), ()))
NT = (((1,), (1,)), ((), ()))
TN = (((0,), (0,)), ((), ()))
HIGHEST = lax.Precision.HIGHEST


GATE_ROW, TAPS_ROW, BIAS_ROW, TAPS_BC_ROW, BIAS_BC_ROW, HEAD_ROW, FLAT_ROWS = 12, 36, 132, 156, 164, 166, 168


def mm(a, b, dims=NN):
    return lax.dot_general(a, b, dims, preferred_element_type=f32)


def mm_exact(a, b, dims=NN):
    return lax.dot_general(a, b, dims, preferred_element_type=f32, precision=HIGHEST)


def sigmoid(v):
    return 0.5 * jnp.tanh(0.5 * v) + 0.5


def softplus(v):
    return jnp.maximum(v, 0.0) + jnp.log1p(jnp.exp(-jnp.abs(v)))


def spread(col):
    return jnp.broadcast_to(col, (T, LANES))


def block_iota(axis):
    return lax.broadcasted_iota(jnp.int32, (T, LANES), axis)


HEADS = 16
LOG2_E = 1.4426950408889634


def pieces(value, count):
    parts = []
    for k in range(count):
        part = value.astype(bf16)
        parts.append(part)
        if k < count - 1:
            value = value - part.astype(f32)
    return jnp.concatenate(parts, axis=1)


def columns_of(rows):
    return jnp.concatenate([rows, jnp.zeros((LANES - HEADS, T), f32)], axis=0).T


def set_heads(head_ref, head_t, until):
    turned = jnp.concatenate([head_ref[...], jnp.zeros((LANES - 8, LANES), f32)], axis=0).T
    head_t[0] = spread(turned[:, 0:1])[:HEADS]
    head_t[1] = spread(turned[:, 1:2])[:HEADS]
    matrix = jnp.where(block_iota(0) <= block_iota(1), 1.0, 0.0).astype(bf16)
    for k in range(3):
        until[k * T : (k + 1) * T, :] = matrix


def head_rows(dr_ref, head_t, until, rows):
    raw = dr_ref[rows, :].T[:HEADS] + head_t[0]
    dt = softplus(raw)
    decay = mm(pieces(dt * (head_t[1] * LOG2_E), 3), until[...])
    return raw, dt, decay, columns_of(dt), columns_of(decay)


def ring_place(n):
    me = lax.axis_index("dp")
    z, x = lax.div(me, 2), lax.rem(me, 2)
    return z + x * (n - 1 - 2 * z)


def ring_index(pos, n):
    back = lax.div(pos, n // 2)
    return 2 * pos + back * (2 * n - 1 - 4 * pos)


def neighbours(n):
    pos = ring_place(n)
    right = ring_index(lax.rem(pos + 1, n), n)
    left = ring_index(lax.rem(pos + n - 1, n), n)
    me = lax.axis_index("tensor")
    y, core = lax.div(me, 2), lax.rem(me, 2)
    across = 2 * (1 - y) + core
    beside = 2 * y + 1 - core
    return pos, ({"dp": right}, {"dp": left}), me, {"tensor": across}, {"tensor": beside}


def greet(peers):
    barrier = pltpu.get_barrier_semaphore()
    for peer in peers:
        pl.semaphore_signal(barrier, inc=1, device_id=peer, device_id_type=pl.DeviceIdType.MESH)


def enter(peers):
    greet(peers)
    pl.semaphore_wait(pltpu.get_barrier_semaphore(), len(peers))


def remote(src, dst, send_sem, recv_sem, peer):
    return pltpu.make_async_remote_copy(
        src_ref=src, dst_ref=dst, send_sem=send_sem, recv_sem=recv_sem,
        device_id=peer, device_id_type=pl.DeviceIdType.MESH,
    )


def span(start, size):
    return pl.ds(pl.multiple_of(start, 16), size)


def strip(rows):
    return next(size for size in (48, 32, 16) if rows % size == 0)


def cut_rows(rows):
    top = rows // 32 * 16
    return ((0, top), (top, rows - top))


def forward_body(
    n, rows, tokens, width,
    in_ref, cot_ref, flat_ref, wzx_ref, wbc_ref, wdt_ref, wout_ref,
    v_ref, xc_ref, dr_ref, st_ref, dy_ref, dz_ref, branch_ref, early_ref, gate_ref, gain_ref,
    xg_ref, ws_ref, wps_ref, taps_ref, head_ref, chan_ref,
    halo, state, y_all, z_all, dn_all, nl_all, dz_all, xg, cots, ws, wps, sums, red, head_t, until, across_state, tails,
    own_keep, early_keep, lead_keep, lead_send, lead_recv, x_keep, x_over_send, x_over_recv, x_side_send, x_side_recv,
    x_pass_send, x_pass_recv, ring_keep, ring_send, ring_recv, over_send, over_recv,
    side_send, side_recv, pass_send, pass_recv, sum_send, sum_recv,
):
    pairs = width // LANES
    wide = width + 2 * NS
    step = pl.program_id(0)
    steps = LEN // ROWS
    tall = 2 * ROWS
    norming = steps // 2
    gating = norming + 1
    forming = gating + 1
    products = forming + steps // 2
    pos, ring, me, across, beside = neighbours(n)
    opposite = lax.rem(me + 2, 4)
    next_door = me + 1 - 2 * lax.rem(me, 2)
    far = lax.rem(next_door + 2, 4)
    askew = {"tensor": far}
    quarter = tokens // 4
    hops = n // 2
    cuts = cut_rows(rows)
    mine = ring_index(pos, n)

    late = wide + LANES
    parts_of = ((0, width), (width, width))

    def hop(k, part, way, h):
        first, size = cuts[part]
        cols = pl.ds(*parts_of[k])
        block = ring_index(lax.rem(pos + (h if way else n - h), n), n)
        here = wps.at[span(block * rows + first, size), cols]
        return remote(here, here, ring_send.at[way, part, k, h], ring_recv.at[way, part, k, h], ring[way])

    def hop_lands(k, part, way, h):
        first, size = cuts[part]
        block = ring_index(lax.rem(pos + (h + 1 if way else n - h - 1), n), n)
        return span(block * rows + first, size), pl.ds(*parts_of[k])

    def hop_arrival(k, part, way, h):
        here = wps.at[hop_lands(k, part, way, h)]
        return remote(here, here, ring_send.at[way, part, k, h], ring_recv.at[way, part, k, h], ring[way])

    def hop_keep(part, way, h):
        at = hop_lands(1, part, way, h)
        return pltpu.make_async_copy(wps.at[at], wps_ref.at[at], ring_keep.at[way, part, h])

    def hop_ways(h):
        return [(part, way) for part in (0, 1) for way in (0, 1) if h < hops - 1 or part == way]

    def hop_on(k, h):
        for part, way in hop_ways(h - 1) if h > 0 else ():
            hop_arrival(k, part, way, h - 1).wait_recv()
            if k == 1:
                hop_keep(part, way, h - 1).start()
            if h < hops and (part, way) in hop_ways(h):
                hop(k, part, way, h).start()
        if h == 0:
            for part, way in hop_ways(0):
                hop(k, part, way, 0).start()

    def over(k):
        return remote(
            cot_ref.at[pl.ds(k * quarter, quarter)], cots.at[span(me * tokens + k * quarter, quarter)],
            over_send.at[k], over_recv.at[k], across,
        )

    def landed(start, size, send, recv, peer):
        here = cots.at[span(start, size)]
        return remote(here, here, send, recv, peer)

    def over_arrival(k):
        return landed(opposite * tokens + k * quarter, quarter, over_send.at[k], over_recv.at[k], across)

    def passing(k):
        return landed(opposite * tokens + k * quarter, quarter, pass_send.at[k], pass_recv.at[k], beside)

    def pass_arrival(k):
        return landed(far * tokens + k * quarter, quarter, pass_send.at[k], pass_recv.at[k], beside)

    def side():
        return remote(cot_ref, cots.at[span(me * tokens, tokens)], side_send.at[0], side_recv.at[0], beside)

    def side_arrival():
        return landed(next_door * tokens, tokens, side_send.at[0], side_recv.at[0], beside)

    def own_cot():
        return pltpu.make_async_copy(cot_ref, cots.at[span(me * tokens, tokens)], own_keep.at[0])

    def own_z():
        at = span(mine * rows, rows), pl.ds(*parts_of[1])
        return pltpu.make_async_copy(wps.at[at], wps_ref.at[at], own_keep.at[1])

    def pass_on(*pieces):
        for k in pieces:
            over_arrival(k).wait_recv()
            passing(k).start()

    def normalize(k):
        def some(i, _):
            at = span(me * tokens + k * quarter + i * 64, 64)
            squares = jnp.zeros((64, LANES), f32)
            for c in range(D // LANES):
                x = xg[at, c * LANES : (c + 1) * LANES].astype(f32)
                squares = squares + x * x
            inverse = lax.rsqrt(jnp.sum(squares, axis=-1, keepdims=True) / D + norm_eps)
            inverse = jnp.broadcast_to(inverse, (64, LANES))
            for c in range(D // LANES):
                cols = slice(c * LANES, (c + 1) * LANES)
                xg[at, cols] = (xg[at, cols].astype(f32) * inverse * flat_ref[c : c + 1, :]).astype(bf16)
            return 0

        lax.fori_loop(0, quarter // 64, some, 0)

    @pl.when(step == 0)
    def _():
        own_rows = span(me * tokens, tokens)
        greet((*ring, across, beside, askew))
        load = pltpu.make_async_copy(in_ref, xg.at[own_rows], own_keep.at[2])
        load.start()
        own_cot().start()
        mine_at = span(mine * rows, rows)
        ws[mine_at, :width] = wzx_ref[:, 1, :].astype(bf16)
        ws[mine_at, width:wide] = wbc_ref[...].astype(bf16)
        heads = wdt_ref.shape[0]
        unit = jnp.where(
            lax.broadcasted_iota(jnp.int32, (16, LANES), 0) == lax.broadcasted_iota(jnp.int32, (16, LANES), 1), 1.0, 0.0
        ).astype(bf16)
        steps_w = jnp.concatenate([wdt_ref[...], jnp.zeros((16 - heads, rows), f32)], axis=0).astype(bf16)
        ws[mine_at, wide:] = mm(steps_w, unit, TN).astype(bf16)
        load.wait()
        normalize(0)
        pl.semaphore_wait(pltpu.get_barrier_semaphore(), 5)
        started, kept = [], []

        def go(*args):
            copy = remote(*args)
            copy.start()
            started.append(copy)

        def keep(src, dst, sem):
            copy = pltpu.make_async_copy(src, dst, sem)
            copy.start()
            kept.append(copy)

        def arrived(part, way, h, block):
            first, size = cuts[part]
            at = span(block * rows + first, size)
            remote(
                ws.at[at], ws.at[at], lead_send.at[way, part, h], lead_recv.at[way, part, h], ring[way]
            ).wait_recv()
            keep(ws.at[at], ws_ref.at[at], lead_keep.at[way, part, h])

        def lead(h, parts=(0, 1)):
            for part in parts:
                first, size = cuts[part]
                for way in (0, 1):
                    block = ring_index(lax.rem(pos + (h if way else n - h), n), n)
                    here = ws.at[span(block * rows + first, size)]
                    if h > 0:
                        arrived(part, way, h - 1, block)
                    if h == hops - 1 and part != way:
                        continue
                    go(here, here, lead_send.at[way, part, h], lead_recv.at[way, part, h], ring[way])

        def x_over(k):
            at = span(me * tokens + k * quarter, quarter)
            go(xg.at[at], xg.at[at], x_over_send.at[k], x_over_recv.at[k], across)

        def x_pass(k):
            at = span(opposite * tokens + k * quarter, quarter)
            here = xg.at[at]
            remote(here, here, x_over_send.at[k], x_over_recv.at[k], across).wait_recv()
            go(here, here, x_pass_send.at[k], x_pass_recv.at[k], beside)
            keep(here, xg_ref.at[at], x_keep.at[k])

        def x_pass_lands(k):
            at = span(far * tokens + k * quarter, quarter)
            remote(xg.at[at], xg.at[at], x_pass_send.at[k], x_pass_recv.at[k], beside).wait_recv()
            keep(xg.at[at], xg_ref.at[at], x_keep.at[4 + k])

        lead(0, (0,))
        leading = list(started)
        x_over(0)
        for k in (1, 2, 3):
            normalize(k)
            if k == 1:
                x_over(1)
        go(xg.at[own_rows], xg.at[own_rows], x_side_send.at[0], x_side_recv.at[0], beside)
        keep(xg.at[own_rows], xg_ref.at[own_rows], x_keep.at[8])
        wps[mine_at, :width] = wout_ref[...].astype(bf16)
        wps[mine_at, width:] = wzx_ref[:, 0, :].astype(bf16)
        for copy in leading:
            copy.wait_send()
            started.remove(copy)
        lead(0, (1,))
        keep(ws.at[mine_at], ws_ref.at[mine_at], x_keep.at[9])
        own_z().start()
        halo[0:8, :] = jnp.zeros((8, wide), f32)
        state[...] = jnp.zeros_like(state)
        gate_ref[...] = jnp.zeros_like(gate_ref)
        parameter_rows(me, width, flat_ref, taps_ref, head_ref, chan_ref)
        set_heads(head_ref, head_t, until)
        lead(1)
        x_over(2)
        at = span(next_door * tokens, tokens)
        remote(xg.at[at], xg.at[at], x_side_send.at[0], x_side_recv.at[0], beside).wait_recv()
        keep(xg.at[at], xg_ref.at[at], x_keep.at[10])
        side().start()
        lead(2)
        x_over(3)
        x_pass(0)
        x_pass(1)
        for h in range(3, hops):
            lead(h)
        hop_on(0, 0)
        x_pass(2)
        over(0).start()
        x_pass_lands(0)
        x_pass_lands(1)
        x_pass(3)
        for part in (0, 1):
            arrived(part, part, hops - 1, ring_index(lax.rem(pos + n // 2, n), n))
        hop_on(1, 0)
        over(1).start()
        x_pass_lands(2)
        x_pass_lands(3)
        for copy in kept:
            copy.wait()
        for copy in started:
            copy.wait_send()

    def at_tick(tick):
        for k, times in enumerate(((1, 4, 6), (2, 5, 7))):
            for h in range(1, min(hops, 4)):
                pl.when(tick == times[h - 1])(functools.partial(hop_on, k, h))

        @pl.when(tick == 2)
        def _():
            over(2).start()

        @pl.when(tick == 4)
        def _():
            over(3).start()
            pass_on(0, 1)

        pl.when(tick == steps - 1)(functools.partial(pass_on, 2))

    @pl.when(step < norming)
    def _():
        def chunk(i, _):
            tick = 2 * step + i
            at_tick(tick)
            scan_step(
                width, tick, i, xg, ws, taps_ref, head_ref, chan_ref,
                v_ref, xc_ref, dr_ref, st_ref, halo, state, y_all, head_t, until, across_state, tails,
                functools.partial(pass_on, 3),
            )
            return 0

        lax.fori_loop(0, 2, chunk, 0)

    @pl.when(step == norming)
    def _():
        for k in (0, 1):
            for h in range(4, hops):
                hop_on(k, h)
        hop_on(0, hops)
        side_arrival().wait_recv()
        for k in range(4):
            pass_arrival(k).wait_recv()
        own_cot().wait()
        own_z().wait()

        def some(i, _):
            at = span(i * tall, tall)
            dn_all[at, :] = mm(cots[at, :], wps[:, :width]).astype(bf16)
            return 0

        lax.fori_loop(0, LEN // tall, some, 0)

    @pl.when(step == gating)
    def _():
        hop_on(1, hops)
        ones = jnp.ones((8, LANES), f32)

        def some(i, _):
            at = span(i * tall, tall)
            z_all[at, :] = mm(xg[at, :], wps[:, width:])
            for sub in range(tall // T):
                rows_at = span(i * tall + sub * T, T)
                squares = jnp.zeros((T, LANES), f32)
                inner = jnp.zeros((T, LANES), f32)
                for p in range(pairs):
                    cols = slice(p * LANES, (p + 1) * LANES)
                    z = z_all[rows_at, cols]
                    gated = y_all[rows_at, cols] * (z * sigmoid(z))
                    squares = squares + gated * gated
                    inner = inner + gated * chan_ref[0:1, cols] * dn_all[rows_at, cols].astype(f32)
                lanes = pl.ds(pl.multiple_of(i * tall + sub * T, T), T)
                sums[me, 0:4, lanes] = mm_exact(ones, squares, NT)[0:4]
                sums[me, 4:8, lanes] = mm_exact(ones, inner, NT)[4:8]
            return 0

        lax.fori_loop(0, LEN // tall, some, 0)

    @pl.when(step == forming - 1)
    def _():
        peers = ((beside, next_door), (across, opposite), (askew, far))
        for k, (peer, _) in enumerate(peers):
            remote(sums.at[me], sums.at[me], sum_send.at[k], sum_recv.at[k], peer).start()
        for h in range(hops):
            for part, way in hop_ways(h):
                for k in (0, 1):
                    hop(k, part, way, h).wait_send()
                hop_keep(part, way, h).wait()
        side().wait_send()
        for k in range(4):
            over(k).wait_send()
            passing(k).wait_send()
        for k, (peer, other) in enumerate(peers):
            remote(sums.at[other], sums.at[other], sum_send.at[k], sum_recv.at[k], peer).wait()
        red[...] = ((sums[0] + sums[1]) + sums[2]) + sums[3]

    @pl.when((step >= forming) & (step < products))
    def _():
        def some(i, _):
            first = (step - forming) * tall + i * ROWS
            lanes = pl.ds(pl.multiple_of(first, ROWS), ROWS)
            q_row = lax.rsqrt(red[0:4, lanes] / DI + norm_eps)
            k_row = q_row * q_row * q_row * red[4:8, lanes] / DI
            turned = jnp.concatenate([q_row, k_row], axis=0).T
            for sub in range(ROWS // T):
                rows_at = slice(sub * T, (sub + 1) * T)
                at = span(first + sub * T, T)
                q, kk = spread(turned[rows_at, 0:1]), spread(turned[rows_at, 4:5])
                for p in range(pairs):
                    cols = slice(p * LANES, (p + 1) * LANES)
                    z, y, dn = z_all[at, cols], y_all[at, cols], dn_all[at, cols].astype(f32)
                    gain = chan_ref[0:1, cols]
                    s = sigmoid(z)
                    sz = z * s
                    gated = y * sz
                    gq = gated * q
                    dg = q * gain * dn - gated * kk
                    gate_ref[:, cols] += jnp.sum((gq * dn).reshape(T // 8, 8, LANES), axis=0)
                    nl_all[at, cols] = (gq * gain).astype(bf16)
                    dz_all[at, cols] = (dg * y * (s + sz * (1.0 - s))).astype(bf16)
                    dn_all[at, cols] = (dg * sz).astype(bf16)
            branch_ref[span(i * ROWS, ROWS), :] = mm(nl_all[span(first, ROWS), :], wps[:, :width], NT).astype(bf16)
            return 0

        lax.fori_loop(0, 2, some, 0)

    def rows_out():
        return [
            pltpu.make_async_copy(src, dst, own_keep.at[2 + k])
            for k, (src, dst) in enumerate(((dz_all, dz_ref), (dn_all, dy_ref)))
        ]

    def early_out(i):
        at = span(i * ROWS, ROWS)
        return [
            pltpu.make_async_copy(src.at[at, pl.ds(0, width)], early_ref.at[at, pl.ds(k * width, width)], early_keep.at[k, i])
            for k, src in enumerate((ws, wps))
        ]

    @pl.when(step == products)
    def _():
        for copy in rows_out():
            copy.start()

        def some(i, _):
            at = span(i * ROWS, ROWS)
            lanes = pl.ds(pl.multiple_of(i * ROWS, ROWS), ROWS)
            grad = mm(xg[:, lanes], dz_all[...], TN)
            ws[at, :width] = grad.astype(bf16)
            share = jnp.zeros((ROWS, LANES), f32)
            for p in range(pairs):
                cols = slice(p * LANES, (p + 1) * LANES)
                w = wps[at, width + p * LANES : width + (p + 1) * LANES]
                share = share + grad[:, cols] * w.astype(f32)
            gain_ref[:, lanes] = mm_exact(jnp.ones((8, LANES), f32), share, NT)
            wps[at, :width] = mm(cots[:, lanes], nl_all[...], TN).astype(bf16)
            for copy in early_out(i):
                copy.start()
            return 0

        lax.fori_loop(0, D // ROWS, some, 0)
        for copy in rows_out():
            copy.wait()

        def done(i, _):
            for copy in early_out(i):
                copy.wait()
            return 0

        lax.fori_loop(0, D // ROWS, done, 0)


def parameter_rows(me, width, flat_ref, taps_ref, head_ref, chan_ref):
    pairs = width // LANES
    heads = width // P_SIZE
    taps_ref[...] = jnp.zeros_like(taps_ref)
    chan_ref[...] = jnp.zeros_like(chan_ref)
    for c in range(pairs):
        cols = slice(c * LANES, (c + 1) * LANES)
        chan_ref[0:1, cols] = flat_ref[pl.ds(GATE_ROW + pairs * me + c, 1), :]
        taps_ref[CONV : CONV + 1, cols] = flat_ref[pl.ds(BIAS_ROW + pairs * me + c, 1), :]
        for k in range(CONV):
            taps_ref[k : k + 1, cols] = flat_ref[pl.ds(TAPS_ROW + 4 * pairs * k + pairs * me + c, 1), :]
    for c in range(2):
        cols = slice(width + c * LANES, width + (c + 1) * LANES)
        taps_ref[CONV : CONV + 1, cols] = flat_ref[BIAS_BC_ROW + c : BIAS_BC_ROW + c + 1, :]
        for k in range(CONV):
            row = TAPS_BC_ROW + 2 * k + c
            taps_ref[k : k + 1, cols] = flat_ref[row : row + 1, :]
    both = jnp.concatenate([flat_ref[HEAD_ROW : HEAD_ROW + 1, :], flat_ref[HEAD_ROW + 1 : HEAD_ROW + 2, :]], axis=1)
    both = jnp.broadcast_to(both, (8, 2 * LANES))
    lane = lax.broadcasted_iota(jnp.int32, (2 * LANES, LANES), 0)
    head = lax.broadcasted_iota(jnp.int32, (2 * LANES, LANES), 1)

    def take(kind):
        match = (lane == 4 * heads * kind + heads * me + head) & (head < heads)
        return mm_exact(both, jnp.where(match, 1.0, 0.0).astype(f32))

    valid = lax.broadcasted_iota(jnp.int32, (8, LANES), 1) < heads
    row = lax.broadcasted_iota(jnp.int32, (8, LANES), 0)
    rates = jnp.where(valid, -jnp.exp(take(1)), 0.0)
    head_ref[...] = jnp.where(row == 0, take(0), jnp.where(row == 1, rates, 0.0))
    skip = mm_exact(take(2), picked(width).astype(f32), NT)
    chan_ref[1:2, :] = skip[0:1]


def picked(width):
    channel = lax.broadcasted_iota(jnp.int32, (width, LANES), 0)
    head = lax.broadcasted_iota(jnp.int32, (width, LANES), 1)
    return jnp.where((channel >= head * P_SIZE) & (channel < (head + 1) * P_SIZE), 1.0, 0.0).astype(bf16)


def scan_step(
    width, tick, i, xg, w_ref, taps_ref, head_ref, chan_ref,
    v_ref, xc_ref, dr_ref, st_ref, halo, state, y_all, head_t, until, across_state, tails, late_turn,
):
    pairs = width // LANES
    wide = width + 2 * NS
    mine = span(tick * ROWS, ROWS)
    dr_ref[span(i * ROWS, ROWS), :] = mm(xg[mine, :], w_ref[:, wide:])
    halo[8 : 8 + ROWS, :] = mm(xg[mine, :], w_ref[:, :wide])
    low_half = block_iota(1) < P_SIZE
    causal = block_iota(0) >= block_iota(1)

    def convolved(sub, block):
        cols = slice(block * LANES, (block + 1) * LANES)
        total = taps_ref[CONV : CONV + 1, cols]
        for k in range(CONV):
            first = 8 - (CONV - 1) + k + sub * T
            total = total + taps_ref[k : k + 1, cols] * halo[first : first + T, cols]
        rows = span(i * ROWS + sub * T, T)
        xc_ref[rows, cols] = total.astype(bf16)
        v_ref[rows, cols] = halo[8 + sub * T : 8 + (sub + 1) * T, cols].astype(bf16)
        return total * sigmoid(total)

    for sub in range(ROWS // T):
        rows = span(i * ROWS + sub * T, T)
        _, _, decay_t, dt, decay = head_rows(dr_ref, head_t, until, rows)
        b_low = convolved(sub, pairs).astype(bf16)
        c_low = convolved(sub, pairs + 1).astype(bf16)
        b_t = b_low.T
        scores = jnp.where(causal, mm(c_low, b_low, NT), 0.0)
        entering = state[...].astype(bf16)
        st_ref[i * (ROWS // T) + sub] = entering
        across_state[...] = mm(c_low, entering)
        for p in range(pairs):
            cols = slice(p * LANES, (p + 1) * LANES)
            x = convolved(sub, p)
            l1, l2 = spread(decay[:, 2 * p : 2 * p + 1]), spread(decay[:, 2 * p + 1 : 2 * p + 2])
            both = jnp.where(low_half, l1, l2)
            dtb = jnp.where(
                low_half, spread(dt[:, 2 * p : 2 * p + 1]), spread(dt[:, 2 * p + 1 : 2 * p + 2])
            )
            u = x * dtb
            m1 = scores * jnp.exp2(jnp.minimum(l1 - decay_t[2 * p : 2 * p + 1, :], 0.0))
            m2 = scores * jnp.exp2(jnp.minimum(l2 - decay_t[2 * p + 1 : 2 * p + 2, :], 0.0))
            mixing = jnp.concatenate([m1.astype(bf16), m2.astype(bf16)], axis=1)
            u_low = u.astype(bf16)
            zero = jnp.zeros_like(u_low)
            parts = jnp.concatenate(
                [jnp.where(low_half, u_low, zero), jnp.where(low_half, zero, u_low)], axis=0
            )
            last = both[T - 1 : T, :]
            y = mm(mixing, parts) + jnp.exp2(both) * across_state[:, cols] + chan_ref[1:2, cols] * x
            tails[:, cols] = (u * jnp.exp2(last - both)).astype(bf16)
            state[:, cols] = jnp.exp2(last) * state[:, cols]
            y_all[span(tick * ROWS + sub * T, T), cols] = y
        state[...] = state[...] + mm(b_t, tails[...])
        if sub == 0:
            pl.when(tick == LEN // ROWS - 1)(late_turn)
    halo[0:8, :] = halo[ROWS : ROWS + 8, :]


def ssd_forward(n, layer_input, out_grad, flat, w_zx, w_bc, w_dt, w_out):
    rows, width = w_out.shape
    tokens = layer_input.shape[0]
    length = 4 * tokens
    wide = width + 2 * NS
    tall = 2 * ROWS
    steps = length // tall
    forming = steps + 2
    products = forming + steps
    subs = tall // T
    assert length == LEN
    row = lambda m: pl.BlockSpec((tall, m), lambda i: (jnp.minimum(i, steps - 1), 0))
    form = lambda m: pl.BlockSpec((tall, m), lambda i: (jnp.clip(i - forming, 0, steps - 1), 0))
    whole = lambda a: pl.BlockSpec(a.shape, lambda i: (0,) * a.ndim, pipeline_mode=pl.Buffered(1))
    fixed = lambda m: pl.BlockSpec((8, m), lambda i: (0, 0))
    anywhere = pl.BlockSpec(memory_space=pl.ANY)
    vm, dma = pltpu.VMEM, pltpu.SemaphoreType.DMA
    hops, lead = dma((2, 2, 2, n // 2)), dma((2, 2, n // 2))
    shape = lambda dims, dtype: jax.ShapeDtypeStruct(dims, dtype)
    return pl.pallas_call(
        functools.partial(forward_body, n, rows, tokens, width),
        grid=(products + 1,),
        in_specs=[anywhere, anywhere, *(whole(a) for a in (flat, w_zx, w_bc, w_dt, w_out))],
        out_specs=[
            row(wide), row(wide), row(LANES), pl.BlockSpec((subs, NS, width), lambda i: (jnp.minimum(i, steps - 1), 0, 0)),
            anywhere, anywhere, form(D), anywhere,
            fixed(width), fixed(D), anywhere, anywhere, anywhere, *(fixed(m) for m in (wide, LANES, width)),
        ],
        out_shape=[
            shape((length, wide), bf16), shape((length, wide), bf16), shape((length, LANES), f32),
            shape((length // T, NS, width), bf16), shape((length, width), bf16), shape((length, width), bf16),
            shape((length, D), bf16), shape((D, 2 * width), bf16), shape((8, width), f32), shape((8, D), f32),
            shape((length, D), bf16), shape((D, wide + LANES), bf16), shape((D, 2 * width), bf16),
            *(shape((8, m), f32) for m in (wide, LANES, width)),
        ],
        scratch_shapes=[
            vm((ROWS + 8, wide), f32), vm((NS, width), f32), vm((length, width), f32), vm((length, width), f32),
            *(vm((length, width), bf16) for _ in range(3)),
            vm((length, D), bf16), vm((length, D), bf16), vm((D, wide + LANES), bf16), vm((D, 2 * width), bf16),
            vm((4, 8, length), f32), vm((8, length), f32), vm((2, HEADS, LANES), f32), vm((3 * T, LANES), bf16),
            vm((T, width), f32), vm((T, width), bf16),
            dma((4,)), dma((2, D // ROWS)), lead, lead, lead, dma((11,)), dma((4,)), dma((4,)), dma((1,)), dma((1,)),
            dma((4,)), dma((4,)), lead, hops, hops, dma((4,)), dma((4,)),
            dma((1,)), dma((1,)), dma((4,)), dma((4,)), dma((3,)), dma((3,)),
        ],
        compiler_params=pltpu.CompilerParams(collective_id=2, has_side_effects=True, vmem_limit_bytes=ROOM),
        name="layer_forward",
    )(layer_input, out_grad, flat, w_zx, w_bc, w_dt, w_out)


def backward_body(
    n, own_rows, tokens, width,
    dy_ref, v_ref, xc_ref, dr_ref, st_ref, gate_ref, taps_ref, head_ref, chan_ref, early_ref, branch_ref,
    d_ref, small_ref, oearly_ref, obranch_ref,
    dxh, dstate, yst, bds, dyeb, utb, products, turn, acc, hacc, pick_ref, pick_t, fades, head_t, until_ref, reach_ref,
    own, slots, near, held, over_slot,
    load_sem, ring_send, ring_recv, near_send, near_recv, over_send, over_recv,
):
    pairs = width // LANES
    wide = width + 2 * NS
    step = pl.program_id(0)
    steps = LEN // ROWS
    subs = ROWS // T
    pos, ring, me, across, beside = neighbours(n)
    opposite = lax.rem(me + 2, 4)
    next_door = me + 1 - 2 * lax.rem(me, 2)
    far = lax.rem(next_door + 2, 4)
    half = tokens // 2
    cuts = cut_rows(own_rows)

    def block_at(way, count):
        return ring_index(lax.rem(pos + (count if way else n - count), n), n)

    def hop(k, way, h):
        first, size = cuts[way]
        if h == 0:
            src = early_ref.at[span(block_at(way, 1) * own_rows + first, size), pl.ds(k * width, width)]
        else:
            src = slots[way][k].at[h - 1]
        return remote(
            src, slots[way][k].at[h], ring_send.at[way, k, h], ring_recv.at[way, k, h], ring[way]
        )

    def near_copy(turned, part):
        start = (next_door if turned else far) * tokens + part * half
        return remote(
            branch_ref.at[span(start, half)], near.at[turned, part],
            near_send.at[turned, part], near_recv.at[turned, part], beside,
        )

    def held_copy(turned, part):
        start = (me if turned else opposite) * tokens + part * half
        return pltpu.make_async_copy(
            branch_ref.at[span(start, half)], held.at[turned, part], load_sem.at[2 * turned + part]
        )

    def over_copy(part):
        return remote(held.at[0, part], over_slot.at[part], over_send.at[part], over_recv.at[part], across)

    def own_copy():
        return pltpu.make_async_copy(early_ref, own, load_sem.at[4])

    def ring_turn(k, h):
        for way in (0, 1):
            first, size = cuts[way]
            hop(k, way, h).wait_recv()
            block = block_at(way, 2 + h) if h < n - 2 else block_at(way, 0)

            tile = strip(size)

            def some(i, _, way=way, first=first, block=block, tile=tile):
                cols = slice(k * width, (k + 1) * width)
                came = slots[way][k][h, span(i * tile, tile), :]
                mine = own[span(block * own_rows + first + i * tile, tile), cols]
                if h < n - 2:
                    slots[way][k][h, span(i * tile, tile), :] = came + mine
                else:
                    oearly_ref[span(first + i * tile, tile), cols] = came.astype(f32) + mine.astype(f32)
                return 0

            lax.fori_loop(0, size // tile, some, 0)
            if h < n - 2:
                hop(k, way, h + 1).start()

    def ring_poll(k, tick):
        for h in range(n - 1):
            pl.when(tick == min(h + 1, steps - 1))(functools.partial(ring_turn, k, h))

    def add_near(turned):
        for part in (0, 1):
            held_copy(turned, part).wait()
            near_copy(turned, part).wait_recv()

            def some(i, _, part=part):
                at = span(i * 32, 32)
                held[turned, part, at, :] = held[turned, part, at, :] + near[turned, part, at, :]
                return 0

            lax.fori_loop(0, half // 32, some, 0)
            if not turned:
                over_copy(part).start()

    @pl.when(step == 0)
    def _():
        enter((*ring, across, beside))
        for way in (0, 1):
            hop(0, way, 0).start()
        for turned in (0, 1):
            for part in (0, 1):
                near_copy(turned, part).start()
                held_copy(turned, part).start()
        own_copy().start()
        dxh[T : T + 8, :] = jnp.zeros((8, wide), f32)
        dstate[...] = jnp.zeros_like(dstate)
        acc[...] = jnp.zeros_like(acc)
        hacc[...] = jnp.zeros_like(hacc)
        turn[...] = jnp.zeros_like(turn)
        pick_ref[...] = picked(width)
        channel = lax.broadcasted_iota(jnp.int32, (HEADS, width), 1)
        head = lax.broadcasted_iota(jnp.int32, (HEADS, width), 0)
        mine = (channel >= head * P_SIZE) & (channel < (head + 1) * P_SIZE)
        pick_t[...] = jnp.where(mine, 1.0, 0.0).astype(bf16)
        set_heads(head_ref, head_t, until_ref)
        from_here = jnp.where(block_iota(0) >= block_iota(1), 1.0, 0.0).astype(bf16)
        after = jnp.where(block_iota(0) < block_iota(1), 1.0, 0.0).astype(bf16)
        for k, matrix in enumerate((from_here, from_here, after, after)):
            reach_ref[k * T : (k + 1) * T, :] = matrix
        products[3 * T :, :] = jnp.zeros((HEADS, width), bf16)

    low_half = block_iota(1) < P_SIZE
    row_at, col_at = block_iota(0), block_iota(1)
    until = row_at <= col_at
    pair_lane = lax.broadcasted_iota(jnp.int32, (8, 2 * T), 1)
    pair_row = lax.broadcasted_iota(jnp.int32, (8, 2 * T), 0)
    each = jnp.where(lax.div(pair_lane, T) == pair_row, 1.0, 0.0).astype(bf16)
    ones = jnp.ones((8, T), bf16)

    def add(index, cols, value):
        acc[index, :, cols] += jnp.sum(value.reshape(T // 8, 8, LANES), axis=0)

    def conv_back(rows, block, d_act, xc, s, act):
        cols = slice(block * LANES, (block + 1) * LANES)
        dxh[0:T, cols] = d_act * (s + act * (1.0 - s))
        v = v_ref[rows, cols].astype(f32)
        total = None
        for m in range(CONV):
            moved = dxh[m : m + T, cols]
            if m == 0:
                add(CONV, cols, moved)
            add(CONV - 1 - m, cols, v * moved)
            term = taps_ref[CONV - 1 - m : CONV - m, cols] * moved
            total = term if total is None else total + term
        d_ref[rows, cols] = total.astype(bf16)

    def work(i, _):
        tick = 2 * step + i
        chunk = 1 - i

        @pl.when(tick == 1)
        def _():
            own_copy().wait()
            add_near(0)

        pl.when(tick == 2)(functools.partial(add_near, 1))
        ring_poll(0, tick)
        for sub in reversed(range(subs)):
            rows = span(chunk * ROWS + sub * T, T)
            block_state = chunk * subs + sub
            raw_t, dt_t, decay_t, dt, decay = head_rows(dr_ref, head_t, until_ref, rows)
            b_cols = slice(width, width + NS)
            c_cols = slice(width + NS, width + 2 * NS)
            b_xc, c_xc = xc_ref[rows, b_cols].astype(f32), xc_ref[rows, c_cols].astype(f32)
            b_s, c_s = sigmoid(b_xc), sigmoid(c_xc)
            b_act, c_act = b_xc * b_s, c_xc * c_s
            b_low, c_low = b_act.astype(bf16), c_act.astype(bf16)
            c_t = c_low.T
            scores_t = jnp.where(until, mm(b_low, c_low, NT), 0.0)
            ds_low = dstate[...].astype(bf16)
            yst[...] = mm(c_low, st_ref[block_state])
            bds[...] = mm(b_low, ds_low)
            d_scores = jnp.zeros((T, LANES), f32)
            for p in range(pairs):
                cols = slice(p * LANES, (p + 1) * LANES)
                dy_low = dy_ref[rows, cols]
                dy = dy_low.astype(f32)
                xc = xc_ref[rows, cols].astype(f32)
                xs = sigmoid(xc)
                x = xc * xs
                l1, l2 = spread(decay[:, 2 * p : 2 * p + 1]), spread(decay[:, 2 * p + 1 : 2 * p + 2])
                both = jnp.where(low_half, l1, l2)
                dtb = jnp.where(
                    low_half, spread(dt[:, 2 * p : 2 * p + 1]), spread(dt[:, 2 * p + 1 : 2 * p + 2])
                )
                u = x * dtb
                last = both[T - 1 : T, :]
                e1 = jnp.exp2(jnp.minimum(decay_t[2 * p : 2 * p + 1, :] - l1, 0.0))
                e2 = jnp.exp2(jnp.minimum(decay_t[2 * p + 1 : 2 * p + 2, :] - l2, 0.0))
                zero = jnp.zeros_like(dy_low)
                dy_parts = jnp.concatenate(
                    [jnp.where(low_half, dy_low, zero), jnp.where(low_half, zero, dy_low)], axis=0
                )
                du_in = mm(
                    jnp.concatenate([(scores_t * e1).astype(bf16), (scores_t * e2).astype(bf16)], axis=1), dy_parts
                )
                d_mix = mm(u.astype(bf16), dy_parts, NT)
                d1, d2 = d_mix[:, :T] * e1, d_mix[:, T:] * e2
                d_scores = d_scores + d1 + d2
                held_pairs = jnp.concatenate([(d1 * scores_t).astype(bf16), (d2 * scores_t).astype(bf16)], axis=1)
                reached_by = mm(ones, held_pairs)
                leaving = mm(each, held_pairs, NT)
                turn[2 * p : 2 * p + 1, :] = reached_by[0:1, :T] - leaving[0:1]
                turn[2 * p + 1 : 2 * p + 2, :] = reached_by[0:1, T:] - leaving[1:2]
                tail = jnp.exp2(last - both)
                fades[0:1, cols] = jnp.exp2(last)
                dye = dy * jnp.exp2(both)
                du_out = tail * bds[:, cols]
                du = du_in + du_out
                products[0:T, cols] = (dye * yst[:, cols]).astype(bf16)
                products[T : 2 * T, cols] = (u * du_out).astype(bf16)
                products[2 * T : 3 * T, cols] = (x * du).astype(bf16)
                dyeb[:, cols] = dye.astype(bf16)
                utb[:, cols] = (u * tail).astype(bf16)
                add(CONV + 1, cols, dy * x)
                conv_back(rows, p, dtb * du + chan_ref[1:2, cols] * dy, xc, xs, x)
            d_scores = jnp.where(until, d_scores, 0.0).astype(bf16)
            d_b = mm(d_scores, c_low) + mm(utb[...], ds_low, NT)
            d_c = mm(d_scores, b_low, TN) + mm(dyeb[...], st_ref[block_state], NT)
            conv_back(rows, pairs, d_b, b_xc, b_s, b_act)
            conv_back(rows, pairs + 1, d_c, c_xc, c_s, c_act)
            fade = fades[0:1, :]
            before_ds = dstate[...]
            through = jnp.sum(before_ds * st_ref[block_state].astype(f32), axis=0, keepdims=True) * fade
            products[3 * T : 3 * T + HEADS, :] = jnp.broadcast_to(through, (HEADS, width)).astype(bf16)
            dstate[...] = fade * before_ds + mm(c_t, dyeb[...])
            by_head = mm(pick_t[...], products[...], NT)
            inside = pieces(turn[...] + by_head[:, :T], 2)
            outside = pieces(by_head[:, T : 2 * T], 2)
            reached = mm(jnp.concatenate([inside, outside], axis=1), reach_ref[...])
            reached = reached + jnp.broadcast_to(by_head[:, 3 * T : 3 * T + 1], (HEADS, T))
            d_raw = (head_t[1] * reached + by_head[:, 2 * T : 3 * T]) * sigmoid(raw_t)
            d_ref[rows, wide:] = columns_of(d_raw).astype(bf16)
            hacc[0] += d_raw
            hacc[1] += dt_t * reached
            dxh[T : T + 8, :] = dxh[0:8, :]
            if sub == 1:
                @pl.when(tick == 0)
                def _():
                    for way in (0, 1):
                        hop(1, way, 0).start()

                ring_poll(1, tick)
        return 0

    lax.fori_loop(0, 2, work, 0)

    @pl.when(step == steps // 2 - 1)
    def _():
        total = lambda a: jnp.sum(a, axis=0, keepdims=True)
        for k in range(CONV + 1):
            small_ref[k : k + 1, :] = total(acc[k])
        small_ref[CONV + 1 : CONV + 2, :width] = total(gate_ref[...])
        small_ref[CONV + 1 : CONV + 2, width : width + LANES] = total(columns_of(hacc[0]))
        small_ref[CONV + 1 : CONV + 2, width + LANES :] = total(columns_of(hacc[1])) * head_ref[1:2, :]
        small_ref[CONV + 2 :, :] = jnp.zeros((2, wide), f32)
        skip = mm_exact(acc[CONV + 1, :, :width], pick_ref[...].astype(f32))
        small_ref[CONV + 3 : CONV + 4, 512 : 512 + LANES] = total(skip)
        for part in (0, 1):
            over_copy(part).wait_recv()

            def some(i, _, part=part):
                at = span(part * half + i * 32, 32)
                here = span(i * 32, 32)
                total = held[1, part, here, :].astype(f32) + over_slot[part, here, :].astype(f32)
                obranch_ref[at, :] = total.astype(bf16)
                return 0

            lax.fori_loop(0, half // 32, some, 0)
        for part in (0, 1):
            over_copy(part).wait_send()
            for turned in (0, 1):
                near_copy(turned, part).wait_send()
        for h in range(n - 1):
            for k in (0, 1):
                for way in (0, 1):
                    hop(k, way, h).wait_send()


def ssd_backward(n, dy, v, xc, dr, st, gate, taps, head, chan, early, branch):
    length, width = dy.shape
    wide = width + 2 * NS
    tall = 2 * ROWS
    steps = length // tall
    subs = tall // T
    own_rows, tokens = D // n, length // 4
    half = tokens // 2
    row = lambda m: pl.BlockSpec((tall, m), lambda i: (steps - 1 - i, 0))
    whole = lambda a: pl.BlockSpec(a.shape, lambda i: (0,) * a.ndim, pipeline_mode=pl.Buffered(1))
    fixed = lambda *shape: pl.BlockSpec(shape, lambda i: (0,) * len(shape))
    anywhere = pl.BlockSpec(memory_space=pl.ANY)
    vm, dma = pltpu.VMEM, pltpu.SemaphoreType.DMA
    return pl.pallas_call(
        functools.partial(backward_body, n, own_rows, tokens, width),
        grid=(steps,),
        in_specs=[
            row(width), row(wide), row(wide), row(LANES),
            pl.BlockSpec((subs, NS, width), lambda i: (steps - 1 - i, 0, 0)),
            whole(gate), whole(taps), whole(head), whole(chan), anywhere, anywhere,
        ],
        out_specs=[
            row(wide + LANES), fixed(8, wide), fixed(own_rows, 2 * width), fixed(tokens, D),
        ],
        out_shape=[
            jax.ShapeDtypeStruct((length, wide + LANES), bf16),
            jax.ShapeDtypeStruct((8, wide), f32),
            jax.ShapeDtypeStruct((own_rows, 2 * width), f32),
            jax.ShapeDtypeStruct((tokens, D), bf16),
        ],
        scratch_shapes=[
            vm((T + 8, wide), f32), vm((NS, width), f32), vm((T, width), f32), vm((T, width), f32),
            vm((T, width), bf16), vm((T, width), bf16), vm((3 * T + HEADS, width), bf16),
            vm((HEADS, T), f32), vm((CONV + 2, 8, wide), f32), vm((2, HEADS, T), f32),
            vm((width, LANES), bf16), vm((HEADS, width), bf16), vm((8, width), f32), vm((2, HEADS, LANES), f32),
            vm((3 * T, LANES), bf16), vm((4 * T, LANES), bf16),
            vm((D, 2 * width), bf16),
            [[vm((n - 1, size, width), bf16) for _ in (0, 1)] for _, size in cut_rows(own_rows)],
            vm((2, 2, half, D), bf16), vm((2, 2, half, D), bf16), vm((2, half, D), bf16),
            dma((5,)), dma((2, 2, n - 1)), dma((2, 2, n - 1)), dma((2, 2)), dma((2, 2)), dma((2,)), dma((2,)),
        ],
        compiler_params=pltpu.CompilerParams(
            collective_id=3, has_side_effects=True, vmem_limit_bytes=ROOM
        ),
        name="layer_backward",
    )(dy, v, xc, dr, st, gate, taps, head, chan, early, branch)


def reduce_body(
    n, rows, tokens, starts,
    xg_ref, d_ref, dz_ref, wp_ref, w_ref, small_ref, flat_ref, gain_ref,
    oxs_ref, oback_ref, bc_ref, oflat_ref,
    xg, d, dz, wz, w, work, grads, slots, staged, near, over, smalls, tens, bc_slot,
    load_sem, ring_send, ring_recv, near_send, near_recv, over_send, over_recv,
    small_send, small_recv, ten_send, ten_recv, bc_send, bc_recv,
):
    pos, ring, me, across, beside = neighbours(n)
    cuts = cut_rows(rows)
    core = lax.rem(me, 2)
    opposite = lax.rem(me + 2, 4)
    next_door = me + 1 - 2 * core
    far = lax.rem(next_door + 2, 4)
    half = tokens // 2
    late = d.shape[1]
    width = dz.shape[1]
    tile = 2 * LANES
    tiles = D // tile
    columns = [pl.ds(lo, hi - lo) for lo, hi in starts]
    sources = [(d_ref.at[:, columns[0]], d.at[:, columns[0]])]
    sources += [(xg_ref.at[:, pl.ds(i * tile, tile)], xg.at[:, pl.ds(i * tile, tile)]) for i in range(tiles)]
    sources += [(d_ref.at[:, some], d.at[:, some]) for some in columns[1:]]
    sources += [
        (dz_ref, dz), (w_ref, w), (wp_ref.at[:, pl.ds(width, width)], wz), (small_ref, smalls.at[pos]),
    ]
    loads = [pltpu.make_async_copy(src, dst, load_sem.at[k]) for k, (src, dst) in enumerate(sources)]
    for load in loads:
        load.start()
    askew = {"tensor": far}
    enter((*ring, across, beside, askew))
    started = []

    def go(*args):
        copy = remote(*args)
        copy.start()
        started.append(copy)

    def block_at(way, count):
        return ring_index(lax.rem(pos + (count if way else n - count), n), n)

    def hop(k, way, h):
        lo, hi = starts[k]
        first, size = cuts[way]
        if h == 0:
            src = grads.at[span(block_at(way, 1) * rows + first, size), pl.ds(lo, hi - lo)]
        else:
            src = slots[way][k].at[h - 1]
        return remote(
            src, slots[way][k].at[h], ring_send.at[way, k, h], ring_recv.at[way, k, h], ring[way]
        )

    def product(k):
        lo, hi = starts[k]

        def some(i, _):
            at = pl.ds(pl.multiple_of(i * tile, tile), tile)
            if k == 0:
                pltpu.make_async_copy(xg_ref.at[:, at], xg.at[:, at], load_sem.at[1 + i]).wait()
            grads[at, lo:hi] = mm(xg[:, at], d[:, lo:hi], TN).astype(bf16)
            return 0

        loads[0 if k == 0 else tiles + k].wait()
        lax.fori_loop(0, tiles, some, 0)
        for way in (0, 1):
            hop(k, way, 0).start()

    def near_copy(turned, part):
        return remote(
            staged.at[turned, part], near.at[turned, part],
            near_send.at[turned, part], near_recv.at[turned, part], beside,
        )

    def over_copy(part):
        return remote(near.at[0, part], over.at[part], over_send.at[part], over_recv.at[part], across)

    def ring_turn(k, h):
        lo, hi = starts[k]
        for way in (0, 1):
            first, size = cuts[way]
            slot = slots[way][k].at[h]
            remote(slot, slot, ring_send.at[way, k, h], ring_recv.at[way, k, h], ring[way]).wait_recv()
            block = block_at(way, 2 + h) if h < n - 2 else block_at(way, 0)

            tile = strip(size)

            def some(i, _, way=way, first=first, block=block, tile=tile):
                came = slots[way][k][h, span(i * tile, tile), :]
                mine = grads[span(block * rows + first + i * tile, tile), lo:hi]
                if h < n - 2:
                    slots[way][k][h, span(i * tile, tile), :] = came + mine
                else:
                    oxs_ref[span(first + i * tile, tile), lo:hi] = came.astype(f32) + mine.astype(f32)
                return 0

            lax.fori_loop(0, size // tile, some, 0)
            if h < n - 2:
                hop(k, way, h + 1).start()

    def small_hop(way, h):
        here = smalls.at[lax.rem(pos + (h if way else n - h), n)]
        go(here, here, small_send.at[way, h], small_recv.at[way, h], ring[way])

    def small_lands(way, h):
        here = smalls.at[lax.rem(pos + (h + 1 if way else n - h - 1), n)]
        remote(here, here, small_send.at[way, h], small_recv.at[way, h], ring[way]).wait_recv()

    for k in range(len(starts)):
        product(k)
    for load in loads[tiles + len(starts) :]:
        load.wait()
    turns = {0: [(0, 0)], 1: [(1, 0), (2, 0)], 2: [(0, 1)], 3: [(1, 1), (2, 1)], 4: [(0, 2)], 5: [(1, 2), (2, 2)], 6: [(0, 3)], 7: [(1, 3), (2, 3)]}
    taken = [sum(k == group for some in turns.values() for k, _ in some) for group in range(len(starts))]

    def block(i, _):
        which, part = lax.div(i, 2), lax.rem(i, 2)
        own = lax.rem(which, 2)
        turned = lax.div(which, 2)
        target = lax.rem(next_door + own * (me - next_door) + 2 * (1 - turned), 4)
        at = span(target * tokens + part * half, half)
        total = mm(dz[at, :], wz[...], NT) + mm(d[at, :], w[...], NT)
        work[...] = total

        @pl.when(own == 0)
        def _():
            staged[turned, part] = work[...].astype(bf16)
            near_copy(turned, part).start()

        @pl.when(own == 1)
        def _():
            near_copy(turned, part).wait_recv()

        @pl.when(which == 1)
        def _():
            near[0, part] = (work[...] + near[0, part].astype(f32)).astype(bf16)
            over_copy(part).start()

        @pl.when(which == 3)
        def _():
            near[1, part] = (work[...] + near[1, part].astype(f32)).astype(bf16)

        for at_block, some in turns.items():

            @pl.when(i == at_block)
            def _(some=some):
                for k, h in some:
                    ring_turn(k, h)

        return 0

    lax.fori_loop(0, 8, block, 0)
    for i in range(tiles):
        share = jnp.zeros((tile, LANES), f32)
        for c in range(late // LANES):
            cols = slice(c * LANES, (c + 1) * LANES)
            at = slice(i * tile, (i + 1) * tile)
            share = share + grads[at, cols].astype(f32) * w[at, cols].astype(f32)
        total = mm_exact(jnp.ones((8, LANES), f32), share, NT)[0:1] + gain_ref[0:1, i * tile : (i + 1) * tile]
        for c in range(2 * i, 2 * i + 2):
            row, col = 6 + c // 8, (c % 8) * LANES
            part = total[:, (c - 2 * i) * LANES : (c - 2 * i + 1) * LANES]
            smalls[pos, row : row + 1, col : col + LANES] = part / flat_ref[c : c + 1, :]

    rest = [(k, h) for h in range(n - 1) for k in (0, 1, 2) if h >= taken[k]]
    rest.sort(key=lambda turn: turn[1] - taken[turn[0]])

    def small_step(s):
        for way in (0, 1):
            if s > 0 and (way == 0 or s < n // 2):
                small_lands(way, s - 1)
            if s < n // 2 - way:
                small_hop(way, s)

    small_step(0)
    steps_done = 1
    for at, (k, h) in enumerate(rest):
        ring_turn(k, h)
        if (k, h) == (0, n - 2):
            bc_slot[0] = oxs_ref[:, starts[0][0] : starts[0][0] + 2 * NS]
            go(bc_slot.at[0], bc_slot.at[1], bc_send.at[0], bc_recv.at[0], beside)
        if at % 2 == 1 and steps_done < n // 2:
            small_step(steps_done)
            steps_done += 1
    for s in range(steps_done, n // 2):
        small_step(s)
    small_lands(0, n // 2 - 1)

    total = smalls[0]
    for i in range(1, n):
        total = total + smalls[i]
    tens[me] = total
    others = ((beside, next_door), (across, opposite), (askew, far))
    for k, (peer, _) in enumerate(others):
        go(tens.at[me], tens.at[me], ten_send.at[k], ten_recv.at[k], peer)
    remote(bc_slot.at[1], bc_slot.at[1], bc_send.at[0], bc_recv.at[0], beside).wait_recv()
    bc_slot[2] = bc_slot[0] + bc_slot[1]
    go(bc_slot.at[2], bc_slot.at[3], bc_send.at[1], bc_recv.at[1], across)
    for part in (0, 1):
        over_copy(part).wait_recv()

        def some(i, _, part=part):
            at = span(part * half + i * 32, 32)
            here = span(i * 32, 32)
            oback_ref[at, :] = (near[1, part, here, :].astype(f32) + over[part, here, :].astype(f32)).astype(bf16)
            return 0

        lax.fori_loop(0, half // 32, some, 0)
    for k, (peer, target) in enumerate(others):
        here = tens.at[target]
        remote(here, here, ten_send.at[k], ten_recv.at[k], peer).wait_recv()
    flat_gradients(width, tens, oflat_ref)
    remote(bc_slot.at[3], bc_slot.at[3], bc_send.at[1], bc_recv.at[1], across).wait_recv()
    bc_ref[...] = bc_slot[2] + bc_slot[3]
    for part in (0, 1):
        over_copy(part).wait_send()
        for turned in (0, 1):
            near_copy(turned, part).wait_send()
    for k in range(len(starts)):
        for way in (0, 1):
            for h in range(n - 1):
                hop(k, way, h).wait_send()
    for copy in started:
        copy.wait_send()


def flat_gradients(width, tens, out_ref):
    pairs = width // LANES
    heads = width // P_SIZE

    def sums(row, col):
        total = tens[0, row : row + 1, col : col + LANES]
        for t in range(1, 4):
            total = total + tens[t, row : row + 1, col : col + LANES]
        return total

    def put(row, value):
        out_ref[row : row + 1, :] = value

    for c in range(D // LANES):
        put(c, sums(6 + c // 8, (c % 8) * LANES))
    for t in range(4):
        for c in range(pairs):
            cols = slice(c * LANES, (c + 1) * LANES)
            put(GATE_ROW + pairs * t + c, tens[t, CONV + 1 : CONV + 2, cols])
            put(BIAS_ROW + pairs * t + c, tens[t, CONV : CONV + 1, cols])
            for k in range(CONV):
                put(TAPS_ROW + 4 * pairs * k + pairs * t + c, tens[t, k : k + 1, cols])
    for c in range(2):
        put(BIAS_BC_ROW + c, sums(CONV, width + c * LANES))
        for k in range(CONV):
            put(TAPS_BC_ROW + 2 * k + c, sums(k, width + c * LANES))
    kinds = ((CONV + 1, width), (CONV + 1, width + LANES), (CONV + 3, 512))
    rows = [tens[t, row : row + 1, col : col + LANES] for row, col in kinds for t in range(4)]
    rows = jnp.concatenate(rows + [jnp.zeros((16 - len(rows), LANES), f32)], axis=0)
    lane = lax.broadcasted_iota(jnp.int32, (LANES, 2 * LANES), 1)
    entry = lax.broadcasted_iota(jnp.int32, (LANES, 2 * LANES), 0)
    spread_out = mm_exact(rows, jnp.where(lax.rem(lane, heads) == entry, 1.0, 0.0).astype(f32))
    at = lax.broadcasted_iota(jnp.int32, (16, 2 * LANES), 1)
    source = lax.broadcasted_iota(jnp.int32, (16, 2 * LANES), 0)
    line = jnp.sum(jnp.where(lax.div(at, heads) == source, spread_out, 0.0), axis=0, keepdims=True)
    put(HEAD_ROW, line[:, :LANES])
    put(HEAD_ROW + 1, line[:, LANES:])


def reduce_all(n, xg, d, dz, wp, w, small, flat, gain):
    rows, tokens = D // n, dz.shape[0] // 4
    width, late = dz.shape[1], d.shape[1]
    starts = ((width, late), (0, width // 2), (width // 2, width))
    half = tokens // 2
    dma, vm = pltpu.SemaphoreType.DMA, pltpu.VMEM
    anywhere = pl.BlockSpec(memory_space=pl.ANY)
    inside = pl.BlockSpec(memory_space=pltpu.VMEM)
    return pl.pallas_call(
        functools.partial(reduce_body, n, rows, tokens, starts),
        in_specs=[anywhere] * 6 + [inside] * 2,
        out_specs=[inside] * 4,
        out_shape=[
            jax.ShapeDtypeStruct((rows, late), f32),
            jax.ShapeDtypeStruct((tokens, D), bf16),
            jax.ShapeDtypeStruct((rows, 2 * NS), f32),
            jax.ShapeDtypeStruct((FLAT_ROWS, LANES), f32),
        ],
        scratch_shapes=[
            vm(xg.shape, bf16), vm(d.shape, bf16), vm(dz.shape, bf16), vm((D, width), bf16),
            vm((D, late), bf16),
            vm((half, D), f32), vm((D, late), bf16),
            [[vm((n - 1, size, hi - lo), bf16) for lo, hi in starts] for _, size in cut_rows(rows)],
            vm((2, 2, half, D), bf16), vm((2, 2, half, D), bf16), vm((2, half, D), bf16),
            vm((n, *small.shape), f32), vm((4, *small.shape), f32), vm((4, rows, 2 * NS), f32),
            dma((13,)), dma((2, 3, n - 1)), dma((2, 3, n - 1)), dma((2, 2)), dma((2, 2)), dma((2,)), dma((2,)),
            dma((2, n // 2)), dma((2, n // 2)), dma((3,)), dma((3,)), dma((2,)), dma((2,)),
        ],
        compiler_params=pltpu.CompilerParams(
            collective_id=1, has_side_effects=True, vmem_limit_bytes=ROOM
        ),
        name="reduce_all",
    )(xg, d, dz, wp, w, small, flat, gain)


def adamw_step(weight, first, second, grad, rate, decay):
    first_new = beta_first * first + (1.0 - beta_first) * grad
    second_new = beta_second * second + (1.0 - beta_second) * grad * grad
    hat_first = first_new * (1.0 / (1.0 - beta_first**STEP))
    hat_second = second_new * (1.0 / (1.0 - beta_second**STEP))
    weight_new = weight - rate * (hat_first / (jnp.sqrt(hat_second) + adam_eps) + decay * weight)
    return (weight_new, first_new, second_new)


def finish_body(
    width, heads,
    in_ref, cot_ref, branch_ref, back_ref, flat_ref, early_ref, late_ref, bcg_ref,
    zx_ref, zx1_ref, zx2_ref, bc_ref, bc1_ref, bc2_ref, out_ref, out1_ref, out2_ref, late_all_ref, dt_ref, dt1_ref, dt2_ref,
    layer_ref, grad_ref, zxn_ref, zx1n_ref, zx2n_ref, bcn_ref, bc1n_ref, bc2n_ref,
    outn_ref, out1n_ref, out2n_ref, dtn_ref, dt1n_ref, dt2n_ref,
):
    def update(refs, news, grad):
        fresh = adamw_step(*(ref[...] for ref in refs), grad, matrix_rate, matrix_decay)
        for ref, value in zip(news, fresh):
            ref[...] = value

    for k, grad in ((0, early_ref), (1, late_ref)):
        fresh = adamw_step(
            *(ref[:, k, :] for ref in (zx_ref, zx1_ref, zx2_ref)), grad[:, :width], matrix_rate, matrix_decay
        )
        for ref, value in zip((zxn_ref, zx1n_ref, zx2n_ref), fresh):
            ref[:, k, :] = value
    update((bc_ref, bc1_ref, bc2_ref), (bcn_ref, bc1n_ref, bc2n_ref), bcg_ref[...])
    update((out_ref, out1_ref, out2_ref), (outn_ref, out1n_ref, out2n_ref), early_ref[:, width:])

    @pl.when(pl.program_id(0) == 0)
    def _():
        unit = jnp.where(
            lax.broadcasted_iota(jnp.int32, (16, LANES), 0) == lax.broadcasted_iota(jnp.int32, (16, LANES), 1), 1.0, 0.0
        ).astype(f32)
        turned = mm_exact(unit, late_all_ref[:, width + 2 * NS :], NT)
        update((dt_ref, dt1_ref, dt2_ref), (dtn_ref, dt1n_ref, dt2n_ref), turned[:heads])

    rows = in_ref.shape[0]
    tile = 64

    def some(i, _):
        at = span(i * tile, tile)
        squares = jnp.zeros((tile, LANES), f32)
        inner = jnp.zeros((tile, LANES), f32)
        for c in range(D // LANES):
            cols = slice(c * LANES, (c + 1) * LANES)
            x = in_ref[at, cols].astype(f32)
            squares = squares + x * x
            inner = inner + x * flat_ref[c : c + 1, :] * back_ref[at, cols].astype(f32)
        r = lax.rsqrt(jnp.sum(squares, axis=-1, keepdims=True) / D + norm_eps)
        k = r * r * r * jnp.sum(inner, axis=-1, keepdims=True) / D
        r, k = jnp.broadcast_to(r, (tile, LANES)), jnp.broadcast_to(k, (tile, LANES))
        for c in range(D // LANES):
            cols = slice(c * LANES, (c + 1) * LANES)
            x = in_ref[at, cols].astype(f32)
            layer_ref[at, cols] = (x + branch_ref[at, cols].astype(f32)).astype(bf16)
            back = back_ref[at, cols].astype(f32)
            grad_ref[at, cols] = cot_ref[at, cols].astype(f32) + r * flat_ref[c : c + 1, :] * back - x * k
        return 0

    lax.fori_loop(0, rows // tile, some, 0)


def finish(layer_input, out_grad, branch, back, flat, early, late, bcg, zx, bc, out, dt):
    (rows, width), heads = out[0].shape, dt[0].shape[0]
    steps = 2
    part = lambda a: pl.BlockSpec((a.shape[0] // steps, *a.shape[1:]), lambda i: (i,) + (0,) * (a.ndim - 1))
    whole = lambda a: pl.BlockSpec(a.shape, lambda i: (0,) * a.ndim)
    like = lambda a, dtype=f32: jax.ShapeDtypeStruct(a.shape, dtype)
    weights = (*zx, *bc, *out)
    return pl.pallas_call(
        functools.partial(finish_body, width, heads),
        grid=(steps,),
        in_specs=[
            *(part(a) for a in (layer_input, out_grad, branch, back)), whole(flat),
            *(part(a) for a in (early, late, bcg, *weights)), whole(late), *(whole(a) for a in dt),
        ],
        out_specs=[part(layer_input), part(back), *(part(a) for a in weights), *(whole(a) for a in dt)],
        out_shape=[like(layer_input, bf16), like(layer_input), *(like(a) for a in weights), *(like(a) for a in dt)],
        compiler_params=pltpu.CompilerParams(vmem_limit_bytes=ROOM),
        name="finish",
    )(layer_input, out_grad, branch, back, flat, early, late, bcg, *weights, late, *dt)


def local(
    layer_input,
    out_grad,
    small_params,
    small_first,
    small_second,
    w_zx,
    zx_first,
    zx_second,
    w_bc,
    bc_first,
    bc_second,
    w_dt,
    dt_first,
    dt_second,
    w_out,
    out_first,
    out_second,
):
    n = lax.axis_size("dp")
    flat = jnp.pad(small_params, (0, FLAT_ROWS * LANES - small_params.shape[0])).reshape(FLAT_ROWS, LANES)
    v, xc, dr, st, dy, dz, branch, early, gate, gain, xg, w_all, pair_all, taps, head, chan = ssd_forward(
        n, layer_input, out_grad, flat, w_zx, w_bc, w_dt.T, w_out
    )
    d_late, small, owner_early, own_branch = ssd_backward(
        n, dy, v, xc, dr, st, gate, taps, head, chan, early, branch
    )
    owner_late, d_normed_in, owner_bc, flat_grad = reduce_all(
        n, xg, d_late, dz, pair_all, w_all, small, flat, gain
    )
    small_grad = flat_grad.reshape(-1)[: small_params.shape[0]]
    small_new, small_first_new, small_second_new = adamw_step(
        small_params, small_first, small_second, small_grad, small_rate, 0.0
    )
    (
        layer_output, input_grad, zx_new, zx_first_new, zx_second_new, bc_new, bc_first_new, bc_second_new,
        out_new, out_first_new, out_second_new, dt_new, dt_first_new, dt_second_new,
    ) = finish(
        layer_input, out_grad, own_branch, d_normed_in, flat, owner_early, owner_late, owner_bc,
        (w_zx, zx_first, zx_second), (w_bc, bc_first, bc_second), (w_out, out_first, out_second),
        (w_dt.T, dt_first.T, dt_second.T),
    )
    dt_new, dt_first_new, dt_second_new = dt_new.T, dt_first_new.T, dt_second_new.T
    return (
        layer_output,
        input_grad,
        small_new,
        small_first_new,
        small_second_new,
        zx_new,
        zx_first_new,
        zx_second_new,
        bc_new,
        bc_first_new,
        bc_second_new,
        dt_new,
        dt_first_new,
        dt_second_new,
        out_new,
        out_first_new,
        out_second_new,
    )


def solution(mesh):
    return jax.shard_map(
        local,
        mesh=mesh,
        in_specs=(
            P(("dp", "tensor"), None),
            P(("dp", "tensor"), None),
            P(),
            P(),
            P(),
            P("dp", None, "tensor"),
            P("dp", None, "tensor"),
            P("dp", None, "tensor"),
            P("dp", None),
            P("dp", None),
            P("dp", None),
            P("dp", "tensor"),
            P("dp", "tensor"),
            P("dp", "tensor"),
            P("dp", "tensor"),
            P("dp", "tensor"),
            P("dp", "tensor"),
        ),
        out_specs=(
            P(("dp", "tensor"), None),
            P(("dp", "tensor"), None),
            P(),
            P(),
            P(),
            P("dp", None, "tensor"),
            P("dp", None, "tensor"),
            P("dp", None, "tensor"),
            P("dp", None),
            P("dp", None),
            P("dp", None),
            P("dp", "tensor"),
            P("dp", "tensor"),
            P("dp", "tensor"),
            P("dp", "tensor"),
            P("dp", "tensor"),
            P("dp", "tensor"),
        ),
        check_vma=False,
    )
```

```python
import functools

import jax
import jax.numpy as jnp
from jax import lax
from jax.experimental import pallas as pl
from jax.experimental.pallas import tpu as pltpu
from jax.sharding import PartitionSpec as P

D = 1536
DI = 3072
H = 48
NS = 128
P_SIZE = 64
CONV = 4
LEN = 2048
STEP = 10

T = 128
ROWS = 256
LANES = 128
ROOM = 60 * 2**20

norm_eps = 1e-05
adam_eps = 1e-08
beta_first = 0.9
beta_second = 0.95
matrix_rate = 0.01
small_rate = 0.1
matrix_decay = 0.1

f32 = jnp.float32
bf16 = jnp.bfloat16
NN = (((1,), (0,)), ((), ()))
NT = (((1,), (1,)), ((), ()))
TN = (((0,), (0,)), ((), ()))
HIGHEST = lax.Precision.HIGHEST


GATE_ROW, TAPS_ROW, BIAS_ROW, TAPS_BC_ROW, BIAS_BC_ROW, HEAD_ROW, FLAT_ROWS = 12, 36, 132, 156, 164, 166, 168


def mm(a, b, dims=NN):
    return lax.dot_general(a, b, dims, preferred_element_type=f32)


def mm_exact(a, b, dims=NN):
    return lax.dot_general(a, b, dims, preferred_element_type=f32, precision=HIGHEST)


def sigmoid(v):
    return 0.5 * jnp.tanh(0.5 * v) + 0.5


def softplus(v):
    return jnp.maximum(v, 0.0) + jnp.log1p(jnp.exp(-jnp.abs(v)))


def spread(col):
    return jnp.broadcast_to(col, (T, LANES))


def block_iota(axis):
    return lax.broadcasted_iota(jnp.int32, (T, LANES), axis)


HEADS = 16
LOG2_E = 1.4426950408889634


def pieces(value, count):
    parts = []
    for k in range(count):
        part = value.astype(bf16)
        parts.append(part)
        if k < count - 1:
            value = value - part.astype(f32)
    return jnp.concatenate(parts, axis=1)


def columns_of(rows):
    return jnp.concatenate([rows, jnp.zeros((LANES - HEADS, T), f32)], axis=0).T


def set_heads(head_ref, head_t, until):
    turned = jnp.concatenate([head_ref[...], jnp.zeros((LANES - 8, LANES), f32)], axis=0).T
    head_t[0] = spread(turned[:, 0:1])[:HEADS]
    head_t[1] = spread(turned[:, 1:2])[:HEADS]
    matrix = jnp.where(block_iota(0) <= block_iota(1), 1.0, 0.0).astype(bf16)
    for k in range(3):
        until[k * T : (k + 1) * T, :] = matrix


def head_rows(dr_ref, head_t, until, rows):
    raw = dr_ref[rows, :].T[:HEADS] + head_t[0]
    dt = softplus(raw)
    decay = mm(pieces(dt * (head_t[1] * LOG2_E), 3), until[...])
    return raw, dt, decay, columns_of(dt), columns_of(decay)


def ring_place(n):
    me = lax.axis_index("dp")
    z, x = lax.div(me, 2), lax.rem(me, 2)
    return z + x * (n - 1 - 2 * z)


def ring_index(pos, n):
    back = lax.div(pos, n // 2)
    return 2 * pos + back * (2 * n - 1 - 4 * pos)


def neighbours(n):
    pos = ring_place(n)
    right = ring_index(lax.rem(pos + 1, n), n)
    left = ring_index(lax.rem(pos + n - 1, n), n)
    me = lax.axis_index("tensor")
    y, core = lax.div(me, 2), lax.rem(me, 2)
    across = 2 * (1 - y) + core
    beside = 2 * y + 1 - core
    return pos, ({"dp": right}, {"dp": left}), me, {"tensor": across}, {"tensor": beside}


def greet(peers):
    barrier = pltpu.get_barrier_semaphore()
    for peer in peers:
        pl.semaphore_signal(barrier, inc=1, device_id=peer, device_id_type=pl.DeviceIdType.MESH)


def enter(peers):
    greet(peers)
    pl.semaphore_wait(pltpu.get_barrier_semaphore(), len(peers))


def remote(src, dst, send_sem, recv_sem, peer):
    return pltpu.make_async_remote_copy(
        src_ref=src, dst_ref=dst, send_sem=send_sem, recv_sem=recv_sem,
        device_id=peer, device_id_type=pl.DeviceIdType.MESH,
    )


def span(start, size):
    return pl.ds(pl.multiple_of(start, 16), size)


def strip(rows):
    return next(size for size in (48, 32, 16) if rows % size == 0)


def cut_rows(rows):
    top = rows // 32 * 16
    return ((0, top), (top, rows - top))


def forward_body(
    n, rows, tokens, width,
    in_ref, cot_ref, flat_ref, wzx_ref, wbc_ref, wdt_ref, wout_ref,
    v_ref, xc_ref, dr_ref, st_ref, dy_ref, dz_ref, branch_ref, early_ref, gate_ref, gain_ref,
    xg_ref, ws_ref, wps_ref, taps_ref, head_ref, chan_ref,
    halo, state, y_all, z_all, dn_all, nl_all, dz_all, xg, cots, ws, wps, sums, red, head_t, until, across_state, tails,
    own_keep, early_keep, lead_keep, lead_send, lead_recv, x_keep, x_over_send, x_over_recv, x_side_send, x_side_recv,
    x_pass_send, x_pass_recv, ring_keep, ring_send, ring_recv, over_send, over_recv,
    side_send, side_recv, pass_send, pass_recv, sum_send, sum_recv,
):
    pairs = width // LANES
    wide = width + 2 * NS
    step = pl.program_id(0)
    steps = LEN // ROWS
    tall = 2 * ROWS
    norming = steps // 2
    gating = norming + 1
    forming = gating + 1
    products = forming + steps // 2
    pos, ring, me, across, beside = neighbours(n)
    opposite = lax.rem(me + 2, 4)
    next_door = me + 1 - 2 * lax.rem(me, 2)
    far = lax.rem(next_door + 2, 4)
    askew = {"tensor": far}
    quarter = tokens // 4
    hops = n // 2
    cuts = cut_rows(rows)
    mine = ring_index(pos, n)

    late = wide + LANES
    parts_of = ((0, width), (width, width))

    def hop(k, part, way, h):
        first, size = cuts[part]
        cols = pl.ds(*parts_of[k])
        block = ring_index(lax.rem(pos + (h if way else n - h), n), n)
        here = wps.at[span(block * rows + first, size), cols]
        return remote(here, here, ring_send.at[way, part, k, h], ring_recv.at[way, part, k, h], ring[way])

    def hop_lands(k, part, way, h):
        first, size = cuts[part]
        block = ring_index(lax.rem(pos + (h + 1 if way else n - h - 1), n), n)
        return span(block * rows + first, size), pl.ds(*parts_of[k])

    def hop_arrival(k, part, way, h):
        here = wps.at[hop_lands(k, part, way, h)]
        return remote(here, here, ring_send.at[way, part, k, h], ring_recv.at[way, part, k, h], ring[way])

    def hop_keep(part, way, h):
        at = hop_lands(1, part, way, h)
        return pltpu.make_async_copy(wps.at[at], wps_ref.at[at], ring_keep.at[way, part, h])

    def hop_ways(h):
        return [(part, way) for part in (0, 1) for way in (0, 1) if h < hops - 1 or part == way]

    def hop_on(k, h):
        for part, way in hop_ways(h - 1) if h > 0 else ():
            hop_arrival(k, part, way, h - 1).wait_recv()
            if k == 1:
                hop_keep(part, way, h - 1).start()
            if h < hops and (part, way) in hop_ways(h):
                hop(k, part, way, h).start()
        if h == 0:
            for part, way in hop_ways(0):
                hop(k, part, way, 0).start()

    def over(k):
        return remote(
            cot_ref.at[pl.ds(k * quarter, quarter)], cots.at[span(me * tokens + k * quarter, quarter)],
            over_send.at[k], over_recv.at[k], across,
        )

    def landed(start, size, send, recv, peer):
        here = cots.at[span(start, size)]
        return remote(here, here, send, recv, peer)

    def over_arrival(k):
        return landed(opposite * tokens + k * quarter, quarter, over_send.at[k], over_recv.at[k], across)

    def passing(k):
        return landed(opposite * tokens + k * quarter, quarter, pass_send.at[k], pass_recv.at[k], beside)

    def pass_arrival(k):
        return landed(far * tokens + k * quarter, quarter, pass_send.at[k], pass_recv.at[k], beside)

    def side():
        return remote(cot_ref, cots.at[span(me * tokens, tokens)], side_send.at[0], side_recv.at[0], beside)

    def side_arrival():
        return landed(next_door * tokens, tokens, side_send.at[0], side_recv.at[0], beside)

    def own_cot():
        return pltpu.make_async_copy(cot_ref, cots.at[span(me * tokens, tokens)], own_keep.at[0])

    def own_z():
        at = span(mine * rows, rows), pl.ds(*parts_of[1])
        return pltpu.make_async_copy(wps.at[at], wps_ref.at[at], own_keep.at[1])

    def pass_on(*pieces):
        for k in pieces:
            over_arrival(k).wait_recv()
            passing(k).start()

    def normalize(k):
        def some(i, _):
            at = span(me * tokens + k * quarter + i * 64, 64)
            squares = jnp.zeros((64, LANES), f32)
            for c in range(D // LANES):
                x = xg[at, c * LANES : (c + 1) * LANES].astype(f32)
                squares = squares + x * x
            inverse = lax.rsqrt(jnp.sum(squares, axis=-1, keepdims=True) / D + norm_eps)
            inverse = jnp.broadcast_to(inverse, (64, LANES))
            for c in range(D // LANES):
                cols = slice(c * LANES, (c + 1) * LANES)
                xg[at, cols] = (xg[at, cols].astype(f32) * inverse * flat_ref[c : c + 1, :]).astype(bf16)
            return 0

        lax.fori_loop(0, quarter // 64, some, 0)

    @pl.when(step == 0)
    def _():
        own_rows = span(me * tokens, tokens)
        greet((*ring, across, beside, askew))
        load = pltpu.make_async_copy(in_ref, xg.at[own_rows], own_keep.at[2])
        load.start()
        own_cot().start()
        mine_at = span(mine * rows, rows)
        ws[mine_at, :width] = wzx_ref[:, 1, :].astype(bf16)
        ws[mine_at, width:wide] = wbc_ref[...].astype(bf16)
        heads = wdt_ref.shape[0]
        unit = jnp.where(
            lax.broadcasted_iota(jnp.int32, (16, LANES), 0) == lax.broadcasted_iota(jnp.int32, (16, LANES), 1), 1.0, 0.0
        ).astype(bf16)
        steps_w = jnp.concatenate([wdt_ref[...], jnp.zeros((16 - heads, rows), f32)], axis=0).astype(bf16)
        ws[mine_at, wide:] = mm(steps_w, unit, TN).astype(bf16)
        load.wait()
        normalize(0)
        pl.semaphore_wait(pltpu.get_barrier_semaphore(), 5)
        started, kept = [], []

        def go(*args):
            copy = remote(*args)
            copy.start()
            started.append(copy)

        def keep(src, dst, sem):
            copy = pltpu.make_async_copy(src, dst, sem)
            copy.start()
            kept.append(copy)

        def arrived(part, way, h, block):
            first, size = cuts[part]
            at = span(block * rows + first, size)
            remote(
                ws.at[at], ws.at[at], lead_send.at[way, part, h], lead_recv.at[way, part, h], ring[way]
            ).wait_recv()
            keep(ws.at[at], ws_ref.at[at], lead_keep.at[way, part, h])

        def lead(h, parts=(0, 1)):
            for part in parts:
                first, size = cuts[part]
                for way in (0, 1):
                    block = ring_index(lax.rem(pos + (h if way else n - h), n), n)
                    here = ws.at[span(block * rows + first, size)]
                    if h > 0:
                        arrived(part, way, h - 1, block)
                    if h == hops - 1 and part != way:
                        continue
                    go(here, here, lead_send.at[way, part, h], lead_recv.at[way, part, h], ring[way])

        def x_over(k):
            at = span(me * tokens + k * quarter, quarter)
            go(xg.at[at], xg.at[at], x_over_send.at[k], x_over_recv.at[k], across)

        def x_pass(k):
            at = span(opposite * tokens + k * quarter, quarter)
            here = xg.at[at]
            remote(here, here, x_over_send.at[k], x_over_recv.at[k], across).wait_recv()
            go(here, here, x_pass_send.at[k], x_pass_recv.at[k], beside)
            keep(here, xg_ref.at[at], x_keep.at[k])

        def x_pass_lands(k):
            at = span(far * tokens + k * quarter, quarter)
            remote(xg.at[at], xg.at[at], x_pass_send.at[k], x_pass_recv.at[k], beside).wait_recv()
            keep(xg.at[at], xg_ref.at[at], x_keep.at[4 + k])

        lead(0, (0,))
        leading = list(started)
        x_over(0)
        for k in (1, 2, 3):
            normalize(k)
            if k == 1:
                x_over(1)
        go(xg.at[own_rows], xg.at[own_rows], x_side_send.at[0], x_side_recv.at[0], beside)
        keep(xg.at[own_rows], xg_ref.at[own_rows], x_keep.at[8])
        wps[mine_at, :width] = wout_ref[...].astype(bf16)
        wps[mine_at, width:] = wzx_ref[:, 0, :].astype(bf16)
        for copy in leading:
            copy.wait_send()
            started.remove(copy)
        lead(0, (1,))
        keep(ws.at[mine_at], ws_ref.at[mine_at], x_keep.at[9])
        own_z().start()
        halo[0:8, :] = jnp.zeros((8, wide), f32)
        state[...] = jnp.zeros_like(state)
        gate_ref[...] = jnp.zeros_like(gate_ref)
        parameter_rows(me, width, flat_ref, taps_ref, head_ref, chan_ref)
        set_heads(head_ref, head_t, until)
        lead(1)
        x_over(2)
        at = span(next_door * tokens, tokens)
        remote(xg.at[at], xg.at[at], x_side_send.at[0], x_side_recv.at[0], beside).wait_recv()
        keep(xg.at[at], xg_ref.at[at], x_keep.at[10])
        side().start()
        lead(2)
        x_over(3)
        x_pass(0)
        x_pass(1)
        for h in range(3, hops):
            lead(h)
        hop_on(0, 0)
        x_pass(2)
        over(0).start()
        x_pass_lands(0)
        x_pass_lands(1)
        x_pass(3)
        for part in (0, 1):
            arrived(part, part, hops - 1, ring_index(lax.rem(pos + n // 2, n), n))
        hop_on(1, 0)
        over(1).start()
        x_pass_lands(2)
        x_pass_lands(3)
        for copy in kept:
            copy.wait()
        for copy in started:
            copy.wait_send()

    def at_tick(tick):
        for k, times in enumerate(((1, 4, 6), (2, 5, 7))):
            for h in range(1, min(hops, 4)):
                pl.when(tick == times[h - 1])(functools.partial(hop_on, k, h))

        @pl.when(tick == 2)
        def _():
            over(2).start()

        @pl.when(tick == 4)
        def _():
            over(3).start()
            pass_on(0, 1)

        pl.when(tick == steps - 1)(functools.partial(pass_on, 2))

    @pl.when(step < norming)
    def _():
        def chunk(i, _):
            tick = 2 * step + i
            at_tick(tick)
            scan_step(
                width, tick, i, xg, ws, taps_ref, head_ref, chan_ref,
                v_ref, xc_ref, dr_ref, st_ref, halo, state, y_all, head_t, until, across_state, tails,
                functools.partial(pass_on, 3),
            )
            return 0

        lax.fori_loop(0, 2, chunk, 0)

    @pl.when(step == norming)
    def _():
        for k in (0, 1):
            for h in range(4, hops):
                hop_on(k, h)
        hop_on(0, hops)
        side_arrival().wait_recv()
        for k in range(4):
            pass_arrival(k).wait_recv()
        own_cot().wait()
        own_z().wait()

        def some(i, _):
            at = span(i * tall, tall)
            dn_all[at, :] = mm(cots[at, :], wps[:, :width]).astype(bf16)
            return 0

        lax.fori_loop(0, LEN // tall, some, 0)

    @pl.when(step == gating)
    def _():
        hop_on(1, hops)
        ones = jnp.ones((8, LANES), f32)

        def some(i, _):
            at = span(i * tall, tall)
            z_all[at, :] = mm(xg[at, :], wps[:, width:])
            for sub in range(tall // T):
                rows_at = span(i * tall + sub * T, T)
                squares = jnp.zeros((T, LANES), f32)
                inner = jnp.zeros((T, LANES), f32)
                for p in range(pairs):
                    cols = slice(p * LANES, (p + 1) * LANES)
                    z = z_all[rows_at, cols]
                    gated = y_all[rows_at, cols] * (z * sigmoid(z))
                    squares = squares + gated * gated
                    inner = inner + gated * chan_ref[0:1, cols] * dn_all[rows_at, cols].astype(f32)
                lanes = pl.ds(pl.multiple_of(i * tall + sub * T, T), T)
                sums[me, 0:4, lanes] = mm_exact(ones, squares, NT)[0:4]
                sums[me, 4:8, lanes] = mm_exact(ones, inner, NT)[4:8]
            return 0

        lax.fori_loop(0, LEN // tall, some, 0)

    @pl.when(step == forming - 1)
    def _():
        peers = ((beside, next_door), (across, opposite), (askew, far))
        for k, (peer, _) in enumerate(peers):
            remote(sums.at[me], sums.at[me], sum_send.at[k], sum_recv.at[k], peer).start()
        for h in range(hops):
            for part, way in hop_ways(h):
                for k in (0, 1):
                    hop(k, part, way, h).wait_send()
                hop_keep(part, way, h).wait()
        side().wait_send()
        for k in range(4):
            over(k).wait_send()
            passing(k).wait_send()
        for k, (peer, other) in enumerate(peers):
            remote(sums.at[other], sums.at[other], sum_send.at[k], sum_recv.at[k], peer).wait()
        red[...] = ((sums[0] + sums[1]) + sums[2]) + sums[3]

    @pl.when((step >= forming) & (step < products))
    def _():
        def some(i, _):
            first = (step - forming) * tall + i * ROWS
            lanes = pl.ds(pl.multiple_of(first, ROWS), ROWS)
            q_row = lax.rsqrt(red[0:4, lanes] / DI + norm_eps)
            k_row = q_row * q_row * q_row * red[4:8, lanes] / DI
            turned = jnp.concatenate([q_row, k_row], axis=0).T
            for sub in range(ROWS // T):
                rows_at = slice(sub * T, (sub + 1) * T)
                at = span(first + sub * T, T)
                q, kk = spread(turned[rows_at, 0:1]), spread(turned[rows_at, 4:5])
                for p in range(pairs):
                    cols = slice(p * LANES, (p + 1) * LANES)
                    z, y, dn = z_all[at, cols], y_all[at, cols], dn_all[at, cols].astype(f32)
                    gain = chan_ref[0:1, cols]
                    s = sigmoid(z)
                    sz = z * s
                    gated = y * sz
                    gq = gated * q
                    dg = q * gain * dn - gated * kk
                    gate_ref[:, cols] += jnp.sum((gq * dn).reshape(T // 8, 8, LANES), axis=0)
                    nl_all[at, cols] = (gq * gain).astype(bf16)
                    dz_all[at, cols] = (dg * y * (s + sz * (1.0 - s))).astype(bf16)
                    dn_all[at, cols] = (dg * sz).astype(bf16)
            branch_ref[span(i * ROWS, ROWS), :] = mm(nl_all[span(first, ROWS), :], wps[:, :width], NT).astype(bf16)
            return 0

        lax.fori_loop(0, 2, some, 0, unroll=2)

    def rows_out():
        return [
            pltpu.make_async_copy(src, dst, own_keep.at[2 + k])
            for k, (src, dst) in enumerate(((dz_all, dz_ref), (dn_all, dy_ref)))
        ]

    def early_out(i):
        at = span(i * ROWS, ROWS)
        return [
            pltpu.make_async_copy(src.at[at, pl.ds(0, width)], early_ref.at[at, pl.ds(k * width, width)], early_keep.at[k, i])
            for k, src in enumerate((ws, wps))
        ]

    @pl.when(step == products)
    def _():
        for copy in rows_out():
            copy.start()

        def some(i, _):
            at = span(i * ROWS, ROWS)
            lanes = pl.ds(pl.multiple_of(i * ROWS, ROWS), ROWS)
            grad = mm(xg[:, lanes], dz_all[...], TN)
            ws[at, :width] = grad.astype(bf16)
            share = jnp.zeros((ROWS, LANES), f32)
            for p in range(pairs):
                cols = slice(p * LANES, (p + 1) * LANES)
                w = wps[at, width + p * LANES : width + (p + 1) * LANES]
                share = share + grad[:, cols] * w.astype(f32)
            gain_ref[:, lanes] = mm_exact(jnp.ones((8, LANES), f32), share, NT)
            wps[at, :width] = mm(cots[:, lanes], nl_all[...], TN).astype(bf16)
            for copy in early_out(i):
                copy.start()
            return 0

        lax.fori_loop(0, D // ROWS, some, 0, unroll=2)
        for copy in rows_out():
            copy.wait()

        def done(i, _):
            for copy in early_out(i):
                copy.wait()
            return 0

        lax.fori_loop(0, D // ROWS, done, 0)


def parameter_rows(me, width, flat_ref, taps_ref, head_ref, chan_ref):
    pairs = width // LANES
    heads = width // P_SIZE
    taps_ref[...] = jnp.zeros_like(taps_ref)
    chan_ref[...] = jnp.zeros_like(chan_ref)
    for c in range(pairs):
        cols = slice(c * LANES, (c + 1) * LANES)
        chan_ref[0:1, cols] = flat_ref[pl.ds(GATE_ROW + pairs * me + c, 1), :]
        taps_ref[CONV : CONV + 1, cols] = flat_ref[pl.ds(BIAS_ROW + pairs * me + c, 1), :]
        for k in range(CONV):
            taps_ref[k : k + 1, cols] = flat_ref[pl.ds(TAPS_ROW + 4 * pairs * k + pairs * me + c, 1), :]
    for c in range(2):
        cols = slice(width + c * LANES, width + (c + 1) * LANES)
        taps_ref[CONV : CONV + 1, cols] = flat_ref[BIAS_BC_ROW + c : BIAS_BC_ROW + c + 1, :]
        for k in range(CONV):
            row = TAPS_BC_ROW + 2 * k + c
            taps_ref[k : k + 1, cols] = flat_ref[row : row + 1, :]
    both = jnp.concatenate([flat_ref[HEAD_ROW : HEAD_ROW + 1, :], flat_ref[HEAD_ROW + 1 : HEAD_ROW + 2, :]], axis=1)
    both = jnp.broadcast_to(both, (8, 2 * LANES))
    lane = lax.broadcasted_iota(jnp.int32, (2 * LANES, LANES), 0)
    head = lax.broadcasted_iota(jnp.int32, (2 * LANES, LANES), 1)

    def take(kind):
        match = (lane == 4 * heads * kind + heads * me + head) & (head < heads)
        return mm_exact(both, jnp.where(match, 1.0, 0.0).astype(f32))

    valid = lax.broadcasted_iota(jnp.int32, (8, LANES), 1) < heads
    row = lax.broadcasted_iota(jnp.int32, (8, LANES), 0)
    rates = jnp.where(valid, -jnp.exp(take(1)), 0.0)
    head_ref[...] = jnp.where(row == 0, take(0), jnp.where(row == 1, rates, 0.0))
    skip = mm_exact(take(2), picked(width).astype(f32), NT)
    chan_ref[1:2, :] = skip[0:1]


def picked(width):
    channel = lax.broadcasted_iota(jnp.int32, (width, LANES), 0)
    head = lax.broadcasted_iota(jnp.int32, (width, LANES), 1)
    return jnp.where((channel >= head * P_SIZE) & (channel < (head + 1) * P_SIZE), 1.0, 0.0).astype(bf16)


def scan_step(
    width, tick, i, xg, w_ref, taps_ref, head_ref, chan_ref,
    v_ref, xc_ref, dr_ref, st_ref, halo, state, y_all, head_t, until, across_state, tails, late_turn,
):
    pairs = width // LANES
    wide = width + 2 * NS
    mine = span(tick * ROWS, ROWS)
    dr_ref[span(i * ROWS, ROWS), :] = mm(xg[mine, :], w_ref[:, wide:])
    halo[8 : 8 + ROWS, :] = mm(xg[mine, :], w_ref[:, :wide])
    low_half = block_iota(1) < P_SIZE
    causal = block_iota(0) >= block_iota(1)

    def convolved(sub, block):
        cols = slice(block * LANES, (block + 1) * LANES)
        total = taps_ref[CONV : CONV + 1, cols]
        for k in range(CONV):
            first = 8 - (CONV - 1) + k + sub * T
            total = total + taps_ref[k : k + 1, cols] * halo[first : first + T, cols]
        rows = span(i * ROWS + sub * T, T)
        xc_ref[rows, cols] = total.astype(bf16)
        v_ref[rows, cols] = halo[8 + sub * T : 8 + (sub + 1) * T, cols].astype(bf16)
        return total * sigmoid(total)

    for sub in range(ROWS // T):
        rows = span(i * ROWS + sub * T, T)
        _, _, decay_t, dt, decay = head_rows(dr_ref, head_t, until, rows)
        b_low = convolved(sub, pairs).astype(bf16)
        c_low = convolved(sub, pairs + 1).astype(bf16)
        b_t = b_low.T
        scores = jnp.where(causal, mm(c_low, b_low, NT), 0.0)
        entering = state[...].astype(bf16)
        st_ref[i * (ROWS // T) + sub] = entering
        across_state[...] = mm(c_low, entering)
        for p in range(pairs):
            cols = slice(p * LANES, (p + 1) * LANES)
            x = convolved(sub, p)
            l1, l2 = spread(decay[:, 2 * p : 2 * p + 1]), spread(decay[:, 2 * p + 1 : 2 * p + 2])
            both = jnp.where(low_half, l1, l2)
            dtb = jnp.where(
                low_half, spread(dt[:, 2 * p : 2 * p + 1]), spread(dt[:, 2 * p + 1 : 2 * p + 2])
            )
            u = x * dtb
            m1 = scores * jnp.exp2(jnp.minimum(l1 - decay_t[2 * p : 2 * p + 1, :], 0.0))
            m2 = scores * jnp.exp2(jnp.minimum(l2 - decay_t[2 * p + 1 : 2 * p + 2, :], 0.0))
            mixing = jnp.concatenate([m1.astype(bf16), m2.astype(bf16)], axis=1)
            u_low = u.astype(bf16)
            zero = jnp.zeros_like(u_low)
            parts = jnp.concatenate(
                [jnp.where(low_half, u_low, zero), jnp.where(low_half, zero, u_low)], axis=0
            )
            last = both[T - 1 : T, :]
            y = mm(mixing, parts) + jnp.exp2(both) * across_state[:, cols] + chan_ref[1:2, cols] * x
            tails[:, cols] = (u * jnp.exp2(last - both)).astype(bf16)
            state[:, cols] = jnp.exp2(last) * state[:, cols]
            y_all[span(tick * ROWS + sub * T, T), cols] = y
        state[...] = state[...] + mm(b_t, tails[...])
        if sub == 0:
            pl.when(tick == LEN // ROWS - 1)(late_turn)
    halo[0:8, :] = halo[ROWS : ROWS + 8, :]


def ssd_forward(n, layer_input, out_grad, flat, w_zx, w_bc, w_dt, w_out):
    rows, width = w_out.shape
    tokens = layer_input.shape[0]
    length = 4 * tokens
    wide = width + 2 * NS
    tall = 2 * ROWS
    steps = length // tall
    forming = steps + 2
    products = forming + steps
    subs = tall // T
    assert length == LEN
    row = lambda m: pl.BlockSpec((tall, m), lambda i: (jnp.minimum(i, steps - 1), 0))
    form = lambda m: pl.BlockSpec((tall, m), lambda i: (jnp.clip(i - forming, 0, steps - 1), 0))
    whole = lambda a: pl.BlockSpec(a.shape, lambda i: (0,) * a.ndim, pipeline_mode=pl.Buffered(1))
    fixed = lambda m: pl.BlockSpec((8, m), lambda i: (0, 0))
    anywhere = pl.BlockSpec(memory_space=pl.ANY)
    vm, dma = pltpu.VMEM, pltpu.SemaphoreType.DMA
    hops, lead = dma((2, 2, 2, n // 2)), dma((2, 2, n // 2))
    shape = lambda dims, dtype: jax.ShapeDtypeStruct(dims, dtype)
    return pl.pallas_call(
        functools.partial(forward_body, n, rows, tokens, width),
        grid=(products + 1,),
        in_specs=[anywhere, anywhere, *(whole(a) for a in (flat, w_zx, w_bc, w_dt, w_out))],
        out_specs=[
            row(wide), row(wide), row(LANES), pl.BlockSpec((subs, NS, width), lambda i: (jnp.minimum(i, steps - 1), 0, 0)),
            anywhere, anywhere, form(D), anywhere,
            fixed(width), fixed(D), anywhere, anywhere, anywhere, *(fixed(m) for m in (wide, LANES, width)),
        ],
        out_shape=[
            shape((length, wide), bf16), shape((length, wide), bf16), shape((length, LANES), f32),
            shape((length // T, NS, width), bf16), shape((length, width), bf16), shape((length, width), bf16),
            shape((length, D), bf16), shape((D, 2 * width), bf16), shape((8, width), f32), shape((8, D), f32),
            shape((length, D), bf16), shape((D, wide + LANES), bf16), shape((D, 2 * width), bf16),
            *(shape((8, m), f32) for m in (wide, LANES, width)),
        ],
        scratch_shapes=[
            vm((ROWS + 8, wide), f32), vm((NS, width), f32), vm((length, width), f32), vm((length, width), f32),
            *(vm((length, width), bf16) for _ in range(3)),
            vm((length, D), bf16), vm((length, D), bf16), vm((D, wide + LANES), bf16), vm((D, 2 * width), bf16),
            vm((4, 8, length), f32), vm((8, length), f32), vm((2, HEADS, LANES), f32), vm((3 * T, LANES), bf16),
            vm((T, width), f32), vm((T, width), bf16),
            dma((4,)), dma((2, D // ROWS)), lead, lead, lead, dma((11,)), dma((4,)), dma((4,)), dma((1,)), dma((1,)),
            dma((4,)), dma((4,)), lead, hops, hops, dma((4,)), dma((4,)),
            dma((1,)), dma((1,)), dma((4,)), dma((4,)), dma((3,)), dma((3,)),
        ],
        compiler_params=pltpu.CompilerParams(collective_id=2, has_side_effects=True, vmem_limit_bytes=ROOM),
        name="layer_forward",
    )(layer_input, out_grad, flat, w_zx, w_bc, w_dt, w_out)


def backward_body(
    n, own_rows, tokens, width,
    dy_ref, v_ref, xc_ref, dr_ref, st_ref, gate_ref, taps_ref, head_ref, chan_ref, early_ref, branch_ref,
    d_ref, small_ref, oearly_ref, obranch_ref,
    dxh, dstate, yst, bds, dyeb, utb, products, turn, acc, hacc, pick_ref, pick_t, fades, head_t, until_ref, reach_ref,
    own, slots, near, held, over_slot,
    load_sem, ring_send, ring_recv, near_send, near_recv, over_send, over_recv,
):
    pairs = width // LANES
    wide = width + 2 * NS
    step = pl.program_id(0)
    steps = LEN // ROWS
    subs = ROWS // T
    pos, ring, me, across, beside = neighbours(n)
    opposite = lax.rem(me + 2, 4)
    next_door = me + 1 - 2 * lax.rem(me, 2)
    far = lax.rem(next_door + 2, 4)
    half = tokens // 2
    cuts = cut_rows(own_rows)

    def block_at(way, count):
        return ring_index(lax.rem(pos + (count if way else n - count), n), n)

    def hop(k, way, h):
        first, size = cuts[way]
        if h == 0:
            src = early_ref.at[span(block_at(way, 1) * own_rows + first, size), pl.ds(k * width, width)]
        else:
            src = slots[way][k].at[h - 1]
        return remote(
            src, slots[way][k].at[h], ring_send.at[way, k, h], ring_recv.at[way, k, h], ring[way]
        )

    def near_copy(turned, part):
        start = (next_door if turned else far) * tokens + part * half
        return remote(
            branch_ref.at[span(start, half)], near.at[turned, part],
            near_send.at[turned, part], near_recv.at[turned, part], beside,
        )

    def held_copy(turned, part):
        start = (me if turned else opposite) * tokens + part * half
        return pltpu.make_async_copy(
            branch_ref.at[span(start, half)], held.at[turned, part], load_sem.at[2 * turned + part]
        )

    def over_copy(part):
        return remote(held.at[0, part], over_slot.at[part], over_send.at[part], over_recv.at[part], across)

    def own_copy():
        return pltpu.make_async_copy(early_ref, own, load_sem.at[4])

    def ring_turn(k, h):
        for way in (0, 1):
            first, size = cuts[way]
            hop(k, way, h).wait_recv()
            block = block_at(way, 2 + h) if h < n - 2 else block_at(way, 0)

            tile = strip(size)

            def some(i, _, way=way, first=first, block=block, tile=tile):
                cols = slice(k * width, (k + 1) * width)
                came = slots[way][k][h, span(i * tile, tile), :]
                mine = own[span(block * own_rows + first + i * tile, tile), cols]
                if h < n - 2:
                    slots[way][k][h, span(i * tile, tile), :] = came + mine
                else:
                    oearly_ref[span(first + i * tile, tile), cols] = came.astype(f32) + mine.astype(f32)
                return 0

            lax.fori_loop(0, size // tile, some, 0)
            if h < n - 2:
                hop(k, way, h + 1).start()

    def ring_poll(k, tick):
        for h in range(n - 1):
            pl.when(tick == min(h + 1, steps - 1))(functools.partial(ring_turn, k, h))

    def add_near(turned):
        for part in (0, 1):
            held_copy(turned, part).wait()
            near_copy(turned, part).wait_recv()

            def some(i, _, part=part):
                at = span(i * 32, 32)
                held[turned, part, at, :] = held[turned, part, at, :] + near[turned, part, at, :]
                return 0

            lax.fori_loop(0, half // 32, some, 0)
            if not turned:
                over_copy(part).start()

    @pl.when(step == 0)
    def _():
        enter((*ring, across, beside))
        for way in (0, 1):
            hop(0, way, 0).start()
        for turned in (0, 1):
            for part in (0, 1):
                near_copy(turned, part).start()
                held_copy(turned, part).start()
        own_copy().start()
        dxh[T : T + 8, :] = jnp.zeros((8, wide), f32)
        dstate[...] = jnp.zeros_like(dstate)
        acc[...] = jnp.zeros_like(acc)
        hacc[...] = jnp.zeros_like(hacc)
        turn[...] = jnp.zeros_like(turn)
        pick_ref[...] = picked(width)
        channel = lax.broadcasted_iota(jnp.int32, (HEADS, width), 1)
        head = lax.broadcasted_iota(jnp.int32, (HEADS, width), 0)
        mine = (channel >= head * P_SIZE) & (channel < (head + 1) * P_SIZE)
        pick_t[...] = jnp.where(mine, 1.0, 0.0).astype(bf16)
        set_heads(head_ref, head_t, until_ref)
        from_here = jnp.where(block_iota(0) >= block_iota(1), 1.0, 0.0).astype(bf16)
        after = jnp.where(block_iota(0) < block_iota(1), 1.0, 0.0).astype(bf16)
        for k, matrix in enumerate((from_here, from_here, after, after)):
            reach_ref[k * T : (k + 1) * T, :] = matrix
        products[3 * T :, :] = jnp.zeros((HEADS, width), bf16)

    low_half = block_iota(1) < P_SIZE
    row_at, col_at = block_iota(0), block_iota(1)
    until = row_at <= col_at
    pair_lane = lax.broadcasted_iota(jnp.int32, (8, 2 * T), 1)
    pair_row = lax.broadcasted_iota(jnp.int32, (8, 2 * T), 0)
    each = jnp.where(lax.div(pair_lane, T) == pair_row, 1.0, 0.0).astype(bf16)
    ones = jnp.ones((8, T), bf16)

    def add(index, cols, value):
        acc[index, :, cols] += jnp.sum(value.reshape(T // 8, 8, LANES), axis=0)

    def conv_back(rows, block, d_act, xc, s, act):
        cols = slice(block * LANES, (block + 1) * LANES)
        dxh[0:T, cols] = d_act * (s + act * (1.0 - s))
        v = v_ref[rows, cols].astype(f32)
        total = None
        for m in range(CONV):
            moved = dxh[m : m + T, cols]
            if m == 0:
                add(CONV, cols, moved)
            add(CONV - 1 - m, cols, v * moved)
            term = taps_ref[CONV - 1 - m : CONV - m, cols] * moved
            total = term if total is None else total + term
        d_ref[rows, cols] = total.astype(bf16)

    def work(i, _):
        tick = 2 * step + i
        chunk = 1 - i

        @pl.when(tick == 1)
        def _():
            own_copy().wait()
            add_near(0)

        pl.when(tick == 2)(functools.partial(add_near, 1))
        ring_poll(0, tick)
        for sub in reversed(range(subs)):
            rows = span(chunk * ROWS + sub * T, T)
            block_state = chunk * subs + sub
            raw_t, dt_t, decay_t, dt, decay = head_rows(dr_ref, head_t, until_ref, rows)
            b_cols = slice(width, width + NS)
            c_cols = slice(width + NS, width + 2 * NS)
            b_xc, c_xc = xc_ref[rows, b_cols].astype(f32), xc_ref[rows, c_cols].astype(f32)
            b_s, c_s = sigmoid(b_xc), sigmoid(c_xc)
            b_act, c_act = b_xc * b_s, c_xc * c_s
            b_low, c_low = b_act.astype(bf16), c_act.astype(bf16)
            c_t = c_low.T
            scores_t = jnp.where(until, mm(b_low, c_low, NT), 0.0)
            ds_low = dstate[...].astype(bf16)
            yst[...] = mm(c_low, st_ref[block_state])
            bds[...] = mm(b_low, ds_low)
            d_scores = jnp.zeros((T, LANES), f32)
            for p in range(pairs):
                cols = slice(p * LANES, (p + 1) * LANES)
                dy_low = dy_ref[rows, cols]
                dy = dy_low.astype(f32)
                xc = xc_ref[rows, cols].astype(f32)
                xs = sigmoid(xc)
                x = xc * xs
                l1, l2 = spread(decay[:, 2 * p : 2 * p + 1]), spread(decay[:, 2 * p + 1 : 2 * p + 2])
                both = jnp.where(low_half, l1, l2)
                dtb = jnp.where(
                    low_half, spread(dt[:, 2 * p : 2 * p + 1]), spread(dt[:, 2 * p + 1 : 2 * p + 2])
                )
                u = x * dtb
                last = both[T - 1 : T, :]
                e1 = jnp.exp2(jnp.minimum(decay_t[2 * p : 2 * p + 1, :] - l1, 0.0))
                e2 = jnp.exp2(jnp.minimum(decay_t[2 * p + 1 : 2 * p + 2, :] - l2, 0.0))
                zero = jnp.zeros_like(dy_low)
                dy_parts = jnp.concatenate(
                    [jnp.where(low_half, dy_low, zero), jnp.where(low_half, zero, dy_low)], axis=0
                )
                du_in = mm(
                    jnp.concatenate([(scores_t * e1).astype(bf16), (scores_t * e2).astype(bf16)], axis=1), dy_parts
                )
                d_mix = mm(u.astype(bf16), dy_parts, NT)
                d1, d2 = d_mix[:, :T] * e1, d_mix[:, T:] * e2
                d_scores = d_scores + d1 + d2
                held_pairs = jnp.concatenate([(d1 * scores_t).astype(bf16), (d2 * scores_t).astype(bf16)], axis=1)
                reached_by = mm(ones, held_pairs)
                leaving = mm(each, held_pairs, NT)
                turn[2 * p : 2 * p + 1, :] = reached_by[0:1, :T] - leaving[0:1]
                turn[2 * p + 1 : 2 * p + 2, :] = reached_by[0:1, T:] - leaving[1:2]
                tail = jnp.exp2(last - both)
                fades[0:1, cols] = jnp.exp2(last)
                dye = dy * jnp.exp2(both)
                du_out = tail * bds[:, cols]
                du = du_in + du_out
                products[0:T, cols] = (dye * yst[:, cols]).astype(bf16)
                products[T : 2 * T, cols] = (u * du_out).astype(bf16)
                products[2 * T : 3 * T, cols] = (x * du).astype(bf16)
                dyeb[:, cols] = dye.astype(bf16)
                utb[:, cols] = (u * tail).astype(bf16)
                add(CONV + 1, cols, dy * x)
                conv_back(rows, p, dtb * du + chan_ref[1:2, cols] * dy, xc, xs, x)
            d_scores = jnp.where(until, d_scores, 0.0).astype(bf16)
            d_b = mm(d_scores, c_low) + mm(utb[...], ds_low, NT)
            d_c = mm(d_scores, b_low, TN) + mm(dyeb[...], st_ref[block_state], NT)
            conv_back(rows, pairs, d_b, b_xc, b_s, b_act)
            conv_back(rows, pairs + 1, d_c, c_xc, c_s, c_act)
            fade = fades[0:1, :]
            before_ds = dstate[...]
            through = jnp.sum(before_ds * st_ref[block_state].astype(f32), axis=0, keepdims=True) * fade
            products[3 * T : 3 * T + HEADS, :] = jnp.broadcast_to(through, (HEADS, width)).astype(bf16)
            dstate[...] = fade * before_ds + mm(c_t, dyeb[...])
            by_head = mm(pick_t[...], products[...], NT)
            inside = pieces(turn[...] + by_head[:, :T], 2)
            outside = pieces(by_head[:, T : 2 * T], 2)
            reached = mm(jnp.concatenate([inside, outside], axis=1), reach_ref[...])
            reached = reached + jnp.broadcast_to(by_head[:, 3 * T : 3 * T + 1], (HEADS, T))
            d_raw = (head_t[1] * reached + by_head[:, 2 * T : 3 * T]) * sigmoid(raw_t)
            d_ref[rows, wide:] = columns_of(d_raw).astype(bf16)
            hacc[0] += d_raw
            hacc[1] += dt_t * reached
            dxh[T : T + 8, :] = dxh[0:8, :]
            if sub == 1:
                @pl.when(tick == 0)
                def _():
                    for way in (0, 1):
                        hop(1, way, 0).start()

                ring_poll(1, tick)
        return 0

    lax.fori_loop(0, 2, work, 0)

    @pl.when(step == steps // 2 - 1)
    def _():
        total = lambda a: jnp.sum(a, axis=0, keepdims=True)
        for k in range(CONV + 1):
            small_ref[k : k + 1, :] = total(acc[k])
        small_ref[CONV + 1 : CONV + 2, :width] = total(gate_ref[...])
        small_ref[CONV + 1 : CONV + 2, width : width + LANES] = total(columns_of(hacc[0]))
        small_ref[CONV + 1 : CONV + 2, width + LANES :] = total(columns_of(hacc[1])) * head_ref[1:2, :]
        small_ref[CONV + 2 :, :] = jnp.zeros((2, wide), f32)
        skip = mm_exact(acc[CONV + 1, :, :width], pick_ref[...].astype(f32))
        small_ref[CONV + 3 : CONV + 4, 512 : 512 + LANES] = total(skip)
        for part in (0, 1):
            over_copy(part).wait_recv()

            def some(i, _, part=part):
                at = span(part * half + i * 32, 32)
                here = span(i * 32, 32)
                total = held[1, part, here, :].astype(f32) + over_slot[part, here, :].astype(f32)
                obranch_ref[at, :] = total.astype(bf16)
                return 0

            lax.fori_loop(0, half // 32, some, 0)
        for part in (0, 1):
            over_copy(part).wait_send()
            for turned in (0, 1):
                near_copy(turned, part).wait_send()
        for h in range(n - 1):
            for k in (0, 1):
                for way in (0, 1):
                    hop(k, way, h).wait_send()


def ssd_backward(n, dy, v, xc, dr, st, gate, taps, head, chan, early, branch):
    length, width = dy.shape
    wide = width + 2 * NS
    tall = 2 * ROWS
    steps = length // tall
    subs = tall // T
    own_rows, tokens = D // n, length // 4
    half = tokens // 2
    row = lambda m: pl.BlockSpec((tall, m), lambda i: (steps - 1 - i, 0))
    whole = lambda a: pl.BlockSpec(a.shape, lambda i: (0,) * a.ndim, pipeline_mode=pl.Buffered(1))
    fixed = lambda *shape: pl.BlockSpec(shape, lambda i: (0,) * len(shape))
    anywhere = pl.BlockSpec(memory_space=pl.ANY)
    vm, dma = pltpu.VMEM, pltpu.SemaphoreType.DMA
    return pl.pallas_call(
        functools.partial(backward_body, n, own_rows, tokens, width),
        grid=(steps,),
        in_specs=[
            row(width), row(wide), row(wide), row(LANES),
            pl.BlockSpec((subs, NS, width), lambda i: (steps - 1 - i, 0, 0)),
            whole(gate), whole(taps), whole(head), whole(chan), anywhere, anywhere,
        ],
        out_specs=[
            row(wide + LANES), fixed(8, wide), fixed(own_rows, 2 * width), fixed(tokens, D),
        ],
        out_shape=[
            jax.ShapeDtypeStruct((length, wide + LANES), bf16),
            jax.ShapeDtypeStruct((8, wide), f32),
            jax.ShapeDtypeStruct((own_rows, 2 * width), f32),
            jax.ShapeDtypeStruct((tokens, D), bf16),
        ],
        scratch_shapes=[
            vm((T + 8, wide), f32), vm((NS, width), f32), vm((T, width), f32), vm((T, width), f32),
            vm((T, width), bf16), vm((T, width), bf16), vm((3 * T + HEADS, width), bf16),
            vm((HEADS, T), f32), vm((CONV + 2, 8, wide), f32), vm((2, HEADS, T), f32),
            vm((width, LANES), bf16), vm((HEADS, width), bf16), vm((8, width), f32), vm((2, HEADS, LANES), f32),
            vm((3 * T, LANES), bf16), vm((4 * T, LANES), bf16),
            vm((D, 2 * width), bf16),
            [[vm((n - 1, size, width), bf16) for _ in (0, 1)] for _, size in cut_rows(own_rows)],
            vm((2, 2, half, D), bf16), vm((2, 2, half, D), bf16), vm((2, half, D), bf16),
            dma((5,)), dma((2, 2, n - 1)), dma((2, 2, n - 1)), dma((2, 2)), dma((2, 2)), dma((2,)), dma((2,)),
        ],
        compiler_params=pltpu.CompilerParams(
            collective_id=3, has_side_effects=True, vmem_limit_bytes=ROOM
        ),
        name="layer_backward",
    )(dy, v, xc, dr, st, gate, taps, head, chan, early, branch)


def reduce_body(
    n, rows, tokens, starts,
    xg_ref, d_ref, dz_ref, wp_ref, w_ref, small_ref, flat_ref, gain_ref,
    oxs_ref, oback_ref, bc_ref, oflat_ref,
    xg, d, dz, wz, w, work, grads, slots, staged, near, over, smalls, tens, bc_slot,
    load_sem, ring_send, ring_recv, near_send, near_recv, over_send, over_recv,
    small_send, small_recv, ten_send, ten_recv, bc_send, bc_recv,
):
    pos, ring, me, across, beside = neighbours(n)
    cuts = cut_rows(rows)
    core = lax.rem(me, 2)
    opposite = lax.rem(me + 2, 4)
    next_door = me + 1 - 2 * core
    far = lax.rem(next_door + 2, 4)
    half = tokens // 2
    late = d.shape[1]
    width = dz.shape[1]
    tile = 2 * LANES
    tiles = D // tile
    columns = [pl.ds(lo, hi - lo) for lo, hi in starts]
    sources = [(d_ref.at[:, columns[0]], d.at[:, columns[0]])]
    sources += [(xg_ref.at[:, pl.ds(i * tile, tile)], xg.at[:, pl.ds(i * tile, tile)]) for i in range(tiles)]
    sources += [(d_ref.at[:, some], d.at[:, some]) for some in columns[1:]]
    sources += [
        (dz_ref, dz), (w_ref, w), (wp_ref.at[:, pl.ds(width, width)], wz), (small_ref, smalls.at[pos]),
    ]
    loads = [pltpu.make_async_copy(src, dst, load_sem.at[k]) for k, (src, dst) in enumerate(sources)]
    for load in loads:
        load.start()
    askew = {"tensor": far}
    enter((*ring, across, beside, askew))
    started = []

    def go(*args):
        copy = remote(*args)
        copy.start()
        started.append(copy)

    def block_at(way, count):
        return ring_index(lax.rem(pos + (count if way else n - count), n), n)

    def hop(k, way, h):
        lo, hi = starts[k]
        first, size = cuts[way]
        if h == 0:
            src = grads.at[span(block_at(way, 1) * rows + first, size), pl.ds(lo, hi - lo)]
        else:
            src = slots[way][k].at[h - 1]
        return remote(
            src, slots[way][k].at[h], ring_send.at[way, k, h], ring_recv.at[way, k, h], ring[way]
        )

    def product(k):
        lo, hi = starts[k]

        def some(i, _):
            at = pl.ds(pl.multiple_of(i * tile, tile), tile)
            if k == 0:
                pltpu.make_async_copy(xg_ref.at[:, at], xg.at[:, at], load_sem.at[1 + i]).wait()
            grads[at, lo:hi] = mm(xg[:, at], d[:, lo:hi], TN).astype(bf16)
            return 0

        loads[0 if k == 0 else tiles + k].wait()
        lax.fori_loop(0, tiles, some, 0)
        for way in (0, 1):
            hop(k, way, 0).start()

    def near_copy(turned, part):
        return remote(
            staged.at[turned, part], near.at[turned, part],
            near_send.at[turned, part], near_recv.at[turned, part], beside,
        )

    def over_copy(part):
        return remote(near.at[0, part], over.at[part], over_send.at[part], over_recv.at[part], across)

    def ring_turn(k, h):
        lo, hi = starts[k]
        for way in (0, 1):
            first, size = cuts[way]
            slot = slots[way][k].at[h]
            remote(slot, slot, ring_send.at[way, k, h], ring_recv.at[way, k, h], ring[way]).wait_recv()
            block = block_at(way, 2 + h) if h < n - 2 else block_at(way, 0)

            tile = strip(size)

            def some(i, _, way=way, first=first, block=block, tile=tile):
                came = slots[way][k][h, span(i * tile, tile), :]
                mine = grads[span(block * rows + first + i * tile, tile), lo:hi]
                if h < n - 2:
                    slots[way][k][h, span(i * tile, tile), :] = came + mine
                else:
                    oxs_ref[span(first + i * tile, tile), lo:hi] = came.astype(f32) + mine.astype(f32)
                return 0

            lax.fori_loop(0, size // tile, some, 0)
            if h < n - 2:
                hop(k, way, h + 1).start()

    def small_hop(way, h):
        here = smalls.at[lax.rem(pos + (h if way else n - h), n)]
        go(here, here, small_send.at[way, h], small_recv.at[way, h], ring[way])

    def small_lands(way, h):
        here = smalls.at[lax.rem(pos + (h + 1 if way else n - h - 1), n)]
        remote(here, here, small_send.at[way, h], small_recv.at[way, h], ring[way]).wait_recv()

    for k in range(len(starts)):
        product(k)
    for load in loads[tiles + len(starts) :]:
        load.wait()
    turns = {0: [(0, 0)], 1: [(1, 0), (2, 0)], 2: [(0, 1)], 3: [(1, 1), (2, 1)], 4: [(0, 2)], 5: [(1, 2), (2, 2)], 6: [(0, 3)], 7: [(1, 3), (2, 3)]}
    taken = [sum(k == group for some in turns.values() for k, _ in some) for group in range(len(starts))]

    def block(i, _):
        which, part = lax.div(i, 2), lax.rem(i, 2)
        own = lax.rem(which, 2)
        turned = lax.div(which, 2)
        target = lax.rem(next_door + own * (me - next_door) + 2 * (1 - turned), 4)
        at = span(target * tokens + part * half, half)
        total = mm(dz[at, :], wz[...], NT) + mm(d[at, :], w[...], NT)
        work[...] = total

        @pl.when(own == 0)
        def _():
            staged[turned, part] = work[...].astype(bf16)
            near_copy(turned, part).start()

        @pl.when(own == 1)
        def _():
            near_copy(turned, part).wait_recv()

        @pl.when(which == 1)
        def _():
            near[0, part] = (work[...] + near[0, part].astype(f32)).astype(bf16)
            over_copy(part).start()

        @pl.when(which == 3)
        def _():
            near[1, part] = (work[...] + near[1, part].astype(f32)).astype(bf16)

        for at_block, some in turns.items():

            @pl.when(i == at_block)
            def _(some=some):
                for k, h in some:
                    ring_turn(k, h)

        return 0

    lax.fori_loop(0, 8, block, 0)
    for i in range(tiles):
        share = jnp.zeros((tile, LANES), f32)
        for c in range(late // LANES):
            cols = slice(c * LANES, (c + 1) * LANES)
            at = slice(i * tile, (i + 1) * tile)
            share = share + grads[at, cols].astype(f32) * w[at, cols].astype(f32)
        total = mm_exact(jnp.ones((8, LANES), f32), share, NT)[0:1] + gain_ref[0:1, i * tile : (i + 1) * tile]
        for c in range(2 * i, 2 * i + 2):
            row, col = 6 + c // 8, (c % 8) * LANES
            part = total[:, (c - 2 * i) * LANES : (c - 2 * i + 1) * LANES]
            smalls[pos, row : row + 1, col : col + LANES] = part / flat_ref[c : c + 1, :]

    rest = [(k, h) for h in range(n - 1) for k in (0, 1, 2) if h >= taken[k]]
    rest.sort(key=lambda turn: turn[1] - taken[turn[0]])

    def small_step(s):
        for way in (0, 1):
            if s > 0 and (way == 0 or s < n // 2):
                small_lands(way, s - 1)
            if s < n // 2 - way:
                small_hop(way, s)

    small_step(0)
    steps_done = 1
    for at, (k, h) in enumerate(rest):
        ring_turn(k, h)
        if (k, h) == (0, n - 2):
            bc_slot[0] = oxs_ref[:, starts[0][0] : starts[0][0] + 2 * NS]
            go(bc_slot.at[0], bc_slot.at[1], bc_send.at[0], bc_recv.at[0], beside)
        if at % 2 == 1 and steps_done < n // 2:
            small_step(steps_done)
            steps_done += 1
    for s in range(steps_done, n // 2):
        small_step(s)
    small_lands(0, n // 2 - 1)

    total = smalls[0]
    for i in range(1, n):
        total = total + smalls[i]
    tens[me] = total
    others = ((beside, next_door), (across, opposite), (askew, far))
    for k, (peer, _) in enumerate(others):
        go(tens.at[me], tens.at[me], ten_send.at[k], ten_recv.at[k], peer)
    remote(bc_slot.at[1], bc_slot.at[1], bc_send.at[0], bc_recv.at[0], beside).wait_recv()
    bc_slot[2] = bc_slot[0] + bc_slot[1]
    go(bc_slot.at[2], bc_slot.at[3], bc_send.at[1], bc_recv.at[1], across)
    for part in (0, 1):
        over_copy(part).wait_recv()

        def some(i, _, part=part):
            at = span(part * half + i * 32, 32)
            here = span(i * 32, 32)
            oback_ref[at, :] = (near[1, part, here, :].astype(f32) + over[part, here, :].astype(f32)).astype(bf16)
            return 0

        lax.fori_loop(0, half // 32, some, 0)
    for k, (peer, target) in enumerate(others):
        here = tens.at[target]
        remote(here, here, ten_send.at[k], ten_recv.at[k], peer).wait_recv()
    flat_gradients(width, tens, oflat_ref)
    remote(bc_slot.at[3], bc_slot.at[3], bc_send.at[1], bc_recv.at[1], across).wait_recv()
    bc_ref[...] = bc_slot[2] + bc_slot[3]
    for part in (0, 1):
        over_copy(part).wait_send()
        for turned in (0, 1):
            near_copy(turned, part).wait_send()
    for k in range(len(starts)):
        for way in (0, 1):
            for h in range(n - 1):
                hop(k, way, h).wait_send()
    for copy in started:
        copy.wait_send()


def flat_gradients(width, tens, out_ref):
    pairs = width // LANES
    heads = width // P_SIZE

    def sums(row, col):
        total = tens[0, row : row + 1, col : col + LANES]
        for t in range(1, 4):
            total = total + tens[t, row : row + 1, col : col + LANES]
        return total

    def put(row, value):
        out_ref[row : row + 1, :] = value

    for c in range(D // LANES):
        put(c, sums(6 + c // 8, (c % 8) * LANES))
    for t in range(4):
        for c in range(pairs):
            cols = slice(c * LANES, (c + 1) * LANES)
            put(GATE_ROW + pairs * t + c, tens[t, CONV + 1 : CONV + 2, cols])
            put(BIAS_ROW + pairs * t + c, tens[t, CONV : CONV + 1, cols])
            for k in range(CONV):
                put(TAPS_ROW + 4 * pairs * k + pairs * t + c, tens[t, k : k + 1, cols])
    for c in range(2):
        put(BIAS_BC_ROW + c, sums(CONV, width + c * LANES))
        for k in range(CONV):
            put(TAPS_BC_ROW + 2 * k + c, sums(k, width + c * LANES))
    kinds = ((CONV + 1, width), (CONV + 1, width + LANES), (CONV + 3, 512))
    rows = [tens[t, row : row + 1, col : col + LANES] for row, col in kinds for t in range(4)]
    rows = jnp.concatenate(rows + [jnp.zeros((16 - len(rows), LANES), f32)], axis=0)
    lane = lax.broadcasted_iota(jnp.int32, (LANES, 2 * LANES), 1)
    entry = lax.broadcasted_iota(jnp.int32, (LANES, 2 * LANES), 0)
    spread_out = mm_exact(rows, jnp.where(lax.rem(lane, heads) == entry, 1.0, 0.0).astype(f32))
    at = lax.broadcasted_iota(jnp.int32, (16, 2 * LANES), 1)
    source = lax.broadcasted_iota(jnp.int32, (16, 2 * LANES), 0)
    line = jnp.sum(jnp.where(lax.div(at, heads) == source, spread_out, 0.0), axis=0, keepdims=True)
    put(HEAD_ROW, line[:, :LANES])
    put(HEAD_ROW + 1, line[:, LANES:])


def reduce_all(n, xg, d, dz, wp, w, small, flat, gain):
    rows, tokens = D // n, dz.shape[0] // 4
    width, late = dz.shape[1], d.shape[1]
    starts = ((width, late), (0, width // 2), (width // 2, width))
    half = tokens // 2
    dma, vm = pltpu.SemaphoreType.DMA, pltpu.VMEM
    anywhere = pl.BlockSpec(memory_space=pl.ANY)
    inside = pl.BlockSpec(memory_space=pltpu.VMEM)
    return pl.pallas_call(
        functools.partial(reduce_body, n, rows, tokens, starts),
        in_specs=[anywhere] * 6 + [inside] * 2,
        out_specs=[inside] * 4,
        out_shape=[
            jax.ShapeDtypeStruct((rows, late), f32),
            jax.ShapeDtypeStruct((tokens, D), bf16),
            jax.ShapeDtypeStruct((rows, 2 * NS), f32),
            jax.ShapeDtypeStruct((FLAT_ROWS, LANES), f32),
        ],
        scratch_shapes=[
            vm(xg.shape, bf16), vm(d.shape, bf16), vm(dz.shape, bf16), vm((D, width), bf16),
            vm((D, late), bf16),
            vm((half, D), f32), vm((D, late), bf16),
            [[vm((n - 1, size, hi - lo), bf16) for lo, hi in starts] for _, size in cut_rows(rows)],
            vm((2, 2, half, D), bf16), vm((2, 2, half, D), bf16), vm((2, half, D), bf16),
            vm((n, *small.shape), f32), vm((4, *small.shape), f32), vm((4, rows, 2 * NS), f32),
            dma((13,)), dma((2, 3, n - 1)), dma((2, 3, n - 1)), dma((2, 2)), dma((2, 2)), dma((2,)), dma((2,)),
            dma((2, n // 2)), dma((2, n // 2)), dma((3,)), dma((3,)), dma((2,)), dma((2,)),
        ],
        compiler_params=pltpu.CompilerParams(
            collective_id=1, has_side_effects=True, vmem_limit_bytes=46 * 2**20
        ),
        name="reduce_all",
    )(xg, d, dz, wp, w, small, flat, gain)


def adamw_step(weight, first, second, grad, rate, decay):
    first_new = beta_first * first + (1.0 - beta_first) * grad
    second_new = beta_second * second + (1.0 - beta_second) * grad * grad
    hat_first = first_new * (1.0 / (1.0 - beta_first**STEP))
    hat_second = second_new * (1.0 / (1.0 - beta_second**STEP))
    weight_new = weight - rate * (hat_first / (jnp.sqrt(hat_second) + adam_eps) + decay * weight)
    return (weight_new, first_new, second_new)


def finish_body(
    width, heads,
    in_ref, cot_ref, branch_ref, back_ref, flat_ref, early_ref, late_ref, bcg_ref,
    zx_ref, zx1_ref, zx2_ref, bc_ref, bc1_ref, bc2_ref, out_ref, out1_ref, out2_ref, late_all_ref, dt_ref, dt1_ref, dt2_ref,
    layer_ref, grad_ref, zxn_ref, zx1n_ref, zx2n_ref, bcn_ref, bc1n_ref, bc2n_ref,
    outn_ref, out1n_ref, out2n_ref, dtn_ref, dt1n_ref, dt2n_ref,
):
    def update(refs, news, grad):
        fresh = adamw_step(*(ref[...] for ref in refs), grad, matrix_rate, matrix_decay)
        for ref, value in zip(news, fresh):
            ref[...] = value

    for k, grad in ((0, early_ref), (1, late_ref)):
        fresh = adamw_step(
            *(ref[:, k, :] for ref in (zx_ref, zx1_ref, zx2_ref)), grad[:, :width], matrix_rate, matrix_decay
        )
        for ref, value in zip((zxn_ref, zx1n_ref, zx2n_ref), fresh):
            ref[:, k, :] = value
    update((bc_ref, bc1_ref, bc2_ref), (bcn_ref, bc1n_ref, bc2n_ref), bcg_ref[...])
    update((out_ref, out1_ref, out2_ref), (outn_ref, out1n_ref, out2n_ref), early_ref[:, width:])

    @pl.when(pl.program_id(0) == 0)
    def _():
        unit = jnp.where(
            lax.broadcasted_iota(jnp.int32, (16, LANES), 0) == lax.broadcasted_iota(jnp.int32, (16, LANES), 1), 1.0, 0.0
        ).astype(f32)
        turned = mm_exact(unit, late_all_ref[:, width + 2 * NS :], NT)
        update((dt_ref, dt1_ref, dt2_ref), (dtn_ref, dt1n_ref, dt2n_ref), turned[:heads])

    rows = in_ref.shape[0]
    tile = 64

    def some(i, _):
        at = span(i * tile, tile)
        squares = jnp.zeros((tile, LANES), f32)
        inner = jnp.zeros((tile, LANES), f32)
        for c in range(D // LANES):
            cols = slice(c * LANES, (c + 1) * LANES)
            x = in_ref[at, cols].astype(f32)
            squares = squares + x * x
            inner = inner + x * flat_ref[c : c + 1, :] * back_ref[at, cols].astype(f32)
        r = lax.rsqrt(jnp.sum(squares, axis=-1, keepdims=True) / D + norm_eps)
        k = r * r * r * jnp.sum(inner, axis=-1, keepdims=True) / D
        r, k = jnp.broadcast_to(r, (tile, LANES)), jnp.broadcast_to(k, (tile, LANES))
        for c in range(D // LANES):
            cols = slice(c * LANES, (c + 1) * LANES)
            x = in_ref[at, cols].astype(f32)
            layer_ref[at, cols] = (x + branch_ref[at, cols].astype(f32)).astype(bf16)
            back = back_ref[at, cols].astype(f32)
            grad_ref[at, cols] = cot_ref[at, cols].astype(f32) + r * flat_ref[c : c + 1, :] * back - x * k
        return 0

    lax.fori_loop(0, rows // tile, some, 0)


def finish(layer_input, out_grad, branch, back, flat, early, late, bcg, zx, bc, out, dt):
    (rows, width), heads = out[0].shape, dt[0].shape[0]
    steps = 2
    part = lambda a: pl.BlockSpec((a.shape[0] // steps, *a.shape[1:]), lambda i: (i,) + (0,) * (a.ndim - 1))
    whole = lambda a: pl.BlockSpec(a.shape, lambda i: (0,) * a.ndim)
    like = lambda a, dtype=f32: jax.ShapeDtypeStruct(a.shape, dtype)
    weights = (*zx, *bc, *out)
    return pl.pallas_call(
        functools.partial(finish_body, width, heads),
        grid=(steps,),
        in_specs=[
            *(part(a) for a in (layer_input, out_grad, branch, back)), whole(flat),
            *(part(a) for a in (early, late, bcg, *weights)), whole(late), *(whole(a) for a in dt),
        ],
        out_specs=[part(layer_input), part(back), *(part(a) for a in weights), *(whole(a) for a in dt)],
        out_shape=[like(layer_input, bf16), like(layer_input), *(like(a) for a in weights), *(like(a) for a in dt)],
        compiler_params=pltpu.CompilerParams(vmem_limit_bytes=32 * 2**20),
        name="finish",
    )(layer_input, out_grad, branch, back, flat, early, late, bcg, *weights, late, *dt)


def local(
    layer_input,
    out_grad,
    small_params,
    small_first,
    small_second,
    w_zx,
    zx_first,
    zx_second,
    w_bc,
    bc_first,
    bc_second,
    w_dt,
    dt_first,
    dt_second,
    w_out,
    out_first,
    out_second,
):
    n = lax.axis_size("dp")
    flat = jnp.pad(small_params, (0, FLAT_ROWS * LANES - small_params.shape[0])).reshape(FLAT_ROWS, LANES)
    v, xc, dr, st, dy, dz, branch, early, gate, gain, xg, w_all, pair_all, taps, head, chan = ssd_forward(
        n, layer_input, out_grad, flat, w_zx, w_bc, w_dt.T, w_out
    )
    d_late, small, owner_early, own_branch = ssd_backward(
        n, dy, v, xc, dr, st, gate, taps, head, chan, early, branch
    )
    owner_late, d_normed_in, owner_bc, flat_grad = reduce_all(
        n, xg, d_late, dz, pair_all, w_all, small, flat, gain
    )
    small_grad = flat_grad.reshape(-1)[: small_params.shape[0]]
    small_new, small_first_new, small_second_new = adamw_step(
        small_params, small_first, small_second, small_grad, small_rate, 0.0
    )
    (
        layer_output, input_grad, zx_new, zx_first_new, zx_second_new, bc_new, bc_first_new, bc_second_new,
        out_new, out_first_new, out_second_new, dt_new, dt_first_new, dt_second_new,
    ) = finish(
        layer_input, out_grad, own_branch, d_normed_in, flat, owner_early, owner_late, owner_bc,
        (w_zx, zx_first, zx_second), (w_bc, bc_first, bc_second), (w_out, out_first, out_second),
        (w_dt.T, dt_first.T, dt_second.T),
    )
    dt_new, dt_first_new, dt_second_new = dt_new.T, dt_first_new.T, dt_second_new.T
    return (
        layer_output,
        input_grad,
        small_new,
        small_first_new,
        small_second_new,
        zx_new,
        zx_first_new,
        zx_second_new,
        bc_new,
        bc_first_new,
        bc_second_new,
        dt_new,
        dt_first_new,
        dt_second_new,
        out_new,
        out_first_new,
        out_second_new,
    )


def solution(mesh):
    return jax.shard_map(
        local,
        mesh=mesh,
        in_specs=(
            P(("dp", "tensor"), None),
            P(("dp", "tensor"), None),
            P(),
            P(),
            P(),
            P("dp", None, "tensor"),
            P("dp", None, "tensor"),
            P("dp", None, "tensor"),
            P("dp", None),
            P("dp", None),
            P("dp", None),
            P("dp", "tensor"),
            P("dp", "tensor"),
            P("dp", "tensor"),
            P("dp", "tensor"),
            P("dp", "tensor"),
            P("dp", "tensor"),
        ),
        out_specs=(
            P(("dp", "tensor"), None),
            P(("dp", "tensor"), None),
            P(),
            P(),
            P(),
            P("dp", None, "tensor"),
            P("dp", None, "tensor"),
            P("dp", None, "tensor"),
            P("dp", None),
            P("dp", None),
            P("dp", None),
            P("dp", "tensor"),
            P("dp", "tensor"),
            P("dp", "tensor"),
            P("dp", "tensor"),
            P("dp", "tensor"),
            P("dp", "tensor"),
        ),
        check_vma=False,
    )
```

```python
import functools

import jax
import jax.numpy as jnp
from jax import lax
from jax.experimental import pallas as pl
from jax.experimental.pallas import tpu as pltpu
from jax.sharding import PartitionSpec as P

D = 1536
DI = 3072
H = 48
NS = 128
P_SIZE = 64
CONV = 4
LEN = 2048
STEP = 10

T = 128
ROWS = 256
LANES = 128
ROOM = 60 * 2**20

norm_eps = 1e-05
adam_eps = 1e-08
beta_first = 0.9
beta_second = 0.95
matrix_rate = 0.01
small_rate = 0.1
matrix_decay = 0.1

f32 = jnp.float32
bf16 = jnp.bfloat16
NN = (((1,), (0,)), ((), ()))
NT = (((1,), (1,)), ((), ()))
TN = (((0,), (0,)), ((), ()))
HIGHEST = lax.Precision.HIGHEST


GATE_ROW, TAPS_ROW, BIAS_ROW, TAPS_BC_ROW, BIAS_BC_ROW, HEAD_ROW, FLAT_ROWS = 12, 36, 132, 156, 164, 166, 168


def mm(a, b, dims=NN):
    return lax.dot_general(a, b, dims, preferred_element_type=f32)


def mm_exact(a, b, dims=NN):
    return lax.dot_general(a, b, dims, preferred_element_type=f32, precision=HIGHEST)


def sigmoid(v):
    return 0.5 * jnp.tanh(0.5 * v) + 0.5


def softplus(v):
    return jnp.maximum(v, 0.0) + jnp.log1p(jnp.exp(-jnp.abs(v)))


def spread(col):
    return jnp.broadcast_to(col, (T, LANES))


def block_iota(axis):
    return lax.broadcasted_iota(jnp.int32, (T, LANES), axis)


HEADS = 16
LOG2_E = 1.4426950408889634


def pieces(value, count):
    parts = []
    for k in range(count):
        part = value.astype(bf16)
        parts.append(part)
        if k < count - 1:
            value = value - part.astype(f32)
    return jnp.concatenate(parts, axis=1)


def columns_of(rows):
    return jnp.concatenate([rows, jnp.zeros((LANES - HEADS, T), f32)], axis=0).T


def set_heads(head_ref, head_t, until):
    turned = jnp.concatenate([head_ref[...], jnp.zeros((LANES - 8, LANES), f32)], axis=0).T
    head_t[0] = spread(turned[:, 0:1])[:HEADS]
    head_t[1] = spread(turned[:, 1:2])[:HEADS]
    matrix = jnp.where(block_iota(0) <= block_iota(1), 1.0, 0.0).astype(bf16)
    for k in range(3):
        until[k * T : (k + 1) * T, :] = matrix


def head_rows(dr_ref, head_t, until, rows):
    raw = dr_ref[rows, :].T[:HEADS] + head_t[0]
    dt = softplus(raw)
    decay = mm(pieces(dt * (head_t[1] * LOG2_E), 3), until[...])
    return raw, dt, decay, columns_of(dt), columns_of(decay)


def ring_place(n):
    me = lax.axis_index("dp")
    z, x = lax.div(me, 2), lax.rem(me, 2)
    return z + x * (n - 1 - 2 * z)


def ring_index(pos, n):
    back = lax.div(pos, n // 2)
    return 2 * pos + back * (2 * n - 1 - 4 * pos)


def neighbours(n):
    pos = ring_place(n)
    right = ring_index(lax.rem(pos + 1, n), n)
    left = ring_index(lax.rem(pos + n - 1, n), n)
    me = lax.axis_index("tensor")
    y, core = lax.div(me, 2), lax.rem(me, 2)
    across = 2 * (1 - y) + core
    beside = 2 * y + 1 - core
    return pos, ({"dp": right}, {"dp": left}), me, {"tensor": across}, {"tensor": beside}


def greet(peers):
    barrier = pltpu.get_barrier_semaphore()
    for peer in peers:
        pl.semaphore_signal(barrier, inc=1, device_id=peer, device_id_type=pl.DeviceIdType.MESH)


def enter(peers):
    greet(peers)
    pl.semaphore_wait(pltpu.get_barrier_semaphore(), len(peers))


def remote(src, dst, send_sem, recv_sem, peer):
    return pltpu.make_async_remote_copy(
        src_ref=src, dst_ref=dst, send_sem=send_sem, recv_sem=recv_sem,
        device_id=peer, device_id_type=pl.DeviceIdType.MESH,
    )


def span(start, size):
    return pl.ds(pl.multiple_of(start, 16), size)


def strip(rows):
    return next(size for size in (48, 32, 16) if rows % size == 0)


def cut_rows(rows):
    top = rows // 32 * 16
    return ((0, top), (top, rows - top))


def forward_body(
    n, rows, tokens, width,
    in_ref, cot_ref, flat_ref, wzx_ref, wbc_ref, wdt_ref, wout_ref,
    v_ref, xc_ref, dr_ref, st_ref, dy_ref, dz_ref, branch_ref, early_ref, gate_ref, gain_ref,
    xg_ref, ws_ref, wps_ref, taps_ref, head_ref, chan_ref,
    halo, state, y_all, z_all, dn_all, nl_all, dz_all, xg, cots, ws, wps, sums, red, head_t, until, across_state, tails,
    own_keep, early_keep, lead_keep, lead_send, lead_recv, x_keep, x_over_send, x_over_recv, x_side_send, x_side_recv,
    x_pass_send, x_pass_recv, ring_keep, ring_send, ring_recv, over_send, over_recv,
    side_send, side_recv, pass_send, pass_recv, sum_send, sum_recv,
):
    pairs = width // LANES
    wide = width + 2 * NS
    step = pl.program_id(0)
    steps = LEN // ROWS
    tall = 2 * ROWS
    norming = steps // 2
    gating = norming + 1
    forming = gating + 1
    products = forming + steps // 2
    pos, ring, me, across, beside = neighbours(n)
    opposite = lax.rem(me + 2, 4)
    next_door = me + 1 - 2 * lax.rem(me, 2)
    far = lax.rem(next_door + 2, 4)
    askew = {"tensor": far}
    quarter = tokens // 4
    hops = n // 2
    cuts = cut_rows(rows)
    mine = ring_index(pos, n)

    late = wide + LANES
    parts_of = ((0, width), (width, width))

    def hop(k, part, way, h):
        first, size = cuts[part]
        cols = pl.ds(*parts_of[k])
        block = ring_index(lax.rem(pos + (h if way else n - h), n), n)
        here = wps.at[span(block * rows + first, size), cols]
        return remote(here, here, ring_send.at[way, part, k, h], ring_recv.at[way, part, k, h], ring[way])

    def hop_lands(k, part, way, h):
        first, size = cuts[part]
        block = ring_index(lax.rem(pos + (h + 1 if way else n - h - 1), n), n)
        return span(block * rows + first, size), pl.ds(*parts_of[k])

    def hop_arrival(k, part, way, h):
        here = wps.at[hop_lands(k, part, way, h)]
        return remote(here, here, ring_send.at[way, part, k, h], ring_recv.at[way, part, k, h], ring[way])

    def hop_keep(part, way, h):
        at = hop_lands(1, part, way, h)
        return pltpu.make_async_copy(wps.at[at], wps_ref.at[at], ring_keep.at[way, part, h])

    def hop_ways(h):
        return [(part, way) for part in (0, 1) for way in (0, 1) if h < hops - 1 or part == way]

    def hop_on(k, h):
        for part, way in hop_ways(h - 1) if h > 0 else ():
            hop_arrival(k, part, way, h - 1).wait_recv()
            if k == 1:
                hop_keep(part, way, h - 1).start()
            if h < hops and (part, way) in hop_ways(h):
                hop(k, part, way, h).start()
        if h == 0:
            for part, way in hop_ways(0):
                hop(k, part, way, 0).start()

    def over(k):
        return remote(
            cot_ref.at[pl.ds(k * quarter, quarter)], cots.at[span(me * tokens + k * quarter, quarter)],
            over_send.at[k], over_recv.at[k], across,
        )

    def landed(start, size, send, recv, peer):
        here = cots.at[span(start, size)]
        return remote(here, here, send, recv, peer)

    def over_arrival(k):
        return landed(opposite * tokens + k * quarter, quarter, over_send.at[k], over_recv.at[k], across)

    def passing(k):
        return landed(opposite * tokens + k * quarter, quarter, pass_send.at[k], pass_recv.at[k], beside)

    def pass_arrival(k):
        return landed(far * tokens + k * quarter, quarter, pass_send.at[k], pass_recv.at[k], beside)

    def side():
        return remote(cot_ref, cots.at[span(me * tokens, tokens)], side_send.at[0], side_recv.at[0], beside)

    def side_arrival():
        return landed(next_door * tokens, tokens, side_send.at[0], side_recv.at[0], beside)

    def own_cot():
        return pltpu.make_async_copy(cot_ref, cots.at[span(me * tokens, tokens)], own_keep.at[0])

    def own_z():
        at = span(mine * rows, rows), pl.ds(*parts_of[1])
        return pltpu.make_async_copy(wps.at[at], wps_ref.at[at], own_keep.at[1])

    def pass_on(*pieces):
        for k in pieces:
            over_arrival(k).wait_recv()
            passing(k).start()

    def normalize(k):
        def some(i, _):
            at = span(me * tokens + k * quarter + i * 64, 64)
            squares = jnp.zeros((64, LANES), f32)
            for c in range(D // LANES):
                x = xg[at, c * LANES : (c + 1) * LANES].astype(f32)
                squares = squares + x * x
            inverse = lax.rsqrt(jnp.sum(squares, axis=-1, keepdims=True) / D + norm_eps)
            inverse = jnp.broadcast_to(inverse, (64, LANES))
            for c in range(D // LANES):
                cols = slice(c * LANES, (c + 1) * LANES)
                xg[at, cols] = (xg[at, cols].astype(f32) * inverse * flat_ref[c : c + 1, :]).astype(bf16)
            return 0

        lax.fori_loop(0, quarter // 64, some, 0)

    @pl.when(step == 0)
    def _():
        own_rows = span(me * tokens, tokens)
        greet((*ring, across, beside, askew))
        load = pltpu.make_async_copy(in_ref, xg.at[own_rows], own_keep.at[2])
        load.start()
        own_cot().start()
        mine_at = span(mine * rows, rows)
        ws[mine_at, :width] = wzx_ref[:, 1, :].astype(bf16)
        ws[mine_at, width:wide] = wbc_ref[...].astype(bf16)
        heads = wdt_ref.shape[0]
        unit = jnp.where(
            lax.broadcasted_iota(jnp.int32, (16, LANES), 0) == lax.broadcasted_iota(jnp.int32, (16, LANES), 1), 1.0, 0.0
        ).astype(bf16)
        steps_w = jnp.concatenate([wdt_ref[...], jnp.zeros((16 - heads, rows), f32)], axis=0).astype(bf16)
        ws[mine_at, wide:] = mm(steps_w, unit, TN).astype(bf16)
        load.wait()
        normalize(0)
        pl.semaphore_wait(pltpu.get_barrier_semaphore(), 5)
        started, kept = [], []

        def go(*args):
            copy = remote(*args)
            copy.start()
            started.append(copy)
            return copy

        latest = [None, None]

        def go_after(way, *args):
            if latest[way] is not None:
                latest[way].wait_send()
                started[:] = [copy for copy in started if copy is not latest[way]]
            latest[way] = go(*args)

        def keep(src, dst, sem):
            copy = pltpu.make_async_copy(src, dst, sem)
            copy.start()
            kept.append(copy)

        def arrived(part, way, h, block):
            first, size = cuts[part]
            at = span(block * rows + first, size)
            remote(
                ws.at[at], ws.at[at], lead_send.at[way, part, h], lead_recv.at[way, part, h], ring[way]
            ).wait_recv()
            keep(ws.at[at], ws_ref.at[at], lead_keep.at[way, part, h])

        def lead(h, parts=(0, 1)):
            for part in parts:
                first, size = cuts[part]
                for way in (0, 1):
                    block = ring_index(lax.rem(pos + (h if way else n - h), n), n)
                    here = ws.at[span(block * rows + first, size)]
                    if h > 0:
                        arrived(part, way, h - 1, block)
                    if h == hops - 1 and part != way:
                        continue
                    go_after(way, here, here, lead_send.at[way, part, h], lead_recv.at[way, part, h], ring[way])

        def x_over(k):
            at = span(me * tokens + k * quarter, quarter)
            go(xg.at[at], xg.at[at], x_over_send.at[k], x_over_recv.at[k], across)

        def x_pass(k):
            at = span(opposite * tokens + k * quarter, quarter)
            here = xg.at[at]
            remote(here, here, x_over_send.at[k], x_over_recv.at[k], across).wait_recv()
            go(here, here, x_pass_send.at[k], x_pass_recv.at[k], beside)
            keep(here, xg_ref.at[at], x_keep.at[k])

        def x_pass_lands(k):
            at = span(far * tokens + k * quarter, quarter)
            remote(xg.at[at], xg.at[at], x_pass_send.at[k], x_pass_recv.at[k], beside).wait_recv()
            keep(xg.at[at], xg_ref.at[at], x_keep.at[4 + k])

        lead(0, (0,))
        x_over(0)
        for k in (1, 2, 3):
            normalize(k)
            if k == 1:
                x_over(1)
        go(xg.at[own_rows], xg.at[own_rows], x_side_send.at[0], x_side_recv.at[0], beside)
        keep(xg.at[own_rows], xg_ref.at[own_rows], x_keep.at[8])
        wps[mine_at, :width] = wout_ref[...].astype(bf16)
        wps[mine_at, width:] = wzx_ref[:, 0, :].astype(bf16)
        lead(0, (1,))
        keep(ws.at[mine_at], ws_ref.at[mine_at], x_keep.at[9])
        own_z().start()
        halo[0:8, :] = jnp.zeros((8, wide), f32)
        state[...] = jnp.zeros_like(state)
        gate_ref[...] = jnp.zeros_like(gate_ref)
        parameter_rows(me, width, flat_ref, taps_ref, head_ref, chan_ref)
        set_heads(head_ref, head_t, until)
        lead(1)
        x_over(2)
        at = span(next_door * tokens, tokens)
        remote(xg.at[at], xg.at[at], x_side_send.at[0], x_side_recv.at[0], beside).wait_recv()
        keep(xg.at[at], xg_ref.at[at], x_keep.at[10])
        side().start()
        lead(2)
        x_over(3)
        x_pass(0)
        x_pass(1)
        for h in range(3, hops):
            lead(h)
        hop_on(0, 0)
        x_pass(2)
        over(0).start()
        x_pass_lands(0)
        x_pass_lands(1)
        x_pass(3)
        for part in (0, 1):
            arrived(part, part, hops - 1, ring_index(lax.rem(pos + n // 2, n), n))
        hop_on(1, 0)
        over(1).start()
        x_pass_lands(2)
        x_pass_lands(3)
        for copy in kept:
            copy.wait()
        for copy in started:
            copy.wait_send()

    def at_tick(tick):
        for k, times in enumerate(((1, 4, 6), (2, 5, 7))):
            for h in range(1, min(hops, 4)):
                pl.when(tick == times[h - 1])(functools.partial(hop_on, k, h))

        @pl.when(tick == 2)
        def _():
            over(2).start()

        @pl.when(tick == 4)
        def _():
            over(3).start()
            pass_on(0, 1)

        pl.when(tick == steps - 1)(functools.partial(pass_on, 2))

    @pl.when(step < norming)
    def _():
        def chunk(i, _):
            tick = 2 * step + i
            at_tick(tick)
            scan_step(
                width, tick, i, xg, ws, taps_ref, head_ref, chan_ref,
                v_ref, xc_ref, dr_ref, st_ref, halo, state, y_all, head_t, until, across_state, tails,
                functools.partial(pass_on, 3),
            )
            return 0

        lax.fori_loop(0, 2, chunk, 0)

    @pl.when(step == norming)
    def _():
        for k in (0, 1):
            for h in range(4, hops):
                hop_on(k, h)
        hop_on(0, hops)
        side_arrival().wait_recv()
        for k in range(4):
            pass_arrival(k).wait_recv()
        own_cot().wait()
        own_z().wait()

        def some(i, _):
            at = span(i * tall, tall)
            dn_all[at, :] = mm(cots[at, :], wps[:, :width]).astype(bf16)
            return 0

        lax.fori_loop(0, LEN // tall, some, 0)

    @pl.when(step == gating)
    def _():
        hop_on(1, hops)
        ones = jnp.ones((8, LANES), f32)

        def some(i, _):
            at = span(i * tall, tall)
            z_all[at, :] = mm(xg[at, :], wps[:, width:])
            for sub in range(tall // T):
                rows_at = span(i * tall + sub * T, T)
                squares = jnp.zeros((T, LANES), f32)
                inner = jnp.zeros((T, LANES), f32)
                for p in range(pairs):
                    cols = slice(p * LANES, (p + 1) * LANES)
                    z = z_all[rows_at, cols]
                    gated = y_all[rows_at, cols] * (z * sigmoid(z))
                    squares = squares + gated * gated
                    inner = inner + gated * chan_ref[0:1, cols] * dn_all[rows_at, cols].astype(f32)
                lanes = pl.ds(pl.multiple_of(i * tall + sub * T, T), T)
                sums[me, 0:4, lanes] = mm_exact(ones, squares, NT)[0:4]
                sums[me, 4:8, lanes] = mm_exact(ones, inner, NT)[4:8]
            return 0

        lax.fori_loop(0, LEN // tall, some, 0)

    @pl.when(step == forming - 1)
    def _():
        peers = ((beside, next_door), (across, opposite), (askew, far))
        for k, (peer, _) in enumerate(peers):
            remote(sums.at[me], sums.at[me], sum_send.at[k], sum_recv.at[k], peer).start()
        for h in range(hops):
            for part, way in hop_ways(h):
                for k in (0, 1):
                    hop(k, part, way, h).wait_send()
                hop_keep(part, way, h).wait()
        side().wait_send()
        for k in range(4):
            over(k).wait_send()
            passing(k).wait_send()
        for k, (peer, other) in enumerate(peers):
            remote(sums.at[other], sums.at[other], sum_send.at[k], sum_recv.at[k], peer).wait()
        red[...] = ((sums[0] + sums[1]) + sums[2]) + sums[3]

    @pl.when((step >= forming) & (step < products))
    def _():
        def some(i, _):
            first = (step - forming) * tall + i * ROWS
            lanes = pl.ds(pl.multiple_of(first, ROWS), ROWS)
            q_row = lax.rsqrt(red[0:4, lanes] / DI + norm_eps)
            k_row = q_row * q_row * q_row * red[4:8, lanes] / DI
            turned = jnp.concatenate([q_row, k_row], axis=0).T
            for sub in range(ROWS // T):
                rows_at = slice(sub * T, (sub + 1) * T)
                at = span(first + sub * T, T)
                q, kk = spread(turned[rows_at, 0:1]), spread(turned[rows_at, 4:5])
                for p in range(pairs):
                    cols = slice(p * LANES, (p + 1) * LANES)
                    z, y, dn = z_all[at, cols], y_all[at, cols], dn_all[at, cols].astype(f32)
                    gain = chan_ref[0:1, cols]
                    s = sigmoid(z)
                    sz = z * s
                    gated = y * sz
                    gq = gated * q
                    dg = q * gain * dn - gated * kk
                    gate_ref[:, cols] += jnp.sum((gq * dn).reshape(T // 8, 8, LANES), axis=0)
                    nl_all[at, cols] = (gq * gain).astype(bf16)
                    dz_all[at, cols] = (dg * y * (s + sz * (1.0 - s))).astype(bf16)
                    dn_all[at, cols] = (dg * sz).astype(bf16)
            branch_ref[span(i * ROWS, ROWS), :] = mm(nl_all[span(first, ROWS), :], wps[:, :width], NT).astype(bf16)
            return 0

        lax.fori_loop(0, 2, some, 0, unroll=2)

    def rows_out():
        return [
            pltpu.make_async_copy(src, dst, own_keep.at[2 + k])
            for k, (src, dst) in enumerate(((dz_all, dz_ref), (dn_all, dy_ref)))
        ]

    def early_out(i):
        at = span(i * ROWS, ROWS)
        return [
            pltpu.make_async_copy(src.at[at, pl.ds(0, width)], early_ref.at[at, pl.ds(k * width, width)], early_keep.at[k, i])
            for k, src in enumerate((ws, wps))
        ]

    @pl.when(step == products)
    def _():
        for copy in rows_out():
            copy.start()

        def some(i, _):
            at = span(i * ROWS, ROWS)
            lanes = pl.ds(pl.multiple_of(i * ROWS, ROWS), ROWS)
            grad = mm(xg[:, lanes], dz_all[...], TN)
            ws[at, :width] = grad.astype(bf16)
            share = jnp.zeros((ROWS, LANES), f32)
            for p in range(pairs):
                cols = slice(p * LANES, (p + 1) * LANES)
                w = wps[at, width + p * LANES : width + (p + 1) * LANES]
                share = share + grad[:, cols] * w.astype(f32)
            gain_ref[:, lanes] = mm_exact(jnp.ones((8, LANES), f32), share, NT)
            wps[at, :width] = mm(cots[:, lanes], nl_all[...], TN).astype(bf16)
            for copy in early_out(i):
                copy.start()
            return 0

        lax.fori_loop(0, D // ROWS, some, 0, unroll=2)
        for copy in rows_out():
            copy.wait()

        def done(i, _):
            for copy in early_out(i):
                copy.wait()
            return 0

        lax.fori_loop(0, D // ROWS, done, 0)


def parameter_rows(me, width, flat_ref, taps_ref, head_ref, chan_ref):
    pairs = width // LANES
    heads = width // P_SIZE
    taps_ref[...] = jnp.zeros_like(taps_ref)
    chan_ref[...] = jnp.zeros_like(chan_ref)
    for c in range(pairs):
        cols = slice(c * LANES, (c + 1) * LANES)
        chan_ref[0:1, cols] = flat_ref[pl.ds(GATE_ROW + pairs * me + c, 1), :]
        taps_ref[CONV : CONV + 1, cols] = flat_ref[pl.ds(BIAS_ROW + pairs * me + c, 1), :]
        for k in range(CONV):
            taps_ref[k : k + 1, cols] = flat_ref[pl.ds(TAPS_ROW + 4 * pairs * k + pairs * me + c, 1), :]
    for c in range(2):
        cols = slice(width + c * LANES, width + (c + 1) * LANES)
        taps_ref[CONV : CONV + 1, cols] = flat_ref[BIAS_BC_ROW + c : BIAS_BC_ROW + c + 1, :]
        for k in range(CONV):
            row = TAPS_BC_ROW + 2 * k + c
            taps_ref[k : k + 1, cols] = flat_ref[row : row + 1, :]
    both = jnp.concatenate([flat_ref[HEAD_ROW : HEAD_ROW + 1, :], flat_ref[HEAD_ROW + 1 : HEAD_ROW + 2, :]], axis=1)
    both = jnp.broadcast_to(both, (8, 2 * LANES))
    lane = lax.broadcasted_iota(jnp.int32, (2 * LANES, LANES), 0)
    head = lax.broadcasted_iota(jnp.int32, (2 * LANES, LANES), 1)

    def take(kind):
        match = (lane == 4 * heads * kind + heads * me + head) & (head < heads)
        return mm_exact(both, jnp.where(match, 1.0, 0.0).astype(f32))

    valid = lax.broadcasted_iota(jnp.int32, (8, LANES), 1) < heads
    row = lax.broadcasted_iota(jnp.int32, (8, LANES), 0)
    rates = jnp.where(valid, -jnp.exp(take(1)), 0.0)
    head_ref[...] = jnp.where(row == 0, take(0), jnp.where(row == 1, rates, 0.0))
    skip = mm_exact(take(2), picked(width).astype(f32), NT)
    chan_ref[1:2, :] = skip[0:1]


def picked(width):
    channel = lax.broadcasted_iota(jnp.int32, (width, LANES), 0)
    head = lax.broadcasted_iota(jnp.int32, (width, LANES), 1)
    return jnp.where((channel >= head * P_SIZE) & (channel < (head + 1) * P_SIZE), 1.0, 0.0).astype(bf16)


def scan_step(
    width, tick, i, xg, w_ref, taps_ref, head_ref, chan_ref,
    v_ref, xc_ref, dr_ref, st_ref, halo, state, y_all, head_t, until, across_state, tails, late_turn,
):
    pairs = width // LANES
    wide = width + 2 * NS
    mine = span(tick * ROWS, ROWS)
    dr_ref[span(i * ROWS, ROWS), :] = mm(xg[mine, :], w_ref[:, wide:])
    halo[8 : 8 + ROWS, :] = mm(xg[mine, :], w_ref[:, :wide])
    low_half = block_iota(1) < P_SIZE
    causal = block_iota(0) >= block_iota(1)

    def convolved(sub, block):
        cols = slice(block * LANES, (block + 1) * LANES)
        total = taps_ref[CONV : CONV + 1, cols]
        for k in range(CONV):
            first = 8 - (CONV - 1) + k + sub * T
            total = total + taps_ref[k : k + 1, cols] * halo[first : first + T, cols]
        rows = span(i * ROWS + sub * T, T)
        xc_ref[rows, cols] = total.astype(bf16)
        v_ref[rows, cols] = halo[8 + sub * T : 8 + (sub + 1) * T, cols].astype(bf16)
        return total * sigmoid(total)

    for sub in range(ROWS // T):
        rows = span(i * ROWS + sub * T, T)
        _, _, decay_t, dt, decay = head_rows(dr_ref, head_t, until, rows)
        b_low = convolved(sub, pairs).astype(bf16)
        c_low = convolved(sub, pairs + 1).astype(bf16)
        b_t = b_low.T
        scores = jnp.where(causal, mm(c_low, b_low, NT), 0.0)
        entering = state[...].astype(bf16)
        st_ref[i * (ROWS // T) + sub] = entering
        across_state[...] = mm(c_low, entering)
        for p in range(pairs):
            cols = slice(p * LANES, (p + 1) * LANES)
            x = convolved(sub, p)
            l1, l2 = spread(decay[:, 2 * p : 2 * p + 1]), spread(decay[:, 2 * p + 1 : 2 * p + 2])
            both = jnp.where(low_half, l1, l2)
            dtb = jnp.where(
                low_half, spread(dt[:, 2 * p : 2 * p + 1]), spread(dt[:, 2 * p + 1 : 2 * p + 2])
            )
            u = x * dtb
            m1 = scores * jnp.exp2(jnp.minimum(l1 - decay_t[2 * p : 2 * p + 1, :], 0.0))
            m2 = scores * jnp.exp2(jnp.minimum(l2 - decay_t[2 * p + 1 : 2 * p + 2, :], 0.0))
            mixing = jnp.concatenate([m1.astype(bf16), m2.astype(bf16)], axis=1)
            u_low = u.astype(bf16)
            zero = jnp.zeros_like(u_low)
            parts = jnp.concatenate(
                [jnp.where(low_half, u_low, zero), jnp.where(low_half, zero, u_low)], axis=0
            )
            last = both[T - 1 : T, :]
            y = mm(mixing, parts) + jnp.exp2(both) * across_state[:, cols] + chan_ref[1:2, cols] * x
            tails[:, cols] = (u * jnp.exp2(last - both)).astype(bf16)
            state[:, cols] = jnp.exp2(last) * state[:, cols]
            y_all[span(tick * ROWS + sub * T, T), cols] = y
        state[...] = state[...] + mm(b_t, tails[...])
        if sub == 0:
            pl.when(tick == LEN // ROWS - 1)(late_turn)
    halo[0:8, :] = halo[ROWS : ROWS + 8, :]


def ssd_forward(n, layer_input, out_grad, flat, w_zx, w_bc, w_dt, w_out):
    rows, width = w_out.shape
    tokens = layer_input.shape[0]
    length = 4 * tokens
    wide = width + 2 * NS
    tall = 2 * ROWS
    steps = length // tall
    forming = steps + 2
    products = forming + steps
    subs = tall // T
    assert length == LEN
    row = lambda m: pl.BlockSpec((tall, m), lambda i: (jnp.minimum(i, steps - 1), 0))
    form = lambda m: pl.BlockSpec((tall, m), lambda i: (jnp.clip(i - forming, 0, steps - 1), 0))
    whole = lambda a: pl.BlockSpec(a.shape, lambda i: (0,) * a.ndim, pipeline_mode=pl.Buffered(1))
    fixed = lambda m: pl.BlockSpec((8, m), lambda i: (0, 0))
    anywhere = pl.BlockSpec(memory_space=pl.ANY)
    vm, dma = pltpu.VMEM, pltpu.SemaphoreType.DMA
    hops, lead = dma((2, 2, 2, n // 2)), dma((2, 2, n // 2))
    shape = lambda dims, dtype: jax.ShapeDtypeStruct(dims, dtype)
    return pl.pallas_call(
        functools.partial(forward_body, n, rows, tokens, width),
        grid=(products + 1,),
        in_specs=[anywhere, anywhere, *(whole(a) for a in (flat, w_zx, w_bc, w_dt, w_out))],
        out_specs=[
            row(wide), row(wide), row(LANES), pl.BlockSpec((subs, NS, width), lambda i: (jnp.minimum(i, steps - 1), 0, 0)),
            anywhere, anywhere, form(D), anywhere,
            fixed(width), fixed(D), anywhere, anywhere, anywhere, *(fixed(m) for m in (wide, LANES, width)),
        ],
        out_shape=[
            shape((length, wide), bf16), shape((length, wide), bf16), shape((length, LANES), f32),
            shape((length // T, NS, width), bf16), shape((length, width), bf16), shape((length, width), bf16),
            shape((length, D), bf16), shape((D, 2 * width), bf16), shape((8, width), f32), shape((8, D), f32),
            shape((length, D), bf16), shape((D, wide + LANES), bf16), shape((D, 2 * width), bf16),
            *(shape((8, m), f32) for m in (wide, LANES, width)),
        ],
        scratch_shapes=[
            vm((ROWS + 8, wide), f32), vm((NS, width), f32), vm((length, width), f32), vm((length, width), f32),
            *(vm((length, width), bf16) for _ in range(3)),
            vm((length, D), bf16), vm((length, D), bf16), vm((D, wide + LANES), bf16), vm((D, 2 * width), bf16),
            vm((4, 8, length), f32), vm((8, length), f32), vm((2, HEADS, LANES), f32), vm((3 * T, LANES), bf16),
            vm((T, width), f32), vm((T, width), bf16),
            dma((4,)), dma((2, D // ROWS)), lead, lead, lead, dma((11,)), dma((4,)), dma((4,)), dma((1,)), dma((1,)),
            dma((4,)), dma((4,)), lead, hops, hops, dma((4,)), dma((4,)),
            dma((1,)), dma((1,)), dma((4,)), dma((4,)), dma((3,)), dma((3,)),
        ],
        compiler_params=pltpu.CompilerParams(collective_id=2, has_side_effects=True, vmem_limit_bytes=ROOM),
        name="layer_forward",
    )(layer_input, out_grad, flat, w_zx, w_bc, w_dt, w_out)


def backward_body(
    n, own_rows, tokens, width,
    dy_ref, v_ref, xc_ref, dr_ref, st_ref, gate_ref, taps_ref, head_ref, chan_ref, early_ref, branch_ref,
    d_ref, small_ref, oearly_ref, obranch_ref,
    dxh, dstate, yst, bds, dyeb, utb, products, turn, acc, hacc, pick_ref, pick_t, fades, head_t, until_ref, reach_ref,
    own, slots, near, held, over_slot,
    load_sem, ring_send, ring_recv, near_send, near_recv, over_send, over_recv,
):
    pairs = width // LANES
    wide = width + 2 * NS
    step = pl.program_id(0)
    steps = LEN // ROWS
    subs = ROWS // T
    pos, ring, me, across, beside = neighbours(n)
    opposite = lax.rem(me + 2, 4)
    next_door = me + 1 - 2 * lax.rem(me, 2)
    far = lax.rem(next_door + 2, 4)
    half = tokens // 2
    cuts = cut_rows(own_rows)

    def block_at(way, count):
        return ring_index(lax.rem(pos + (count if way else n - count), n), n)

    def hop(k, way, h):
        first, size = cuts[way]
        if h == 0:
            src = early_ref.at[span(block_at(way, 1) * own_rows + first, size), pl.ds(k * width, width)]
        else:
            src = slots[way][k].at[h - 1]
        return remote(
            src, slots[way][k].at[h], ring_send.at[way, k, h], ring_recv.at[way, k, h], ring[way]
        )

    def near_copy(turned, part):
        start = (next_door if turned else far) * tokens + part * half
        return remote(
            branch_ref.at[span(start, half)], near.at[turned, part],
            near_send.at[turned, part], near_recv.at[turned, part], beside,
        )

    def held_copy(turned, part):
        start = (me if turned else opposite) * tokens + part * half
        return pltpu.make_async_copy(
            branch_ref.at[span(start, half)], held.at[turned, part], load_sem.at[2 * turned + part]
        )

    def over_copy(part):
        return remote(held.at[0, part], over_slot.at[part], over_send.at[part], over_recv.at[part], across)

    def own_copy():
        return pltpu.make_async_copy(early_ref, own, load_sem.at[4])

    def ring_turn(k, h):
        for way in (0, 1):
            first, size = cuts[way]
            hop(k, way, h).wait_recv()
            block = block_at(way, 2 + h) if h < n - 2 else block_at(way, 0)

            tile = strip(size)

            def some(i, _, way=way, first=first, block=block, tile=tile):
                cols = slice(k * width, (k + 1) * width)
                came = slots[way][k][h, span(i * tile, tile), :]
                mine = own[span(block * own_rows + first + i * tile, tile), cols]
                if h < n - 2:
                    slots[way][k][h, span(i * tile, tile), :] = came + mine
                else:
                    oearly_ref[span(first + i * tile, tile), cols] = came.astype(f32) + mine.astype(f32)
                return 0

            lax.fori_loop(0, size // tile, some, 0)
            if h < n - 2:
                hop(k, way, h + 1).start()

    def ring_poll(k, tick):
        for h in range(n - 1):
            pl.when(tick == min(h + 1, steps - 1))(functools.partial(ring_turn, k, h))

    def add_near(turned):
        for part in (0, 1):
            held_copy(turned, part).wait()
            near_copy(turned, part).wait_recv()

            def some(i, _, part=part):
                at = span(i * 32, 32)
                held[turned, part, at, :] = held[turned, part, at, :] + near[turned, part, at, :]
                return 0

            lax.fori_loop(0, half // 32, some, 0)
            if not turned:
                over_copy(part).start()

    @pl.when(step == 0)
    def _():
        enter((*ring, across, beside))
        for way in (0, 1):
            hop(0, way, 0).start()
        for turned in (0, 1):
            for part in (0, 1):
                near_copy(turned, part).start()
                held_copy(turned, part).start()
        own_copy().start()
        dxh[T : T + 8, :] = jnp.zeros((8, wide), f32)
        dstate[...] = jnp.zeros_like(dstate)
        acc[...] = jnp.zeros_like(acc)
        hacc[...] = jnp.zeros_like(hacc)
        turn[...] = jnp.zeros_like(turn)
        pick_ref[...] = picked(width)
        channel = lax.broadcasted_iota(jnp.int32, (HEADS, width), 1)
        head = lax.broadcasted_iota(jnp.int32, (HEADS, width), 0)
        mine = (channel >= head * P_SIZE) & (channel < (head + 1) * P_SIZE)
        pick_t[...] = jnp.where(mine, 1.0, 0.0).astype(bf16)
        set_heads(head_ref, head_t, until_ref)
        from_here = jnp.where(block_iota(0) >= block_iota(1), 1.0, 0.0).astype(bf16)
        after = jnp.where(block_iota(0) < block_iota(1), 1.0, 0.0).astype(bf16)
        for k, matrix in enumerate((from_here, from_here, after, after)):
            reach_ref[k * T : (k + 1) * T, :] = matrix
        products[3 * T :, :] = jnp.zeros((HEADS, width), bf16)

    low_half = block_iota(1) < P_SIZE
    row_at, col_at = block_iota(0), block_iota(1)
    until = row_at <= col_at
    pair_lane = lax.broadcasted_iota(jnp.int32, (8, 2 * T), 1)
    pair_row = lax.broadcasted_iota(jnp.int32, (8, 2 * T), 0)
    each = jnp.where(lax.div(pair_lane, T) == pair_row, 1.0, 0.0).astype(bf16)
    ones = jnp.ones((8, T), bf16)

    def add(index, cols, value):
        acc[index, :, cols] += jnp.sum(value.reshape(T // 8, 8, LANES), axis=0)

    def conv_back(rows, block, d_act, xc, s, act):
        cols = slice(block * LANES, (block + 1) * LANES)
        dxh[0:T, cols] = d_act * (s + act * (1.0 - s))
        v = v_ref[rows, cols].astype(f32)
        total = None
        for m in range(CONV):
            moved = dxh[m : m + T, cols]
            if m == 0:
                add(CONV, cols, moved)
            add(CONV - 1 - m, cols, v * moved)
            term = taps_ref[CONV - 1 - m : CONV - m, cols] * moved
            total = term if total is None else total + term
        d_ref[rows, cols] = total.astype(bf16)

    def work(i, _):
        tick = 2 * step + i
        chunk = 1 - i

        @pl.when(tick == 1)
        def _():
            own_copy().wait()
            add_near(0)

        pl.when(tick == 2)(functools.partial(add_near, 1))
        ring_poll(0, tick)
        for sub in reversed(range(subs)):
            rows = span(chunk * ROWS + sub * T, T)
            block_state = chunk * subs + sub
            raw_t, dt_t, decay_t, dt, decay = head_rows(dr_ref, head_t, until_ref, rows)
            b_cols = slice(width, width + NS)
            c_cols = slice(width + NS, width + 2 * NS)
            b_xc, c_xc = xc_ref[rows, b_cols].astype(f32), xc_ref[rows, c_cols].astype(f32)
            b_s, c_s = sigmoid(b_xc), sigmoid(c_xc)
            b_act, c_act = b_xc * b_s, c_xc * c_s
            b_low, c_low = b_act.astype(bf16), c_act.astype(bf16)
            c_t = c_low.T
            scores_t = jnp.where(until, mm(b_low, c_low, NT), 0.0)
            ds_low = dstate[...].astype(bf16)
            yst[...] = mm(c_low, st_ref[block_state])
            bds[...] = mm(b_low, ds_low)
            d_scores = jnp.zeros((T, LANES), f32)
            for p in range(pairs):
                cols = slice(p * LANES, (p + 1) * LANES)
                dy_low = dy_ref[rows, cols]
                dy = dy_low.astype(f32)
                xc = xc_ref[rows, cols].astype(f32)
                xs = sigmoid(xc)
                x = xc * xs
                l1, l2 = spread(decay[:, 2 * p : 2 * p + 1]), spread(decay[:, 2 * p + 1 : 2 * p + 2])
                both = jnp.where(low_half, l1, l2)
                dtb = jnp.where(
                    low_half, spread(dt[:, 2 * p : 2 * p + 1]), spread(dt[:, 2 * p + 1 : 2 * p + 2])
                )
                u = x * dtb
                last = both[T - 1 : T, :]
                e1 = jnp.exp2(jnp.minimum(decay_t[2 * p : 2 * p + 1, :] - l1, 0.0))
                e2 = jnp.exp2(jnp.minimum(decay_t[2 * p + 1 : 2 * p + 2, :] - l2, 0.0))
                zero = jnp.zeros_like(dy_low)
                dy_parts = jnp.concatenate(
                    [jnp.where(low_half, dy_low, zero), jnp.where(low_half, zero, dy_low)], axis=0
                )
                du_in = mm(
                    jnp.concatenate([(scores_t * e1).astype(bf16), (scores_t * e2).astype(bf16)], axis=1), dy_parts
                )
                d_mix = mm(u.astype(bf16), dy_parts, NT)
                d1, d2 = d_mix[:, :T] * e1, d_mix[:, T:] * e2
                d_scores = d_scores + d1 + d2
                held_pairs = jnp.concatenate([(d1 * scores_t).astype(bf16), (d2 * scores_t).astype(bf16)], axis=1)
                reached_by = mm(ones, held_pairs)
                leaving = mm(each, held_pairs, NT)
                turn[2 * p : 2 * p + 1, :] = reached_by[0:1, :T] - leaving[0:1]
                turn[2 * p + 1 : 2 * p + 2, :] = reached_by[0:1, T:] - leaving[1:2]
                tail = jnp.exp2(last - both)
                fades[0:1, cols] = jnp.exp2(last)
                dye = dy * jnp.exp2(both)
                du_out = tail * bds[:, cols]
                du = du_in + du_out
                products[0:T, cols] = (dye * yst[:, cols]).astype(bf16)
                products[T : 2 * T, cols] = (u * du_out).astype(bf16)
                products[2 * T : 3 * T, cols] = (x * du).astype(bf16)
                dyeb[:, cols] = dye.astype(bf16)
                utb[:, cols] = (u * tail).astype(bf16)
                add(CONV + 1, cols, dy * x)
                conv_back(rows, p, dtb * du + chan_ref[1:2, cols] * dy, xc, xs, x)
            d_scores = jnp.where(until, d_scores, 0.0).astype(bf16)
            d_b = mm(d_scores, c_low) + mm(utb[...], ds_low, NT)
            d_c = mm(d_scores, b_low, TN) + mm(dyeb[...], st_ref[block_state], NT)
            conv_back(rows, pairs, d_b, b_xc, b_s, b_act)
            conv_back(rows, pairs + 1, d_c, c_xc, c_s, c_act)
            fade = fades[0:1, :]
            before_ds = dstate[...]
            through = jnp.sum(before_ds * st_ref[block_state].astype(f32), axis=0, keepdims=True) * fade
            products[3 * T : 3 * T + HEADS, :] = jnp.broadcast_to(through, (HEADS, width)).astype(bf16)
            dstate[...] = fade * before_ds + mm(c_t, dyeb[...])
            by_head = mm(pick_t[...], products[...], NT)
            inside = pieces(turn[...] + by_head[:, :T], 2)
            outside = pieces(by_head[:, T : 2 * T], 2)
            reached = mm(jnp.concatenate([inside, outside], axis=1), reach_ref[...])
            reached = reached + jnp.broadcast_to(by_head[:, 3 * T : 3 * T + 1], (HEADS, T))
            d_raw = (head_t[1] * reached + by_head[:, 2 * T : 3 * T]) * sigmoid(raw_t)
            d_ref[rows, wide:] = columns_of(d_raw).astype(bf16)
            hacc[0] += d_raw
            hacc[1] += dt_t * reached
            dxh[T : T + 8, :] = dxh[0:8, :]
            if sub == 1:
                @pl.when(tick == 0)
                def _():
                    for way in (0, 1):
                        hop(1, way, 0).start()

                ring_poll(1, tick)
        return 0

    lax.fori_loop(0, 2, work, 0)

    @pl.when(step == steps // 2 - 1)
    def _():
        total = lambda a: jnp.sum(a, axis=0, keepdims=True)
        for k in range(CONV + 1):
            small_ref[k : k + 1, :] = total(acc[k])
        small_ref[CONV + 1 : CONV + 2, :width] = total(gate_ref[...])
        small_ref[CONV + 1 : CONV + 2, width : width + LANES] = total(columns_of(hacc[0]))
        small_ref[CONV + 1 : CONV + 2, width + LANES :] = total(columns_of(hacc[1])) * head_ref[1:2, :]
        small_ref[CONV + 2 :, :] = jnp.zeros((2, wide), f32)
        skip = mm_exact(acc[CONV + 1, :, :width], pick_ref[...].astype(f32))
        small_ref[CONV + 3 : CONV + 4, 512 : 512 + LANES] = total(skip)
        for part in (0, 1):
            over_copy(part).wait_recv()

            def some(i, _, part=part):
                at = span(part * half + i * 32, 32)
                here = span(i * 32, 32)
                total = held[1, part, here, :].astype(f32) + over_slot[part, here, :].astype(f32)
                obranch_ref[at, :] = total.astype(bf16)
                return 0

            lax.fori_loop(0, half // 32, some, 0)
        for part in (0, 1):
            over_copy(part).wait_send()
            for turned in (0, 1):
                near_copy(turned, part).wait_send()
        for h in range(n - 1):
            for k in (0, 1):
                for way in (0, 1):
                    hop(k, way, h).wait_send()


def ssd_backward(n, dy, v, xc, dr, st, gate, taps, head, chan, early, branch):
    length, width = dy.shape
    wide = width + 2 * NS
    tall = 2 * ROWS
    steps = length // tall
    subs = tall // T
    own_rows, tokens = D // n, length // 4
    half = tokens // 2
    row = lambda m: pl.BlockSpec((tall, m), lambda i: (steps - 1 - i, 0))
    whole = lambda a: pl.BlockSpec(a.shape, lambda i: (0,) * a.ndim, pipeline_mode=pl.Buffered(1))
    fixed = lambda *shape: pl.BlockSpec(shape, lambda i: (0,) * len(shape))
    anywhere = pl.BlockSpec(memory_space=pl.ANY)
    vm, dma = pltpu.VMEM, pltpu.SemaphoreType.DMA
    return pl.pallas_call(
        functools.partial(backward_body, n, own_rows, tokens, width),
        grid=(steps,),
        in_specs=[
            row(width), row(wide), row(wide), row(LANES),
            pl.BlockSpec((subs, NS, width), lambda i: (steps - 1 - i, 0, 0)),
            whole(gate), whole(taps), whole(head), whole(chan), anywhere, anywhere,
        ],
        out_specs=[
            row(wide + LANES), fixed(8, wide), fixed(own_rows, 2 * width), fixed(tokens, D),
        ],
        out_shape=[
            jax.ShapeDtypeStruct((length, wide + LANES), bf16),
            jax.ShapeDtypeStruct((8, wide), f32),
            jax.ShapeDtypeStruct((own_rows, 2 * width), f32),
            jax.ShapeDtypeStruct((tokens, D), bf16),
        ],
        scratch_shapes=[
            vm((T + 8, wide), f32), vm((NS, width), f32), vm((T, width), f32), vm((T, width), f32),
            vm((T, width), bf16), vm((T, width), bf16), vm((3 * T + HEADS, width), bf16),
            vm((HEADS, T), f32), vm((CONV + 2, 8, wide), f32), vm((2, HEADS, T), f32),
            vm((width, LANES), bf16), vm((HEADS, width), bf16), vm((8, width), f32), vm((2, HEADS, LANES), f32),
            vm((3 * T, LANES), bf16), vm((4 * T, LANES), bf16),
            vm((D, 2 * width), bf16),
            [[vm((n - 1, size, width), bf16) for _ in (0, 1)] for _, size in cut_rows(own_rows)],
            vm((2, 2, half, D), bf16), vm((2, 2, half, D), bf16), vm((2, half, D), bf16),
            dma((5,)), dma((2, 2, n - 1)), dma((2, 2, n - 1)), dma((2, 2)), dma((2, 2)), dma((2,)), dma((2,)),
        ],
        compiler_params=pltpu.CompilerParams(
            collective_id=3, has_side_effects=True, vmem_limit_bytes=ROOM
        ),
        name="layer_backward",
    )(dy, v, xc, dr, st, gate, taps, head, chan, early, branch)


def reduce_body(
    n, rows, tokens, starts,
    xg_ref, d_ref, dz_ref, wp_ref, w_ref, small_ref, flat_ref, gain_ref,
    oxs_ref, oback_ref, bc_ref, oflat_ref,
    xg, d, dz, wz, w, work, grads, slots, staged, near, over, smalls, tens, bc_slot,
    load_sem, ring_send, ring_recv, near_send, near_recv, over_send, over_recv,
    small_send, small_recv, ten_send, ten_recv, bc_send, bc_recv,
):
    pos, ring, me, across, beside = neighbours(n)
    cuts = cut_rows(rows)
    core = lax.rem(me, 2)
    opposite = lax.rem(me + 2, 4)
    next_door = me + 1 - 2 * core
    far = lax.rem(next_door + 2, 4)
    half = tokens // 2
    late = d.shape[1]
    width = dz.shape[1]
    tile = 2 * LANES
    tiles = D // tile
    columns = [pl.ds(lo, hi - lo) for lo, hi in starts]
    sources = [(d_ref.at[:, columns[0]], d.at[:, columns[0]])]
    sources += [(xg_ref.at[:, pl.ds(i * tile, tile)], xg.at[:, pl.ds(i * tile, tile)]) for i in range(tiles)]
    sources += [(d_ref.at[:, some], d.at[:, some]) for some in columns[1:]]
    sources += [
        (dz_ref, dz), (w_ref, w), (wp_ref.at[:, pl.ds(width, width)], wz), (small_ref, smalls.at[pos]),
    ]
    loads = [pltpu.make_async_copy(src, dst, load_sem.at[k]) for k, (src, dst) in enumerate(sources)]
    for load in loads:
        load.start()
    askew = {"tensor": far}
    enter((*ring, across, beside, askew))
    started = []

    def go(*args):
        copy = remote(*args)
        copy.start()
        started.append(copy)

    def block_at(way, count):
        return ring_index(lax.rem(pos + (count if way else n - count), n), n)

    def hop(k, way, h):
        lo, hi = starts[k]
        first, size = cuts[way]
        if h == 0:
            src = grads.at[span(block_at(way, 1) * rows + first, size), pl.ds(lo, hi - lo)]
        else:
            src = slots[way][k].at[h - 1]
        return remote(
            src, slots[way][k].at[h], ring_send.at[way, k, h], ring_recv.at[way, k, h], ring[way]
        )

    def product(k):
        lo, hi = starts[k]

        def some(i, _):
            at = pl.ds(pl.multiple_of(i * tile, tile), tile)
            if k == 0:
                pltpu.make_async_copy(xg_ref.at[:, at], xg.at[:, at], load_sem.at[1 + i]).wait()
            grads[at, lo:hi] = mm(xg[:, at], d[:, lo:hi], TN).astype(bf16)
            return 0

        loads[0 if k == 0 else tiles + k].wait()
        lax.fori_loop(0, tiles, some, 0)
        for way in (0, 1):
            hop(k, way, 0).start()

    def near_copy(turned, part):
        return remote(
            staged.at[turned, part], near.at[turned, part],
            near_send.at[turned, part], near_recv.at[turned, part], beside,
        )

    def over_copy(part):
        return remote(near.at[0, part], over.at[part], over_send.at[part], over_recv.at[part], across)

    def ring_turn(k, h, before=None):
        lo, hi = starts[k]
        for way in (0, 1):
            first, size = cuts[way]
            slot = slots[way][k].at[h]
            remote(slot, slot, ring_send.at[way, k, h], ring_recv.at[way, k, h], ring[way]).wait_recv()
            block = block_at(way, 2 + h) if h < n - 2 else block_at(way, 0)

            tile = strip(size)

            def some(i, _, way=way, first=first, block=block, tile=tile):
                came = slots[way][k][h, span(i * tile, tile), :]
                mine = grads[span(block * rows + first + i * tile, tile), lo:hi]
                if h < n - 2:
                    slots[way][k][h, span(i * tile, tile), :] = came + mine
                else:
                    oxs_ref[span(first + i * tile, tile), lo:hi] = came.astype(f32) + mine.astype(f32)
                return 0

            lax.fori_loop(0, size // tile, some, 0)
            if h < n - 2:
                if before is not None:
                    hop(before[0], way, before[1]).wait_send()
                hop(k, way, h + 1).start()

    def small_hop(way, h):
        here = smalls.at[lax.rem(pos + (h if way else n - h), n)]
        go(here, here, small_send.at[way, h], small_recv.at[way, h], ring[way])

    def small_lands(way, h):
        here = smalls.at[lax.rem(pos + (h + 1 if way else n - h - 1), n)]
        remote(here, here, small_send.at[way, h], small_recv.at[way, h], ring[way]).wait_recv()

    for k in range(len(starts)):
        product(k)
    for load in loads[tiles + len(starts) :]:
        load.wait()
    turns = {0: [(0, 0)], 1: [(1, 0), (2, 0)], 2: [(0, 1)], 3: [(1, 1), (2, 1)], 4: [(0, 2)], 5: [(1, 2), (2, 2)], 6: [(0, 3)], 7: [(1, 3), (2, 3)]}
    taken = [sum(k == group for some in turns.values() for k, _ in some) for group in range(len(starts))]

    def block(i, _):
        which, part = lax.div(i, 2), lax.rem(i, 2)
        own = lax.rem(which, 2)
        turned = lax.div(which, 2)
        target = lax.rem(next_door + own * (me - next_door) + 2 * (1 - turned), 4)
        at = span(target * tokens + part * half, half)
        total = mm(dz[at, :], wz[...], NT) + mm(d[at, :], w[...], NT)
        work[...] = total

        @pl.when(own == 0)
        def _():
            staged[turned, part] = work[...].astype(bf16)
            near_copy(turned, part).start()

        @pl.when(own == 1)
        def _():
            near_copy(turned, part).wait_recv()

        @pl.when(which == 1)
        def _():
            near[0, part] = (work[...] + near[0, part].astype(f32)).astype(bf16)
            over_copy(part).start()

        @pl.when(which == 3)
        def _():
            near[1, part] = (work[...] + near[1, part].astype(f32)).astype(bf16)

        for at_block, some in turns.items():

            @pl.when(i == at_block)
            def _(some=some):
                for k, h in some:
                    ring_turn(k, h)

        return 0

    lax.fori_loop(0, 8, block, 0)
    for i in range(tiles):
        share = jnp.zeros((tile, LANES), f32)
        for c in range(late // LANES):
            cols = slice(c * LANES, (c + 1) * LANES)
            at = slice(i * tile, (i + 1) * tile)
            share = share + grads[at, cols].astype(f32) * w[at, cols].astype(f32)
        total = mm_exact(jnp.ones((8, LANES), f32), share, NT)[0:1] + gain_ref[0:1, i * tile : (i + 1) * tile]
        for c in range(2 * i, 2 * i + 2):
            row, col = 6 + c // 8, (c % 8) * LANES
            part = total[:, (c - 2 * i) * LANES : (c - 2 * i + 1) * LANES]
            smalls[pos, row : row + 1, col : col + LANES] = part / flat_ref[c : c + 1, :]

    rest = [(k, h) for h in range(n - 1) for k in (0, 1, 2) if h >= taken[k]]
    rest.sort(key=lambda turn: turn[1] - taken[turn[0]])

    def small_step(s):
        for way in (0, 1):
            if s > 0 and (way == 0 or s < n // 2):
                small_lands(way, s - 1)
            if s < n // 2 - way:
                small_hop(way, s)

    small_step(0)
    steps_done = 1
    latest, left = None, set()
    for at, (k, h) in enumerate(rest):
        ring_turn(k, h, latest)
        if h < n - 2:
            left.add(latest)
            latest = (k, h + 1)
        if (k, h) == (0, n - 2):
            bc_slot[0] = oxs_ref[:, starts[0][0] : starts[0][0] + 2 * NS]
            go(bc_slot.at[0], bc_slot.at[1], bc_send.at[0], bc_recv.at[0], beside)
        if at % 2 == 1 and steps_done < n // 2:
            small_step(steps_done)
            steps_done += 1
    for s in range(steps_done, n // 2):
        small_step(s)
    small_lands(0, n // 2 - 1)

    total = smalls[0]
    for i in range(1, n):
        total = total + smalls[i]
    tens[me] = total
    others = ((beside, next_door), (across, opposite), (askew, far))
    for k, (peer, _) in enumerate(others):
        go(tens.at[me], tens.at[me], ten_send.at[k], ten_recv.at[k], peer)
    remote(bc_slot.at[1], bc_slot.at[1], bc_send.at[0], bc_recv.at[0], beside).wait_recv()
    bc_slot[2] = bc_slot[0] + bc_slot[1]
    go(bc_slot.at[2], bc_slot.at[3], bc_send.at[1], bc_recv.at[1], across)
    for part in (0, 1):
        over_copy(part).wait_recv()

        def some(i, _, part=part):
            at = span(part * half + i * 32, 32)
            here = span(i * 32, 32)
            oback_ref[at, :] = (near[1, part, here, :].astype(f32) + over[part, here, :].astype(f32)).astype(bf16)
            return 0

        lax.fori_loop(0, half // 32, some, 0)
    for k, (peer, target) in enumerate(others):
        here = tens.at[target]
        remote(here, here, ten_send.at[k], ten_recv.at[k], peer).wait_recv()
    flat_gradients(width, tens, oflat_ref)
    remote(bc_slot.at[3], bc_slot.at[3], bc_send.at[1], bc_recv.at[1], across).wait_recv()
    bc_ref[...] = bc_slot[2] + bc_slot[3]
    for part in (0, 1):
        over_copy(part).wait_send()
        for turned in (0, 1):
            near_copy(turned, part).wait_send()
    for k in range(len(starts)):
        for way in (0, 1):
            for h in range(n - 1):
                if (k, h) not in left:
                    hop(k, way, h).wait_send()
    for copy in started:
        copy.wait_send()


def flat_gradients(width, tens, out_ref):
    pairs = width // LANES
    heads = width // P_SIZE

    def sums(row, col):
        total = tens[0, row : row + 1, col : col + LANES]
        for t in range(1, 4):
            total = total + tens[t, row : row + 1, col : col + LANES]
        return total

    def put(row, value):
        out_ref[row : row + 1, :] = value

    for c in range(D // LANES):
        put(c, sums(6 + c // 8, (c % 8) * LANES))
    for t in range(4):
        for c in range(pairs):
            cols = slice(c * LANES, (c + 1) * LANES)
            put(GATE_ROW + pairs * t + c, tens[t, CONV + 1 : CONV + 2, cols])
            put(BIAS_ROW + pairs * t + c, tens[t, CONV : CONV + 1, cols])
            for k in range(CONV):
                put(TAPS_ROW + 4 * pairs * k + pairs * t + c, tens[t, k : k + 1, cols])
    for c in range(2):
        put(BIAS_BC_ROW + c, sums(CONV, width + c * LANES))
        for k in range(CONV):
            put(TAPS_BC_ROW + 2 * k + c, sums(k, width + c * LANES))
    kinds = ((CONV + 1, width), (CONV + 1, width + LANES), (CONV + 3, 512))
    rows = [tens[t, row : row + 1, col : col + LANES] for row, col in kinds for t in range(4)]
    rows = jnp.concatenate(rows + [jnp.zeros((16 - len(rows), LANES), f32)], axis=0)
    lane = lax.broadcasted_iota(jnp.int32, (LANES, 2 * LANES), 1)
    entry = lax.broadcasted_iota(jnp.int32, (LANES, 2 * LANES), 0)
    spread_out = mm_exact(rows, jnp.where(lax.rem(lane, heads) == entry, 1.0, 0.0).astype(f32))
    at = lax.broadcasted_iota(jnp.int32, (16, 2 * LANES), 1)
    source = lax.broadcasted_iota(jnp.int32, (16, 2 * LANES), 0)
    line = jnp.sum(jnp.where(lax.div(at, heads) == source, spread_out, 0.0), axis=0, keepdims=True)
    put(HEAD_ROW, line[:, :LANES])
    put(HEAD_ROW + 1, line[:, LANES:])


def reduce_all(n, xg, d, dz, wp, w, small, flat, gain):
    rows, tokens = D // n, dz.shape[0] // 4
    width, late = dz.shape[1], d.shape[1]
    starts = ((width, late), (0, width // 2), (width // 2, width))
    half = tokens // 2
    dma, vm = pltpu.SemaphoreType.DMA, pltpu.VMEM
    anywhere = pl.BlockSpec(memory_space=pl.ANY)
    inside = pl.BlockSpec(memory_space=pltpu.VMEM)
    return pl.pallas_call(
        functools.partial(reduce_body, n, rows, tokens, starts),
        in_specs=[anywhere] * 6 + [inside] * 2,
        out_specs=[inside] * 4,
        out_shape=[
            jax.ShapeDtypeStruct((rows, late), f32),
            jax.ShapeDtypeStruct((tokens, D), bf16),
            jax.ShapeDtypeStruct((rows, 2 * NS), f32),
            jax.ShapeDtypeStruct((FLAT_ROWS, LANES), f32),
        ],
        scratch_shapes=[
            vm(xg.shape, bf16), vm(d.shape, bf16), vm(dz.shape, bf16), vm((D, width), bf16),
            vm((D, late), bf16),
            vm((half, D), f32), vm((D, late), bf16),
            [[vm((n - 1, size, hi - lo), bf16) for lo, hi in starts] for _, size in cut_rows(rows)],
            vm((2, 2, half, D), bf16), vm((2, 2, half, D), bf16), vm((2, half, D), bf16),
            vm((n, *small.shape), f32), vm((4, *small.shape), f32), vm((4, rows, 2 * NS), f32),
            dma((13,)), dma((2, 3, n - 1)), dma((2, 3, n - 1)), dma((2, 2)), dma((2, 2)), dma((2,)), dma((2,)),
            dma((2, n // 2)), dma((2, n // 2)), dma((3,)), dma((3,)), dma((2,)), dma((2,)),
        ],
        compiler_params=pltpu.CompilerParams(
            collective_id=1, has_side_effects=True, vmem_limit_bytes=46 * 2**20
        ),
        name="reduce_all",
    )(xg, d, dz, wp, w, small, flat, gain)


def adamw_step(weight, first, second, grad, rate, decay):
    first_new = beta_first * first + (1.0 - beta_first) * grad
    second_new = beta_second * second + (1.0 - beta_second) * grad * grad
    hat_first = first_new * (1.0 / (1.0 - beta_first**STEP))
    hat_second = second_new * (1.0 / (1.0 - beta_second**STEP))
    weight_new = weight - rate * (hat_first / (jnp.sqrt(hat_second) + adam_eps) + decay * weight)
    return (weight_new, first_new, second_new)


def finish_body(
    width, heads,
    in_ref, cot_ref, branch_ref, back_ref, flat_ref, early_ref, late_ref, bcg_ref,
    zx_ref, zx1_ref, zx2_ref, bc_ref, bc1_ref, bc2_ref, out_ref, out1_ref, out2_ref, late_all_ref, dt_ref, dt1_ref, dt2_ref,
    layer_ref, grad_ref, zxn_ref, zx1n_ref, zx2n_ref, bcn_ref, bc1n_ref, bc2n_ref,
    outn_ref, out1n_ref, out2n_ref, dtn_ref, dt1n_ref, dt2n_ref,
):
    def update(refs, news, grad):
        fresh = adamw_step(*(ref[...] for ref in refs), grad, matrix_rate, matrix_decay)
        for ref, value in zip(news, fresh):
            ref[...] = value

    for k, grad in ((0, early_ref), (1, late_ref)):
        fresh = adamw_step(
            *(ref[:, k, :] for ref in (zx_ref, zx1_ref, zx2_ref)), grad[:, :width], matrix_rate, matrix_decay
        )
        for ref, value in zip((zxn_ref, zx1n_ref, zx2n_ref), fresh):
            ref[:, k, :] = value
    update((bc_ref, bc1_ref, bc2_ref), (bcn_ref, bc1n_ref, bc2n_ref), bcg_ref[...])
    update((out_ref, out1_ref, out2_ref), (outn_ref, out1n_ref, out2n_ref), early_ref[:, width:])

    @pl.when(pl.program_id(0) == 0)
    def _():
        unit = jnp.where(
            lax.broadcasted_iota(jnp.int32, (16, LANES), 0) == lax.broadcasted_iota(jnp.int32, (16, LANES), 1), 1.0, 0.0
        ).astype(f32)
        turned = mm_exact(unit, late_all_ref[:, width + 2 * NS :], NT)
        update((dt_ref, dt1_ref, dt2_ref), (dtn_ref, dt1n_ref, dt2n_ref), turned[:heads])

    rows = in_ref.shape[0]
    tile = 64

    def some(i, _):
        at = span(i * tile, tile)
        squares = jnp.zeros((tile, LANES), f32)
        inner = jnp.zeros((tile, LANES), f32)
        for c in range(D // LANES):
            cols = slice(c * LANES, (c + 1) * LANES)
            x = in_ref[at, cols].astype(f32)
            squares = squares + x * x
            inner = inner + x * flat_ref[c : c + 1, :] * back_ref[at, cols].astype(f32)
        r = lax.rsqrt(jnp.sum(squares, axis=-1, keepdims=True) / D + norm_eps)
        k = r * r * r * jnp.sum(inner, axis=-1, keepdims=True) / D
        r, k = jnp.broadcast_to(r, (tile, LANES)), jnp.broadcast_to(k, (tile, LANES))
        for c in range(D // LANES):
            cols = slice(c * LANES, (c + 1) * LANES)
            x = in_ref[at, cols].astype(f32)
            layer_ref[at, cols] = (x + branch_ref[at, cols].astype(f32)).astype(bf16)
            back = back_ref[at, cols].astype(f32)
            grad_ref[at, cols] = cot_ref[at, cols].astype(f32) + r * flat_ref[c : c + 1, :] * back - x * k
        return 0

    lax.fori_loop(0, rows // tile, some, 0)


def finish(layer_input, out_grad, branch, back, flat, early, late, bcg, zx, bc, out, dt):
    (rows, width), heads = out[0].shape, dt[0].shape[0]
    steps = 2
    part = lambda a: pl.BlockSpec((a.shape[0] // steps, *a.shape[1:]), lambda i: (i,) + (0,) * (a.ndim - 1))
    whole = lambda a: pl.BlockSpec(a.shape, lambda i: (0,) * a.ndim)
    like = lambda a, dtype=f32: jax.ShapeDtypeStruct(a.shape, dtype)
    weights = (*zx, *bc, *out)
    return pl.pallas_call(
        functools.partial(finish_body, width, heads),
        grid=(steps,),
        in_specs=[
            *(part(a) for a in (layer_input, out_grad, branch, back)), whole(flat),
            *(part(a) for a in (early, late, bcg, *weights)), whole(late), *(whole(a) for a in dt),
        ],
        out_specs=[part(layer_input), part(back), *(part(a) for a in weights), *(whole(a) for a in dt)],
        out_shape=[like(layer_input, bf16), like(layer_input), *(like(a) for a in weights), *(like(a) for a in dt)],
        compiler_params=pltpu.CompilerParams(vmem_limit_bytes=32 * 2**20),
        name="finish",
    )(layer_input, out_grad, branch, back, flat, early, late, bcg, *weights, late, *dt)


def local(
    layer_input,
    out_grad,
    small_params,
    small_first,
    small_second,
    w_zx,
    zx_first,
    zx_second,
    w_bc,
    bc_first,
    bc_second,
    w_dt,
    dt_first,
    dt_second,
    w_out,
    out_first,
    out_second,
):
    n = lax.axis_size("dp")
    flat = jnp.pad(small_params, (0, FLAT_ROWS * LANES - small_params.shape[0])).reshape(FLAT_ROWS, LANES)
    v, xc, dr, st, dy, dz, branch, early, gate, gain, xg, w_all, pair_all, taps, head, chan = ssd_forward(
        n, layer_input, out_grad, flat, w_zx, w_bc, w_dt.T, w_out
    )
    d_late, small, owner_early, own_branch = ssd_backward(
        n, dy, v, xc, dr, st, gate, taps, head, chan, early, branch
    )
    owner_late, d_normed_in, owner_bc, flat_grad = reduce_all(
        n, xg, d_late, dz, pair_all, w_all, small, flat, gain
    )
    small_grad = flat_grad.reshape(-1)[: small_params.shape[0]]
    small_new, small_first_new, small_second_new = adamw_step(
        small_params, small_first, small_second, small_grad, small_rate, 0.0
    )
    (
        layer_output, input_grad, zx_new, zx_first_new, zx_second_new, bc_new, bc_first_new, bc_second_new,
        out_new, out_first_new, out_second_new, dt_new, dt_first_new, dt_second_new,
    ) = finish(
        layer_input, out_grad, own_branch, d_normed_in, flat, owner_early, owner_late, owner_bc,
        (w_zx, zx_first, zx_second), (w_bc, bc_first, bc_second), (w_out, out_first, out_second),
        (w_dt.T, dt_first.T, dt_second.T),
    )
    dt_new, dt_first_new, dt_second_new = dt_new.T, dt_first_new.T, dt_second_new.T
    return (
        layer_output,
        input_grad,
        small_new,
        small_first_new,
        small_second_new,
        zx_new,
        zx_first_new,
        zx_second_new,
        bc_new,
        bc_first_new,
        bc_second_new,
        dt_new,
        dt_first_new,
        dt_second_new,
        out_new,
        out_first_new,
        out_second_new,
    )


def solution(mesh):
    return jax.shard_map(
        local,
        mesh=mesh,
        in_specs=(
            P(("dp", "tensor"), None),
            P(("dp", "tensor"), None),
            P(),
            P(),
            P(),
            P("dp", None, "tensor"),
            P("dp", None, "tensor"),
            P("dp", None, "tensor"),
            P("dp", None),
            P("dp", None),
            P("dp", None),
            P("dp", "tensor"),
            P("dp", "tensor"),
            P("dp", "tensor"),
            P("dp", "tensor"),
            P("dp", "tensor"),
            P("dp", "tensor"),
        ),
        out_specs=(
            P(("dp", "tensor"), None),
            P(("dp", "tensor"), None),
            P(),
            P(),
            P(),
            P("dp", None, "tensor"),
            P("dp", None, "tensor"),
            P("dp", None, "tensor"),
            P("dp", None),
            P("dp", None),
            P("dp", None),
            P("dp", "tensor"),
            P("dp", "tensor"),
            P("dp", "tensor"),
            P("dp", "tensor"),
            P("dp", "tensor"),
            P("dp", "tensor"),
        ),
        check_vma=False,
    )
```

```python
import functools

import jax
import jax.numpy as jnp
from jax import lax
from jax.experimental import pallas as pl
from jax.experimental.pallas import tpu as pltpu
from jax.sharding import PartitionSpec as P

D = 1536
DI = 3072
H = 48
NS = 128
P_SIZE = 64
CONV = 4
LEN = 2048
STEP = 10

T = 128
ROWS = 256
LANES = 128
ROOM = 60 * 2**20

norm_eps = 1e-05
adam_eps = 1e-08
beta_first = 0.9
beta_second = 0.95
matrix_rate = 0.01
small_rate = 0.1
matrix_decay = 0.1

f32 = jnp.float32
bf16 = jnp.bfloat16
NN = (((1,), (0,)), ((), ()))
NT = (((1,), (1,)), ((), ()))
TN = (((0,), (0,)), ((), ()))
HIGHEST = lax.Precision.HIGHEST


GATE_ROW, TAPS_ROW, BIAS_ROW, TAPS_BC_ROW, BIAS_BC_ROW, HEAD_ROW, FLAT_ROWS = 12, 36, 132, 156, 164, 166, 168


def mm(a, b, dims=NN):
    return lax.dot_general(a, b, dims, preferred_element_type=f32)


def mm_exact(a, b, dims=NN):
    return lax.dot_general(a, b, dims, preferred_element_type=f32, precision=HIGHEST)


def sigmoid(v):
    return 0.5 * jnp.tanh(0.5 * v) + 0.5


def softplus(v):
    return jnp.maximum(v, 0.0) + jnp.log1p(jnp.exp(-jnp.abs(v)))


def spread(col):
    return jnp.broadcast_to(col, (T, LANES))


def block_iota(axis):
    return lax.broadcasted_iota(jnp.int32, (T, LANES), axis)


HEADS = 16
LOG2_E = 1.4426950408889634


def pieces(value, count):
    parts = []
    for k in range(count):
        part = value.astype(bf16)
        parts.append(part)
        if k < count - 1:
            value = value - part.astype(f32)
    return jnp.concatenate(parts, axis=1)


def columns_of(rows):
    return jnp.concatenate([rows, jnp.zeros((LANES - HEADS, T), f32)], axis=0).T


def set_heads(head_ref, head_t, until):
    turned = jnp.concatenate([head_ref[...], jnp.zeros((LANES - 8, LANES), f32)], axis=0).T
    head_t[0] = spread(turned[:, 0:1])[:HEADS]
    head_t[1] = spread(turned[:, 1:2])[:HEADS]
    matrix = jnp.where(block_iota(0) <= block_iota(1), 1.0, 0.0).astype(bf16)
    for k in range(3):
        until[k * T : (k + 1) * T, :] = matrix


def head_rows(dr_ref, head_t, until, rows):
    raw = dr_ref[rows, :].T[:HEADS] + head_t[0]
    dt = softplus(raw)
    decay = mm(pieces(dt * (head_t[1] * LOG2_E), 3), until[...])
    return raw, dt, decay, columns_of(dt), columns_of(decay)


def ring_place(n):
    me = lax.axis_index("dp")
    z, x = lax.div(me, 2), lax.rem(me, 2)
    return z + x * (n - 1 - 2 * z)


def ring_index(pos, n):
    back = lax.div(pos, n // 2)
    return 2 * pos + back * (2 * n - 1 - 4 * pos)


def neighbours(n):
    pos = ring_place(n)
    right = ring_index(lax.rem(pos + 1, n), n)
    left = ring_index(lax.rem(pos + n - 1, n), n)
    me = lax.axis_index("tensor")
    y, core = lax.div(me, 2), lax.rem(me, 2)
    across = 2 * (1 - y) + core
    beside = 2 * y + 1 - core
    return pos, ({"dp": right}, {"dp": left}), me, {"tensor": across}, {"tensor": beside}


def greet(peers):
    barrier = pltpu.get_barrier_semaphore()
    for peer in peers:
        pl.semaphore_signal(barrier, inc=1, device_id=peer, device_id_type=pl.DeviceIdType.MESH)


def enter(peers):
    greet(peers)
    pl.semaphore_wait(pltpu.get_barrier_semaphore(), len(peers))


def remote(src, dst, send_sem, recv_sem, peer):
    return pltpu.make_async_remote_copy(
        src_ref=src, dst_ref=dst, send_sem=send_sem, recv_sem=recv_sem,
        device_id=peer, device_id_type=pl.DeviceIdType.MESH,
    )


def span(start, size):
    return pl.ds(pl.multiple_of(start, 16), size)


def strip(rows):
    return next(size for size in (48, 32, 16) if rows % size == 0)


def cut_rows(rows):
    top = rows // 32 * 16
    return ((0, top), (top, rows - top))


def forward_body(
    n, rows, tokens, width,
    in_ref, cot_ref, flat_ref, wzx_ref, wbc_ref, wdt_ref, wout_ref,
    v_ref, xc_ref, dr_ref, st_ref, dy_ref, dz_ref, branch_ref, early_ref, gate_ref, gain_ref,
    xg_ref, ws_ref, wps_ref, taps_ref, head_ref, chan_ref,
    halo, state, y_all, z_all, dn_all, nl_all, dz_all, xg, cots, ws, wps, sums, red, head_t, until, across_state, tails,
    own_keep, early_keep, lead_keep, lead_send, lead_recv, x_keep, x_over_send, x_over_recv, x_side_send, x_side_recv,
    x_pass_send, x_pass_recv, ring_keep, ring_send, ring_recv, over_send, over_recv,
    side_send, side_recv, pass_send, pass_recv, sum_send, sum_recv,
):
    pairs = width // LANES
    wide = width + 2 * NS
    step = pl.program_id(0)
    steps = LEN // ROWS
    tall = 2 * ROWS
    norming = steps // 2
    gating = norming + 1
    forming = gating + 1
    products = forming + steps // 2
    pos, ring, me, across, beside = neighbours(n)
    opposite = lax.rem(me + 2, 4)
    next_door = me + 1 - 2 * lax.rem(me, 2)
    far = lax.rem(next_door + 2, 4)
    askew = {"tensor": far}
    quarter = tokens // 4
    hops = n // 2
    cuts = cut_rows(rows)
    mine = ring_index(pos, n)

    late = wide + LANES
    parts_of = ((0, width), (width, width))

    def hop(k, part, way, h):
        first, size = cuts[part]
        cols = pl.ds(*parts_of[k])
        block = ring_index(lax.rem(pos + (h if way else n - h), n), n)
        here = wps.at[span(block * rows + first, size), cols]
        return remote(here, here, ring_send.at[way, part, k, h], ring_recv.at[way, part, k, h], ring[way])

    def hop_lands(k, part, way, h):
        first, size = cuts[part]
        block = ring_index(lax.rem(pos + (h + 1 if way else n - h - 1), n), n)
        return span(block * rows + first, size), pl.ds(*parts_of[k])

    def hop_arrival(k, part, way, h):
        here = wps.at[hop_lands(k, part, way, h)]
        return remote(here, here, ring_send.at[way, part, k, h], ring_recv.at[way, part, k, h], ring[way])

    def hop_keep(part, way, h):
        at = hop_lands(1, part, way, h)
        return pltpu.make_async_copy(wps.at[at], wps_ref.at[at], ring_keep.at[way, part, h])

    def hop_ways(h):
        return [(part, way) for part in (0, 1) for way in (0, 1) if h < hops - 1 or part == way]

    def hop_on(k, h):
        for part, way in hop_ways(h - 1) if h > 0 else ():
            hop_arrival(k, part, way, h - 1).wait_recv()
            if k == 1:
                hop_keep(part, way, h - 1).start()
            if h < hops and (part, way) in hop_ways(h):
                hop(k, part, way, h).start()
        if h == 0:
            for part, way in hop_ways(0):
                hop(k, part, way, 0).start()

    def over(k):
        return remote(
            cot_ref.at[pl.ds(k * quarter, quarter)], cots.at[span(me * tokens + k * quarter, quarter)],
            over_send.at[k], over_recv.at[k], across,
        )

    def landed(start, size, send, recv, peer):
        here = cots.at[span(start, size)]
        return remote(here, here, send, recv, peer)

    def over_arrival(k):
        return landed(opposite * tokens + k * quarter, quarter, over_send.at[k], over_recv.at[k], across)

    def passing(k):
        return landed(opposite * tokens + k * quarter, quarter, pass_send.at[k], pass_recv.at[k], beside)

    def pass_arrival(k):
        return landed(far * tokens + k * quarter, quarter, pass_send.at[k], pass_recv.at[k], beside)

    def side():
        return remote(cot_ref, cots.at[span(me * tokens, tokens)], side_send.at[0], side_recv.at[0], beside)

    def side_arrival():
        return landed(next_door * tokens, tokens, side_send.at[0], side_recv.at[0], beside)

    def own_cot():
        return pltpu.make_async_copy(cot_ref, cots.at[span(me * tokens, tokens)], own_keep.at[0])

    def own_z():
        at = span(mine * rows, rows), pl.ds(*parts_of[1])
        return pltpu.make_async_copy(wps.at[at], wps_ref.at[at], own_keep.at[1])

    def pass_on(*pieces):
        for k in pieces:
            over_arrival(k).wait_recv()
            passing(k).start()

    def normalize(k):
        def some(i, _):
            at = span(me * tokens + k * quarter + i * 64, 64)
            squares = jnp.zeros((64, LANES), f32)
            for c in range(D // LANES):
                x = xg[at, c * LANES : (c + 1) * LANES].astype(f32)
                squares = squares + x * x
            inverse = lax.rsqrt(jnp.sum(squares, axis=-1, keepdims=True) / D + norm_eps)
            inverse = jnp.broadcast_to(inverse, (64, LANES))
            for c in range(D // LANES):
                cols = slice(c * LANES, (c + 1) * LANES)
                xg[at, cols] = (xg[at, cols].astype(f32) * inverse * flat_ref[c : c + 1, :]).astype(bf16)
            return 0

        lax.fori_loop(0, quarter // 64, some, 0)

    @pl.when(step == 0)
    def _():
        own_rows = span(me * tokens, tokens)
        greet((*ring, across, beside, askew))
        load = pltpu.make_async_copy(in_ref, xg.at[own_rows], own_keep.at[2])
        load.start()
        own_cot().start()
        mine_at = span(mine * rows, rows)
        ws[mine_at, :width] = wzx_ref[:, 1, :].astype(bf16)
        ws[mine_at, width:wide] = wbc_ref[...].astype(bf16)
        heads = wdt_ref.shape[0]
        unit = jnp.where(
            lax.broadcasted_iota(jnp.int32, (16, LANES), 0) == lax.broadcasted_iota(jnp.int32, (16, LANES), 1), 1.0, 0.0
        ).astype(bf16)
        steps_w = jnp.concatenate([wdt_ref[...], jnp.zeros((16 - heads, rows), f32)], axis=0).astype(bf16)
        ws[mine_at, wide:] = mm(steps_w, unit, TN).astype(bf16)
        load.wait()
        normalize(0)
        pl.semaphore_wait(pltpu.get_barrier_semaphore(), 5)
        started, kept = [], []

        def go(*args):
            copy = remote(*args)
            copy.start()
            started.append(copy)

        def keep(src, dst, sem):
            copy = pltpu.make_async_copy(src, dst, sem)
            copy.start()
            kept.append(copy)

        def arrived(part, way, h, block):
            first, size = cuts[part]
            at = span(block * rows + first, size)
            remote(
                ws.at[at], ws.at[at], lead_send.at[way, part, h], lead_recv.at[way, part, h], ring[way]
            ).wait_recv()
            keep(ws.at[at], ws_ref.at[at], lead_keep.at[way, part, h])

        def lead(h, parts=(0, 1)):
            for part in parts:
                first, size = cuts[part]
                for way in (0, 1):
                    block = ring_index(lax.rem(pos + (h if way else n - h), n), n)
                    here = ws.at[span(block * rows + first, size)]
                    if h > 0:
                        arrived(part, way, h - 1, block)
                    if h == hops - 1 and part != way:
                        continue
                    go(here, here, lead_send.at[way, part, h], lead_recv.at[way, part, h], ring[way])

        def x_over(k):
            at = span(me * tokens + k * quarter, quarter)
            go(xg.at[at], xg.at[at], x_over_send.at[k], x_over_recv.at[k], across)

        def x_pass(k):
            at = span(opposite * tokens + k * quarter, quarter)
            here = xg.at[at]
            remote(here, here, x_over_send.at[k], x_over_recv.at[k], across).wait_recv()
            go(here, here, x_pass_send.at[k], x_pass_recv.at[k], beside)
            keep(here, xg_ref.at[at], x_keep.at[k])

        def x_pass_lands(k):
            at = span(far * tokens + k * quarter, quarter)
            remote(xg.at[at], xg.at[at], x_pass_send.at[k], x_pass_recv.at[k], beside).wait_recv()
            keep(xg.at[at], xg_ref.at[at], x_keep.at[4 + k])

        lead(0, (0,))
        leading = list(started)
        x_over(0)
        for k in (1, 2, 3):
            normalize(k)
            if k == 1:
                x_over(1)
        go(xg.at[own_rows], xg.at[own_rows], x_side_send.at[0], x_side_recv.at[0], beside)
        keep(xg.at[own_rows], xg_ref.at[own_rows], x_keep.at[8])
        wps[mine_at, :width] = wout_ref[...].astype(bf16)
        wps[mine_at, width:] = wzx_ref[:, 0, :].astype(bf16)
        for copy in leading:
            copy.wait_send()
            started.remove(copy)
        lead(0, (1,))
        keep(ws.at[mine_at], ws_ref.at[mine_at], x_keep.at[9])
        own_z().start()
        halo[0:8, :] = jnp.zeros((8, wide), f32)
        state[...] = jnp.zeros_like(state)
        gate_ref[...] = jnp.zeros_like(gate_ref)
        parameter_rows(me, width, flat_ref, taps_ref, head_ref, chan_ref)
        set_heads(head_ref, head_t, until)
        lead(1)
        x_over(2)
        at = span(next_door * tokens, tokens)
        remote(xg.at[at], xg.at[at], x_side_send.at[0], x_side_recv.at[0], beside).wait_recv()
        keep(xg.at[at], xg_ref.at[at], x_keep.at[10])
        side().start()
        lead(2)
        x_over(3)
        x_pass(0)
        x_pass(1)
        for h in range(3, hops):
            lead(h)
        hop_on(0, 0)
        x_pass(2)
        over(0).start()
        x_pass_lands(0)
        x_pass_lands(1)
        x_pass(3)
        for part in (0, 1):
            arrived(part, part, hops - 1, ring_index(lax.rem(pos + n // 2, n), n))
        hop_on(1, 0)
        over(1).start()
        x_pass_lands(2)
        x_pass_lands(3)
        for copy in kept:
            copy.wait()
        for copy in started:
            copy.wait_send()

    def at_tick(tick):
        for k, times in enumerate(((1, 4, 6), (2, 5, 7))):
            for h in range(1, min(hops, 4)):
                pl.when(tick == times[h - 1])(functools.partial(hop_on, k, h))

        @pl.when(tick == 2)
        def _():
            over(2).start()

        @pl.when(tick == 4)
        def _():
            over(3).start()
            pass_on(0, 1)

        pl.when(tick == steps - 1)(functools.partial(pass_on, 2))

    @pl.when(step < norming)
    def _():
        def chunk(i, _):
            tick = 2 * step + i
            at_tick(tick)
            scan_step(
                width, tick, i, xg, ws, taps_ref, head_ref, chan_ref,
                v_ref, xc_ref, dr_ref, st_ref, halo, state, y_all, head_t, until, across_state, tails,
                functools.partial(pass_on, 3),
            )
            return 0

        lax.fori_loop(0, 2, chunk, 0)

    @pl.when(step == norming)
    def _():
        for k in (0, 1):
            for h in range(4, hops):
                hop_on(k, h)
        hop_on(0, hops)
        side_arrival().wait_recv()
        for k in range(4):
            pass_arrival(k).wait_recv()
        own_cot().wait()
        own_z().wait()

        def some(i, _):
            at = span(i * tall, tall)
            dn_all[at, :] = mm(cots[at, :], wps[:, :width]).astype(bf16)
            return 0

        lax.fori_loop(0, LEN // tall, some, 0)

    @pl.when(step == gating)
    def _():
        hop_on(1, hops)
        ones = jnp.ones((8, LANES), f32)

        def some(i, _):
            at = span(i * tall, tall)
            z_all[at, :] = mm(xg[at, :], wps[:, width:])
            for sub in range(tall // T):
                rows_at = span(i * tall + sub * T, T)
                squares = jnp.zeros((T, LANES), f32)
                inner = jnp.zeros((T, LANES), f32)
                for p in range(pairs):
                    cols = slice(p * LANES, (p + 1) * LANES)
                    z = z_all[rows_at, cols]
                    gated = y_all[rows_at, cols] * (z * sigmoid(z))
                    squares = squares + gated * gated
                    inner = inner + gated * chan_ref[0:1, cols] * dn_all[rows_at, cols].astype(f32)
                lanes = pl.ds(pl.multiple_of(i * tall + sub * T, T), T)
                sums[me, 0:4, lanes] = mm_exact(ones, squares, NT)[0:4]
                sums[me, 4:8, lanes] = mm_exact(ones, inner, NT)[4:8]
            return 0

        lax.fori_loop(0, LEN // tall, some, 0)

    @pl.when(step == forming - 1)
    def _():
        peers = ((beside, next_door), (across, opposite), (askew, far))
        for k, (peer, _) in enumerate(peers):
            remote(sums.at[me], sums.at[me], sum_send.at[k], sum_recv.at[k], peer).start()
        for h in range(hops):
            for part, way in hop_ways(h):
                for k in (0, 1):
                    hop(k, part, way, h).wait_send()
                hop_keep(part, way, h).wait()
        side().wait_send()
        for k in range(4):
            over(k).wait_send()
            passing(k).wait_send()
        for k, (peer, other) in enumerate(peers):
            remote(sums.at[other], sums.at[other], sum_send.at[k], sum_recv.at[k], peer).wait()
        red[...] = ((sums[0] + sums[1]) + sums[2]) + sums[3]

    @pl.when((step >= forming) & (step < products))
    def _():
        def some(i, _):
            first = (step - forming) * tall + i * ROWS
            lanes = pl.ds(pl.multiple_of(first, ROWS), ROWS)
            q_row = lax.rsqrt(red[0:4, lanes] / DI + norm_eps)
            k_row = q_row * q_row * q_row * red[4:8, lanes] / DI
            turned = jnp.concatenate([q_row, k_row], axis=0).T
            for sub in range(ROWS // T):
                rows_at = slice(sub * T, (sub + 1) * T)
                at = span(first + sub * T, T)
                q, kk = spread(turned[rows_at, 0:1]), spread(turned[rows_at, 4:5])
                for p in range(pairs):
                    cols = slice(p * LANES, (p + 1) * LANES)
                    z, y, dn = z_all[at, cols], y_all[at, cols], dn_all[at, cols].astype(f32)
                    gain = chan_ref[0:1, cols]
                    s = sigmoid(z)
                    sz = z * s
                    gated = y * sz
                    gq = gated * q
                    dg = q * gain * dn - gated * kk
                    gate_ref[:, cols] += jnp.sum((gq * dn).reshape(T // 8, 8, LANES), axis=0)
                    nl_all[at, cols] = (gq * gain).astype(bf16)
                    dz_all[at, cols] = (dg * y * (s + sz * (1.0 - s))).astype(bf16)
                    dn_all[at, cols] = (dg * sz).astype(bf16)
            branch_ref[span(i * ROWS, ROWS), :] = mm(nl_all[span(first, ROWS), :], wps[:, :width], NT).astype(bf16)
            return 0

        lax.fori_loop(0, 2, some, 0, unroll=2)

    def rows_out():
        return [
            pltpu.make_async_copy(src, dst, own_keep.at[2 + k])
            for k, (src, dst) in enumerate(((dz_all, dz_ref), (dn_all, dy_ref)))
        ]

    def early_out(i):
        at = span(i * ROWS, ROWS)
        return [
            pltpu.make_async_copy(src.at[at, pl.ds(0, width)], early_ref.at[at, pl.ds(k * width, width)], early_keep.at[k, i])
            for k, src in enumerate((ws, wps))
        ]

    @pl.when(step == products)
    def _():
        for copy in rows_out():
            copy.start()

        def some(i, _):
            at = span(i * ROWS, ROWS)
            lanes = pl.ds(pl.multiple_of(i * ROWS, ROWS), ROWS)
            grad = mm(xg[:, lanes], dz_all[...], TN)
            ws[at, :width] = grad.astype(bf16)
            share = jnp.zeros((ROWS, LANES), f32)
            for p in range(pairs):
                cols = slice(p * LANES, (p + 1) * LANES)
                w = wps[at, width + p * LANES : width + (p + 1) * LANES]
                share = share + grad[:, cols] * w.astype(f32)
            gain_ref[:, lanes] = mm_exact(jnp.ones((8, LANES), f32), share, NT)
            wps[at, :width] = mm(cots[:, lanes], nl_all[...], TN).astype(bf16)
            for copy in early_out(i):
                copy.start()
            return 0

        lax.fori_loop(0, D // ROWS, some, 0, unroll=2)
        for copy in rows_out():
            copy.wait()

        def done(i, _):
            for copy in early_out(i):
                copy.wait()
            return 0

        lax.fori_loop(0, D // ROWS, done, 0)


def parameter_rows(me, width, flat_ref, taps_ref, head_ref, chan_ref):
    pairs = width // LANES
    heads = width // P_SIZE
    taps_ref[...] = jnp.zeros_like(taps_ref)
    chan_ref[...] = jnp.zeros_like(chan_ref)
    for c in range(pairs):
        cols = slice(c * LANES, (c + 1) * LANES)
        chan_ref[0:1, cols] = flat_ref[pl.ds(GATE_ROW + pairs * me + c, 1), :]
        taps_ref[CONV : CONV + 1, cols] = flat_ref[pl.ds(BIAS_ROW + pairs * me + c, 1), :]
        for k in range(CONV):
            taps_ref[k : k + 1, cols] = flat_ref[pl.ds(TAPS_ROW + 4 * pairs * k + pairs * me + c, 1), :]
    for c in range(2):
        cols = slice(width + c * LANES, width + (c + 1) * LANES)
        taps_ref[CONV : CONV + 1, cols] = flat_ref[BIAS_BC_ROW + c : BIAS_BC_ROW + c + 1, :]
        for k in range(CONV):
            row = TAPS_BC_ROW + 2 * k + c
            taps_ref[k : k + 1, cols] = flat_ref[row : row + 1, :]
    both = jnp.concatenate([flat_ref[HEAD_ROW : HEAD_ROW + 1, :], flat_ref[HEAD_ROW + 1 : HEAD_ROW + 2, :]], axis=1)
    both = jnp.broadcast_to(both, (8, 2 * LANES))
    lane = lax.broadcasted_iota(jnp.int32, (2 * LANES, LANES), 0)
    head = lax.broadcasted_iota(jnp.int32, (2 * LANES, LANES), 1)

    def take(kind):
        match = (lane == 4 * heads * kind + heads * me + head) & (head < heads)
        return mm_exact(both, jnp.where(match, 1.0, 0.0).astype(f32))

    valid = lax.broadcasted_iota(jnp.int32, (8, LANES), 1) < heads
    row = lax.broadcasted_iota(jnp.int32, (8, LANES), 0)
    rates = jnp.where(valid, -jnp.exp(take(1)), 0.0)
    head_ref[...] = jnp.where(row == 0, take(0), jnp.where(row == 1, rates, 0.0))
    skip = mm_exact(take(2), picked(width).astype(f32), NT)
    chan_ref[1:2, :] = skip[0:1]


def picked(width):
    channel = lax.broadcasted_iota(jnp.int32, (width, LANES), 0)
    head = lax.broadcasted_iota(jnp.int32, (width, LANES), 1)
    return jnp.where((channel >= head * P_SIZE) & (channel < (head + 1) * P_SIZE), 1.0, 0.0).astype(bf16)


def scan_step(
    width, tick, i, xg, w_ref, taps_ref, head_ref, chan_ref,
    v_ref, xc_ref, dr_ref, st_ref, halo, state, y_all, head_t, until, across_state, tails, late_turn,
):
    pairs = width // LANES
    wide = width + 2 * NS
    mine = span(tick * ROWS, ROWS)
    dr_ref[span(i * ROWS, ROWS), :] = mm(xg[mine, :], w_ref[:, wide:])
    halo[8 : 8 + ROWS, :] = mm(xg[mine, :], w_ref[:, :wide])
    low_half = block_iota(1) < P_SIZE
    causal = block_iota(0) >= block_iota(1)

    def convolved(sub, block):
        cols = slice(block * LANES, (block + 1) * LANES)
        total = taps_ref[CONV : CONV + 1, cols]
        for k in range(CONV):
            first = 8 - (CONV - 1) + k + sub * T
            total = total + taps_ref[k : k + 1, cols] * halo[first : first + T, cols]
        rows = span(i * ROWS + sub * T, T)
        xc_ref[rows, cols] = total.astype(bf16)
        v_ref[rows, cols] = halo[8 + sub * T : 8 + (sub + 1) * T, cols].astype(bf16)
        return total * sigmoid(total)

    for sub in range(ROWS // T):
        rows = span(i * ROWS + sub * T, T)
        _, _, decay_t, dt, decay = head_rows(dr_ref, head_t, until, rows)
        b_low = convolved(sub, pairs).astype(bf16)
        c_low = convolved(sub, pairs + 1).astype(bf16)
        b_t = b_low.T
        scores = jnp.where(causal, mm(c_low, b_low, NT), 0.0)
        entering = state[...].astype(bf16)
        st_ref[i * (ROWS // T) + sub] = entering
        across_state[...] = mm(c_low, entering)
        for p in range(pairs):
            cols = slice(p * LANES, (p + 1) * LANES)
            x = convolved(sub, p)
            l1, l2 = spread(decay[:, 2 * p : 2 * p + 1]), spread(decay[:, 2 * p + 1 : 2 * p + 2])
            both = jnp.where(low_half, l1, l2)
            dtb = jnp.where(
                low_half, spread(dt[:, 2 * p : 2 * p + 1]), spread(dt[:, 2 * p + 1 : 2 * p + 2])
            )
            u = x * dtb
            m1 = scores * jnp.exp2(jnp.minimum(l1 - decay_t[2 * p : 2 * p + 1, :], 0.0))
            m2 = scores * jnp.exp2(jnp.minimum(l2 - decay_t[2 * p + 1 : 2 * p + 2, :], 0.0))
            mixing = jnp.concatenate([m1.astype(bf16), m2.astype(bf16)], axis=1)
            u_low = u.astype(bf16)
            zero = jnp.zeros_like(u_low)
            parts = jnp.concatenate(
                [jnp.where(low_half, u_low, zero), jnp.where(low_half, zero, u_low)], axis=0
            )
            last = both[T - 1 : T, :]
            y = mm(mixing, parts) + jnp.exp2(both) * across_state[:, cols] + chan_ref[1:2, cols] * x
            tails[:, cols] = (u * jnp.exp2(last - both)).astype(bf16)
            state[:, cols] = jnp.exp2(last) * state[:, cols]
            y_all[span(tick * ROWS + sub * T, T), cols] = y
        state[...] = state[...] + mm(b_t, tails[...])
        if sub == 0:
            pl.when(tick == LEN // ROWS - 1)(late_turn)
    halo[0:8, :] = halo[ROWS : ROWS + 8, :]


def ssd_forward(n, layer_input, out_grad, flat, w_zx, w_bc, w_dt, w_out):
    rows, width = w_out.shape
    tokens = layer_input.shape[0]
    length = 4 * tokens
    wide = width + 2 * NS
    tall = 2 * ROWS
    steps = length // tall
    forming = steps + 2
    products = forming + steps
    subs = tall // T
    assert length == LEN
    row = lambda m: pl.BlockSpec((tall, m), lambda i: (jnp.minimum(i, steps - 1), 0))
    form = lambda m: pl.BlockSpec((tall, m), lambda i: (jnp.clip(i - forming, 0, steps - 1), 0))
    whole = lambda a: pl.BlockSpec(a.shape, lambda i: (0,) * a.ndim, pipeline_mode=pl.Buffered(1))
    fixed = lambda m: pl.BlockSpec((8, m), lambda i: (0, 0))
    anywhere = pl.BlockSpec(memory_space=pl.ANY)
    vm, dma = pltpu.VMEM, pltpu.SemaphoreType.DMA
    hops, lead = dma((2, 2, 2, n // 2)), dma((2, 2, n // 2))
    shape = lambda dims, dtype: jax.ShapeDtypeStruct(dims, dtype)
    return pl.pallas_call(
        functools.partial(forward_body, n, rows, tokens, width),
        grid=(products + 1,),
        in_specs=[anywhere, anywhere, *(whole(a) for a in (flat, w_zx, w_bc, w_dt, w_out))],
        out_specs=[
            row(wide), row(wide), row(LANES), pl.BlockSpec((subs, NS, width), lambda i: (jnp.minimum(i, steps - 1), 0, 0)),
            anywhere, anywhere, form(D), anywhere,
            fixed(width), fixed(D), anywhere, anywhere, anywhere, *(fixed(m) for m in (wide, LANES, width)),
        ],
        out_shape=[
            shape((length, wide), bf16), shape((length, wide), bf16), shape((length, LANES), f32),
            shape((length // T, NS, width), bf16), shape((length, width), bf16), shape((length, width), bf16),
            shape((length, D), bf16), shape((D, 2 * width), bf16), shape((8, width), f32), shape((8, D), f32),
            shape((length, D), bf16), shape((D, wide + LANES), bf16), shape((D, 2 * width), bf16),
            *(shape((8, m), f32) for m in (wide, LANES, width)),
        ],
        scratch_shapes=[
            vm((ROWS + 8, wide), f32), vm((NS, width), f32), vm((length, width), f32), vm((length, width), f32),
            *(vm((length, width), bf16) for _ in range(3)),
            vm((length, D), bf16), vm((length, D), bf16), vm((D, wide + LANES), bf16), vm((D, 2 * width), bf16),
            vm((4, 8, length), f32), vm((8, length), f32), vm((2, HEADS, LANES), f32), vm((3 * T, LANES), bf16),
            vm((T, width), f32), vm((T, width), bf16),
            dma((4,)), dma((2, D // ROWS)), lead, lead, lead, dma((11,)), dma((4,)), dma((4,)), dma((1,)), dma((1,)),
            dma((4,)), dma((4,)), lead, hops, hops, dma((4,)), dma((4,)),
            dma((1,)), dma((1,)), dma((4,)), dma((4,)), dma((3,)), dma((3,)),
        ],
        compiler_params=pltpu.CompilerParams(collective_id=2, has_side_effects=True, vmem_limit_bytes=ROOM),
        name="layer_forward",
    )(layer_input, out_grad, flat, w_zx, w_bc, w_dt, w_out)


def backward_body(
    n, own_rows, tokens, width,
    dy_ref, v_ref, xc_ref, dr_ref, st_ref, gate_ref, taps_ref, head_ref, chan_ref, early_ref, branch_ref,
    d_ref, small_ref, oearly_ref, obranch_ref,
    dxh, dstate, yst, bds, dyeb, utb, products, turn, acc, hacc, pick_ref, pick_t, fades, head_t, until_ref, reach_ref,
    own, slots, near, held, over_slot,
    load_sem, ring_send, ring_recv, near_send, near_recv, over_send, over_recv,
):
    pairs = width // LANES
    wide = width + 2 * NS
    step = pl.program_id(0)
    steps = LEN // ROWS
    subs = ROWS // T
    pos, ring, me, across, beside = neighbours(n)
    opposite = lax.rem(me + 2, 4)
    next_door = me + 1 - 2 * lax.rem(me, 2)
    far = lax.rem(next_door + 2, 4)
    half = tokens // 2
    cuts = cut_rows(own_rows)

    def block_at(way, count):
        return ring_index(lax.rem(pos + (count if way else n - count), n), n)

    def hop(k, way, h):
        first, size = cuts[way]
        if h == 0:
            src = early_ref.at[span(block_at(way, 1) * own_rows + first, size), pl.ds(k * width, width)]
        else:
            src = slots[way][k].at[h - 1]
        return remote(
            src, slots[way][k].at[h], ring_send.at[way, k, h], ring_recv.at[way, k, h], ring[way]
        )

    def near_copy(turned, part):
        start = (next_door if turned else far) * tokens + part * half
        return remote(
            branch_ref.at[span(start, half)], near.at[turned, part],
            near_send.at[turned, part], near_recv.at[turned, part], beside,
        )

    def held_copy(turned, part):
        start = (me if turned else opposite) * tokens + part * half
        return pltpu.make_async_copy(
            branch_ref.at[span(start, half)], held.at[turned, part], load_sem.at[2 * turned + part]
        )

    def over_copy(part):
        return remote(held.at[0, part], over_slot.at[part], over_send.at[part], over_recv.at[part], across)

    def own_copy():
        return pltpu.make_async_copy(early_ref, own, load_sem.at[4])

    def ring_turn(k, h):
        for way in (0, 1):
            first, size = cuts[way]
            hop(k, way, h).wait_recv()
            block = block_at(way, 2 + h) if h < n - 2 else block_at(way, 0)

            tile = strip(size)

            def some(i, _, way=way, first=first, block=block, tile=tile):
                cols = slice(k * width, (k + 1) * width)
                came = slots[way][k][h, span(i * tile, tile), :]
                mine = own[span(block * own_rows + first + i * tile, tile), cols]
                if h < n - 2:
                    slots[way][k][h, span(i * tile, tile), :] = came + mine
                else:
                    oearly_ref[span(first + i * tile, tile), cols] = came.astype(f32) + mine.astype(f32)
                return 0

            lax.fori_loop(0, size // tile, some, 0)
            if h < n - 2:
                hop(k, way, h + 1).start()

    def ring_poll(k, tick):
        for h in range(n - 1):
            pl.when(tick == min(h + 1, steps - 1))(functools.partial(ring_turn, k, h))

    def add_near(turned):
        for part in (0, 1):
            held_copy(turned, part).wait()
            near_copy(turned, part).wait_recv()

            def some(i, _, part=part):
                at = span(i * 32, 32)
                held[turned, part, at, :] = held[turned, part, at, :] + near[turned, part, at, :]
                return 0

            lax.fori_loop(0, half // 32, some, 0)
            if not turned:
                over_copy(part).start()

    @pl.when(step == 0)
    def _():
        enter((*ring, across, beside))
        for way in (0, 1):
            hop(0, way, 0).start()
        for turned in (0, 1):
            for part in (0, 1):
                near_copy(turned, part).start()
                held_copy(turned, part).start()
        own_copy().start()
        dxh[T : T + 8, :] = jnp.zeros((8, wide), f32)
        dstate[...] = jnp.zeros_like(dstate)
        acc[...] = jnp.zeros_like(acc)
        hacc[...] = jnp.zeros_like(hacc)
        turn[...] = jnp.zeros_like(turn)
        pick_ref[...] = picked(width)
        channel = lax.broadcasted_iota(jnp.int32, (HEADS, width), 1)
        head = lax.broadcasted_iota(jnp.int32, (HEADS, width), 0)
        mine = (channel >= head * P_SIZE) & (channel < (head + 1) * P_SIZE)
        pick_t[...] = jnp.where(mine, 1.0, 0.0).astype(bf16)
        set_heads(head_ref, head_t, until_ref)
        from_here = jnp.where(block_iota(0) >= block_iota(1), 1.0, 0.0).astype(bf16)
        after = jnp.where(block_iota(0) < block_iota(1), 1.0, 0.0).astype(bf16)
        for k, matrix in enumerate((from_here, from_here, after, after)):
            reach_ref[k * T : (k + 1) * T, :] = matrix
        products[3 * T :, :] = jnp.zeros((HEADS, width), bf16)

    low_half = block_iota(1) < P_SIZE
    row_at, col_at = block_iota(0), block_iota(1)
    until = row_at <= col_at
    pair_lane = lax.broadcasted_iota(jnp.int32, (8, 2 * T), 1)
    pair_row = lax.broadcasted_iota(jnp.int32, (8, 2 * T), 0)
    each = jnp.where(lax.div(pair_lane, T) == pair_row, 1.0, 0.0).astype(bf16)
    ones = jnp.ones((8, T), bf16)

    def add(index, cols, value):
        acc[index, :, cols] += jnp.sum(value.reshape(T // 8, 8, LANES), axis=0)

    def conv_back(rows, block, d_act, xc, s, act):
        cols = slice(block * LANES, (block + 1) * LANES)
        dxh[0:T, cols] = d_act * (s + act * (1.0 - s))
        v = v_ref[rows, cols].astype(f32)
        total = None
        for m in range(CONV):
            moved = dxh[m : m + T, cols]
            if m == 0:
                add(CONV, cols, moved)
            add(CONV - 1 - m, cols, v * moved)
            term = taps_ref[CONV - 1 - m : CONV - m, cols] * moved
            total = term if total is None else total + term
        d_ref[rows, cols] = total.astype(bf16)

    def work(i, _):
        tick = 2 * step + i
        chunk = 1 - i

        @pl.when(tick == 1)
        def _():
            own_copy().wait()
            add_near(0)

        pl.when(tick == 2)(functools.partial(add_near, 1))
        ring_poll(0, tick)
        for sub in reversed(range(subs)):
            rows = span(chunk * ROWS + sub * T, T)
            block_state = chunk * subs + sub
            raw_t, dt_t, decay_t, dt, decay = head_rows(dr_ref, head_t, until_ref, rows)
            b_cols = slice(width, width + NS)
            c_cols = slice(width + NS, width + 2 * NS)
            b_xc, c_xc = xc_ref[rows, b_cols].astype(f32), xc_ref[rows, c_cols].astype(f32)
            b_s, c_s = sigmoid(b_xc), sigmoid(c_xc)
            b_act, c_act = b_xc * b_s, c_xc * c_s
            b_low, c_low = b_act.astype(bf16), c_act.astype(bf16)
            c_t = c_low.T
            scores_t = jnp.where(until, mm(b_low, c_low, NT), 0.0)
            ds_low = dstate[...].astype(bf16)
            yst[...] = mm(c_low, st_ref[block_state])
            bds[...] = mm(b_low, ds_low)
            d_scores = jnp.zeros((T, LANES), f32)
            for p in range(pairs):
                cols = slice(p * LANES, (p + 1) * LANES)
                dy_low = dy_ref[rows, cols]
                dy = dy_low.astype(f32)
                xc = xc_ref[rows, cols].astype(f32)
                xs = sigmoid(xc)
                x = xc * xs
                l1, l2 = spread(decay[:, 2 * p : 2 * p + 1]), spread(decay[:, 2 * p + 1 : 2 * p + 2])
                both = jnp.where(low_half, l1, l2)
                dtb = jnp.where(
                    low_half, spread(dt[:, 2 * p : 2 * p + 1]), spread(dt[:, 2 * p + 1 : 2 * p + 2])
                )
                u = x * dtb
                last = both[T - 1 : T, :]
                e1 = jnp.exp2(jnp.minimum(decay_t[2 * p : 2 * p + 1, :] - l1, 0.0))
                e2 = jnp.exp2(jnp.minimum(decay_t[2 * p + 1 : 2 * p + 2, :] - l2, 0.0))
                zero = jnp.zeros_like(dy_low)
                dy_parts = jnp.concatenate(
                    [jnp.where(low_half, dy_low, zero), jnp.where(low_half, zero, dy_low)], axis=0
                )
                du_in = mm(
                    jnp.concatenate([(scores_t * e1).astype(bf16), (scores_t * e2).astype(bf16)], axis=1), dy_parts
                )
                d_mix = mm(u.astype(bf16), dy_parts, NT)
                d1, d2 = d_mix[:, :T] * e1, d_mix[:, T:] * e2
                d_scores = d_scores + d1 + d2
                held_pairs = jnp.concatenate([(d1 * scores_t).astype(bf16), (d2 * scores_t).astype(bf16)], axis=1)
                reached_by = mm(ones, held_pairs)
                leaving = mm(each, held_pairs, NT)
                turn[2 * p : 2 * p + 1, :] = reached_by[0:1, :T] - leaving[0:1]
                turn[2 * p + 1 : 2 * p + 2, :] = reached_by[0:1, T:] - leaving[1:2]
                tail = jnp.exp2(last - both)
                fades[0:1, cols] = jnp.exp2(last)
                dye = dy * jnp.exp2(both)
                du_out = tail * bds[:, cols]
                du = du_in + du_out
                products[0:T, cols] = (dye * yst[:, cols]).astype(bf16)
                products[T : 2 * T, cols] = (u * du_out).astype(bf16)
                products[2 * T : 3 * T, cols] = (x * du).astype(bf16)
                dyeb[:, cols] = dye.astype(bf16)
                utb[:, cols] = (u * tail).astype(bf16)
                add(CONV + 1, cols, dy * x)
                conv_back(rows, p, dtb * du + chan_ref[1:2, cols] * dy, xc, xs, x)
            d_scores = jnp.where(until, d_scores, 0.0).astype(bf16)
            d_b = mm(d_scores, c_low) + mm(utb[...], ds_low, NT)
            d_c = mm(d_scores, b_low, TN) + mm(dyeb[...], st_ref[block_state], NT)
            conv_back(rows, pairs, d_b, b_xc, b_s, b_act)
            conv_back(rows, pairs + 1, d_c, c_xc, c_s, c_act)
            fade = fades[0:1, :]
            before_ds = dstate[...]
            through = jnp.sum(before_ds * st_ref[block_state].astype(f32), axis=0, keepdims=True) * fade
            products[3 * T : 3 * T + HEADS, :] = jnp.broadcast_to(through, (HEADS, width)).astype(bf16)
            dstate[...] = fade * before_ds + mm(c_t, dyeb[...])
            by_head = mm(pick_t[...], products[...], NT)
            inside = pieces(turn[...] + by_head[:, :T], 2)
            outside = pieces(by_head[:, T : 2 * T], 2)
            reached = mm(jnp.concatenate([inside, outside], axis=1), reach_ref[...])
            reached = reached + jnp.broadcast_to(by_head[:, 3 * T : 3 * T + 1], (HEADS, T))
            d_raw = (head_t[1] * reached + by_head[:, 2 * T : 3 * T]) * sigmoid(raw_t)
            d_ref[rows, wide:] = columns_of(d_raw).astype(bf16)
            hacc[0] += d_raw
            hacc[1] += dt_t * reached
            dxh[T : T + 8, :] = dxh[0:8, :]
            if sub == 1:
                @pl.when(tick == 0)
                def _():
                    for way in (0, 1):
                        hop(1, way, 0).start()

                ring_poll(1, tick)
        return 0

    lax.fori_loop(0, 2, work, 0)

    @pl.when(step == steps // 2 - 1)
    def _():
        total = lambda a: jnp.sum(a, axis=0, keepdims=True)
        for k in range(CONV + 1):
            small_ref[k : k + 1, :] = total(acc[k])
        small_ref[CONV + 1 : CONV + 2, :width] = total(gate_ref[...])
        small_ref[CONV + 1 : CONV + 2, width : width + LANES] = total(columns_of(hacc[0]))
        small_ref[CONV + 1 : CONV + 2, width + LANES :] = total(columns_of(hacc[1])) * head_ref[1:2, :]
        small_ref[CONV + 2 :, :] = jnp.zeros((2, wide), f32)
        skip = mm_exact(acc[CONV + 1, :, :width], pick_ref[...].astype(f32))
        small_ref[CONV + 3 : CONV + 4, 512 : 512 + LANES] = total(skip)
        for part in (0, 1):
            over_copy(part).wait_recv()

            def some(i, _, part=part):
                at = span(part * half + i * 32, 32)
                here = span(i * 32, 32)
                total = held[1, part, here, :].astype(f32) + over_slot[part, here, :].astype(f32)
                obranch_ref[at, :] = total.astype(bf16)
                return 0

            lax.fori_loop(0, half // 32, some, 0)
        for part in (0, 1):
            over_copy(part).wait_send()
            for turned in (0, 1):
                near_copy(turned, part).wait_send()
        for h in range(n - 1):
            for k in (0, 1):
                for way in (0, 1):
                    hop(k, way, h).wait_send()


def ssd_backward(n, dy, v, xc, dr, st, gate, taps, head, chan, early, branch):
    length, width = dy.shape
    wide = width + 2 * NS
    tall = 2 * ROWS
    steps = length // tall
    subs = tall // T
    own_rows, tokens = D // n, length // 4
    half = tokens // 2
    row = lambda m: pl.BlockSpec((tall, m), lambda i: (steps - 1 - i, 0))
    whole = lambda a: pl.BlockSpec(a.shape, lambda i: (0,) * a.ndim, pipeline_mode=pl.Buffered(1))
    fixed = lambda *shape: pl.BlockSpec(shape, lambda i: (0,) * len(shape))
    anywhere = pl.BlockSpec(memory_space=pl.ANY)
    vm, dma = pltpu.VMEM, pltpu.SemaphoreType.DMA
    return pl.pallas_call(
        functools.partial(backward_body, n, own_rows, tokens, width),
        grid=(steps,),
        in_specs=[
            row(width), row(wide), row(wide), row(LANES),
            pl.BlockSpec((subs, NS, width), lambda i: (steps - 1 - i, 0, 0)),
            whole(gate), whole(taps), whole(head), whole(chan), anywhere, anywhere,
        ],
        out_specs=[
            row(wide + LANES), fixed(8, wide), fixed(own_rows, 2 * width), fixed(tokens, D),
        ],
        out_shape=[
            jax.ShapeDtypeStruct((length, wide + LANES), bf16),
            jax.ShapeDtypeStruct((8, wide), f32),
            jax.ShapeDtypeStruct((own_rows, 2 * width), f32),
            jax.ShapeDtypeStruct((tokens, D), bf16),
        ],
        scratch_shapes=[
            vm((T + 8, wide), f32), vm((NS, width), f32), vm((T, width), f32), vm((T, width), f32),
            vm((T, width), bf16), vm((T, width), bf16), vm((3 * T + HEADS, width), bf16),
            vm((HEADS, T), f32), vm((CONV + 2, 8, wide), f32), vm((2, HEADS, T), f32),
            vm((width, LANES), bf16), vm((HEADS, width), bf16), vm((8, width), f32), vm((2, HEADS, LANES), f32),
            vm((3 * T, LANES), bf16), vm((4 * T, LANES), bf16),
            vm((D, 2 * width), bf16),
            [[vm((n - 1, size, width), bf16) for _ in (0, 1)] for _, size in cut_rows(own_rows)],
            vm((2, 2, half, D), bf16), vm((2, 2, half, D), bf16), vm((2, half, D), bf16),
            dma((5,)), dma((2, 2, n - 1)), dma((2, 2, n - 1)), dma((2, 2)), dma((2, 2)), dma((2,)), dma((2,)),
        ],
        compiler_params=pltpu.CompilerParams(
            collective_id=3, has_side_effects=True, vmem_limit_bytes=ROOM
        ),
        name="layer_backward",
    )(dy, v, xc, dr, st, gate, taps, head, chan, early, branch)


def reduce_body(
    n, rows, tokens, starts,
    xg_ref, d_ref, dz_ref, wp_ref, w_ref, small_ref, flat_ref, gain_ref,
    oxs_ref, oback_ref, bc_ref, oflat_ref,
    xg, d, dz, wz, w, work, grads, slots, staged, near, over, smalls, tens, bc_slot,
    load_sem, ring_send, ring_recv, near_send, near_recv, over_send, over_recv,
    small_send, small_recv, ten_send, ten_recv, bc_send, bc_recv,
):
    pos, ring, me, across, beside = neighbours(n)
    cuts = cut_rows(rows)
    core = lax.rem(me, 2)
    opposite = lax.rem(me + 2, 4)
    next_door = me + 1 - 2 * core
    far = lax.rem(next_door + 2, 4)
    half = tokens // 2
    late = d.shape[1]
    width = dz.shape[1]
    tile = 2 * LANES
    tiles = D // tile
    columns = [pl.ds(lo, hi - lo) for lo, hi in starts]
    sources = [(d_ref.at[:, columns[0]], d.at[:, columns[0]])]
    sources += [(xg_ref.at[:, pl.ds(i * tile, tile)], xg.at[:, pl.ds(i * tile, tile)]) for i in range(tiles)]
    sources += [(d_ref.at[:, some], d.at[:, some]) for some in columns[1:]]
    sources += [
        (dz_ref, dz), (w_ref, w), (wp_ref.at[:, pl.ds(width, width)], wz), (small_ref, smalls.at[pos]),
    ]
    loads = [pltpu.make_async_copy(src, dst, load_sem.at[k]) for k, (src, dst) in enumerate(sources)]
    for load in loads:
        load.start()
    askew = {"tensor": far}
    enter((*ring, across, beside, askew))
    started = []

    def go(*args):
        copy = remote(*args)
        copy.start()
        started.append(copy)

    def block_at(way, count):
        return ring_index(lax.rem(pos + (count if way else n - count), n), n)

    def hop(k, way, h):
        lo, hi = starts[k]
        first, size = cuts[way]
        if h == 0:
            src = grads.at[span(block_at(way, 1) * rows + first, size), pl.ds(lo, hi - lo)]
        else:
            src = slots[way][k].at[h - 1]
        return remote(
            src, slots[way][k].at[h], ring_send.at[way, k, h], ring_recv.at[way, k, h], ring[way]
        )

    def product(k):
        lo, hi = starts[k]

        def some(i, _):
            at = pl.ds(pl.multiple_of(i * tile, tile), tile)
            if k == 0:
                pltpu.make_async_copy(xg_ref.at[:, at], xg.at[:, at], load_sem.at[1 + i]).wait()
            grads[at, lo:hi] = mm(xg[:, at], d[:, lo:hi], TN).astype(bf16)
            return 0

        if k < 2:
            loads[0 if k == 0 else tiles + k].wait()
        lax.fori_loop(0, tiles, some, 0)
        for way in (0, 1):
            hop(k, way, 0).start()

    def near_copy(turned, part):
        return remote(
            staged.at[turned, part], near.at[turned, part],
            near_send.at[turned, part], near_recv.at[turned, part], beside,
        )

    def over_copy(part):
        return remote(near.at[0, part], over.at[part], over_send.at[part], over_recv.at[part], across)

    def ring_turn(k, h):
        lo, hi = starts[k]
        for way in (0, 1):
            first, size = cuts[way]
            slot = slots[way][k].at[h]
            remote(slot, slot, ring_send.at[way, k, h], ring_recv.at[way, k, h], ring[way]).wait_recv()
            block = block_at(way, 2 + h) if h < n - 2 else block_at(way, 0)

            tile = strip(size)

            def some(i, _, way=way, first=first, block=block, tile=tile):
                came = slots[way][k][h, span(i * tile, tile), :]
                mine = grads[span(block * rows + first + i * tile, tile), lo:hi]
                if h < n - 2:
                    slots[way][k][h, span(i * tile, tile), :] = came + mine
                else:
                    oxs_ref[span(first + i * tile, tile), lo:hi] = came.astype(f32) + mine.astype(f32)
                return 0

            lax.fori_loop(0, size // tile, some, 0)
            if h < n - 2:
                hop(k, way, h + 1).start()

    def small_hop(way, h):
        here = smalls.at[lax.rem(pos + (h if way else n - h), n)]
        go(here, here, small_send.at[way, h], small_recv.at[way, h], ring[way])

    def small_lands(way, h):
        here = smalls.at[lax.rem(pos + (h + 1 if way else n - h - 1), n)]
        remote(here, here, small_send.at[way, h], small_recv.at[way, h], ring[way]).wait_recv()

    product(0)
    product(1)
    for load in loads[tiles + 2 :]:
        load.wait()
    turns = {0: [(0, 0)], 1: [(1, 0)], 2: [(0, 1)], 3: [(1, 1)], 4: [(0, 2), (1, 2)], 5: [(2, 0)], 6: [(0, 3), (1, 3)], 7: [(2, 1)]}
    taken = [sum(k == group for some in turns.values() for k, _ in some) for group in range(len(starts))]

    def block(i, _):
        pl.when(i == 4)(functools.partial(product, 2))
        which, part = lax.div(i, 2), lax.rem(i, 2)
        own = lax.rem(which, 2)
        turned = lax.div(which, 2)
        target = lax.rem(next_door + own * (me - next_door) + 2 * (1 - turned), 4)
        at = span(target * tokens + part * half, half)
        total = mm(dz[at, :], wz[...], NT) + mm(d[at, :], w[...], NT)
        work[...] = total

        @pl.when(own == 0)
        def _():
            staged[turned, part] = work[...].astype(bf16)
            near_copy(turned, part).start()

        @pl.when(own == 1)
        def _():
            near_copy(turned, part).wait_recv()

        @pl.when(which == 1)
        def _():
            near[0, part] = (work[...] + near[0, part].astype(f32)).astype(bf16)
            over_copy(part).start()

        @pl.when(which == 3)
        def _():
            near[1, part] = (work[...] + near[1, part].astype(f32)).astype(bf16)

        for at_block, some in turns.items():

            @pl.when(i == at_block)
            def _(some=some):
                for k, h in some:
                    ring_turn(k, h)

        return 0

    lax.fori_loop(0, 8, block, 0)
    for i in range(tiles):
        share = jnp.zeros((tile, LANES), f32)
        for c in range(late // LANES):
            cols = slice(c * LANES, (c + 1) * LANES)
            at = slice(i * tile, (i + 1) * tile)
            share = share + grads[at, cols].astype(f32) * w[at, cols].astype(f32)
        total = mm_exact(jnp.ones((8, LANES), f32), share, NT)[0:1] + gain_ref[0:1, i * tile : (i + 1) * tile]
        for c in range(2 * i, 2 * i + 2):
            row, col = 6 + c // 8, (c % 8) * LANES
            part = total[:, (c - 2 * i) * LANES : (c - 2 * i + 1) * LANES]
            smalls[pos, row : row + 1, col : col + LANES] = part / flat_ref[c : c + 1, :]

    rest = [(k, h) for h in range(n - 1) for k in (2, 0, 1) if h >= taken[k]]
    rest.sort(key=lambda turn: turn[1] - taken[turn[0]])

    def small_step(s):
        for way in (0, 1):
            if s > 0 and (way == 0 or s < n // 2):
                small_lands(way, s - 1)
            if s < n // 2 - way:
                small_hop(way, s)

    small_step(0)
    steps_done = 1
    for at, (k, h) in enumerate(rest):
        ring_turn(k, h)
        if (k, h) == (0, n - 2):
            bc_slot[0] = oxs_ref[:, starts[0][0] : starts[0][0] + 2 * NS]
            go(bc_slot.at[0], bc_slot.at[1], bc_send.at[0], bc_recv.at[0], beside)
        if at % 2 == 1 and steps_done < n // 2:
            small_step(steps_done)
            steps_done += 1
    for s in range(steps_done, n // 2):
        small_step(s)
    small_lands(0, n // 2 - 1)

    total = smalls[0]
    for i in range(1, n):
        total = total + smalls[i]
    tens[me] = total
    others = ((beside, next_door), (across, opposite), (askew, far))
    for k, (peer, _) in enumerate(others):
        go(tens.at[me], tens.at[me], ten_send.at[k], ten_recv.at[k], peer)
    remote(bc_slot.at[1], bc_slot.at[1], bc_send.at[0], bc_recv.at[0], beside).wait_recv()
    bc_slot[2] = bc_slot[0] + bc_slot[1]
    go(bc_slot.at[2], bc_slot.at[3], bc_send.at[1], bc_recv.at[1], across)
    for part in (0, 1):
        over_copy(part).wait_recv()

        def some(i, _, part=part):
            at = span(part * half + i * 32, 32)
            here = span(i * 32, 32)
            oback_ref[at, :] = (near[1, part, here, :].astype(f32) + over[part, here, :].astype(f32)).astype(bf16)
            return 0

        lax.fori_loop(0, half // 32, some, 0)
    for k, (peer, target) in enumerate(others):
        here = tens.at[target]
        remote(here, here, ten_send.at[k], ten_recv.at[k], peer).wait_recv()
    flat_gradients(width, tens, oflat_ref)
    remote(bc_slot.at[3], bc_slot.at[3], bc_send.at[1], bc_recv.at[1], across).wait_recv()
    bc_ref[...] = bc_slot[2] + bc_slot[3]
    for part in (0, 1):
        over_copy(part).wait_send()
        for turned in (0, 1):
            near_copy(turned, part).wait_send()
    for k in range(len(starts)):
        for way in (0, 1):
            for h in range(n - 1):
                hop(k, way, h).wait_send()
    for copy in started:
        copy.wait_send()


def flat_gradients(width, tens, out_ref):
    pairs = width // LANES
    heads = width // P_SIZE

    def sums(row, col):
        total = tens[0, row : row + 1, col : col + LANES]
        for t in range(1, 4):
            total = total + tens[t, row : row + 1, col : col + LANES]
        return total

    def put(row, value):
        out_ref[row : row + 1, :] = value

    for c in range(D // LANES):
        put(c, sums(6 + c // 8, (c % 8) * LANES))
    for t in range(4):
        for c in range(pairs):
            cols = slice(c * LANES, (c + 1) * LANES)
            put(GATE_ROW + pairs * t + c, tens[t, CONV + 1 : CONV + 2, cols])
            put(BIAS_ROW + pairs * t + c, tens[t, CONV : CONV + 1, cols])
            for k in range(CONV):
                put(TAPS_ROW + 4 * pairs * k + pairs * t + c, tens[t, k : k + 1, cols])
    for c in range(2):
        put(BIAS_BC_ROW + c, sums(CONV, width + c * LANES))
        for k in range(CONV):
            put(TAPS_BC_ROW + 2 * k + c, sums(k, width + c * LANES))
    kinds = ((CONV + 1, width), (CONV + 1, width + LANES), (CONV + 3, 512))
    rows = [tens[t, row : row + 1, col : col + LANES] for row, col in kinds for t in range(4)]
    rows = jnp.concatenate(rows + [jnp.zeros((16 - len(rows), LANES), f32)], axis=0)
    lane = lax.broadcasted_iota(jnp.int32, (LANES, 2 * LANES), 1)
    entry = lax.broadcasted_iota(jnp.int32, (LANES, 2 * LANES), 0)
    spread_out = mm_exact(rows, jnp.where(lax.rem(lane, heads) == entry, 1.0, 0.0).astype(f32))
    at = lax.broadcasted_iota(jnp.int32, (16, 2 * LANES), 1)
    source = lax.broadcasted_iota(jnp.int32, (16, 2 * LANES), 0)
    line = jnp.sum(jnp.where(lax.div(at, heads) == source, spread_out, 0.0), axis=0, keepdims=True)
    put(HEAD_ROW, line[:, :LANES])
    put(HEAD_ROW + 1, line[:, LANES:])


def reduce_all(n, xg, d, dz, wp, w, small, flat, gain):
    rows, tokens = D // n, dz.shape[0] // 4
    width, late = dz.shape[1], d.shape[1]
    starts = ((width, late), (0, width // 2), (width // 2, width))
    half = tokens // 2
    dma, vm = pltpu.SemaphoreType.DMA, pltpu.VMEM
    anywhere = pl.BlockSpec(memory_space=pl.ANY)
    inside = pl.BlockSpec(memory_space=pltpu.VMEM)
    return pl.pallas_call(
        functools.partial(reduce_body, n, rows, tokens, starts),
        in_specs=[anywhere] * 6 + [inside] * 2,
        out_specs=[inside] * 4,
        out_shape=[
            jax.ShapeDtypeStruct((rows, late), f32),
            jax.ShapeDtypeStruct((tokens, D), bf16),
            jax.ShapeDtypeStruct((rows, 2 * NS), f32),
            jax.ShapeDtypeStruct((FLAT_ROWS, LANES), f32),
        ],
        scratch_shapes=[
            vm(xg.shape, bf16), vm(d.shape, bf16), vm(dz.shape, bf16), vm((D, width), bf16),
            vm((D, late), bf16),
            vm((half, D), f32), vm((D, late), bf16),
            [[vm((n - 1, size, hi - lo), bf16) for lo, hi in starts] for _, size in cut_rows(rows)],
            vm((2, 2, half, D), bf16), vm((2, 2, half, D), bf16), vm((2, half, D), bf16),
            vm((n, *small.shape), f32), vm((4, *small.shape), f32), vm((4, rows, 2 * NS), f32),
            dma((13,)), dma((2, 3, n - 1)), dma((2, 3, n - 1)), dma((2, 2)), dma((2, 2)), dma((2,)), dma((2,)),
            dma((2, n // 2)), dma((2, n // 2)), dma((3,)), dma((3,)), dma((2,)), dma((2,)),
        ],
        compiler_params=pltpu.CompilerParams(
            collective_id=1, has_side_effects=True, vmem_limit_bytes=46 * 2**20
        ),
        name="reduce_all",
    )(xg, d, dz, wp, w, small, flat, gain)


def adamw_step(weight, first, second, grad, rate, decay):
    first_new = beta_first * first + (1.0 - beta_first) * grad
    second_new = beta_second * second + (1.0 - beta_second) * grad * grad
    hat_first = first_new * (1.0 / (1.0 - beta_first**STEP))
    hat_second = second_new * (1.0 / (1.0 - beta_second**STEP))
    weight_new = weight - rate * (hat_first / (jnp.sqrt(hat_second) + adam_eps) + decay * weight)
    return (weight_new, first_new, second_new)


def finish_body(
    width, heads,
    in_ref, cot_ref, branch_ref, back_ref, flat_ref, early_ref, late_ref, bcg_ref,
    zx_ref, zx1_ref, zx2_ref, bc_ref, bc1_ref, bc2_ref, out_ref, out1_ref, out2_ref, late_all_ref, dt_ref, dt1_ref, dt2_ref,
    layer_ref, grad_ref, zxn_ref, zx1n_ref, zx2n_ref, bcn_ref, bc1n_ref, bc2n_ref,
    outn_ref, out1n_ref, out2n_ref, dtn_ref, dt1n_ref, dt2n_ref,
):
    def update(refs, news, grad):
        fresh = adamw_step(*(ref[...] for ref in refs), grad, matrix_rate, matrix_decay)
        for ref, value in zip(news, fresh):
            ref[...] = value

    for k, grad in ((0, early_ref), (1, late_ref)):
        fresh = adamw_step(
            *(ref[:, k, :] for ref in (zx_ref, zx1_ref, zx2_ref)), grad[:, :width], matrix_rate, matrix_decay
        )
        for ref, value in zip((zxn_ref, zx1n_ref, zx2n_ref), fresh):
            ref[:, k, :] = value
    update((bc_ref, bc1_ref, bc2_ref), (bcn_ref, bc1n_ref, bc2n_ref), bcg_ref[...])
    update((out_ref, out1_ref, out2_ref), (outn_ref, out1n_ref, out2n_ref), early_ref[:, width:])

    @pl.when(pl.program_id(0) == 0)
    def _():
        unit = jnp.where(
            lax.broadcasted_iota(jnp.int32, (16, LANES), 0) == lax.broadcasted_iota(jnp.int32, (16, LANES), 1), 1.0, 0.0
        ).astype(f32)
        turned = mm_exact(unit, late_all_ref[:, width + 2 * NS :], NT)
        update((dt_ref, dt1_ref, dt2_ref), (dtn_ref, dt1n_ref, dt2n_ref), turned[:heads])

    rows = in_ref.shape[0]
    tile = 64

    def some(i, _):
        at = span(i * tile, tile)
        squares = jnp.zeros((tile, LANES), f32)
        inner = jnp.zeros((tile, LANES), f32)
        for c in range(D // LANES):
            cols = slice(c * LANES, (c + 1) * LANES)
            x = in_ref[at, cols].astype(f32)
            squares = squares + x * x
            inner = inner + x * flat_ref[c : c + 1, :] * back_ref[at, cols].astype(f32)
        r = lax.rsqrt(jnp.sum(squares, axis=-1, keepdims=True) / D + norm_eps)
        k = r * r * r * jnp.sum(inner, axis=-1, keepdims=True) / D
        r, k = jnp.broadcast_to(r, (tile, LANES)), jnp.broadcast_to(k, (tile, LANES))
        for c in range(D // LANES):
            cols = slice(c * LANES, (c + 1) * LANES)
            x = in_ref[at, cols].astype(f32)
            layer_ref[at, cols] = (x + branch_ref[at, cols].astype(f32)).astype(bf16)
            back = back_ref[at, cols].astype(f32)
            grad_ref[at, cols] = cot_ref[at, cols].astype(f32) + r * flat_ref[c : c + 1, :] * back - x * k
        return 0

    lax.fori_loop(0, rows // tile, some, 0)


def finish(layer_input, out_grad, branch, back, flat, early, late, bcg, zx, bc, out, dt):
    (rows, width), heads = out[0].shape, dt[0].shape[0]
    steps = 2
    part = lambda a: pl.BlockSpec((a.shape[0] // steps, *a.shape[1:]), lambda i: (i,) + (0,) * (a.ndim - 1))
    whole = lambda a: pl.BlockSpec(a.shape, lambda i: (0,) * a.ndim)
    like = lambda a, dtype=f32: jax.ShapeDtypeStruct(a.shape, dtype)
    weights = (*zx, *bc, *out)
    return pl.pallas_call(
        functools.partial(finish_body, width, heads),
        grid=(steps,),
        in_specs=[
            *(part(a) for a in (layer_input, out_grad, branch, back)), whole(flat),
            *(part(a) for a in (early, late, bcg, *weights)), whole(late), *(whole(a) for a in dt),
        ],
        out_specs=[part(layer_input), part(back), *(part(a) for a in weights), *(whole(a) for a in dt)],
        out_shape=[like(layer_input, bf16), like(layer_input), *(like(a) for a in weights), *(like(a) for a in dt)],
        compiler_params=pltpu.CompilerParams(vmem_limit_bytes=32 * 2**20),
        name="finish",
    )(layer_input, out_grad, branch, back, flat, early, late, bcg, *weights, late, *dt)


def local(
    layer_input,
    out_grad,
    small_params,
    small_first,
    small_second,
    w_zx,
    zx_first,
    zx_second,
    w_bc,
    bc_first,
    bc_second,
    w_dt,
    dt_first,
    dt_second,
    w_out,
    out_first,
    out_second,
):
    n = lax.axis_size("dp")
    flat = jnp.pad(small_params, (0, FLAT_ROWS * LANES - small_params.shape[0])).reshape(FLAT_ROWS, LANES)
    v, xc, dr, st, dy, dz, branch, early, gate, gain, xg, w_all, pair_all, taps, head, chan = ssd_forward(
        n, layer_input, out_grad, flat, w_zx, w_bc, w_dt.T, w_out
    )
    d_late, small, owner_early, own_branch = ssd_backward(
        n, dy, v, xc, dr, st, gate, taps, head, chan, early, branch
    )
    owner_late, d_normed_in, owner_bc, flat_grad = reduce_all(
        n, xg, d_late, dz, pair_all, w_all, small, flat, gain
    )
    small_grad = flat_grad.reshape(-1)[: small_params.shape[0]]
    small_new, small_first_new, small_second_new = adamw_step(
        small_params, small_first, small_second, small_grad, small_rate, 0.0
    )
    (
        layer_output, input_grad, zx_new, zx_first_new, zx_second_new, bc_new, bc_first_new, bc_second_new,
        out_new, out_first_new, out_second_new, dt_new, dt_first_new, dt_second_new,
    ) = finish(
        layer_input, out_grad, own_branch, d_normed_in, flat, owner_early, owner_late, owner_bc,
        (w_zx, zx_first, zx_second), (w_bc, bc_first, bc_second), (w_out, out_first, out_second),
        (w_dt.T, dt_first.T, dt_second.T),
    )
    dt_new, dt_first_new, dt_second_new = dt_new.T, dt_first_new.T, dt_second_new.T
    return (
        layer_output,
        input_grad,
        small_new,
        small_first_new,
        small_second_new,
        zx_new,
        zx_first_new,
        zx_second_new,
        bc_new,
        bc_first_new,
        bc_second_new,
        dt_new,
        dt_first_new,
        dt_second_new,
        out_new,
        out_first_new,
        out_second_new,
    )


def solution(mesh):
    return jax.shard_map(
        local,
        mesh=mesh,
        in_specs=(
            P(("dp", "tensor"), None),
            P(("dp", "tensor"), None),
            P(),
            P(),
            P(),
            P("dp", None, "tensor"),
            P("dp", None, "tensor"),
            P("dp", None, "tensor"),
            P("dp", None),
            P("dp", None),
            P("dp", None),
            P("dp", "tensor"),
            P("dp", "tensor"),
            P("dp", "tensor"),
            P("dp", "tensor"),
            P("dp", "tensor"),
            P("dp", "tensor"),
        ),
        out_specs=(
            P(("dp", "tensor"), None),
            P(("dp", "tensor"), None),
            P(),
            P(),
            P(),
            P("dp", None, "tensor"),
            P("dp", None, "tensor"),
            P("dp", None, "tensor"),
            P("dp", None),
            P("dp", None),
            P("dp", None),
            P("dp", "tensor"),
            P("dp", "tensor"),
            P("dp", "tensor"),
            P("dp", "tensor"),
            P("dp", "tensor"),
            P("dp", "tensor"),
        ),
        check_vma=False,
    )
```

```python
import functools

import jax
import jax.numpy as jnp
from jax import lax
from jax.experimental import pallas as pl
from jax.experimental.pallas import tpu as pltpu
from jax.sharding import PartitionSpec as P

D = 1536
DI = 3072
H = 48
NS = 128
P_SIZE = 64
CONV = 4
LEN = 2048
STEP = 10

T = 128
ROWS = 256
LANES = 128
ROOM = 60 * 2**20

norm_eps = 1e-05
adam_eps = 1e-08
beta_first = 0.9
beta_second = 0.95
matrix_rate = 0.01
small_rate = 0.1
matrix_decay = 0.1

f32 = jnp.float32
bf16 = jnp.bfloat16
NN = (((1,), (0,)), ((), ()))
NT = (((1,), (1,)), ((), ()))
TN = (((0,), (0,)), ((), ()))
HIGHEST = lax.Precision.HIGHEST


GATE_ROW, TAPS_ROW, BIAS_ROW, TAPS_BC_ROW, BIAS_BC_ROW, HEAD_ROW, FLAT_ROWS = 12, 36, 132, 156, 164, 166, 168


def mm(a, b, dims=NN):
    return lax.dot_general(a, b, dims, preferred_element_type=f32)


def mm_exact(a, b, dims=NN):
    return lax.dot_general(a, b, dims, preferred_element_type=f32, precision=HIGHEST)


def sigmoid(v):
    return 0.5 * jnp.tanh(0.5 * v) + 0.5


def softplus(v):
    return jnp.maximum(v, 0.0) + jnp.log1p(jnp.exp(-jnp.abs(v)))


def spread(col):
    return jnp.broadcast_to(col, (T, LANES))


def block_iota(axis):
    return lax.broadcasted_iota(jnp.int32, (T, LANES), axis)


HEADS = 16
LOG2_E = 1.4426950408889634


def pieces(value, count):
    parts = []
    for k in range(count):
        part = value.astype(bf16)
        parts.append(part)
        if k < count - 1:
            value = value - part.astype(f32)
    return jnp.concatenate(parts, axis=1)


def columns_of(rows):
    return jnp.concatenate([rows, jnp.zeros((LANES - HEADS, T), f32)], axis=0).T


def set_heads(head_ref, head_t, until):
    turned = jnp.concatenate([head_ref[...], jnp.zeros((LANES - 8, LANES), f32)], axis=0).T
    head_t[0] = spread(turned[:, 0:1])[:HEADS]
    head_t[1] = spread(turned[:, 1:2])[:HEADS]
    matrix = jnp.where(block_iota(0) <= block_iota(1), 1.0, 0.0).astype(bf16)
    for k in range(3):
        until[k * T : (k + 1) * T, :] = matrix


def head_rows(dr_ref, head_t, until, rows):
    raw = dr_ref[rows, :].T[:HEADS] + head_t[0]
    dt = softplus(raw)
    decay = mm(pieces(dt * (head_t[1] * LOG2_E), 3), until[...])
    return raw, dt, decay, columns_of(dt), columns_of(decay)


def ring_place(n):
    me = lax.axis_index("dp")
    z, x = lax.div(me, 2), lax.rem(me, 2)
    return z + x * (n - 1 - 2 * z)


def ring_index(pos, n):
    back = lax.div(pos, n // 2)
    return 2 * pos + back * (2 * n - 1 - 4 * pos)


def neighbours(n):
    pos = ring_place(n)
    right = ring_index(lax.rem(pos + 1, n), n)
    left = ring_index(lax.rem(pos + n - 1, n), n)
    me = lax.axis_index("tensor")
    y, core = lax.div(me, 2), lax.rem(me, 2)
    across = 2 * (1 - y) + core
    beside = 2 * y + 1 - core
    return pos, ({"dp": right}, {"dp": left}), me, {"tensor": across}, {"tensor": beside}


def greet(peers):
    barrier = pltpu.get_barrier_semaphore()
    for peer in peers:
        pl.semaphore_signal(barrier, inc=1, device_id=peer, device_id_type=pl.DeviceIdType.MESH)


def enter(peers):
    greet(peers)
    pl.semaphore_wait(pltpu.get_barrier_semaphore(), len(peers))


def remote(src, dst, send_sem, recv_sem, peer):
    return pltpu.make_async_remote_copy(
        src_ref=src, dst_ref=dst, send_sem=send_sem, recv_sem=recv_sem,
        device_id=peer, device_id_type=pl.DeviceIdType.MESH,
    )


def span(start, size):
    return pl.ds(pl.multiple_of(start, 16), size)


def strip(rows):
    return next(size for size in (48, 32, 16) if rows % size == 0)


def cut_rows(rows):
    top = rows // 32 * 16
    return ((0, top), (top, rows - top))


def forward_body(
    n, rows, tokens, width,
    in_ref, cot_ref, flat_ref, wzx_ref, wbc_ref, wdt_ref, wout_ref,
    v_ref, xc_ref, dr_ref, st_ref, dy_ref, dz_ref, branch_ref, early_ref, gate_ref, gain_ref,
    xg_ref, ws_ref, wps_ref, taps_ref, head_ref, chan_ref,
    halo, state, y_all, z_all, dn_all, nl_all, dz_all, xg, cots, ws, wps, sums, red, head_t, until, across_state, tails,
    own_keep, early_keep, lead_keep, lead_send, lead_recv, x_keep, x_over_send, x_over_recv, x_side_send, x_side_recv,
    x_pass_send, x_pass_recv, ring_keep, ring_send, ring_recv, over_send, over_recv,
    side_send, side_recv, pass_send, pass_recv, sum_send, sum_recv,
):
    pairs = width // LANES
    wide = width + 2 * NS
    step = pl.program_id(0)
    steps = LEN // ROWS
    tall = 2 * ROWS
    norming = steps // 2
    gating = norming + 1
    forming = gating + 1
    products = forming + steps // 2
    pos, ring, me, across, beside = neighbours(n)
    opposite = lax.rem(me + 2, 4)
    next_door = me + 1 - 2 * lax.rem(me, 2)
    far = lax.rem(next_door + 2, 4)
    askew = {"tensor": far}
    quarter = tokens // 4
    hops = n // 2
    cuts = cut_rows(rows)
    mine = ring_index(pos, n)

    late = wide + LANES
    parts_of = ((0, width), (width, width))

    def hop(k, part, way, h):
        first, size = cuts[part]
        cols = pl.ds(*parts_of[k])
        block = ring_index(lax.rem(pos + (h if way else n - h), n), n)
        here = wps.at[span(block * rows + first, size), cols]
        return remote(here, here, ring_send.at[way, part, k, h], ring_recv.at[way, part, k, h], ring[way])

    def hop_lands(k, part, way, h):
        first, size = cuts[part]
        block = ring_index(lax.rem(pos + (h + 1 if way else n - h - 1), n), n)
        return span(block * rows + first, size), pl.ds(*parts_of[k])

    def hop_arrival(k, part, way, h):
        here = wps.at[hop_lands(k, part, way, h)]
        return remote(here, here, ring_send.at[way, part, k, h], ring_recv.at[way, part, k, h], ring[way])

    def hop_keep(part, way, h):
        at = hop_lands(1, part, way, h)
        return pltpu.make_async_copy(wps.at[at], wps_ref.at[at], ring_keep.at[way, part, h])

    def hop_ways(h):
        return [(part, way) for part in (0, 1) for way in (0, 1) if h < hops - 1 or part == way]

    def hop_on(k, h):
        for part, way in hop_ways(h - 1) if h > 0 else ():
            hop_arrival(k, part, way, h - 1).wait_recv()
            if k == 1:
                hop_keep(part, way, h - 1).start()
            if h < hops and (part, way) in hop_ways(h):
                hop(k, part, way, h).start()
        if h == 0:
            for part, way in hop_ways(0):
                hop(k, part, way, 0).start()

    def over(k):
        return remote(
            cot_ref.at[pl.ds(k * quarter, quarter)], cots.at[span(me * tokens + k * quarter, quarter)],
            over_send.at[k], over_recv.at[k], across,
        )

    def landed(start, size, send, recv, peer):
        here = cots.at[span(start, size)]
        return remote(here, here, send, recv, peer)

    def over_arrival(k):
        return landed(opposite * tokens + k * quarter, quarter, over_send.at[k], over_recv.at[k], across)

    def passing(k):
        return landed(opposite * tokens + k * quarter, quarter, pass_send.at[k], pass_recv.at[k], beside)

    def pass_arrival(k):
        return landed(far * tokens + k * quarter, quarter, pass_send.at[k], pass_recv.at[k], beside)

    def side():
        return remote(cot_ref, cots.at[span(me * tokens, tokens)], side_send.at[0], side_recv.at[0], beside)

    def side_arrival():
        return landed(next_door * tokens, tokens, side_send.at[0], side_recv.at[0], beside)

    def own_cot():
        return pltpu.make_async_copy(cot_ref, cots.at[span(me * tokens, tokens)], own_keep.at[0])

    def own_z():
        at = span(mine * rows, rows), pl.ds(*parts_of[1])
        return pltpu.make_async_copy(wps.at[at], wps_ref.at[at], own_keep.at[1])

    def pass_on(*pieces):
        for k in pieces:
            over_arrival(k).wait_recv()
            passing(k).start()

    def normalize(k):
        def some(i, _):
            at = span(me * tokens + k * quarter + i * 64, 64)
            squares = jnp.zeros((64, LANES), f32)
            for c in range(D // LANES):
                x = xg[at, c * LANES : (c + 1) * LANES].astype(f32)
                squares = squares + x * x
            inverse = lax.rsqrt(jnp.sum(squares, axis=-1, keepdims=True) / D + norm_eps)
            inverse = jnp.broadcast_to(inverse, (64, LANES))
            for c in range(D // LANES):
                cols = slice(c * LANES, (c + 1) * LANES)
                xg[at, cols] = (xg[at, cols].astype(f32) * inverse * flat_ref[c : c + 1, :]).astype(bf16)
            return 0

        lax.fori_loop(0, quarter // 64, some, 0)

    @pl.when(step == 0)
    def _():
        own_rows = span(me * tokens, tokens)
        greet((*ring, across, beside, askew))
        load = pltpu.make_async_copy(in_ref, xg.at[own_rows], own_keep.at[2])
        load.start()
        own_cot().start()
        mine_at = span(mine * rows, rows)
        ws[mine_at, :width] = wzx_ref[:, 1, :].astype(bf16)
        ws[mine_at, width:wide] = wbc_ref[...].astype(bf16)
        heads = wdt_ref.shape[0]
        unit = jnp.where(
            lax.broadcasted_iota(jnp.int32, (16, LANES), 0) == lax.broadcasted_iota(jnp.int32, (16, LANES), 1), 1.0, 0.0
        ).astype(bf16)
        steps_w = jnp.concatenate([wdt_ref[...], jnp.zeros((16 - heads, rows), f32)], axis=0).astype(bf16)
        ws[mine_at, wide:] = mm(steps_w, unit, TN).astype(bf16)
        load.wait()
        normalize(0)
        pl.semaphore_wait(pltpu.get_barrier_semaphore(), 5)
        started, kept = [], []

        def go(*args):
            copy = remote(*args)
            copy.start()
            started.append(copy)

        def keep(src, dst, sem):
            copy = pltpu.make_async_copy(src, dst, sem)
            copy.start()
            kept.append(copy)

        def arrived(part, way, h, block):
            first, size = cuts[part]
            at = span(block * rows + first, size)
            remote(
                ws.at[at], ws.at[at], lead_send.at[way, part, h], lead_recv.at[way, part, h], ring[way]
            ).wait_recv()
            keep(ws.at[at], ws_ref.at[at], lead_keep.at[way, part, h])

        def lead(h, parts=(0, 1)):
            for part in parts:
                first, size = cuts[part]
                for way in (0, 1):
                    block = ring_index(lax.rem(pos + (h if way else n - h), n), n)
                    here = ws.at[span(block * rows + first, size)]
                    if h > 0:
                        arrived(part, way, h - 1, block)
                    if h == hops - 1 and part != way:
                        continue
                    go(here, here, lead_send.at[way, part, h], lead_recv.at[way, part, h], ring[way])

        def x_over(k):
            at = span(me * tokens + k * quarter, quarter)
            go(xg.at[at], xg.at[at], x_over_send.at[k], x_over_recv.at[k], across)

        def x_pass(k):
            at = span(opposite * tokens + k * quarter, quarter)
            here = xg.at[at]
            remote(here, here, x_over_send.at[k], x_over_recv.at[k], across).wait_recv()
            go(here, here, x_pass_send.at[k], x_pass_recv.at[k], beside)
            keep(here, xg_ref.at[at], x_keep.at[k])

        def x_pass_lands(k):
            at = span(far * tokens + k * quarter, quarter)
            remote(xg.at[at], xg.at[at], x_pass_send.at[k], x_pass_recv.at[k], beside).wait_recv()
            keep(xg.at[at], xg_ref.at[at], x_keep.at[4 + k])

        lead(0, (0,))
        leading = list(started)
        x_over(0)
        for k in (1, 2, 3):
            normalize(k)
            if k == 1:
                x_over(1)
        go(xg.at[own_rows], xg.at[own_rows], x_side_send.at[0], x_side_recv.at[0], beside)
        keep(xg.at[own_rows], xg_ref.at[own_rows], x_keep.at[8])
        wps[mine_at, :width] = wout_ref[...].astype(bf16)
        wps[mine_at, width:] = wzx_ref[:, 0, :].astype(bf16)
        for copy in leading:
            copy.wait_send()
            started.remove(copy)
        lead(0, (1,))
        keep(ws.at[mine_at], ws_ref.at[mine_at], x_keep.at[9])
        own_z().start()
        halo[0:8, :] = jnp.zeros((8, wide), f32)
        state[...] = jnp.zeros_like(state)
        gate_ref[...] = jnp.zeros_like(gate_ref)
        parameter_rows(me, width, flat_ref, taps_ref, head_ref, chan_ref)
        set_heads(head_ref, head_t, until)
        lead(1)
        x_over(2)
        at = span(next_door * tokens, tokens)
        remote(xg.at[at], xg.at[at], x_side_send.at[0], x_side_recv.at[0], beside).wait_recv()
        keep(xg.at[at], xg_ref.at[at], x_keep.at[10])
        side().start()
        lead(2)
        x_over(3)
        x_pass(0)
        x_pass(1)
        for h in range(3, hops):
            lead(h)
        hop_on(0, 0)
        x_pass(2)
        over(0).start()
        x_pass_lands(0)
        x_pass_lands(1)
        x_pass(3)
        for part in (0, 1):
            arrived(part, part, hops - 1, ring_index(lax.rem(pos + n // 2, n), n))
        hop_on(1, 0)
        over(1).start()
        x_pass_lands(2)
        x_pass_lands(3)
        for copy in kept:
            copy.wait()
        for copy in started:
            copy.wait_send()

    def at_tick(tick):
        for k, times in enumerate(((1, 5), (3, 6))):
            for h in (1, 2):
                pl.when(tick == times[h - 1])(functools.partial(hop_on, k, h))

        @pl.when(tick == 2)
        def _():
            over(2).start()

        @pl.when(tick == 4)
        def _():
            over(3).start()
            pass_on(0, 1)

        pl.when(tick == steps - 1)(functools.partial(pass_on, 2))

    @pl.when(step < norming)
    def _():
        def chunk(i, _):
            tick = 2 * step + i
            at_tick(tick)
            scan_step(
                width, tick, i, xg, ws, taps_ref, head_ref, chan_ref,
                v_ref, xc_ref, dr_ref, st_ref, halo, state, y_all, head_t, until, across_state, tails,
                functools.partial(pass_on, 3),
            )
            return 0

        lax.fori_loop(0, 2, chunk, 0)

    @pl.when(step == norming)
    def _():
        for h in range(3, hops):
            for k in (0, 1):
                hop_on(k, h)
        hop_on(0, hops)
        side_arrival().wait_recv()
        for k in range(4):
            pass_arrival(k).wait_recv()
        own_cot().wait()
        own_z().wait()

        def some(i, _):
            at = span(i * tall, tall)
            dn_all[at, :] = mm(cots[at, :], wps[:, :width]).astype(bf16)
            return 0

        lax.fori_loop(0, LEN // tall, some, 0)

    @pl.when(step == gating)
    def _():
        hop_on(1, hops)
        ones = jnp.ones((8, LANES), f32)

        def some(i, _):
            at = span(i * tall, tall)
            z_all[at, :] = mm(xg[at, :], wps[:, width:])
            for sub in range(tall // T):
                rows_at = span(i * tall + sub * T, T)
                squares = jnp.zeros((T, LANES), f32)
                inner = jnp.zeros((T, LANES), f32)
                for p in range(pairs):
                    cols = slice(p * LANES, (p + 1) * LANES)
                    z = z_all[rows_at, cols]
                    gated = y_all[rows_at, cols] * (z * sigmoid(z))
                    squares = squares + gated * gated
                    inner = inner + gated * chan_ref[0:1, cols] * dn_all[rows_at, cols].astype(f32)
                lanes = pl.ds(pl.multiple_of(i * tall + sub * T, T), T)
                sums[me, 0:4, lanes] = mm_exact(ones, squares, NT)[0:4]
                sums[me, 4:8, lanes] = mm_exact(ones, inner, NT)[4:8]
            return 0

        lax.fori_loop(0, LEN // tall, some, 0)

    @pl.when(step == forming - 1)
    def _():
        peers = ((beside, next_door), (across, opposite), (askew, far))
        for k, (peer, _) in enumerate(peers):
            remote(sums.at[me], sums.at[me], sum_send.at[k], sum_recv.at[k], peer).start()
        for h in range(hops):
            for part, way in hop_ways(h):
                for k in (0, 1):
                    hop(k, part, way, h).wait_send()
                hop_keep(part, way, h).wait()
        side().wait_send()
        for k in range(4):
            over(k).wait_send()
            passing(k).wait_send()
        for k, (peer, other) in enumerate(peers):
            remote(sums.at[other], sums.at[other], sum_send.at[k], sum_recv.at[k], peer).wait()
        red[...] = ((sums[0] + sums[1]) + sums[2]) + sums[3]

    @pl.when((step >= forming) & (step < products))
    def _():
        def some(i, _):
            first = (step - forming) * tall + i * ROWS
            lanes = pl.ds(pl.multiple_of(first, ROWS), ROWS)
            q_row = lax.rsqrt(red[0:4, lanes] / DI + norm_eps)
            k_row = q_row * q_row * q_row * red[4:8, lanes] / DI
            turned = jnp.concatenate([q_row, k_row], axis=0).T
            for sub in range(ROWS // T):
                rows_at = slice(sub * T, (sub + 1) * T)
                at = span(first + sub * T, T)
                q, kk = spread(turned[rows_at, 0:1]), spread(turned[rows_at, 4:5])
                for p in range(pairs):
                    cols = slice(p * LANES, (p + 1) * LANES)
                    z, y, dn = z_all[at, cols], y_all[at, cols], dn_all[at, cols].astype(f32)
                    gain = chan_ref[0:1, cols]
                    s = sigmoid(z)
                    sz = z * s
                    gated = y * sz
                    gq = gated * q
                    dg = q * gain * dn - gated * kk
                    gate_ref[:, cols] += jnp.sum((gq * dn).reshape(T // 8, 8, LANES), axis=0)
                    nl_all[at, cols] = (gq * gain).astype(bf16)
                    dz_all[at, cols] = (dg * y * (s + sz * (1.0 - s))).astype(bf16)
                    dn_all[at, cols] = (dg * sz).astype(bf16)
            branch_ref[span(i * ROWS, ROWS), :] = mm(nl_all[span(first, ROWS), :], wps[:, :width], NT).astype(bf16)
            return 0

        lax.fori_loop(0, 2, some, 0, unroll=2)

    def rows_out():
        return [
            pltpu.make_async_copy(src, dst, own_keep.at[2 + k])
            for k, (src, dst) in enumerate(((dz_all, dz_ref), (dn_all, dy_ref)))
        ]

    def early_out(i):
        at = span(i * ROWS, ROWS)
        return [
            pltpu.make_async_copy(src.at[at, pl.ds(0, width)], early_ref.at[at, pl.ds(k * width, width)], early_keep.at[k, i])
            for k, src in enumerate((ws, wps))
        ]

    @pl.when(step == products)
    def _():
        for copy in rows_out():
            copy.start()

        def some(i, _):
            at = span(i * ROWS, ROWS)
            lanes = pl.ds(pl.multiple_of(i * ROWS, ROWS), ROWS)
            grad = mm(xg[:, lanes], dz_all[...], TN)
            ws[at, :width] = grad.astype(bf16)
            share = jnp.zeros((ROWS, LANES), f32)
            for p in range(pairs):
                cols = slice(p * LANES, (p + 1) * LANES)
                w = wps[at, width + p * LANES : width + (p + 1) * LANES]
                share = share + grad[:, cols] * w.astype(f32)
            gain_ref[:, lanes] = mm_exact(jnp.ones((8, LANES), f32), share, NT)
            wps[at, :width] = mm(cots[:, lanes], nl_all[...], TN).astype(bf16)
            for copy in early_out(i):
                copy.start()
            return 0

        lax.fori_loop(0, D // ROWS, some, 0, unroll=3)
        for copy in rows_out():
            copy.wait()

        def done(i, _):
            for copy in early_out(i):
                copy.wait()
            return 0

        lax.fori_loop(0, D // ROWS, done, 0)


def parameter_rows(me, width, flat_ref, taps_ref, head_ref, chan_ref):
    pairs = width // LANES
    heads = width // P_SIZE
    taps_ref[...] = jnp.zeros_like(taps_ref)
    chan_ref[...] = jnp.zeros_like(chan_ref)
    for c in range(pairs):
        cols = slice(c * LANES, (c + 1) * LANES)
        chan_ref[0:1, cols] = flat_ref[pl.ds(GATE_ROW + pairs * me + c, 1), :]
        taps_ref[CONV : CONV + 1, cols] = flat_ref[pl.ds(BIAS_ROW + pairs * me + c, 1), :]
        for k in range(CONV):
            taps_ref[k : k + 1, cols] = flat_ref[pl.ds(TAPS_ROW + 4 * pairs * k + pairs * me + c, 1), :]
    for c in range(2):
        cols = slice(width + c * LANES, width + (c + 1) * LANES)
        taps_ref[CONV : CONV + 1, cols] = flat_ref[BIAS_BC_ROW + c : BIAS_BC_ROW + c + 1, :]
        for k in range(CONV):
            row = TAPS_BC_ROW + 2 * k + c
            taps_ref[k : k + 1, cols] = flat_ref[row : row + 1, :]
    both = jnp.concatenate([flat_ref[HEAD_ROW : HEAD_ROW + 1, :], flat_ref[HEAD_ROW + 1 : HEAD_ROW + 2, :]], axis=1)
    both = jnp.broadcast_to(both, (8, 2 * LANES))
    lane = lax.broadcasted_iota(jnp.int32, (2 * LANES, LANES), 0)
    head = lax.broadcasted_iota(jnp.int32, (2 * LANES, LANES), 1)

    def take(kind):
        match = (lane == 4 * heads * kind + heads * me + head) & (head < heads)
        return mm_exact(both, jnp.where(match, 1.0, 0.0).astype(f32))

    valid = lax.broadcasted_iota(jnp.int32, (8, LANES), 1) < heads
    row = lax.broadcasted_iota(jnp.int32, (8, LANES), 0)
    rates = jnp.where(valid, -jnp.exp(take(1)), 0.0)
    head_ref[...] = jnp.where(row == 0, take(0), jnp.where(row == 1, rates, 0.0))
    skip = mm_exact(take(2), picked(width).astype(f32), NT)
    chan_ref[1:2, :] = skip[0:1]


def picked(width):
    channel = lax.broadcasted_iota(jnp.int32, (width, LANES), 0)
    head = lax.broadcasted_iota(jnp.int32, (width, LANES), 1)
    return jnp.where((channel >= head * P_SIZE) & (channel < (head + 1) * P_SIZE), 1.0, 0.0).astype(bf16)


def scan_step(
    width, tick, i, xg, w_ref, taps_ref, head_ref, chan_ref,
    v_ref, xc_ref, dr_ref, st_ref, halo, state, y_all, head_t, until, across_state, tails, late_turn,
):
    pairs = width // LANES
    wide = width + 2 * NS
    mine = span(tick * ROWS, ROWS)
    dr_ref[span(i * ROWS, ROWS), :] = mm(xg[mine, :], w_ref[:, wide:])
    halo[8 : 8 + ROWS, :] = mm(xg[mine, :], w_ref[:, :wide])
    low_half = block_iota(1) < P_SIZE
    causal = block_iota(0) >= block_iota(1)

    def convolved(sub, block):
        cols = slice(block * LANES, (block + 1) * LANES)
        total = taps_ref[CONV : CONV + 1, cols]
        for k in range(CONV):
            first = 8 - (CONV - 1) + k + sub * T
            total = total + taps_ref[k : k + 1, cols] * halo[first : first + T, cols]
        rows = span(i * ROWS + sub * T, T)
        xc_ref[rows, cols] = total.astype(bf16)
        v_ref[rows, cols] = halo[8 + sub * T : 8 + (sub + 1) * T, cols].astype(bf16)
        return total * sigmoid(total)

    for sub in range(ROWS // T):
        rows = span(i * ROWS + sub * T, T)
        _, _, decay_t, dt, decay = head_rows(dr_ref, head_t, until, rows)
        b_low = convolved(sub, pairs).astype(bf16)
        c_low = convolved(sub, pairs + 1).astype(bf16)
        b_t = b_low.T
        scores = jnp.where(causal, mm(c_low, b_low, NT), 0.0)
        entering = state[...].astype(bf16)
        st_ref[i * (ROWS // T) + sub] = entering
        across_state[...] = mm(c_low, entering)
        for p in range(pairs):
            cols = slice(p * LANES, (p + 1) * LANES)
            x = convolved(sub, p)
            l1, l2 = spread(decay[:, 2 * p : 2 * p + 1]), spread(decay[:, 2 * p + 1 : 2 * p + 2])
            both = jnp.where(low_half, l1, l2)
            dtb = jnp.where(
                low_half, spread(dt[:, 2 * p : 2 * p + 1]), spread(dt[:, 2 * p + 1 : 2 * p + 2])
            )
            u = x * dtb
            m1 = scores * jnp.exp2(jnp.minimum(l1 - decay_t[2 * p : 2 * p + 1, :], 0.0))
            m2 = scores * jnp.exp2(jnp.minimum(l2 - decay_t[2 * p + 1 : 2 * p + 2, :], 0.0))
            mixing = jnp.concatenate([m1.astype(bf16), m2.astype(bf16)], axis=1)
            u_low = u.astype(bf16)
            zero = jnp.zeros_like(u_low)
            parts = jnp.concatenate(
                [jnp.where(low_half, u_low, zero), jnp.where(low_half, zero, u_low)], axis=0
            )
            last = both[T - 1 : T, :]
            y = mm(mixing, parts) + jnp.exp2(both) * across_state[:, cols] + chan_ref[1:2, cols] * x
            tails[:, cols] = (u * jnp.exp2(last - both)).astype(bf16)
            state[:, cols] = jnp.exp2(last) * state[:, cols]
            y_all[span(tick * ROWS + sub * T, T), cols] = y
        state[...] = state[...] + mm(b_t, tails[...])
        if sub == 0:
            pl.when(tick == LEN // ROWS - 1)(late_turn)
    halo[0:8, :] = halo[ROWS : ROWS + 8, :]


def ssd_forward(n, layer_input, out_grad, flat, w_zx, w_bc, w_dt, w_out):
    rows, width = w_out.shape
    tokens = layer_input.shape[0]
    length = 4 * tokens
    wide = width + 2 * NS
    tall = 2 * ROWS
    steps = length // tall
    forming = steps + 2
    products = forming + steps
    subs = tall // T
    assert length == LEN
    row = lambda m: pl.BlockSpec((tall, m), lambda i: (jnp.minimum(i, steps - 1), 0))
    form = lambda m: pl.BlockSpec((tall, m), lambda i: (jnp.clip(i - forming, 0, steps - 1), 0))
    whole = lambda a: pl.BlockSpec(a.shape, lambda i: (0,) * a.ndim, pipeline_mode=pl.Buffered(1))
    fixed = lambda m: pl.BlockSpec((8, m), lambda i: (0, 0))
    anywhere = pl.BlockSpec(memory_space=pl.ANY)
    vm, dma = pltpu.VMEM, pltpu.SemaphoreType.DMA
    hops, lead = dma((2, 2, 2, n // 2)), dma((2, 2, n // 2))
    shape = lambda dims, dtype: jax.ShapeDtypeStruct(dims, dtype)
    return pl.pallas_call(
        functools.partial(forward_body, n, rows, tokens, width),
        grid=(products + 1,),
        in_specs=[anywhere, anywhere, *(whole(a) for a in (flat, w_zx, w_bc, w_dt, w_out))],
        out_specs=[
            row(wide), row(wide), row(LANES), pl.BlockSpec((subs, NS, width), lambda i: (jnp.minimum(i, steps - 1), 0, 0)),
            anywhere, anywhere, form(D), anywhere,
            fixed(width), fixed(D), anywhere, anywhere, anywhere, *(fixed(m) for m in (wide, LANES, width)),
        ],
        out_shape=[
            shape((length, wide), bf16), shape((length, wide), bf16), shape((length, LANES), f32),
            shape((length // T, NS, width), bf16), shape((length, width), bf16), shape((length, width), bf16),
            shape((length, D), bf16), shape((D, 2 * width), bf16), shape((8, width), f32), shape((8, D), f32),
            shape((length, D), bf16), shape((D, wide + LANES), bf16), shape((D, 2 * width), bf16),
            *(shape((8, m), f32) for m in (wide, LANES, width)),
        ],
        scratch_shapes=[
            vm((ROWS + 8, wide), f32), vm((NS, width), f32), vm((length, width), f32), vm((length, width), f32),
            *(vm((length, width), bf16) for _ in range(3)),
            vm((length, D), bf16), vm((length, D), bf16), vm((D, wide + LANES), bf16), vm((D, 2 * width), bf16),
            vm((4, 8, length), f32), vm((8, length), f32), vm((2, HEADS, LANES), f32), vm((3 * T, LANES), bf16),
            vm((T, width), f32), vm((T, width), bf16),
            dma((4,)), dma((2, D // ROWS)), lead, lead, lead, dma((11,)), dma((4,)), dma((4,)), dma((1,)), dma((1,)),
            dma((4,)), dma((4,)), lead, hops, hops, dma((4,)), dma((4,)),
            dma((1,)), dma((1,)), dma((4,)), dma((4,)), dma((3,)), dma((3,)),
        ],
        compiler_params=pltpu.CompilerParams(collective_id=2, has_side_effects=True, vmem_limit_bytes=ROOM),
        name="layer_forward",
    )(layer_input, out_grad, flat, w_zx, w_bc, w_dt, w_out)


def backward_body(
    n, own_rows, tokens, width,
    dy_ref, v_ref, xc_ref, dr_ref, st_ref, gate_ref, taps_ref, head_ref, chan_ref, early_ref, branch_ref,
    d_ref, small_ref, oearly_ref, obranch_ref,
    dxh, dstate, yst, bds, dyeb, utb, products, turn, acc, hacc, pick_ref, pick_t, fades, head_t, until_ref, reach_ref,
    own, slots, near, held, over_slot,
    load_sem, ring_send, ring_recv, near_send, near_recv, over_send, over_recv,
):
    pairs = width // LANES
    wide = width + 2 * NS
    step = pl.program_id(0)
    steps = LEN // ROWS
    subs = ROWS // T
    pos, ring, me, across, beside = neighbours(n)
    opposite = lax.rem(me + 2, 4)
    next_door = me + 1 - 2 * lax.rem(me, 2)
    far = lax.rem(next_door + 2, 4)
    half = tokens // 2
    cuts = cut_rows(own_rows)

    def block_at(way, count):
        return ring_index(lax.rem(pos + (count if way else n - count), n), n)

    def hop(k, way, h):
        first, size = cuts[way]
        if h == 0:
            src = early_ref.at[span(block_at(way, 1) * own_rows + first, size), pl.ds(k * width, width)]
        else:
            src = slots[way][k].at[h - 1]
        return remote(
            src, slots[way][k].at[h], ring_send.at[way, k, h], ring_recv.at[way, k, h], ring[way]
        )

    def near_copy(turned, part):
        start = (next_door if turned else far) * tokens + part * half
        return remote(
            branch_ref.at[span(start, half)], near.at[turned, part],
            near_send.at[turned, part], near_recv.at[turned, part], beside,
        )

    def held_copy(turned, part):
        start = (me if turned else opposite) * tokens + part * half
        return pltpu.make_async_copy(
            branch_ref.at[span(start, half)], held.at[turned, part], load_sem.at[2 * turned + part]
        )

    def over_copy(part):
        return remote(held.at[0, part], over_slot.at[part], over_send.at[part], over_recv.at[part], across)

    def own_copy():
        return pltpu.make_async_copy(early_ref, own, load_sem.at[4])

    def ring_turn(k, h):
        for way in (0, 1):
            first, size = cuts[way]
            hop(k, way, h).wait_recv()
            block = block_at(way, 2 + h) if h < n - 2 else block_at(way, 0)

            tile = strip(size)

            def some(i, _, way=way, first=first, block=block, tile=tile):
                cols = slice(k * width, (k + 1) * width)
                came = slots[way][k][h, span(i * tile, tile), :]
                mine = own[span(block * own_rows + first + i * tile, tile), cols]
                if h < n - 2:
                    slots[way][k][h, span(i * tile, tile), :] = came + mine
                else:
                    oearly_ref[span(first + i * tile, tile), cols] = came.astype(f32) + mine.astype(f32)
                return 0

            lax.fori_loop(0, size // tile, some, 0)
            if h < n - 2:
                hop(k, way, h + 1).start()

    def ring_poll(k, tick):
        for h in range(n - 1):
            pl.when(tick == min(h + 1, steps - 1))(functools.partial(ring_turn, k, h))

    def add_near(turned):
        for part in (0, 1):
            held_copy(turned, part).wait()
            near_copy(turned, part).wait_recv()

            def some(i, _, part=part):
                at = span(i * 32, 32)
                held[turned, part, at, :] = held[turned, part, at, :] + near[turned, part, at, :]
                return 0

            lax.fori_loop(0, half // 32, some, 0)
            if not turned:
                over_copy(part).start()

    @pl.when(step == 0)
    def _():
        enter((*ring, across, beside))
        for way in (0, 1):
            hop(0, way, 0).start()
        for turned in (0, 1):
            for part in (0, 1):
                near_copy(turned, part).start()
                held_copy(turned, part).start()
        own_copy().start()
        dxh[T : T + 8, :] = jnp.zeros((8, wide), f32)
        dstate[...] = jnp.zeros_like(dstate)
        acc[...] = jnp.zeros_like(acc)
        hacc[...] = jnp.zeros_like(hacc)
        turn[...] = jnp.zeros_like(turn)
        pick_ref[...] = picked(width)
        channel = lax.broadcasted_iota(jnp.int32, (HEADS, width), 1)
        head = lax.broadcasted_iota(jnp.int32, (HEADS, width), 0)
        mine = (channel >= head * P_SIZE) & (channel < (head + 1) * P_SIZE)
        pick_t[...] = jnp.where(mine, 1.0, 0.0).astype(bf16)
        set_heads(head_ref, head_t, until_ref)
        from_here = jnp.where(block_iota(0) >= block_iota(1), 1.0, 0.0).astype(bf16)
        after = jnp.where(block_iota(0) < block_iota(1), 1.0, 0.0).astype(bf16)
        for k, matrix in enumerate((from_here, from_here, after, after)):
            reach_ref[k * T : (k + 1) * T, :] = matrix
        products[3 * T :, :] = jnp.zeros((HEADS, width), bf16)

    low_half = block_iota(1) < P_SIZE
    row_at, col_at = block_iota(0), block_iota(1)
    until = row_at <= col_at
    pair_lane = lax.broadcasted_iota(jnp.int32, (8, 2 * T), 1)
    pair_row = lax.broadcasted_iota(jnp.int32, (8, 2 * T), 0)
    each = jnp.where(lax.div(pair_lane, T) == pair_row, 1.0, 0.0).astype(bf16)
    ones = jnp.ones((8, T), bf16)

    def add(index, cols, value):
        acc[index, :, cols] += jnp.sum(value.reshape(T // 8, 8, LANES), axis=0)

    def conv_back(rows, block, d_act, xc, s, act):
        cols = slice(block * LANES, (block + 1) * LANES)
        dxh[0:T, cols] = d_act * (s + act * (1.0 - s))
        v = v_ref[rows, cols].astype(f32)
        total = None
        for m in range(CONV):
            moved = dxh[m : m + T, cols]
            if m == 0:
                add(CONV, cols, moved)
            add(CONV - 1 - m, cols, v * moved)
            term = taps_ref[CONV - 1 - m : CONV - m, cols] * moved
            total = term if total is None else total + term
        d_ref[rows, cols] = total.astype(bf16)

    def work(i, _):
        tick = 2 * step + i
        chunk = 1 - i

        @pl.when(tick == 1)
        def _():
            own_copy().wait()
            add_near(0)

        pl.when(tick == 2)(functools.partial(add_near, 1))
        ring_poll(0, tick)
        for sub in reversed(range(subs)):
            rows = span(chunk * ROWS + sub * T, T)
            block_state = chunk * subs + sub
            raw_t, dt_t, decay_t, dt, decay = head_rows(dr_ref, head_t, until_ref, rows)
            b_cols = slice(width, width + NS)
            c_cols = slice(width + NS, width + 2 * NS)
            b_xc, c_xc = xc_ref[rows, b_cols].astype(f32), xc_ref[rows, c_cols].astype(f32)
            b_s, c_s = sigmoid(b_xc), sigmoid(c_xc)
            b_act, c_act = b_xc * b_s, c_xc * c_s
            b_low, c_low = b_act.astype(bf16), c_act.astype(bf16)
            c_t = c_low.T
            scores_t = jnp.where(until, mm(b_low, c_low, NT), 0.0)
            ds_low = dstate[...].astype(bf16)
            yst[...] = mm(c_low, st_ref[block_state])
            bds[...] = mm(b_low, ds_low)
            d_scores = jnp.zeros((T, LANES), f32)
            for p in range(pairs):
                cols = slice(p * LANES, (p + 1) * LANES)
                dy_low = dy_ref[rows, cols]
                dy = dy_low.astype(f32)
                xc = xc_ref[rows, cols].astype(f32)
                xs = sigmoid(xc)
                x = xc * xs
                l1, l2 = spread(decay[:, 2 * p : 2 * p + 1]), spread(decay[:, 2 * p + 1 : 2 * p + 2])
                both = jnp.where(low_half, l1, l2)
                dtb = jnp.where(
                    low_half, spread(dt[:, 2 * p : 2 * p + 1]), spread(dt[:, 2 * p + 1 : 2 * p + 2])
                )
                u = x * dtb
                last = both[T - 1 : T, :]
                e1 = jnp.exp2(jnp.minimum(decay_t[2 * p : 2 * p + 1, :] - l1, 0.0))
                e2 = jnp.exp2(jnp.minimum(decay_t[2 * p + 1 : 2 * p + 2, :] - l2, 0.0))
                zero = jnp.zeros_like(dy_low)
                dy_parts = jnp.concatenate(
                    [jnp.where(low_half, dy_low, zero), jnp.where(low_half, zero, dy_low)], axis=0
                )
                du_in = mm(
                    jnp.concatenate([(scores_t * e1).astype(bf16), (scores_t * e2).astype(bf16)], axis=1), dy_parts
                )
                d_mix = mm(u.astype(bf16), dy_parts, NT)
                d1, d2 = d_mix[:, :T] * e1, d_mix[:, T:] * e2
                d_scores = d_scores + d1 + d2
                held_pairs = jnp.concatenate([(d1 * scores_t).astype(bf16), (d2 * scores_t).astype(bf16)], axis=1)
                reached_by = mm(ones, held_pairs)
                leaving = mm(each, held_pairs, NT)
                turn[2 * p : 2 * p + 1, :] = reached_by[0:1, :T] - leaving[0:1]
                turn[2 * p + 1 : 2 * p + 2, :] = reached_by[0:1, T:] - leaving[1:2]
                tail = jnp.exp2(last - both)
                fades[0:1, cols] = jnp.exp2(last)
                dye = dy * jnp.exp2(both)
                du_out = tail * bds[:, cols]
                du = du_in + du_out
                products[0:T, cols] = (dye * yst[:, cols]).astype(bf16)
                products[T : 2 * T, cols] = (u * du_out).astype(bf16)
                products[2 * T : 3 * T, cols] = (x * du).astype(bf16)
                dyeb[:, cols] = dye.astype(bf16)
                utb[:, cols] = (u * tail).astype(bf16)
                add(CONV + 1, cols, dy * x)
                conv_back(rows, p, dtb * du + chan_ref[1:2, cols] * dy, xc, xs, x)
            d_scores = jnp.where(until, d_scores, 0.0).astype(bf16)
            d_b = mm(d_scores, c_low) + mm(utb[...], ds_low, NT)
            d_c = mm(d_scores, b_low, TN) + mm(dyeb[...], st_ref[block_state], NT)
            conv_back(rows, pairs, d_b, b_xc, b_s, b_act)
            conv_back(rows, pairs + 1, d_c, c_xc, c_s, c_act)
            fade = fades[0:1, :]
            before_ds = dstate[...]
            through = jnp.sum(before_ds * st_ref[block_state].astype(f32), axis=0, keepdims=True) * fade
            products[3 * T : 3 * T + HEADS, :] = jnp.broadcast_to(through, (HEADS, width)).astype(bf16)
            dstate[...] = fade * before_ds + mm(c_t, dyeb[...])
            by_head = mm(pick_t[...], products[...], NT)
            inside = pieces(turn[...] + by_head[:, :T], 2)
            outside = pieces(by_head[:, T : 2 * T], 2)
            reached = mm(jnp.concatenate([inside, outside], axis=1), reach_ref[...])
            reached = reached + jnp.broadcast_to(by_head[:, 3 * T : 3 * T + 1], (HEADS, T))
            d_raw = (head_t[1] * reached + by_head[:, 2 * T : 3 * T]) * sigmoid(raw_t)
            d_ref[rows, wide:] = columns_of(d_raw).astype(bf16)
            hacc[0] += d_raw
            hacc[1] += dt_t * reached
            dxh[T : T + 8, :] = dxh[0:8, :]
            if sub == 1:
                @pl.when(tick == 0)
                def _():
                    for way in (0, 1):
                        hop(1, way, 0).start()

                ring_poll(1, tick)
        return 0

    lax.fori_loop(0, 2, work, 0)

    @pl.when(step == steps // 2 - 1)
    def _():
        total = lambda a: jnp.sum(a, axis=0, keepdims=True)
        for k in range(CONV + 1):
            small_ref[k : k + 1, :] = total(acc[k])
        small_ref[CONV + 1 : CONV + 2, :width] = total(gate_ref[...])
        small_ref[CONV + 1 : CONV + 2, width : width + LANES] = total(columns_of(hacc[0]))
        small_ref[CONV + 1 : CONV + 2, width + LANES :] = total(columns_of(hacc[1])) * head_ref[1:2, :]
        small_ref[CONV + 2 :, :] = jnp.zeros((2, wide), f32)
        skip = mm_exact(acc[CONV + 1, :, :width], pick_ref[...].astype(f32))
        small_ref[CONV + 3 : CONV + 4, 512 : 512 + LANES] = total(skip)
        for part in (0, 1):
            over_copy(part).wait_recv()

            def some(i, _, part=part):
                at = span(part * half + i * 32, 32)
                here = span(i * 32, 32)
                total = held[1, part, here, :].astype(f32) + over_slot[part, here, :].astype(f32)
                obranch_ref[at, :] = total.astype(bf16)
                return 0

            lax.fori_loop(0, half // 32, some, 0)
        for part in (0, 1):
            over_copy(part).wait_send()
            for turned in (0, 1):
                near_copy(turned, part).wait_send()
        for h in range(n - 1):
            for k in (0, 1):
                for way in (0, 1):
                    hop(k, way, h).wait_send()


def ssd_backward(n, dy, v, xc, dr, st, gate, taps, head, chan, early, branch):
    length, width = dy.shape
    wide = width + 2 * NS
    tall = 2 * ROWS
    steps = length // tall
    subs = tall // T
    own_rows, tokens = D // n, length // 4
    half = tokens // 2
    row = lambda m: pl.BlockSpec((tall, m), lambda i: (steps - 1 - i, 0))
    whole = lambda a: pl.BlockSpec(a.shape, lambda i: (0,) * a.ndim, pipeline_mode=pl.Buffered(1))
    fixed = lambda *shape: pl.BlockSpec(shape, lambda i: (0,) * len(shape))
    anywhere = pl.BlockSpec(memory_space=pl.ANY)
    vm, dma = pltpu.VMEM, pltpu.SemaphoreType.DMA
    return pl.pallas_call(
        functools.partial(backward_body, n, own_rows, tokens, width),
        grid=(steps,),
        in_specs=[
            row(width), row(wide), row(wide), row(LANES),
            pl.BlockSpec((subs, NS, width), lambda i: (steps - 1 - i, 0, 0)),
            whole(gate), whole(taps), whole(head), whole(chan), anywhere, anywhere,
        ],
        out_specs=[
            row(wide + LANES), fixed(8, wide), fixed(own_rows, 2 * width), fixed(tokens, D),
        ],
        out_shape=[
            jax.ShapeDtypeStruct((length, wide + LANES), bf16),
            jax.ShapeDtypeStruct((8, wide), f32),
            jax.ShapeDtypeStruct((own_rows, 2 * width), f32),
            jax.ShapeDtypeStruct((tokens, D), bf16),
        ],
        scratch_shapes=[
            vm((T + 8, wide), f32), vm((NS, width), f32), vm((T, width), f32), vm((T, width), f32),
            vm((T, width), bf16), vm((T, width), bf16), vm((3 * T + HEADS, width), bf16),
            vm((HEADS, T), f32), vm((CONV + 2, 8, wide), f32), vm((2, HEADS, T), f32),
            vm((width, LANES), bf16), vm((HEADS, width), bf16), vm((8, width), f32), vm((2, HEADS, LANES), f32),
            vm((3 * T, LANES), bf16), vm((4 * T, LANES), bf16),
            vm((D, 2 * width), bf16),
            [[vm((n - 1, size, width), bf16) for _ in (0, 1)] for _, size in cut_rows(own_rows)],
            vm((2, 2, half, D), bf16), vm((2, 2, half, D), bf16), vm((2, half, D), bf16),
            dma((5,)), dma((2, 2, n - 1)), dma((2, 2, n - 1)), dma((2, 2)), dma((2, 2)), dma((2,)), dma((2,)),
        ],
        compiler_params=pltpu.CompilerParams(
            collective_id=3, has_side_effects=True, vmem_limit_bytes=ROOM
        ),
        name="layer_backward",
    )(dy, v, xc, dr, st, gate, taps, head, chan, early, branch)


def reduce_body(
    n, rows, tokens, starts,
    xg_ref, d_ref, dz_ref, wp_ref, w_ref, small_ref, flat_ref, gain_ref,
    oxs_ref, oback_ref, bc_ref, oflat_ref,
    xg, d, dz, wz, w, work, grads, slots, staged, near, over, smalls, tens, bc_slot,
    load_sem, ring_send, ring_recv, near_send, near_recv, over_send, over_recv,
    small_send, small_recv, ten_send, ten_recv, bc_send, bc_recv,
):
    pos, ring, me, across, beside = neighbours(n)
    cuts = cut_rows(rows)
    core = lax.rem(me, 2)
    opposite = lax.rem(me + 2, 4)
    next_door = me + 1 - 2 * core
    far = lax.rem(next_door + 2, 4)
    half = tokens // 2
    late = d.shape[1]
    width = dz.shape[1]
    tile = 2 * LANES
    tiles = D // tile
    columns = [pl.ds(lo, hi - lo) for lo, hi in starts]
    sources = [(d_ref.at[:, columns[0]], d.at[:, columns[0]])]
    sources += [(xg_ref.at[:, pl.ds(i * tile, tile)], xg.at[:, pl.ds(i * tile, tile)]) for i in range(tiles)]
    sources += [(d_ref.at[:, some], d.at[:, some]) for some in columns[1:]]
    sources += [
        (dz_ref, dz), (w_ref, w), (wp_ref.at[:, pl.ds(width, width)], wz), (small_ref, smalls.at[pos]),
    ]
    loads = [pltpu.make_async_copy(src, dst, load_sem.at[k]) for k, (src, dst) in enumerate(sources)]
    for load in loads:
        load.start()
    askew = {"tensor": far}
    enter((*ring, across, beside, askew))
    started = []

    def go(*args):
        copy = remote(*args)
        copy.start()
        started.append(copy)

    def block_at(way, count):
        return ring_index(lax.rem(pos + (count if way else n - count), n), n)

    def hop(k, way, h):
        lo, hi = starts[k]
        first, size = cuts[way]
        if h == 0:
            src = grads.at[span(block_at(way, 1) * rows + first, size), pl.ds(lo, hi - lo)]
        else:
            src = slots[way][k].at[h - 1]
        return remote(
            src, slots[way][k].at[h], ring_send.at[way, k, h], ring_recv.at[way, k, h], ring[way]
        )

    def product(k):
        lo, hi = starts[k]

        def some(i, _):
            at = pl.ds(pl.multiple_of(i * tile, tile), tile)
            if k == 0:
                pltpu.make_async_copy(xg_ref.at[:, at], xg.at[:, at], load_sem.at[1 + i]).wait()
            grads[at, lo:hi] = mm(xg[:, at], d[:, lo:hi], TN).astype(bf16)
            return 0

        if k < 2:
            loads[0 if k == 0 else tiles + k].wait()
        lax.fori_loop(0, tiles, some, 0)
        for way in (0, 1):
            hop(k, way, 0).start()

    def near_copy(turned, part):
        return remote(
            staged.at[turned, part], near.at[turned, part],
            near_send.at[turned, part], near_recv.at[turned, part], beside,
        )

    def over_copy(part):
        return remote(near.at[0, part], over.at[part], over_send.at[part], over_recv.at[part], across)

    def ring_turn(k, h):
        lo, hi = starts[k]
        for way in (0, 1):
            first, size = cuts[way]
            slot = slots[way][k].at[h]
            remote(slot, slot, ring_send.at[way, k, h], ring_recv.at[way, k, h], ring[way]).wait_recv()
            block = block_at(way, 2 + h) if h < n - 2 else block_at(way, 0)

            tile = strip(size)

            def some(i, _, way=way, first=first, block=block, tile=tile):
                came = slots[way][k][h, span(i * tile, tile), :]
                mine = grads[span(block * rows + first + i * tile, tile), lo:hi]
                if h < n - 2:
                    slots[way][k][h, span(i * tile, tile), :] = came + mine
                else:
                    oxs_ref[span(first + i * tile, tile), lo:hi] = came.astype(f32) + mine.astype(f32)
                return 0

            lax.fori_loop(0, size // tile, some, 0)
            if h < n - 2:
                hop(k, way, h + 1).start()

    def small_hop(way, h):
        here = smalls.at[lax.rem(pos + (h if way else n - h), n)]
        go(here, here, small_send.at[way, h], small_recv.at[way, h], ring[way])

    def small_lands(way, h):
        here = smalls.at[lax.rem(pos + (h + 1 if way else n - h - 1), n)]
        remote(here, here, small_send.at[way, h], small_recv.at[way, h], ring[way]).wait_recv()

    product(0)
    product(1)
    for load in loads[tiles + 2 :]:
        load.wait()
    turns = {0: [(0, 0)], 1: [(1, 0)], 2: [(0, 1)], 3: [(1, 1)], 4: [(0, 2), (1, 2)], 5: [(2, 0)], 6: [(0, 3), (1, 3)], 7: [(2, 1)]}
    taken = [sum(k == group for some in turns.values() for k, _ in some) for group in range(len(starts))]

    def block(i, _):
        pl.when(i == 4)(functools.partial(product, 2))
        which, part = lax.div(i, 2), lax.rem(i, 2)
        own = lax.rem(which, 2)
        turned = lax.div(which, 2)
        target = lax.rem(next_door + own * (me - next_door) + 2 * (1 - turned), 4)
        at = span(target * tokens + part * half, half)
        total = mm(dz[at, :], wz[...], NT) + mm(d[at, :], w[...], NT)
        work[...] = total

        @pl.when(own == 0)
        def _():
            staged[turned, part] = work[...].astype(bf16)
            near_copy(turned, part).start()

        @pl.when(own == 1)
        def _():
            near_copy(turned, part).wait_recv()

        @pl.when(which == 1)
        def _():
            near[0, part] = (work[...] + near[0, part].astype(f32)).astype(bf16)
            over_copy(part).start()

        @pl.when(which == 3)
        def _():
            near[1, part] = (work[...] + near[1, part].astype(f32)).astype(bf16)

        for at_block, some in turns.items():

            @pl.when(i == at_block)
            def _(some=some):
                for k, h in some:
                    ring_turn(k, h)

        return 0

    lax.fori_loop(0, 8, block, 0)
    for i in range(tiles):
        share = jnp.zeros((tile, LANES), f32)
        for c in range(late // LANES):
            cols = slice(c * LANES, (c + 1) * LANES)
            at = slice(i * tile, (i + 1) * tile)
            share = share + grads[at, cols].astype(f32) * w[at, cols].astype(f32)
        total = mm_exact(jnp.ones((8, LANES), f32), share, NT)[0:1] + gain_ref[0:1, i * tile : (i + 1) * tile]
        for c in range(2 * i, 2 * i + 2):
            row, col = 6 + c // 8, (c % 8) * LANES
            part = total[:, (c - 2 * i) * LANES : (c - 2 * i + 1) * LANES]
            smalls[pos, row : row + 1, col : col + LANES] = part / flat_ref[c : c + 1, :]

    rest = [(k, h) for h in range(n - 1) for k in (2, 0, 1) if h >= taken[k]]
    rest.sort(key=lambda turn: turn[1] - taken[turn[0]])

    def small_step(s):
        for way in (0, 1):
            if s > 0 and (way == 0 or s < n // 2):
                small_lands(way, s - 1)
            if s < n // 2 - way:
                small_hop(way, s)

    small_step(0)
    steps_done = 1
    for at, (k, h) in enumerate(rest):
        ring_turn(k, h)
        if (k, h) == (0, n - 2):
            bc_slot[0] = oxs_ref[:, starts[0][0] : starts[0][0] + 2 * NS]
            go(bc_slot.at[0], bc_slot.at[1], bc_send.at[0], bc_recv.at[0], beside)
        if at % 2 == 1 and steps_done < n // 2:
            small_step(steps_done)
            steps_done += 1
    for s in range(steps_done, n // 2):
        small_step(s)
    small_lands(0, n // 2 - 1)

    total = smalls[0]
    for i in range(1, n):
        total = total + smalls[i]
    tens[me] = total
    others = ((beside, next_door), (across, opposite), (askew, far))
    for k, (peer, _) in enumerate(others):
        go(tens.at[me], tens.at[me], ten_send.at[k], ten_recv.at[k], peer)
    remote(bc_slot.at[1], bc_slot.at[1], bc_send.at[0], bc_recv.at[0], beside).wait_recv()
    bc_slot[2] = bc_slot[0] + bc_slot[1]
    go(bc_slot.at[2], bc_slot.at[3], bc_send.at[1], bc_recv.at[1], across)
    for part in (0, 1):
        over_copy(part).wait_recv()

        def some(i, _, part=part):
            at = span(part * half + i * 32, 32)
            here = span(i * 32, 32)
            oback_ref[at, :] = (near[1, part, here, :].astype(f32) + over[part, here, :].astype(f32)).astype(bf16)
            return 0

        lax.fori_loop(0, half // 32, some, 0)
    for k, (peer, target) in enumerate(others):
        here = tens.at[target]
        remote(here, here, ten_send.at[k], ten_recv.at[k], peer).wait_recv()
    flat_gradients(width, tens, oflat_ref)
    remote(bc_slot.at[3], bc_slot.at[3], bc_send.at[1], bc_recv.at[1], across).wait_recv()
    bc_ref[...] = bc_slot[2] + bc_slot[3]
    for part in (0, 1):
        over_copy(part).wait_send()
        for turned in (0, 1):
            near_copy(turned, part).wait_send()
    for k in range(len(starts)):
        for way in (0, 1):
            for h in range(n - 1):
                hop(k, way, h).wait_send()
    for copy in started:
        copy.wait_send()


def flat_gradients(width, tens, out_ref):
    pairs = width // LANES
    heads = width // P_SIZE

    def sums(row, col):
        total = tens[0, row : row + 1, col : col + LANES]
        for t in range(1, 4):
            total = total + tens[t, row : row + 1, col : col + LANES]
        return total

    def put(row, value):
        out_ref[row : row + 1, :] = value

    for c in range(D // LANES):
        put(c, sums(6 + c // 8, (c % 8) * LANES))
    for t in range(4):
        for c in range(pairs):
            cols = slice(c * LANES, (c + 1) * LANES)
            put(GATE_ROW + pairs * t + c, tens[t, CONV + 1 : CONV + 2, cols])
            put(BIAS_ROW + pairs * t + c, tens[t, CONV : CONV + 1, cols])
            for k in range(CONV):
                put(TAPS_ROW + 4 * pairs * k + pairs * t + c, tens[t, k : k + 1, cols])
    for c in range(2):
        put(BIAS_BC_ROW + c, sums(CONV, width + c * LANES))
        for k in range(CONV):
            put(TAPS_BC_ROW + 2 * k + c, sums(k, width + c * LANES))
    kinds = ((CONV + 1, width), (CONV + 1, width + LANES), (CONV + 3, 512))
    rows = [tens[t, row : row + 1, col : col + LANES] for row, col in kinds for t in range(4)]
    rows = jnp.concatenate(rows + [jnp.zeros((16 - len(rows), LANES), f32)], axis=0)
    lane = lax.broadcasted_iota(jnp.int32, (LANES, 2 * LANES), 1)
    entry = lax.broadcasted_iota(jnp.int32, (LANES, 2 * LANES), 0)
    spread_out = mm_exact(rows, jnp.where(lax.rem(lane, heads) == entry, 1.0, 0.0).astype(f32))
    at = lax.broadcasted_iota(jnp.int32, (16, 2 * LANES), 1)
    source = lax.broadcasted_iota(jnp.int32, (16, 2 * LANES), 0)
    line = jnp.sum(jnp.where(lax.div(at, heads) == source, spread_out, 0.0), axis=0, keepdims=True)
    put(HEAD_ROW, line[:, :LANES])
    put(HEAD_ROW + 1, line[:, LANES:])


def reduce_all(n, xg, d, dz, wp, w, small, flat, gain):
    rows, tokens = D // n, dz.shape[0] // 4
    width, late = dz.shape[1], d.shape[1]
    starts = ((width, late), (0, width // 2), (width // 2, width))
    half = tokens // 2
    dma, vm = pltpu.SemaphoreType.DMA, pltpu.VMEM
    anywhere = pl.BlockSpec(memory_space=pl.ANY)
    inside = pl.BlockSpec(memory_space=pltpu.VMEM)
    return pl.pallas_call(
        functools.partial(reduce_body, n, rows, tokens, starts),
        in_specs=[anywhere] * 6 + [inside] * 2,
        out_specs=[inside] * 4,
        out_shape=[
            jax.ShapeDtypeStruct((rows, late), f32),
            jax.ShapeDtypeStruct((tokens, D), bf16),
            jax.ShapeDtypeStruct((rows, 2 * NS), f32),
            jax.ShapeDtypeStruct((FLAT_ROWS, LANES), f32),
        ],
        scratch_shapes=[
            vm(xg.shape, bf16), vm(d.shape, bf16), vm(dz.shape, bf16), vm((D, width), bf16),
            vm((D, late), bf16),
            vm((half, D), f32), vm((D, late), bf16),
            [[vm((n - 1, size, hi - lo), bf16) for lo, hi in starts] for _, size in cut_rows(rows)],
            vm((2, 2, half, D), bf16), vm((2, 2, half, D), bf16), vm((2, half, D), bf16),
            vm((n, *small.shape), f32), vm((4, *small.shape), f32), vm((4, rows, 2 * NS), f32),
            dma((13,)), dma((2, 3, n - 1)), dma((2, 3, n - 1)), dma((2, 2)), dma((2, 2)), dma((2,)), dma((2,)),
            dma((2, n // 2)), dma((2, n // 2)), dma((3,)), dma((3,)), dma((2,)), dma((2,)),
        ],
        compiler_params=pltpu.CompilerParams(
            collective_id=1, has_side_effects=True, vmem_limit_bytes=46 * 2**20
        ),
        name="reduce_all",
    )(xg, d, dz, wp, w, small, flat, gain)


def adamw_step(weight, first, second, grad, rate, decay):
    first_new = beta_first * first + (1.0 - beta_first) * grad
    second_new = beta_second * second + (1.0 - beta_second) * grad * grad
    hat_first = first_new * (1.0 / (1.0 - beta_first**STEP))
    hat_second = second_new * (1.0 / (1.0 - beta_second**STEP))
    weight_new = weight - rate * (hat_first / (jnp.sqrt(hat_second) + adam_eps) + decay * weight)
    return (weight_new, first_new, second_new)


def finish_body(
    width, heads,
    in_ref, cot_ref, branch_ref, back_ref, flat_ref, early_ref, late_ref, bcg_ref,
    zx_ref, zx1_ref, zx2_ref, bc_ref, bc1_ref, bc2_ref, out_ref, out1_ref, out2_ref, late_all_ref, dt_ref, dt1_ref, dt2_ref,
    layer_ref, grad_ref, zxn_ref, zx1n_ref, zx2n_ref, bcn_ref, bc1n_ref, bc2n_ref,
    outn_ref, out1n_ref, out2n_ref, dtn_ref, dt1n_ref, dt2n_ref,
):
    def update(refs, news, grad):
        fresh = adamw_step(*(ref[...] for ref in refs), grad, matrix_rate, matrix_decay)
        for ref, value in zip(news, fresh):
            ref[...] = value

    for k, grad in ((0, early_ref), (1, late_ref)):
        fresh = adamw_step(
            *(ref[:, k, :] for ref in (zx_ref, zx1_ref, zx2_ref)), grad[:, :width], matrix_rate, matrix_decay
        )
        for ref, value in zip((zxn_ref, zx1n_ref, zx2n_ref), fresh):
            ref[:, k, :] = value
    update((bc_ref, bc1_ref, bc2_ref), (bcn_ref, bc1n_ref, bc2n_ref), bcg_ref[...])
    update((out_ref, out1_ref, out2_ref), (outn_ref, out1n_ref, out2n_ref), early_ref[:, width:])

    @pl.when(pl.program_id(0) == 0)
    def _():
        unit = jnp.where(
            lax.broadcasted_iota(jnp.int32, (16, LANES), 0) == lax.broadcasted_iota(jnp.int32, (16, LANES), 1), 1.0, 0.0
        ).astype(f32)
        turned = mm_exact(unit, late_all_ref[:, width + 2 * NS :], NT)
        update((dt_ref, dt1_ref, dt2_ref), (dtn_ref, dt1n_ref, dt2n_ref), turned[:heads])

    rows = in_ref.shape[0]
    tile = 64

    def some(i, _):
        at = span(i * tile, tile)
        squares = jnp.zeros((tile, LANES), f32)
        inner = jnp.zeros((tile, LANES), f32)
        for c in range(D // LANES):
            cols = slice(c * LANES, (c + 1) * LANES)
            x = in_ref[at, cols].astype(f32)
            squares = squares + x * x
            inner = inner + x * flat_ref[c : c + 1, :] * back_ref[at, cols].astype(f32)
        r = lax.rsqrt(jnp.sum(squares, axis=-1, keepdims=True) / D + norm_eps)
        k = r * r * r * jnp.sum(inner, axis=-1, keepdims=True) / D
        r, k = jnp.broadcast_to(r, (tile, LANES)), jnp.broadcast_to(k, (tile, LANES))
        for c in range(D // LANES):
            cols = slice(c * LANES, (c + 1) * LANES)
            x = in_ref[at, cols].astype(f32)
            layer_ref[at, cols] = (x + branch_ref[at, cols].astype(f32)).astype(bf16)
            back = back_ref[at, cols].astype(f32)
            grad_ref[at, cols] = cot_ref[at, cols].astype(f32) + r * flat_ref[c : c + 1, :] * back - x * k
        return 0

    lax.fori_loop(0, rows // tile, some, 0)


def finish(layer_input, out_grad, branch, back, flat, early, late, bcg, zx, bc, out, dt):
    (rows, width), heads = out[0].shape, dt[0].shape[0]
    steps = 2
    part = lambda a: pl.BlockSpec((a.shape[0] // steps, *a.shape[1:]), lambda i: (i,) + (0,) * (a.ndim - 1))
    whole = lambda a: pl.BlockSpec(a.shape, lambda i: (0,) * a.ndim)
    like = lambda a, dtype=f32: jax.ShapeDtypeStruct(a.shape, dtype)
    weights = (*zx, *bc, *out)
    return pl.pallas_call(
        functools.partial(finish_body, width, heads),
        grid=(steps,),
        in_specs=[
            *(part(a) for a in (layer_input, out_grad, branch, back)), whole(flat),
            *(part(a) for a in (early, late, bcg, *weights)), whole(late), *(whole(a) for a in dt),
        ],
        out_specs=[part(layer_input), part(back), *(part(a) for a in weights), *(whole(a) for a in dt)],
        out_shape=[like(layer_input, bf16), like(layer_input), *(like(a) for a in weights), *(like(a) for a in dt)],
        compiler_params=pltpu.CompilerParams(vmem_limit_bytes=32 * 2**20),
        name="finish",
    )(layer_input, out_grad, branch, back, flat, early, late, bcg, *weights, late, *dt)


def local(
    layer_input,
    out_grad,
    small_params,
    small_first,
    small_second,
    w_zx,
    zx_first,
    zx_second,
    w_bc,
    bc_first,
    bc_second,
    w_dt,
    dt_first,
    dt_second,
    w_out,
    out_first,
    out_second,
):
    n = lax.axis_size("dp")
    flat = jnp.pad(small_params, (0, FLAT_ROWS * LANES - small_params.shape[0])).reshape(FLAT_ROWS, LANES)
    v, xc, dr, st, dy, dz, branch, early, gate, gain, xg, w_all, pair_all, taps, head, chan = ssd_forward(
        n, layer_input, out_grad, flat, w_zx, w_bc, w_dt.T, w_out
    )
    d_late, small, owner_early, own_branch = ssd_backward(
        n, dy, v, xc, dr, st, gate, taps, head, chan, early, branch
    )
    owner_late, d_normed_in, owner_bc, flat_grad = reduce_all(
        n, xg, d_late, dz, pair_all, w_all, small, flat, gain
    )
    small_grad = flat_grad.reshape(-1)[: small_params.shape[0]]
    small_new, small_first_new, small_second_new = adamw_step(
        small_params, small_first, small_second, small_grad, small_rate, 0.0
    )
    (
        layer_output, input_grad, zx_new, zx_first_new, zx_second_new, bc_new, bc_first_new, bc_second_new,
        out_new, out_first_new, out_second_new, dt_new, dt_first_new, dt_second_new,
    ) = finish(
        layer_input, out_grad, own_branch, d_normed_in, flat, owner_early, owner_late, owner_bc,
        (w_zx, zx_first, zx_second), (w_bc, bc_first, bc_second), (w_out, out_first, out_second),
        (w_dt.T, dt_first.T, dt_second.T),
    )
    dt_new, dt_first_new, dt_second_new = dt_new.T, dt_first_new.T, dt_second_new.T
    return (
        layer_output,
        input_grad,
        small_new,
        small_first_new,
        small_second_new,
        zx_new,
        zx_first_new,
        zx_second_new,
        bc_new,
        bc_first_new,
        bc_second_new,
        dt_new,
        dt_first_new,
        dt_second_new,
        out_new,
        out_first_new,
        out_second_new,
    )


def solution(mesh):
    return jax.shard_map(
        local,
        mesh=mesh,
        in_specs=(
            P(("dp", "tensor"), None),
            P(("dp", "tensor"), None),
            P(),
            P(),
            P(),
            P("dp", None, "tensor"),
            P("dp", None, "tensor"),
            P("dp", None, "tensor"),
            P("dp", None),
            P("dp", None),
            P("dp", None),
            P("dp", "tensor"),
            P("dp", "tensor"),
            P("dp", "tensor"),
            P("dp", "tensor"),
            P("dp", "tensor"),
            P("dp", "tensor"),
        ),
        out_specs=(
            P(("dp", "tensor"), None),
            P(("dp", "tensor"), None),
            P(),
            P(),
            P(),
            P("dp", None, "tensor"),
            P("dp", None, "tensor"),
            P("dp", None, "tensor"),
            P("dp", None),
            P("dp", None),
            P("dp", None),
            P("dp", "tensor"),
            P("dp", "tensor"),
            P("dp", "tensor"),
            P("dp", "tensor"),
            P("dp", "tensor"),
            P("dp", "tensor"),
        ),
        check_vma=False,
    )
```

```python
import functools

import jax
import jax.numpy as jnp
from jax import lax
from jax.experimental import pallas as pl
from jax.experimental.pallas import tpu as pltpu
from jax.sharding import PartitionSpec as P

D = 1536
DI = 3072
H = 48
NS = 128
P_SIZE = 64
CONV = 4
LEN = 2048
STEP = 10

T = 128
ROWS = 256
LANES = 128
ROOM = 60 * 2**20

norm_eps = 1e-05
adam_eps = 1e-08
beta_first = 0.9
beta_second = 0.95
matrix_rate = 0.01
small_rate = 0.1
matrix_decay = 0.1

f32 = jnp.float32
bf16 = jnp.bfloat16
NN = (((1,), (0,)), ((), ()))
NT = (((1,), (1,)), ((), ()))
TN = (((0,), (0,)), ((), ()))
HIGHEST = lax.Precision.HIGHEST


GATE_ROW, TAPS_ROW, BIAS_ROW, TAPS_BC_ROW, BIAS_BC_ROW, HEAD_ROW, FLAT_ROWS = 12, 36, 132, 156, 164, 166, 168


def mm(a, b, dims=NN):
    return lax.dot_general(a, b, dims, preferred_element_type=f32)


def mm_exact(a, b, dims=NN):
    return lax.dot_general(a, b, dims, preferred_element_type=f32, precision=HIGHEST)


def sigmoid(v):
    return 0.5 * jnp.tanh(0.5 * v) + 0.5


def softplus(v):
    return jnp.maximum(v, 0.0) + jnp.log1p(jnp.exp(-jnp.abs(v)))


def spread(col):
    return jnp.broadcast_to(col, (T, LANES))


def block_iota(axis):
    return lax.broadcasted_iota(jnp.int32, (T, LANES), axis)


HEADS = 16
LOG2_E = 1.4426950408889634


def pieces(value, count):
    parts = []
    for k in range(count):
        part = value.astype(bf16)
        parts.append(part)
        if k < count - 1:
            value = value - part.astype(f32)
    return jnp.concatenate(parts, axis=1)


def columns_of(rows):
    return jnp.concatenate([rows, jnp.zeros((LANES - HEADS, T), f32)], axis=0).T


def set_heads(head_ref, head_t, until):
    turned = jnp.concatenate([head_ref[...], jnp.zeros((LANES - 8, LANES), f32)], axis=0).T
    head_t[0] = spread(turned[:, 0:1])[:HEADS]
    head_t[1] = spread(turned[:, 1:2])[:HEADS]
    matrix = jnp.where(block_iota(0) <= block_iota(1), 1.0, 0.0).astype(bf16)
    for k in range(3):
        until[k * T : (k + 1) * T, :] = matrix


def head_rows(dr_ref, head_t, until, rows):
    raw = dr_ref[rows, :].T[:HEADS] + head_t[0]
    dt = softplus(raw)
    decay = mm(pieces(dt * (head_t[1] * LOG2_E), 3), until[...])
    return raw, dt, decay, columns_of(dt), columns_of(decay)


def ring_place(n):
    me = lax.axis_index("dp")
    z, x = lax.div(me, 2), lax.rem(me, 2)
    return z + x * (n - 1 - 2 * z)


def ring_index(pos, n):
    back = lax.div(pos, n // 2)
    return 2 * pos + back * (2 * n - 1 - 4 * pos)


def neighbours(n):
    pos = ring_place(n)
    right = ring_index(lax.rem(pos + 1, n), n)
    left = ring_index(lax.rem(pos + n - 1, n), n)
    me = lax.axis_index("tensor")
    y, core = lax.div(me, 2), lax.rem(me, 2)
    across = 2 * (1 - y) + core
    beside = 2 * y + 1 - core
    return pos, ({"dp": right}, {"dp": left}), me, {"tensor": across}, {"tensor": beside}


def greet(peers):
    barrier = pltpu.get_barrier_semaphore()
    for peer in peers:
        pl.semaphore_signal(barrier, inc=1, device_id=peer, device_id_type=pl.DeviceIdType.MESH)


def enter(peers):
    greet(peers)
    pl.semaphore_wait(pltpu.get_barrier_semaphore(), len(peers))


def remote(src, dst, send_sem, recv_sem, peer):
    return pltpu.make_async_remote_copy(
        src_ref=src, dst_ref=dst, send_sem=send_sem, recv_sem=recv_sem,
        device_id=peer, device_id_type=pl.DeviceIdType.MESH,
    )


def span(start, size):
    return pl.ds(pl.multiple_of(start, 16), size)


def strip(rows):
    return next(size for size in (48, 32, 16) if rows % size == 0)


def cut_rows(rows):
    top = rows // 32 * 16
    return ((0, top), (top, rows - top))


def forward_body(
    n, rows, tokens, width,
    in_ref, cot_ref, flat_ref, wzx_ref, wbc_ref, wdt_ref, wout_ref,
    v_ref, xc_ref, dr_ref, st_ref, dy_ref, dz_ref, branch_ref, early_ref, gate_ref, gain_ref,
    xg_ref, ws_ref, wps_ref, taps_ref, head_ref, chan_ref,
    halo, state, y_all, z_all, dn_all, nl_all, dz_all, xg, cots, ws, wps, sums, red, head_t, until, across_state, tails,
    own_keep, early_keep, lead_keep, lead_send, lead_recv, x_keep, x_over_send, x_over_recv, x_side_send, x_side_recv,
    x_pass_send, x_pass_recv, ring_keep, ring_send, ring_recv, over_send, over_recv,
    side_send, side_recv, pass_send, pass_recv, sum_send, sum_recv,
):
    pairs = width // LANES
    wide = width + 2 * NS
    step = pl.program_id(0)
    steps = LEN // ROWS
    tall = 2 * ROWS
    norming = steps // 2
    gating = norming + 1
    forming = gating + 1
    products = forming + steps // 2
    pos, ring, me, across, beside = neighbours(n)
    opposite = lax.rem(me + 2, 4)
    next_door = me + 1 - 2 * lax.rem(me, 2)
    far = lax.rem(next_door + 2, 4)
    askew = {"tensor": far}
    quarter = tokens // 4
    hops = n // 2
    cuts = cut_rows(rows)
    mine = ring_index(pos, n)

    late = wide + LANES
    parts_of = ((0, width), (width, width))

    def hop(k, part, way, h):
        first, size = cuts[part]
        cols = pl.ds(*parts_of[k])
        block = ring_index(lax.rem(pos + (h if way else n - h), n), n)
        here = wps.at[span(block * rows + first, size), cols]
        return remote(here, here, ring_send.at[way, part, k, h], ring_recv.at[way, part, k, h], ring[way])

    def hop_lands(k, part, way, h):
        first, size = cuts[part]
        block = ring_index(lax.rem(pos + (h + 1 if way else n - h - 1), n), n)
        return span(block * rows + first, size), pl.ds(*parts_of[k])

    def hop_arrival(k, part, way, h):
        here = wps.at[hop_lands(k, part, way, h)]
        return remote(here, here, ring_send.at[way, part, k, h], ring_recv.at[way, part, k, h], ring[way])

    def hop_keep(part, way, h):
        at = hop_lands(1, part, way, h)
        return pltpu.make_async_copy(wps.at[at], wps_ref.at[at], ring_keep.at[way, part, h])

    def hop_ways(h):
        return [(part, way) for part in (0, 1) for way in (0, 1) if h < hops - 1 or part == way]

    def hop_on(k, h):
        for part, way in hop_ways(h - 1) if h > 0 else ():
            hop_arrival(k, part, way, h - 1).wait_recv()
            if k == 1:
                hop_keep(part, way, h - 1).start()
            if h < hops and (part, way) in hop_ways(h):
                hop(k, part, way, h).start()
        if h == 0:
            for part, way in hop_ways(0):
                hop(k, part, way, 0).start()

    def over(k):
        return remote(
            cot_ref.at[pl.ds(k * quarter, quarter)], cots.at[span(me * tokens + k * quarter, quarter)],
            over_send.at[k], over_recv.at[k], across,
        )

    def landed(start, size, send, recv, peer):
        here = cots.at[span(start, size)]
        return remote(here, here, send, recv, peer)

    def over_arrival(k):
        return landed(opposite * tokens + k * quarter, quarter, over_send.at[k], over_recv.at[k], across)

    def passing(k):
        return landed(opposite * tokens + k * quarter, quarter, pass_send.at[k], pass_recv.at[k], beside)

    def pass_arrival(k):
        return landed(far * tokens + k * quarter, quarter, pass_send.at[k], pass_recv.at[k], beside)

    def side():
        return remote(cot_ref, cots.at[span(me * tokens, tokens)], side_send.at[0], side_recv.at[0], beside)

    def side_arrival():
        return landed(next_door * tokens, tokens, side_send.at[0], side_recv.at[0], beside)

    def own_cot():
        return pltpu.make_async_copy(cot_ref, cots.at[span(me * tokens, tokens)], own_keep.at[0])

    def own_z():
        at = span(mine * rows, rows), pl.ds(*parts_of[1])
        return pltpu.make_async_copy(wps.at[at], wps_ref.at[at], own_keep.at[1])

    def pass_on(*pieces):
        for k in pieces:
            over_arrival(k).wait_recv()
            passing(k).start()

    def normalize(k):
        def some(i, _):
            at = span(me * tokens + k * quarter + i * 64, 64)
            squares = jnp.zeros((64, LANES), f32)
            for c in range(D // LANES):
                x = xg[at, c * LANES : (c + 1) * LANES].astype(f32)
                squares = squares + x * x
            inverse = lax.rsqrt(jnp.sum(squares, axis=-1, keepdims=True) / D + norm_eps)
            inverse = jnp.broadcast_to(inverse, (64, LANES))
            for c in range(D // LANES):
                cols = slice(c * LANES, (c + 1) * LANES)
                xg[at, cols] = (xg[at, cols].astype(f32) * inverse * flat_ref[c : c + 1, :]).astype(bf16)
            return 0

        lax.fori_loop(0, quarter // 64, some, 0)

    @pl.when(step == 0)
    def _():
        own_rows = span(me * tokens, tokens)
        greet((*ring, across, beside, askew))
        load = pltpu.make_async_copy(in_ref, xg.at[own_rows], own_keep.at[2])
        load.start()
        own_cot().start()
        mine_at = span(mine * rows, rows)
        ws[mine_at, :width] = wzx_ref[:, 1, :].astype(bf16)
        ws[mine_at, width:wide] = wbc_ref[...].astype(bf16)
        heads = wdt_ref.shape[0]
        unit = jnp.where(
            lax.broadcasted_iota(jnp.int32, (16, LANES), 0) == lax.broadcasted_iota(jnp.int32, (16, LANES), 1), 1.0, 0.0
        ).astype(bf16)
        steps_w = jnp.concatenate([wdt_ref[...], jnp.zeros((16 - heads, rows), f32)], axis=0).astype(bf16)
        ws[mine_at, wide:] = mm(steps_w, unit, TN).astype(bf16)
        load.wait()
        normalize(0)
        pl.semaphore_wait(pltpu.get_barrier_semaphore(), 5)
        started, kept = [], []

        def go(*args):
            copy = remote(*args)
            copy.start()
            started.append(copy)

        def keep(src, dst, sem):
            copy = pltpu.make_async_copy(src, dst, sem)
            copy.start()
            kept.append(copy)

        def arrived(part, way, h, block):
            first, size = cuts[part]
            at = span(block * rows + first, size)
            remote(
                ws.at[at], ws.at[at], lead_send.at[way, part, h], lead_recv.at[way, part, h], ring[way]
            ).wait_recv()
            keep(ws.at[at], ws_ref.at[at], lead_keep.at[way, part, h])

        def lead(h, parts=(0, 1)):
            for part in parts:
                first, size = cuts[part]
                for way in (0, 1):
                    block = ring_index(lax.rem(pos + (h if way else n - h), n), n)
                    here = ws.at[span(block * rows + first, size)]
                    if h > 0:
                        arrived(part, way, h - 1, block)
                    if h == hops - 1 and part != way:
                        continue
                    go(here, here, lead_send.at[way, part, h], lead_recv.at[way, part, h], ring[way])

        def x_over(k):
            at = span(me * tokens + k * quarter, quarter)
            go(xg.at[at], xg.at[at], x_over_send.at[k], x_over_recv.at[k], across)

        def x_pass(k):
            at = span(opposite * tokens + k * quarter, quarter)
            here = xg.at[at]
            remote(here, here, x_over_send.at[k], x_over_recv.at[k], across).wait_recv()
            go(here, here, x_pass_send.at[k], x_pass_recv.at[k], beside)
            keep(here, xg_ref.at[at], x_keep.at[k])

        def x_pass_lands(k):
            at = span(far * tokens + k * quarter, quarter)
            remote(xg.at[at], xg.at[at], x_pass_send.at[k], x_pass_recv.at[k], beside).wait_recv()
            keep(xg.at[at], xg_ref.at[at], x_keep.at[4 + k])

        lead(0, (0,))
        leading = list(started)
        x_over(0)
        for k in (1, 2, 3):
            normalize(k)
            if k == 1:
                x_over(1)
        go(xg.at[own_rows], xg.at[own_rows], x_side_send.at[0], x_side_recv.at[0], beside)
        keep(xg.at[own_rows], xg_ref.at[own_rows], x_keep.at[8])
        wps[mine_at, :width] = wout_ref[...].astype(bf16)
        wps[mine_at, width:] = wzx_ref[:, 0, :].astype(bf16)
        for copy in leading:
            copy.wait_send()
            started.remove(copy)
        lead(0, (1,))
        keep(ws.at[mine_at], ws_ref.at[mine_at], x_keep.at[9])
        own_z().start()
        halo[0:8, :] = jnp.zeros((8, wide), f32)
        state[...] = jnp.zeros_like(state)
        gate_ref[...] = jnp.zeros_like(gate_ref)
        parameter_rows(me, width, flat_ref, taps_ref, head_ref, chan_ref)
        set_heads(head_ref, head_t, until)
        lead(1)
        x_over(2)
        at = span(next_door * tokens, tokens)
        remote(xg.at[at], xg.at[at], x_side_send.at[0], x_side_recv.at[0], beside).wait_recv()
        keep(xg.at[at], xg_ref.at[at], x_keep.at[10])
        side().start()
        lead(2)
        x_over(3)
        x_pass(0)
        x_pass(1)
        for h in range(3, hops):
            lead(h)
        hop_on(0, 0)
        x_pass(2)
        over(0).start()
        x_pass_lands(0)
        x_pass_lands(1)
        x_pass(3)
        for part in (0, 1):
            arrived(part, part, hops - 1, ring_index(lax.rem(pos + n // 2, n), n))
        hop_on(1, 0)
        over(1).start()
        x_pass_lands(2)
        x_pass_lands(3)
        for copy in kept:
            copy.wait()
        for copy in started:
            copy.wait_send()

    def at_tick(tick):
        for k, times in enumerate(((1, 5), (3, 6))):
            for h in (1, 2):
                pl.when(tick == times[h - 1])(functools.partial(hop_on, k, h))

        @pl.when(tick == 1)
        def _():
            over(2).start()

        @pl.when(tick == 3)
        def _():
            over(3).start()

        pl.when(tick == 4)(functools.partial(pass_on, 0, 1))
        pl.when(tick == steps - 2)(functools.partial(pass_on, 2))

    def late_turn():
        pass_on(3)
        hop_on(0, 3)

    @pl.when(step < norming)
    def _():
        def chunk(i, _):
            tick = 2 * step + i
            at_tick(tick)
            scan_step(
                width, tick, i, xg, ws, taps_ref, head_ref, chan_ref,
                v_ref, xc_ref, dr_ref, st_ref, halo, state, y_all, head_t, until, across_state, tails,
                late_turn,
            )
            return 0

        lax.fori_loop(0, 2, chunk, 0)

    @pl.when(step == norming)
    def _():
        for h in range(3, hops):
            for k in (0, 1):
                if (k, h) != (0, 3):
                    hop_on(k, h)
        hop_on(0, hops)
        side_arrival().wait_recv()
        for k in range(4):
            pass_arrival(k).wait_recv()
        own_cot().wait()
        own_z().wait()

        def some(i, _):
            at = span(i * tall, tall)
            dn_all[at, :] = mm(cots[at, :], wps[:, :width]).astype(bf16)
            return 0

        lax.fori_loop(0, LEN // tall, some, 0)

    @pl.when(step == gating)
    def _():
        hop_on(1, hops)
        ones = jnp.ones((8, LANES), f32)

        def some(i, _):
            at = span(i * tall, tall)
            z_all[at, :] = mm(xg[at, :], wps[:, width:])
            for sub in range(tall // T):
                rows_at = span(i * tall + sub * T, T)
                squares = jnp.zeros((T, LANES), f32)
                inner = jnp.zeros((T, LANES), f32)
                for p in range(pairs):
                    cols = slice(p * LANES, (p + 1) * LANES)
                    z = z_all[rows_at, cols]
                    gated = y_all[rows_at, cols] * (z * sigmoid(z))
                    squares = squares + gated * gated
                    inner = inner + gated * chan_ref[0:1, cols] * dn_all[rows_at, cols].astype(f32)
                lanes = pl.ds(pl.multiple_of(i * tall + sub * T, T), T)
                sums[me, 0:4, lanes] = mm_exact(ones, squares, NT)[0:4]
                sums[me, 4:8, lanes] = mm_exact(ones, inner, NT)[4:8]
            return 0

        lax.fori_loop(0, LEN // tall, some, 0)

    @pl.when(step == forming - 1)
    def _():
        peers = ((beside, next_door), (across, opposite), (askew, far))
        for k, (peer, _) in enumerate(peers):
            remote(sums.at[me], sums.at[me], sum_send.at[k], sum_recv.at[k], peer).start()
        for h in range(hops):
            for part, way in hop_ways(h):
                for k in (0, 1):
                    hop(k, part, way, h).wait_send()
                hop_keep(part, way, h).wait()
        side().wait_send()
        for k in range(4):
            over(k).wait_send()
            passing(k).wait_send()
        for k, (peer, other) in enumerate(peers):
            remote(sums.at[other], sums.at[other], sum_send.at[k], sum_recv.at[k], peer).wait()
        red[...] = ((sums[0] + sums[1]) + sums[2]) + sums[3]

    @pl.when((step >= forming) & (step < products))
    def _():
        def some(i, _):
            first = (step - forming) * tall + i * ROWS
            lanes = pl.ds(pl.multiple_of(first, ROWS), ROWS)
            q_row = lax.rsqrt(red[0:4, lanes] / DI + norm_eps)
            k_row = q_row * q_row * q_row * red[4:8, lanes] / DI
            turned = jnp.concatenate([q_row, k_row], axis=0).T
            for sub in range(ROWS // T):
                rows_at = slice(sub * T, (sub + 1) * T)
                at = span(first + sub * T, T)
                q, kk = spread(turned[rows_at, 0:1]), spread(turned[rows_at, 4:5])
                for p in range(pairs):
                    cols = slice(p * LANES, (p + 1) * LANES)
                    z, y, dn = z_all[at, cols], y_all[at, cols], dn_all[at, cols].astype(f32)
                    gain = chan_ref[0:1, cols]
                    s = sigmoid(z)
                    sz = z * s
                    gated = y * sz
                    gq = gated * q
                    dg = q * gain * dn - gated * kk
                    gate_ref[:, cols] += jnp.sum((gq * dn).reshape(T // 8, 8, LANES), axis=0)
                    nl_all[at, cols] = (gq * gain).astype(bf16)
                    dz_all[at, cols] = (dg * y * (s + sz * (1.0 - s))).astype(bf16)
                    dn_all[at, cols] = (dg * sz).astype(bf16)
            branch_ref[span(i * ROWS, ROWS), :] = mm(nl_all[span(first, ROWS), :], wps[:, :width], NT).astype(bf16)
            return 0

        lax.fori_loop(0, 2, some, 0, unroll=2)

    def rows_out():
        return [
            pltpu.make_async_copy(src, dst, own_keep.at[2 + k])
            for k, (src, dst) in enumerate(((dz_all, dz_ref), (dn_all, dy_ref)))
        ]

    def early_out(i):
        at = span(i * ROWS, ROWS)
        return [
            pltpu.make_async_copy(src.at[at, pl.ds(0, width)], early_ref.at[at, pl.ds(k * width, width)], early_keep.at[k, i])
            for k, src in enumerate((ws, wps))
        ]

    @pl.when(step == products)
    def _():
        for copy in rows_out():
            copy.start()

        def some(i, _):
            at = span(i * ROWS, ROWS)
            lanes = pl.ds(pl.multiple_of(i * ROWS, ROWS), ROWS)
            grad = mm(xg[:, lanes], dz_all[...], TN)
            ws[at, :width] = grad.astype(bf16)
            share = jnp.zeros((ROWS, LANES), f32)
            for p in range(pairs):
                cols = slice(p * LANES, (p + 1) * LANES)
                w = wps[at, width + p * LANES : width + (p + 1) * LANES]
                share = share + grad[:, cols] * w.astype(f32)
            gain_ref[:, lanes] = mm_exact(jnp.ones((8, LANES), f32), share, NT)
            wps[at, :width] = mm(cots[:, lanes], nl_all[...], TN).astype(bf16)
            for copy in early_out(i):
                copy.start()
            return 0

        lax.fori_loop(0, D // ROWS, some, 0, unroll=3)
        for copy in rows_out():
            copy.wait()

        def done(i, _):
            for copy in early_out(i):
                copy.wait()
            return 0

        lax.fori_loop(0, D // ROWS, done, 0)


def parameter_rows(me, width, flat_ref, taps_ref, head_ref, chan_ref):
    pairs = width // LANES
    heads = width // P_SIZE
    taps_ref[...] = jnp.zeros_like(taps_ref)
    chan_ref[...] = jnp.zeros_like(chan_ref)
    for c in range(pairs):
        cols = slice(c * LANES, (c + 1) * LANES)
        chan_ref[0:1, cols] = flat_ref[pl.ds(GATE_ROW + pairs * me + c, 1), :]
        taps_ref[CONV : CONV + 1, cols] = flat_ref[pl.ds(BIAS_ROW + pairs * me + c, 1), :]
        for k in range(CONV):
            taps_ref[k : k + 1, cols] = flat_ref[pl.ds(TAPS_ROW + 4 * pairs * k + pairs * me + c, 1), :]
    for c in range(2):
        cols = slice(width + c * LANES, width + (c + 1) * LANES)
        taps_ref[CONV : CONV + 1, cols] = flat_ref[BIAS_BC_ROW + c : BIAS_BC_ROW + c + 1, :]
        for k in range(CONV):
            row = TAPS_BC_ROW + 2 * k + c
            taps_ref[k : k + 1, cols] = flat_ref[row : row + 1, :]
    both = jnp.concatenate([flat_ref[HEAD_ROW : HEAD_ROW + 1, :], flat_ref[HEAD_ROW + 1 : HEAD_ROW + 2, :]], axis=1)
    both = jnp.broadcast_to(both, (8, 2 * LANES))
    lane = lax.broadcasted_iota(jnp.int32, (2 * LANES, LANES), 0)
    head = lax.broadcasted_iota(jnp.int32, (2 * LANES, LANES), 1)

    def take(kind):
        match = (lane == 4 * heads * kind + heads * me + head) & (head < heads)
        return mm_exact(both, jnp.where(match, 1.0, 0.0).astype(f32))

    valid = lax.broadcasted_iota(jnp.int32, (8, LANES), 1) < heads
    row = lax.broadcasted_iota(jnp.int32, (8, LANES), 0)
    rates = jnp.where(valid, -jnp.exp(take(1)), 0.0)
    head_ref[...] = jnp.where(row == 0, take(0), jnp.where(row == 1, rates, 0.0))
    skip = mm_exact(take(2), picked(width).astype(f32), NT)
    chan_ref[1:2, :] = skip[0:1]


def picked(width):
    channel = lax.broadcasted_iota(jnp.int32, (width, LANES), 0)
    head = lax.broadcasted_iota(jnp.int32, (width, LANES), 1)
    return jnp.where((channel >= head * P_SIZE) & (channel < (head + 1) * P_SIZE), 1.0, 0.0).astype(bf16)


def scan_step(
    width, tick, i, xg, w_ref, taps_ref, head_ref, chan_ref,
    v_ref, xc_ref, dr_ref, st_ref, halo, state, y_all, head_t, until, across_state, tails, late_turn,
):
    pairs = width // LANES
    wide = width + 2 * NS
    mine = span(tick * ROWS, ROWS)
    dr_ref[span(i * ROWS, ROWS), :] = mm(xg[mine, :], w_ref[:, wide:])
    halo[8 : 8 + ROWS, :] = mm(xg[mine, :], w_ref[:, :wide])
    low_half = block_iota(1) < P_SIZE
    causal = block_iota(0) >= block_iota(1)

    def convolved(sub, block):
        cols = slice(block * LANES, (block + 1) * LANES)
        total = taps_ref[CONV : CONV + 1, cols]
        for k in range(CONV):
            first = 8 - (CONV - 1) + k + sub * T
            total = total + taps_ref[k : k + 1, cols] * halo[first : first + T, cols]
        rows = span(i * ROWS + sub * T, T)
        xc_ref[rows, cols] = total.astype(bf16)
        v_ref[rows, cols] = halo[8 + sub * T : 8 + (sub + 1) * T, cols].astype(bf16)
        return total * sigmoid(total)

    for sub in range(ROWS // T):
        rows = span(i * ROWS + sub * T, T)
        _, _, decay_t, dt, decay = head_rows(dr_ref, head_t, until, rows)
        b_low = convolved(sub, pairs).astype(bf16)
        c_low = convolved(sub, pairs + 1).astype(bf16)
        b_t = b_low.T
        scores = jnp.where(causal, mm(c_low, b_low, NT), 0.0)
        entering = state[...].astype(bf16)
        st_ref[i * (ROWS // T) + sub] = entering
        across_state[...] = mm(c_low, entering)
        for p in range(pairs):
            cols = slice(p * LANES, (p + 1) * LANES)
            x = convolved(sub, p)
            l1, l2 = spread(decay[:, 2 * p : 2 * p + 1]), spread(decay[:, 2 * p + 1 : 2 * p + 2])
            both = jnp.where(low_half, l1, l2)
            dtb = jnp.where(
                low_half, spread(dt[:, 2 * p : 2 * p + 1]), spread(dt[:, 2 * p + 1 : 2 * p + 2])
            )
            u = x * dtb
            m1 = scores * jnp.exp2(jnp.minimum(l1 - decay_t[2 * p : 2 * p + 1, :], 0.0))
            m2 = scores * jnp.exp2(jnp.minimum(l2 - decay_t[2 * p + 1 : 2 * p + 2, :], 0.0))
            mixing = jnp.concatenate([m1.astype(bf16), m2.astype(bf16)], axis=1)
            u_low = u.astype(bf16)
            zero = jnp.zeros_like(u_low)
            parts = jnp.concatenate(
                [jnp.where(low_half, u_low, zero), jnp.where(low_half, zero, u_low)], axis=0
            )
            last = both[T - 1 : T, :]
            y = mm(mixing, parts) + jnp.exp2(both) * across_state[:, cols] + chan_ref[1:2, cols] * x
            tails[:, cols] = (u * jnp.exp2(last - both)).astype(bf16)
            state[:, cols] = jnp.exp2(last) * state[:, cols]
            y_all[span(tick * ROWS + sub * T, T), cols] = y
        state[...] = state[...] + mm(b_t, tails[...])
        if sub == 0:
            pl.when(tick == LEN // ROWS - 1)(late_turn)
    halo[0:8, :] = halo[ROWS : ROWS + 8, :]


def ssd_forward(n, layer_input, out_grad, flat, w_zx, w_bc, w_dt, w_out):
    rows, width = w_out.shape
    tokens = layer_input.shape[0]
    length = 4 * tokens
    wide = width + 2 * NS
    tall = 2 * ROWS
    steps = length // tall
    forming = steps + 2
    products = forming + steps
    subs = tall // T
    assert length == LEN
    row = lambda m: pl.BlockSpec((tall, m), lambda i: (jnp.minimum(i, steps - 1), 0))
    form = lambda m: pl.BlockSpec((tall, m), lambda i: (jnp.clip(i - forming, 0, steps - 1), 0))
    whole = lambda a: pl.BlockSpec(a.shape, lambda i: (0,) * a.ndim, pipeline_mode=pl.Buffered(1))
    fixed = lambda m: pl.BlockSpec((8, m), lambda i: (0, 0))
    anywhere = pl.BlockSpec(memory_space=pl.ANY)
    vm, dma = pltpu.VMEM, pltpu.SemaphoreType.DMA
    hops, lead = dma((2, 2, 2, n // 2)), dma((2, 2, n // 2))
    shape = lambda dims, dtype: jax.ShapeDtypeStruct(dims, dtype)
    return pl.pallas_call(
        functools.partial(forward_body, n, rows, tokens, width),
        grid=(products + 1,),
        in_specs=[anywhere, anywhere, *(whole(a) for a in (flat, w_zx, w_bc, w_dt, w_out))],
        out_specs=[
            row(wide), row(wide), row(LANES), pl.BlockSpec((subs, NS, width), lambda i: (jnp.minimum(i, steps - 1), 0, 0)),
            anywhere, anywhere, form(D), anywhere,
            fixed(width), fixed(D), anywhere, anywhere, anywhere, *(fixed(m) for m in (wide, LANES, width)),
        ],
        out_shape=[
            shape((length, wide), bf16), shape((length, wide), bf16), shape((length, LANES), f32),
            shape((length // T, NS, width), bf16), shape((length, width), bf16), shape((length, width), bf16),
            shape((length, D), bf16), shape((D, 2 * width), bf16), shape((8, width), f32), shape((8, D), f32),
            shape((length, D), bf16), shape((D, wide + LANES), bf16), shape((D, 2 * width), bf16),
            *(shape((8, m), f32) for m in (wide, LANES, width)),
        ],
        scratch_shapes=[
            vm((ROWS + 8, wide), f32), vm((NS, width), f32), vm((length, width), f32), vm((length, width), f32),
            *(vm((length, width), bf16) for _ in range(3)),
            vm((length, D), bf16), vm((length, D), bf16), vm((D, wide + LANES), bf16), vm((D, 2 * width), bf16),
            vm((4, 8, length), f32), vm((8, length), f32), vm((2, HEADS, LANES), f32), vm((3 * T, LANES), bf16),
            vm((T, width), f32), vm((T, width), bf16),
            dma((4,)), dma((2, D // ROWS)), lead, lead, lead, dma((11,)), dma((4,)), dma((4,)), dma((1,)), dma((1,)),
            dma((4,)), dma((4,)), lead, hops, hops, dma((4,)), dma((4,)),
            dma((1,)), dma((1,)), dma((4,)), dma((4,)), dma((3,)), dma((3,)),
        ],
        compiler_params=pltpu.CompilerParams(collective_id=2, has_side_effects=True, vmem_limit_bytes=ROOM),
        name="layer_forward",
    )(layer_input, out_grad, flat, w_zx, w_bc, w_dt, w_out)


def backward_body(
    n, own_rows, tokens, width,
    dy_ref, v_ref, xc_ref, dr_ref, st_ref, gate_ref, taps_ref, head_ref, chan_ref, early_ref, branch_ref,
    d_ref, small_ref, oearly_ref, obranch_ref,
    dxh, dstate, yst, bds, dyeb, utb, products, turn, acc, hacc, pick_ref, pick_t, fades, head_t, until_ref, reach_ref,
    own, slots, near, held, over_slot,
    load_sem, ring_send, ring_recv, near_send, near_recv, over_send, over_recv,
):
    pairs = width // LANES
    wide = width + 2 * NS
    step = pl.program_id(0)
    steps = LEN // ROWS
    subs = ROWS // T
    pos, ring, me, across, beside = neighbours(n)
    opposite = lax.rem(me + 2, 4)
    next_door = me + 1 - 2 * lax.rem(me, 2)
    far = lax.rem(next_door + 2, 4)
    half = tokens // 2
    cuts = cut_rows(own_rows)

    def block_at(way, count):
        return ring_index(lax.rem(pos + (count if way else n - count), n), n)

    def hop(k, way, h):
        first, size = cuts[way]
        if h == 0:
            src = early_ref.at[span(block_at(way, 1) * own_rows + first, size), pl.ds(k * width, width)]
        else:
            src = slots[way][k].at[h - 1]
        return remote(
            src, slots[way][k].at[h], ring_send.at[way, k, h], ring_recv.at[way, k, h], ring[way]
        )

    def near_copy(turned, part):
        start = (next_door if turned else far) * tokens + part * half
        return remote(
            branch_ref.at[span(start, half)], near.at[turned, part],
            near_send.at[turned, part], near_recv.at[turned, part], beside,
        )

    def held_copy(turned, part):
        start = (me if turned else opposite) * tokens + part * half
        return pltpu.make_async_copy(
            branch_ref.at[span(start, half)], held.at[turned, part], load_sem.at[2 * turned + part]
        )

    def over_copy(part):
        return remote(held.at[0, part], over_slot.at[part], over_send.at[part], over_recv.at[part], across)

    def own_copy():
        return pltpu.make_async_copy(early_ref, own, load_sem.at[4])

    def ring_turn(k, h):
        for way in (0, 1):
            first, size = cuts[way]
            hop(k, way, h).wait_recv()
            block = block_at(way, 2 + h) if h < n - 2 else block_at(way, 0)

            tile = strip(size)

            def some(i, _, way=way, first=first, block=block, tile=tile):
                cols = slice(k * width, (k + 1) * width)
                came = slots[way][k][h, span(i * tile, tile), :]
                mine = own[span(block * own_rows + first + i * tile, tile), cols]
                if h < n - 2:
                    slots[way][k][h, span(i * tile, tile), :] = came + mine
                else:
                    oearly_ref[span(first + i * tile, tile), cols] = came.astype(f32) + mine.astype(f32)
                return 0

            lax.fori_loop(0, size // tile, some, 0)
            if h < n - 2:
                hop(k, way, h + 1).start()

    def ring_poll(k, tick):
        for h in range(n - 1):
            pl.when(tick == min(h + 1, steps - 1))(functools.partial(ring_turn, k, h))

    def add_near(turned):
        for part in (0, 1):
            held_copy(turned, part).wait()
            near_copy(turned, part).wait_recv()

            def some(i, _, part=part):
                at = span(i * 32, 32)
                held[turned, part, at, :] = held[turned, part, at, :] + near[turned, part, at, :]
                return 0

            lax.fori_loop(0, half // 32, some, 0)
            if not turned:
                over_copy(part).start()

    @pl.when(step == 0)
    def _():
        enter((*ring, across, beside))
        for way in (0, 1):
            hop(0, way, 0).start()
        for turned in (0, 1):
            for part in (0, 1):
                near_copy(turned, part).start()
                held_copy(turned, part).start()
        own_copy().start()
        dxh[T : T + 8, :] = jnp.zeros((8, wide), f32)
        dstate[...] = jnp.zeros_like(dstate)
        acc[...] = jnp.zeros_like(acc)
        hacc[...] = jnp.zeros_like(hacc)
        turn[...] = jnp.zeros_like(turn)
        pick_ref[...] = picked(width)
        channel = lax.broadcasted_iota(jnp.int32, (HEADS, width), 1)
        head = lax.broadcasted_iota(jnp.int32, (HEADS, width), 0)
        mine = (channel >= head * P_SIZE) & (channel < (head + 1) * P_SIZE)
        pick_t[...] = jnp.where(mine, 1.0, 0.0).astype(bf16)
        set_heads(head_ref, head_t, until_ref)
        from_here = jnp.where(block_iota(0) >= block_iota(1), 1.0, 0.0).astype(bf16)
        after = jnp.where(block_iota(0) < block_iota(1), 1.0, 0.0).astype(bf16)
        for k, matrix in enumerate((from_here, from_here, after, after)):
            reach_ref[k * T : (k + 1) * T, :] = matrix
        products[3 * T :, :] = jnp.zeros((HEADS, width), bf16)

    low_half = block_iota(1) < P_SIZE
    row_at, col_at = block_iota(0), block_iota(1)
    until = row_at <= col_at
    pair_lane = lax.broadcasted_iota(jnp.int32, (8, 2 * T), 1)
    pair_row = lax.broadcasted_iota(jnp.int32, (8, 2 * T), 0)
    each = jnp.where(lax.div(pair_lane, T) == pair_row, 1.0, 0.0).astype(bf16)
    ones = jnp.ones((8, T), bf16)

    def add(index, cols, value):
        acc[index, :, cols] += jnp.sum(value.reshape(T // 8, 8, LANES), axis=0)

    def conv_back(rows, block, d_act, xc, s, act):
        cols = slice(block * LANES, (block + 1) * LANES)
        dxh[0:T, cols] = d_act * (s + act * (1.0 - s))
        v = v_ref[rows, cols].astype(f32)
        total = None
        for m in range(CONV):
            moved = dxh[m : m + T, cols]
            if m == 0:
                add(CONV, cols, moved)
            add(CONV - 1 - m, cols, v * moved)
            term = taps_ref[CONV - 1 - m : CONV - m, cols] * moved
            total = term if total is None else total + term
        d_ref[rows, cols] = total.astype(bf16)

    def work(i, _):
        tick = 2 * step + i
        chunk = 1 - i

        @pl.when(tick == 1)
        def _():
            own_copy().wait()
            add_near(0)

        pl.when(tick == 2)(functools.partial(add_near, 1))
        ring_poll(0, tick)
        for sub in reversed(range(subs)):
            rows = span(chunk * ROWS + sub * T, T)
            block_state = chunk * subs + sub
            raw_t, dt_t, decay_t, dt, decay = head_rows(dr_ref, head_t, until_ref, rows)
            b_cols = slice(width, width + NS)
            c_cols = slice(width + NS, width + 2 * NS)
            b_xc, c_xc = xc_ref[rows, b_cols].astype(f32), xc_ref[rows, c_cols].astype(f32)
            b_s, c_s = sigmoid(b_xc), sigmoid(c_xc)
            b_act, c_act = b_xc * b_s, c_xc * c_s
            b_low, c_low = b_act.astype(bf16), c_act.astype(bf16)
            c_t = c_low.T
            scores_t = jnp.where(until, mm(b_low, c_low, NT), 0.0)
            ds_low = dstate[...].astype(bf16)
            yst[...] = mm(c_low, st_ref[block_state])
            bds[...] = mm(b_low, ds_low)
            d_scores = jnp.zeros((T, LANES), f32)
            for p in range(pairs):
                cols = slice(p * LANES, (p + 1) * LANES)
                dy_low = dy_ref[rows, cols]
                dy = dy_low.astype(f32)
                xc = xc_ref[rows, cols].astype(f32)
                xs = sigmoid(xc)
                x = xc * xs
                l1, l2 = spread(decay[:, 2 * p : 2 * p + 1]), spread(decay[:, 2 * p + 1 : 2 * p + 2])
                both = jnp.where(low_half, l1, l2)
                dtb = jnp.where(
                    low_half, spread(dt[:, 2 * p : 2 * p + 1]), spread(dt[:, 2 * p + 1 : 2 * p + 2])
                )
                u = x * dtb
                last = both[T - 1 : T, :]
                e1 = jnp.exp2(jnp.minimum(decay_t[2 * p : 2 * p + 1, :] - l1, 0.0))
                e2 = jnp.exp2(jnp.minimum(decay_t[2 * p + 1 : 2 * p + 2, :] - l2, 0.0))
                zero = jnp.zeros_like(dy_low)
                dy_parts = jnp.concatenate(
                    [jnp.where(low_half, dy_low, zero), jnp.where(low_half, zero, dy_low)], axis=0
                )
                du_in = mm(
                    jnp.concatenate([(scores_t * e1).astype(bf16), (scores_t * e2).astype(bf16)], axis=1), dy_parts
                )
                d_mix = mm(u.astype(bf16), dy_parts, NT)
                d1, d2 = d_mix[:, :T] * e1, d_mix[:, T:] * e2
                d_scores = d_scores + d1 + d2
                held_pairs = jnp.concatenate([(d1 * scores_t).astype(bf16), (d2 * scores_t).astype(bf16)], axis=1)
                reached_by = mm(ones, held_pairs)
                leaving = mm(each, held_pairs, NT)
                turn[2 * p : 2 * p + 1, :] = reached_by[0:1, :T] - leaving[0:1]
                turn[2 * p + 1 : 2 * p + 2, :] = reached_by[0:1, T:] - leaving[1:2]
                tail = jnp.exp2(last - both)
                fades[0:1, cols] = jnp.exp2(last)
                dye = dy * jnp.exp2(both)
                du_out = tail * bds[:, cols]
                du = du_in + du_out
                products[0:T, cols] = (dye * yst[:, cols]).astype(bf16)
                products[T : 2 * T, cols] = (u * du_out).astype(bf16)
                products[2 * T : 3 * T, cols] = (x * du).astype(bf16)
                dyeb[:, cols] = dye.astype(bf16)
                utb[:, cols] = (u * tail).astype(bf16)
                add(CONV + 1, cols, dy * x)
                conv_back(rows, p, dtb * du + chan_ref[1:2, cols] * dy, xc, xs, x)
            d_scores = jnp.where(until, d_scores, 0.0).astype(bf16)
            d_b = mm(d_scores, c_low) + mm(utb[...], ds_low, NT)
            d_c = mm(d_scores, b_low, TN) + mm(dyeb[...], st_ref[block_state], NT)
            conv_back(rows, pairs, d_b, b_xc, b_s, b_act)
            conv_back(rows, pairs + 1, d_c, c_xc, c_s, c_act)
            fade = fades[0:1, :]
            before_ds = dstate[...]
            through = jnp.sum(before_ds * st_ref[block_state].astype(f32), axis=0, keepdims=True) * fade
            products[3 * T : 3 * T + HEADS, :] = jnp.broadcast_to(through, (HEADS, width)).astype(bf16)
            dstate[...] = fade * before_ds + mm(c_t, dyeb[...])
            by_head = mm(pick_t[...], products[...], NT)
            inside = pieces(turn[...] + by_head[:, :T], 2)
            outside = pieces(by_head[:, T : 2 * T], 2)
            reached = mm(jnp.concatenate([inside, outside], axis=1), reach_ref[...])
            reached = reached + jnp.broadcast_to(by_head[:, 3 * T : 3 * T + 1], (HEADS, T))
            d_raw = (head_t[1] * reached + by_head[:, 2 * T : 3 * T]) * sigmoid(raw_t)
            d_ref[rows, wide:] = columns_of(d_raw).astype(bf16)
            hacc[0] += d_raw
            hacc[1] += dt_t * reached
            dxh[T : T + 8, :] = dxh[0:8, :]
            if sub == 1:
                @pl.when(tick == 0)
                def _():
                    for way in (0, 1):
                        hop(1, way, 0).start()

                ring_poll(1, tick)
        return 0

    lax.fori_loop(0, 2, work, 0)

    @pl.when(step == steps // 2 - 1)
    def _():
        total = lambda a: jnp.sum(a, axis=0, keepdims=True)
        for k in range(CONV + 1):
            small_ref[k : k + 1, :] = total(acc[k])
        small_ref[CONV + 1 : CONV + 2, :width] = total(gate_ref[...])
        small_ref[CONV + 1 : CONV + 2, width : width + LANES] = total(columns_of(hacc[0]))
        small_ref[CONV + 1 : CONV + 2, width + LANES :] = total(columns_of(hacc[1])) * head_ref[1:2, :]
        small_ref[CONV + 2 :, :] = jnp.zeros((2, wide), f32)
        skip = mm_exact(acc[CONV + 1, :, :width], pick_ref[...].astype(f32))
        small_ref[CONV + 3 : CONV + 4, 512 : 512 + LANES] = total(skip)
        for part in (0, 1):
            over_copy(part).wait_recv()

            def some(i, _, part=part):
                at = span(part * half + i * 32, 32)
                here = span(i * 32, 32)
                total = held[1, part, here, :].astype(f32) + over_slot[part, here, :].astype(f32)
                obranch_ref[at, :] = total.astype(bf16)
                return 0

            lax.fori_loop(0, half // 32, some, 0)
        for part in (0, 1):
            over_copy(part).wait_send()
            for turned in (0, 1):
                near_copy(turned, part).wait_send()
        for h in range(n - 1):
            for k in (0, 1):
                for way in (0, 1):
                    hop(k, way, h).wait_send()


def ssd_backward(n, dy, v, xc, dr, st, gate, taps, head, chan, early, branch):
    length, width = dy.shape
    wide = width + 2 * NS
    tall = 2 * ROWS
    steps = length // tall
    subs = tall // T
    own_rows, tokens = D // n, length // 4
    half = tokens // 2
    row = lambda m: pl.BlockSpec((tall, m), lambda i: (steps - 1 - i, 0))
    whole = lambda a: pl.BlockSpec(a.shape, lambda i: (0,) * a.ndim, pipeline_mode=pl.Buffered(1))
    fixed = lambda *shape: pl.BlockSpec(shape, lambda i: (0,) * len(shape))
    anywhere = pl.BlockSpec(memory_space=pl.ANY)
    vm, dma = pltpu.VMEM, pltpu.SemaphoreType.DMA
    return pl.pallas_call(
        functools.partial(backward_body, n, own_rows, tokens, width),
        grid=(steps,),
        in_specs=[
            row(width), row(wide), row(wide), row(LANES),
            pl.BlockSpec((subs, NS, width), lambda i: (steps - 1 - i, 0, 0)),
            whole(gate), whole(taps), whole(head), whole(chan), anywhere, anywhere,
        ],
        out_specs=[
            row(wide + LANES), fixed(8, wide), fixed(own_rows, 2 * width), fixed(tokens, D),
        ],
        out_shape=[
            jax.ShapeDtypeStruct((length, wide + LANES), bf16),
            jax.ShapeDtypeStruct((8, wide), f32),
            jax.ShapeDtypeStruct((own_rows, 2 * width), f32),
            jax.ShapeDtypeStruct((tokens, D), bf16),
        ],
        scratch_shapes=[
            vm((T + 8, wide), f32), vm((NS, width), f32), vm((T, width), f32), vm((T, width), f32),
            vm((T, width), bf16), vm((T, width), bf16), vm((3 * T + HEADS, width), bf16),
            vm((HEADS, T), f32), vm((CONV + 2, 8, wide), f32), vm((2, HEADS, T), f32),
            vm((width, LANES), bf16), vm((HEADS, width), bf16), vm((8, width), f32), vm((2, HEADS, LANES), f32),
            vm((3 * T, LANES), bf16), vm((4 * T, LANES), bf16),
            vm((D, 2 * width), bf16),
            [[vm((n - 1, size, width), bf16) for _ in (0, 1)] for _, size in cut_rows(own_rows)],
            vm((2, 2, half, D), bf16), vm((2, 2, half, D), bf16), vm((2, half, D), bf16),
            dma((5,)), dma((2, 2, n - 1)), dma((2, 2, n - 1)), dma((2, 2)), dma((2, 2)), dma((2,)), dma((2,)),
        ],
        compiler_params=pltpu.CompilerParams(
            collective_id=3, has_side_effects=True, vmem_limit_bytes=ROOM
        ),
        name="layer_backward",
    )(dy, v, xc, dr, st, gate, taps, head, chan, early, branch)


def reduce_body(
    n, rows, tokens, starts,
    xg_ref, d_ref, dz_ref, wp_ref, w_ref, small_ref, flat_ref, gain_ref,
    oxs_ref, oback_ref, bc_ref, oflat_ref,
    xg, d, dz, wz, w, work, grads, slots, staged, near, over, smalls, tens, bc_slot,
    load_sem, ring_send, ring_recv, near_send, near_recv, over_send, over_recv,
    small_send, small_recv, ten_send, ten_recv, bc_send, bc_recv,
):
    pos, ring, me, across, beside = neighbours(n)
    cuts = cut_rows(rows)
    core = lax.rem(me, 2)
    opposite = lax.rem(me + 2, 4)
    next_door = me + 1 - 2 * core
    far = lax.rem(next_door + 2, 4)
    half = tokens // 2
    late = d.shape[1]
    width = dz.shape[1]
    tile = 2 * LANES
    tiles = D // tile
    columns = [pl.ds(lo, hi - lo) for lo, hi in starts]
    sources = [(d_ref.at[:, columns[0]], d.at[:, columns[0]])]
    sources += [(xg_ref.at[:, pl.ds(i * tile, tile)], xg.at[:, pl.ds(i * tile, tile)]) for i in range(tiles)]
    sources += [(d_ref.at[:, some], d.at[:, some]) for some in columns[1:]]
    sources += [
        (dz_ref, dz), (w_ref, w), (wp_ref.at[:, pl.ds(width, width)], wz), (small_ref, smalls.at[pos]),
    ]
    loads = [pltpu.make_async_copy(src, dst, load_sem.at[k]) for k, (src, dst) in enumerate(sources)]
    for load in loads:
        load.start()
    askew = {"tensor": far}
    enter((*ring, across, beside, askew))
    started = []

    def go(*args):
        copy = remote(*args)
        copy.start()
        started.append(copy)

    def block_at(way, count):
        return ring_index(lax.rem(pos + (count if way else n - count), n), n)

    def hop(k, way, h):
        lo, hi = starts[k]
        first, size = cuts[way]
        if h == 0:
            src = grads.at[span(block_at(way, 1) * rows + first, size), pl.ds(lo, hi - lo)]
        else:
            src = slots[way][k].at[h - 1]
        return remote(
            src, slots[way][k].at[h], ring_send.at[way, k, h], ring_recv.at[way, k, h], ring[way]
        )

    def product(k):
        lo, hi = starts[k]

        def some(i, _):
            at = pl.ds(pl.multiple_of(i * tile, tile), tile)
            if k == 0:
                pltpu.make_async_copy(xg_ref.at[:, at], xg.at[:, at], load_sem.at[1 + i]).wait()
            grads[at, lo:hi] = mm(xg[:, at], d[:, lo:hi], TN).astype(bf16)
            return 0

        if k < 2:
            loads[0 if k == 0 else tiles + k].wait()
        lax.fori_loop(0, tiles, some, 0)
        for way in (0, 1):
            hop(k, way, 0).start()

    def near_copy(turned, part):
        return remote(
            staged.at[turned, part], near.at[turned, part],
            near_send.at[turned, part], near_recv.at[turned, part], beside,
        )

    def over_copy(part):
        return remote(near.at[0, part], over.at[part], over_send.at[part], over_recv.at[part], across)

    def ring_turn(k, h):
        lo, hi = starts[k]
        for way in (0, 1):
            first, size = cuts[way]
            slot = slots[way][k].at[h]
            remote(slot, slot, ring_send.at[way, k, h], ring_recv.at[way, k, h], ring[way]).wait_recv()
            block = block_at(way, 2 + h) if h < n - 2 else block_at(way, 0)

            tile = strip(size)

            def some(i, _, way=way, first=first, block=block, tile=tile):
                came = slots[way][k][h, span(i * tile, tile), :]
                mine = grads[span(block * rows + first + i * tile, tile), lo:hi]
                if h < n - 2:
                    slots[way][k][h, span(i * tile, tile), :] = came + mine
                else:
                    oxs_ref[span(first + i * tile, tile), lo:hi] = came.astype(f32) + mine.astype(f32)
                return 0

            lax.fori_loop(0, size // tile, some, 0)
            if h < n - 2:
                hop(k, way, h + 1).start()

    def small_hop(way, h):
        here = smalls.at[lax.rem(pos + (h if way else n - h), n)]
        go(here, here, small_send.at[way, h], small_recv.at[way, h], ring[way])

    def small_lands(way, h):
        here = smalls.at[lax.rem(pos + (h + 1 if way else n - h - 1), n)]
        remote(here, here, small_send.at[way, h], small_recv.at[way, h], ring[way]).wait_recv()

    product(0)
    product(1)
    for load in loads[tiles + 2 :]:
        load.wait()
    turns = {0: [(0, 0)], 1: [(1, 0)], 2: [(0, 1)], 3: [(1, 1)], 4: [(0, 2), (1, 2)], 5: [(2, 0)], 6: [(0, 3), (1, 3)], 7: [(2, 1)]}
    taken = [sum(k == group for some in turns.values() for k, _ in some) for group in range(len(starts))]

    def block(i, _):
        pl.when(i == 4)(functools.partial(product, 2))
        which, part = lax.div(i, 2), lax.rem(i, 2)
        own = lax.rem(which, 2)
        turned = lax.div(which, 2)
        target = lax.rem(next_door + own * (me - next_door) + 2 * (1 - turned), 4)
        at = span(target * tokens + part * half, half)
        total = mm(dz[at, :], wz[...], NT) + mm(d[at, :], w[...], NT)
        work[...] = total

        @pl.when(own == 0)
        def _():
            staged[turned, part] = work[...].astype(bf16)
            near_copy(turned, part).start()

        @pl.when(own == 1)
        def _():
            near_copy(turned, part).wait_recv()

        @pl.when(which == 1)
        def _():
            near[0, part] = (work[...] + near[0, part].astype(f32)).astype(bf16)
            over_copy(part).start()

        @pl.when(which == 3)
        def _():
            near[1, part] = (work[...] + near[1, part].astype(f32)).astype(bf16)

        for at_block, some in turns.items():

            @pl.when(i == at_block)
            def _(some=some):
                for k, h in some:
                    ring_turn(k, h)

        return 0

    lax.fori_loop(0, 8, block, 0)
    for i in range(tiles):
        share = jnp.zeros((tile, LANES), f32)
        for c in range(late // LANES):
            cols = slice(c * LANES, (c + 1) * LANES)
            at = slice(i * tile, (i + 1) * tile)
            share = share + grads[at, cols].astype(f32) * w[at, cols].astype(f32)
        total = mm_exact(jnp.ones((8, LANES), f32), share, NT)[0:1] + gain_ref[0:1, i * tile : (i + 1) * tile]
        for c in range(2 * i, 2 * i + 2):
            row, col = 6 + c // 8, (c % 8) * LANES
            part = total[:, (c - 2 * i) * LANES : (c - 2 * i + 1) * LANES]
            smalls[pos, row : row + 1, col : col + LANES] = part / flat_ref[c : c + 1, :]

    rest = [(k, h) for h in range(n - 1) for k in (2, 0, 1) if h >= taken[k]]
    rest.sort(key=lambda turn: turn[1] - taken[turn[0]])

    def small_step(s):
        for way in (0, 1):
            if s > 0 and (way == 0 or s < n // 2):
                small_lands(way, s - 1)
            if s < n // 2 - way:
                small_hop(way, s)

    small_step(0)
    steps_done = 1
    for at, (k, h) in enumerate(rest):
        ring_turn(k, h)
        if (k, h) == (0, n - 2):
            bc_slot[0] = oxs_ref[:, starts[0][0] : starts[0][0] + 2 * NS]
            go(bc_slot.at[0], bc_slot.at[1], bc_send.at[0], bc_recv.at[0], beside)
        if at % 2 == 1 and steps_done < n // 2:
            small_step(steps_done)
            steps_done += 1
    for s in range(steps_done, n // 2):
        small_step(s)
    small_lands(0, n // 2 - 1)

    total = smalls[0]
    for i in range(1, n):
        total = total + smalls[i]
    tens[me] = total
    others = ((beside, next_door), (across, opposite), (askew, far))
    for k, (peer, _) in enumerate(others):
        go(tens.at[me], tens.at[me], ten_send.at[k], ten_recv.at[k], peer)
    remote(bc_slot.at[1], bc_slot.at[1], bc_send.at[0], bc_recv.at[0], beside).wait_recv()
    bc_slot[2] = bc_slot[0] + bc_slot[1]
    go(bc_slot.at[2], bc_slot.at[3], bc_send.at[1], bc_recv.at[1], across)
    for part in (0, 1):
        over_copy(part).wait_recv()

        def some(i, _, part=part):
            at = span(part * half + i * 32, 32)
            here = span(i * 32, 32)
            oback_ref[at, :] = (near[1, part, here, :].astype(f32) + over[part, here, :].astype(f32)).astype(bf16)
            return 0

        lax.fori_loop(0, half // 32, some, 0)
    for k, (peer, target) in enumerate(others):
        here = tens.at[target]
        remote(here, here, ten_send.at[k], ten_recv.at[k], peer).wait_recv()
    flat_gradients(width, tens, oflat_ref)
    remote(bc_slot.at[3], bc_slot.at[3], bc_send.at[1], bc_recv.at[1], across).wait_recv()
    bc_ref[...] = bc_slot[2] + bc_slot[3]
    for part in (0, 1):
        over_copy(part).wait_send()
        for turned in (0, 1):
            near_copy(turned, part).wait_send()
    for k in range(len(starts)):
        for way in (0, 1):
            for h in range(n - 1):
                hop(k, way, h).wait_send()
    for copy in started:
        copy.wait_send()


def flat_gradients(width, tens, out_ref):
    pairs = width // LANES
    heads = width // P_SIZE

    def sums(row, col):
        total = tens[0, row : row + 1, col : col + LANES]
        for t in range(1, 4):
            total = total + tens[t, row : row + 1, col : col + LANES]
        return total

    def put(row, value):
        out_ref[row : row + 1, :] = value

    for c in range(D // LANES):
        put(c, sums(6 + c // 8, (c % 8) * LANES))
    for t in range(4):
        for c in range(pairs):
            cols = slice(c * LANES, (c + 1) * LANES)
            put(GATE_ROW + pairs * t + c, tens[t, CONV + 1 : CONV + 2, cols])
            put(BIAS_ROW + pairs * t + c, tens[t, CONV : CONV + 1, cols])
            for k in range(CONV):
                put(TAPS_ROW + 4 * pairs * k + pairs * t + c, tens[t, k : k + 1, cols])
    for c in range(2):
        put(BIAS_BC_ROW + c, sums(CONV, width + c * LANES))
        for k in range(CONV):
            put(TAPS_BC_ROW + 2 * k + c, sums(k, width + c * LANES))
    kinds = ((CONV + 1, width), (CONV + 1, width + LANES), (CONV + 3, 512))
    rows = [tens[t, row : row + 1, col : col + LANES] for row, col in kinds for t in range(4)]
    rows = jnp.concatenate(rows + [jnp.zeros((16 - len(rows), LANES), f32)], axis=0)
    lane = lax.broadcasted_iota(jnp.int32, (LANES, 2 * LANES), 1)
    entry = lax.broadcasted_iota(jnp.int32, (LANES, 2 * LANES), 0)
    spread_out = mm_exact(rows, jnp.where(lax.rem(lane, heads) == entry, 1.0, 0.0).astype(f32))
    at = lax.broadcasted_iota(jnp.int32, (16, 2 * LANES), 1)
    source = lax.broadcasted_iota(jnp.int32, (16, 2 * LANES), 0)
    line = jnp.sum(jnp.where(lax.div(at, heads) == source, spread_out, 0.0), axis=0, keepdims=True)
    put(HEAD_ROW, line[:, :LANES])
    put(HEAD_ROW + 1, line[:, LANES:])


def reduce_all(n, xg, d, dz, wp, w, small, flat, gain):
    rows, tokens = D // n, dz.shape[0] // 4
    width, late = dz.shape[1], d.shape[1]
    starts = ((width, late), (0, width // 2), (width // 2, width))
    half = tokens // 2
    dma, vm = pltpu.SemaphoreType.DMA, pltpu.VMEM
    anywhere = pl.BlockSpec(memory_space=pl.ANY)
    inside = pl.BlockSpec(memory_space=pltpu.VMEM)
    return pl.pallas_call(
        functools.partial(reduce_body, n, rows, tokens, starts),
        in_specs=[anywhere] * 6 + [inside] * 2,
        out_specs=[inside] * 4,
        out_shape=[
            jax.ShapeDtypeStruct((rows, late), f32),
            jax.ShapeDtypeStruct((tokens, D), bf16),
            jax.ShapeDtypeStruct((rows, 2 * NS), f32),
            jax.ShapeDtypeStruct((FLAT_ROWS, LANES), f32),
        ],
        scratch_shapes=[
            vm(xg.shape, bf16), vm(d.shape, bf16), vm(dz.shape, bf16), vm((D, width), bf16),
            vm((D, late), bf16),
            vm((half, D), f32), vm((D, late), bf16),
            [[vm((n - 1, size, hi - lo), bf16) for lo, hi in starts] for _, size in cut_rows(rows)],
            vm((2, 2, half, D), bf16), vm((2, 2, half, D), bf16), vm((2, half, D), bf16),
            vm((n, *small.shape), f32), vm((4, *small.shape), f32), vm((4, rows, 2 * NS), f32),
            dma((13,)), dma((2, 3, n - 1)), dma((2, 3, n - 1)), dma((2, 2)), dma((2, 2)), dma((2,)), dma((2,)),
            dma((2, n // 2)), dma((2, n // 2)), dma((3,)), dma((3,)), dma((2,)), dma((2,)),
        ],
        compiler_params=pltpu.CompilerParams(
            collective_id=1, has_side_effects=True, vmem_limit_bytes=46 * 2**20
        ),
        name="reduce_all",
    )(xg, d, dz, wp, w, small, flat, gain)


def adamw_step(weight, first, second, grad, rate, decay):
    first_new = beta_first * first + (1.0 - beta_first) * grad
    second_new = beta_second * second + (1.0 - beta_second) * grad * grad
    hat_first = first_new * (1.0 / (1.0 - beta_first**STEP))
    hat_second = second_new * (1.0 / (1.0 - beta_second**STEP))
    weight_new = weight - rate * (hat_first / (jnp.sqrt(hat_second) + adam_eps) + decay * weight)
    return (weight_new, first_new, second_new)


def finish_body(
    width, heads,
    in_ref, cot_ref, branch_ref, back_ref, flat_ref, early_ref, late_ref, bcg_ref,
    zx_ref, zx1_ref, zx2_ref, bc_ref, bc1_ref, bc2_ref, out_ref, out1_ref, out2_ref, late_all_ref, dt_ref, dt1_ref, dt2_ref,
    layer_ref, grad_ref, zxn_ref, zx1n_ref, zx2n_ref, bcn_ref, bc1n_ref, bc2n_ref,
    outn_ref, out1n_ref, out2n_ref, dtn_ref, dt1n_ref, dt2n_ref,
):
    def update(refs, news, grad):
        fresh = adamw_step(*(ref[...] for ref in refs), grad, matrix_rate, matrix_decay)
        for ref, value in zip(news, fresh):
            ref[...] = value

    for k, grad in ((0, early_ref), (1, late_ref)):
        fresh = adamw_step(
            *(ref[:, k, :] for ref in (zx_ref, zx1_ref, zx2_ref)), grad[:, :width], matrix_rate, matrix_decay
        )
        for ref, value in zip((zxn_ref, zx1n_ref, zx2n_ref), fresh):
            ref[:, k, :] = value
    update((bc_ref, bc1_ref, bc2_ref), (bcn_ref, bc1n_ref, bc2n_ref), bcg_ref[...])
    update((out_ref, out1_ref, out2_ref), (outn_ref, out1n_ref, out2n_ref), early_ref[:, width:])

    @pl.when(pl.program_id(0) == 0)
    def _():
        unit = jnp.where(
            lax.broadcasted_iota(jnp.int32, (16, LANES), 0) == lax.broadcasted_iota(jnp.int32, (16, LANES), 1), 1.0, 0.0
        ).astype(f32)
        turned = mm_exact(unit, late_all_ref[:, width + 2 * NS :], NT)
        update((dt_ref, dt1_ref, dt2_ref), (dtn_ref, dt1n_ref, dt2n_ref), turned[:heads])

    rows = in_ref.shape[0]
    tile = 64

    def some(i, _):
        at = span(i * tile, tile)
        squares = jnp.zeros((tile, LANES), f32)
        inner = jnp.zeros((tile, LANES), f32)
        for c in range(D // LANES):
            cols = slice(c * LANES, (c + 1) * LANES)
            x = in_ref[at, cols].astype(f32)
            squares = squares + x * x
            inner = inner + x * flat_ref[c : c + 1, :] * back_ref[at, cols].astype(f32)
        r = lax.rsqrt(jnp.sum(squares, axis=-1, keepdims=True) / D + norm_eps)
        k = r * r * r * jnp.sum(inner, axis=-1, keepdims=True) / D
        r, k = jnp.broadcast_to(r, (tile, LANES)), jnp.broadcast_to(k, (tile, LANES))
        for c in range(D // LANES):
            cols = slice(c * LANES, (c + 1) * LANES)
            x = in_ref[at, cols].astype(f32)
            layer_ref[at, cols] = (x + branch_ref[at, cols].astype(f32)).astype(bf16)
            back = back_ref[at, cols].astype(f32)
            grad_ref[at, cols] = cot_ref[at, cols].astype(f32) + r * flat_ref[c : c + 1, :] * back - x * k
        return 0

    lax.fori_loop(0, rows // tile, some, 0)


def finish(layer_input, out_grad, branch, back, flat, early, late, bcg, zx, bc, out, dt):
    (rows, width), heads = out[0].shape, dt[0].shape[0]
    steps = 2
    part = lambda a: pl.BlockSpec((a.shape[0] // steps, *a.shape[1:]), lambda i: (i,) + (0,) * (a.ndim - 1))
    whole = lambda a: pl.BlockSpec(a.shape, lambda i: (0,) * a.ndim)
    like = lambda a, dtype=f32: jax.ShapeDtypeStruct(a.shape, dtype)
    weights = (*zx, *bc, *out)
    return pl.pallas_call(
        functools.partial(finish_body, width, heads),
        grid=(steps,),
        in_specs=[
            *(part(a) for a in (layer_input, out_grad, branch, back)), whole(flat),
            *(part(a) for a in (early, late, bcg, *weights)), whole(late), *(whole(a) for a in dt),
        ],
        out_specs=[part(layer_input), part(back), *(part(a) for a in weights), *(whole(a) for a in dt)],
        out_shape=[like(layer_input, bf16), like(layer_input), *(like(a) for a in weights), *(like(a) for a in dt)],
        compiler_params=pltpu.CompilerParams(vmem_limit_bytes=32 * 2**20),
        name="finish",
    )(layer_input, out_grad, branch, back, flat, early, late, bcg, *weights, late, *dt)


def local(
    layer_input,
    out_grad,
    small_params,
    small_first,
    small_second,
    w_zx,
    zx_first,
    zx_second,
    w_bc,
    bc_first,
    bc_second,
    w_dt,
    dt_first,
    dt_second,
    w_out,
    out_first,
    out_second,
):
    n = lax.axis_size("dp")
    flat = jnp.pad(small_params, (0, FLAT_ROWS * LANES - small_params.shape[0])).reshape(FLAT_ROWS, LANES)
    v, xc, dr, st, dy, dz, branch, early, gate, gain, xg, w_all, pair_all, taps, head, chan = ssd_forward(
        n, layer_input, out_grad, flat, w_zx, w_bc, w_dt.T, w_out
    )
    d_late, small, owner_early, own_branch = ssd_backward(
        n, dy, v, xc, dr, st, gate, taps, head, chan, early, branch
    )
    owner_late, d_normed_in, owner_bc, flat_grad = reduce_all(
        n, xg, d_late, dz, pair_all, w_all, small, flat, gain
    )
    small_grad = flat_grad.reshape(-1)[: small_params.shape[0]]
    small_new, small_first_new, small_second_new = adamw_step(
        small_params, small_first, small_second, small_grad, small_rate, 0.0
    )
    (
        layer_output, input_grad, zx_new, zx_first_new, zx_second_new, bc_new, bc_first_new, bc_second_new,
        out_new, out_first_new, out_second_new, dt_new, dt_first_new, dt_second_new,
    ) = finish(
        layer_input, out_grad, own_branch, d_normed_in, flat, owner_early, owner_late, owner_bc,
        (w_zx, zx_first, zx_second), (w_bc, bc_first, bc_second), (w_out, out_first, out_second),
        (w_dt.T, dt_first.T, dt_second.T),
    )
    dt_new, dt_first_new, dt_second_new = dt_new.T, dt_first_new.T, dt_second_new.T
    return (
        layer_output,
        input_grad,
        small_new,
        small_first_new,
        small_second_new,
        zx_new,
        zx_first_new,
        zx_second_new,
        bc_new,
        bc_first_new,
        bc_second_new,
        dt_new,
        dt_first_new,
        dt_second_new,
        out_new,
        out_first_new,
        out_second_new,
    )


def solution(mesh):
    return jax.shard_map(
        local,
        mesh=mesh,
        in_specs=(
            P(("dp", "tensor"), None),
            P(("dp", "tensor"), None),
            P(),
            P(),
            P(),
            P("dp", None, "tensor"),
            P("dp", None, "tensor"),
            P("dp", None, "tensor"),
            P("dp", None),
            P("dp", None),
            P("dp", None),
            P("dp", "tensor"),
            P("dp", "tensor"),
            P("dp", "tensor"),
            P("dp", "tensor"),
            P("dp", "tensor"),
            P("dp", "tensor"),
        ),
        out_specs=(
            P(("dp", "tensor"), None),
            P(("dp", "tensor"), None),
            P(),
            P(),
            P(),
            P("dp", None, "tensor"),
            P("dp", None, "tensor"),
            P("dp", None, "tensor"),
            P("dp", None),
            P("dp", None),
            P("dp", None),
            P("dp", "tensor"),
            P("dp", "tensor"),
            P("dp", "tensor"),
            P("dp", "tensor"),
            P("dp", "tensor"),
            P("dp", "tensor"),
        ),
        check_vma=False,
    )
```

```python
import functools

import jax
import jax.numpy as jnp
from jax import lax
from jax.experimental import pallas as pl
from jax.experimental.pallas import tpu as pltpu
from jax.sharding import PartitionSpec as P

D = 1536
DI = 3072
H = 48
NS = 128
P_SIZE = 64
CONV = 4
LEN = 2048
STEP = 10

T = 128
ROWS = 256
LANES = 128
ROOM = 60 * 2**20

norm_eps = 1e-05
adam_eps = 1e-08
beta_first = 0.9
beta_second = 0.95
matrix_rate = 0.01
small_rate = 0.1
matrix_decay = 0.1

f32 = jnp.float32
bf16 = jnp.bfloat16
NN = (((1,), (0,)), ((), ()))
NT = (((1,), (1,)), ((), ()))
TN = (((0,), (0,)), ((), ()))
HIGHEST = lax.Precision.HIGHEST


GATE_ROW, TAPS_ROW, BIAS_ROW, TAPS_BC_ROW, BIAS_BC_ROW, HEAD_ROW, FLAT_ROWS = 12, 36, 132, 156, 164, 166, 168


def mm(a, b, dims=NN):
    return lax.dot_general(a, b, dims, preferred_element_type=f32)


def mm_exact(a, b, dims=NN):
    return lax.dot_general(a, b, dims, preferred_element_type=f32, precision=HIGHEST)


def sigmoid(v):
    return 0.5 * jnp.tanh(0.5 * v) + 0.5


def softplus(v):
    return jnp.maximum(v, 0.0) + jnp.log1p(jnp.exp(-jnp.abs(v)))


def spread(col):
    return jnp.broadcast_to(col, (T, LANES))


def block_iota(axis):
    return lax.broadcasted_iota(jnp.int32, (T, LANES), axis)


HEADS = 16
LOG2_E = 1.4426950408889634


def pieces(value, count):
    parts = []
    for k in range(count):
        part = value.astype(bf16)
        parts.append(part)
        if k < count - 1:
            value = value - part.astype(f32)
    return jnp.concatenate(parts, axis=1)


def columns_of(rows):
    return jnp.concatenate([rows, jnp.zeros((LANES - HEADS, T), f32)], axis=0).T


def set_heads(head_ref, head_t, until):
    turned = jnp.concatenate([head_ref[...], jnp.zeros((LANES - 8, LANES), f32)], axis=0).T
    head_t[0] = spread(turned[:, 0:1])[:HEADS]
    head_t[1] = spread(turned[:, 1:2])[:HEADS]
    matrix = jnp.where(block_iota(0) <= block_iota(1), 1.0, 0.0).astype(bf16)
    for k in range(3):
        until[k * T : (k + 1) * T, :] = matrix


def head_rows(dr_ref, head_t, until, rows):
    raw = dr_ref[rows, :].T[:HEADS] + head_t[0]
    dt = softplus(raw)
    decay = mm(pieces(dt * (head_t[1] * LOG2_E), 3), until[...])
    return raw, dt, decay, columns_of(dt), columns_of(decay)


def ring_place(n):
    me = lax.axis_index("dp")
    z, x = lax.div(me, 2), lax.rem(me, 2)
    return z + x * (n - 1 - 2 * z)


def ring_index(pos, n):
    back = lax.div(pos, n // 2)
    return 2 * pos + back * (2 * n - 1 - 4 * pos)


def neighbours(n):
    pos = ring_place(n)
    right = ring_index(lax.rem(pos + 1, n), n)
    left = ring_index(lax.rem(pos + n - 1, n), n)
    me = lax.axis_index("tensor")
    y, core = lax.div(me, 2), lax.rem(me, 2)
    across = 2 * (1 - y) + core
    beside = 2 * y + 1 - core
    return pos, ({"dp": right}, {"dp": left}), me, {"tensor": across}, {"tensor": beside}


def greet(peers):
    barrier = pltpu.get_barrier_semaphore()
    for peer in peers:
        pl.semaphore_signal(barrier, inc=1, device_id=peer, device_id_type=pl.DeviceIdType.MESH)


def enter(peers):
    greet(peers)
    pl.semaphore_wait(pltpu.get_barrier_semaphore(), len(peers))


def remote(src, dst, send_sem, recv_sem, peer):
    return pltpu.make_async_remote_copy(
        src_ref=src, dst_ref=dst, send_sem=send_sem, recv_sem=recv_sem,
        device_id=peer, device_id_type=pl.DeviceIdType.MESH,
    )


def span(start, size):
    return pl.ds(pl.multiple_of(start, 16), size)


def strip(rows):
    return next(size for size in (48, 32, 16) if rows % size == 0)


def cut_rows(rows):
    top = rows // 32 * 16
    return ((0, top), (top, rows - top))


def forward_body(
    n, rows, tokens, width,
    in_ref, cot_ref, flat_ref, wzx_ref, wbc_ref, wdt_ref, wout_ref,
    v_ref, xc_ref, dr_ref, st_ref, dy_ref, dz_ref, branch_ref, early_ref, gate_ref, gain_ref,
    xg_ref, ws_ref, wps_ref, taps_ref, head_ref, chan_ref,
    halo, state, y_all, z_all, dn_all, nl_all, dz_all, xg, cots, ws, wps, sums, red, head_t, until, across_state, tails,
    own_keep, early_keep, lead_keep, lead_send, lead_recv, x_keep, x_over_send, x_over_recv, x_side_send, x_side_recv,
    x_pass_send, x_pass_recv, ring_keep, ring_send, ring_recv, over_send, over_recv,
    side_send, side_recv, pass_send, pass_recv, sum_send, sum_recv,
):
    pairs = width // LANES
    wide = width + 2 * NS
    step = pl.program_id(0)
    steps = LEN // ROWS
    tall = 2 * ROWS
    norming = steps // 2
    gating = norming + 1
    forming = gating + 1
    products = forming + steps // 2
    pos, ring, me, across, beside = neighbours(n)
    opposite = lax.rem(me + 2, 4)
    next_door = me + 1 - 2 * lax.rem(me, 2)
    far = lax.rem(next_door + 2, 4)
    askew = {"tensor": far}
    quarter = tokens // 4
    hops = n // 2
    cuts = cut_rows(rows)
    mine = ring_index(pos, n)

    late = wide + LANES
    parts_of = ((0, width), (width, width))

    def hop(k, part, way, h):
        first, size = cuts[part]
        cols = pl.ds(*parts_of[k])
        block = ring_index(lax.rem(pos + (h if way else n - h), n), n)
        here = wps.at[span(block * rows + first, size), cols]
        return remote(here, here, ring_send.at[way, part, k, h], ring_recv.at[way, part, k, h], ring[way])

    def hop_lands(k, part, way, h):
        first, size = cuts[part]
        block = ring_index(lax.rem(pos + (h + 1 if way else n - h - 1), n), n)
        return span(block * rows + first, size), pl.ds(*parts_of[k])

    def hop_arrival(k, part, way, h):
        here = wps.at[hop_lands(k, part, way, h)]
        return remote(here, here, ring_send.at[way, part, k, h], ring_recv.at[way, part, k, h], ring[way])

    def hop_keep(part, way, h):
        at = hop_lands(1, part, way, h)
        return pltpu.make_async_copy(wps.at[at], wps_ref.at[at], ring_keep.at[way, part, h])

    def hop_ways(h):
        return [(part, way) for part in (0, 1) for way in (0, 1) if h < hops - 1 or part == way]

    def hop_on(k, h):
        for part, way in hop_ways(h - 1) if h > 0 else ():
            hop_arrival(k, part, way, h - 1).wait_recv()
            if k == 1:
                hop_keep(part, way, h - 1).start()
            if h < hops and (part, way) in hop_ways(h):
                hop(k, part, way, h).start()
        if h == 0:
            for part, way in hop_ways(0):
                hop(k, part, way, 0).start()

    def over(k):
        return remote(
            cot_ref.at[pl.ds(k * quarter, quarter)], cots.at[span(me * tokens + k * quarter, quarter)],
            over_send.at[k], over_recv.at[k], across,
        )

    def landed(start, size, send, recv, peer):
        here = cots.at[span(start, size)]
        return remote(here, here, send, recv, peer)

    def over_arrival(k):
        return landed(opposite * tokens + k * quarter, quarter, over_send.at[k], over_recv.at[k], across)

    def passing(k):
        return landed(opposite * tokens + k * quarter, quarter, pass_send.at[k], pass_recv.at[k], beside)

    def pass_arrival(k):
        return landed(far * tokens + k * quarter, quarter, pass_send.at[k], pass_recv.at[k], beside)

    def side():
        return remote(cot_ref, cots.at[span(me * tokens, tokens)], side_send.at[0], side_recv.at[0], beside)

    def side_arrival():
        return landed(next_door * tokens, tokens, side_send.at[0], side_recv.at[0], beside)

    def own_cot():
        return pltpu.make_async_copy(cot_ref, cots.at[span(me * tokens, tokens)], own_keep.at[0])

    def own_z():
        at = span(mine * rows, rows), pl.ds(*parts_of[1])
        return pltpu.make_async_copy(wps.at[at], wps_ref.at[at], own_keep.at[1])

    def pass_on(*pieces):
        for k in pieces:
            over_arrival(k).wait_recv()
            passing(k).start()

    def normalize(k):
        def some(i, _):
            at = span(me * tokens + k * quarter + i * 64, 64)
            squares = jnp.zeros((64, LANES), f32)
            for c in range(D // LANES):
                x = xg[at, c * LANES : (c + 1) * LANES].astype(f32)
                squares = squares + x * x
            inverse = lax.rsqrt(jnp.sum(squares, axis=-1, keepdims=True) / D + norm_eps)
            inverse = jnp.broadcast_to(inverse, (64, LANES))
            for c in range(D // LANES):
                cols = slice(c * LANES, (c + 1) * LANES)
                xg[at, cols] = (xg[at, cols].astype(f32) * inverse * flat_ref[c : c + 1, :]).astype(bf16)
            return 0

        lax.fori_loop(0, quarter // 64, some, 0)

    @pl.when(step == 0)
    def _():
        own_rows = span(me * tokens, tokens)
        greet((*ring, across, beside, askew))
        load = pltpu.make_async_copy(in_ref, xg.at[own_rows], own_keep.at[2])
        load.start()
        own_cot().start()
        mine_at = span(mine * rows, rows)
        ws[mine_at, :width] = wzx_ref[:, 1, :].astype(bf16)
        ws[mine_at, width:wide] = wbc_ref[...].astype(bf16)
        heads = wdt_ref.shape[0]
        unit = jnp.where(
            lax.broadcasted_iota(jnp.int32, (16, LANES), 0) == lax.broadcasted_iota(jnp.int32, (16, LANES), 1), 1.0, 0.0
        ).astype(bf16)
        steps_w = jnp.concatenate([wdt_ref[...], jnp.zeros((16 - heads, rows), f32)], axis=0).astype(bf16)
        ws[mine_at, wide:] = mm(steps_w, unit, TN).astype(bf16)
        load.wait()
        normalize(0)
        pl.semaphore_wait(pltpu.get_barrier_semaphore(), 5)
        started, kept = [], []

        def go(*args):
            copy = remote(*args)
            copy.start()
            started.append(copy)

        def keep(src, dst, sem):
            copy = pltpu.make_async_copy(src, dst, sem)
            copy.start()
            kept.append(copy)

        def arrived(part, way, h, block):
            first, size = cuts[part]
            at = span(block * rows + first, size)
            remote(
                ws.at[at], ws.at[at], lead_send.at[way, part, h], lead_recv.at[way, part, h], ring[way]
            ).wait_recv()
            keep(ws.at[at], ws_ref.at[at], lead_keep.at[way, part, h])

        def lead(h, parts=(0, 1)):
            for part in parts:
                first, size = cuts[part]
                for way in (0, 1):
                    block = ring_index(lax.rem(pos + (h if way else n - h), n), n)
                    here = ws.at[span(block * rows + first, size)]
                    if h > 0:
                        arrived(part, way, h - 1, block)
                    if h == hops - 1 and part != way:
                        continue
                    go(here, here, lead_send.at[way, part, h], lead_recv.at[way, part, h], ring[way])

        def x_over(k):
            at = span(me * tokens + k * quarter, quarter)
            go(xg.at[at], xg.at[at], x_over_send.at[k], x_over_recv.at[k], across)

        def x_pass(k):
            at = span(opposite * tokens + k * quarter, quarter)
            here = xg.at[at]
            remote(here, here, x_over_send.at[k], x_over_recv.at[k], across).wait_recv()
            go(here, here, x_pass_send.at[k], x_pass_recv.at[k], beside)
            keep(here, xg_ref.at[at], x_keep.at[k])

        def x_pass_lands(k):
            at = span(far * tokens + k * quarter, quarter)
            remote(xg.at[at], xg.at[at], x_pass_send.at[k], x_pass_recv.at[k], beside).wait_recv()
            keep(xg.at[at], xg_ref.at[at], x_keep.at[4 + k])

        lead(0, (0,))
        leading = list(started)
        x_over(0)
        for k in (1, 2, 3):
            normalize(k)
            if k == 1:
                x_over(1)
        go(xg.at[own_rows], xg.at[own_rows], x_side_send.at[0], x_side_recv.at[0], beside)
        keep(xg.at[own_rows], xg_ref.at[own_rows], x_keep.at[8])
        wps[mine_at, :width] = wout_ref[...].astype(bf16)
        wps[mine_at, width:] = wzx_ref[:, 0, :].astype(bf16)
        for copy in leading:
            copy.wait_send()
            started.remove(copy)
        lead(0, (1,))
        keep(ws.at[mine_at], ws_ref.at[mine_at], x_keep.at[9])
        own_z().start()
        halo[0:8, :] = jnp.zeros((8, wide), f32)
        state[...] = jnp.zeros_like(state)
        gate_ref[...] = jnp.zeros_like(gate_ref)
        parameter_rows(me, width, flat_ref, taps_ref, head_ref, chan_ref)
        set_heads(head_ref, head_t, until)
        lead(1)
        x_over(2)
        at = span(next_door * tokens, tokens)
        remote(xg.at[at], xg.at[at], x_side_send.at[0], x_side_recv.at[0], beside).wait_recv()
        keep(xg.at[at], xg_ref.at[at], x_keep.at[10])
        side().start()
        lead(2)
        x_over(3)
        x_pass(0)
        x_pass(1)
        for h in range(3, hops):
            lead(h)
        hop_on(0, 0)
        x_pass(2)
        over(0).start()
        x_pass_lands(0)
        x_pass_lands(1)
        x_pass(3)
        for part in (0, 1):
            arrived(part, part, hops - 1, ring_index(lax.rem(pos + n // 2, n), n))
        hop_on(1, 0)
        over(1).start()
        x_pass_lands(2)
        x_pass_lands(3)
        for copy in kept:
            copy.wait()
        for copy in started:
            copy.wait_send()

    def at_tick(tick):
        for k, times in enumerate(((1, 5), (3, 6))):
            for h in (1, 2):
                pl.when(tick == times[h - 1])(functools.partial(hop_on, k, h))

        @pl.when(tick == 2)
        def _():
            over(2).start()

        @pl.when(tick == 4)
        def _():
            over(3).start()
            pass_on(0, 1)

        pl.when(tick == steps - 1)(functools.partial(pass_on, 2))

    @pl.when(step < norming)
    def _():
        def chunk(i, _):
            tick = 2 * step + i
            at_tick(tick)
            scan_step(
                width, tick, i, xg, ws, taps_ref, head_ref, chan_ref,
                v_ref, xc_ref, dr_ref, st_ref, halo, state, y_all, head_t, until, across_state, tails,
                functools.partial(pass_on, 3),
            )
            return 0

        lax.fori_loop(0, 2, chunk, 0)

    @pl.when(step == norming)
    def _():
        for h in range(3, hops):
            for k in (0, 1):
                hop_on(k, h)
        hop_on(0, hops)
        side_arrival().wait_recv()
        for k in range(4):
            pass_arrival(k).wait_recv()
        own_cot().wait()
        own_z().wait()

        def some(i, _):
            at = span(i * tall, tall)
            dn_all[at, :] = mm(cots[at, :], wps[:, :width]).astype(bf16)
            return 0

        lax.fori_loop(0, LEN // tall, some, 0)

    @pl.when(step == gating)
    def _():
        hop_on(1, hops)
        ones = jnp.ones((8, LANES), f32)

        def some(i, _):
            at = span(i * tall, tall)
            z_all[at, :] = mm(xg[at, :], wps[:, width:])
            for sub in range(tall // T):
                rows_at = span(i * tall + sub * T, T)
                squares = jnp.zeros((T, LANES), f32)
                inner = jnp.zeros((T, LANES), f32)
                for p in range(pairs):
                    cols = slice(p * LANES, (p + 1) * LANES)
                    z = z_all[rows_at, cols]
                    gated = y_all[rows_at, cols] * (z * sigmoid(z))
                    squares = squares + gated * gated
                    inner = inner + gated * chan_ref[0:1, cols] * dn_all[rows_at, cols].astype(f32)
                lanes = pl.ds(pl.multiple_of(i * tall + sub * T, T), T)
                sums[me, 0:4, lanes] = mm_exact(ones, squares, NT)[0:4]
                sums[me, 4:8, lanes] = mm_exact(ones, inner, NT)[4:8]
            return 0

        lax.fori_loop(0, LEN // tall, some, 0)

    @pl.when(step == forming - 1)
    def _():
        peers = ((beside, next_door), (across, opposite), (askew, far))
        for k, (peer, _) in enumerate(peers):
            remote(sums.at[me], sums.at[me], sum_send.at[k], sum_recv.at[k], peer).start()
        for h in range(hops):
            for part, way in hop_ways(h):
                for k in (0, 1):
                    hop(k, part, way, h).wait_send()
                hop_keep(part, way, h).wait()
        side().wait_send()
        for k in range(4):
            over(k).wait_send()
            passing(k).wait_send()
        for k, (peer, other) in enumerate(peers):
            remote(sums.at[other], sums.at[other], sum_send.at[k], sum_recv.at[k], peer).wait()
        red[...] = ((sums[0] + sums[1]) + sums[2]) + sums[3]

    @pl.when((step >= forming) & (step < products))
    def _():
        def some(i, _):
            first = (step - forming) * tall + i * ROWS
            lanes = pl.ds(pl.multiple_of(first, ROWS), ROWS)
            q_row = lax.rsqrt(red[0:4, lanes] / DI + norm_eps)
            k_row = q_row * q_row * q_row * red[4:8, lanes] / DI
            turned = jnp.concatenate([q_row, k_row], axis=0).T
            for sub in range(ROWS // T):
                rows_at = slice(sub * T, (sub + 1) * T)
                at = span(first + sub * T, T)
                q, kk = spread(turned[rows_at, 0:1]), spread(turned[rows_at, 4:5])
                for p in range(pairs):
                    cols = slice(p * LANES, (p + 1) * LANES)
                    z, y, dn = z_all[at, cols], y_all[at, cols], dn_all[at, cols].astype(f32)
                    gain = chan_ref[0:1, cols]
                    s = sigmoid(z)
                    sz = z * s
                    gated = y * sz
                    gq = gated * q
                    dg = q * gain * dn - gated * kk
                    gate_ref[:, cols] += jnp.sum((gq * dn).reshape(T // 8, 8, LANES), axis=0)
                    nl_all[at, cols] = (gq * gain).astype(bf16)
                    dz_all[at, cols] = (dg * y * (s + sz * (1.0 - s))).astype(bf16)
                    dn_all[at, cols] = (dg * sz).astype(bf16)
            branch_ref[span(i * ROWS, ROWS), :] = mm(nl_all[span(first, ROWS), :], wps[:, :width], NT).astype(bf16)
            return 0

        lax.fori_loop(0, 2, some, 0, unroll=2)

    def rows_out():
        return [
            pltpu.make_async_copy(src, dst, own_keep.at[2 + k])
            for k, (src, dst) in enumerate(((dz_all, dz_ref), (dn_all, dy_ref)))
        ]

    def early_out(i):
        at = span(i * ROWS, ROWS)
        return [
            pltpu.make_async_copy(src.at[at, pl.ds(0, width)], early_ref.at[at, pl.ds(k * width, width)], early_keep.at[k, i])
            for k, src in enumerate((ws, wps))
        ]

    @pl.when(step == products)
    def _():
        for copy in rows_out():
            copy.start()

        def some(i, _):
            at = span(i * ROWS, ROWS)
            lanes = pl.ds(pl.multiple_of(i * ROWS, ROWS), ROWS)
            grad = mm(xg[:, lanes], dz_all[...], TN)
            ws[at, :width] = grad.astype(bf16)
            share = jnp.zeros((ROWS, LANES), f32)
            for p in range(pairs):
                cols = slice(p * LANES, (p + 1) * LANES)
                w = wps[at, width + p * LANES : width + (p + 1) * LANES]
                share = share + grad[:, cols] * w.astype(f32)
            gain_ref[:, lanes] = mm_exact(jnp.ones((8, LANES), f32), share, NT)
            wps[at, :width] = mm(cots[:, lanes], nl_all[...], TN).astype(bf16)
            for copy in early_out(i):
                copy.start()
            return 0

        lax.fori_loop(0, D // ROWS, some, 0, unroll=3)
        for copy in rows_out():
            copy.wait()

        def done(i, _):
            for copy in early_out(i):
                copy.wait()
            return 0

        lax.fori_loop(0, D // ROWS, done, 0)


def parameter_rows(me, width, flat_ref, taps_ref, head_ref, chan_ref):
    pairs = width // LANES
    heads = width // P_SIZE
    taps_ref[...] = jnp.zeros_like(taps_ref)
    chan_ref[...] = jnp.zeros_like(chan_ref)
    for c in range(pairs):
        cols = slice(c * LANES, (c + 1) * LANES)
        chan_ref[0:1, cols] = flat_ref[pl.ds(GATE_ROW + pairs * me + c, 1), :]
        taps_ref[CONV : CONV + 1, cols] = flat_ref[pl.ds(BIAS_ROW + pairs * me + c, 1), :]
        for k in range(CONV):
            taps_ref[k : k + 1, cols] = flat_ref[pl.ds(TAPS_ROW + 4 * pairs * k + pairs * me + c, 1), :]
    for c in range(2):
        cols = slice(width + c * LANES, width + (c + 1) * LANES)
        taps_ref[CONV : CONV + 1, cols] = flat_ref[BIAS_BC_ROW + c : BIAS_BC_ROW + c + 1, :]
        for k in range(CONV):
            row = TAPS_BC_ROW + 2 * k + c
            taps_ref[k : k + 1, cols] = flat_ref[row : row + 1, :]
    both = jnp.concatenate([flat_ref[HEAD_ROW : HEAD_ROW + 1, :], flat_ref[HEAD_ROW + 1 : HEAD_ROW + 2, :]], axis=1)
    both = jnp.broadcast_to(both, (8, 2 * LANES))
    lane = lax.broadcasted_iota(jnp.int32, (2 * LANES, LANES), 0)
    head = lax.broadcasted_iota(jnp.int32, (2 * LANES, LANES), 1)

    def take(kind):
        match = (lane == 4 * heads * kind + heads * me + head) & (head < heads)
        return mm_exact(both, jnp.where(match, 1.0, 0.0).astype(f32))

    valid = lax.broadcasted_iota(jnp.int32, (8, LANES), 1) < heads
    row = lax.broadcasted_iota(jnp.int32, (8, LANES), 0)
    rates = jnp.where(valid, -jnp.exp(take(1)), 0.0)
    head_ref[...] = jnp.where(row == 0, take(0), jnp.where(row == 1, rates, 0.0))
    skip = mm_exact(take(2), picked(width).astype(f32), NT)
    chan_ref[1:2, :] = skip[0:1]


def picked(width):
    channel = lax.broadcasted_iota(jnp.int32, (width, LANES), 0)
    head = lax.broadcasted_iota(jnp.int32, (width, LANES), 1)
    return jnp.where((channel >= head * P_SIZE) & (channel < (head + 1) * P_SIZE), 1.0, 0.0).astype(bf16)


def scan_step(
    width, tick, i, xg, w_ref, taps_ref, head_ref, chan_ref,
    v_ref, xc_ref, dr_ref, st_ref, halo, state, y_all, head_t, until, across_state, tails, late_turn,
):
    pairs = width // LANES
    wide = width + 2 * NS
    mine = span(tick * ROWS, ROWS)
    dr_ref[span(i * ROWS, ROWS), :] = mm(xg[mine, :], w_ref[:, wide:])
    halo[8 : 8 + ROWS, :] = mm(xg[mine, :], w_ref[:, :wide])
    low_half = block_iota(1) < P_SIZE
    causal = block_iota(0) >= block_iota(1)

    def convolved(sub, block):
        cols = slice(block * LANES, (block + 1) * LANES)
        total = taps_ref[CONV : CONV + 1, cols]
        for k in range(CONV):
            first = 8 - (CONV - 1) + k + sub * T
            total = total + taps_ref[k : k + 1, cols] * halo[first : first + T, cols]
        rows = span(i * ROWS + sub * T, T)
        xc_ref[rows, cols] = total.astype(bf16)
        v_ref[rows, cols] = halo[8 + sub * T : 8 + (sub + 1) * T, cols].astype(bf16)
        return total * sigmoid(total)

    for sub in range(ROWS // T):
        rows = span(i * ROWS + sub * T, T)
        _, _, decay_t, dt, decay = head_rows(dr_ref, head_t, until, rows)
        b_low = convolved(sub, pairs).astype(bf16)
        c_low = convolved(sub, pairs + 1).astype(bf16)
        b_t = b_low.T
        scores = jnp.where(causal, mm(c_low, b_low, NT), 0.0)
        entering = state[...].astype(bf16)
        st_ref[i * (ROWS // T) + sub] = entering
        across_state[...] = mm(c_low, entering)
        for p in range(pairs):
            cols = slice(p * LANES, (p + 1) * LANES)
            x = convolved(sub, p)
            l1, l2 = spread(decay[:, 2 * p : 2 * p + 1]), spread(decay[:, 2 * p + 1 : 2 * p + 2])
            both = jnp.where(low_half, l1, l2)
            dtb = jnp.where(
                low_half, spread(dt[:, 2 * p : 2 * p + 1]), spread(dt[:, 2 * p + 1 : 2 * p + 2])
            )
            u = x * dtb
            m1 = scores * jnp.exp2(jnp.minimum(l1 - decay_t[2 * p : 2 * p + 1, :], 0.0))
            m2 = scores * jnp.exp2(jnp.minimum(l2 - decay_t[2 * p + 1 : 2 * p + 2, :], 0.0))
            mixing = jnp.concatenate([m1.astype(bf16), m2.astype(bf16)], axis=1)
            u_low = u.astype(bf16)
            zero = jnp.zeros_like(u_low)
            parts = jnp.concatenate(
                [jnp.where(low_half, u_low, zero), jnp.where(low_half, zero, u_low)], axis=0
            )
            last = both[T - 1 : T, :]
            y = mm(mixing, parts) + jnp.exp2(both) * across_state[:, cols] + chan_ref[1:2, cols] * x
            tails[:, cols] = (u * jnp.exp2(last - both)).astype(bf16)
            state[:, cols] = jnp.exp2(last) * state[:, cols]
            y_all[span(tick * ROWS + sub * T, T), cols] = y
        state[...] = state[...] + mm(b_t, tails[...])
        if sub == 0:
            pl.when(tick == LEN // ROWS - 1)(late_turn)
    halo[0:8, :] = halo[ROWS : ROWS + 8, :]


def ssd_forward(n, layer_input, out_grad, flat, w_zx, w_bc, w_dt, w_out):
    rows, width = w_out.shape
    tokens = layer_input.shape[0]
    length = 4 * tokens
    wide = width + 2 * NS
    tall = 2 * ROWS
    steps = length // tall
    forming = steps + 2
    products = forming + steps
    subs = tall // T
    assert length == LEN
    row = lambda m: pl.BlockSpec((tall, m), lambda i: (jnp.minimum(i, steps - 1), 0))
    form = lambda m: pl.BlockSpec((tall, m), lambda i: (jnp.clip(i - forming, 0, steps - 1), 0))
    whole = lambda a: pl.BlockSpec(a.shape, lambda i: (0,) * a.ndim, pipeline_mode=pl.Buffered(1))
    fixed = lambda m: pl.BlockSpec((8, m), lambda i: (0, 0))
    anywhere = pl.BlockSpec(memory_space=pl.ANY)
    vm, dma = pltpu.VMEM, pltpu.SemaphoreType.DMA
    hops, lead = dma((2, 2, 2, n // 2)), dma((2, 2, n // 2))
    shape = lambda dims, dtype: jax.ShapeDtypeStruct(dims, dtype)
    return pl.pallas_call(
        functools.partial(forward_body, n, rows, tokens, width),
        grid=(products + 1,),
        in_specs=[anywhere, anywhere, *(whole(a) for a in (flat, w_zx, w_bc, w_dt, w_out))],
        out_specs=[
            row(wide), row(wide), row(LANES), pl.BlockSpec((subs, NS, width), lambda i: (jnp.minimum(i, steps - 1), 0, 0)),
            anywhere, anywhere, form(D), anywhere,
            fixed(width), fixed(D), anywhere, anywhere, anywhere, *(fixed(m) for m in (wide, LANES, width)),
        ],
        out_shape=[
            shape((length, wide), bf16), shape((length, wide), bf16), shape((length, LANES), f32),
            shape((length // T, NS, width), bf16), shape((length, width), bf16), shape((length, width), bf16),
            shape((length, D), bf16), shape((D, 2 * width), bf16), shape((8, width), f32), shape((8, D), f32),
            shape((length, D), bf16), shape((D, wide + LANES), bf16), shape((D, 2 * width), bf16),
            *(shape((8, m), f32) for m in (wide, LANES, width)),
        ],
        scratch_shapes=[
            vm((ROWS + 8, wide), f32), vm((NS, width), f32), vm((length, width), f32), vm((length, width), f32),
            *(vm((length, width), bf16) for _ in range(3)),
            vm((length, D), bf16), vm((length, D), bf16), vm((D, wide + LANES), bf16), vm((D, 2 * width), bf16),
            vm((4, 8, length), f32), vm((8, length), f32), vm((2, HEADS, LANES), f32), vm((3 * T, LANES), bf16),
            vm((T, width), f32), vm((T, width), bf16),
            dma((4,)), dma((2, D // ROWS)), lead, lead, lead, dma((11,)), dma((4,)), dma((4,)), dma((1,)), dma((1,)),
            dma((4,)), dma((4,)), lead, hops, hops, dma((4,)), dma((4,)),
            dma((1,)), dma((1,)), dma((4,)), dma((4,)), dma((3,)), dma((3,)),
        ],
        compiler_params=pltpu.CompilerParams(collective_id=2, has_side_effects=True, vmem_limit_bytes=ROOM),
        name="layer_forward",
    )(layer_input, out_grad, flat, w_zx, w_bc, w_dt, w_out)


def backward_body(
    n, own_rows, tokens, width,
    dy_ref, v_ref, xc_ref, dr_ref, st_ref, gate_ref, taps_ref, head_ref, chan_ref, early_ref, branch_ref,
    d_ref, small_ref, oearly_ref, obranch_ref,
    dxh, dstate, yst, bds, dyeb, utb, products, turn, acc, hacc, pick_ref, pick_t, fades, head_t, until_ref, reach_ref,
    own, slots, near, held, over_slot,
    load_sem, ring_send, ring_recv, near_send, near_recv, over_send, over_recv,
):
    pairs = width // LANES
    wide = width + 2 * NS
    step = pl.program_id(0)
    steps = LEN // ROWS
    subs = ROWS // T
    pos, ring, me, across, beside = neighbours(n)
    opposite = lax.rem(me + 2, 4)
    next_door = me + 1 - 2 * lax.rem(me, 2)
    far = lax.rem(next_door + 2, 4)
    half = tokens // 2
    cuts = cut_rows(own_rows)

    def block_at(way, count):
        return ring_index(lax.rem(pos + (count if way else n - count), n), n)

    def hop(k, way, h):
        first, size = cuts[way]
        if h == 0:
            src = early_ref.at[span(block_at(way, 1) * own_rows + first, size), pl.ds(k * width, width)]
        else:
            src = slots[way][k].at[h - 1]
        return remote(
            src, slots[way][k].at[h], ring_send.at[way, k, h], ring_recv.at[way, k, h], ring[way]
        )

    def near_copy(turned, part):
        start = (next_door if turned else far) * tokens + part * half
        return remote(
            branch_ref.at[span(start, half)], near.at[turned, part],
            near_send.at[turned, part], near_recv.at[turned, part], beside,
        )

    def held_copy(turned, part):
        start = (me if turned else opposite) * tokens + part * half
        return pltpu.make_async_copy(
            branch_ref.at[span(start, half)], held.at[turned, part], load_sem.at[2 * turned + part]
        )

    def over_copy(part):
        return remote(held.at[0, part], over_slot.at[part], over_send.at[part], over_recv.at[part], across)

    def own_copy():
        return pltpu.make_async_copy(early_ref, own, load_sem.at[4])

    def ring_turn(k, h):
        for way in (0, 1):
            first, size = cuts[way]
            hop(k, way, h).wait_recv()
            block = block_at(way, 2 + h) if h < n - 2 else block_at(way, 0)

            tile = strip(size)

            def some(i, _, way=way, first=first, block=block, tile=tile):
                cols = slice(k * width, (k + 1) * width)
                came = slots[way][k][h, span(i * tile, tile), :]
                mine = own[span(block * own_rows + first + i * tile, tile), cols]
                if h < n - 2:
                    slots[way][k][h, span(i * tile, tile), :] = came + mine
                else:
                    oearly_ref[span(first + i * tile, tile), cols] = came.astype(f32) + mine.astype(f32)
                return 0

            lax.fori_loop(0, size // tile, some, 0)
            if h < n - 2:
                hop(k, way, h + 1).start()

    def ring_poll(k, tick):
        for h in range(n - 1):
            pl.when(tick == min(h + 1, steps - 1))(functools.partial(ring_turn, k, h))

    def add_near(turned):
        for part in (0, 1):
            held_copy(turned, part).wait()
            near_copy(turned, part).wait_recv()

            def some(i, _, part=part):
                at = span(i * 32, 32)
                held[turned, part, at, :] = held[turned, part, at, :] + near[turned, part, at, :]
                return 0

            lax.fori_loop(0, half // 32, some, 0)
            if not turned:
                over_copy(part).start()

    @pl.when(step == 0)
    def _():
        enter((*ring, across, beside))
        for way in (0, 1):
            hop(0, way, 0).start()
        for turned in (0, 1):
            for part in (0, 1):
                near_copy(turned, part).start()
                held_copy(turned, part).start()
        own_copy().start()
        dxh[T : T + 8, :] = jnp.zeros((8, wide), f32)
        dstate[...] = jnp.zeros_like(dstate)
        acc[...] = jnp.zeros_like(acc)
        hacc[...] = jnp.zeros_like(hacc)
        turn[...] = jnp.zeros_like(turn)
        pick_ref[...] = picked(width)
        channel = lax.broadcasted_iota(jnp.int32, (HEADS, width), 1)
        head = lax.broadcasted_iota(jnp.int32, (HEADS, width), 0)
        mine = (channel >= head * P_SIZE) & (channel < (head + 1) * P_SIZE)
        pick_t[...] = jnp.where(mine, 1.0, 0.0).astype(bf16)
        set_heads(head_ref, head_t, until_ref)
        from_here = jnp.where(block_iota(0) >= block_iota(1), 1.0, 0.0).astype(bf16)
        after = jnp.where(block_iota(0) < block_iota(1), 1.0, 0.0).astype(bf16)
        for k, matrix in enumerate((from_here, from_here, after, after)):
            reach_ref[k * T : (k + 1) * T, :] = matrix
        products[3 * T :, :] = jnp.zeros((HEADS, width), bf16)

    low_half = block_iota(1) < P_SIZE
    row_at, col_at = block_iota(0), block_iota(1)
    until = row_at <= col_at
    pair_lane = lax.broadcasted_iota(jnp.int32, (8, 2 * T), 1)
    pair_row = lax.broadcasted_iota(jnp.int32, (8, 2 * T), 0)
    each = jnp.where(lax.div(pair_lane, T) == pair_row, 1.0, 0.0).astype(bf16)
    ones = jnp.ones((8, T), bf16)

    def add(index, cols, value):
        acc[index, :, cols] += jnp.sum(value.reshape(T // 8, 8, LANES), axis=0)

    def conv_back(rows, block, d_act, xc, s, act):
        cols = slice(block * LANES, (block + 1) * LANES)
        dxh[0:T, cols] = d_act * (s + act * (1.0 - s))
        v = v_ref[rows, cols].astype(f32)
        total = None
        for m in range(CONV):
            moved = dxh[m : m + T, cols]
            if m == 0:
                add(CONV, cols, moved)
            add(CONV - 1 - m, cols, v * moved)
            term = taps_ref[CONV - 1 - m : CONV - m, cols] * moved
            total = term if total is None else total + term
        d_ref[rows, cols] = total.astype(bf16)

    def work(i, _):
        tick = 2 * step + i
        chunk = 1 - i

        @pl.when(tick == 1)
        def _():
            own_copy().wait()
            add_near(0)

        pl.when(tick == 2)(functools.partial(add_near, 1))
        ring_poll(0, tick)
        for sub in reversed(range(subs)):
            rows = span(chunk * ROWS + sub * T, T)
            block_state = chunk * subs + sub
            raw_t, dt_t, decay_t, dt, decay = head_rows(dr_ref, head_t, until_ref, rows)
            b_cols = slice(width, width + NS)
            c_cols = slice(width + NS, width + 2 * NS)
            b_xc, c_xc = xc_ref[rows, b_cols].astype(f32), xc_ref[rows, c_cols].astype(f32)
            b_s, c_s = sigmoid(b_xc), sigmoid(c_xc)
            b_act, c_act = b_xc * b_s, c_xc * c_s
            b_low, c_low = b_act.astype(bf16), c_act.astype(bf16)
            c_t = c_low.T
            scores_t = jnp.where(until, mm(b_low, c_low, NT), 0.0)
            ds_low = dstate[...].astype(bf16)
            yst[...] = mm(c_low, st_ref[block_state])
            bds[...] = mm(b_low, ds_low)
            d_scores = jnp.zeros((T, LANES), f32)
            for p in range(pairs):
                cols = slice(p * LANES, (p + 1) * LANES)
                dy_low = dy_ref[rows, cols]
                dy = dy_low.astype(f32)
                xc = xc_ref[rows, cols].astype(f32)
                xs = sigmoid(xc)
                x = xc * xs
                l1, l2 = spread(decay[:, 2 * p : 2 * p + 1]), spread(decay[:, 2 * p + 1 : 2 * p + 2])
                both = jnp.where(low_half, l1, l2)
                dtb = jnp.where(
                    low_half, spread(dt[:, 2 * p : 2 * p + 1]), spread(dt[:, 2 * p + 1 : 2 * p + 2])
                )
                u = x * dtb
                last = both[T - 1 : T, :]
                e1 = jnp.exp2(jnp.minimum(decay_t[2 * p : 2 * p + 1, :] - l1, 0.0))
                e2 = jnp.exp2(jnp.minimum(decay_t[2 * p + 1 : 2 * p + 2, :] - l2, 0.0))
                zero = jnp.zeros_like(dy_low)
                dy_parts = jnp.concatenate(
                    [jnp.where(low_half, dy_low, zero), jnp.where(low_half, zero, dy_low)], axis=0
                )
                du_in = mm(
                    jnp.concatenate([(scores_t * e1).astype(bf16), (scores_t * e2).astype(bf16)], axis=1), dy_parts
                )
                d_mix = mm(u.astype(bf16), dy_parts, NT)
                d1, d2 = d_mix[:, :T] * e1, d_mix[:, T:] * e2
                d_scores = d_scores + d1 + d2
                held_pairs = jnp.concatenate([(d1 * scores_t).astype(bf16), (d2 * scores_t).astype(bf16)], axis=1)
                reached_by = mm(ones, held_pairs)
                leaving = mm(each, held_pairs, NT)
                turn[2 * p : 2 * p + 1, :] = reached_by[0:1, :T] - leaving[0:1]
                turn[2 * p + 1 : 2 * p + 2, :] = reached_by[0:1, T:] - leaving[1:2]
                tail = jnp.exp2(last - both)
                fades[0:1, cols] = jnp.exp2(last)
                dye = dy * jnp.exp2(both)
                du_out = tail * bds[:, cols]
                du = du_in + du_out
                products[0:T, cols] = (dye * yst[:, cols]).astype(bf16)
                products[T : 2 * T, cols] = (u * du_out).astype(bf16)
                products[2 * T : 3 * T, cols] = (x * du).astype(bf16)
                dyeb[:, cols] = dye.astype(bf16)
                utb[:, cols] = (u * tail).astype(bf16)
                add(CONV + 1, cols, dy * x)
                conv_back(rows, p, dtb * du + chan_ref[1:2, cols] * dy, xc, xs, x)
            d_scores = jnp.where(until, d_scores, 0.0).astype(bf16)
            d_b = mm(d_scores, c_low) + mm(utb[...], ds_low, NT)
            d_c = mm(d_scores, b_low, TN) + mm(dyeb[...], st_ref[block_state], NT)
            conv_back(rows, pairs, d_b, b_xc, b_s, b_act)
            conv_back(rows, pairs + 1, d_c, c_xc, c_s, c_act)
            fade = fades[0:1, :]
            before_ds = dstate[...]
            through = jnp.sum(before_ds * st_ref[block_state].astype(f32), axis=0, keepdims=True) * fade
            products[3 * T : 3 * T + HEADS, :] = jnp.broadcast_to(through, (HEADS, width)).astype(bf16)
            dstate[...] = fade * before_ds + mm(c_t, dyeb[...])
            by_head = mm(pick_t[...], products[...], NT)
            inside = pieces(turn[...] + by_head[:, :T], 2)
            outside = pieces(by_head[:, T : 2 * T], 2)
            reached = mm(jnp.concatenate([inside, outside], axis=1), reach_ref[...])
            reached = reached + jnp.broadcast_to(by_head[:, 3 * T : 3 * T + 1], (HEADS, T))
            d_raw = (head_t[1] * reached + by_head[:, 2 * T : 3 * T]) * sigmoid(raw_t)
            d_ref[rows, wide:] = columns_of(d_raw).astype(bf16)
            hacc[0] += d_raw
            hacc[1] += dt_t * reached
            dxh[T : T + 8, :] = dxh[0:8, :]
            if sub == 1:
                @pl.when(tick == 0)
                def _():
                    for way in (0, 1):
                        hop(1, way, 0).start()

                ring_poll(1, tick)
        return 0

    lax.fori_loop(0, 2, work, 0)

    @pl.when(step == steps // 2 - 1)
    def _():
        total = lambda a: jnp.sum(a, axis=0, keepdims=True)
        for k in range(CONV + 1):
            small_ref[k : k + 1, :] = total(acc[k])
        small_ref[CONV + 1 : CONV + 2, :width] = total(gate_ref[...])
        small_ref[CONV + 1 : CONV + 2, width : width + LANES] = total(columns_of(hacc[0]))
        small_ref[CONV + 1 : CONV + 2, width + LANES :] = total(columns_of(hacc[1])) * head_ref[1:2, :]
        small_ref[CONV + 2 :, :] = jnp.zeros((2, wide), f32)
        skip = mm_exact(acc[CONV + 1, :, :width], pick_ref[...].astype(f32))
        small_ref[CONV + 3 : CONV + 4, 512 : 512 + LANES] = total(skip)
        for part in (0, 1):
            over_copy(part).wait_recv()

            def some(i, _, part=part):
                at = span(part * half + i * 32, 32)
                here = span(i * 32, 32)
                total = held[1, part, here, :].astype(f32) + over_slot[part, here, :].astype(f32)
                obranch_ref[at, :] = total.astype(bf16)
                return 0

            lax.fori_loop(0, half // 32, some, 0)
        for part in (0, 1):
            over_copy(part).wait_send()
            for turned in (0, 1):
                near_copy(turned, part).wait_send()
        for h in range(n - 1):
            for k in (0, 1):
                for way in (0, 1):
                    hop(k, way, h).wait_send()


def ssd_backward(n, dy, v, xc, dr, st, gate, taps, head, chan, early, branch):
    length, width = dy.shape
    wide = width + 2 * NS
    tall = 2 * ROWS
    steps = length // tall
    subs = tall // T
    own_rows, tokens = D // n, length // 4
    half = tokens // 2
    row = lambda m: pl.BlockSpec((tall, m), lambda i: (steps - 1 - i, 0))
    whole = lambda a: pl.BlockSpec(a.shape, lambda i: (0,) * a.ndim, pipeline_mode=pl.Buffered(1))
    fixed = lambda *shape: pl.BlockSpec(shape, lambda i: (0,) * len(shape))
    anywhere = pl.BlockSpec(memory_space=pl.ANY)
    vm, dma = pltpu.VMEM, pltpu.SemaphoreType.DMA
    return pl.pallas_call(
        functools.partial(backward_body, n, own_rows, tokens, width),
        grid=(steps,),
        in_specs=[
            row(width), row(wide), row(wide), row(LANES),
            pl.BlockSpec((subs, NS, width), lambda i: (steps - 1 - i, 0, 0)),
            whole(gate), whole(taps), whole(head), whole(chan), anywhere, anywhere,
        ],
        out_specs=[
            row(wide + LANES), fixed(8, wide), fixed(own_rows, 2 * width), fixed(tokens, D),
        ],
        out_shape=[
            jax.ShapeDtypeStruct((length, wide + LANES), bf16),
            jax.ShapeDtypeStruct((8, wide), f32),
            jax.ShapeDtypeStruct((own_rows, 2 * width), f32),
            jax.ShapeDtypeStruct((tokens, D), bf16),
        ],
        scratch_shapes=[
            vm((T + 8, wide), f32), vm((NS, width), f32), vm((T, width), f32), vm((T, width), f32),
            vm((T, width), bf16), vm((T, width), bf16), vm((3 * T + HEADS, width), bf16),
            vm((HEADS, T), f32), vm((CONV + 2, 8, wide), f32), vm((2, HEADS, T), f32),
            vm((width, LANES), bf16), vm((HEADS, width), bf16), vm((8, width), f32), vm((2, HEADS, LANES), f32),
            vm((3 * T, LANES), bf16), vm((4 * T, LANES), bf16),
            vm((D, 2 * width), bf16),
            [[vm((n - 1, size, width), bf16) for _ in (0, 1)] for _, size in cut_rows(own_rows)],
            vm((2, 2, half, D), bf16), vm((2, 2, half, D), bf16), vm((2, half, D), bf16),
            dma((5,)), dma((2, 2, n - 1)), dma((2, 2, n - 1)), dma((2, 2)), dma((2, 2)), dma((2,)), dma((2,)),
        ],
        compiler_params=pltpu.CompilerParams(
            collective_id=3, has_side_effects=True, vmem_limit_bytes=ROOM
        ),
        name="layer_backward",
    )(dy, v, xc, dr, st, gate, taps, head, chan, early, branch)


def reduce_body(
    n, rows, tokens, starts,
    xg_ref, d_ref, dz_ref, wp_ref, w_ref, small_ref, flat_ref, gain_ref,
    oxs_ref, oback_ref, bc_ref, oflat_ref,
    xg, d, dz, wz, w, work, grads, slots, staged, near, over, smalls, tens, bc_slot,
    load_sem, ring_send, ring_recv, near_send, near_recv, over_send, over_recv,
    small_send, small_recv, ten_send, ten_recv, bc_send, bc_recv,
):
    pos, ring, me, across, beside = neighbours(n)
    cuts = cut_rows(rows)
    core = lax.rem(me, 2)
    opposite = lax.rem(me + 2, 4)
    next_door = me + 1 - 2 * core
    far = lax.rem(next_door + 2, 4)
    half = tokens // 2
    late = d.shape[1]
    width = dz.shape[1]
    tile = 2 * LANES
    tiles = D // tile
    columns = [pl.ds(lo, hi - lo) for lo, hi in starts]
    sources = [(d_ref.at[:, columns[0]], d.at[:, columns[0]])]
    sources += [(xg_ref.at[:, pl.ds(i * tile, tile)], xg.at[:, pl.ds(i * tile, tile)]) for i in range(tiles)]
    sources += [(d_ref.at[:, some], d.at[:, some]) for some in columns[1:]]
    sources += [
        (dz_ref, dz), (w_ref, w), (wp_ref.at[:, pl.ds(width, width)], wz), (small_ref, smalls.at[pos]),
    ]
    loads = [pltpu.make_async_copy(src, dst, load_sem.at[k]) for k, (src, dst) in enumerate(sources)]
    for load in loads:
        load.start()
    askew = {"tensor": far}
    enter((*ring, across, beside, askew))
    started = []

    def go(*args):
        copy = remote(*args)
        copy.start()
        started.append(copy)

    def block_at(way, count):
        return ring_index(lax.rem(pos + (count if way else n - count), n), n)

    def hop(k, way, h):
        lo, hi = starts[k]
        first, size = cuts[way]
        if h == 0:
            src = grads.at[span(block_at(way, 1) * rows + first, size), pl.ds(lo, hi - lo)]
        else:
            src = slots[way][k].at[h - 1]
        return remote(
            src, slots[way][k].at[h], ring_send.at[way, k, h], ring_recv.at[way, k, h], ring[way]
        )

    def product(k):
        lo, hi = starts[k]

        def some(i, _):
            at = pl.ds(pl.multiple_of(i * tile, tile), tile)
            if k == 0:
                pltpu.make_async_copy(xg_ref.at[:, at], xg.at[:, at], load_sem.at[1 + i]).wait()
            grads[at, lo:hi] = mm(xg[:, at], d[:, lo:hi], TN).astype(bf16)
            return 0

        if k < 2:
            loads[0 if k == 0 else tiles + k].wait()
        lax.fori_loop(0, tiles, some, 0)
        for way in (0, 1):
            hop(k, way, 0).start()

    def near_copy(turned, part):
        return remote(
            staged.at[turned, part], near.at[turned, part],
            near_send.at[turned, part], near_recv.at[turned, part], beside,
        )

    def over_copy(part):
        return remote(near.at[0, part], over.at[part], over_send.at[part], over_recv.at[part], across)

    def ring_turn(k, h):
        lo, hi = starts[k]
        for way in (0, 1):
            first, size = cuts[way]
            slot = slots[way][k].at[h]
            remote(slot, slot, ring_send.at[way, k, h], ring_recv.at[way, k, h], ring[way]).wait_recv()
            block = block_at(way, 2 + h) if h < n - 2 else block_at(way, 0)

            tile = strip(size)

            def some(i, _, way=way, first=first, block=block, tile=tile):
                came = slots[way][k][h, span(i * tile, tile), :]
                mine = grads[span(block * rows + first + i * tile, tile), lo:hi]
                if h < n - 2:
                    slots[way][k][h, span(i * tile, tile), :] = came + mine
                else:
                    oxs_ref[span(first + i * tile, tile), lo:hi] = came.astype(f32) + mine.astype(f32)
                return 0

            lax.fori_loop(0, size // tile, some, 0)
            if h < n - 2:
                hop(k, way, h + 1).start()

    def small_hop(way, h):
        here = smalls.at[lax.rem(pos + (h if way else n - h), n)]
        go(here, here, small_send.at[way, h], small_recv.at[way, h], ring[way])

    def small_lands(way, h):
        here = smalls.at[lax.rem(pos + (h + 1 if way else n - h - 1), n)]
        remote(here, here, small_send.at[way, h], small_recv.at[way, h], ring[way]).wait_recv()

    product(0)
    product(1)
    for load in loads[tiles + 2 :]:
        load.wait()
    turns = {0: [(0, 0)], 1: [(1, 0)], 2: [(0, 1)], 3: [(1, 1)], 4: [(0, 2), (1, 2)], 5: [(2, 0)], 6: [(0, 3), (1, 3)], 7: [(2, 1)]}
    taken = [sum(k == group for some in turns.values() for k, _ in some) for group in range(len(starts))]

    def block(i, _):
        pl.when(i == 4)(functools.partial(product, 2))
        which, part = lax.div(i, 2), lax.rem(i, 2)
        own = lax.rem(which, 2)
        turned = lax.div(which, 2)
        target = lax.rem(next_door + own * (me - next_door) + 2 * (1 - turned), 4)
        at = span(target * tokens + part * half, half)
        total = mm(dz[at, :], wz[...], NT) + mm(d[at, :], w[...], NT)
        work[...] = total

        @pl.when(own == 0)
        def _():
            staged[turned, part] = work[...].astype(bf16)
            near_copy(turned, part).start()

        @pl.when(own == 1)
        def _():
            near_copy(turned, part).wait_recv()

        @pl.when(which == 1)
        def _():
            near[0, part] = (work[...] + near[0, part].astype(f32)).astype(bf16)
            over_copy(part).start()

        @pl.when(which == 3)
        def _():
            near[1, part] = (work[...] + near[1, part].astype(f32)).astype(bf16)

        for at_block, some in turns.items():

            @pl.when(i == at_block)
            def _(some=some):
                for k, h in some:
                    ring_turn(k, h)

        return 0

    lax.fori_loop(0, 8, block, 0)
    for i in range(tiles):
        share = jnp.zeros((tile, LANES), f32)
        for c in range(late // LANES):
            cols = slice(c * LANES, (c + 1) * LANES)
            at = slice(i * tile, (i + 1) * tile)
            share = share + grads[at, cols].astype(f32) * w[at, cols].astype(f32)
        total = mm_exact(jnp.ones((8, LANES), f32), share, NT)[0:1] + gain_ref[0:1, i * tile : (i + 1) * tile]
        for c in range(2 * i, 2 * i + 2):
            row, col = 6 + c // 8, (c % 8) * LANES
            part = total[:, (c - 2 * i) * LANES : (c - 2 * i + 1) * LANES]
            smalls[pos, row : row + 1, col : col + LANES] = part / flat_ref[c : c + 1, :]

    rest = [(k, h) for h in range(n - 1) for k in (2, 0, 1) if h >= taken[k]]
    rest.sort(key=lambda turn: turn[1] - taken[turn[0]])

    def small_step(s):
        for way in (0, 1):
            if s > 0 and (way == 0 or s < n // 2):
                small_lands(way, s - 1)
            if s < n // 2 - way:
                small_hop(way, s)

    small_step(0)
    steps_done = 1
    for at, (k, h) in enumerate(rest):
        ring_turn(k, h)
        if (k, h) == (0, n - 2):
            bc_slot[0] = oxs_ref[:, starts[0][0] : starts[0][0] + 2 * NS]
            go(bc_slot.at[0], bc_slot.at[1], bc_send.at[0], bc_recv.at[0], beside)
        if at % 2 == 1 and steps_done < n // 2:
            small_step(steps_done)
            steps_done += 1
    for s in range(steps_done, n // 2):
        small_step(s)
    small_lands(0, n // 2 - 1)

    total = smalls[0]
    for i in range(1, n):
        total = total + smalls[i]
    tens[me] = total
    others = ((beside, next_door), (across, opposite), (askew, far))
    for k, (peer, _) in enumerate(others):
        go(tens.at[me], tens.at[me], ten_send.at[k], ten_recv.at[k], peer)
    remote(bc_slot.at[1], bc_slot.at[1], bc_send.at[0], bc_recv.at[0], beside).wait_recv()
    bc_slot[2] = bc_slot[0] + bc_slot[1]
    go(bc_slot.at[2], bc_slot.at[3], bc_send.at[1], bc_recv.at[1], across)
    for part in (0, 1):
        over_copy(part).wait_recv()

        def some(i, _, part=part):
            at = span(part * half + i * 32, 32)
            here = span(i * 32, 32)
            oback_ref[at, :] = (near[1, part, here, :].astype(f32) + over[part, here, :].astype(f32)).astype(bf16)
            return 0

        lax.fori_loop(0, half // 32, some, 0)
    for k, (peer, target) in enumerate(others):
        here = tens.at[target]
        remote(here, here, ten_send.at[k], ten_recv.at[k], peer).wait_recv()
    flat_gradients(width, tens, oflat_ref)
    remote(bc_slot.at[3], bc_slot.at[3], bc_send.at[1], bc_recv.at[1], across).wait_recv()
    bc_ref[...] = bc_slot[2] + bc_slot[3]
    for part in (0, 1):
        over_copy(part).wait_send()
        for turned in (0, 1):
            near_copy(turned, part).wait_send()
    for k in range(len(starts)):
        for way in (0, 1):
            for h in range(n - 1):
                hop(k, way, h).wait_send()
    for copy in started:
        copy.wait_send()


def flat_gradients(width, tens, out_ref):
    pairs = width // LANES
    heads = width // P_SIZE

    def sums(row, col):
        total = tens[0, row : row + 1, col : col + LANES]
        for t in range(1, 4):
            total = total + tens[t, row : row + 1, col : col + LANES]
        return total

    def put(row, value):
        out_ref[row : row + 1, :] = value

    for c in range(D // LANES):
        put(c, sums(6 + c // 8, (c % 8) * LANES))
    for t in range(4):
        for c in range(pairs):
            cols = slice(c * LANES, (c + 1) * LANES)
            put(GATE_ROW + pairs * t + c, tens[t, CONV + 1 : CONV + 2, cols])
            put(BIAS_ROW + pairs * t + c, tens[t, CONV : CONV + 1, cols])
            for k in range(CONV):
                put(TAPS_ROW + 4 * pairs * k + pairs * t + c, tens[t, k : k + 1, cols])
    for c in range(2):
        put(BIAS_BC_ROW + c, sums(CONV, width + c * LANES))
        for k in range(CONV):
            put(TAPS_BC_ROW + 2 * k + c, sums(k, width + c * LANES))
    kinds = ((CONV + 1, width), (CONV + 1, width + LANES), (CONV + 3, 512))
    rows = [tens[t, row : row + 1, col : col + LANES] for row, col in kinds for t in range(4)]
    rows = jnp.concatenate(rows + [jnp.zeros((16 - len(rows), LANES), f32)], axis=0)
    lane = lax.broadcasted_iota(jnp.int32, (LANES, 2 * LANES), 1)
    entry = lax.broadcasted_iota(jnp.int32, (LANES, 2 * LANES), 0)
    spread_out = mm_exact(rows, jnp.where(lax.rem(lane, heads) == entry, 1.0, 0.0).astype(f32))
    at = lax.broadcasted_iota(jnp.int32, (16, 2 * LANES), 1)
    source = lax.broadcasted_iota(jnp.int32, (16, 2 * LANES), 0)
    line = jnp.sum(jnp.where(lax.div(at, heads) == source, spread_out, 0.0), axis=0, keepdims=True)
    put(HEAD_ROW, line[:, :LANES])
    put(HEAD_ROW + 1, line[:, LANES:])


def reduce_all(n, xg, d, dz, wp, w, small, flat, gain):
    rows, tokens = D // n, dz.shape[0] // 4
    width, late = dz.shape[1], d.shape[1]
    starts = ((width, late), (0, width // 2), (width // 2, width))
    half = tokens // 2
    dma, vm = pltpu.SemaphoreType.DMA, pltpu.VMEM
    anywhere = pl.BlockSpec(memory_space=pl.ANY)
    inside = pl.BlockSpec(memory_space=pltpu.VMEM)
    return pl.pallas_call(
        functools.partial(reduce_body, n, rows, tokens, starts),
        in_specs=[anywhere] * 6 + [inside] * 2,
        out_specs=[inside] * 4,
        out_shape=[
            jax.ShapeDtypeStruct((rows, late), f32),
            jax.ShapeDtypeStruct((tokens, D), bf16),
            jax.ShapeDtypeStruct((rows, 2 * NS), f32),
            jax.ShapeDtypeStruct((FLAT_ROWS, LANES), f32),
        ],
        scratch_shapes=[
            vm(xg.shape, bf16), vm(d.shape, bf16), vm(dz.shape, bf16), vm((D, width), bf16),
            vm((D, late), bf16),
            vm((half, D), f32), vm((D, late), bf16),
            [[vm((n - 1, size, hi - lo), bf16) for lo, hi in starts] for _, size in cut_rows(rows)],
            vm((2, 2, half, D), bf16), vm((2, 2, half, D), bf16), vm((2, half, D), bf16),
            vm((n, *small.shape), f32), vm((4, *small.shape), f32), vm((4, rows, 2 * NS), f32),
            dma((13,)), dma((2, 3, n - 1)), dma((2, 3, n - 1)), dma((2, 2)), dma((2, 2)), dma((2,)), dma((2,)),
            dma((2, n // 2)), dma((2, n // 2)), dma((3,)), dma((3,)), dma((2,)), dma((2,)),
        ],
        compiler_params=pltpu.CompilerParams(
            collective_id=1, has_side_effects=True, vmem_limit_bytes=46 * 2**20
        ),
        name="reduce_all",
    )(xg, d, dz, wp, w, small, flat, gain)


def adamw_step(weight, first, second, grad, rate, decay):
    first_new = beta_first * first + (1.0 - beta_first) * grad
    second_new = beta_second * second + (1.0 - beta_second) * grad * grad
    hat_first = first_new * (1.0 / (1.0 - beta_first**STEP))
    hat_second = second_new * (1.0 / (1.0 - beta_second**STEP))
    weight_new = weight - rate * (hat_first / (jnp.sqrt(hat_second) + adam_eps) + decay * weight)
    return (weight_new, first_new, second_new)


def finish_body(
    width, heads,
    in_ref, cot_ref, branch_ref, back_ref, flat_ref, early_ref, late_ref, bcg_ref,
    zx_ref, zx1_ref, zx2_ref, bc_ref, bc1_ref, bc2_ref, out_ref, out1_ref, out2_ref, late_all_ref, dt_ref, dt1_ref, dt2_ref,
    layer_ref, grad_ref, zxn_ref, zx1n_ref, zx2n_ref, bcn_ref, bc1n_ref, bc2n_ref,
    outn_ref, out1n_ref, out2n_ref, dtn_ref, dt1n_ref, dt2n_ref,
):
    def update(refs, news, grad):
        fresh = adamw_step(*(ref[...] for ref in refs), grad, matrix_rate, matrix_decay)
        for ref, value in zip(news, fresh):
            ref[...] = value

    for k, grad in ((0, early_ref), (1, late_ref)):
        fresh = adamw_step(
            *(ref[:, k, :] for ref in (zx_ref, zx1_ref, zx2_ref)), grad[:, :width], matrix_rate, matrix_decay
        )
        for ref, value in zip((zxn_ref, zx1n_ref, zx2n_ref), fresh):
            ref[:, k, :] = value
    update((bc_ref, bc1_ref, bc2_ref), (bcn_ref, bc1n_ref, bc2n_ref), bcg_ref[...])
    update((out_ref, out1_ref, out2_ref), (outn_ref, out1n_ref, out2n_ref), early_ref[:, width:])

    @pl.when(pl.program_id(0) == 0)
    def _():
        unit = jnp.where(
            lax.broadcasted_iota(jnp.int32, (16, LANES), 0) == lax.broadcasted_iota(jnp.int32, (16, LANES), 1), 1.0, 0.0
        ).astype(f32)
        turned = mm_exact(unit, late_all_ref[:, width + 2 * NS :], NT)
        update((dt_ref, dt1_ref, dt2_ref), (dtn_ref, dt1n_ref, dt2n_ref), turned[:heads])

    rows = in_ref.shape[0]
    tile = 64

    def some(i, _):
        at = span(i * tile, tile)
        squares = jnp.zeros((tile, LANES), f32)
        inner = jnp.zeros((tile, LANES), f32)
        for c in range(D // LANES):
            cols = slice(c * LANES, (c + 1) * LANES)
            x = in_ref[at, cols].astype(f32)
            squares = squares + x * x
            inner = inner + x * flat_ref[c : c + 1, :] * back_ref[at, cols].astype(f32)
        r = lax.rsqrt(jnp.sum(squares, axis=-1, keepdims=True) / D + norm_eps)
        k = r * r * r * jnp.sum(inner, axis=-1, keepdims=True) / D
        r, k = jnp.broadcast_to(r, (tile, LANES)), jnp.broadcast_to(k, (tile, LANES))
        for c in range(D // LANES):
            cols = slice(c * LANES, (c + 1) * LANES)
            x = in_ref[at, cols].astype(f32)
            layer_ref[at, cols] = (x + branch_ref[at, cols].astype(f32)).astype(bf16)
            back = back_ref[at, cols].astype(f32)
            grad_ref[at, cols] = cot_ref[at, cols].astype(f32) + r * flat_ref[c : c + 1, :] * back - x * k
        return 0

    lax.fori_loop(0, rows // tile, some, 0)


def finish(layer_input, out_grad, branch, back, flat, early, late, bcg, zx, bc, out, dt):
    (rows, width), heads = out[0].shape, dt[0].shape[0]
    steps = 4 if rows % 32 == 0 else 2
    part = lambda a: pl.BlockSpec((a.shape[0] // steps, *a.shape[1:]), lambda i: (i,) + (0,) * (a.ndim - 1))
    whole = lambda a: pl.BlockSpec(a.shape, lambda i: (0,) * a.ndim)
    like = lambda a, dtype=f32: jax.ShapeDtypeStruct(a.shape, dtype)
    weights = (*zx, *bc, *out)
    return pl.pallas_call(
        functools.partial(finish_body, width, heads),
        grid=(steps,),
        in_specs=[
            *(part(a) for a in (layer_input, out_grad, branch, back)), whole(flat),
            *(part(a) for a in (early, late, bcg, *weights)), whole(late), *(whole(a) for a in dt),
        ],
        out_specs=[part(layer_input), part(back), *(part(a) for a in weights), *(whole(a) for a in dt)],
        out_shape=[like(layer_input, bf16), like(layer_input), *(like(a) for a in weights), *(like(a) for a in dt)],
        compiler_params=pltpu.CompilerParams(vmem_limit_bytes=32 * 2**20),
        name="finish",
    )(layer_input, out_grad, branch, back, flat, early, late, bcg, *weights, late, *dt)


def local(
    layer_input,
    out_grad,
    small_params,
    small_first,
    small_second,
    w_zx,
    zx_first,
    zx_second,
    w_bc,
    bc_first,
    bc_second,
    w_dt,
    dt_first,
    dt_second,
    w_out,
    out_first,
    out_second,
):
    n = lax.axis_size("dp")
    flat = jnp.pad(small_params, (0, FLAT_ROWS * LANES - small_params.shape[0])).reshape(FLAT_ROWS, LANES)
    v, xc, dr, st, dy, dz, branch, early, gate, gain, xg, w_all, pair_all, taps, head, chan = ssd_forward(
        n, layer_input, out_grad, flat, w_zx, w_bc, w_dt.T, w_out
    )
    d_late, small, owner_early, own_branch = ssd_backward(
        n, dy, v, xc, dr, st, gate, taps, head, chan, early, branch
    )
    owner_late, d_normed_in, owner_bc, flat_grad = reduce_all(
        n, xg, d_late, dz, pair_all, w_all, small, flat, gain
    )
    small_grad = flat_grad.reshape(-1)[: small_params.shape[0]]
    small_new, small_first_new, small_second_new = adamw_step(
        small_params, small_first, small_second, small_grad, small_rate, 0.0
    )
    (
        layer_output, input_grad, zx_new, zx_first_new, zx_second_new, bc_new, bc_first_new, bc_second_new,
        out_new, out_first_new, out_second_new, dt_new, dt_first_new, dt_second_new,
    ) = finish(
        layer_input, out_grad, own_branch, d_normed_in, flat, owner_early, owner_late, owner_bc,
        (w_zx, zx_first, zx_second), (w_bc, bc_first, bc_second), (w_out, out_first, out_second),
        (w_dt.T, dt_first.T, dt_second.T),
    )
    dt_new, dt_first_new, dt_second_new = dt_new.T, dt_first_new.T, dt_second_new.T
    return (
        layer_output,
        input_grad,
        small_new,
        small_first_new,
        small_second_new,
        zx_new,
        zx_first_new,
        zx_second_new,
        bc_new,
        bc_first_new,
        bc_second_new,
        dt_new,
        dt_first_new,
        dt_second_new,
        out_new,
        out_first_new,
        out_second_new,
    )


def solution(mesh):
    return jax.shard_map(
        local,
        mesh=mesh,
        in_specs=(
            P(("dp", "tensor"), None),
            P(("dp", "tensor"), None),
            P(),
            P(),
            P(),
            P("dp", None, "tensor"),
            P("dp", None, "tensor"),
            P("dp", None, "tensor"),
            P("dp", None),
            P("dp", None),
            P("dp", None),
            P("dp", "tensor"),
            P("dp", "tensor"),
            P("dp", "tensor"),
            P("dp", "tensor"),
            P("dp", "tensor"),
            P("dp", "tensor"),
        ),
        out_specs=(
            P(("dp", "tensor"), None),
            P(("dp", "tensor"), None),
            P(),
            P(),
            P(),
            P("dp", None, "tensor"),
            P("dp", None, "tensor"),
            P("dp", None, "tensor"),
            P("dp", None),
            P("dp", None),
            P("dp", None),
            P("dp", "tensor"),
            P("dp", "tensor"),
            P("dp", "tensor"),
            P("dp", "tensor"),
            P("dp", "tensor"),
            P("dp", "tensor"),
        ),
        check_vma=False,
    )
```
